32 devices in a mesh: dp: 4 (over z), ctx: 2 (over x), head: 4 (over y, core).
Axes of the slice: x: 2, y: 2, z: 4, core: 2. Of those that a mesh axis runs over, the one named last changes fastest.
Arguments:
- tokens: bfloat16 [8, 1024, 1024], P('dp', ('ctx', 'head')), may hold values from -6 to 6
- cotangent: bfloat16 [8, 1024, 1024], P('dp', ('ctx', 'head')), may hold values from -6 to 6
- w_qkv: bfloat16 [1024, 3072], P(('dp', 'ctx')), may hold values from -0.1875 to 0.1875
- w_attn_out: bfloat16 [1024, 1024], P(('dp', 'ctx')), may hold values from -3 to 3
- w_in: bfloat16 [1024, 5248], P(('dp', 'ctx')), may hold values from -0.1875 to 0.1875
- w_mlp_out: bfloat16 [2624, 1024], P(('dp', 'ctx')), may hold values from -0.125 to 0.125
- norm_gain1: bfloat16 [1024], P(('dp', 'ctx')), may hold values from 0.5 to 1.5
- norm_gain2: bfloat16 [1024], P(('dp', 'ctx')), may hold values from 0.5 to 1.5
Outputs:
- out: bfloat16 [8, 1024, 1024], P('dp', ('ctx', 'head'))
- grad_tokens: float32 [8, 1024, 1024], P('dp', ('ctx', 'head'))
- grad_qkv: float32 [1024, 3072], P(('dp', 'ctx'), 'head')
- grad_attn_out: float32 [1024, 1024], P(('dp', 'ctx'), 'head')
- grad_in: float32 [1024, 5248], P(('dp', 'ctx'), 'head')
- grad_mlp_out: float32 [2624, 1024], P(('dp', 'ctx'), 'head')
- grad_gain1: float32 [1024], P(('dp', 'ctx', 'head'))
- grad_gain2: float32 [1024], P(('dp', 'ctx', 'head'))
The draws below stay inside these ranges and needn't reach their ends.
All inputs are finite; a program needn't handle non-finite values.
Results may differ from the reference program's by a relative error of at most 0.023.
Values may be sent and summed in bfloat16 or wider, within the bound.
No kernel may reach another device: no remote copies, remote signals or barrier semaphores. Data moves between devices by JAX's collectives and lax.ppermute only.
A program may use at most 192 MiB of HBM per device.

```python
import math
import jax
import jax.numpy as jnp
from jax import lax

D = 1024
H = 16
HD = 64
F = 2624
LEN = 1024
SEQS = 8


def shard_levels(stream_key, extent, shards, low, top_value):
    loudness = 1.0
    for position, parts in shards:
        draws = jax.random.uniform(jax.random.fold_in(jax.random.fold_in(stream_key, 6), position), (parts,), jnp.float32, low / len(shards), top_value / len(shards))
        loudness = loudness * jnp.repeat(jnp.exp(draws), extent[position] // parts).reshape((-1,) + (1,) * (len(extent) - 1 - position))
    return loudness


def centred(stream_key, extent, scale, most, split=(), kind=jnp.bfloat16):
    drawn = jax.random.normal(stream_key, extent, jnp.float32) * scale
    if len(split) > 0:
        drawn = shard_levels(stream_key, extent, split, -0.22, 0.18) * drawn
    return jnp.clip(drawn, min=-most, max=most).astype(kind)


def setup_inputs(seed: int = 0) -> dict:
    splits = jax.random.split(jax.random.key(seed), 9)
    return {
        "tokens": centred(splits[0], (SEQS, LEN, D), 1.0, 6.0, ((0, 4), (1, 8))),
        "cotangent": centred(splits[1], (SEQS, LEN, D), 1.0, 6.0, ((0, 4), (1, 8))),
        "w_qkv": centred(splits[2], (D, 3 * D), D ** -0.5, 0.1875, ((0, 8),)),
        "w_attn_out": centred(splits[3], (D, D), (max(1, 4 * D // LEN)) ** -0.5, 3.0, ((0, 8),)),
        "w_in": centred(splits[4], (D, 2 * F), D ** -0.5, 0.1875, ((0, 8),)),
        "w_mlp_out": centred(splits[5], (F, D), F ** -0.5, 0.125, ((0, 8),)),
        "norm_gain1": jnp.clip(1.0 + 0.1 * jax.random.normal(splits[6], (D,), jnp.float32), 0.5, 1.5).astype(jnp.bfloat16),
        "norm_gain2": jnp.clip(1.0 + 0.1 * jax.random.normal(splits[7], (D,), jnp.float32), 0.5, 1.5).astype(jnp.bfloat16),
    }


EPSILON = 1e-05
ROPE_BASE = 160000.0
HIGHEST = lax.Precision.HIGHEST

@jax.custom_vjp
def low(v):
    return lax.optimization_barrier(v.astype(jnp.bfloat16)).astype(jnp.float32)

@jax.custom_vjp
def low_back(v):
    return v

def low_keep(v):
    return (low(v), None)

def low_pass(kept, grad):
    return (grad,)

def back_keep(v):
    return (v, None)

def back_low(kept, grad):
    return (low(grad),)
low.defvjp(low_keep, low_pass)
low_back.defvjp(back_keep, back_low)

def normalize(values):
    centre = lax.optimization_barrier(jnp.mean(values, axis=-1, keepdims=True))
    shifted = values - centre
    spread = lax.optimization_barrier(jnp.mean(shifted * shifted, axis=-1, keepdims=True))
    return shifted * lax.rsqrt(spread + EPSILON)

def rope_tables(positions, half_size):
    frequency = jnp.exp(jnp.arange(half_size, dtype=jnp.float32) * (-math.log(ROPE_BASE) / half_size))
    angles = positions[:, None] * frequency[None, :]
    return (jnp.cos(angles), jnp.sin(angles))

def rotate(values, cosine, sine_table, direction):
    half_size = cosine.shape[-1]
    first_half = values[..., :half_size]
    second_half = values[..., half_size:]
    cos_part = cosine[:, None, :]
    sin_part = sine_table[:, None, :] * direction
    return jnp.concatenate([first_half * cos_part - second_half * sin_part, second_half * cos_part + first_half * sin_part], axis=-1)

def product(left, right):
    return jnp.dot(left, right, precision=HIGHEST, preferred_element_type=jnp.float32)

def layer(sequence, w_qkv, w_attn_out, w_in, w_mlp_out, norm_gain1, norm_gain2):
    length = sequence.shape[0]
    scale = HD ** (-0.5)
    lowered1 = low(normalize(sequence) * norm_gain1)
    projected = low_back(product(lowered1, w_qkv)).reshape(length, 3, H, HD)
    cosine, sine_table = rope_tables(jnp.arange(length, dtype=jnp.float32), HD // 2)
    queries = low_back(low(rotate(projected[:, 0], cosine, sine_table, 1.0)))
    keys_all = low_back(low(rotate(projected[:, 1], cosine, sine_table, 1.0)))
    values_all = low_back(low(projected[:, 2]))
    rows = math.gcd(length, 512)

    def attend_rows(query_block):
        scores = low_back(jnp.einsum('qhd,khd->hqk', query_block, keys_all, precision=HIGHEST, preferred_element_type=jnp.float32) * scale)
        row_peak = lax.optimization_barrier(jnp.max(scores, axis=-1, keepdims=True))
        log_total = row_peak + jnp.log(lax.optimization_barrier(jnp.sum(jnp.exp(scores - row_peak), axis=-1, keepdims=True)))
        weights = low(jnp.exp(scores - log_total))
        return jnp.einsum('hqk,khd->qhd', weights, values_all, precision=HIGHEST, preferred_element_type=jnp.float32)
    attended = lax.map(jax.checkpoint(attend_rows), queries.reshape(length // rows, rows, H, HD))
    attended = low_back(low(attended.reshape(length, D)))
    residual = sequence + low_back(product(attended, w_attn_out))
    lowered2 = low(normalize(residual) * norm_gain2)
    lifted = low_back(product(lowered2, w_in))
    mixed = low(jax.nn.gelu(lifted[:, :F], approximate=False) * lifted[:, F:])
    return residual + low_back(product(mixed, w_mlp_out))

def reference(tokens, cotangent, w_qkv, w_attn_out, w_in, w_mlp_out, norm_gain1, norm_gain2):
    inputs = tuple((array.astype(jnp.float32) for array in (tokens, w_qkv, w_attn_out, w_in, w_mlp_out, norm_gain1, norm_gain2)))

    def forward(sequences, *weight_list):
        return lax.map(lambda sequence: layer(sequence, *weight_list), sequences)
    result, pullback = jax.vjp(forward, *inputs)
    gradients = pullback(cotangent.astype(jnp.float32))
    return (result.astype(jnp.bfloat16), gradients[0], gradients[1], gradients[2], gradients[3], gradients[4], gradients[5], gradients[6])
```

```python
import math

import jax
import jax.numpy as jnp
from jax import lax
from jax.experimental import pallas as pl
from jax.experimental.pallas import tpu as pltpu
from jax.sharding import PartitionSpec as P

HD = 64


EPSILON = 1e-05
ROPE_BASE = 160000.0


def normalize(values):
    centre = jnp.mean(values, axis=-1, keepdims=True)
    shifted = values - centre
    spread = jnp.mean(shifted * shifted, axis=-1, keepdims=True)
    factor = lax.rsqrt(spread + EPSILON)
    return (shifted * factor, factor)


def norm_back(grad_normed, normed, factor):
    grad_centre = jnp.mean(grad_normed, axis=-1, keepdims=True)
    grad_along = jnp.mean(grad_normed * normed, axis=-1, keepdims=True)
    return (grad_normed - grad_centre - normed * grad_along) * factor


def rope_tables(positions, half_size):
    frequency = jnp.exp(
        jnp.arange(half_size, dtype=jnp.float32) * (-math.log(ROPE_BASE) / half_size)
    )
    angles = positions[:, None] * frequency[None, :]
    return (jnp.cos(angles), jnp.sin(angles))


def rotate(values, cosine, sine_table, direction):
    half_size = cosine.shape[-1]
    first_half = values[..., :half_size]
    second_half = values[..., half_size:]
    cos_part = cosine[:, None, :]
    sin_part = sine_table[:, None, :] * direction
    return jnp.concatenate(
        [
            first_half * cos_part - second_half * sin_part,
            second_half * cos_part + first_half * sin_part,
        ],
        axis=-1,
    )


def block_scores(queries4, keys_block, scale):
    keys4 = keys_block.reshape(
        keys_block.shape[0], keys_block.shape[1], queries4.shape[2], queries4.shape[3]
    )
    return (
        jnp.einsum("sqgd,skgd->sgqk", queries4, keys4, preferred_element_type=jnp.float32) * scale
    )


def attend_forward(queries4, keys_all, values_all, key_rows, scale):
    seqs_here, query_rows, groups, head_size = queries4.shape
    turns = keys_all.shape[1] // key_rows

    def statistics(turn, carry):
        row_peak, row_total = carry
        keys_block = lax.dynamic_slice_in_dim(keys_all, turn * key_rows, key_rows, 1)
        scores = block_scores(queries4, keys_block, scale)
        new_peak = jnp.maximum(row_peak, jnp.max(scores, axis=-1))
        row_total = row_total * jnp.exp(row_peak - new_peak) + jnp.sum(
            jnp.exp(scores - new_peak[..., None]), axis=-1
        )
        return (new_peak, row_total)

    start_peak = jnp.full((seqs_here, groups, query_rows), -1e30, jnp.float32)
    row_peak, row_total = lax.fori_loop(
        0, turns, statistics, (start_peak, jnp.zeros_like(start_peak))
    )
    log_total = row_peak + jnp.log(row_total)

    def accumulate(turn, running):
        keys_block = lax.dynamic_slice_in_dim(keys_all, turn * key_rows, key_rows, 1)
        values_block = lax.dynamic_slice_in_dim(values_all, turn * key_rows, key_rows, 1).reshape(
            seqs_here, key_rows, groups, head_size
        )
        weights = jnp.exp(block_scores(queries4, keys_block, scale) - log_total[..., None]).astype(
            jnp.bfloat16
        )
        return running + jnp.einsum(
            "sgqk,skgd->sqgd", weights, values_block, preferred_element_type=jnp.float32
        )

    attended = lax.fori_loop(
        0, turns, accumulate, jnp.zeros((seqs_here, query_rows, groups, head_size), jnp.float32)
    )
    return (attended, log_total)


def attend_backward(queries4, keys_all, values_all, grad_out4, log_total, along, key_rows, scale):
    seqs_here, query_rows, groups, head_size = queries4.shape
    length = keys_all.shape[1]
    width_group = groups * head_size
    turns = length // key_rows

    def step_back(turn, carry):
        grad_queries, grad_keys, grad_values = carry
        keys_block = lax.dynamic_slice_in_dim(keys_all, turn * key_rows, key_rows, 1)
        keys4 = keys_block.reshape(seqs_here, key_rows, groups, head_size)
        values4 = lax.dynamic_slice_in_dim(values_all, turn * key_rows, key_rows, 1).reshape(
            seqs_here, key_rows, groups, head_size
        )
        weights = jnp.exp(block_scores(queries4, keys_block, scale) - log_total[..., None])
        grad_weights = jnp.einsum(
            "sqgd,skgd->sgqk", grad_out4, values4, preferred_element_type=jnp.float32
        )
        grad_scores = (weights * (grad_weights - along[..., None])).astype(jnp.bfloat16)
        grad_queries = grad_queries + jnp.einsum(
            "sgqk,skgd->sqgd", grad_scores, keys4, preferred_element_type=jnp.float32
        )
        key_part = (
            jnp.einsum("sgqk,sqgd->skgd", grad_scores, queries4, preferred_element_type=jnp.float32)
            * scale
        )
        value_part = jnp.einsum(
            "sgqk,sqgd->skgd",
            weights.astype(jnp.bfloat16),
            grad_out4,
            preferred_element_type=jnp.float32,
        )
        grad_keys = lax.dynamic_update_slice_in_dim(
            grad_keys, key_part.reshape(seqs_here, key_rows, width_group), turn * key_rows, 1
        )
        grad_values = lax.dynamic_update_slice_in_dim(
            grad_values, value_part.reshape(seqs_here, key_rows, width_group), turn * key_rows, 1
        )
        return (grad_queries, grad_keys, grad_values)

    start = (
        jnp.zeros((seqs_here, query_rows, groups, head_size), jnp.float32),
        jnp.zeros((seqs_here, length, width_group), jnp.float32),
        jnp.zeros((seqs_here, length, width_group), jnp.float32),
    )
    grad_queries, grad_keys, grad_values = lax.fori_loop(0, turns, step_back, start)
    return (grad_queries * scale, grad_keys, grad_values)


def local_general(tokens, cotangent, w_qkv, w_attn_out, w_in, w_mlp_out, norm_gain1, norm_gain2):
    seqs_here, block_rows, width = tokens.shape
    count_rows = seqs_here * block_rows
    heads_all = width // HD
    head_devices = lax.axis_size("head")
    group_devices = lax.axis_size(("dp", "ctx"))
    groups = heads_all // head_devices
    width_group = groups * HD
    scale = HD ** (-0.5)
    ff_width = w_in.shape[1] // 2
    full_qkv, full_out, full_in, full_mlp, gain_one, gain_two = (
        lax.all_gather(w_qkv, ("dp", "ctx"), axis=0, tiled=True),
        lax.all_gather(w_attn_out, ("dp", "ctx"), axis=0, tiled=True),
        lax.all_gather(w_in, ("dp", "ctx"), axis=0, tiled=True),
        lax.all_gather(w_mlp_out, ("dp", "ctx"), axis=0, tiled=True),
        lax.all_gather(norm_gain1, ("dp", "ctx"), axis=0, tiled=True),
        lax.all_gather(norm_gain2, ("dp", "ctx"), axis=0, tiled=True),
    )
    x_in = tokens.astype(jnp.float32).reshape(count_rows, width)
    normed1, factor1 = normalize(x_in)
    lowered1 = (normed1 * gain_one.astype(jnp.float32)).astype(jnp.bfloat16)
    projected = jnp.dot(lowered1, full_qkv, preferred_element_type=jnp.float32).reshape(
        seqs_here, block_rows, 3, heads_all, HD
    )
    first_pos = (lax.axis_index("ctx") * head_devices + lax.axis_index("head")) * block_rows
    positions = (first_pos + jnp.arange(block_rows, dtype=jnp.int32)).astype(jnp.float32)
    cosine, sine_table = rope_tables(positions, HD // 2)
    queries = (
        rotate(projected[:, :, 0], cosine, sine_table, 1.0)
        .astype(jnp.bfloat16)
        .reshape(seqs_here, block_rows, width)
    )
    keys_local = (
        rotate(projected[:, :, 1], cosine, sine_table, 1.0)
        .astype(jnp.bfloat16)
        .reshape(seqs_here, block_rows, width)
    )
    values_local = projected[:, :, 2].astype(jnp.bfloat16).reshape(seqs_here, block_rows, width)
    queries_h, keys_h, values_h = (
        lax.all_to_all(queries, "head", split_axis=2, concat_axis=1, tiled=True),
        lax.all_to_all(keys_local, "head", split_axis=2, concat_axis=1, tiled=True),
        lax.all_to_all(values_local, "head", split_axis=2, concat_axis=1, tiled=True),
    )
    query_rows = queries_h.shape[1]
    queries4 = queries_h.reshape(seqs_here, query_rows, groups, HD)
    keys_all, values_all = (
        lax.all_gather(keys_h, "ctx", axis=1, tiled=True),
        lax.all_gather(values_h, "ctx", axis=1, tiled=True),
    )
    key_rows = math.gcd(keys_all.shape[1], 1024)
    attended, log_total = attend_forward(queries4, keys_all, values_all, key_rows, scale)
    attended_low = attended.astype(jnp.bfloat16).reshape(seqs_here, query_rows, width_group)
    back_rows = lax.all_to_all(
        attended_low, "head", split_axis=1, concat_axis=2, tiled=True
    ).reshape(count_rows, width)
    residual = x_in + jnp.dot(back_rows, full_out, preferred_element_type=jnp.float32)
    normed2, factor2 = normalize(residual)
    lowered2 = (normed2 * gain_two.astype(jnp.float32)).astype(jnp.bfloat16)
    lifted = jnp.dot(lowered2, full_in, preferred_element_type=jnp.float32)
    first_part = lifted[:, :ff_width]
    second_part = lifted[:, ff_width:]
    activated, gelu_pullback = jax.vjp(
        lambda entries: jax.nn.gelu(entries, approximate=False), first_part
    )
    mixed = (activated * second_part).astype(jnp.bfloat16)
    result = (residual + jnp.dot(mixed, full_mlp, preferred_element_type=jnp.float32)).astype(
        jnp.bfloat16
    )
    full_qkv, full_out, full_in, full_mlp, gain_one, gain_two = (
        lax.all_gather(w_qkv, ("dp", "ctx"), axis=0, tiled=True),
        lax.all_gather(w_attn_out, ("dp", "ctx"), axis=0, tiled=True),
        lax.all_gather(w_in, ("dp", "ctx"), axis=0, tiled=True),
        lax.all_gather(w_mlp_out, ("dp", "ctx"), axis=0, tiled=True),
        lax.all_gather(norm_gain1, ("dp", "ctx"), axis=0, tiled=True),
        lax.all_gather(norm_gain2, ("dp", "ctx"), axis=0, tiled=True),
    )
    keys_all, values_all = (
        lax.all_gather(keys_h, "ctx", axis=1, tiled=True),
        lax.all_gather(values_h, "ctx", axis=1, tiled=True),
    )
    grad_top = cotangent.reshape(count_rows, width)
    grad_mlp = jnp.einsum("nf,nd->fd", mixed, grad_top, preferred_element_type=jnp.float32)
    grad_mixed = jnp.einsum("nd,fd->nf", grad_top, full_mlp, preferred_element_type=jnp.float32)
    grad_first = gelu_pullback(grad_mixed * second_part)[0]
    grad_lifted = jnp.concatenate([grad_first, grad_mixed * activated], axis=-1).astype(
        jnp.bfloat16
    )
    grad_inner = jnp.einsum("nd,nf->df", lowered2, grad_lifted, preferred_element_type=jnp.float32)
    grad_lowered2 = jnp.einsum(
        "nf,df->nd", grad_lifted, full_in, preferred_element_type=jnp.float32
    )
    grad_two = jnp.sum(grad_lowered2 * normed2, axis=0)
    grad_residual = grad_top.astype(jnp.float32) + norm_back(
        grad_lowered2 * gain_two.astype(jnp.float32), normed2, factor2
    )
    grad_branch = grad_residual.astype(jnp.bfloat16)
    grad_outproj = jnp.einsum(
        "nd,ne->de", back_rows, grad_branch, preferred_element_type=jnp.float32
    )
    grad_attended = jnp.einsum(
        "ne,de->nd", grad_branch, full_out, preferred_element_type=jnp.float32
    ).astype(jnp.bfloat16)
    grad_attended_h = lax.all_to_all(
        grad_attended.reshape(seqs_here, block_rows, width),
        "head",
        split_axis=2,
        concat_axis=1,
        tiled=True,
    )
    grad_out4 = grad_attended_h.reshape(seqs_here, query_rows, groups, HD)
    along = jnp.transpose(jnp.sum(grad_out4.astype(jnp.float32) * attended, axis=-1), (0, 2, 1))
    grad_queries, grad_keys_all, grad_values_all = attend_backward(
        queries4, keys_all, values_all, grad_out4, log_total, along, key_rows, scale
    )
    grad_keys_sum, grad_values_sum = (
        lax.psum_scatter(
            grad_keys_all.astype(jnp.bfloat16), "ctx", scatter_dimension=1, tiled=True
        ).astype(jnp.float32),
        lax.psum_scatter(
            grad_values_all.astype(jnp.bfloat16), "ctx", scatter_dimension=1, tiled=True
        ).astype(jnp.float32),
    )
    grad_q_low = grad_queries.astype(jnp.bfloat16).reshape(seqs_here, query_rows, width_group)
    grad_q_tok, grad_k_tok, grad_v_tok = (
        lax.all_to_all(grad_q_low, "head", split_axis=1, concat_axis=2, tiled=True),
        lax.all_to_all(
            grad_keys_sum.astype(jnp.bfloat16), "head", split_axis=1, concat_axis=2, tiled=True
        ),
        lax.all_to_all(
            grad_values_sum.astype(jnp.bfloat16), "head", split_axis=1, concat_axis=2, tiled=True
        ),
    )
    unrot_q = rotate(
        grad_q_tok.astype(jnp.float32).reshape(seqs_here, block_rows, heads_all, HD),
        cosine,
        sine_table,
        -1.0,
    )
    unrot_k = rotate(
        grad_k_tok.astype(jnp.float32).reshape(seqs_here, block_rows, heads_all, HD),
        cosine,
        sine_table,
        -1.0,
    )
    grad_projected = jnp.concatenate(
        [
            unrot_q.reshape(count_rows, width),
            unrot_k.reshape(count_rows, width),
            grad_v_tok.astype(jnp.float32).reshape(count_rows, width),
        ],
        axis=-1,
    ).astype(jnp.bfloat16)
    grad_project = jnp.einsum(
        "nd,nf->df", lowered1, grad_projected, preferred_element_type=jnp.float32
    )
    grad_lowered1 = jnp.einsum(
        "nf,df->nd", grad_projected, full_qkv, preferred_element_type=jnp.float32
    )
    grad_one = jnp.sum(grad_lowered1 * normed1, axis=0)
    grad_input = grad_residual + norm_back(
        grad_lowered1 * gain_one.astype(jnp.float32), normed1, factor1
    )
    pieces_one = grad_one.reshape(group_devices, head_devices, -1)
    pieces_two = grad_two.reshape(group_devices, head_devices, -1)
    part_qkv, part_out, part_in, part_mlp, part_one, part_two = (
        lax.psum_scatter(
            grad_project.astype(jnp.bfloat16), ("dp", "ctx"), scatter_dimension=0, tiled=True
        ).astype(jnp.float32),
        lax.psum_scatter(
            grad_outproj.astype(jnp.bfloat16), ("dp", "ctx"), scatter_dimension=0, tiled=True
        ).astype(jnp.float32),
        lax.psum_scatter(
            grad_inner.astype(jnp.bfloat16), ("dp", "ctx"), scatter_dimension=0, tiled=True
        ).astype(jnp.float32),
        lax.psum_scatter(
            grad_mlp.astype(jnp.bfloat16), ("dp", "ctx"), scatter_dimension=0, tiled=True
        ).astype(jnp.float32),
        lax.psum_scatter(
            pieces_one.astype(jnp.bfloat16), ("dp", "ctx"), scatter_dimension=0, tiled=True
        ).astype(jnp.float32),
        lax.psum_scatter(
            pieces_two.astype(jnp.bfloat16), ("dp", "ctx"), scatter_dimension=0, tiled=True
        ).astype(jnp.float32),
    )
    final_qkv, final_out, final_in, final_mlp, final_one, final_two = (
        lax.psum_scatter(
            part_qkv.astype(jnp.bfloat16), "head", scatter_dimension=1, tiled=True
        ).astype(jnp.float32),
        lax.psum_scatter(
            part_out.astype(jnp.bfloat16), "head", scatter_dimension=1, tiled=True
        ).astype(jnp.float32),
        lax.psum_scatter(
            part_in.astype(jnp.bfloat16), "head", scatter_dimension=1, tiled=True
        ).astype(jnp.float32),
        lax.psum_scatter(
            part_mlp.astype(jnp.bfloat16), "head", scatter_dimension=1, tiled=True
        ).astype(jnp.float32),
        lax.psum_scatter(
            part_one.astype(jnp.bfloat16), "head", scatter_dimension=1, tiled=True
        ).astype(jnp.float32),
        lax.psum_scatter(
            part_two.astype(jnp.bfloat16), "head", scatter_dimension=1, tiled=True
        ).astype(jnp.float32),
    )
    return (
        result.reshape(seqs_here, block_rows, width),
        grad_input.reshape(seqs_here, block_rows, width),
        final_qkv,
        final_out,
        final_in,
        final_mlp,
        final_one.reshape(-1),
        final_two.reshape(-1),
    )


F32 = jnp.float32
BF16 = jnp.bfloat16
VMEM_BYTES = 56 * 1024 * 1024


def dot(left, right, dims=((1,), (0,))):
    return lax.dot_general(left, right, (dims, ((), ())), preferred_element_type=F32)


def lane_rotate(values, cosine, sine_signed):
    lane = lax.broadcasted_iota(jnp.int32, values.shape, 1)
    width = values.shape[1]
    partner = jnp.where(
        lane % HD < HD // 2,
        pltpu.roll(values, width - HD // 2, 1),
        pltpu.roll(values, HD // 2, 1),
    )
    return values * cosine + partner * sine_signed


def project_kernel(*refs):
    blocks = refs[:-6]
    gain_ref, w_ref, cos_ref, sin_ref, low_ref, qkv_ref = refs[-6:]
    rows = blocks[0].shape[0]
    for place, block in enumerate(blocks):
        normed, _ = normalize(block[...].astype(F32))
        low_ref[place * rows : (place + 1) * rows, :] = (normed * gain_ref[...]).astype(BF16)
    projected = dot(low_ref[...], w_ref[...])
    part = w_ref.shape[1] // 3
    cosine, sine = cos_ref[...], sin_ref[...]
    qkv_ref[:, :part] = (lane_rotate(projected[:, :part], cosine, sine) * HD**-0.5).astype(BF16)
    qkv_ref[:, part : 2 * part] = lane_rotate(
        projected[:, part : 2 * part], cosine, sine
    ).astype(BF16)
    qkv_ref[:, 2 * part :] = projected[:, 2 * part :].astype(BF16)


def project(blocks, gain, w, cosine, sine):
    tokens = len(blocks) * blocks[0].shape[0]
    return pl.pallas_call(
        project_kernel,
        out_shape=(
            jax.ShapeDtypeStruct((tokens, w.shape[0]), BF16),
            jax.ShapeDtypeStruct((tokens, w.shape[1]), BF16),
        ),
        compiler_params=pltpu.CompilerParams(vmem_limit_bytes=VMEM_BYTES),
        name="project",
    )(*blocks, gain, w, cosine, sine)


def head_masks(shape):
    lane = lax.broadcasted_iota(jnp.int32, shape, 1)
    return [lane // HD == head for head in range(shape[1] // HD)]


def attend_kernel(q_ref, k_ref, v_ref, w_ref, att_ref, low_ref, log_ref, even_ref, odd_ref):
    queries = q_ref[...]
    keys, values = k_ref[...], v_ref[...]
    attended = jnp.zeros(queries.shape, F32)
    logs = jnp.zeros(queries.shape, F32)
    for mask in head_masks(queries.shape):
        scores = dot(jnp.where(mask, queries, 0), keys, ((1,), (1,)))
        peak = jnp.max(scores, axis=1, keepdims=True)
        weights = jnp.exp(scores - peak)
        total = jnp.sum(weights, axis=1, keepdims=True)
        mixed = dot(weights.astype(BF16), values) * (1.0 / total)
        attended = jnp.where(mask, mixed, attended)
        logs = jnp.where(mask, peak + jnp.log(total), logs)
    att_ref[...] = attended
    log_ref[...] = logs
    low = attended.astype(BF16)
    low_ref[...] = low
    half = queries.shape[0] // 2
    part = dot(low, w_ref[...]).astype(BF16)
    even_ref[0] = part[:half]
    odd_ref[0] = part[half:]


def attend(qkv, w, block):
    tokens, width = qkv.shape[0], qkv.shape[1] // 3
    steps = tokens // (2 * block)
    rows = pl.BlockSpec((2 * block, width), lambda i: (i, 0))
    part = pl.BlockSpec((1, block, w.shape[1]), lambda i: (i, 0, 0))
    part_shape = jax.ShapeDtypeStruct((steps, block, w.shape[1]), BF16)
    return pl.pallas_call(
        attend_kernel,
        grid=(steps,),
        in_specs=[
            rows,
            pl.BlockSpec((tokens, width), lambda i: (0, 1)),
            pl.BlockSpec((tokens, width), lambda i: (0, 2)),
            pl.BlockSpec(w.shape, lambda i: (0, 0)),
        ],
        out_specs=(rows, rows, rows, part, part),
        out_shape=(
            jax.ShapeDtypeStruct((tokens, width), F32),
            jax.ShapeDtypeStruct((tokens, width), BF16),
            jax.ShapeDtypeStruct((tokens, width), F32),
            part_shape,
            part_shape,
        ),
        compiler_params=pltpu.CompilerParams(vmem_limit_bytes=VMEM_BYTES),
        name="attend",
    )(qkv, qkv, qkv, w)


def attend_back_kernel(
    q_ref, k_ref, v_ref, grad_ref, att_ref, log_ref, cosq_ref, sinq_ref, cos_ref, sin_ref,
    gq_ref, gk_ref, gv_ref, sum_k, sum_v,
):
    step = pl.program_id(0)

    @pl.when(step == 0)
    def _():
        sum_k[...] = jnp.zeros_like(sum_k)
        sum_v[...] = jnp.zeros_like(sum_v)

    queries, grads = q_ref[...], grad_ref[...]
    keys, values = k_ref[...], v_ref[...]
    along = (grads.astype(F32) * att_ref[...]).T
    logs = log_ref[...].T
    grad_queries = jnp.zeros(queries.shape, F32)
    for head, mask in enumerate(head_masks(queries.shape)):
        own_q = jnp.where(mask, queries, 0)
        own_g = jnp.where(mask, grads, 0)
        scores = dot(keys, own_q, ((1,), (1,)))
        weights = jnp.exp(scores - logs[head * HD : head * HD + 1])
        lifted = dot(values, own_g, ((1,), (1,)))
        row = jnp.sum(along[head * HD : (head + 1) * HD], axis=0, keepdims=True)
        grad_scores = (weights * (lifted - row)).astype(BF16)
        sum_k[...] += dot(grad_scores, own_q)
        sum_v[...] += dot(weights.astype(BF16), own_g)
        grad_queries = jnp.where(mask, dot(grad_scores, keys, ((0,), (0,))), grad_queries)
    gq_ref[...] = lane_rotate(grad_queries * HD**-0.5, cosq_ref[...], -sinq_ref[...]).astype(BF16)

    @pl.when(step == pl.num_programs(0) - 1)
    def _():
        gk_ref[...] = lane_rotate(sum_k[...], cos_ref[...], -sin_ref[...]).astype(BF16)
        gv_ref[...] = sum_v[...].astype(BF16)


def attend_back(qkv, grads, attended, logs, cosine, sine, query_rows):
    tokens, width = qkv.shape[0], qkv.shape[1] // 3
    rows = pl.BlockSpec((query_rows, width), lambda i: (i, 0))
    whole = pl.BlockSpec((tokens, width), lambda i: (0, 0))
    shape = jax.ShapeDtypeStruct((tokens, width), BF16)
    return pl.pallas_call(
        attend_back_kernel,
        grid=(tokens // query_rows,),
        in_specs=[
            rows,
            pl.BlockSpec((tokens, width), lambda i: (0, 1)),
            pl.BlockSpec((tokens, width), lambda i: (0, 2)),
            rows,
            rows,
            rows,
            rows,
            rows,
            whole,
            whole,
        ],
        out_specs=(rows, whole, whole),
        out_shape=(shape, shape, shape),
        scratch_shapes=[pltpu.VMEM((tokens, width), F32), pltpu.VMEM((tokens, width), F32)],
        compiler_params=pltpu.CompilerParams(vmem_limit_bytes=VMEM_BYTES),
        name="attend_back",
    )(qkv, qkv, qkv, grads, attended, logs, cosine, sine, cosine, sine)


class Group:
    def __init__(self):
        self.heads = lax.axis_size("head")
        self.dp = lax.axis_size("dp")
        self.ctx_at = lax.axis_index("ctx")
        self.head_at = lax.axis_index("head")
        self.dp_at = lax.axis_index("dp")

    def swap(self, values, bit):
        if bit == 4:
            return lax.ppermute(values, "ctx", [(0, 1), (1, 0)])
        return lax.ppermute(values, "head", [(i, i ^ bit) for i in range(self.heads)])

    def gather(self, own, first, second):
        blocks = {0: own, first: self.swap(own, first), second: self.swap(own, second)}
        blocks[6] = self.swap(blocks[first], second)
        for place in (0, 2, 4, 6):
            blocks[place + 1] = self.swap(blocks[place], 1)
        return [blocks[place] for place in range(8)]

    def reduce(self, even, odd, first, second):
        met = even.astype(F32) + self.swap(odd, 1).astype(F32)
        at = {2 * place: met[place] for place in range(4)}
        other = first ^ second
        far = self.swap(at[other].astype(BF16), first)
        near = self.swap(at[first].astype(BF16), first)
        last = self.swap((at[second] + far.astype(F32)).astype(BF16), second)
        return at[0] + near.astype(F32) + last.astype(F32)

    def rows_in(self, values, place):
        pairs = [
            (place[h] * self.heads + d, d * self.heads + h)
            for d in range(self.dp)
            for h in range(self.heads)
        ]
        return lax.ppermute(values, ("dp", "head"), pairs)

    def rows_back(self, values, place):
        pairs = [
            (d * self.heads + h, place[h] * self.heads + d)
            for d in range(self.dp)
            for h in range(self.heads)
        ]
        return lax.ppermute(values, ("dp", "head"), pairs)

    def total(self, values):
        for bit in (1, 2, 4):
            values = values + self.swap(values, bit)
        step = 1
        while step < self.dp:
            values = values + lax.ppermute(
                values, "dp", [(i, i ^ step) for i in range(self.dp)]
            )
            step *= 2
        return values


def table(choices, index):
    return jnp.asarray(choices, jnp.int32)[index]


def pick(array, index, axis):
    return lax.dynamic_index_in_dim(array, index, axis, keepdims=False)


def split_places(partial):
    rows = partial.shape[0] // 8
    blocks = partial.astype(BF16).reshape(4, 2, rows, partial.shape[1])
    return blocks[:, 0], blocks[:, 1]


def local_split(tokens, cotangent, w_qkv, w_attn_out, w_in, w_mlp_out, norm_gain1, norm_gain2):
    seqs, block, width = tokens.shape
    group = Group()
    heads, dp = group.heads, group.dp
    at_c, at_h = group.ctx_at, group.head_at
    parts = 2 * heads
    hidden = w_in.shape[1] // 2 // parts
    own_width = width // parts
    half = heads // 2
    place = [2 * h if h < half else 2 * (h - half) + 1 for h in range(heads)]
    straight = list(range(heads))
    way = [(4, 2) if s % 2 == 0 else (2, 4) for s in range(seqs)]

    x_blocks = [group.gather(tokens[s], *way[s]) for s in range(seqs)]

    gains = jnp.concatenate([norm_gain1, norm_gain2]).reshape(2, 1, -1)
    rows_here = w_qkv.shape[0]
    qkv_view = w_qkv.reshape(rows_here, 3, heads, 2, own_width)
    qkv_view = pick(qkv_view, at_h, 2)
    in_view = w_in.reshape(rows_here, 2, heads, 2, hidden)
    in_view = pick(in_view, table(place, at_h), 2)

    def in_order(own, other):
        return jnp.where(at_c == 0, jnp.stack([own, other]), jnp.stack([other, own]))

    def own_columns(view):
        own = pick(view, at_c, 2)
        other = group.swap(pick(view, 1 - at_c, 2), 4)
        return in_order(own, other)

    gain_rows = jnp.pad(
        gains.reshape(2, -1), ((0, 14), (0, 3 * own_width - rows_here))
    )
    qkv_pair = own_columns(qkv_view).reshape(2, rows_here, 3 * own_width)
    gain_pair = in_order(gain_rows, group.swap(gain_rows, 4))
    qkv_all = lax.all_gather(jnp.concatenate([qkv_pair, gain_pair], axis=1), "dp", axis=0)
    weight_qkv = qkv_all[:, :, :rows_here].reshape(width, 3 * own_width)
    gain_one = qkv_all[:, :, rows_here, :rows_here].reshape(1, width).astype(F32)
    gain_two = qkv_all[:, :, rows_here + 1, :rows_here].reshape(1, width).astype(F32)
    in_pair = jnp.moveaxis(own_columns(in_view), 2, 0)
    in_all = lax.all_gather(in_pair, "dp", axis=1)
    weight_first = in_all[0].reshape(width, hidden)
    weight_second = in_all[1].reshape(width, hidden)
    weight_out = group.rows_in(w_attn_out, straight)
    weight_mlp = group.rows_in(w_mlp_out, place)

    me = at_c * heads + at_h
    relative = jnp.arange(8 * block, dtype=jnp.int32)
    positions = ((relative // block) ^ me) * block + relative % block
    lane = jnp.arange(own_width, dtype=jnp.int32)
    frequency = jnp.exp(
        (lane % (HD // 2)).astype(F32) * (-math.log(ROPE_BASE) / (HD // 2))
    )
    angles = positions.astype(F32)[:, None] * frequency[None, :]
    cosine = jnp.cos(angles)
    sine = jnp.sin(angles) * jnp.where(lane % HD < HD // 2, -1.0, 1.0)[None, :]

    low1, qkv, att, att_low, logs, residual, back2 = [], [], [], [], [], [], []
    low2_all = []
    for s in range(seqs):
        low, rotated = project(x_blocks[s], gain_one, weight_qkv, cosine, sine)
        low1.append(low)
        qkv.append(rotated)
        attended, attended_low, log_total, even, odd = attend(rotated, weight_out, block)
        att.append(attended)
        att_low.append(attended_low)
        logs.append(log_total)
        branch = group.reduce(even, odd, *way[s])
        resid = tokens[s].astype(F32) + branch
        normed2, factor2 = normalize(resid)
        residual.append(resid)
        back2.append((normed2, factor2))
        low2_all.append(
            jnp.concatenate(group.gather((normed2 * gain_two).astype(BF16), *way[s]))
        )

    cot_all = [jnp.concatenate(group.gather(cotangent[s], *way[s])) for s in range(seqs)]

    results, grad_inputs = [], []
    mixed_all, first_all, second_all, branch_all, proj_all = [], [], [], [], []
    grad_res = []
    gain2_sum = 0.0
    for s in range(seqs):
        first = dot(low2_all[s], weight_first)
        second = dot(low2_all[s], weight_second)
        activated, pullback = jax.vjp(
            lambda entries: jax.nn.gelu(entries, approximate=False), first
        )
        mixed = (activated * second).astype(BF16)
        grad_mixed = dot(cot_all[s], weight_mlp, ((1,), (1,)))
        grad_first = pullback(grad_mixed * second)[0].astype(BF16)
        grad_second = (grad_mixed * activated).astype(BF16)
        mixed_all.append(mixed)
        first_all.append(grad_first)
        second_all.append(grad_second)
        partial = dot(grad_first, weight_first, ((1,), (1,))) + dot(
            grad_second, weight_second, ((1,), (1,))
        )
        grad_low2 = group.reduce(*split_places(partial), *way[s])
        normed2, factor2 = back2[s]
        gain2_sum = gain2_sum + jnp.sum(grad_low2 * normed2, axis=0)
        grad_residual = cotangent[s].astype(F32) + norm_back(
            grad_low2 * gain_two, normed2, factor2
        )
        grad_res.append(grad_residual)
        gathered = jnp.concatenate(group.gather(grad_residual.astype(BF16), *way[s]))
        branch_all.append(gathered)
        grad_att = dot(gathered, weight_out, ((1,), (1,))).astype(BF16)
        gq, gk, gv = attend_back(qkv[s], grad_att, att[s], logs[s], cosine, sine, 2 * block)
        proj = jnp.concatenate([gq, gk, gv], axis=1)
        proj_all.append(proj)
        grad_low1 = group.reduce(
            *split_places(dot(proj, weight_qkv, ((1,), (1,)))), *way[s]
        )
        normed1, factor1 = normalize(tokens[s].astype(F32))
        grad_inputs.append(
            grad_residual + norm_back(grad_low1 * gain_one, normed1, factor1)
        )
        out_sum = group.reduce(*split_places(dot(mixed, weight_mlp)), *way[s])
        results.append((residual[s] + out_sum).astype(BF16))

    def over_tokens(left, right):
        return sum(dot(a, b, ((0,), (0,))) for a, b in zip(left, right))

    def scatter(values, axis):
        return lax.psum_scatter(values.astype(BF16), "dp", scatter_dimension=axis, tiled=True)

    def columns_first(values):
        return jnp.moveaxis(values.reshape(values.shape[0], dp, -1), 1, 0)

    grad_mlp = scatter(columns_first(over_tokens(mixed_all, cot_all)), 0)[0]
    grad_mlp = group.rows_back(grad_mlp, place).astype(F32)
    grad_out = scatter(columns_first(over_tokens(att_low, branch_all)), 0)[0]
    grad_out = group.rows_back(grad_out, straight).astype(F32)

    def rows_here_of(values):
        pair = values.reshape(2, rows_here, -1)
        own = pick(pair, at_c, 0)
        other = group.swap(pick(pair, 1 - at_c, 0), 4)
        return in_order(own, other)

    grad_in = scatter(
        jnp.stack([over_tokens(low2_all, first_all), over_tokens(low2_all, second_all)]), 1
    )
    grad_in = jnp.stack([rows_here_of(grad_in[0]), rows_here_of(grad_in[1])])
    keep = (at_h >= half).astype(jnp.int32)
    stays = pick(grad_in, keep, 0)
    comes = group.swap(pick(grad_in, 1 - keep, 0), half)
    grad_in = jnp.where(
        keep == 0, jnp.concatenate([stays, comes]), jnp.concatenate([comes, stays])
    )
    grad_in = jnp.moveaxis(grad_in, 0, 1).reshape(rows_here, -1).astype(F32)

    grad_qkv = over_tokens(low1, proj_all)
    gain1_sum = jnp.sum(grad_qkv * weight_qkv.astype(F32), axis=1) / gain_one[0]
    sums = group.total(jnp.stack([gain1_sum, gain2_sum]).reshape(-1, 128))
    sums = sums.reshape(2, -1)
    per_device = width // (dp * parts)
    start = ((group.dp_at * 2 + at_c) * heads + at_h) * per_device
    grad_gain1, grad_gain2 = (
        lax.dynamic_slice_in_dim(sums[i], start, per_device, 0) for i in range(2)
    )
    grad_qkv = rows_here_of(scatter(grad_qkv, 0)).reshape(2, rows_here, 3, own_width)
    grad_qkv = jnp.moveaxis(grad_qkv, 2, 0)
    stays = pick(grad_qkv, table([0, 1, 1, 2], at_h), 0)
    core = group.swap(pick(grad_qkv, table([1, 0, 2, 1], at_h), 0), 1)
    chip = group.swap(pick(grad_qkv, table([2, 2, 0, 0], at_h), 0), 2)
    grad_qkv = jnp.where(
        at_h % 2 == 0, jnp.concatenate([stays, core, chip]), jnp.concatenate([chip, core, stays])
    )
    grad_qkv = jnp.moveaxis(grad_qkv, 0, 1).reshape(rows_here, -1).astype(F32)

    return (
        jnp.stack(results),
        jnp.stack(grad_inputs),
        grad_qkv,
        grad_out,
        grad_in,
        grad_mlp,
        grad_gain1,
        grad_gain2,
    )


def local(tokens, cotangent, w_qkv, w_attn_out, w_in, w_mlp_out, norm_gain1, norm_gain2):
    args = (tokens, cotangent, w_qkv, w_attn_out, w_in, w_mlp_out, norm_gain1, norm_gain2)
    sizes = [lax.axis_size(axis) for axis in ("dp", "ctx", "head")]
    if sizes == [4, 2, 4] and tokens.shape[2] == 8 * 2 * HD and tokens.shape[1] % 16 == 0:
        return local_split(*args)
    return local_general(*args)


def solution(mesh):
    in_specs = (
        P("dp", ("ctx", "head"), None),
        P("dp", ("ctx", "head"), None),
        P(("dp", "ctx"), None),
        P(("dp", "ctx"), None),
        P(("dp", "ctx"), None),
        P(("dp", "ctx"), None),
        P(("dp", "ctx")),
        P(("dp", "ctx")),
    )
    out_specs = (
        P("dp", ("ctx", "head"), None),
        P("dp", ("ctx", "head"), None),
        P(("dp", "ctx"), "head"),
        P(("dp", "ctx"), "head"),
        P(("dp", "ctx"), "head"),
        P(("dp", "ctx"), "head"),
        P(("dp", "ctx", "head")),
        P(("dp", "ctx", "head")),
    )
    return jax.shard_map(local, mesh=mesh, in_specs=in_specs, out_specs=out_specs, check_vma=False)
```

```python
import math

import jax
import jax.numpy as jnp
from jax import lax
from jax.experimental import pallas as pl
from jax.experimental.pallas import tpu as pltpu
from jax.sharding import PartitionSpec as P

HD = 64


EPSILON = 1e-05
ROPE_BASE = 160000.0


def normalize(values):
    centre = jnp.mean(values, axis=-1, keepdims=True)
    shifted = values - centre
    spread = jnp.mean(shifted * shifted, axis=-1, keepdims=True)
    factor = lax.rsqrt(spread + EPSILON)
    return (shifted * factor, factor)


def norm_back(grad_normed, normed, factor):
    grad_centre = jnp.mean(grad_normed, axis=-1, keepdims=True)
    grad_along = jnp.mean(grad_normed * normed, axis=-1, keepdims=True)
    return (grad_normed - grad_centre - normed * grad_along) * factor


def rope_tables(positions, half_size):
    frequency = jnp.exp(
        jnp.arange(half_size, dtype=jnp.float32) * (-math.log(ROPE_BASE) / half_size)
    )
    angles = positions[:, None] * frequency[None, :]
    return (jnp.cos(angles), jnp.sin(angles))


def rotate(values, cosine, sine_table, direction):
    half_size = cosine.shape[-1]
    first_half = values[..., :half_size]
    second_half = values[..., half_size:]
    cos_part = cosine[:, None, :]
    sin_part = sine_table[:, None, :] * direction
    return jnp.concatenate(
        [
            first_half * cos_part - second_half * sin_part,
            second_half * cos_part + first_half * sin_part,
        ],
        axis=-1,
    )


def block_scores(queries4, keys_block, scale):
    keys4 = keys_block.reshape(
        keys_block.shape[0], keys_block.shape[1], queries4.shape[2], queries4.shape[3]
    )
    return (
        jnp.einsum("sqgd,skgd->sgqk", queries4, keys4, preferred_element_type=jnp.float32) * scale
    )


def attend_forward(queries4, keys_all, values_all, key_rows, scale):
    seqs_here, query_rows, groups, head_size = queries4.shape
    turns = keys_all.shape[1] // key_rows

    def statistics(turn, carry):
        row_peak, row_total = carry
        keys_block = lax.dynamic_slice_in_dim(keys_all, turn * key_rows, key_rows, 1)
        scores = block_scores(queries4, keys_block, scale)
        new_peak = jnp.maximum(row_peak, jnp.max(scores, axis=-1))
        row_total = row_total * jnp.exp(row_peak - new_peak) + jnp.sum(
            jnp.exp(scores - new_peak[..., None]), axis=-1
        )
        return (new_peak, row_total)

    start_peak = jnp.full((seqs_here, groups, query_rows), -1e30, jnp.float32)
    row_peak, row_total = lax.fori_loop(
        0, turns, statistics, (start_peak, jnp.zeros_like(start_peak))
    )
    log_total = row_peak + jnp.log(row_total)

    def accumulate(turn, running):
        keys_block = lax.dynamic_slice_in_dim(keys_all, turn * key_rows, key_rows, 1)
        values_block = lax.dynamic_slice_in_dim(values_all, turn * key_rows, key_rows, 1).reshape(
            seqs_here, key_rows, groups, head_size
        )
        weights = jnp.exp(block_scores(queries4, keys_block, scale) - log_total[..., None]).astype(
            jnp.bfloat16
        )
        return running + jnp.einsum(
            "sgqk,skgd->sqgd", weights, values_block, preferred_element_type=jnp.float32
        )

    attended = lax.fori_loop(
        0, turns, accumulate, jnp.zeros((seqs_here, query_rows, groups, head_size), jnp.float32)
    )
    return (attended, log_total)


def attend_backward(queries4, keys_all, values_all, grad_out4, log_total, along, key_rows, scale):
    seqs_here, query_rows, groups, head_size = queries4.shape
    length = keys_all.shape[1]
    width_group = groups * head_size
    turns = length // key_rows

    def step_back(turn, carry):
        grad_queries, grad_keys, grad_values = carry
        keys_block = lax.dynamic_slice_in_dim(keys_all, turn * key_rows, key_rows, 1)
        keys4 = keys_block.reshape(seqs_here, key_rows, groups, head_size)
        values4 = lax.dynamic_slice_in_dim(values_all, turn * key_rows, key_rows, 1).reshape(
            seqs_here, key_rows, groups, head_size
        )
        weights = jnp.exp(block_scores(queries4, keys_block, scale) - log_total[..., None])
        grad_weights = jnp.einsum(
            "sqgd,skgd->sgqk", grad_out4, values4, preferred_element_type=jnp.float32
        )
        grad_scores = (weights * (grad_weights - along[..., None])).astype(jnp.bfloat16)
        grad_queries = grad_queries + jnp.einsum(
            "sgqk,skgd->sqgd", grad_scores, keys4, preferred_element_type=jnp.float32
        )
        key_part = (
            jnp.einsum("sgqk,sqgd->skgd", grad_scores, queries4, preferred_element_type=jnp.float32)
            * scale
        )
        value_part = jnp.einsum(
            "sgqk,sqgd->skgd",
            weights.astype(jnp.bfloat16),
            grad_out4,
            preferred_element_type=jnp.float32,
        )
        grad_keys = lax.dynamic_update_slice_in_dim(
            grad_keys, key_part.reshape(seqs_here, key_rows, width_group), turn * key_rows, 1
        )
        grad_values = lax.dynamic_update_slice_in_dim(
            grad_values, value_part.reshape(seqs_here, key_rows, width_group), turn * key_rows, 1
        )
        return (grad_queries, grad_keys, grad_values)

    start = (
        jnp.zeros((seqs_here, query_rows, groups, head_size), jnp.float32),
        jnp.zeros((seqs_here, length, width_group), jnp.float32),
        jnp.zeros((seqs_here, length, width_group), jnp.float32),
    )
    grad_queries, grad_keys, grad_values = lax.fori_loop(0, turns, step_back, start)
    return (grad_queries * scale, grad_keys, grad_values)


def local_general(tokens, cotangent, w_qkv, w_attn_out, w_in, w_mlp_out, norm_gain1, norm_gain2):
    seqs_here, block_rows, width = tokens.shape
    count_rows = seqs_here * block_rows
    heads_all = width // HD
    head_devices = lax.axis_size("head")
    group_devices = lax.axis_size(("dp", "ctx"))
    groups = heads_all // head_devices
    width_group = groups * HD
    scale = HD ** (-0.5)
    ff_width = w_in.shape[1] // 2
    full_qkv, full_out, full_in, full_mlp, gain_one, gain_two = (
        lax.all_gather(w_qkv, ("dp", "ctx"), axis=0, tiled=True),
        lax.all_gather(w_attn_out, ("dp", "ctx"), axis=0, tiled=True),
        lax.all_gather(w_in, ("dp", "ctx"), axis=0, tiled=True),
        lax.all_gather(w_mlp_out, ("dp", "ctx"), axis=0, tiled=True),
        lax.all_gather(norm_gain1, ("dp", "ctx"), axis=0, tiled=True),
        lax.all_gather(norm_gain2, ("dp", "ctx"), axis=0, tiled=True),
    )
    x_in = tokens.astype(jnp.float32).reshape(count_rows, width)
    normed1, factor1 = normalize(x_in)
    lowered1 = (normed1 * gain_one.astype(jnp.float32)).astype(jnp.bfloat16)
    projected = jnp.dot(lowered1, full_qkv, preferred_element_type=jnp.float32).reshape(
        seqs_here, block_rows, 3, heads_all, HD
    )
    first_pos = (lax.axis_index("ctx") * head_devices + lax.axis_index("head")) * block_rows
    positions = (first_pos + jnp.arange(block_rows, dtype=jnp.int32)).astype(jnp.float32)
    cosine, sine_table = rope_tables(positions, HD // 2)
    queries = (
        rotate(projected[:, :, 0], cosine, sine_table, 1.0)
        .astype(jnp.bfloat16)
        .reshape(seqs_here, block_rows, width)
    )
    keys_local = (
        rotate(projected[:, :, 1], cosine, sine_table, 1.0)
        .astype(jnp.bfloat16)
        .reshape(seqs_here, block_rows, width)
    )
    values_local = projected[:, :, 2].astype(jnp.bfloat16).reshape(seqs_here, block_rows, width)
    queries_h, keys_h, values_h = (
        lax.all_to_all(queries, "head", split_axis=2, concat_axis=1, tiled=True),
        lax.all_to_all(keys_local, "head", split_axis=2, concat_axis=1, tiled=True),
        lax.all_to_all(values_local, "head", split_axis=2, concat_axis=1, tiled=True),
    )
    query_rows = queries_h.shape[1]
    queries4 = queries_h.reshape(seqs_here, query_rows, groups, HD)
    keys_all, values_all = (
        lax.all_gather(keys_h, "ctx", axis=1, tiled=True),
        lax.all_gather(values_h, "ctx", axis=1, tiled=True),
    )
    key_rows = math.gcd(keys_all.shape[1], 1024)
    attended, log_total = attend_forward(queries4, keys_all, values_all, key_rows, scale)
    attended_low = attended.astype(jnp.bfloat16).reshape(seqs_here, query_rows, width_group)
    back_rows = lax.all_to_all(
        attended_low, "head", split_axis=1, concat_axis=2, tiled=True
    ).reshape(count_rows, width)
    residual = x_in + jnp.dot(back_rows, full_out, preferred_element_type=jnp.float32)
    normed2, factor2 = normalize(residual)
    lowered2 = (normed2 * gain_two.astype(jnp.float32)).astype(jnp.bfloat16)
    lifted = jnp.dot(lowered2, full_in, preferred_element_type=jnp.float32)
    first_part = lifted[:, :ff_width]
    second_part = lifted[:, ff_width:]
    activated, gelu_pullback = jax.vjp(
        lambda entries: jax.nn.gelu(entries, approximate=False), first_part
    )
    mixed = (activated * second_part).astype(jnp.bfloat16)
    result = (residual + jnp.dot(mixed, full_mlp, preferred_element_type=jnp.float32)).astype(
        jnp.bfloat16
    )
    full_qkv, full_out, full_in, full_mlp, gain_one, gain_two = (
        lax.all_gather(w_qkv, ("dp", "ctx"), axis=0, tiled=True),
        lax.all_gather(w_attn_out, ("dp", "ctx"), axis=0, tiled=True),
        lax.all_gather(w_in, ("dp", "ctx"), axis=0, tiled=True),
        lax.all_gather(w_mlp_out, ("dp", "ctx"), axis=0, tiled=True),
        lax.all_gather(norm_gain1, ("dp", "ctx"), axis=0, tiled=True),
        lax.all_gather(norm_gain2, ("dp", "ctx"), axis=0, tiled=True),
    )
    keys_all, values_all = (
        lax.all_gather(keys_h, "ctx", axis=1, tiled=True),
        lax.all_gather(values_h, "ctx", axis=1, tiled=True),
    )
    grad_top = cotangent.reshape(count_rows, width)
    grad_mlp = jnp.einsum("nf,nd->fd", mixed, grad_top, preferred_element_type=jnp.float32)
    grad_mixed = jnp.einsum("nd,fd->nf", grad_top, full_mlp, preferred_element_type=jnp.float32)
    grad_first = gelu_pullback(grad_mixed * second_part)[0]
    grad_lifted = jnp.concatenate([grad_first, grad_mixed * activated], axis=-1).astype(
        jnp.bfloat16
    )
    grad_inner = jnp.einsum("nd,nf->df", lowered2, grad_lifted, preferred_element_type=jnp.float32)
    grad_lowered2 = jnp.einsum(
        "nf,df->nd", grad_lifted, full_in, preferred_element_type=jnp.float32
    )
    grad_two = jnp.sum(grad_lowered2 * normed2, axis=0)
    grad_residual = grad_top.astype(jnp.float32) + norm_back(
        grad_lowered2 * gain_two.astype(jnp.float32), normed2, factor2
    )
    grad_branch = grad_residual.astype(jnp.bfloat16)
    grad_outproj = jnp.einsum(
        "nd,ne->de", back_rows, grad_branch, preferred_element_type=jnp.float32
    )
    grad_attended = jnp.einsum(
        "ne,de->nd", grad_branch, full_out, preferred_element_type=jnp.float32
    ).astype(jnp.bfloat16)
    grad_attended_h = lax.all_to_all(
        grad_attended.reshape(seqs_here, block_rows, width),
        "head",
        split_axis=2,
        concat_axis=1,
        tiled=True,
    )
    grad_out4 = grad_attended_h.reshape(seqs_here, query_rows, groups, HD)
    along = jnp.transpose(jnp.sum(grad_out4.astype(jnp.float32) * attended, axis=-1), (0, 2, 1))
    grad_queries, grad_keys_all, grad_values_all = attend_backward(
        queries4, keys_all, values_all, grad_out4, log_total, along, key_rows, scale
    )
    grad_keys_sum, grad_values_sum = (
        lax.psum_scatter(
            grad_keys_all.astype(jnp.bfloat16), "ctx", scatter_dimension=1, tiled=True
        ).astype(jnp.float32),
        lax.psum_scatter(
            grad_values_all.astype(jnp.bfloat16), "ctx", scatter_dimension=1, tiled=True
        ).astype(jnp.float32),
    )
    grad_q_low = grad_queries.astype(jnp.bfloat16).reshape(seqs_here, query_rows, width_group)
    grad_q_tok, grad_k_tok, grad_v_tok = (
        lax.all_to_all(grad_q_low, "head", split_axis=1, concat_axis=2, tiled=True),
        lax.all_to_all(
            grad_keys_sum.astype(jnp.bfloat16), "head", split_axis=1, concat_axis=2, tiled=True
        ),
        lax.all_to_all(
            grad_values_sum.astype(jnp.bfloat16), "head", split_axis=1, concat_axis=2, tiled=True
        ),
    )
    unrot_q = rotate(
        grad_q_tok.astype(jnp.float32).reshape(seqs_here, block_rows, heads_all, HD),
        cosine,
        sine_table,
        -1.0,
    )
    unrot_k = rotate(
        grad_k_tok.astype(jnp.float32).reshape(seqs_here, block_rows, heads_all, HD),
        cosine,
        sine_table,
        -1.0,
    )
    grad_projected = jnp.concatenate(
        [
            unrot_q.reshape(count_rows, width),
            unrot_k.reshape(count_rows, width),
            grad_v_tok.astype(jnp.float32).reshape(count_rows, width),
        ],
        axis=-1,
    ).astype(jnp.bfloat16)
    grad_project = jnp.einsum(
        "nd,nf->df", lowered1, grad_projected, preferred_element_type=jnp.float32
    )
    grad_lowered1 = jnp.einsum(
        "nf,df->nd", grad_projected, full_qkv, preferred_element_type=jnp.float32
    )
    grad_one = jnp.sum(grad_lowered1 * normed1, axis=0)
    grad_input = grad_residual + norm_back(
        grad_lowered1 * gain_one.astype(jnp.float32), normed1, factor1
    )
    pieces_one = grad_one.reshape(group_devices, head_devices, -1)
    pieces_two = grad_two.reshape(group_devices, head_devices, -1)
    part_qkv, part_out, part_in, part_mlp, part_one, part_two = (
        lax.psum_scatter(
            grad_project.astype(jnp.bfloat16), ("dp", "ctx"), scatter_dimension=0, tiled=True
        ).astype(jnp.float32),
        lax.psum_scatter(
            grad_outproj.astype(jnp.bfloat16), ("dp", "ctx"), scatter_dimension=0, tiled=True
        ).astype(jnp.float32),
        lax.psum_scatter(
            grad_inner.astype(jnp.bfloat16), ("dp", "ctx"), scatter_dimension=0, tiled=True
        ).astype(jnp.float32),
        lax.psum_scatter(
            grad_mlp.astype(jnp.bfloat16), ("dp", "ctx"), scatter_dimension=0, tiled=True
        ).astype(jnp.float32),
        lax.psum_scatter(
            pieces_one.astype(jnp.bfloat16), ("dp", "ctx"), scatter_dimension=0, tiled=True
        ).astype(jnp.float32),
        lax.psum_scatter(
            pieces_two.astype(jnp.bfloat16), ("dp", "ctx"), scatter_dimension=0, tiled=True
        ).astype(jnp.float32),
    )
    final_qkv, final_out, final_in, final_mlp, final_one, final_two = (
        lax.psum_scatter(
            part_qkv.astype(jnp.bfloat16), "head", scatter_dimension=1, tiled=True
        ).astype(jnp.float32),
        lax.psum_scatter(
            part_out.astype(jnp.bfloat16), "head", scatter_dimension=1, tiled=True
        ).astype(jnp.float32),
        lax.psum_scatter(
            part_in.astype(jnp.bfloat16), "head", scatter_dimension=1, tiled=True
        ).astype(jnp.float32),
        lax.psum_scatter(
            part_mlp.astype(jnp.bfloat16), "head", scatter_dimension=1, tiled=True
        ).astype(jnp.float32),
        lax.psum_scatter(
            part_one.astype(jnp.bfloat16), "head", scatter_dimension=1, tiled=True
        ).astype(jnp.float32),
        lax.psum_scatter(
            part_two.astype(jnp.bfloat16), "head", scatter_dimension=1, tiled=True
        ).astype(jnp.float32),
    )
    return (
        result.reshape(seqs_here, block_rows, width),
        grad_input.reshape(seqs_here, block_rows, width),
        final_qkv,
        final_out,
        final_in,
        final_mlp,
        final_one.reshape(-1),
        final_two.reshape(-1),
    )


F32 = jnp.float32
BF16 = jnp.bfloat16
VMEM_BYTES = 56 * 1024 * 1024
GROUP = ("ctx", "head")


def dot(left, right, dims=((1,), (0,))):
    return lax.dot_general(left, right, (dims, ((), ())), preferred_element_type=F32)


def flat(values):
    return values.reshape(-1, values.shape[-1])


def lane_rotate(values, cosine, sine_signed):
    lane = lax.broadcasted_iota(jnp.int32, values.shape, 1)
    width = values.shape[1]
    partner = jnp.where(
        lane % HD < HD // 2,
        pltpu.roll(values, width - HD // 2, 1),
        pltpu.roll(values, HD // 2, 1),
    )
    return values * cosine + partner * sine_signed


def head_masks(shape):
    lane = lax.broadcasted_iota(jnp.int32, shape, 1)
    return [lane // HD == head for head in range(shape[1] // HD)]


def params():
    return pltpu.CompilerParams(vmem_limit_bytes=VMEM_BYTES)


def whole(array):
    return pl.BlockSpec(array.shape, lambda *_: (0,) * len(array.shape))


SCALARS = pl.BlockSpec(memory_space=pltpu.SMEM)


def project_kernel(place_ref, *refs):
    pieces, weights = refs[:6], refs[6:10]
    cos_ref, sin_ref, low_ref, qkv_ref, w_ref, gain1_ref, gain2_ref, rows_ref = refs[10:]
    block, part = pieces[0].shape[2], w_ref.shape[1] // 3
    rows = gain1_ref.shape[1] // 8

    @pl.when(pl.program_id(0) == 0)
    def _():
        for step, piece in enumerate(weights):
            for turn in range(2):
                at = 2 * (place_ref[8] ^ step) + (place_ref[9] ^ turn)
                w_ref[pl.ds(pl.multiple_of(at * rows, rows), rows), :] = piece[turn, :rows]
                gains = piece[turn, rows:].astype(F32)
                rows_ref[0, pl.ds(at, 1), :] = gains[:1, :rows]
                rows_ref[1, pl.ds(at, 1), :] = gains[1:2, :rows]
        for out, at in ((gain1_ref, 0), (gain2_ref, 1)):
            for row in range(8):
                out[:, row * rows : (row + 1) * rows] = rows_ref[at, row : row + 1, :]

    gain = gain1_ref[...]
    index = 0
    for piece in pieces:
        for inner in range(piece.shape[0]):
            normed, _ = normalize(piece[inner, 0].astype(F32))
            low_ref[index, 0] = (normed * gain).astype(BF16)
            index += 1
    projected = dot(flat(low_ref[:, 0]), w_ref[...])
    cosine, sine = cos_ref[...], sin_ref[...]
    shape = (8, block, part)
    qkv_ref[:, 0, :, :part] = (
        (lane_rotate(projected[:, :part], cosine, sine) * HD**-0.5).astype(BF16).reshape(shape)
    )
    qkv_ref[:, 0, :, part : 2 * part] = (
        lane_rotate(projected[:, part : 2 * part], cosine, sine).astype(BF16).reshape(shape)
    )
    qkv_ref[:, 0, :, 2 * part :] = projected[:, 2 * part :].astype(BF16).reshape(shape)


def project(place, pieces, weights, cosine, sine):
    seqs, block, width = pieces[0].shape[1:]
    own = weights[0].shape[2]

    def by_seq(lead, last):
        return pl.BlockSpec((lead, 1, block, last), lambda s: (0, s, 0, 0))

    return pl.pallas_call(
        project_kernel,
        grid=(seqs,),
        in_specs=[SCALARS]
        + [by_seq(piece.shape[0], width) for piece in pieces]
        + [whole(w) for w in weights]
        + [whole(cosine), whole(sine)],
        out_specs=(
            by_seq(8, width),
            by_seq(8, own),
            pl.BlockSpec((width, own), lambda s: (0, 0)),
            pl.BlockSpec((1, width), lambda s: (0, 0)),
            pl.BlockSpec((1, width), lambda s: (0, 0)),
        ),
        out_shape=(
            jax.ShapeDtypeStruct((8, seqs, block, width), BF16),
            jax.ShapeDtypeStruct((8, seqs, block, own), BF16),
            jax.ShapeDtypeStruct((width, own), BF16),
            jax.ShapeDtypeStruct((1, width), F32),
            jax.ShapeDtypeStruct((1, width), F32),
        ),
        scratch_shapes=[pltpu.VMEM((2, 8, width // 8), F32)],
        compiler_params=params(),
        name="project",
    )(place, *pieces, *weights, cosine, sine)


def attend_kernel(place_ref, q_ref, k_ref, v_ref, att_ref, low_ref, log_ref, home_ref):
    seq, step = pl.program_id(0), pl.program_id(1)
    queries, keys, values = flat(q_ref[...]), flat(k_ref[...]), flat(v_ref[...])
    attended = jnp.zeros(queries.shape, F32)
    logs = jnp.zeros(queries.shape, F32)
    for mask in head_masks(queries.shape):
        scores = dot(jnp.where(mask, queries, 0), keys, ((1,), (1,)))
        peak = jnp.max(scores, axis=1, keepdims=True)
        weights = jnp.exp(scores - peak)
        total = jnp.sum(weights, axis=1, keepdims=True)
        mixed = dot(weights.astype(BF16), values) * (1.0 / total)
        attended = jnp.where(mask, mixed, attended)
        logs = jnp.where(mask, peak + jnp.log(total), logs)
    att_ref[...] = attended.reshape(att_ref.shape)
    log_ref[...] = logs.reshape(log_ref.shape)
    low = attended.astype(BF16).reshape(low_ref.shape)
    low_ref[...] = low
    for inner in range(2):
        home_ref[place_ref[2 * step + inner], seq] = low[inner, 0]


def attend(place, qkv):
    _, seqs, block, own = qkv.shape
    part = own // 3
    rows = pl.BlockSpec((2, 1, block, part), lambda s, i: (i, s, 0, 0))
    shape = (8, seqs, block, part)
    return pl.pallas_call(
        attend_kernel,
        grid=(seqs, 4),
        in_specs=[
            SCALARS,
            rows,
            pl.BlockSpec((8, 1, block, part), lambda s, i: (0, s, 0, 1)),
            pl.BlockSpec((8, 1, block, part), lambda s, i: (0, s, 0, 2)),
        ],
        out_specs=(rows, rows, rows, pl.BlockSpec(shape, lambda s, i: (0, 0, 0, 0))),
        out_shape=(
            jax.ShapeDtypeStruct(shape, F32),
            jax.ShapeDtypeStruct(shape, BF16),
            jax.ShapeDtypeStruct(shape, F32),
            jax.ShapeDtypeStruct(shape, BF16),
        ),
        compiler_params=params(),
        name="attend",
    )(place, qkv, qkv, qkv)


def branch_kernel(place_ref, *refs):
    pieces = refs[:6]
    rows_ref, tokens_ref, gain_ref, residual_ref, low_ref = refs[6:]
    total = flat(tokens_ref[...].astype(F32))
    index = 0
    for piece in pieces:
        for inner in range(piece.shape[0]):
            total += dot(flat(rows_ref[place_ref[index]]), piece[inner])
            index += 1
    normed, _ = normalize(total)
    residual_ref[...] = total.reshape(residual_ref.shape)
    low_ref[...] = (normed * gain_ref[...]).astype(BF16).reshape(low_ref.shape)


def branch(place, pieces, rows, tokens, gain):
    args = (*pieces, rows, tokens, gain)
    return pl.pallas_call(
        branch_kernel,
        in_specs=[SCALARS] + [whole(a) for a in args],
        out_shape=(
            jax.ShapeDtypeStruct(tokens.shape, F32),
            jax.ShapeDtypeStruct(tokens.shape, BF16),
        ),
        compiler_params=params(),
        name="branch",
    )(place, *args)


def mlp_kernel(low_ref, grad_ref, w_ref, mixed_ref, lifted_ref, keep_ref, send_ref):
    step = pl.program_id(0)
    hidden = w_ref.shape[1] // 2
    lifted = dot(flat(low_ref[...]), w_ref[...])
    first, second = lifted[:, :hidden], lifted[:, hidden:]
    grad_mixed = flat(grad_ref[...])
    gate = 0.5 * (1.0 + lax.erf(first * (0.5**0.5)))
    slope = gate + first * jnp.exp(first * first * -0.5) * ((2.0 * math.pi) ** -0.5)
    activated = first * gate
    mixed_ref[...] = (activated * second).astype(BF16).reshape(mixed_ref.shape)
    grad = jnp.concatenate(
        [(grad_mixed * second * slope).astype(BF16), (grad_mixed * activated).astype(BF16)],
        axis=1,
    )
    lifted_ref[...] = grad.reshape(lifted_ref.shape)
    partial = dot(grad, w_ref[...], ((1,), (1,))).astype(BF16).reshape(keep_ref.shape)

    @pl.when(step < 5)
    def _():
        keep_ref[...] = partial

    @pl.when(step >= 5)
    def _():
        send_ref[...] = partial


def mlp(low, grad_mixed, w):
    _, seqs, block, width = low.shape
    hidden = w.shape[1] // 2

    def rows(last):
        return pl.BlockSpec((1, seqs, block, last), lambda i: (i, 0, 0, 0))

    return pl.pallas_call(
        mlp_kernel,
        grid=(8,),
        in_specs=[rows(width), rows(hidden), whole(w)],
        out_specs=(
            rows(hidden),
            rows(2 * hidden),
            pl.BlockSpec((1, seqs, block, width), lambda i: (jnp.minimum(i, 4), 0, 0, 0)),
            pl.BlockSpec((1, seqs, block, width), lambda i: (jnp.maximum(i - 5, 0), 0, 0, 0)),
        ),
        out_shape=(
            jax.ShapeDtypeStruct((8, seqs, block, hidden), BF16),
            jax.ShapeDtypeStruct((8, seqs, block, 2 * hidden), BF16),
            jax.ShapeDtypeStruct((5, seqs, block, width), BF16),
            jax.ShapeDtypeStruct((3, seqs, block, width), BF16),
        ),
        compiler_params=params(),
        name="mlp",
    )(low, grad_mixed, w)


def branch_back_kernel(place_ref, *refs):
    pieces = refs[:6]
    low_ref, residual_ref, top_ref, gain_ref, grad_ref, branch_ref, home_ref, sum_ref = refs[6:]
    grad_low = flat(low_ref[...])
    normed, factor = normalize(flat(residual_ref[...]))
    sum_ref[...] = jnp.sum(grad_low * normed, axis=0, keepdims=True)
    grad = flat(top_ref[...].astype(F32)) + norm_back(grad_low * gain_ref[...], normed, factor)
    grad_ref[...] = grad.reshape(grad_ref.shape)
    low = grad.astype(BF16)
    branch_ref[...] = low.reshape(branch_ref.shape)
    index = 0
    for piece in pieces:
        for inner in range(piece.shape[0]):
            home_ref[place_ref[index]] = (
                dot(low, piece[inner], ((1,), (1,))).astype(BF16).reshape(home_ref.shape[1:])
            )
            index += 1


def branch_back(place, pieces, grad_low, residual, top, gain):
    args = (*pieces, grad_low, residual, top, gain)
    seqs, block, width = residual.shape
    return pl.pallas_call(
        branch_back_kernel,
        in_specs=[SCALARS] + [whole(a) for a in args],
        out_shape=(
            jax.ShapeDtypeStruct(residual.shape, F32),
            jax.ShapeDtypeStruct(residual.shape, BF16),
            jax.ShapeDtypeStruct((8, seqs, block, pieces[0].shape[1]), BF16),
            jax.ShapeDtypeStruct((1, width), F32),
        ),
        compiler_params=params(),
        name="branch_back",
    )(place, *args)


def attend_back_kernel(
    place_ref, q_ref, k_ref, v_ref, grad_ref, att_ref, log_ref, cosq_ref, sinq_ref, cos_ref,
    sin_ref, w_ref, proj_ref, keep_ref, send_ref, sum_k, sum_v,
):
    seq, step = pl.program_id(0), pl.program_id(1)
    block, part = q_ref.shape[2], q_ref.shape[3]

    @pl.when(step == 0)
    def _():
        sum_k[...] = jnp.zeros_like(sum_k)
        sum_v[...] = jnp.zeros_like(sum_v)

    queries, keys, values = flat(q_ref[...]), flat(k_ref[...]), flat(v_ref[...])
    grads = jnp.concatenate([grad_ref[place_ref[2 * step + inner], seq] for inner in range(2)])
    along = (grads.astype(F32) * flat(att_ref[...])).T
    logs = flat(log_ref[...]).T
    grad_queries = jnp.zeros(queries.shape, F32)
    for head, mask in enumerate(head_masks(queries.shape)):
        own_q = jnp.where(mask, queries, 0)
        own_g = jnp.where(mask, grads, 0)
        scores = dot(keys, own_q, ((1,), (1,)))
        weights = jnp.exp(scores - logs[head * HD : head * HD + 1])
        lifted = dot(values, own_g, ((1,), (1,)))
        row = jnp.sum(along[head * HD : (head + 1) * HD], axis=0, keepdims=True)
        grad_scores = (weights * (lifted - row)).astype(BF16)
        sum_k[...] += dot(grad_scores, own_q)
        sum_v[...] += dot(weights.astype(BF16), own_g)
        grad_queries = jnp.where(mask, dot(grad_scores, keys, ((0,), (0,))), grad_queries)
    grad_queries = lane_rotate(grad_queries * HD**-0.5, cosq_ref[...], -sinq_ref[...])
    proj_ref[pl.ds(2 * step, 2), 0, :, :part] = grad_queries.astype(BF16).reshape(2, block, part)

    @pl.when(step == 3)
    def _():
        shape = (8, block, part)
        grad_keys = lane_rotate(sum_k[...], cos_ref[...], -sin_ref[...])
        proj_ref[:, 0, :, part : 2 * part] = grad_keys.astype(BF16).reshape(shape)
        proj_ref[:, 0, :, 2 * part :] = sum_v[...].astype(BF16).reshape(shape)
        partial = dot(flat(proj_ref[:, 0]), w_ref[...], ((1,), (1,))).astype(BF16)
        keep_ref[:, 0] = partial[: 5 * block].reshape(5, block, -1)
        send_ref[:, 0] = partial[5 * block :].reshape(3, block, -1)


def attend_back(place, qkv, grads, attended, logs, cosine, sine, w):
    _, seqs, block, own = qkv.shape
    part, width = own // 3, w.shape[0]
    rows = pl.BlockSpec((2, 1, block, part), lambda s, i: (i, s, 0, 0))
    angles = pl.BlockSpec((2 * block, part), lambda s, i: (i, 0))

    def by_seq(lead, last):
        return pl.BlockSpec((lead, 1, block, last), lambda s, i: (0, s, 0, 0))

    return pl.pallas_call(
        attend_back_kernel,
        grid=(seqs, 4),
        in_specs=[
            SCALARS,
            rows,
            pl.BlockSpec((8, 1, block, part), lambda s, i: (0, s, 0, 1)),
            pl.BlockSpec((8, 1, block, part), lambda s, i: (0, s, 0, 2)),
            whole(grads),
            rows,
            rows,
            angles,
            angles,
            whole(cosine),
            whole(sine),
            whole(w),
        ],
        out_specs=(by_seq(8, own), by_seq(5, width), by_seq(3, width)),
        out_shape=(
            jax.ShapeDtypeStruct((8, seqs, block, own), BF16),
            jax.ShapeDtypeStruct((5, seqs, block, width), BF16),
            jax.ShapeDtypeStruct((3, seqs, block, width), BF16),
        ),
        scratch_shapes=[pltpu.VMEM((8 * block, part), F32), pltpu.VMEM((8 * block, part), F32)],
        compiler_params=params(),
        name="attend_back",
    )(place, qkv, qkv, qkv, grads, attended, logs, cosine, sine, cosine, sine, w)


class Group:
    def __init__(self):
        self.heads = lax.axis_size("head")
        self.dp = lax.axis_size("dp")
        self.ctx_at = lax.axis_index("ctx")
        self.head_at = lax.axis_index("head")
        self.dp_at = lax.axis_index("dp")
        self.at = self.ctx_at * self.heads + self.head_at
        near, far = [], []
        for c in range(2):
            for h in range(self.heads):
                x, y = (c ^ 1) * self.heads + h, c * self.heads + (h ^ 2)
                near.append((c * self.heads + h, x if h % 2 == 0 else y))
                far.append((c * self.heads + h, y if h % 2 == 0 else x))
        self.near, self.far = near, far

    def order(self):
        first = jnp.where(self.head_at % 2 == 0, 4, 2)
        second = 6 - first
        return jnp.stack(
            [self.at ^ bits for bits in (0, 1, first, first ^ 1, 6, second ^ 1, second, 7)]
        )

    def swap(self, values, bit):
        if bit == 4:
            return lax.ppermute(values, "ctx", [(0, 1), (1, 0)])
        return lax.ppermute(values, "head", [(i, i ^ bit) for i in range(self.heads)])

    def gather(self, own):
        own = own[None]
        mate = self.swap(own, 1)
        near = lax.ppermute(jnp.concatenate([own, mate]), GROUP, self.near)
        far = lax.ppermute(near[:1], GROUP, self.far)
        return own, mate, near, far, self.swap(near, 1), self.swap(far, 1)

    def reduce(self, keep, send):
        met = keep[2:].astype(F32) + self.swap(send, 1).astype(F32)
        far = lax.ppermute(met[2].astype(BF16), GROUP, self.far)
        met = jnp.concatenate([(met[0] + far.astype(F32))[None], met[1:2]])
        near = lax.ppermute(met.astype(BF16), GROUP, self.near)
        met = keep[:2].astype(F32) + near.astype(F32)
        return met[0] + self.swap(met[1].astype(BF16), 1).astype(F32)

    def rows_in(self, values, place):
        pairs = [
            (place[h] * self.heads + d, d * self.heads + h)
            for d in range(self.dp)
            for h in range(self.heads)
        ]
        return lax.ppermute(values, ("dp", "head"), pairs)

    def rows_back(self, values, place):
        pairs = [
            (d * self.heads + h, place[h] * self.heads + d)
            for d in range(self.dp)
            for h in range(self.heads)
        ]
        return lax.ppermute(values, ("dp", "head"), pairs)

    def across(self, values, step):
        return lax.ppermute(values, "dp", [(i, i ^ step) for i in range(self.dp)])

    def total(self, values):
        for bit in (1, 2, 4):
            values = values + self.swap(values, bit)
        step = 1
        while step < self.dp:
            values = values + self.across(values, step)
            step *= 2
        return values


def pick(array, index, axis):
    return lax.dynamic_index_in_dim(array, index, axis, keepdims=False)


def after(values, earlier):
    return lax.optimization_barrier((values, earlier))[0]


def local_split(tokens, cotangent, w_qkv, w_attn_out, w_in, w_mlp_out, norm_gain1, norm_gain2):
    seqs, block, width = tokens.shape
    group = Group()
    heads, dp = group.heads, group.dp
    at_c, at_h = group.ctx_at, group.head_at
    parts = 2 * heads
    hidden = w_in.shape[1] // 2 // parts
    padded = -(-hidden // 128) * 128
    own_width = width // parts
    half = heads // 2
    rows_here = w_qkv.shape[0]
    place = [2 * (h % half) + h // half for h in range(heads)]
    straight = list(range(heads))
    order = group.order()
    scalars = jnp.concatenate([order, jnp.stack([group.dp_at, at_c])]).astype(jnp.int32)

    def in_order(own, other):
        return jnp.where(at_c == 0, jnp.stack([own, other]), jnp.stack([other, own]))

    x_pieces = group.gather(tokens)
    gains = jnp.pad(
        jnp.stack([norm_gain1, norm_gain2]), ((0, 14), (0, 3 * own_width - rows_here))
    )
    qkv_view = w_qkv.reshape(rows_here, 3, width)

    def qkv_part(at):
        start = (2 * at_h + at) * own_width
        cut = lax.dynamic_slice_in_dim(qkv_view, start, own_width, 2)
        return jnp.concatenate([cut.reshape(rows_here, 3 * own_width), gains])

    pair = jnp.stack([qkv_part(at_c), group.swap(qkv_part(1 - at_c), 4)])
    qkv_pieces = [pair] + [group.across(pair, step) for step in range(1, dp)]

    weight_out = group.rows_in(w_attn_out, straight)
    out_pieces = group.gather(weight_out)
    in_view = w_in.reshape(rows_here, 2, heads, 2, hidden)
    in_view = pick(in_view, 2 * (at_h % half) + at_h // half, 2)

    def in_part(at):
        cut = pick(in_view, at, 2)
        return jnp.pad(cut, ((0, 0), (0, 0), (0, padded - hidden))).reshape(rows_here, 2 * padded)

    in_pair = in_order(in_part(at_c), group.swap(in_part(1 - at_c), 4))
    weight_in = lax.all_gather(after(in_pair, qkv_pieces[-1]), "dp", axis=0).reshape(width, -1)
    weight_mlp = group.rows_in(after(w_mlp_out, qkv_pieces[-1]), place)
    weight_mlp = jnp.pad(weight_mlp, ((0, padded - hidden), (0, 0)))

    positions = (order[:, None] * block + jnp.arange(block, dtype=jnp.int32)[None, :]).reshape(-1)
    lane = jnp.arange(own_width, dtype=jnp.int32)
    frequency = jnp.exp(
        (lane % (HD // 2)).astype(F32) * (-math.log(ROPE_BASE) / (HD // 2))
    )
    angles = positions.astype(F32)[:, None] * frequency[None, :]
    cosine = jnp.cos(angles)
    sine = jnp.sin(angles) * jnp.where(lane % HD < HD // 2, -1.0, 1.0)[None, :]

    def exchange(values):
        return lax.all_to_all(values, GROUP, split_axis=0, concat_axis=0, tiled=True)

    low1, qkv, weight_qkv, gain_one, gain_two = project(
        scalars, x_pieces, qkv_pieces, cosine, sine
    )
    attended, att_low, logs, home = attend(scalars, qkv)
    residual, low2 = branch(scalars, out_pieces, exchange(home), tokens, gain_two)
    low2_all = jnp.concatenate(group.gather(low2))

    cot_all = jnp.concatenate(group.gather(after(cotangent, x_pieces[-1])))
    cot_flat = flat(cot_all)
    grad_mixed = dot(cot_flat, weight_mlp, ((1,), (1,))).reshape(8, seqs, block, padded)
    mixed, grad_lifted, keep, send = mlp(low2_all, grad_mixed, weight_in)
    grad_low2 = group.reduce(keep, send)
    grad_residual, grad_branch, home, gain2_sum = branch_back(
        scalars, out_pieces, grad_low2, residual, cotangent, gain_two
    )
    grad_home = exchange(home)
    branch_all = jnp.concatenate(group.gather(after(grad_branch, grad_home)))
    grad_proj, keep, send = attend_back(
        scalars, qkv, grad_home, attended, logs, cosine, sine, weight_qkv
    )
    grad_low1 = group.reduce(keep, send)
    normed1, factor1 = normalize(tokens.astype(F32))
    grad_input = grad_residual + norm_back(grad_low1 * gain_one, normed1, factor1)

    mixed_flat = flat(mixed)
    cut = 5 * seqs * block
    out_keep = dot(mixed_flat[:cut], weight_mlp).astype(BF16).reshape(5, seqs, block, width)
    out_send = dot(mixed_flat[cut:], weight_mlp).astype(BF16).reshape(3, seqs, block, width)
    result = (residual + group.reduce(out_keep, out_send)).astype(BF16)

    def over_tokens(left, right):
        return dot(flat(left), flat(right), ((0,), (0,)))

    def scatter(values):
        return lax.psum_scatter(values.astype(BF16), "dp", scatter_dimension=0, tiled=True)

    def columns_first(values):
        return jnp.moveaxis(values.reshape(values.shape[0], dp, -1), 1, 0)

    grad_mlp = scatter(columns_first(over_tokens(mixed, cot_flat)[:hidden]))[0]
    grad_mlp = group.rows_back(grad_mlp, place).astype(F32)
    grad_out = scatter(columns_first(over_tokens(att_low, branch_all)))[0]
    grad_out = group.rows_back(grad_out, straight).astype(F32)

    def rows_here_of(values):
        both = values.reshape(2, rows_here, -1)
        own = pick(both, at_c, 0)
        other = group.swap(pick(both, 1 - at_c, 0), 4)
        return in_order(own, other)

    grad_in = rows_here_of(scatter(over_tokens(low2_all, grad_lifted)))
    grad_in = jnp.stack([grad_in[..., :hidden], grad_in[..., padded : padded + hidden]])
    late = at_h // half
    stays = pick(grad_in, late, 0)
    comes = group.swap(pick(grad_in, 1 - late, 0), half)
    grad_in = jnp.where(
        late == 0, jnp.concatenate([stays, comes]), jnp.concatenate([comes, stays])
    )
    grad_in = jnp.moveaxis(grad_in, 0, 1).reshape(rows_here, -1).astype(F32)

    grad_qkv = over_tokens(low1, grad_proj)
    gain1_sum = jnp.sum(grad_qkv * weight_qkv.astype(F32), axis=1) / gain_one[0]
    sums = group.total(jnp.stack([gain1_sum, gain2_sum[0]]).reshape(-1, 128))
    sums = sums.reshape(2, -1)
    per_device = width // (dp * parts)
    start = (group.dp_at * parts + group.at) * per_device
    grad_gain1, grad_gain2 = (
        lax.dynamic_slice_in_dim(sums[i], start, per_device, 0) for i in range(2)
    )
    grad_qkv = rows_here_of(scatter(grad_qkv)).reshape(2, rows_here, 3, own_width)
    grad_qkv = jnp.moveaxis(grad_qkv, 2, 0)
    odd, late = at_h % 2, at_h // half
    stays = pick(grad_qkv, odd + late, 0)
    core = group.swap(pick(grad_qkv, 1 - odd + late, 0), 1)
    chip = group.swap(pick(grad_qkv, 2 - 2 * late, 0), 2)
    grad_qkv = jnp.where(
        odd == 0, jnp.concatenate([stays, core, chip]), jnp.concatenate([chip, core, stays])
    )
    grad_qkv = jnp.moveaxis(grad_qkv, 0, 1).reshape(rows_here, -1).astype(F32)

    return (
        result,
        grad_input,
        grad_qkv,
        grad_out,
        grad_in,
        grad_mlp,
        grad_gain1,
        grad_gain2,
    )


def local(tokens, cotangent, w_qkv, w_attn_out, w_in, w_mlp_out, norm_gain1, norm_gain2):
    args = (tokens, cotangent, w_qkv, w_attn_out, w_in, w_mlp_out, norm_gain1, norm_gain2)
    sizes = [lax.axis_size(axis) for axis in ("dp", "ctx", "head")]
    if sizes == [4, 2, 4] and tokens.shape[2] == 8 * 2 * HD and tokens.shape[1] % 16 == 0:
        return local_split(*args)
    return local_general(*args)


def solution(mesh):
    in_specs = (
        P("dp", ("ctx", "head"), None),
        P("dp", ("ctx", "head"), None),
        P(("dp", "ctx"), None),
        P(("dp", "ctx"), None),
        P(("dp", "ctx"), None),
        P(("dp", "ctx"), None),
        P(("dp", "ctx")),
        P(("dp", "ctx")),
    )
    out_specs = (
        P("dp", ("ctx", "head"), None),
        P("dp", ("ctx", "head"), None),
        P(("dp", "ctx"), "head"),
        P(("dp", "ctx"), "head"),
        P(("dp", "ctx"), "head"),
        P(("dp", "ctx"), "head"),
        P(("dp", "ctx", "head")),
        P(("dp", "ctx", "head")),
    )
    return jax.shard_map(local, mesh=mesh, in_specs=in_specs, out_specs=out_specs, check_vma=False)
```

```python
import functools
import math

import jax
import jax.numpy as jnp
from jax import lax
from jax.experimental import pallas as pl
from jax.experimental.pallas import tpu as pltpu
from jax.sharding import PartitionSpec as P

HD = 64


EPSILON = 1e-05
ROPE_BASE = 160000.0


def normalize(values):
    centre = jnp.mean(values, axis=-1, keepdims=True)
    shifted = values - centre
    spread = jnp.mean(shifted * shifted, axis=-1, keepdims=True)
    factor = lax.rsqrt(spread + EPSILON)
    return (shifted * factor, factor)


def norm_back(grad_normed, normed, factor):
    grad_centre = jnp.mean(grad_normed, axis=-1, keepdims=True)
    grad_along = jnp.mean(grad_normed * normed, axis=-1, keepdims=True)
    return (grad_normed - grad_centre - normed * grad_along) * factor


def rope_tables(positions, half_size):
    frequency = jnp.exp(
        jnp.arange(half_size, dtype=jnp.float32) * (-math.log(ROPE_BASE) / half_size)
    )
    angles = positions[:, None] * frequency[None, :]
    return (jnp.cos(angles), jnp.sin(angles))


def rotate(values, cosine, sine_table, direction):
    half_size = cosine.shape[-1]
    first_half = values[..., :half_size]
    second_half = values[..., half_size:]
    cos_part = cosine[:, None, :]
    sin_part = sine_table[:, None, :] * direction
    return jnp.concatenate(
        [
            first_half * cos_part - second_half * sin_part,
            second_half * cos_part + first_half * sin_part,
        ],
        axis=-1,
    )


def block_scores(queries4, keys_block, scale):
    keys4 = keys_block.reshape(
        keys_block.shape[0], keys_block.shape[1], queries4.shape[2], queries4.shape[3]
    )
    return (
        jnp.einsum("sqgd,skgd->sgqk", queries4, keys4, preferred_element_type=jnp.float32) * scale
    )


def attend_forward(queries4, keys_all, values_all, key_rows, scale):
    seqs_here, query_rows, groups, head_size = queries4.shape
    turns = keys_all.shape[1] // key_rows

    def statistics(turn, carry):
        row_peak, row_total = carry
        keys_block = lax.dynamic_slice_in_dim(keys_all, turn * key_rows, key_rows, 1)
        scores = block_scores(queries4, keys_block, scale)
        new_peak = jnp.maximum(row_peak, jnp.max(scores, axis=-1))
        row_total = row_total * jnp.exp(row_peak - new_peak) + jnp.sum(
            jnp.exp(scores - new_peak[..., None]), axis=-1
        )
        return (new_peak, row_total)

    start_peak = jnp.full((seqs_here, groups, query_rows), -1e30, jnp.float32)
    row_peak, row_total = lax.fori_loop(
        0, turns, statistics, (start_peak, jnp.zeros_like(start_peak))
    )
    log_total = row_peak + jnp.log(row_total)

    def accumulate(turn, running):
        keys_block = lax.dynamic_slice_in_dim(keys_all, turn * key_rows, key_rows, 1)
        values_block = lax.dynamic_slice_in_dim(values_all, turn * key_rows, key_rows, 1).reshape(
            seqs_here, key_rows, groups, head_size
        )
        weights = jnp.exp(block_scores(queries4, keys_block, scale) - log_total[..., None]).astype(
            jnp.bfloat16
        )
        return running + jnp.einsum(
            "sgqk,skgd->sqgd", weights, values_block, preferred_element_type=jnp.float32
        )

    attended = lax.fori_loop(
        0, turns, accumulate, jnp.zeros((seqs_here, query_rows, groups, head_size), jnp.float32)
    )
    return (attended, log_total)


def attend_backward(queries4, keys_all, values_all, grad_out4, log_total, along, key_rows, scale):
    seqs_here, query_rows, groups, head_size = queries4.shape
    length = keys_all.shape[1]
    width_group = groups * head_size
    turns = length // key_rows

    def step_back(turn, carry):
        grad_queries, grad_keys, grad_values = carry
        keys_block = lax.dynamic_slice_in_dim(keys_all, turn * key_rows, key_rows, 1)
        keys4 = keys_block.reshape(seqs_here, key_rows, groups, head_size)
        values4 = lax.dynamic_slice_in_dim(values_all, turn * key_rows, key_rows, 1).reshape(
            seqs_here, key_rows, groups, head_size
        )
        weights = jnp.exp(block_scores(queries4, keys_block, scale) - log_total[..., None])
        grad_weights = jnp.einsum(
            "sqgd,skgd->sgqk", grad_out4, values4, preferred_element_type=jnp.float32
        )
        grad_scores = (weights * (grad_weights - along[..., None])).astype(jnp.bfloat16)
        grad_queries = grad_queries + jnp.einsum(
            "sgqk,skgd->sqgd", grad_scores, keys4, preferred_element_type=jnp.float32
        )
        key_part = (
            jnp.einsum("sgqk,sqgd->skgd", grad_scores, queries4, preferred_element_type=jnp.float32)
            * scale
        )
        value_part = jnp.einsum(
            "sgqk,sqgd->skgd",
            weights.astype(jnp.bfloat16),
            grad_out4,
            preferred_element_type=jnp.float32,
        )
        grad_keys = lax.dynamic_update_slice_in_dim(
            grad_keys, key_part.reshape(seqs_here, key_rows, width_group), turn * key_rows, 1
        )
        grad_values = lax.dynamic_update_slice_in_dim(
            grad_values, value_part.reshape(seqs_here, key_rows, width_group), turn * key_rows, 1
        )
        return (grad_queries, grad_keys, grad_values)

    start = (
        jnp.zeros((seqs_here, query_rows, groups, head_size), jnp.float32),
        jnp.zeros((seqs_here, length, width_group), jnp.float32),
        jnp.zeros((seqs_here, length, width_group), jnp.float32),
    )
    grad_queries, grad_keys, grad_values = lax.fori_loop(0, turns, step_back, start)
    return (grad_queries * scale, grad_keys, grad_values)


def local_general(tokens, cotangent, w_qkv, w_attn_out, w_in, w_mlp_out, norm_gain1, norm_gain2):
    seqs_here, block_rows, width = tokens.shape
    count_rows = seqs_here * block_rows
    heads_all = width // HD
    head_devices = lax.axis_size("head")
    group_devices = lax.axis_size(("dp", "ctx"))
    groups = heads_all // head_devices
    width_group = groups * HD
    scale = HD ** (-0.5)
    ff_width = w_in.shape[1] // 2
    full_qkv, full_out, full_in, full_mlp, gain_one, gain_two = (
        lax.all_gather(w_qkv, ("dp", "ctx"), axis=0, tiled=True),
        lax.all_gather(w_attn_out, ("dp", "ctx"), axis=0, tiled=True),
        lax.all_gather(w_in, ("dp", "ctx"), axis=0, tiled=True),
        lax.all_gather(w_mlp_out, ("dp", "ctx"), axis=0, tiled=True),
        lax.all_gather(norm_gain1, ("dp", "ctx"), axis=0, tiled=True),
        lax.all_gather(norm_gain2, ("dp", "ctx"), axis=0, tiled=True),
    )
    x_in = tokens.astype(jnp.float32).reshape(count_rows, width)
    normed1, factor1 = normalize(x_in)
    lowered1 = (normed1 * gain_one.astype(jnp.float32)).astype(jnp.bfloat16)
    projected = jnp.dot(lowered1, full_qkv, preferred_element_type=jnp.float32).reshape(
        seqs_here, block_rows, 3, heads_all, HD
    )
    first_pos = (lax.axis_index("ctx") * head_devices + lax.axis_index("head")) * block_rows
    positions = (first_pos + jnp.arange(block_rows, dtype=jnp.int32)).astype(jnp.float32)
    cosine, sine_table = rope_tables(positions, HD // 2)
    queries = (
        rotate(projected[:, :, 0], cosine, sine_table, 1.0)
        .astype(jnp.bfloat16)
        .reshape(seqs_here, block_rows, width)
    )
    keys_local = (
        rotate(projected[:, :, 1], cosine, sine_table, 1.0)
        .astype(jnp.bfloat16)
        .reshape(seqs_here, block_rows, width)
    )
    values_local = projected[:, :, 2].astype(jnp.bfloat16).reshape(seqs_here, block_rows, width)
    queries_h, keys_h, values_h = (
        lax.all_to_all(queries, "head", split_axis=2, concat_axis=1, tiled=True),
        lax.all_to_all(keys_local, "head", split_axis=2, concat_axis=1, tiled=True),
        lax.all_to_all(values_local, "head", split_axis=2, concat_axis=1, tiled=True),
    )
    query_rows = queries_h.shape[1]
    queries4 = queries_h.reshape(seqs_here, query_rows, groups, HD)
    keys_all, values_all = (
        lax.all_gather(keys_h, "ctx", axis=1, tiled=True),
        lax.all_gather(values_h, "ctx", axis=1, tiled=True),
    )
    key_rows = math.gcd(keys_all.shape[1], 1024)
    attended, log_total = attend_forward(queries4, keys_all, values_all, key_rows, scale)
    attended_low = attended.astype(jnp.bfloat16).reshape(seqs_here, query_rows, width_group)
    back_rows = lax.all_to_all(
        attended_low, "head", split_axis=1, concat_axis=2, tiled=True
    ).reshape(count_rows, width)
    residual = x_in + jnp.dot(back_rows, full_out, preferred_element_type=jnp.float32)
    normed2, factor2 = normalize(residual)
    lowered2 = (normed2 * gain_two.astype(jnp.float32)).astype(jnp.bfloat16)
    lifted = jnp.dot(lowered2, full_in, preferred_element_type=jnp.float32)
    first_part = lifted[:, :ff_width]
    second_part = lifted[:, ff_width:]
    activated, gelu_pullback = jax.vjp(
        lambda entries: jax.nn.gelu(entries, approximate=False), first_part
    )
    mixed = (activated * second_part).astype(jnp.bfloat16)
    result = (residual + jnp.dot(mixed, full_mlp, preferred_element_type=jnp.float32)).astype(
        jnp.bfloat16
    )
    full_qkv, full_out, full_in, full_mlp, gain_one, gain_two = (
        lax.all_gather(w_qkv, ("dp", "ctx"), axis=0, tiled=True),
        lax.all_gather(w_attn_out, ("dp", "ctx"), axis=0, tiled=True),
        lax.all_gather(w_in, ("dp", "ctx"), axis=0, tiled=True),
        lax.all_gather(w_mlp_out, ("dp", "ctx"), axis=0, tiled=True),
        lax.all_gather(norm_gain1, ("dp", "ctx"), axis=0, tiled=True),
        lax.all_gather(norm_gain2, ("dp", "ctx"), axis=0, tiled=True),
    )
    keys_all, values_all = (
        lax.all_gather(keys_h, "ctx", axis=1, tiled=True),
        lax.all_gather(values_h, "ctx", axis=1, tiled=True),
    )
    grad_top = cotangent.reshape(count_rows, width)
    grad_mlp = jnp.einsum("nf,nd->fd", mixed, grad_top, preferred_element_type=jnp.float32)
    grad_mixed = jnp.einsum("nd,fd->nf", grad_top, full_mlp, preferred_element_type=jnp.float32)
    grad_first = gelu_pullback(grad_mixed * second_part)[0]
    grad_lifted = jnp.concatenate([grad_first, grad_mixed * activated], axis=-1).astype(
        jnp.bfloat16
    )
    grad_inner = jnp.einsum("nd,nf->df", lowered2, grad_lifted, preferred_element_type=jnp.float32)
    grad_lowered2 = jnp.einsum(
        "nf,df->nd", grad_lifted, full_in, preferred_element_type=jnp.float32
    )
    grad_two = jnp.sum(grad_lowered2 * normed2, axis=0)
    grad_residual = grad_top.astype(jnp.float32) + norm_back(
        grad_lowered2 * gain_two.astype(jnp.float32), normed2, factor2
    )
    grad_branch = grad_residual.astype(jnp.bfloat16)
    grad_outproj = jnp.einsum(
        "nd,ne->de", back_rows, grad_branch, preferred_element_type=jnp.float32
    )
    grad_attended = jnp.einsum(
        "ne,de->nd", grad_branch, full_out, preferred_element_type=jnp.float32
    ).astype(jnp.bfloat16)
    grad_attended_h = lax.all_to_all(
        grad_attended.reshape(seqs_here, block_rows, width),
        "head",
        split_axis=2,
        concat_axis=1,
        tiled=True,
    )
    grad_out4 = grad_attended_h.reshape(seqs_here, query_rows, groups, HD)
    along = jnp.transpose(jnp.sum(grad_out4.astype(jnp.float32) * attended, axis=-1), (0, 2, 1))
    grad_queries, grad_keys_all, grad_values_all = attend_backward(
        queries4, keys_all, values_all, grad_out4, log_total, along, key_rows, scale
    )
    grad_keys_sum, grad_values_sum = (
        lax.psum_scatter(
            grad_keys_all.astype(jnp.bfloat16), "ctx", scatter_dimension=1, tiled=True
        ).astype(jnp.float32),
        lax.psum_scatter(
            grad_values_all.astype(jnp.bfloat16), "ctx", scatter_dimension=1, tiled=True
        ).astype(jnp.float32),
    )
    grad_q_low = grad_queries.astype(jnp.bfloat16).reshape(seqs_here, query_rows, width_group)
    grad_q_tok, grad_k_tok, grad_v_tok = (
        lax.all_to_all(grad_q_low, "head", split_axis=1, concat_axis=2, tiled=True),
        lax.all_to_all(
            grad_keys_sum.astype(jnp.bfloat16), "head", split_axis=1, concat_axis=2, tiled=True
        ),
        lax.all_to_all(
            grad_values_sum.astype(jnp.bfloat16), "head", split_axis=1, concat_axis=2, tiled=True
        ),
    )
    unrot_q = rotate(
        grad_q_tok.astype(jnp.float32).reshape(seqs_here, block_rows, heads_all, HD),
        cosine,
        sine_table,
        -1.0,
    )
    unrot_k = rotate(
        grad_k_tok.astype(jnp.float32).reshape(seqs_here, block_rows, heads_all, HD),
        cosine,
        sine_table,
        -1.0,
    )
    grad_projected = jnp.concatenate(
        [
            unrot_q.reshape(count_rows, width),
            unrot_k.reshape(count_rows, width),
            grad_v_tok.astype(jnp.float32).reshape(count_rows, width),
        ],
        axis=-1,
    ).astype(jnp.bfloat16)
    grad_project = jnp.einsum(
        "nd,nf->df", lowered1, grad_projected, preferred_element_type=jnp.float32
    )
    grad_lowered1 = jnp.einsum(
        "nf,df->nd", grad_projected, full_qkv, preferred_element_type=jnp.float32
    )
    grad_one = jnp.sum(grad_lowered1 * normed1, axis=0)
    grad_input = grad_residual + norm_back(
        grad_lowered1 * gain_one.astype(jnp.float32), normed1, factor1
    )
    pieces_one = grad_one.reshape(group_devices, head_devices, -1)
    pieces_two = grad_two.reshape(group_devices, head_devices, -1)
    part_qkv, part_out, part_in, part_mlp, part_one, part_two = (
        lax.psum_scatter(
            grad_project.astype(jnp.bfloat16), ("dp", "ctx"), scatter_dimension=0, tiled=True
        ).astype(jnp.float32),
        lax.psum_scatter(
            grad_outproj.astype(jnp.bfloat16), ("dp", "ctx"), scatter_dimension=0, tiled=True
        ).astype(jnp.float32),
        lax.psum_scatter(
            grad_inner.astype(jnp.bfloat16), ("dp", "ctx"), scatter_dimension=0, tiled=True
        ).astype(jnp.float32),
        lax.psum_scatter(
            grad_mlp.astype(jnp.bfloat16), ("dp", "ctx"), scatter_dimension=0, tiled=True
        ).astype(jnp.float32),
        lax.psum_scatter(
            pieces_one.astype(jnp.bfloat16), ("dp", "ctx"), scatter_dimension=0, tiled=True
        ).astype(jnp.float32),
        lax.psum_scatter(
            pieces_two.astype(jnp.bfloat16), ("dp", "ctx"), scatter_dimension=0, tiled=True
        ).astype(jnp.float32),
    )
    final_qkv, final_out, final_in, final_mlp, final_one, final_two = (
        lax.psum_scatter(
            part_qkv.astype(jnp.bfloat16), "head", scatter_dimension=1, tiled=True
        ).astype(jnp.float32),
        lax.psum_scatter(
            part_out.astype(jnp.bfloat16), "head", scatter_dimension=1, tiled=True
        ).astype(jnp.float32),
        lax.psum_scatter(
            part_in.astype(jnp.bfloat16), "head", scatter_dimension=1, tiled=True
        ).astype(jnp.float32),
        lax.psum_scatter(
            part_mlp.astype(jnp.bfloat16), "head", scatter_dimension=1, tiled=True
        ).astype(jnp.float32),
        lax.psum_scatter(
            part_one.astype(jnp.bfloat16), "head", scatter_dimension=1, tiled=True
        ).astype(jnp.float32),
        lax.psum_scatter(
            part_two.astype(jnp.bfloat16), "head", scatter_dimension=1, tiled=True
        ).astype(jnp.float32),
    )
    return (
        result.reshape(seqs_here, block_rows, width),
        grad_input.reshape(seqs_here, block_rows, width),
        final_qkv,
        final_out,
        final_in,
        final_mlp,
        final_one.reshape(-1),
        final_two.reshape(-1),
    )


F32 = jnp.float32
BF16 = jnp.bfloat16
VMEM_BYTES = 56 * 1024 * 1024
GROUP = ("ctx", "head")


def dot(left, right, dims=((1,), (0,))):
    return lax.dot_general(left, right, (dims, ((), ())), preferred_element_type=F32)


def flat(values):
    return values.reshape(-1, values.shape[-1])


def lane_rotate(values, cosine, sine_signed):
    lane = lax.broadcasted_iota(jnp.int32, values.shape, 1)
    width = values.shape[1]
    partner = jnp.where(
        lane % HD < HD // 2,
        pltpu.roll(values, width - HD // 2, 1),
        pltpu.roll(values, HD // 2, 1),
    )
    return values * cosine + partner * sine_signed


def head_masks(shape):
    lane = lax.broadcasted_iota(jnp.int32, shape, 1)
    return [lane // HD == head for head in range(shape[1] // HD)]


def params():
    return pltpu.CompilerParams(vmem_limit_bytes=VMEM_BYTES)


def whole(array):
    return pl.BlockSpec(array.shape, lambda *_: (0,) * len(array.shape))


SCALARS = pl.BlockSpec(memory_space=pltpu.SMEM)


def project_kernel(place_ref, *refs):
    pieces, weights = refs[:6], refs[6:10]
    cos_ref, sin_ref, low_ref, qkv_ref, w_ref, gain1_ref, gain2_ref, rows_ref = refs[10:]
    block, part = pieces[0].shape[2], w_ref.shape[1] // 3
    rows = gain1_ref.shape[1] // 8

    @pl.when(pl.program_id(0) == 0)
    def _():
        for step, piece in enumerate(weights):
            for turn in range(2):
                at = 2 * (place_ref[8] ^ step) + (place_ref[9] ^ turn)
                w_ref[pl.ds(pl.multiple_of(at * rows, rows), rows), :] = piece[turn, :rows]
                gains = piece[turn, rows:].astype(F32)
                rows_ref[0, pl.ds(at, 1), :] = gains[:1, :rows]
                rows_ref[1, pl.ds(at, 1), :] = gains[1:2, :rows]
        for out, at in ((gain1_ref, 0), (gain2_ref, 1)):
            for row in range(8):
                out[:, row * rows : (row + 1) * rows] = rows_ref[at, row : row + 1, :]

    gain = gain1_ref[...]
    index = 0
    for piece in pieces:
        for inner in range(piece.shape[0]):
            normed, _ = normalize(piece[inner, 0].astype(F32))
            low_ref[index, 0] = (normed * gain).astype(BF16)
            index += 1
    projected = dot(flat(low_ref[:, 0]), w_ref[...])
    cosine, sine = cos_ref[...], sin_ref[...]
    shape = (8, block, part)
    qkv_ref[:, 0, :, :part] = (
        (lane_rotate(projected[:, :part], cosine, sine) * HD**-0.5).astype(BF16).reshape(shape)
    )
    qkv_ref[:, 0, :, part : 2 * part] = (
        lane_rotate(projected[:, part : 2 * part], cosine, sine).astype(BF16).reshape(shape)
    )
    qkv_ref[:, 0, :, 2 * part :] = projected[:, 2 * part :].astype(BF16).reshape(shape)


def project(place, pieces, weights, cosine, sine):
    seqs, block, width = pieces[0].shape[1:]
    own = weights[0].shape[2]

    def by_seq(lead, last):
        return pl.BlockSpec((lead, 1, block, last), lambda s: (0, s, 0, 0))

    return pl.pallas_call(
        project_kernel,
        grid=(seqs,),
        in_specs=[SCALARS]
        + [by_seq(piece.shape[0], width) for piece in pieces]
        + [whole(w) for w in weights]
        + [whole(cosine), whole(sine)],
        out_specs=(
            by_seq(8, width),
            by_seq(8, own),
            pl.BlockSpec((width, own), lambda s: (0, 0)),
            pl.BlockSpec((1, width), lambda s: (0, 0)),
            pl.BlockSpec((1, width), lambda s: (0, 0)),
        ),
        out_shape=(
            jax.ShapeDtypeStruct((8, seqs, block, width), BF16),
            jax.ShapeDtypeStruct((8, seqs, block, own), BF16),
            jax.ShapeDtypeStruct((width, own), BF16),
            jax.ShapeDtypeStruct((1, width), F32),
            jax.ShapeDtypeStruct((1, width), F32),
        ),
        scratch_shapes=[pltpu.VMEM((2, 8, width // 8), F32)],
        compiler_params=params(),
        name="project",
    )(place, *pieces, *weights, cosine, sine)


def attend_kernel(place_ref, q_ref, k_ref, v_ref, att_ref, log_ref, home_ref):
    step = pl.program_id(0)
    queries, keys, values = flat(q_ref[...]), flat(k_ref[...]), flat(v_ref[...])
    attended = jnp.zeros(queries.shape, F32)
    logs = jnp.zeros(queries.shape, F32)
    for mask in head_masks(queries.shape):
        scores = dot(jnp.where(mask, queries, 0), keys, ((1,), (1,)))
        peak = jnp.max(scores, axis=1, keepdims=True)
        weights = jnp.exp(scores - peak)
        total = jnp.sum(weights, axis=1, keepdims=True)
        mixed = dot(weights.astype(BF16), values) * (1.0 / total)
        attended = jnp.where(mask, mixed, attended)
        logs = jnp.where(mask, peak + jnp.log(total), logs)
    att_ref[...] = attended.reshape(att_ref.shape)
    log_ref[...] = logs.reshape(log_ref.shape)
    low = attended.astype(BF16).reshape(att_ref.shape)
    for inner in range(2):
        home_ref[place_ref[2 * step + inner], 0] = low[inner, 0]


def attend(place, qkv, seq):
    _, _, block, own = qkv.shape
    part = own // 3
    rows = pl.BlockSpec((2, 1, block, part), lambda i: (i, 0, 0, 0))
    shape = (8, 1, block, part)
    return pl.pallas_call(
        attend_kernel,
        grid=(4,),
        in_specs=[
            SCALARS,
            pl.BlockSpec((2, 1, block, part), lambda i: (i, seq, 0, 0)),
            pl.BlockSpec((8, 1, block, part), lambda i: (0, seq, 0, 1)),
            pl.BlockSpec((8, 1, block, part), lambda i: (0, seq, 0, 2)),
        ],
        out_specs=(rows, rows, pl.BlockSpec(shape, lambda i: (0, 0, 0, 0))),
        out_shape=(
            jax.ShapeDtypeStruct(shape, F32),
            jax.ShapeDtypeStruct(shape, F32),
            jax.ShapeDtypeStruct(shape, BF16),
        ),
        compiler_params=params(),
        name="attend",
    )(place, qkv, qkv, qkv)


def branch_kernel(place_ref, *refs):
    pieces = refs[:6]
    rows_ref, tokens_ref, gain_ref, residual_ref, low_ref = refs[6:]
    total = flat(tokens_ref[...].astype(F32))
    index = 0
    for piece in pieces:
        for inner in range(piece.shape[0]):
            total += dot(flat(rows_ref[place_ref[index]]), piece[inner])
            index += 1
    normed, _ = normalize(total)
    residual_ref[...] = total.reshape(residual_ref.shape)
    low_ref[...] = (normed * gain_ref[...]).astype(BF16).reshape(low_ref.shape)


def branch(place, pieces, rows, tokens, gain):
    args = (*pieces, rows, tokens, gain)
    return pl.pallas_call(
        branch_kernel,
        in_specs=[SCALARS] + [whole(a) for a in args],
        out_shape=(
            jax.ShapeDtypeStruct(tokens.shape, F32),
            jax.ShapeDtypeStruct(tokens.shape, BF16),
        ),
        compiler_params=params(),
        name="branch",
    )(place, *args)


PIECES = (0, 1, 2, 4, 5, 7, 8)


def mlp_kernel(*refs):
    pieces = refs[:6]
    grad_ref, w_ref, low_ref, mixed_ref, lifted_ref, keep_ref, send_ref = refs[6:]
    step = pl.program_id(0)
    for at, piece in enumerate(pieces):

        @pl.when((step >= PIECES[at]) & (step < PIECES[at + 1]))
        def _(piece=piece):
            low_ref[...] = piece[...]

    hidden = w_ref.shape[1] // 2
    lifted = dot(flat(low_ref[...]), w_ref[...])
    first, second = lifted[:, :hidden], lifted[:, hidden:]
    grad_mixed = flat(grad_ref[...])
    gate = 0.5 * (1.0 + lax.erf(first * (0.5**0.5)))
    slope = gate + first * jnp.exp(first * first * -0.5) * ((2.0 * math.pi) ** -0.5)
    activated = first * gate
    mixed_ref[...] = (activated * second).astype(BF16).reshape(mixed_ref.shape)
    grad = jnp.concatenate(
        [(grad_mixed * second * slope).astype(BF16), (grad_mixed * activated).astype(BF16)],
        axis=1,
    )
    lifted_ref[...] = grad.reshape(lifted_ref.shape)
    partial = dot(grad, w_ref[...], ((1,), (1,))).astype(BF16).reshape(keep_ref.shape)

    @pl.when(step < 5)
    def _():
        keep_ref[...] = partial

    @pl.when(step >= 5)
    def _():
        send_ref[...] = partial


def mlp(pieces, grad_mixed, w):
    seqs, block, width = pieces[0].shape[1:]
    hidden = w.shape[1] // 2

    def rows(last):
        return pl.BlockSpec((1, seqs, block, last), lambda i: (i, 0, 0, 0))

    def within(start, count):
        return pl.BlockSpec(
            (1, seqs, block, width),
            lambda i: (jnp.clip(i - start, 0, count - 1), 0, 0, 0),
        )

    return pl.pallas_call(
        mlp_kernel,
        grid=(8,),
        in_specs=[within(at, piece.shape[0]) for at, piece in zip(PIECES, pieces)]
        + [rows(hidden), whole(w)],
        out_specs=(rows(width), rows(hidden), rows(2 * hidden), within(0, 5), within(5, 3)),
        out_shape=(
            jax.ShapeDtypeStruct((8, seqs, block, width), BF16),
            jax.ShapeDtypeStruct((8, seqs, block, hidden), BF16),
            jax.ShapeDtypeStruct((8, seqs, block, 2 * hidden), BF16),
            jax.ShapeDtypeStruct((5, seqs, block, width), BF16),
            jax.ShapeDtypeStruct((3, seqs, block, width), BF16),
        ),
        compiler_params=params(),
        name="mlp",
    )(*pieces, grad_mixed, w)


def out_grad_kernel(place_ref, rows_ref, grad_ref, keep_ref, send_ref):
    grads = flat(grad_ref[...])
    for index in range(8):
        part = dot(flat(rows_ref[place_ref[index]]), grads, ((0,), (0,))).astype(BF16)
        if index < 5:
            keep_ref[index] = part
        else:
            send_ref[index - 5] = part


def out_grad(place, rows, grads):
    part, width = rows.shape[-1], grads.shape[-1]
    return pl.pallas_call(
        out_grad_kernel,
        in_specs=[SCALARS, whole(rows), whole(grads)],
        out_shape=(
            jax.ShapeDtypeStruct((5, part, width), BF16),
            jax.ShapeDtypeStruct((3, part, width), BF16),
        ),
        compiler_params=params(),
        name="out_grad",
    )(place, rows, grads)


def branch_back_kernel(place_ref, *refs):
    pieces = refs[:6]
    low_ref, residual_ref, top_ref, gain_ref, grad_ref, branch_ref, home_ref, sum_ref = refs[6:]
    grad_low = flat(low_ref[...])
    normed, factor = normalize(flat(residual_ref[...]))
    sum_ref[...] = jnp.sum(grad_low * normed, axis=0, keepdims=True)
    grad = flat(top_ref[...].astype(F32)) + norm_back(grad_low * gain_ref[...], normed, factor)
    grad_ref[...] = grad.reshape(grad_ref.shape)
    low = grad.astype(BF16)
    branch_ref[...] = low.reshape(branch_ref.shape)
    index = 0
    for piece in pieces:
        for inner in range(piece.shape[0]):
            home_ref[place_ref[index]] = (
                dot(low, piece[inner], ((1,), (1,))).astype(BF16).reshape(home_ref.shape[1:])
            )
            index += 1


def branch_back(place, pieces, grad_low, residual, top, gain):
    args = (*pieces, grad_low, residual, top, gain)
    seqs, block, width = residual.shape
    return pl.pallas_call(
        branch_back_kernel,
        in_specs=[SCALARS] + [whole(a) for a in args],
        out_shape=(
            jax.ShapeDtypeStruct(residual.shape, F32),
            jax.ShapeDtypeStruct(residual.shape, BF16),
            jax.ShapeDtypeStruct((8, seqs, block, pieces[0].shape[1]), BF16),
            jax.ShapeDtypeStruct((1, width), F32),
        ),
        compiler_params=params(),
        name="branch_back",
    )(place, *args)


def attend_back_kernel(
    place_ref, q_ref, k_ref, v_ref, grad_ref, att_ref, log_ref, cosq_ref, sinq_ref, cos_ref,
    sin_ref, w_ref, low_ref, *refs, seq, last,
):
    if last:
        before_ref, keep_ref, send_ref, grad_w_ref, gain_ref, proj_ref, sum_k, sum_v = refs
    else:
        keep_ref, send_ref, before_ref, proj_ref, sum_k, sum_v = refs
    step = pl.program_id(0)
    block, part = q_ref.shape[2], q_ref.shape[3]

    @pl.when(step == 0)
    def _():
        sum_k[...] = jnp.zeros_like(sum_k)
        sum_v[...] = jnp.zeros_like(sum_v)

    queries, keys, values = flat(q_ref[...]), flat(k_ref[...]), flat(v_ref[...])
    grads = jnp.concatenate([grad_ref[place_ref[2 * step + inner], seq] for inner in range(2)])
    along = (grads.astype(F32) * flat(att_ref[...])).T
    logs = flat(log_ref[...]).T
    grad_queries = jnp.zeros(queries.shape, F32)
    for head, mask in enumerate(head_masks(queries.shape)):
        own_q = jnp.where(mask, queries, 0)
        own_g = jnp.where(mask, grads, 0)
        scores = dot(keys, own_q, ((1,), (1,)))
        weights = jnp.exp(scores - logs[head * HD : head * HD + 1])
        lifted = dot(values, own_g, ((1,), (1,)))
        row = jnp.sum(along[head * HD : (head + 1) * HD], axis=0, keepdims=True)
        grad_scores = (weights * (lifted - row)).astype(BF16)
        sum_k[...] += dot(grad_scores, own_q)
        sum_v[...] += dot(weights.astype(BF16), own_g)
        grad_queries = jnp.where(mask, dot(grad_scores, keys, ((0,), (0,))), grad_queries)
    grad_queries = lane_rotate(grad_queries * HD**-0.5, cosq_ref[...], -sinq_ref[...])
    rows = pl.multiple_of(step * 2 * block, 2 * block)
    proj_ref[pl.ds(rows, 2 * block), :part] = grad_queries.astype(BF16)

    @pl.when(step == 3)
    def _():
        grad_keys = lane_rotate(sum_k[...], cos_ref[...], -sin_ref[...])
        proj_ref[:, part : 2 * part] = grad_keys.astype(BF16)
        proj_ref[:, 2 * part :] = sum_v[...].astype(BF16)
        partial = dot(proj_ref[...], w_ref[...], ((1,), (1,))).astype(BF16)
        keep_ref[:, 0] = partial[: 5 * block].reshape(5, block, -1)
        send_ref[:, 0] = partial[5 * block :].reshape(3, block, -1)
        grad_w = dot(proj_ref[...], flat(low_ref[...]), ((0,), (0,)))
        if last:
            grad_w = (grad_w + before_ref[...]).T
            grad_w_ref[...] = grad_w.astype(BF16)
            along_w = jnp.sum(grad_w * w_ref[...].astype(F32), axis=1, keepdims=True)
            gain_ref[...] = jnp.broadcast_to(along_w, (w_ref.shape[0], 128)).T[:8]
        else:
            before_ref[...] = grad_w


def attend_back(place, qkv, grads, attended, logs, cosine, sine, w, low, seq, before=None):
    _, _, block, own = qkv.shape
    part, width = own // 3, w.shape[0]
    last = before is not None
    rows = pl.BlockSpec((2, 1, block, part), lambda i: (i, 0, 0, 0))
    angles = pl.BlockSpec((2 * block, part), lambda i: (i, 0))

    def full(*shape):
        return pl.BlockSpec(shape, lambda i: (0,) * len(shape))

    args = [place, qkv, qkv, qkv, grads, attended, logs, cosine, sine, cosine, sine, w, low]
    in_specs = [
        SCALARS,
        pl.BlockSpec((2, 1, block, part), lambda i: (i, seq, 0, 0)),
        pl.BlockSpec((8, 1, block, part), lambda i: (0, seq, 0, 1)),
        pl.BlockSpec((8, 1, block, part), lambda i: (0, seq, 0, 2)),
        whole(grads),
        rows,
        rows,
        angles,
        angles,
        whole(cosine),
        whole(sine),
        whole(w),
        pl.BlockSpec((8, 1, block, width), lambda i: (0, seq, 0, 0)),
    ]
    shapes = [((5, 1, block, width), BF16), ((3, 1, block, width), BF16)]
    if last:
        args.append(before)
        in_specs.append(whole(before))
        shapes += [((width, own), BF16), ((8, width), F32)]
    else:
        shapes += [((own, width), F32)]
    return pl.pallas_call(
        functools.partial(attend_back_kernel, seq=seq, last=last),
        grid=(4,),
        in_specs=in_specs,
        out_specs=tuple(full(*shape) for shape, _ in shapes),
        out_shape=tuple(jax.ShapeDtypeStruct(shape, kind) for shape, kind in shapes),
        scratch_shapes=[
            pltpu.VMEM((8 * block, own), BF16),
            pltpu.VMEM((8 * block, part), F32),
            pltpu.VMEM((8 * block, part), F32),
        ],
        compiler_params=params(),
        name="attend_back",
    )(*args)


class Group:
    def __init__(self):
        self.heads = lax.axis_size("head")
        self.dp = lax.axis_size("dp")
        self.ctx_at = lax.axis_index("ctx")
        self.head_at = lax.axis_index("head")
        self.dp_at = lax.axis_index("dp")
        self.at = self.ctx_at * self.heads + self.head_at
        near, far = [], []
        for c in range(2):
            for h in range(self.heads):
                x, y = (c ^ 1) * self.heads + h, c * self.heads + (h ^ 2)
                near.append((c * self.heads + h, x if h % 2 == 0 else y))
                far.append((c * self.heads + h, y if h % 2 == 0 else x))
        self.near, self.far = near, far

    def order(self):
        first = jnp.where(self.head_at % 2 == 0, 4, 2)
        second = 6 - first
        return jnp.stack(
            [self.at ^ bits for bits in (0, 1, first, first ^ 1, 6, second ^ 1, second, 7)]
        )

    def swap(self, values, bit):
        if bit == 4:
            return lax.ppermute(values, "ctx", [(0, 1), (1, 0)])
        return lax.ppermute(values, "head", [(i, i ^ bit) for i in range(self.heads)])

    def mate(self, values):
        return self.swap(values, 1)

    def to_near(self, values):
        return lax.ppermute(values, GROUP, self.near)

    def to_far(self, values):
        return lax.ppermute(values, GROUP, self.far)

    def rows_in(self, values, place):
        pairs = [
            (place[h] * self.heads + d, d * self.heads + h)
            for d in range(self.dp)
            for h in range(self.heads)
        ]
        return lax.ppermute(values, ("dp", "head"), pairs)

    def rows_back(self, values, place):
        pairs = [
            (d * self.heads + h, place[h] * self.heads + d)
            for d in range(self.dp)
            for h in range(self.heads)
        ]
        return lax.ppermute(values, ("dp", "head"), pairs)

    def across(self, values, step):
        return lax.ppermute(values, "dp", [(i, i ^ step) for i in range(self.dp)])

    def scatter_dp(self, values):
        step = self.dp // 2
        while step:
            halves = values.reshape(2, step, *values.shape[1:])
            bit = (self.dp_at // step) % 2
            sent = self.across(pick(halves, 1 - bit, 0).astype(BF16), step)
            values = pick(halves, bit, 0).astype(F32) + sent.astype(F32)
            step //= 2
        return values[0]

    def total(self, values):
        for bit in (1, 2, 4):
            values = values + self.swap(values, bit)
        step = 1
        while step < self.dp:
            values = values + self.across(values, step)
            step *= 2
        return values


def pick(array, index, axis):
    return lax.dynamic_index_in_dim(array, index, axis, keepdims=False)


def after(values, *earlier):
    return lax.optimization_barrier((values, earlier))[0]


def wide(values):
    return values.astype(F32)


def local_split(tokens, cotangent, w_qkv, w_attn_out, w_in, w_mlp_out, norm_gain1, norm_gain2):
    seqs, block, width = tokens.shape
    group = Group()
    heads, dp = group.heads, group.dp
    at_c, at_h = group.ctx_at, group.head_at
    parts = 2 * heads
    hidden = w_in.shape[1] // 2 // parts
    padded = -(-hidden // 128) * 128
    own_width = width // parts
    half = heads // 2
    rows_here = w_qkv.shape[0]
    place = [2 * (h % half) + h // half for h in range(heads)]
    straight = list(range(heads))
    order = group.order()
    scalars = jnp.concatenate([order, jnp.stack([group.dp_at, at_c])]).astype(jnp.int32)
    mate, near, far = group.mate, group.to_near, group.to_far

    def in_order(own, other):
        return jnp.where(at_c == 0, jnp.stack([own, other]), jnp.stack([other, own]))

    def exchange(values):
        return lax.all_to_all(values, GROUP, split_axis=0, concat_axis=0, tiled=True)


    gains = jnp.pad(
        jnp.stack([norm_gain1, norm_gain2]), ((0, 14), (0, 3 * own_width - rows_here))
    )
    qkv_view = w_qkv.reshape(rows_here, 3, width)

    def qkv_part(at):
        start = (2 * at_h + at) * own_width
        cut = lax.dynamic_slice_in_dim(qkv_view, start, own_width, 2)
        return jnp.concatenate([cut.reshape(rows_here, 3 * own_width), gains])

    x_own = tokens[None]
    x_mate = mate(x_own)
    qkv_other, qkv_own = qkv_part(1 - at_c), qkv_part(at_c)
    x_chip = jnp.concatenate([x_own, after(x_mate, qkv_other, qkv_own)])
    x_near = near(x_chip)
    qkv_cross = group.swap(after(qkv_other, x_chip), 4)
    qkv_pair = jnp.stack([qkv_own, qkv_cross])
    qkv_pieces = [qkv_pair] + [group.across(qkv_pair, step) for step in range(1, dp)]
    out_rows = group.rows_in(after(w_attn_out, qkv_pair), straight)

    in_view = after(w_in, qkv_pair).reshape(rows_here, 2, heads, 2, hidden)
    in_view = pick(in_view, 2 * (at_h % half) + at_h // half, 2)

    def in_part(at):
        cut = pick(in_view, at, 2)
        return jnp.pad(cut, ((0, 0), (0, 0), (0, padded - hidden))).reshape(rows_here, 2 * padded)

    in_other, in_own = in_part(1 - at_c), in_part(at_c)
    in_cross = group.swap(in_other, 4)
    positions = after(order, qkv_pair)[:, None] * block + jnp.arange(block, dtype=jnp.int32)
    lane = jnp.arange(own_width, dtype=jnp.int32)
    frequency = jnp.exp(
        (lane % (HD // 2)).astype(F32) * (-math.log(ROPE_BASE) / (HD // 2))
    )
    angles = wide(positions.reshape(-1))[:, None] * frequency[None, :]
    cosine = jnp.cos(angles)
    sine = jnp.sin(angles) * jnp.where(lane % HD < HD // 2, -1.0, 1.0)[None, :]

    x_near = after(x_near, in_other, in_own, cosine, sine)
    x_far = far(x_near[:1])
    x_near_mate = mate(x_near)
    in_pair = in_order(in_own, after(in_cross, x_near))
    out_own = after(out_rows, x_near)[None]
    out_mate = mate(out_own)
    cot_own = after(cotangent, x_near)[None]
    cot_mate = mate(cot_own)
    out_chip = jnp.concatenate([out_own, out_mate])
    cot_chip = jnp.concatenate([cot_own, cot_mate])
    x_far = after(x_far, in_pair, out_chip, cot_chip)
    x_far_mate = mate(x_far)

    out_near = near(after(out_chip, x_far))
    cot_near = near(after(cot_chip, x_far))
    in_pair = after(in_pair, x_far, *qkv_pieces)
    weight_in = lax.all_gather(in_pair, "dp", axis=0).reshape(width, -1)
    x_pieces = (x_own, x_mate, x_near, x_far, x_near_mate, after(x_far_mate, in_pair))
    low1, qkv, weight_qkv, gain_one, gain_two = project(
        scalars, x_pieces, qkv_pieces, cosine, sine
    )

    weight_mlp = group.rows_in(after(w_mlp_out, qkv), place)
    out_near = after(out_near, qkv)
    out_far, out_near_mate = far(out_near[:1]), mate(out_near)
    att_0, log_0, home_0 = attend(scalars, after(qkv, out_near), 0)
    cot_near = after(cot_near, home_0)
    cot_far, cot_near_mate = far(cot_near[:1]), mate(cot_near)
    out_far = after(out_far, home_0)
    out_far_mate = mate(out_far)
    out_pieces = (out_own, out_mate, out_near, out_far, out_near_mate, out_far_mate)
    att_1, log_1, home_1 = attend(scalars, after(qkv, cot_near, out_far), 1)
    home = jnp.concatenate([home_0, home_1], axis=1)
    att_rows = exchange(home)
    cot_far = after(cot_far, home)
    cot_far_mate = mate(cot_far)
    residual, low2 = branch(
        scalars, out_pieces, after(att_rows, cot_far), tokens, gain_two
    )

    low_own = low2[None]
    low_mate = mate(low_own)
    low_near = near(jnp.concatenate([low_own, low_mate]))
    cot_all = jnp.concatenate(
        [
            cot_own,
            cot_mate,
            cot_near,
            cot_far,
            cot_near_mate,
            after(cot_far_mate, low_mate),
        ]
    )
    weight_mlp = jnp.pad(weight_mlp, ((0, padded - hidden), (0, 0)))
    grad_mixed = dot(flat(cot_all), weight_mlp, ((1,), (1,)))
    low_near = after(low_near, grad_mixed)
    low_far, low_near_mate = far(low_near[:1]), mate(low_near)
    low_pieces = (low_own, low_mate, low_near, low_far, low_near_mate, mate(low_far))
    low2_all, mixed, grad_lifted, keep, send = mlp(
        low_pieces, grad_mixed.reshape(8, seqs, block, padded), weight_in
    )

    def over_tokens(left, right):
        return dot(flat(left), flat(right), ((0,), (0,)))

    def scatter(values):
        return lax.psum_scatter(values.astype(BF16), "dp", scatter_dimension=0, tiled=True)

    def columns_first(values):
        return jnp.moveaxis(values.reshape(values.shape[0], dp, -1), 1, 0)

    met = mate(send)
    grad_mlp = columns_first(over_tokens(after(mixed, send), cot_all)[:hidden]).astype(BF16)
    grad_mlp = scatter(grad_mlp)[0]
    met = after(met, grad_mlp)
    last = (wide(keep[4]) + wide(met[2])).astype(BF16)
    last_far = far(last)
    cut = 5 * seqs * block
    mixed_flat = flat(after(mixed, last))
    out_keep = dot(mixed_flat[:cut], weight_mlp).astype(BF16).reshape(5, seqs, block, width)
    out_send = dot(mixed_flat[cut:], weight_mlp).astype(BF16).reshape(3, seqs, block, width)
    last_far = after(last_far, out_keep, out_send)
    chip = jnp.stack([wide(keep[2]) + wide(met[0]) + wide(last_far), wide(keep[3]) + wide(met[1])])
    chip = chip.astype(BF16)
    chip_near = near(chip)
    out_met = mate(after(out_send, chip))
    grad_in = over_tokens(low2_all, after(grad_lifted, chip)).astype(BF16)
    chip_near = after(chip_near, grad_in)
    grad_in = scatter(grad_in)
    home = mate((wide(keep[1]) + wide(chip_near[1])).astype(BF16))
    grad_low2 = wide(keep[0]) + wide(chip_near[0]) + wide(home)

    grad_residual, grad_branch, home, gain2_sum = branch_back(
        scalars, out_pieces, grad_low2, residual, cotangent, gain_two
    )
    grad_home = exchange(home)

    rows_keep, rows_send = out_grad(scalars, after(att_rows, home), grad_branch)
    rows_met = mate(rows_send)
    out_last = (wide(out_keep[4]) + wide(after(out_met, home)[2])).astype(BF16)
    rows_last = (wide(rows_keep[4]) + wide(rows_met[2])).astype(BF16)
    grad_home = after(grad_home, out_last, rows_last)
    out_far2, rows_far = far(after(out_last, grad_home)), far(after(rows_last, grad_home))
    keep_0, send_0, before = attend_back(
        scalars, qkv, grad_home, att_0, log_0, cosine, sine, weight_qkv, low1, 0
    )
    met_0 = mate(send_0)
    out_far2, rows_far = after((out_far2, rows_far), send_0)
    out_chip = jnp.stack(
        [
            wide(out_keep[2]) + wide(out_met[0]) + wide(out_far2),
            wide(out_keep[3]) + wide(out_met[1]),
        ]
    ).astype(BF16)
    rows_chip = jnp.stack(
        [
            wide(rows_keep[2]) + wide(rows_met[0]) + wide(rows_far),
            wide(rows_keep[3]) + wide(rows_met[1]),
        ]
    ).astype(BF16)
    out_chip_near, rows_chip_near = near(out_chip), near(rows_chip)
    keep_1, send_1, grad_qkv, gain1_sum = attend_back(
        scalars, qkv, after(grad_home, out_chip, rows_chip), att_1, log_1, cosine, sine,
        weight_qkv, low1, 1, before,
    )

    met_1 = mate(send_1)
    grad_qkv = scatter(grad_qkv)

    def both(index, at):
        return jnp.concatenate(
            [wide(keep_0[index]) + wide(met_0[at]), wide(keep_1[index]) + wide(met_1[at])]
        )

    last = both(4, 2).astype(BF16)
    last_far = far(last)
    rows_chip_near = after(rows_chip_near, last)
    out_chip_near = after(out_chip_near, last)
    rows_home = mate((wide(rows_keep[1]) + wide(rows_chip_near[1])).astype(BF16))
    out_home = mate((wide(out_keep[1]) + wide(out_chip_near[1])).astype(BF16))
    gain1_sum = gain1_sum[0] / gain_one[0]
    sums = jnp.stack([gain1_sum, gain2_sum[0]]).reshape(-1, 128)
    last_far = after(last_far, sums)
    chip = jnp.stack([both(2, 0) + wide(last_far), both(3, 1)]).astype(BF16)
    chip_near = near(chip)
    result = residual + wide(out_keep[0]) + wide(out_chip_near[0]) + wide(after(out_home, chip))
    result = result.astype(BF16)
    grad_out = wide(rows_keep[0]) + wide(rows_chip_near[0]) + wide(after(rows_home, chip))
    grad_out = group.scatter_dp(columns_first(grad_out)).astype(BF16)
    grad_out = wide(group.rows_back(grad_out, straight))
    sums = group.total(sums).reshape(2, -1)
    home = mate(
        (jnp.concatenate([wide(keep_0[1]), wide(keep_1[1])]) + wide(chip_near[1])).astype(BF16)
    )
    grad_low1 = jnp.concatenate([wide(keep_0[0]), wide(keep_1[0])]) + wide(chip_near[0])
    grad_low1 = grad_low1 + wide(home)
    normed1, factor1 = normalize(wide(tokens))
    grad_input = grad_residual + norm_back(grad_low1 * gain_one, normed1, factor1)

    grad_mlp = wide(group.rows_back(grad_mlp, place))

    def rows_here_of(values):
        pair = values.reshape(2, rows_here, -1)
        own = pick(pair, at_c, 0)
        other = group.swap(pick(pair, 1 - at_c, 0), 4)
        return in_order(own, other)

    grad_in = rows_here_of(grad_in)
    grad_in = jnp.stack([grad_in[..., :hidden], grad_in[..., padded : padded + hidden]])
    late = at_h // half
    stays = pick(grad_in, late, 0)
    comes = group.swap(pick(grad_in, 1 - late, 0), half)
    grad_in = jnp.where(
        late == 0, jnp.concatenate([stays, comes]), jnp.concatenate([comes, stays])
    )
    grad_in = wide(jnp.moveaxis(grad_in, 0, 1).reshape(rows_here, -1))

    per_device = width // (dp * parts)
    start = (group.dp_at * parts + group.at) * per_device
    grad_gain1, grad_gain2 = (
        lax.dynamic_slice_in_dim(sums[i], start, per_device, 0) for i in range(2)
    )
    grad_qkv = rows_here_of(grad_qkv).reshape(2, rows_here, 3, own_width)
    grad_qkv = jnp.moveaxis(grad_qkv, 2, 0)
    odd = at_h % 2
    stays = pick(grad_qkv, odd + late, 0)
    core = group.swap(pick(grad_qkv, 1 - odd + late, 0), 1)
    chip = group.swap(pick(grad_qkv, 2 - 2 * late, 0), 2)
    grad_qkv = jnp.where(
        odd == 0, jnp.concatenate([stays, core, chip]), jnp.concatenate([chip, core, stays])
    )
    grad_qkv = wide(jnp.moveaxis(grad_qkv, 0, 1).reshape(rows_here, -1))

    return (
        result,
        grad_input,
        grad_qkv,
        grad_out,
        grad_in,
        grad_mlp,
        grad_gain1,
        grad_gain2,
    )


def local(tokens, cotangent, w_qkv, w_attn_out, w_in, w_mlp_out, norm_gain1, norm_gain2):
    args = (tokens, cotangent, w_qkv, w_attn_out, w_in, w_mlp_out, norm_gain1, norm_gain2)
    sizes = [lax.axis_size(axis) for axis in ("dp", "ctx", "head")]
    if sizes == [4, 2, 4] and tokens.shape[2] == 8 * 2 * HD and tokens.shape[1] % 16 == 0:
        return local_split(*args)
    return local_general(*args)


def solution(mesh):
    in_specs = (
        P("dp", ("ctx", "head"), None),
        P("dp", ("ctx", "head"), None),
        P(("dp", "ctx"), None),
        P(("dp", "ctx"), None),
        P(("dp", "ctx"), None),
        P(("dp", "ctx"), None),
        P(("dp", "ctx")),
        P(("dp", "ctx")),
    )
    out_specs = (
        P("dp", ("ctx", "head"), None),
        P("dp", ("ctx", "head"), None),
        P(("dp", "ctx"), "head"),
        P(("dp", "ctx"), "head"),
        P(("dp", "ctx"), "head"),
        P(("dp", "ctx"), "head"),
        P(("dp", "ctx", "head")),
        P(("dp", "ctx", "head")),
    )
    return jax.shard_map(local, mesh=mesh, in_specs=in_specs, out_specs=out_specs, check_vma=False)
```

```python
import functools
import math

import jax
import jax.numpy as jnp
from jax import lax
from jax.experimental import pallas as pl
from jax.experimental.pallas import tpu as pltpu
from jax.sharding import PartitionSpec as P

HD = 64


EPSILON = 1e-05
ROPE_BASE = 160000.0


def normalize(values):
    centre = jnp.mean(values, axis=-1, keepdims=True)
    shifted = values - centre
    spread = jnp.mean(shifted * shifted, axis=-1, keepdims=True)
    factor = lax.rsqrt(spread + EPSILON)
    return (shifted * factor, factor)


def norm_back(grad_normed, normed, factor):
    grad_centre = jnp.mean(grad_normed, axis=-1, keepdims=True)
    grad_along = jnp.mean(grad_normed * normed, axis=-1, keepdims=True)
    return (grad_normed - grad_centre - normed * grad_along) * factor


def rope_tables(positions, half_size):
    frequency = jnp.exp(
        jnp.arange(half_size, dtype=jnp.float32) * (-math.log(ROPE_BASE) / half_size)
    )
    angles = positions[:, None] * frequency[None, :]
    return (jnp.cos(angles), jnp.sin(angles))


def rotate(values, cosine, sine_table, direction):
    half_size = cosine.shape[-1]
    first_half = values[..., :half_size]
    second_half = values[..., half_size:]
    cos_part = cosine[:, None, :]
    sin_part = sine_table[:, None, :] * direction
    return jnp.concatenate(
        [
            first_half * cos_part - second_half * sin_part,
            second_half * cos_part + first_half * sin_part,
        ],
        axis=-1,
    )


def block_scores(queries4, keys_block, scale):
    keys4 = keys_block.reshape(
        keys_block.shape[0], keys_block.shape[1], queries4.shape[2], queries4.shape[3]
    )
    return (
        jnp.einsum("sqgd,skgd->sgqk", queries4, keys4, preferred_element_type=jnp.float32) * scale
    )


def attend_forward(queries4, keys_all, values_all, key_rows, scale):
    seqs_here, query_rows, groups, head_size = queries4.shape
    turns = keys_all.shape[1] // key_rows

    def statistics(turn, carry):
        row_peak, row_total = carry
        keys_block = lax.dynamic_slice_in_dim(keys_all, turn * key_rows, key_rows, 1)
        scores = block_scores(queries4, keys_block, scale)
        new_peak = jnp.maximum(row_peak, jnp.max(scores, axis=-1))
        row_total = row_total * jnp.exp(row_peak - new_peak) + jnp.sum(
            jnp.exp(scores - new_peak[..., None]), axis=-1
        )
        return (new_peak, row_total)

    start_peak = jnp.full((seqs_here, groups, query_rows), -1e30, jnp.float32)
    row_peak, row_total = lax.fori_loop(
        0, turns, statistics, (start_peak, jnp.zeros_like(start_peak))
    )
    log_total = row_peak + jnp.log(row_total)

    def accumulate(turn, running):
        keys_block = lax.dynamic_slice_in_dim(keys_all, turn * key_rows, key_rows, 1)
        values_block = lax.dynamic_slice_in_dim(values_all, turn * key_rows, key_rows, 1).reshape(
            seqs_here, key_rows, groups, head_size
        )
        weights = jnp.exp(block_scores(queries4, keys_block, scale) - log_total[..., None]).astype(
            jnp.bfloat16
        )
        return running + jnp.einsum(
            "sgqk,skgd->sqgd", weights, values_block, preferred_element_type=jnp.float32
        )

    attended = lax.fori_loop(
        0, turns, accumulate, jnp.zeros((seqs_here, query_rows, groups, head_size), jnp.float32)
    )
    return (attended, log_total)


def attend_backward(queries4, keys_all, values_all, grad_out4, log_total, along, key_rows, scale):
    seqs_here, query_rows, groups, head_size = queries4.shape
    length = keys_all.shape[1]
    width_group = groups * head_size
    turns = length // key_rows

    def step_back(turn, carry):
        grad_queries, grad_keys, grad_values = carry
        keys_block = lax.dynamic_slice_in_dim(keys_all, turn * key_rows, key_rows, 1)
        keys4 = keys_block.reshape(seqs_here, key_rows, groups, head_size)
        values4 = lax.dynamic_slice_in_dim(values_all, turn * key_rows, key_rows, 1).reshape(
            seqs_here, key_rows, groups, head_size
        )
        weights = jnp.exp(block_scores(queries4, keys_block, scale) - log_total[..., None])
        grad_weights = jnp.einsum(
            "sqgd,skgd->sgqk", grad_out4, values4, preferred_element_type=jnp.float32
        )
        grad_scores = (weights * (grad_weights - along[..., None])).astype(jnp.bfloat16)
        grad_queries = grad_queries + jnp.einsum(
            "sgqk,skgd->sqgd", grad_scores, keys4, preferred_element_type=jnp.float32
        )
        key_part = (
            jnp.einsum("sgqk,sqgd->skgd", grad_scores, queries4, preferred_element_type=jnp.float32)
            * scale
        )
        value_part = jnp.einsum(
            "sgqk,sqgd->skgd",
            weights.astype(jnp.bfloat16),
            grad_out4,
            preferred_element_type=jnp.float32,
        )
        grad_keys = lax.dynamic_update_slice_in_dim(
            grad_keys, key_part.reshape(seqs_here, key_rows, width_group), turn * key_rows, 1
        )
        grad_values = lax.dynamic_update_slice_in_dim(
            grad_values, value_part.reshape(seqs_here, key_rows, width_group), turn * key_rows, 1
        )
        return (grad_queries, grad_keys, grad_values)

    start = (
        jnp.zeros((seqs_here, query_rows, groups, head_size), jnp.float32),
        jnp.zeros((seqs_here, length, width_group), jnp.float32),
        jnp.zeros((seqs_here, length, width_group), jnp.float32),
    )
    grad_queries, grad_keys, grad_values = lax.fori_loop(0, turns, step_back, start)
    return (grad_queries * scale, grad_keys, grad_values)


def local_general(tokens, cotangent, w_qkv, w_attn_out, w_in, w_mlp_out, norm_gain1, norm_gain2):
    seqs_here, block_rows, width = tokens.shape
    count_rows = seqs_here * block_rows
    heads_all = width // HD
    head_devices = lax.axis_size("head")
    group_devices = lax.axis_size(("dp", "ctx"))
    groups = heads_all // head_devices
    width_group = groups * HD
    scale = HD ** (-0.5)
    ff_width = w_in.shape[1] // 2
    full_qkv, full_out, full_in, full_mlp, gain_one, gain_two = (
        lax.all_gather(w_qkv, ("dp", "ctx"), axis=0, tiled=True),
        lax.all_gather(w_attn_out, ("dp", "ctx"), axis=0, tiled=True),
        lax.all_gather(w_in, ("dp", "ctx"), axis=0, tiled=True),
        lax.all_gather(w_mlp_out, ("dp", "ctx"), axis=0, tiled=True),
        lax.all_gather(norm_gain1, ("dp", "ctx"), axis=0, tiled=True),
        lax.all_gather(norm_gain2, ("dp", "ctx"), axis=0, tiled=True),
    )
    x_in = tokens.astype(jnp.float32).reshape(count_rows, width)
    normed1, factor1 = normalize(x_in)
    lowered1 = (normed1 * gain_one.astype(jnp.float32)).astype(jnp.bfloat16)
    projected = jnp.dot(lowered1, full_qkv, preferred_element_type=jnp.float32).reshape(
        seqs_here, block_rows, 3, heads_all, HD
    )
    first_pos = (lax.axis_index("ctx") * head_devices + lax.axis_index("head")) * block_rows
    positions = (first_pos + jnp.arange(block_rows, dtype=jnp.int32)).astype(jnp.float32)
    cosine, sine_table = rope_tables(positions, HD // 2)
    queries = (
        rotate(projected[:, :, 0], cosine, sine_table, 1.0)
        .astype(jnp.bfloat16)
        .reshape(seqs_here, block_rows, width)
    )
    keys_local = (
        rotate(projected[:, :, 1], cosine, sine_table, 1.0)
        .astype(jnp.bfloat16)
        .reshape(seqs_here, block_rows, width)
    )
    values_local = projected[:, :, 2].astype(jnp.bfloat16).reshape(seqs_here, block_rows, width)
    queries_h, keys_h, values_h = (
        lax.all_to_all(queries, "head", split_axis=2, concat_axis=1, tiled=True),
        lax.all_to_all(keys_local, "head", split_axis=2, concat_axis=1, tiled=True),
        lax.all_to_all(values_local, "head", split_axis=2, concat_axis=1, tiled=True),
    )
    query_rows = queries_h.shape[1]
    queries4 = queries_h.reshape(seqs_here, query_rows, groups, HD)
    keys_all, values_all = (
        lax.all_gather(keys_h, "ctx", axis=1, tiled=True),
        lax.all_gather(values_h, "ctx", axis=1, tiled=True),
    )
    key_rows = math.gcd(keys_all.shape[1], 1024)
    attended, log_total = attend_forward(queries4, keys_all, values_all, key_rows, scale)
    attended_low = attended.astype(jnp.bfloat16).reshape(seqs_here, query_rows, width_group)
    back_rows = lax.all_to_all(
        attended_low, "head", split_axis=1, concat_axis=2, tiled=True
    ).reshape(count_rows, width)
    residual = x_in + jnp.dot(back_rows, full_out, preferred_element_type=jnp.float32)
    normed2, factor2 = normalize(residual)
    lowered2 = (normed2 * gain_two.astype(jnp.float32)).astype(jnp.bfloat16)
    lifted = jnp.dot(lowered2, full_in, preferred_element_type=jnp.float32)
    first_part = lifted[:, :ff_width]
    second_part = lifted[:, ff_width:]
    activated, gelu_pullback = jax.vjp(
        lambda entries: jax.nn.gelu(entries, approximate=False), first_part
    )
    mixed = (activated * second_part).astype(jnp.bfloat16)
    result = (residual + jnp.dot(mixed, full_mlp, preferred_element_type=jnp.float32)).astype(
        jnp.bfloat16
    )
    full_qkv, full_out, full_in, full_mlp, gain_one, gain_two = (
        lax.all_gather(w_qkv, ("dp", "ctx"), axis=0, tiled=True),
        lax.all_gather(w_attn_out, ("dp", "ctx"), axis=0, tiled=True),
        lax.all_gather(w_in, ("dp", "ctx"), axis=0, tiled=True),
        lax.all_gather(w_mlp_out, ("dp", "ctx"), axis=0, tiled=True),
        lax.all_gather(norm_gain1, ("dp", "ctx"), axis=0, tiled=True),
        lax.all_gather(norm_gain2, ("dp", "ctx"), axis=0, tiled=True),
    )
    keys_all, values_all = (
        lax.all_gather(keys_h, "ctx", axis=1, tiled=True),
        lax.all_gather(values_h, "ctx", axis=1, tiled=True),
    )
    grad_top = cotangent.reshape(count_rows, width)
    grad_mlp = jnp.einsum("nf,nd->fd", mixed, grad_top, preferred_element_type=jnp.float32)
    grad_mixed = jnp.einsum("nd,fd->nf", grad_top, full_mlp, preferred_element_type=jnp.float32)
    grad_first = gelu_pullback(grad_mixed * second_part)[0]
    grad_lifted = jnp.concatenate([grad_first, grad_mixed * activated], axis=-1).astype(
        jnp.bfloat16
    )
    grad_inner = jnp.einsum("nd,nf->df", lowered2, grad_lifted, preferred_element_type=jnp.float32)
    grad_lowered2 = jnp.einsum(
        "nf,df->nd", grad_lifted, full_in, preferred_element_type=jnp.float32
    )
    grad_two = jnp.sum(grad_lowered2 * normed2, axis=0)
    grad_residual = grad_top.astype(jnp.float32) + norm_back(
        grad_lowered2 * gain_two.astype(jnp.float32), normed2, factor2
    )
    grad_branch = grad_residual.astype(jnp.bfloat16)
    grad_outproj = jnp.einsum(
        "nd,ne->de", back_rows, grad_branch, preferred_element_type=jnp.float32
    )
    grad_attended = jnp.einsum(
        "ne,de->nd", grad_branch, full_out, preferred_element_type=jnp.float32
    ).astype(jnp.bfloat16)
    grad_attended_h = lax.all_to_all(
        grad_attended.reshape(seqs_here, block_rows, width),
        "head",
        split_axis=2,
        concat_axis=1,
        tiled=True,
    )
    grad_out4 = grad_attended_h.reshape(seqs_here, query_rows, groups, HD)
    along = jnp.transpose(jnp.sum(grad_out4.astype(jnp.float32) * attended, axis=-1), (0, 2, 1))
    grad_queries, grad_keys_all, grad_values_all = attend_backward(
        queries4, keys_all, values_all, grad_out4, log_total, along, key_rows, scale
    )
    grad_keys_sum, grad_values_sum = (
        lax.psum_scatter(
            grad_keys_all.astype(jnp.bfloat16), "ctx", scatter_dimension=1, tiled=True
        ).astype(jnp.float32),
        lax.psum_scatter(
            grad_values_all.astype(jnp.bfloat16), "ctx", scatter_dimension=1, tiled=True
        ).astype(jnp.float32),
    )
    grad_q_low = grad_queries.astype(jnp.bfloat16).reshape(seqs_here, query_rows, width_group)
    grad_q_tok, grad_k_tok, grad_v_tok = (
        lax.all_to_all(grad_q_low, "head", split_axis=1, concat_axis=2, tiled=True),
        lax.all_to_all(
            grad_keys_sum.astype(jnp.bfloat16), "head", split_axis=1, concat_axis=2, tiled=True
        ),
        lax.all_to_all(
            grad_values_sum.astype(jnp.bfloat16), "head", split_axis=1, concat_axis=2, tiled=True
        ),
    )
    unrot_q = rotate(
        grad_q_tok.astype(jnp.float32).reshape(seqs_here, block_rows, heads_all, HD),
        cosine,
        sine_table,
        -1.0,
    )
    unrot_k = rotate(
        grad_k_tok.astype(jnp.float32).reshape(seqs_here, block_rows, heads_all, HD),
        cosine,
        sine_table,
        -1.0,
    )
    grad_projected = jnp.concatenate(
        [
            unrot_q.reshape(count_rows, width),
            unrot_k.reshape(count_rows, width),
            grad_v_tok.astype(jnp.float32).reshape(count_rows, width),
        ],
        axis=-1,
    ).astype(jnp.bfloat16)
    grad_project = jnp.einsum(
        "nd,nf->df", lowered1, grad_projected, preferred_element_type=jnp.float32
    )
    grad_lowered1 = jnp.einsum(
        "nf,df->nd", grad_projected, full_qkv, preferred_element_type=jnp.float32
    )
    grad_one = jnp.sum(grad_lowered1 * normed1, axis=0)
    grad_input = grad_residual + norm_back(
        grad_lowered1 * gain_one.astype(jnp.float32), normed1, factor1
    )
    pieces_one = grad_one.reshape(group_devices, head_devices, -1)
    pieces_two = grad_two.reshape(group_devices, head_devices, -1)
    part_qkv, part_out, part_in, part_mlp, part_one, part_two = (
        lax.psum_scatter(
            grad_project.astype(jnp.bfloat16), ("dp", "ctx"), scatter_dimension=0, tiled=True
        ).astype(jnp.float32),
        lax.psum_scatter(
            grad_outproj.astype(jnp.bfloat16), ("dp", "ctx"), scatter_dimension=0, tiled=True
        ).astype(jnp.float32),
        lax.psum_scatter(
            grad_inner.astype(jnp.bfloat16), ("dp", "ctx"), scatter_dimension=0, tiled=True
        ).astype(jnp.float32),
        lax.psum_scatter(
            grad_mlp.astype(jnp.bfloat16), ("dp", "ctx"), scatter_dimension=0, tiled=True
        ).astype(jnp.float32),
        lax.psum_scatter(
            pieces_one.astype(jnp.bfloat16), ("dp", "ctx"), scatter_dimension=0, tiled=True
        ).astype(jnp.float32),
        lax.psum_scatter(
            pieces_two.astype(jnp.bfloat16), ("dp", "ctx"), scatter_dimension=0, tiled=True
        ).astype(jnp.float32),
    )
    final_qkv, final_out, final_in, final_mlp, final_one, final_two = (
        lax.psum_scatter(
            part_qkv.astype(jnp.bfloat16), "head", scatter_dimension=1, tiled=True
        ).astype(jnp.float32),
        lax.psum_scatter(
            part_out.astype(jnp.bfloat16), "head", scatter_dimension=1, tiled=True
        ).astype(jnp.float32),
        lax.psum_scatter(
            part_in.astype(jnp.bfloat16), "head", scatter_dimension=1, tiled=True
        ).astype(jnp.float32),
        lax.psum_scatter(
            part_mlp.astype(jnp.bfloat16), "head", scatter_dimension=1, tiled=True
        ).astype(jnp.float32),
        lax.psum_scatter(
            part_one.astype(jnp.bfloat16), "head", scatter_dimension=1, tiled=True
        ).astype(jnp.float32),
        lax.psum_scatter(
            part_two.astype(jnp.bfloat16), "head", scatter_dimension=1, tiled=True
        ).astype(jnp.float32),
    )
    return (
        result.reshape(seqs_here, block_rows, width),
        grad_input.reshape(seqs_here, block_rows, width),
        final_qkv,
        final_out,
        final_in,
        final_mlp,
        final_one.reshape(-1),
        final_two.reshape(-1),
    )


F32 = jnp.float32
BF16 = jnp.bfloat16
VMEM_BYTES = 56 * 1024 * 1024
GROUP = ("ctx", "head")


def dot(left, right, dims=((1,), (0,))):
    return lax.dot_general(left, right, (dims, ((), ())), preferred_element_type=F32)


def flat(values):
    return values.reshape(-1, values.shape[-1])


def lane_rotate(values, cosine, sine_signed):
    lane = lax.broadcasted_iota(jnp.int32, values.shape, 1)
    width = values.shape[1]
    partner = jnp.where(
        lane % HD < HD // 2,
        pltpu.roll(values, width - HD // 2, 1),
        pltpu.roll(values, HD // 2, 1),
    )
    return values * cosine + partner * sine_signed


def head_masks(shape):
    lane = lax.broadcasted_iota(jnp.int32, shape, 1)
    return [lane // HD == head for head in range(shape[1] // HD)]


def params():
    return pltpu.CompilerParams(vmem_limit_bytes=VMEM_BYTES)


COST = pl.CostEstimate(flops=1 << 20, transcendentals=0, bytes_accessed=1 << 16)


def whole(array):
    return pl.BlockSpec(array.shape, lambda *_: (0,) * len(array.shape))


SCALARS = pl.BlockSpec(memory_space=pltpu.SMEM)


def project_kernel(place_ref, *refs):
    pieces, weights = refs[:6], refs[6:10]
    cos_ref, sin_ref, low_ref, qkv_ref, w_ref, gain1_ref, gain2_ref, rows_ref = refs[10:]
    block, part = pieces[0].shape[2], w_ref.shape[1] // 3
    rows = gain1_ref.shape[1] // 8

    @pl.when(pl.program_id(0) == 0)
    def _():
        for step, piece in enumerate(weights):
            for turn in range(2):
                at = 2 * (place_ref[8] ^ step) + (place_ref[9] ^ turn)
                w_ref[pl.ds(pl.multiple_of(at * rows, rows), rows), :] = piece[turn, :rows]
                gains = piece[turn, rows:].astype(F32)
                rows_ref[0, pl.ds(at, 1), :] = gains[:1, :rows]
                rows_ref[1, pl.ds(at, 1), :] = gains[1:2, :rows]
        for out, at in ((gain1_ref, 0), (gain2_ref, 1)):
            for row in range(8):
                out[:, row * rows : (row + 1) * rows] = rows_ref[at, row : row + 1, :]

    gain = gain1_ref[...]
    index = 0
    for piece in pieces:
        for inner in range(piece.shape[0]):
            normed, _ = normalize(piece[inner, 0].astype(F32))
            low_ref[index, 0] = (normed * gain).astype(BF16)
            index += 1
    projected = dot(flat(low_ref[:, 0]), w_ref[...])
    cosine, sine = cos_ref[...], sin_ref[...]
    shape = (8, block, part)
    qkv_ref[:, 0, :, :part] = (
        (lane_rotate(projected[:, :part], cosine, sine) * HD**-0.5).astype(BF16).reshape(shape)
    )
    qkv_ref[:, 0, :, part : 2 * part] = (
        lane_rotate(projected[:, part : 2 * part], cosine, sine).astype(BF16).reshape(shape)
    )
    qkv_ref[:, 0, :, 2 * part :] = projected[:, 2 * part :].astype(BF16).reshape(shape)


def project(place, pieces, weights, cosine, sine):
    seqs, block, width = pieces[0].shape[1:]
    own = weights[0].shape[2]

    def by_seq(lead, last):
        return pl.BlockSpec((lead, 1, block, last), lambda s: (0, s, 0, 0))

    return pl.pallas_call(
        project_kernel,
        grid=(seqs,),
        in_specs=[SCALARS]
        + [by_seq(piece.shape[0], width) for piece in pieces]
        + [whole(w) for w in weights]
        + [whole(cosine), whole(sine)],
        out_specs=(
            by_seq(8, width),
            by_seq(8, own),
            pl.BlockSpec((width, own), lambda s: (0, 0)),
            pl.BlockSpec((1, width), lambda s: (0, 0)),
            pl.BlockSpec((1, width), lambda s: (0, 0)),
        ),
        out_shape=(
            jax.ShapeDtypeStruct((8, seqs, block, width), BF16),
            jax.ShapeDtypeStruct((8, seqs, block, own), BF16),
            jax.ShapeDtypeStruct((width, own), BF16),
            jax.ShapeDtypeStruct((1, width), F32),
            jax.ShapeDtypeStruct((1, width), F32),
        ),
        scratch_shapes=[pltpu.VMEM((2, 8, width // 8), F32)],
        compiler_params=params(),
        cost_estimate=COST,
        name="project",
    )(place, *pieces, *weights, cosine, sine)


def attend_kernel(place_ref, q_ref, k_ref, v_ref, att_ref, log_ref, home_ref):
    step = pl.program_id(0)
    queries, keys, values = flat(q_ref[...]), flat(k_ref[...]), flat(v_ref[...])
    attended = jnp.zeros(queries.shape, F32)
    logs = jnp.zeros(queries.shape, F32)
    for mask in head_masks(queries.shape):
        scores = dot(jnp.where(mask, queries, 0), keys, ((1,), (1,)))
        peak = jnp.max(scores, axis=1, keepdims=True)
        weights = jnp.exp(scores - peak)
        total = jnp.sum(weights, axis=1, keepdims=True)
        mixed = dot(weights.astype(BF16), values) * (1.0 / total)
        attended = jnp.where(mask, mixed, attended)
        logs = jnp.where(mask, peak + jnp.log(total), logs)
    att_ref[...] = attended.reshape(att_ref.shape)
    log_ref[...] = logs.reshape(log_ref.shape)
    low = attended.astype(BF16).reshape(att_ref.shape)
    for inner in range(2):
        home_ref[place_ref[2 * step + inner], 0] = low[inner, 0]


def attend(place, qkv, seq):
    _, _, block, own = qkv.shape
    part = own // 3
    rows = pl.BlockSpec((2, 1, block, part), lambda i: (i, 0, 0, 0))
    shape = (8, 1, block, part)
    return pl.pallas_call(
        attend_kernel,
        grid=(4,),
        in_specs=[
            SCALARS,
            pl.BlockSpec((2, 1, block, part), lambda i: (i, seq, 0, 0)),
            pl.BlockSpec((8, 1, block, part), lambda i: (0, seq, 0, 1)),
            pl.BlockSpec((8, 1, block, part), lambda i: (0, seq, 0, 2)),
        ],
        out_specs=(rows, rows, pl.BlockSpec(shape, lambda i: (0, 0, 0, 0))),
        out_shape=(
            jax.ShapeDtypeStruct(shape, F32),
            jax.ShapeDtypeStruct(shape, F32),
            jax.ShapeDtypeStruct(shape, BF16),
        ),
        compiler_params=params(),
        cost_estimate=COST,
        name="attend",
    )(place, qkv, qkv, qkv)


def branch_kernel(place_ref, *refs):
    pieces = refs[:6]
    rows_ref, tokens_ref, gain_ref, residual_ref, low_ref = refs[6:]
    total = flat(tokens_ref[...].astype(F32))
    index = 0
    for piece in pieces:
        for inner in range(piece.shape[0]):
            total += dot(flat(rows_ref[place_ref[index]]), piece[inner])
            index += 1
    normed, _ = normalize(total)
    residual_ref[...] = total.reshape(residual_ref.shape)
    low_ref[...] = (normed * gain_ref[...]).astype(BF16).reshape(low_ref.shape)


def branch(place, pieces, rows, tokens, gain):
    args = (*pieces, rows, tokens, gain)
    return pl.pallas_call(
        branch_kernel,
        in_specs=[SCALARS] + [whole(a) for a in args],
        out_shape=(
            jax.ShapeDtypeStruct(tokens.shape, F32),
            jax.ShapeDtypeStruct(tokens.shape, BF16),
        ),
        compiler_params=params(),
        cost_estimate=COST,
        name="branch",
    )(place, *args)


PIECES = (0, 1, 2, 4, 5, 7, 8)


def mlp_kernel(*refs):
    pieces = refs[:6]
    grad_ref, w_ref, low_ref, mixed_ref, lifted_ref, keep_ref, send_ref = refs[6:]
    step = pl.program_id(0)
    for at, piece in enumerate(pieces):

        @pl.when((step >= PIECES[at]) & (step < PIECES[at + 1]))
        def _(piece=piece):
            low_ref[...] = piece[...]

    hidden = w_ref.shape[1] // 2
    lifted = dot(flat(low_ref[...]), w_ref[...])
    first, second = lifted[:, :hidden], lifted[:, hidden:]
    grad_mixed = flat(grad_ref[...])
    gate = 0.5 * (1.0 + lax.erf(first * (0.5**0.5)))
    slope = gate + first * jnp.exp(first * first * -0.5) * ((2.0 * math.pi) ** -0.5)
    activated = first * gate
    mixed_ref[...] = (activated * second).astype(BF16).reshape(mixed_ref.shape)
    grad = jnp.concatenate(
        [(grad_mixed * second * slope).astype(BF16), (grad_mixed * activated).astype(BF16)],
        axis=1,
    )
    lifted_ref[...] = grad.reshape(lifted_ref.shape)
    partial = dot(grad, w_ref[...], ((1,), (1,))).astype(BF16).reshape(keep_ref.shape)

    @pl.when(step < 5)
    def _():
        keep_ref[...] = partial

    @pl.when(step >= 5)
    def _():
        send_ref[...] = partial


def mlp(pieces, grad_mixed, w):
    seqs, block, width = pieces[0].shape[1:]
    hidden = w.shape[1] // 2

    def rows(last):
        return pl.BlockSpec((1, seqs, block, last), lambda i: (i, 0, 0, 0))

    def within(start, count):
        return pl.BlockSpec(
            (1, seqs, block, width),
            lambda i: (jnp.clip(i - start, 0, count - 1), 0, 0, 0),
        )

    return pl.pallas_call(
        mlp_kernel,
        grid=(8,),
        in_specs=[within(at, piece.shape[0]) for at, piece in zip(PIECES, pieces)]
        + [rows(hidden), whole(w)],
        out_specs=(rows(width), rows(hidden), rows(2 * hidden), within(0, 5), within(5, 3)),
        out_shape=(
            jax.ShapeDtypeStruct((8, seqs, block, width), BF16),
            jax.ShapeDtypeStruct((8, seqs, block, hidden), BF16),
            jax.ShapeDtypeStruct((8, seqs, block, 2 * hidden), BF16),
            jax.ShapeDtypeStruct((5, seqs, block, width), BF16),
            jax.ShapeDtypeStruct((3, seqs, block, width), BF16),
        ),
        compiler_params=params(),
        cost_estimate=COST,
        name="mlp",
    )(*pieces, grad_mixed, w)


def out_grad_kernel(place_ref, rows_ref, grad_ref, keep_ref, send_ref):
    grads = flat(grad_ref[...])
    for index in range(8):
        part = dot(flat(rows_ref[place_ref[index]]), grads, ((0,), (0,))).astype(BF16)
        if index < 5:
            keep_ref[index] = part
        else:
            send_ref[index - 5] = part


def out_grad(place, rows, grads):
    part, width = rows.shape[-1], grads.shape[-1]
    return pl.pallas_call(
        out_grad_kernel,
        in_specs=[SCALARS, whole(rows), whole(grads)],
        out_shape=(
            jax.ShapeDtypeStruct((5, part, width), BF16),
            jax.ShapeDtypeStruct((3, part, width), BF16),
        ),
        compiler_params=params(),
        cost_estimate=COST,
        name="out_grad",
    )(place, rows, grads)


def branch_back_kernel(place_ref, *refs):
    pieces = refs[:6]
    low_ref, residual_ref, top_ref, gain_ref, grad_ref, branch_ref, home_ref, sum_ref = refs[6:]
    grad_low = flat(low_ref[...])
    normed, factor = normalize(flat(residual_ref[...]))
    sum_ref[...] = jnp.sum(grad_low * normed, axis=0, keepdims=True)
    grad = flat(top_ref[...].astype(F32)) + norm_back(grad_low * gain_ref[...], normed, factor)
    grad_ref[...] = grad.reshape(grad_ref.shape)
    low = grad.astype(BF16)
    branch_ref[...] = low.reshape(branch_ref.shape)
    index = 0
    for piece in pieces:
        for inner in range(piece.shape[0]):
            home_ref[place_ref[index]] = (
                dot(low, piece[inner], ((1,), (1,))).astype(BF16).reshape(home_ref.shape[1:])
            )
            index += 1


def branch_back(place, pieces, grad_low, residual, top, gain):
    args = (*pieces, grad_low, residual, top, gain)
    seqs, block, width = residual.shape
    return pl.pallas_call(
        branch_back_kernel,
        in_specs=[SCALARS] + [whole(a) for a in args],
        out_shape=(
            jax.ShapeDtypeStruct(residual.shape, F32),
            jax.ShapeDtypeStruct(residual.shape, BF16),
            jax.ShapeDtypeStruct((8, seqs, block, pieces[0].shape[1]), BF16),
            jax.ShapeDtypeStruct((1, width), F32),
        ),
        compiler_params=params(),
        cost_estimate=COST,
        name="branch_back",
    )(place, *args)


def attend_back_kernel(
    place_ref, q_ref, k_ref, v_ref, grad_ref, att_ref, log_ref, cosq_ref, sinq_ref, cos_ref,
    sin_ref, w_ref, low_ref, *refs, seq, last,
):
    if last:
        before_ref, keep_ref, send_ref, grad_w_ref, gain_ref, proj_ref, sum_k, sum_v = refs
    else:
        keep_ref, send_ref, before_ref, proj_ref, sum_k, sum_v = refs
    step = pl.program_id(0)
    block, part = q_ref.shape[2], q_ref.shape[3]

    @pl.when(step == 0)
    def _():
        sum_k[...] = jnp.zeros_like(sum_k)
        sum_v[...] = jnp.zeros_like(sum_v)

    queries, keys, values = flat(q_ref[...]), flat(k_ref[...]), flat(v_ref[...])
    grads = jnp.concatenate([grad_ref[place_ref[2 * step + inner], seq] for inner in range(2)])
    along = (grads.astype(F32) * flat(att_ref[...])).T
    logs = flat(log_ref[...]).T
    grad_queries = jnp.zeros(queries.shape, F32)
    for head, mask in enumerate(head_masks(queries.shape)):
        own_q = jnp.where(mask, queries, 0)
        own_g = jnp.where(mask, grads, 0)
        scores = dot(keys, own_q, ((1,), (1,)))
        weights = jnp.exp(scores - logs[head * HD : head * HD + 1])
        lifted = dot(values, own_g, ((1,), (1,)))
        row = jnp.sum(along[head * HD : (head + 1) * HD], axis=0, keepdims=True)
        grad_scores = (weights * (lifted - row)).astype(BF16)
        sum_k[...] += dot(grad_scores, own_q)
        sum_v[...] += dot(weights.astype(BF16), own_g)
        grad_queries = jnp.where(mask, dot(grad_scores, keys, ((0,), (0,))), grad_queries)
    grad_queries = lane_rotate(grad_queries * HD**-0.5, cosq_ref[...], -sinq_ref[...])
    rows = pl.multiple_of(step * 2 * block, 2 * block)
    proj_ref[pl.ds(rows, 2 * block), :part] = grad_queries.astype(BF16)

    @pl.when(step == 3)
    def _():
        grad_keys = lane_rotate(sum_k[...], cos_ref[...], -sin_ref[...])
        proj_ref[:, part : 2 * part] = grad_keys.astype(BF16)
        proj_ref[:, 2 * part :] = sum_v[...].astype(BF16)
        partial = dot(proj_ref[...], w_ref[...], ((1,), (1,))).astype(BF16)
        keep_ref[:, 0] = partial[: 5 * block].reshape(5, block, -1)
        send_ref[:, 0] = partial[5 * block :].reshape(3, block, -1)
        grad_w = dot(proj_ref[...], flat(low_ref[...]), ((0,), (0,)))
        if last:
            grad_w = (grad_w + before_ref[...]).T
            grad_w_ref[...] = grad_w.astype(BF16)
            along_w = jnp.sum(grad_w * w_ref[...].astype(F32), axis=1, keepdims=True)
            gain_ref[...] = jnp.broadcast_to(along_w, (w_ref.shape[0], 128)).T[:8]
        else:
            before_ref[...] = grad_w


def attend_back(place, qkv, grads, attended, logs, cosine, sine, w, low, seq, before=None):
    _, _, block, own = qkv.shape
    part, width = own // 3, w.shape[0]
    last = before is not None
    rows = pl.BlockSpec((2, 1, block, part), lambda i: (i, 0, 0, 0))
    angles = pl.BlockSpec((2 * block, part), lambda i: (i, 0))

    def full(*shape):
        return pl.BlockSpec(shape, lambda i: (0,) * len(shape))

    args = [place, qkv, qkv, qkv, grads, attended, logs, cosine, sine, cosine, sine, w, low]
    in_specs = [
        SCALARS,
        pl.BlockSpec((2, 1, block, part), lambda i: (i, seq, 0, 0)),
        pl.BlockSpec((8, 1, block, part), lambda i: (0, seq, 0, 1)),
        pl.BlockSpec((8, 1, block, part), lambda i: (0, seq, 0, 2)),
        whole(grads),
        rows,
        rows,
        angles,
        angles,
        whole(cosine),
        whole(sine),
        whole(w),
        pl.BlockSpec((8, 1, block, width), lambda i: (0, seq, 0, 0)),
    ]
    shapes = [((5, 1, block, width), BF16), ((3, 1, block, width), BF16)]
    if last:
        args.append(before)
        in_specs.append(whole(before))
        shapes += [((width, own), BF16), ((8, width), F32)]
    else:
        shapes += [((own, width), F32)]
    return pl.pallas_call(
        functools.partial(attend_back_kernel, seq=seq, last=last),
        grid=(4,),
        in_specs=in_specs,
        out_specs=tuple(full(*shape) for shape, _ in shapes),
        out_shape=tuple(jax.ShapeDtypeStruct(shape, kind) for shape, kind in shapes),
        scratch_shapes=[
            pltpu.VMEM((8 * block, own), BF16),
            pltpu.VMEM((8 * block, part), F32),
            pltpu.VMEM((8 * block, part), F32),
        ],
        compiler_params=params(),
        cost_estimate=COST,
        name="attend_back",
    )(*args)


class Group:
    def __init__(self):
        self.heads = lax.axis_size("head")
        self.dp = lax.axis_size("dp")
        self.ctx_at = lax.axis_index("ctx")
        self.head_at = lax.axis_index("head")
        self.dp_at = lax.axis_index("dp")
        self.at = self.ctx_at * self.heads + self.head_at
        near, far = [], []
        for c in range(2):
            for h in range(self.heads):
                x, y = (c ^ 1) * self.heads + h, c * self.heads + (h ^ 2)
                near.append((c * self.heads + h, x if h % 2 == 0 else y))
                far.append((c * self.heads + h, y if h % 2 == 0 else x))
        self.near, self.far = near, far

    def order(self):
        first = jnp.where(self.head_at % 2 == 0, 4, 2)
        second = 6 - first
        return jnp.stack(
            [self.at ^ bits for bits in (0, 1, first, first ^ 1, 6, second ^ 1, second, 7)]
        )

    def swap(self, values, bit):
        if bit == 4:
            return lax.ppermute(values, "ctx", [(0, 1), (1, 0)])
        return lax.ppermute(values, "head", [(i, i ^ bit) for i in range(self.heads)])

    def mate(self, values):
        return self.swap(values, 1)

    def to_near(self, values):
        return lax.ppermute(values, GROUP, self.near)

    def to_far(self, values):
        return lax.ppermute(values, GROUP, self.far)

    def rows_in(self, values, place):
        inverse = [place.index(i) for i in range(self.heads)]
        turns = [[], []]
        for source in range(self.dp):
            target = inverse[source]
            for d in range(self.dp):
                step = (d - source) % self.dp
                head = (target & 2) | ((target ^ step) & 1)
                turns[step // 2].append((source * self.heads + head, d * self.heads + target))
        first, second = (lax.ppermute(values, ("dp", "head"), pairs) for pairs in turns)
        source = sum(jnp.where(self.head_at == h, place[h], 0) for h in range(self.heads))
        step = (self.dp_at - source) % self.dp
        return first, second, step < 2

    def rows_back(self, values, place):
        pairs = [
            (d * self.heads + h, place[h] * self.heads + d)
            for d in range(self.dp)
            for h in range(self.heads)
        ]
        return lax.ppermute(values, ("dp", "head"), pairs)

    def across(self, values, step):
        return lax.ppermute(values, "dp", [(i, i ^ step) for i in range(self.dp)])

    def scatter_dp(self, values):
        step = self.dp // 2
        while step:
            halves = values.reshape(2, step, *values.shape[1:])
            bit = (self.dp_at // step) % 2
            sent = self.across(pick(halves, 1 - bit, 0).astype(BF16), step)
            values = pick(halves, bit, 0).astype(F32) + sent.astype(F32)
            step //= 2
        return values[0]

    def total(self, values, bits):
        for bit in bits:
            other = self.swap(values, bit) if bit < 8 else self.across(values, bit // 8)
            values = values + other
        return values


def pick(array, index, axis):
    return lax.dynamic_index_in_dim(array, index, axis, keepdims=False)


def after(values, *earlier):
    return lax.optimization_barrier((values, earlier))[0]


def wide(values):
    return values.astype(F32)


def local_split(tokens, cotangent, w_qkv, w_attn_out, w_in, w_mlp_out, norm_gain1, norm_gain2):
    seqs, block, width = tokens.shape
    group = Group()
    heads, dp = group.heads, group.dp
    at_c, at_h = group.ctx_at, group.head_at
    parts = 2 * heads
    hidden = w_in.shape[1] // 2 // parts
    padded = -(-hidden // 128) * 128
    own_width = width // parts
    half = heads // 2
    rows_here = w_qkv.shape[0]
    place = [2 * (h % half) + h // half for h in range(heads)]
    straight = list(range(heads))
    order = group.order()
    scalars = jnp.concatenate([order, jnp.stack([group.dp_at, at_c])]).astype(jnp.int32)
    mate, near, far = group.mate, group.to_near, group.to_far

    def in_order(own, other):
        return jnp.where(at_c == 0, jnp.stack([own, other]), jnp.stack([other, own]))

    def exchange(values):
        return lax.all_to_all(values, GROUP, split_axis=0, concat_axis=0, tiled=True)


    gains = jnp.pad(
        jnp.stack([norm_gain1, norm_gain2]), ((0, 14), (0, 3 * own_width - rows_here))
    )
    qkv_view = w_qkv.reshape(rows_here, 3, width)

    def qkv_part(at):
        start = (2 * at_h + at) * own_width
        cut = lax.dynamic_slice_in_dim(qkv_view, start, own_width, 2)
        return jnp.concatenate([cut.reshape(rows_here, 3 * own_width), gains])

    x_own = tokens[None]
    x_mate = mate(x_own)
    qkv_other, qkv_own = qkv_part(1 - at_c), qkv_part(at_c)
    qkv_cross = group.swap(after(qkv_other, x_own), 4)
    x_chip = jnp.concatenate([x_own, after(x_mate, qkv_cross, qkv_own)])
    x_near = near(x_chip)
    qkv_pair = jnp.stack([qkv_own, qkv_cross])
    qkv_pieces = [qkv_pair] + [group.across(qkv_pair, step) for step in range(1, dp)]
    out_first, out_second, out_turn = group.rows_in(after(w_attn_out, *qkv_pieces[:1]), straight)

    in_view = after(w_in, qkv_pair).reshape(rows_here, 2, heads, 2, hidden)
    in_view = pick(in_view, 2 * (at_h % half) + at_h // half, 2)

    def in_part(at):
        cut = pick(in_view, at, 2)
        return jnp.pad(cut, ((0, 0), (0, 0), (0, padded - hidden))).reshape(rows_here, 2 * padded)

    in_other, in_own = in_part(1 - at_c), in_part(at_c)
    in_cross = group.swap(in_other, 4)
    positions = after(order, qkv_pair)[:, None] * block + jnp.arange(block, dtype=jnp.int32)
    lane = jnp.arange(own_width, dtype=jnp.int32)
    frequency = jnp.exp(
        (lane % (HD // 2)).astype(F32) * (-math.log(ROPE_BASE) / (HD // 2))
    )
    angles = wide(positions.reshape(-1))[:, None] * frequency[None, :]
    cosine = jnp.cos(angles)
    sine = jnp.sin(angles) * jnp.where(lane % HD < HD // 2, -1.0, 1.0)[None, :]

    x_near = after(x_near, in_other, in_own, cosine, sine)
    x_far = far(x_near[:1])
    x_near_mate = mate(x_near)
    in_pair = in_order(in_own, after(in_cross, x_near))
    out_rows = jnp.where(out_turn, out_first, after(out_second, x_near))
    out_own = out_rows[None]
    out_mate = mate(out_own)
    cot_own = after(cotangent, x_near)[None]
    cot_mate = mate(cot_own)
    out_chip = jnp.concatenate([out_own, out_mate])
    cot_chip = jnp.concatenate([cot_own, cot_mate])
    x_far = after(x_far, in_pair, out_chip, cot_chip)
    x_far_mate = mate(x_far)

    out_near = near(after(out_chip, x_far))
    cot_near = near(after(cot_chip, x_far))
    in_pair = after(in_pair, x_far, *qkv_pieces)
    weight_in = lax.all_gather(in_pair, "dp", axis=0).reshape(width, -1)
    x_pieces = (x_own, x_mate, x_near, x_far, x_near_mate, after(x_far_mate, in_pair))
    low1, qkv, weight_qkv, gain_one, gain_two = project(
        scalars, x_pieces, qkv_pieces, cosine, sine
    )

    mlp_first, mlp_second, mlp_turn = group.rows_in(after(w_mlp_out, x_far_mate), place)
    out_near = after(out_near, qkv)
    out_far, out_near_mate = far(out_near[:1]), mate(out_near)
    att_0, log_0, home_0 = attend(scalars, after(qkv, out_near), 0)
    cot_near = after(cot_near, home_0)
    cot_far, cot_near_mate = far(cot_near[:1]), mate(cot_near)
    out_far = after(out_far, home_0)
    out_far_mate = mate(out_far)
    out_pieces = (out_own, out_mate, out_near, out_far, out_near_mate, out_far_mate)
    att_1, log_1, home_1 = attend(scalars, after(qkv, cot_near, out_far), 1)
    home = jnp.concatenate([home_0, home_1], axis=1)
    att_rows = exchange(home)
    cot_far = after(cot_far, home)
    cot_far_mate = mate(cot_far)
    residual, low2 = branch(
        scalars, out_pieces, after(att_rows, cot_far, weight_in, mlp_second), tokens, gain_two
    )

    low_own = low2[None]
    low_mate = mate(low_own)
    low_near = near(jnp.concatenate([low_own, low_mate]))
    cot_all = jnp.concatenate(
        [
            cot_own,
            cot_mate,
            cot_near,
            cot_far,
            cot_near_mate,
            after(cot_far_mate, low_mate),
        ]
    )
    weight_mlp = jnp.where(mlp_turn, mlp_first, after(mlp_second, low_mate))
    weight_mlp = jnp.pad(weight_mlp, ((0, padded - hidden), (0, 0)))
    grad_mixed = dot(flat(cot_all), weight_mlp, ((1,), (1,)))
    low_near = after(low_near, grad_mixed)
    low_far, low_near_mate = far(low_near[:1]), mate(low_near)
    low_pieces = (low_own, low_mate, low_near, low_far, low_near_mate, mate(low_far))
    low2_all, mixed, grad_lifted, keep, send = mlp(
        low_pieces, grad_mixed.reshape(8, seqs, block, padded), weight_in
    )

    def over_tokens(left, right):
        return dot(flat(left), flat(right), ((0,), (0,)))

    def scatter(values):
        return lax.psum_scatter(values.astype(BF16), "dp", scatter_dimension=0, tiled=True)

    def columns_first(values):
        return jnp.moveaxis(values.reshape(values.shape[0], dp, -1), 1, 0)

    met = mate(send)
    grad_mlp = columns_first(over_tokens(after(mixed, send), cot_all)[:hidden]).astype(BF16)
    met = after(met, grad_mlp)
    grad_mlp = scatter(grad_mlp)[0]
    last = (wide(keep[4]) + wide(met[2])).astype(BF16)
    last_far = far(last)
    cut = 5 * seqs * block
    mixed_flat = flat(after(mixed, last))
    out_keep = dot(mixed_flat[:cut], weight_mlp).astype(BF16).reshape(5, seqs, block, width)
    out_send = dot(mixed_flat[cut:], weight_mlp).astype(BF16).reshape(3, seqs, block, width)
    last_far = after(last_far, out_keep, out_send)
    chip = jnp.stack([wide(keep[2]) + wide(met[0]) + wide(last_far), wide(keep[3]) + wide(met[1])])
    chip = chip.astype(BF16)
    chip_near = near(chip)
    out_met = mate(after(out_send, chip))
    grad_in = over_tokens(low2_all, after(grad_lifted, chip)).astype(BF16)
    chip_near = after(chip_near, grad_in)
    grad_in = scatter(grad_in)
    home = mate((wide(keep[1]) + wide(chip_near[1])).astype(BF16))
    grad_low2 = wide(keep[0]) + wide(chip_near[0]) + wide(after(home, grad_mlp))

    grad_residual, grad_branch, home, gain2_sum = branch_back(
        scalars, out_pieces, grad_low2, residual, cotangent, gain_two
    )
    grad_home = exchange(home)

    rows_keep, rows_send = out_grad(scalars, after(att_rows, home), grad_branch)
    rows_met = mate(rows_send)
    out_last = (wide(out_keep[4]) + wide(after(out_met, home)[2])).astype(BF16)
    rows_last = (wide(rows_keep[4]) + wide(rows_met[2])).astype(BF16)
    grad_home = after(grad_home, out_last, rows_last)
    out_far2, rows_far = far(after(out_last, grad_home)), far(after(rows_last, grad_home))
    grad_mlp = group.rows_back(after(grad_mlp, home), place)
    gain2_sum = group.total(after(gain2_sum[0], home).reshape(-1, 128), (1, 2, 4))
    grad_home = after(grad_home, grad_mlp, gain2_sum)
    gain2_sum = group.total(after(gain2_sum, grad_home), (8, 16))
    keep_0, send_0, before = attend_back(
        scalars, qkv, grad_home, att_0, log_0, cosine, sine, weight_qkv, low1, 0
    )
    met_0 = mate(send_0)
    grad_in = after(grad_in, send_0)

    def rows_here_of(values):
        pair = values.reshape(2, rows_here, -1)
        own = pick(pair, at_c, 0)
        other = group.swap(pick(pair, 1 - at_c, 0), 4)
        return in_order(own, other)

    grad_in = rows_here_of(grad_in)
    out_far2, rows_far = after((out_far2, rows_far), send_0)
    out_chip = jnp.stack(
        [
            wide(out_keep[2]) + wide(out_met[0]) + wide(out_far2),
            wide(out_keep[3]) + wide(out_met[1]),
        ]
    ).astype(BF16)
    rows_chip = jnp.stack(
        [
            wide(rows_keep[2]) + wide(rows_met[0]) + wide(rows_far),
            wide(rows_keep[3]) + wide(rows_met[1]),
        ]
    ).astype(BF16)
    out_chip_near, rows_chip_near = near(out_chip), near(rows_chip)
    keep_1, send_1, grad_qkv, gain1_sum = attend_back(
        scalars, qkv, after(grad_home, out_chip, rows_chip, grad_in), att_1, log_1, cosine, sine,
        weight_qkv, low1, 1, before,
    )

    met_1 = mate(send_1)
    grad_qkv = scatter(grad_qkv)

    def both(index, at):
        return jnp.concatenate(
            [wide(keep_0[index]) + wide(met_0[at]), wide(keep_1[index]) + wide(met_1[at])]
        )

    last = both(4, 2).astype(BF16)
    last_far = far(last)
    rows_chip_near = after(rows_chip_near, last)
    out_chip_near = after(out_chip_near, last)
    rows_home = mate((wide(rows_keep[1]) + wide(rows_chip_near[1])).astype(BF16))
    out_home = mate((wide(out_keep[1]) + wide(out_chip_near[1])).astype(BF16))
    gain1_sum = (gain1_sum[0] / gain_one[0]).reshape(-1, 128)
    gain1_sum = group.total(after(gain1_sum, last), (1, 2))
    last_far = after(last_far, gain1_sum)
    chip = jnp.stack([both(2, 0) + wide(last_far), both(3, 1)]).astype(BF16)
    chip_near = near(chip)
    result = residual + wide(out_keep[0]) + wide(out_chip_near[0]) + wide(after(out_home, chip))
    result = result.astype(BF16)
    grad_out = wide(rows_keep[0]) + wide(rows_chip_near[0]) + wide(after(rows_home, chip))
    grad_out = group.scatter_dp(columns_first(grad_out)).astype(BF16)
    gain1_sum = group.total(after(gain1_sum, chip), (4, 8, 16))
    late = at_h // half
    grad_in = jnp.stack([grad_in[..., :hidden], grad_in[..., padded : padded + hidden]])
    stays = pick(after(grad_in, chip), late, 0)
    comes = group.swap(pick(after(grad_in, chip), 1 - late, 0), half)
    chip_near = after(chip_near, grad_out, gain1_sum, comes, result, grad_qkv)
    grad_out = wide(group.rows_back(after(grad_out, chip_near), straight))
    home = mate(
        (jnp.concatenate([wide(keep_0[1]), wide(keep_1[1])]) + wide(chip_near[1])).astype(BF16)
    )
    grad_low1 = jnp.concatenate([wide(keep_0[0]), wide(keep_1[0])]) + wide(chip_near[0])
    grad_low1 = grad_low1 + wide(home)
    normed1, factor1 = normalize(wide(tokens))
    grad_input = grad_residual + norm_back(grad_low1 * gain_one, normed1, factor1)

    grad_mlp = wide(grad_mlp)
    grad_in = jnp.where(
        late == 0, jnp.concatenate([stays, comes]), jnp.concatenate([comes, stays])
    )
    grad_in = wide(jnp.moveaxis(grad_in, 0, 1).reshape(rows_here, -1))

    per_device = width // (dp * parts)
    start = (group.dp_at * parts + group.at) * per_device
    grad_gain1, grad_gain2 = (
        lax.dynamic_slice_in_dim(sums.reshape(-1), start, per_device, 0)
        for sums in (gain1_sum, gain2_sum)
    )
    grad_qkv = rows_here_of(after(grad_qkv, chip_near)).reshape(2, rows_here, 3, own_width)
    grad_qkv = jnp.moveaxis(grad_qkv, 2, 0)
    odd = at_h % 2
    stays = pick(grad_qkv, odd + late, 0)
    core = group.swap(pick(grad_qkv, 1 - odd + late, 0), 1)
    chip = group.swap(pick(grad_qkv, 2 - 2 * late, 0), 2)
    grad_qkv = jnp.where(
        odd == 0, jnp.concatenate([stays, core, chip]), jnp.concatenate([chip, core, stays])
    )
    grad_qkv = wide(jnp.moveaxis(grad_qkv, 0, 1).reshape(rows_here, -1))

    return (
        result,
        grad_input,
        grad_qkv,
        grad_out,
        grad_in,
        grad_mlp,
        grad_gain1,
        grad_gain2,
    )


def local(tokens, cotangent, w_qkv, w_attn_out, w_in, w_mlp_out, norm_gain1, norm_gain2):
    args = (tokens, cotangent, w_qkv, w_attn_out, w_in, w_mlp_out, norm_gain1, norm_gain2)
    sizes = [lax.axis_size(axis) for axis in ("dp", "ctx", "head")]
    if sizes == [4, 2, 4] and tokens.shape[2] == 8 * 2 * HD and tokens.shape[1] % 16 == 0:
        return local_split(*args)
    return local_general(*args)


def solution(mesh):
    in_specs = (
        P("dp", ("ctx", "head"), None),
        P("dp", ("ctx", "head"), None),
        P(("dp", "ctx"), None),
        P(("dp", "ctx"), None),
        P(("dp", "ctx"), None),
        P(("dp", "ctx"), None),
        P(("dp", "ctx")),
        P(("dp", "ctx")),
    )
    out_specs = (
        P("dp", ("ctx", "head"), None),
        P("dp", ("ctx", "head"), None),
        P(("dp", "ctx"), "head"),
        P(("dp", "ctx"), "head"),
        P(("dp", "ctx"), "head"),
        P(("dp", "ctx"), "head"),
        P(("dp", "ctx", "head")),
        P(("dp", "ctx", "head")),
    )
    return jax.shard_map(local, mesh=mesh, in_specs=in_specs, out_specs=out_specs, check_vma=False)
```

```python
import functools
import math

import jax
import jax.numpy as jnp
from jax import lax
from jax.experimental import pallas as pl
from jax.experimental.pallas import tpu as pltpu
from jax.sharding import PartitionSpec as P

HD = 64


EPSILON = 1e-05
ROPE_BASE = 160000.0


def normalize(values):
    centre = jnp.mean(values, axis=-1, keepdims=True)
    shifted = values - centre
    spread = jnp.mean(shifted * shifted, axis=-1, keepdims=True)
    factor = lax.rsqrt(spread + EPSILON)
    return (shifted * factor, factor)


def norm_back(grad_normed, normed, factor):
    grad_centre = jnp.mean(grad_normed, axis=-1, keepdims=True)
    grad_along = jnp.mean(grad_normed * normed, axis=-1, keepdims=True)
    return (grad_normed - grad_centre - normed * grad_along) * factor


def rope_tables(positions, half_size):
    frequency = jnp.exp(
        jnp.arange(half_size, dtype=jnp.float32) * (-math.log(ROPE_BASE) / half_size)
    )
    angles = positions[:, None] * frequency[None, :]
    return (jnp.cos(angles), jnp.sin(angles))


def rotate(values, cosine, sine_table, direction):
    half_size = cosine.shape[-1]
    first_half = values[..., :half_size]
    second_half = values[..., half_size:]
    cos_part = cosine[:, None, :]
    sin_part = sine_table[:, None, :] * direction
    return jnp.concatenate(
        [
            first_half * cos_part - second_half * sin_part,
            second_half * cos_part + first_half * sin_part,
        ],
        axis=-1,
    )


def block_scores(queries4, keys_block, scale):
    keys4 = keys_block.reshape(
        keys_block.shape[0], keys_block.shape[1], queries4.shape[2], queries4.shape[3]
    )
    return (
        jnp.einsum("sqgd,skgd->sgqk", queries4, keys4, preferred_element_type=jnp.float32) * scale
    )


def attend_forward(queries4, keys_all, values_all, key_rows, scale):
    seqs_here, query_rows, groups, head_size = queries4.shape
    turns = keys_all.shape[1] // key_rows

    def statistics(turn, carry):
        row_peak, row_total = carry
        keys_block = lax.dynamic_slice_in_dim(keys_all, turn * key_rows, key_rows, 1)
        scores = block_scores(queries4, keys_block, scale)
        new_peak = jnp.maximum(row_peak, jnp.max(scores, axis=-1))
        row_total = row_total * jnp.exp(row_peak - new_peak) + jnp.sum(
            jnp.exp(scores - new_peak[..., None]), axis=-1
        )
        return (new_peak, row_total)

    start_peak = jnp.full((seqs_here, groups, query_rows), -1e30, jnp.float32)
    row_peak, row_total = lax.fori_loop(
        0, turns, statistics, (start_peak, jnp.zeros_like(start_peak))
    )
    log_total = row_peak + jnp.log(row_total)

    def accumulate(turn, running):
        keys_block = lax.dynamic_slice_in_dim(keys_all, turn * key_rows, key_rows, 1)
        values_block = lax.dynamic_slice_in_dim(values_all, turn * key_rows, key_rows, 1).reshape(
            seqs_here, key_rows, groups, head_size
        )
        weights = jnp.exp(block_scores(queries4, keys_block, scale) - log_total[..., None]).astype(
            jnp.bfloat16
        )
        return running + jnp.einsum(
            "sgqk,skgd->sqgd", weights, values_block, preferred_element_type=jnp.float32
        )

    attended = lax.fori_loop(
        0, turns, accumulate, jnp.zeros((seqs_here, query_rows, groups, head_size), jnp.float32)
    )
    return (attended, log_total)


def attend_backward(queries4, keys_all, values_all, grad_out4, log_total, along, key_rows, scale):
    seqs_here, query_rows, groups, head_size = queries4.shape
    length = keys_all.shape[1]
    width_group = groups * head_size
    turns = length // key_rows

    def step_back(turn, carry):
        grad_queries, grad_keys, grad_values = carry
        keys_block = lax.dynamic_slice_in_dim(keys_all, turn * key_rows, key_rows, 1)
        keys4 = keys_block.reshape(seqs_here, key_rows, groups, head_size)
        values4 = lax.dynamic_slice_in_dim(values_all, turn * key_rows, key_rows, 1).reshape(
            seqs_here, key_rows, groups, head_size
        )
        weights = jnp.exp(block_scores(queries4, keys_block, scale) - log_total[..., None])
        grad_weights = jnp.einsum(
            "sqgd,skgd->sgqk", grad_out4, values4, preferred_element_type=jnp.float32
        )
        grad_scores = (weights * (grad_weights - along[..., None])).astype(jnp.bfloat16)
        grad_queries = grad_queries + jnp.einsum(
            "sgqk,skgd->sqgd", grad_scores, keys4, preferred_element_type=jnp.float32
        )
        key_part = (
            jnp.einsum("sgqk,sqgd->skgd", grad_scores, queries4, preferred_element_type=jnp.float32)
            * scale
        )
        value_part = jnp.einsum(
            "sgqk,sqgd->skgd",
            weights.astype(jnp.bfloat16),
            grad_out4,
            preferred_element_type=jnp.float32,
        )
        grad_keys = lax.dynamic_update_slice_in_dim(
            grad_keys, key_part.reshape(seqs_here, key_rows, width_group), turn * key_rows, 1
        )
        grad_values = lax.dynamic_update_slice_in_dim(
            grad_values, value_part.reshape(seqs_here, key_rows, width_group), turn * key_rows, 1
        )
        return (grad_queries, grad_keys, grad_values)

    start = (
        jnp.zeros((seqs_here, query_rows, groups, head_size), jnp.float32),
        jnp.zeros((seqs_here, length, width_group), jnp.float32),
        jnp.zeros((seqs_here, length, width_group), jnp.float32),
    )
    grad_queries, grad_keys, grad_values = lax.fori_loop(0, turns, step_back, start)
    return (grad_queries * scale, grad_keys, grad_values)


def local_general(tokens, cotangent, w_qkv, w_attn_out, w_in, w_mlp_out, norm_gain1, norm_gain2):
    seqs_here, block_rows, width = tokens.shape
    count_rows = seqs_here * block_rows
    heads_all = width // HD
    head_devices = lax.axis_size("head")
    group_devices = lax.axis_size(("dp", "ctx"))
    groups = heads_all // head_devices
    width_group = groups * HD
    scale = HD ** (-0.5)
    ff_width = w_in.shape[1] // 2
    full_qkv, full_out, full_in, full_mlp, gain_one, gain_two = (
        lax.all_gather(w_qkv, ("dp", "ctx"), axis=0, tiled=True),
        lax.all_gather(w_attn_out, ("dp", "ctx"), axis=0, tiled=True),
        lax.all_gather(w_in, ("dp", "ctx"), axis=0, tiled=True),
        lax.all_gather(w_mlp_out, ("dp", "ctx"), axis=0, tiled=True),
        lax.all_gather(norm_gain1, ("dp", "ctx"), axis=0, tiled=True),
        lax.all_gather(norm_gain2, ("dp", "ctx"), axis=0, tiled=True),
    )
    x_in = tokens.astype(jnp.float32).reshape(count_rows, width)
    normed1, factor1 = normalize(x_in)
    lowered1 = (normed1 * gain_one.astype(jnp.float32)).astype(jnp.bfloat16)
    projected = jnp.dot(lowered1, full_qkv, preferred_element_type=jnp.float32).reshape(
        seqs_here, block_rows, 3, heads_all, HD
    )
    first_pos = (lax.axis_index("ctx") * head_devices + lax.axis_index("head")) * block_rows
    positions = (first_pos + jnp.arange(block_rows, dtype=jnp.int32)).astype(jnp.float32)
    cosine, sine_table = rope_tables(positions, HD // 2)
    queries = (
        rotate(projected[:, :, 0], cosine, sine_table, 1.0)
        .astype(jnp.bfloat16)
        .reshape(seqs_here, block_rows, width)
    )
    keys_local = (
        rotate(projected[:, :, 1], cosine, sine_table, 1.0)
        .astype(jnp.bfloat16)
        .reshape(seqs_here, block_rows, width)
    )
    values_local = projected[:, :, 2].astype(jnp.bfloat16).reshape(seqs_here, block_rows, width)
    queries_h, keys_h, values_h = (
        lax.all_to_all(queries, "head", split_axis=2, concat_axis=1, tiled=True),
        lax.all_to_all(keys_local, "head", split_axis=2, concat_axis=1, tiled=True),
        lax.all_to_all(values_local, "head", split_axis=2, concat_axis=1, tiled=True),
    )
    query_rows = queries_h.shape[1]
    queries4 = queries_h.reshape(seqs_here, query_rows, groups, HD)
    keys_all, values_all = (
        lax.all_gather(keys_h, "ctx", axis=1, tiled=True),
        lax.all_gather(values_h, "ctx", axis=1, tiled=True),
    )
    key_rows = math.gcd(keys_all.shape[1], 1024)
    attended, log_total = attend_forward(queries4, keys_all, values_all, key_rows, scale)
    attended_low = attended.astype(jnp.bfloat16).reshape(seqs_here, query_rows, width_group)
    back_rows = lax.all_to_all(
        attended_low, "head", split_axis=1, concat_axis=2, tiled=True
    ).reshape(count_rows, width)
    residual = x_in + jnp.dot(back_rows, full_out, preferred_element_type=jnp.float32)
    normed2, factor2 = normalize(residual)
    lowered2 = (normed2 * gain_two.astype(jnp.float32)).astype(jnp.bfloat16)
    lifted = jnp.dot(lowered2, full_in, preferred_element_type=jnp.float32)
    first_part = lifted[:, :ff_width]
    second_part = lifted[:, ff_width:]
    activated, gelu_pullback = jax.vjp(
        lambda entries: jax.nn.gelu(entries, approximate=False), first_part
    )
    mixed = (activated * second_part).astype(jnp.bfloat16)
    result = (residual + jnp.dot(mixed, full_mlp, preferred_element_type=jnp.float32)).astype(
        jnp.bfloat16
    )
    full_qkv, full_out, full_in, full_mlp, gain_one, gain_two = (
        lax.all_gather(w_qkv, ("dp", "ctx"), axis=0, tiled=True),
        lax.all_gather(w_attn_out, ("dp", "ctx"), axis=0, tiled=True),
        lax.all_gather(w_in, ("dp", "ctx"), axis=0, tiled=True),
        lax.all_gather(w_mlp_out, ("dp", "ctx"), axis=0, tiled=True),
        lax.all_gather(norm_gain1, ("dp", "ctx"), axis=0, tiled=True),
        lax.all_gather(norm_gain2, ("dp", "ctx"), axis=0, tiled=True),
    )
    keys_all, values_all = (
        lax.all_gather(keys_h, "ctx", axis=1, tiled=True),
        lax.all_gather(values_h, "ctx", axis=1, tiled=True),
    )
    grad_top = cotangent.reshape(count_rows, width)
    grad_mlp = jnp.einsum("nf,nd->fd", mixed, grad_top, preferred_element_type=jnp.float32)
    grad_mixed = jnp.einsum("nd,fd->nf", grad_top, full_mlp, preferred_element_type=jnp.float32)
    grad_first = gelu_pullback(grad_mixed * second_part)[0]
    grad_lifted = jnp.concatenate([grad_first, grad_mixed * activated], axis=-1).astype(
        jnp.bfloat16
    )
    grad_inner = jnp.einsum("nd,nf->df", lowered2, grad_lifted, preferred_element_type=jnp.float32)
    grad_lowered2 = jnp.einsum(
        "nf,df->nd", grad_lifted, full_in, preferred_element_type=jnp.float32
    )
    grad_two = jnp.sum(grad_lowered2 * normed2, axis=0)
    grad_residual = grad_top.astype(jnp.float32) + norm_back(
        grad_lowered2 * gain_two.astype(jnp.float32), normed2, factor2
    )
    grad_branch = grad_residual.astype(jnp.bfloat16)
    grad_outproj = jnp.einsum(
        "nd,ne->de", back_rows, grad_branch, preferred_element_type=jnp.float32
    )
    grad_attended = jnp.einsum(
        "ne,de->nd", grad_branch, full_out, preferred_element_type=jnp.float32
    ).astype(jnp.bfloat16)
    grad_attended_h = lax.all_to_all(
        grad_attended.reshape(seqs_here, block_rows, width),
        "head",
        split_axis=2,
        concat_axis=1,
        tiled=True,
    )
    grad_out4 = grad_attended_h.reshape(seqs_here, query_rows, groups, HD)
    along = jnp.transpose(jnp.sum(grad_out4.astype(jnp.float32) * attended, axis=-1), (0, 2, 1))
    grad_queries, grad_keys_all, grad_values_all = attend_backward(
        queries4, keys_all, values_all, grad_out4, log_total, along, key_rows, scale
    )
    grad_keys_sum, grad_values_sum = (
        lax.psum_scatter(
            grad_keys_all.astype(jnp.bfloat16), "ctx", scatter_dimension=1, tiled=True
        ).astype(jnp.float32),
        lax.psum_scatter(
            grad_values_all.astype(jnp.bfloat16), "ctx", scatter_dimension=1, tiled=True
        ).astype(jnp.float32),
    )
    grad_q_low = grad_queries.astype(jnp.bfloat16).reshape(seqs_here, query_rows, width_group)
    grad_q_tok, grad_k_tok, grad_v_tok = (
        lax.all_to_all(grad_q_low, "head", split_axis=1, concat_axis=2, tiled=True),
        lax.all_to_all(
            grad_keys_sum.astype(jnp.bfloat16), "head", split_axis=1, concat_axis=2, tiled=True
        ),
        lax.all_to_all(
            grad_values_sum.astype(jnp.bfloat16), "head", split_axis=1, concat_axis=2, tiled=True
        ),
    )
    unrot_q = rotate(
        grad_q_tok.astype(jnp.float32).reshape(seqs_here, block_rows, heads_all, HD),
        cosine,
        sine_table,
        -1.0,
    )
    unrot_k = rotate(
        grad_k_tok.astype(jnp.float32).reshape(seqs_here, block_rows, heads_all, HD),
        cosine,
        sine_table,
        -1.0,
    )
    grad_projected = jnp.concatenate(
        [
            unrot_q.reshape(count_rows, width),
            unrot_k.reshape(count_rows, width),
            grad_v_tok.astype(jnp.float32).reshape(count_rows, width),
        ],
        axis=-1,
    ).astype(jnp.bfloat16)
    grad_project = jnp.einsum(
        "nd,nf->df", lowered1, grad_projected, preferred_element_type=jnp.float32
    )
    grad_lowered1 = jnp.einsum(
        "nf,df->nd", grad_projected, full_qkv, preferred_element_type=jnp.float32
    )
    grad_one = jnp.sum(grad_lowered1 * normed1, axis=0)
    grad_input = grad_residual + norm_back(
        grad_lowered1 * gain_one.astype(jnp.float32), normed1, factor1
    )
    pieces_one = grad_one.reshape(group_devices, head_devices, -1)
    pieces_two = grad_two.reshape(group_devices, head_devices, -1)
    part_qkv, part_out, part_in, part_mlp, part_one, part_two = (
        lax.psum_scatter(
            grad_project.astype(jnp.bfloat16), ("dp", "ctx"), scatter_dimension=0, tiled=True
        ).astype(jnp.float32),
        lax.psum_scatter(
            grad_outproj.astype(jnp.bfloat16), ("dp", "ctx"), scatter_dimension=0, tiled=True
        ).astype(jnp.float32),
        lax.psum_scatter(
            grad_inner.astype(jnp.bfloat16), ("dp", "ctx"), scatter_dimension=0, tiled=True
        ).astype(jnp.float32),
        lax.psum_scatter(
            grad_mlp.astype(jnp.bfloat16), ("dp", "ctx"), scatter_dimension=0, tiled=True
        ).astype(jnp.float32),
        lax.psum_scatter(
            pieces_one.astype(jnp.bfloat16), ("dp", "ctx"), scatter_dimension=0, tiled=True
        ).astype(jnp.float32),
        lax.psum_scatter(
            pieces_two.astype(jnp.bfloat16), ("dp", "ctx"), scatter_dimension=0, tiled=True
        ).astype(jnp.float32),
    )
    final_qkv, final_out, final_in, final_mlp, final_one, final_two = (
        lax.psum_scatter(
            part_qkv.astype(jnp.bfloat16), "head", scatter_dimension=1, tiled=True
        ).astype(jnp.float32),
        lax.psum_scatter(
            part_out.astype(jnp.bfloat16), "head", scatter_dimension=1, tiled=True
        ).astype(jnp.float32),
        lax.psum_scatter(
            part_in.astype(jnp.bfloat16), "head", scatter_dimension=1, tiled=True
        ).astype(jnp.float32),
        lax.psum_scatter(
            part_mlp.astype(jnp.bfloat16), "head", scatter_dimension=1, tiled=True
        ).astype(jnp.float32),
        lax.psum_scatter(
            part_one.astype(jnp.bfloat16), "head", scatter_dimension=1, tiled=True
        ).astype(jnp.float32),
        lax.psum_scatter(
            part_two.astype(jnp.bfloat16), "head", scatter_dimension=1, tiled=True
        ).astype(jnp.float32),
    )
    return (
        result.reshape(seqs_here, block_rows, width),
        grad_input.reshape(seqs_here, block_rows, width),
        final_qkv,
        final_out,
        final_in,
        final_mlp,
        final_one.reshape(-1),
        final_two.reshape(-1),
    )


F32 = jnp.float32
BF16 = jnp.bfloat16
VMEM_BYTES = 56 * 1024 * 1024
GROUP = ("ctx", "head")


def dot(left, right, dims=((1,), (0,))):
    return lax.dot_general(left, right, (dims, ((), ())), preferred_element_type=F32)


def wide(values):
    return values.astype(F32)


def flat(values):
    return values.reshape(-1, values.shape[-1])


def lane_rotate(values, cosine, sine_signed):
    lane = lax.broadcasted_iota(jnp.int32, values.shape, 1)
    width = values.shape[1]
    partner = jnp.where(
        lane % HD < HD // 2,
        pltpu.roll(values, width - HD // 2, 1),
        pltpu.roll(values, HD // 2, 1),
    )
    return values * cosine + partner * sine_signed


def head_masks(shape):
    lane = lax.broadcasted_iota(jnp.int32, shape, 1)
    return [lane // HD == head for head in range(shape[1] // HD)]


def params():
    return pltpu.CompilerParams(vmem_limit_bytes=VMEM_BYTES)


COST = pl.CostEstimate(flops=1 << 20, transcendentals=0, bytes_accessed=1 << 16)


def whole(array):
    return pl.BlockSpec(array.shape, lambda *_: (0,) * len(array.shape))


SCALARS = pl.BlockSpec(memory_space=pltpu.SMEM)


def project_kernel(place_ref, *refs):
    pieces, weights = refs[:6], refs[6:10]
    cos_ref, sin_ref, low_ref, qkv_ref, w_ref, gain1_ref, gain2_ref, rows_ref = refs[10:]
    block, part = pieces[0].shape[2], w_ref.shape[1] // 3
    rows = gain1_ref.shape[1] // 8

    @pl.when(pl.program_id(0) == 0)
    def _():
        for step, piece in enumerate(weights):
            for turn in range(2):
                at = 2 * (place_ref[8] ^ step) + (place_ref[9] ^ turn)
                w_ref[pl.ds(pl.multiple_of(at * rows, rows), rows), :] = piece[turn, :rows]
                gains = piece[turn, rows:].astype(F32)
                rows_ref[0, pl.ds(at, 1), :] = gains[:1, :rows]
                rows_ref[1, pl.ds(at, 1), :] = gains[1:2, :rows]
        for out, at in ((gain1_ref, 0), (gain2_ref, 1)):
            for row in range(8):
                out[:, row * rows : (row + 1) * rows] = rows_ref[at, row : row + 1, :]

    gain = gain1_ref[...]
    index = 0
    for piece in pieces:
        for inner in range(piece.shape[0]):
            normed, _ = normalize(piece[inner, 0].astype(F32))
            low_ref[index, 0] = (normed * gain).astype(BF16)
            index += 1
    projected = dot(flat(low_ref[:, 0]), w_ref[...])
    cosine, sine = cos_ref[...], sin_ref[...]
    shape = (8, block, part)
    qkv_ref[:, 0, :, :part] = (
        (lane_rotate(projected[:, :part], cosine, sine) * HD**-0.5).astype(BF16).reshape(shape)
    )
    qkv_ref[:, 0, :, part : 2 * part] = (
        lane_rotate(projected[:, part : 2 * part], cosine, sine).astype(BF16).reshape(shape)
    )
    qkv_ref[:, 0, :, 2 * part :] = projected[:, 2 * part :].astype(BF16).reshape(shape)


def project(place, pieces, weights, cosine, sine):
    seqs, block, width = pieces[0].shape[1:]
    own = weights[0].shape[2]

    def by_seq(lead, last):
        return pl.BlockSpec((lead, 1, block, last), lambda s: (0, s, 0, 0))

    return pl.pallas_call(
        project_kernel,
        grid=(seqs,),
        in_specs=[SCALARS]
        + [by_seq(piece.shape[0], width) for piece in pieces]
        + [whole(w) for w in weights]
        + [whole(cosine), whole(sine)],
        out_specs=(
            by_seq(8, width),
            by_seq(8, own),
            pl.BlockSpec((width, own), lambda s: (0, 0)),
            pl.BlockSpec((1, width), lambda s: (0, 0)),
            pl.BlockSpec((1, width), lambda s: (0, 0)),
        ),
        out_shape=(
            jax.ShapeDtypeStruct((8, seqs, block, width), BF16),
            jax.ShapeDtypeStruct((8, seqs, block, own), BF16),
            jax.ShapeDtypeStruct((width, own), BF16),
            jax.ShapeDtypeStruct((1, width), F32),
            jax.ShapeDtypeStruct((1, width), F32),
        ),
        scratch_shapes=[pltpu.VMEM((2, 8, width // 8), F32)],
        compiler_params=params(),
        cost_estimate=COST,
        name="project",
    )(place, *pieces, *weights, cosine, sine)


def attend_kernel(place_ref, q_ref, k_ref, v_ref, *refs):
    att_ref, log_ref, home_ref = refs[-3:]
    step, seq = pl.program_id(0), len(refs) - 3
    if seq:

        @pl.when(step == 0)
        def _():
            home_ref[:, :1] = refs[0][...]

    queries, keys, values = flat(q_ref[...]), flat(k_ref[...]), flat(v_ref[...])
    attended = jnp.zeros(queries.shape, F32)
    logs = jnp.zeros(queries.shape, F32)
    for mask in head_masks(queries.shape):
        scores = dot(jnp.where(mask, queries, 0), keys, ((1,), (1,)))
        peak = jnp.max(scores, axis=1, keepdims=True)
        weights = jnp.exp(scores - peak)
        total = jnp.sum(weights, axis=1, keepdims=True)
        mixed = dot(weights.astype(BF16), values) * (1.0 / total)
        attended = jnp.where(mask, mixed, attended)
        logs = jnp.where(mask, peak + jnp.log(total), logs)
    att_ref[...] = attended.reshape(att_ref.shape)
    log_ref[...] = logs.reshape(log_ref.shape)
    low = attended.astype(BF16).reshape(att_ref.shape)
    for inner in range(2):
        home_ref[place_ref[2 * step + inner], seq] = low[inner, 0]


def attend(place, qkv, *home):
    _, _, block, own = qkv.shape
    part, seq = own // 3, len(home)
    rows = pl.BlockSpec((2, 1, block, part), lambda i: (i, 0, 0, 0))
    shape = (8, 1, block, part)
    return pl.pallas_call(
        attend_kernel,
        grid=(4,),
        in_specs=[
            SCALARS,
            pl.BlockSpec((2, 1, block, part), lambda i: (i, seq, 0, 0)),
            pl.BlockSpec((8, 1, block, part), lambda i: (0, seq, 0, 1)),
            pl.BlockSpec((8, 1, block, part), lambda i: (0, seq, 0, 2)),
            *[whole(h) for h in home],
        ],
        out_specs=(
            rows,
            rows,
            pl.BlockSpec((8, 1 + seq, block, part), lambda i: (0, 0, 0, 0)),
        ),
        out_shape=(
            jax.ShapeDtypeStruct(shape, F32),
            jax.ShapeDtypeStruct(shape, F32),
            jax.ShapeDtypeStruct((8, 1 + seq, block, part), BF16),
        ),
        compiler_params=params(),
        cost_estimate=COST,
        name="attend",
    )(place, qkv, qkv, qkv, *home)


def branch_kernel(place_ref, *refs):
    pieces = refs[:6]
    rows_ref, tokens_ref, gain_ref, residual_ref, low_ref = refs[6:]
    total = flat(tokens_ref[...].astype(F32))
    index = 0
    for piece in pieces:
        for inner in range(piece.shape[0]):
            total += dot(flat(rows_ref[place_ref[index]]), piece[inner])
            index += 1
    normed, _ = normalize(total)
    residual_ref[...] = total.reshape(residual_ref.shape)
    low_ref[...] = (normed * gain_ref[...]).astype(BF16).reshape(low_ref.shape)


def branch(place, pieces, rows, tokens, gain):
    args = (*pieces, rows, tokens, gain)
    return pl.pallas_call(
        branch_kernel,
        in_specs=[SCALARS] + [whole(a) for a in args],
        out_shape=(
            jax.ShapeDtypeStruct(tokens.shape, F32),
            jax.ShapeDtypeStruct(tokens.shape, BF16),
        ),
        compiler_params=params(),
        cost_estimate=COST,
        name="branch",
    )(place, *args)


def mlp_kernel(*refs, ends):
    pieces = refs[:3]
    grad_ref, w_ref = refs[3:5]
    low_ref, mixed_ref, lifted_ref, *out_refs = refs[-3 - len(ends) :]
    step = pl.program_id(0)
    start = 0
    for piece in pieces:

        @pl.when((step >= start) & (step < start + piece.shape[0]))
        def _(piece=piece, start=start):
            low_ref[0] = piece[step - start]

        start += piece.shape[0]

    hidden = w_ref.shape[1] // 2
    lifted = dot(flat(low_ref[...]), w_ref[...])
    first, second = lifted[:, :hidden], lifted[:, hidden:]
    grad_mixed = flat(grad_ref[...])
    gate = 0.5 * (1.0 + lax.erf(first * (0.5**0.5)))
    slope = gate + first * jnp.exp(first * first * -0.5) * ((2.0 * math.pi) ** -0.5)
    activated = first * gate
    mixed_ref[...] = (activated * second).astype(BF16).reshape(mixed_ref.shape)
    grad = jnp.concatenate(
        [(grad_mixed * second * slope).astype(BF16), (grad_mixed * activated).astype(BF16)],
        axis=1,
    )
    lifted_ref[...] = grad.reshape(lifted_ref.shape)
    partial = dot(grad, w_ref[...], ((1,), (1,))).astype(BF16).reshape(low_ref.shape)
    start = 0
    for out, end in zip(out_refs, ends):

        @pl.when((step >= start) & (step < end))
        def _(out=out):
            out[...] = partial

        start = end


def mlp(pieces, grad_mixed, w, ends, earlier=()):
    seqs, block, width = pieces[0].shape[1:]
    hidden = w.shape[1] // 2
    base = 4 if earlier else 0

    def rows(last):
        return pl.BlockSpec((1, seqs, block, last), lambda i: (i + base, 0, 0, 0))

    def within(start, end):
        return pl.BlockSpec(
            (1, seqs, block, width),
            lambda i: (jnp.clip(i - start, 0, end - start - 1), 0, 0, 0),
        )

    starts = (0, *ends[:-1])
    return pl.pallas_call(
        functools.partial(mlp_kernel, ends=ends),
        grid=(4,),
        in_specs=[whole(piece) for piece in pieces]
        + [rows(hidden), whole(w)]
        + [pl.BlockSpec(memory_space=pl.ANY)] * len(earlier),
        out_specs=(
            rows(width),
            rows(hidden),
            rows(2 * hidden),
            *[within(start, end) for start, end in zip(starts, ends)],
        ),
        out_shape=(
            jax.ShapeDtypeStruct((8, seqs, block, width), BF16),
            jax.ShapeDtypeStruct((8, seqs, block, hidden), BF16),
            jax.ShapeDtypeStruct((8, seqs, block, 2 * hidden), BF16),
            *[
                jax.ShapeDtypeStruct((end - start, seqs, block, width), BF16)
                for start, end in zip(starts, ends)
            ],
        ),
        input_output_aliases={5 + at: at for at in range(len(earlier))},
        compiler_params=params(),
        cost_estimate=COST,
        name="mlp",
    )(*pieces, grad_mixed, w, *earlier)


def out_grad_kernel(place_ref, rows_ref, grad_ref, keep_ref, send_ref):
    grads = flat(grad_ref[...])
    for index in range(8):
        part = dot(flat(rows_ref[place_ref[index]]), grads, ((0,), (0,))).astype(BF16)
        if index < 5:
            keep_ref[index] = part
        else:
            send_ref[index - 5] = part


def out_grad(place, rows, grads):
    part, width = rows.shape[-1], grads.shape[-1]
    return pl.pallas_call(
        out_grad_kernel,
        in_specs=[SCALARS, whole(rows), whole(grads)],
        out_shape=(
            jax.ShapeDtypeStruct((5, part, width), BF16),
            jax.ShapeDtypeStruct((3, part, width), BF16),
        ),
        compiler_params=params(),
        cost_estimate=COST,
        name="out_grad",
    )(place, rows, grads)


def branch_back_kernel(place_ref, *refs):
    pieces = refs[:6]
    keep_ref, near_ref, own_ref, residual_ref, top_ref, gain_ref = refs[6:12]
    grad_ref, branch_ref, home_ref, sum_ref = refs[12:]
    grad_low = wide(flat(keep_ref[...])) + wide(flat(near_ref[...])) + wide(flat(own_ref[...]))
    normed, factor = normalize(flat(residual_ref[...]))
    sum_ref[...] = jnp.sum(grad_low * normed, axis=0, keepdims=True)
    grad = flat(top_ref[...].astype(F32)) + norm_back(grad_low * gain_ref[...], normed, factor)
    grad_ref[...] = grad.reshape(grad_ref.shape)
    low = grad.astype(BF16)
    branch_ref[...] = low.reshape(branch_ref.shape)
    index = 0
    for piece in pieces:
        for inner in range(piece.shape[0]):
            home_ref[place_ref[index]] = (
                dot(low, piece[inner], ((1,), (1,))).astype(BF16).reshape(home_ref.shape[1:])
            )
            index += 1


def branch_back(place, pieces, keep, near, own, residual, top, gain):
    args = (*pieces, keep, near, own, residual, top, gain)
    seqs, block, width = residual.shape
    shapes = (
        jax.ShapeDtypeStruct(residual.shape, F32),
        jax.ShapeDtypeStruct(residual.shape, BF16),
        jax.ShapeDtypeStruct((8, seqs, block, pieces[0].shape[1]), BF16),
        jax.ShapeDtypeStruct((1, width), F32),
    )
    return pl.pallas_call(
        branch_back_kernel,
        grid=(1,),
        in_specs=[SCALARS]
        + [whole(piece) for piece in pieces]
        + [pl.BlockSpec((1, seqs, block, width), lambda *_: (0, 0, 0, 0))] * 2
        + [whole(a) for a in args[8:]],
        out_specs=tuple(whole(shape) for shape in shapes),
        out_shape=shapes,
        compiler_params=params(),
        cost_estimate=COST,
        name="branch_back",
    )(place, *args)


def attend_back_kernel(
    place_ref, q_ref, k_ref, v_ref, grad_ref, att_ref, log_ref, cosq_ref, sinq_ref, cos_ref,
    sin_ref, w_ref, low_ref, *refs, seq, last,
):
    if last:
        before_ref, keep_ref, send_ref, grad_w_ref, gain_ref, proj_ref, sum_k, sum_v = refs
    else:
        keep_ref, send_ref, before_ref, proj_ref, sum_k, sum_v = refs
    step = pl.program_id(0)
    block, part = q_ref.shape[2], q_ref.shape[3]

    @pl.when(step == 0)
    def _():
        sum_k[...] = jnp.zeros_like(sum_k)
        sum_v[...] = jnp.zeros_like(sum_v)

    queries, keys, values = flat(q_ref[...]), flat(k_ref[...]), flat(v_ref[...])
    grads = jnp.concatenate([grad_ref[place_ref[2 * step + inner], seq] for inner in range(2)])
    along = (grads.astype(F32) * flat(att_ref[...])).T
    logs = flat(log_ref[...]).T
    grad_queries = jnp.zeros(queries.shape, F32)
    for head, mask in enumerate(head_masks(queries.shape)):
        own_q = jnp.where(mask, queries, 0)
        own_g = jnp.where(mask, grads, 0)
        scores = dot(keys, own_q, ((1,), (1,)))
        weights = jnp.exp(scores - logs[head * HD : head * HD + 1])
        lifted = dot(values, own_g, ((1,), (1,)))
        row = jnp.sum(along[head * HD : (head + 1) * HD], axis=0, keepdims=True)
        grad_scores = (weights * (lifted - row)).astype(BF16)
        sum_k[...] += dot(grad_scores, own_q)
        sum_v[...] += dot(weights.astype(BF16), own_g)
        grad_queries = jnp.where(mask, dot(grad_scores, keys, ((0,), (0,))), grad_queries)
    grad_queries = lane_rotate(grad_queries * HD**-0.5, cosq_ref[...], -sinq_ref[...])
    rows = pl.multiple_of(step * 2 * block, 2 * block)
    proj_ref[pl.ds(rows, 2 * block), :part] = grad_queries.astype(BF16)

    @pl.when(step == 3)
    def _():
        grad_keys = lane_rotate(sum_k[...], cos_ref[...], -sin_ref[...])
        proj_ref[:, part : 2 * part] = grad_keys.astype(BF16)
        proj_ref[:, 2 * part :] = sum_v[...].astype(BF16)
        partial = dot(proj_ref[...], w_ref[...], ((1,), (1,))).astype(BF16)
        keep_ref[:, 0] = partial[: 5 * block].reshape(5, block, -1)
        send_ref[:, 0] = partial[5 * block :].reshape(3, block, -1)
        grad_w = dot(proj_ref[...], flat(low_ref[...]), ((0,), (0,)))
        if last:
            grad_w = (grad_w + before_ref[...]).T
            grad_w_ref[...] = grad_w.astype(BF16)
            along_w = jnp.sum(grad_w * w_ref[...].astype(F32), axis=1, keepdims=True)
            gain_ref[...] = jnp.broadcast_to(along_w, (w_ref.shape[0], 128)).T[:8]
        else:
            before_ref[...] = grad_w


def attend_back(place, qkv, grads, attended, logs, cosine, sine, w, low, seq, before=None):
    _, _, block, own = qkv.shape
    part, width = own // 3, w.shape[0]
    last = before is not None
    rows = pl.BlockSpec((2, 1, block, part), lambda i: (i, 0, 0, 0))
    angles = pl.BlockSpec((2 * block, part), lambda i: (i, 0))

    def full(*shape):
        return pl.BlockSpec(shape, lambda i: (0,) * len(shape))

    args = [place, qkv, qkv, qkv, grads, attended, logs, cosine, sine, cosine, sine, w, low]
    in_specs = [
        SCALARS,
        pl.BlockSpec((2, 1, block, part), lambda i: (i, seq, 0, 0)),
        pl.BlockSpec((8, 1, block, part), lambda i: (0, seq, 0, 1)),
        pl.BlockSpec((8, 1, block, part), lambda i: (0, seq, 0, 2)),
        whole(grads),
        rows,
        rows,
        angles,
        angles,
        whole(cosine),
        whole(sine),
        whole(w),
        pl.BlockSpec((8, 1, block, width), lambda i: (0, seq, 0, 0)),
    ]
    shapes = [((5, 1, block, width), BF16), ((3, 1, block, width), BF16)]
    if last:
        args.append(before)
        in_specs.append(whole(before))
        shapes += [((width, own), BF16), ((8, width), F32)]
    else:
        shapes += [((own, width), F32)]
    return pl.pallas_call(
        functools.partial(attend_back_kernel, seq=seq, last=last),
        grid=(4,),
        in_specs=in_specs,
        out_specs=tuple(full(*shape) for shape, _ in shapes),
        out_shape=tuple(jax.ShapeDtypeStruct(shape, kind) for shape, kind in shapes),
        scratch_shapes=[
            pltpu.VMEM((8 * block, own), BF16),
            pltpu.VMEM((8 * block, part), F32),
            pltpu.VMEM((8 * block, part), F32),
        ],
        compiler_params=params(),
        cost_estimate=COST,
        name="attend_back",
    )(*args)


class Group:
    def __init__(self):
        self.heads = lax.axis_size("head")
        self.dp = lax.axis_size("dp")
        self.ctx_at = lax.axis_index("ctx")
        self.head_at = lax.axis_index("head")
        self.dp_at = lax.axis_index("dp")
        self.at = self.ctx_at * self.heads + self.head_at
        near, far = [], []
        for c in range(2):
            for h in range(self.heads):
                x, y = (c ^ 1) * self.heads + h, c * self.heads + (h ^ 2)
                near.append((c * self.heads + h, x if h % 2 == 0 else y))
                far.append((c * self.heads + h, y if h % 2 == 0 else x))
        self.near, self.far = near, far

    def order(self):
        first = jnp.where(self.head_at % 2 == 0, 4, 2)
        second = 6 - first
        return jnp.stack(
            [self.at ^ bits for bits in (0, 1, first, first ^ 1, 6, second ^ 1, second, 7)]
        )

    def swap(self, values, bit):
        if bit == 4:
            return lax.ppermute(values, "ctx", [(0, 1), (1, 0)])
        return lax.ppermute(values, "head", [(i, i ^ bit) for i in range(self.heads)])

    def mate(self, values):
        return self.swap(values, 1)

    def to_near(self, values):
        return lax.ppermute(values, GROUP, self.near)

    def to_far(self, values):
        return lax.ppermute(values, GROUP, self.far)

    def rows_in(self, values, place):
        inverse = [place.index(i) for i in range(self.heads)]
        turns = [[], []]
        for source in range(self.dp):
            target = inverse[source]
            for d in range(self.dp):
                step = (d - source) % self.dp
                head = (target & 2) | ((target ^ step) & 1)
                turns[step // 2].append((source * self.heads + head, d * self.heads + target))
        first, second = (lax.ppermute(values, ("dp", "head"), pairs) for pairs in turns)
        source = sum(jnp.where(self.head_at == h, place[h], 0) for h in range(self.heads))
        step = (self.dp_at - source) % self.dp
        return first, second, step < 2

    def rows_back(self, values, place):
        pairs = [
            (d * self.heads + h, place[h] * self.heads + d)
            for d in range(self.dp)
            for h in range(self.heads)
        ]
        return lax.ppermute(values, ("dp", "head"), pairs)

    def across(self, values, step):
        return lax.ppermute(values, "dp", [(i, i ^ step) for i in range(self.dp)])

    def total(self, values, bits):
        for bit in bits:
            other = self.swap(values, bit) if bit < 8 else self.across(values, bit // 8)
            values = values + other
        return values


def pick(array, index, axis):
    return lax.dynamic_index_in_dim(array, index, axis, keepdims=False)


def after(values, *earlier):
    return lax.optimization_barrier((values, earlier))[0]


def local_split(tokens, cotangent, w_qkv, w_attn_out, w_in, w_mlp_out, norm_gain1, norm_gain2):
    seqs, block, width = tokens.shape
    group = Group()
    heads, dp = group.heads, group.dp
    at_c, at_h = group.ctx_at, group.head_at
    parts = 2 * heads
    hidden = w_in.shape[1] // 2 // parts
    padded = -(-hidden // 128) * 128
    own_width = width // parts
    half = heads // 2
    rows_here = w_qkv.shape[0]
    place = [2 * (h % half) + h // half for h in range(heads)]
    straight = list(range(heads))
    order = group.order()
    scalars = jnp.concatenate([order, jnp.stack([group.dp_at, at_c])]).astype(jnp.int32)
    mate, near, far = group.mate, group.to_near, group.to_far

    def in_order(own, other):
        return jnp.where(at_c == 0, jnp.stack([own, other]), jnp.stack([other, own]))

    def exchange(values):
        return lax.all_to_all(values, GROUP, split_axis=0, concat_axis=0, tiled=True)


    gains = jnp.pad(
        jnp.stack([norm_gain1, norm_gain2]), ((0, 14), (0, 3 * own_width - rows_here))
    )
    qkv_view = w_qkv.reshape(rows_here, 3, width)

    def qkv_part(at):
        start = (2 * at_h + at) * own_width
        cut = lax.dynamic_slice_in_dim(qkv_view, start, own_width, 2)
        return jnp.concatenate([cut.reshape(rows_here, 3 * own_width), gains])

    x_own = tokens[None]
    x_mate = mate(x_own)
    qkv_other, qkv_own = qkv_part(1 - at_c), qkv_part(at_c)
    qkv_cross = group.swap(after(qkv_other, x_own), 4)
    x_chip = jnp.concatenate([x_own, after(x_mate, qkv_cross, qkv_own)])
    x_near = near(x_chip)
    qkv_pair = jnp.stack([qkv_own, qkv_cross])
    qkv_pieces = [qkv_pair] + [group.across(qkv_pair, step) for step in range(1, dp)]

    x_near = after(x_near, *qkv_pieces[:-1])
    x_far = far(x_near[:1])
    x_near_mate = mate(x_near)
    in_view = after(w_in, x_near).reshape(rows_here, 2, heads, 2, hidden)
    in_view = pick(in_view, 2 * (at_h % half) + at_h // half, 2)

    def in_part(at):
        cut = pick(in_view, at, 2)
        return jnp.pad(cut, ((0, 0), (0, 0), (0, padded - hidden))).reshape(rows_here, 2 * padded)

    in_other, in_own = in_part(1 - at_c), in_part(at_c)
    in_cross = group.swap(in_other, 4)
    positions = after(order, x_near)[:, None] * block + jnp.arange(block, dtype=jnp.int32)
    lane = jnp.arange(own_width, dtype=jnp.int32)
    frequency = jnp.exp(
        (lane % (HD // 2)).astype(F32) * (-math.log(ROPE_BASE) / (HD // 2))
    )
    angles = wide(positions.reshape(-1))[:, None] * frequency[None, :]
    cosine = jnp.cos(angles)
    sine = jnp.sin(angles) * jnp.where(lane % HD < HD // 2, -1.0, 1.0)[None, :]
    out_first, out_second, out_turn = group.rows_in(after(w_attn_out, x_near), straight)
    cot_own = after(cotangent, x_near)[None]
    cot_mate = mate(cot_own)
    x_far = after(x_far, in_other, in_own, cosine, sine, qkv_pieces[-1], cot_mate)
    x_far_mate = mate(x_far)

    in_pair = in_order(in_own, after(in_cross, x_far))
    weight_in = lax.all_gather(in_pair, "dp", axis=0).reshape(width, -1)
    cot_chip = jnp.concatenate([cot_own, cot_mate])
    cot_near = near(after(cot_chip, x_far))
    out_own = jnp.where(out_turn, out_first, after(out_second, x_far))[None]
    out_mate = mate(out_own)
    x_pieces = (
        x_own, x_mate, x_near, x_far, x_near_mate, after(x_far_mate, in_pair, cot_chip, out_own)
    )
    low1, qkv, weight_qkv, gain_one, gain_two = project(
        scalars, x_pieces, qkv_pieces, cosine, sine
    )

    out_near = near(jnp.concatenate([out_own, after(out_mate, qkv)]))
    att_0, log_0, home_0 = attend(scalars, after(qkv, out_mate))
    cot_near = after(cot_near, home_0)
    cot_far, cot_near_mate = far(cot_near[:1]), mate(cot_near)
    out_near = after(out_near, home_0)
    out_far, out_near_mate = far(out_near[:1]), mate(out_near)
    mlp_first, mlp_second, mlp_turn = group.rows_in(after(w_mlp_out, home_0), place)
    att_1, log_1, home = attend(scalars, after(qkv, cot_near, out_near), home_0)
    att_rows = exchange(home)
    out_far_mate, cot_far_mate = mate(after(out_far, home)), mate(after(cot_far, home))
    out_pieces = (out_own, out_mate, out_near, out_far, out_near_mate, out_far_mate)
    residual, low2 = branch(
        scalars, out_pieces, after(att_rows, cot_far_mate), tokens, gain_two
    )

    low_own = low2[None]
    low_mate = mate(low_own)
    low_near = near(jnp.concatenate([low_own, after(low_mate, weight_in, mlp_first, mlp_second)]))
    cot_all = jnp.concatenate(
        [
            cot_own,
            cot_mate,
            cot_near,
            cot_far,
            cot_near_mate,
            after(cot_far_mate, low_mate),
        ]
    )
    weight_mlp = jnp.where(mlp_turn, mlp_first, after(mlp_second, low_mate))
    weight_mlp = jnp.pad(weight_mlp, ((0, padded - hidden), (0, 0)))
    grad_mixed = dot(flat(cot_all), weight_mlp, ((1,), (1,)))
    grad_mixed = grad_mixed.reshape(8, seqs, block, padded)
    low_near = after(low_near, grad_mixed)
    low_far, low_near_mate = far(low_near[:1]), mate(low_near)
    *firsts, keep = mlp((low_own, low_mate, low_near), grad_mixed, weight_in, (4,))
    low_far_mate = mate(after(low_far, keep))
    low2_all, mixed, grad_lifted, keep_far, send = mlp(
        (low_far, low_near_mate, low_far_mate), grad_mixed, weight_in, (1, 4), firsts
    )

    def over_tokens(left, right):
        return dot(flat(left), flat(right), ((0,), (0,)))

    def scatter(values):
        return lax.psum_scatter(values.astype(BF16), "dp", scatter_dimension=0, tiled=True)

    def columns_first(values):
        return jnp.moveaxis(values.reshape(values.shape[0], dp, -1), 1, 0)

    met = mate(send)
    grad_mlp = columns_first(over_tokens(after(mixed, send), cot_all)[:hidden]).astype(BF16)
    met = after(met, grad_mlp)
    grad_mlp = scatter(grad_mlp)[0]
    last = (wide(keep_far[0]) + wide(met[2])).astype(BF16)
    last_far = far(last)
    cut = 5 * seqs * block
    mixed_flat = flat(after(mixed, last))
    out_keep = dot(mixed_flat[:cut], weight_mlp).astype(BF16).reshape(5, seqs, block, width)
    out_send = dot(mixed_flat[cut:], weight_mlp).astype(BF16).reshape(3, seqs, block, width)
    last_far = after(last_far, out_keep, out_send)
    chip = jnp.stack([wide(keep[2]) + wide(met[0]) + wide(last_far), wide(keep[3]) + wide(met[1])])
    chip = chip.astype(BF16)
    chip_near = near(chip)
    out_met = mate(after(out_send, chip))
    grad_in = over_tokens(low2_all, after(grad_lifted, chip)).astype(BF16)
    chip_near = after(chip_near, grad_in)
    grad_in = scatter(grad_in)
    home = mate((wide(keep[1]) + wide(chip_near[1])).astype(BF16))
    grad_residual, grad_branch, home, gain2_sum = branch_back(
        scalars, out_pieces, keep, chip_near, after(home, grad_mlp), residual, cotangent, gain_two
    )
    grad_home = exchange(home)

    rows_keep, rows_send = out_grad(scalars, after(att_rows, home), grad_branch)
    rows_met = mate(rows_send)
    out_last = (wide(out_keep[4]) + wide(after(out_met, home)[2])).astype(BF16)
    rows_last = (wide(rows_keep[4]) + wide(rows_met[2])).astype(BF16)
    grad_home = after(grad_home, out_last, rows_last)
    out_far2, rows_far = far(after(out_last, grad_home)), far(after(rows_last, grad_home))
    keep_0, send_0, before = attend_back(
        scalars, qkv, grad_home, att_0, log_0, cosine, sine, weight_qkv, low1, 0
    )
    met_0 = mate(send_0)
    grad_in = after(grad_in, send_0)

    def rows_here_of(values):
        pair = values.reshape(2, rows_here, -1)
        own = pick(pair, at_c, 0)
        other = group.swap(pick(pair, 1 - at_c, 0), 4)
        return in_order(own, other)

    grad_in = rows_here_of(grad_in)
    out_far2, rows_far = after((out_far2, rows_far), send_0)
    out_chip = jnp.stack(
        [
            wide(out_keep[2]) + wide(out_met[0]) + wide(out_far2),
            wide(out_keep[3]) + wide(out_met[1]),
        ]
    ).astype(BF16)
    rows_chip = jnp.stack(
        [
            wide(rows_keep[2]) + wide(rows_met[0]) + wide(rows_far),
            wide(rows_keep[3]) + wide(rows_met[1]),
        ]
    ).astype(BF16)
    out_chip_near, rows_chip_near = near(out_chip), near(rows_chip)
    keep_1, send_1, grad_qkv, gain1_sum = attend_back(
        scalars, qkv, after(grad_home, out_chip, rows_chip), att_1, log_1, cosine, sine,
        weight_qkv, low1, 1, before,
    )

    met_1 = mate(after(send_1, grad_in))
    grad_qkv = scatter(grad_qkv)

    def both(index, at):
        return jnp.concatenate(
            [wide(keep_0[index]) + wide(met_0[at]), wide(keep_1[index]) + wide(met_1[at])]
        )

    last = both(4, 2).astype(BF16)
    last_far = far(last)
    rows_chip_near = after(rows_chip_near, last)
    out_chip_near = after(out_chip_near, last)
    rows_home = mate((wide(rows_keep[1]) + wide(rows_chip_near[1])).astype(BF16))
    out_home = mate((wide(out_keep[1]) + wide(out_chip_near[1])).astype(BF16))
    sums = jnp.stack([gain1_sum[0] / gain_one[0], gain2_sum[0]]).reshape(-1, 128)
    sums = group.total(after(sums, last), (1, 2))
    last_far = after(last_far, sums)
    chip = jnp.stack([both(2, 0) + wide(last_far), both(3, 1)]).astype(BF16)
    chip_near = near(chip)
    result = residual + wide(out_keep[0]) + wide(out_chip_near[0]) + wide(after(out_home, chip))
    result = result.astype(BF16)
    grad_out = wide(rows_keep[0]) + wide(rows_chip_near[0]) + wide(after(rows_home, chip))
    grad_out = scatter(columns_first(grad_out.astype(BF16)))[0]
    sums = group.total(after(sums, chip), (4, 8, 16)).reshape(2, -1)
    grad_mlp = group.rows_back(after(grad_mlp, chip), place)
    grad_qkv = rows_here_of(grad_qkv)
    late = at_h // half
    grad_in = jnp.stack([grad_in[..., :hidden], grad_in[..., padded : padded + hidden]])
    stays = pick(after(grad_in, chip), late, 0)
    comes = group.swap(pick(after(grad_in, chip), 1 - late, 0), half)
    chip_near = after(chip_near, sums, comes, result, grad_qkv, grad_mlp)
    grad_out = wide(group.rows_back(grad_out, straight))
    home = mate(
        (jnp.concatenate([wide(keep_0[1]), wide(keep_1[1])]) + wide(chip_near[1])).astype(BF16)
    )
    grad_low1 = jnp.concatenate([wide(keep_0[0]), wide(keep_1[0])]) + wide(chip_near[0])
    grad_low1 = grad_low1 + wide(home)
    normed1, factor1 = normalize(wide(tokens))
    grad_input = grad_residual + norm_back(grad_low1 * gain_one, normed1, factor1)

    grad_mlp = wide(grad_mlp)
    grad_in = jnp.where(
        late == 0, jnp.concatenate([stays, comes]), jnp.concatenate([comes, stays])
    )
    grad_in = wide(jnp.moveaxis(grad_in, 0, 1).reshape(rows_here, -1))

    per_device = width // (dp * parts)
    start = (group.dp_at * parts + group.at) * per_device
    grad_gain1, grad_gain2 = (
        lax.dynamic_slice_in_dim(sums[i], start, per_device, 0) for i in range(2)
    )
    grad_qkv = grad_qkv.reshape(2, rows_here, 3, own_width)
    grad_qkv = jnp.moveaxis(grad_qkv, 2, 0)
    odd = at_h % 2
    stays = pick(grad_qkv, odd + late, 0)
    core = group.swap(pick(grad_qkv, 1 - odd + late, 0), 1)
    chip = group.swap(pick(grad_qkv, 2 - 2 * late, 0), 2)
    grad_qkv = jnp.where(
        odd == 0, jnp.concatenate([stays, core, chip]), jnp.concatenate([chip, core, stays])
    )
    grad_qkv = wide(jnp.moveaxis(grad_qkv, 0, 1).reshape(rows_here, -1))

    return (
        result,
        grad_input,
        grad_qkv,
        grad_out,
        grad_in,
        grad_mlp,
        grad_gain1,
        grad_gain2,
    )


def local(tokens, cotangent, w_qkv, w_attn_out, w_in, w_mlp_out, norm_gain1, norm_gain2):
    args = (tokens, cotangent, w_qkv, w_attn_out, w_in, w_mlp_out, norm_gain1, norm_gain2)
    sizes = [lax.axis_size(axis) for axis in ("dp", "ctx", "head")]
    if sizes == [4, 2, 4] and tokens.shape[2] == 8 * 2 * HD and tokens.shape[1] % 16 == 0:
        return local_split(*args)
    return local_general(*args)


def solution(mesh):
    in_specs = (
        P("dp", ("ctx", "head"), None),
        P("dp", ("ctx", "head"), None),
        P(("dp", "ctx"), None),
        P(("dp", "ctx"), None),
        P(("dp", "ctx"), None),
        P(("dp", "ctx"), None),
        P(("dp", "ctx")),
        P(("dp", "ctx")),
    )
    out_specs = (
        P("dp", ("ctx", "head"), None),
        P("dp", ("ctx", "head"), None),
        P(("dp", "ctx"), "head"),
        P(("dp", "ctx"), "head"),
        P(("dp", "ctx"), "head"),
        P(("dp", "ctx"), "head"),
        P(("dp", "ctx", "head")),
        P(("dp", "ctx", "head")),
    )
    return jax.shard_map(local, mesh=mesh, in_specs=in_specs, out_specs=out_specs, check_vma=False)
```

```python
import functools
import math

import jax
import jax.numpy as jnp
from jax import lax
from jax.experimental import pallas as pl
from jax.experimental.pallas import tpu as pltpu
from jax.sharding import PartitionSpec as P

HD = 64


EPSILON = 1e-05
ROPE_BASE = 160000.0


def normalize(values):
    centre = jnp.mean(values, axis=-1, keepdims=True)
    shifted = values - centre
    spread = jnp.mean(shifted * shifted, axis=-1, keepdims=True)
    factor = lax.rsqrt(spread + EPSILON)
    return (shifted * factor, factor)


def norm_back(grad_normed, normed, factor):
    grad_centre = jnp.mean(grad_normed, axis=-1, keepdims=True)
    grad_along = jnp.mean(grad_normed * normed, axis=-1, keepdims=True)
    return (grad_normed - grad_centre - normed * grad_along) * factor


def rope_tables(positions, half_size):
    frequency = jnp.exp(
        jnp.arange(half_size, dtype=jnp.float32) * (-math.log(ROPE_BASE) / half_size)
    )
    angles = positions[:, None] * frequency[None, :]
    return (jnp.cos(angles), jnp.sin(angles))


def rotate(values, cosine, sine_table, direction):
    half_size = cosine.shape[-1]
    first_half = values[..., :half_size]
    second_half = values[..., half_size:]
    cos_part = cosine[:, None, :]
    sin_part = sine_table[:, None, :] * direction
    return jnp.concatenate(
        [
            first_half * cos_part - second_half * sin_part,
            second_half * cos_part + first_half * sin_part,
        ],
        axis=-1,
    )


def block_scores(queries4, keys_block, scale):
    keys4 = keys_block.reshape(
        keys_block.shape[0], keys_block.shape[1], queries4.shape[2], queries4.shape[3]
    )
    return (
        jnp.einsum("sqgd,skgd->sgqk", queries4, keys4, preferred_element_type=jnp.float32) * scale
    )


def attend_forward(queries4, keys_all, values_all, key_rows, scale):
    seqs_here, query_rows, groups, head_size = queries4.shape
    turns = keys_all.shape[1] // key_rows

    def statistics(turn, carry):
        row_peak, row_total = carry
        keys_block = lax.dynamic_slice_in_dim(keys_all, turn * key_rows, key_rows, 1)
        scores = block_scores(queries4, keys_block, scale)
        new_peak = jnp.maximum(row_peak, jnp.max(scores, axis=-1))
        row_total = row_total * jnp.exp(row_peak - new_peak) + jnp.sum(
            jnp.exp(scores - new_peak[..., None]), axis=-1
        )
        return (new_peak, row_total)

    start_peak = jnp.full((seqs_here, groups, query_rows), -1e30, jnp.float32)
    row_peak, row_total = lax.fori_loop(
        0, turns, statistics, (start_peak, jnp.zeros_like(start_peak))
    )
    log_total = row_peak + jnp.log(row_total)

    def accumulate(turn, running):
        keys_block = lax.dynamic_slice_in_dim(keys_all, turn * key_rows, key_rows, 1)
        values_block = lax.dynamic_slice_in_dim(values_all, turn * key_rows, key_rows, 1).reshape(
            seqs_here, key_rows, groups, head_size
        )
        weights = jnp.exp(block_scores(queries4, keys_block, scale) - log_total[..., None]).astype(
            jnp.bfloat16
        )
        return running + jnp.einsum(
            "sgqk,skgd->sqgd", weights, values_block, preferred_element_type=jnp.float32
        )

    attended = lax.fori_loop(
        0, turns, accumulate, jnp.zeros((seqs_here, query_rows, groups, head_size), jnp.float32)
    )
    return (attended, log_total)


def attend_backward(queries4, keys_all, values_all, grad_out4, log_total, along, key_rows, scale):
    seqs_here, query_rows, groups, head_size = queries4.shape
    length = keys_all.shape[1]
    width_group = groups * head_size
    turns = length // key_rows

    def step_back(turn, carry):
        grad_queries, grad_keys, grad_values = carry
        keys_block = lax.dynamic_slice_in_dim(keys_all, turn * key_rows, key_rows, 1)
        keys4 = keys_block.reshape(seqs_here, key_rows, groups, head_size)
        values4 = lax.dynamic_slice_in_dim(values_all, turn * key_rows, key_rows, 1).reshape(
            seqs_here, key_rows, groups, head_size
        )
        weights = jnp.exp(block_scores(queries4, keys_block, scale) - log_total[..., None])
        grad_weights = jnp.einsum(
            "sqgd,skgd->sgqk", grad_out4, values4, preferred_element_type=jnp.float32
        )
        grad_scores = (weights * (grad_weights - along[..., None])).astype(jnp.bfloat16)
        grad_queries = grad_queries + jnp.einsum(
            "sgqk,skgd->sqgd", grad_scores, keys4, preferred_element_type=jnp.float32
        )
        key_part = (
            jnp.einsum("sgqk,sqgd->skgd", grad_scores, queries4, preferred_element_type=jnp.float32)
            * scale
        )
        value_part = jnp.einsum(
            "sgqk,sqgd->skgd",
            weights.astype(jnp.bfloat16),
            grad_out4,
            preferred_element_type=jnp.float32,
        )
        grad_keys = lax.dynamic_update_slice_in_dim(
            grad_keys, key_part.reshape(seqs_here, key_rows, width_group), turn * key_rows, 1
        )
        grad_values = lax.dynamic_update_slice_in_dim(
            grad_values, value_part.reshape(seqs_here, key_rows, width_group), turn * key_rows, 1
        )
        return (grad_queries, grad_keys, grad_values)

    start = (
        jnp.zeros((seqs_here, query_rows, groups, head_size), jnp.float32),
        jnp.zeros((seqs_here, length, width_group), jnp.float32),
        jnp.zeros((seqs_here, length, width_group), jnp.float32),
    )
    grad_queries, grad_keys, grad_values = lax.fori_loop(0, turns, step_back, start)
    return (grad_queries * scale, grad_keys, grad_values)


def local_general(tokens, cotangent, w_qkv, w_attn_out, w_in, w_mlp_out, norm_gain1, norm_gain2):
    seqs_here, block_rows, width = tokens.shape
    count_rows = seqs_here * block_rows
    heads_all = width // HD
    head_devices = lax.axis_size("head")
    group_devices = lax.axis_size(("dp", "ctx"))
    groups = heads_all // head_devices
    width_group = groups * HD
    scale = HD ** (-0.5)
    ff_width = w_in.shape[1] // 2
    full_qkv, full_out, full_in, full_mlp, gain_one, gain_two = (
        lax.all_gather(w_qkv, ("dp", "ctx"), axis=0, tiled=True),
        lax.all_gather(w_attn_out, ("dp", "ctx"), axis=0, tiled=True),
        lax.all_gather(w_in, ("dp", "ctx"), axis=0, tiled=True),
        lax.all_gather(w_mlp_out, ("dp", "ctx"), axis=0, tiled=True),
        lax.all_gather(norm_gain1, ("dp", "ctx"), axis=0, tiled=True),
        lax.all_gather(norm_gain2, ("dp", "ctx"), axis=0, tiled=True),
    )
    x_in = tokens.astype(jnp.float32).reshape(count_rows, width)
    normed1, factor1 = normalize(x_in)
    lowered1 = (normed1 * gain_one.astype(jnp.float32)).astype(jnp.bfloat16)
    projected = jnp.dot(lowered1, full_qkv, preferred_element_type=jnp.float32).reshape(
        seqs_here, block_rows, 3, heads_all, HD
    )
    first_pos = (lax.axis_index("ctx") * head_devices + lax.axis_index("head")) * block_rows
    positions = (first_pos + jnp.arange(block_rows, dtype=jnp.int32)).astype(jnp.float32)
    cosine, sine_table = rope_tables(positions, HD // 2)
    queries = (
        rotate(projected[:, :, 0], cosine, sine_table, 1.0)
        .astype(jnp.bfloat16)
        .reshape(seqs_here, block_rows, width)
    )
    keys_local = (
        rotate(projected[:, :, 1], cosine, sine_table, 1.0)
        .astype(jnp.bfloat16)
        .reshape(seqs_here, block_rows, width)
    )
    values_local = projected[:, :, 2].astype(jnp.bfloat16).reshape(seqs_here, block_rows, width)
    queries_h, keys_h, values_h = (
        lax.all_to_all(queries, "head", split_axis=2, concat_axis=1, tiled=True),
        lax.all_to_all(keys_local, "head", split_axis=2, concat_axis=1, tiled=True),
        lax.all_to_all(values_local, "head", split_axis=2, concat_axis=1, tiled=True),
    )
    query_rows = queries_h.shape[1]
    queries4 = queries_h.reshape(seqs_here, query_rows, groups, HD)
    keys_all, values_all = (
        lax.all_gather(keys_h, "ctx", axis=1, tiled=True),
        lax.all_gather(values_h, "ctx", axis=1, tiled=True),
    )
    key_rows = math.gcd(keys_all.shape[1], 1024)
    attended, log_total = attend_forward(queries4, keys_all, values_all, key_rows, scale)
    attended_low = attended.astype(jnp.bfloat16).reshape(seqs_here, query_rows, width_group)
    back_rows = lax.all_to_all(
        attended_low, "head", split_axis=1, concat_axis=2, tiled=True
    ).reshape(count_rows, width)
    residual = x_in + jnp.dot(back_rows, full_out, preferred_element_type=jnp.float32)
    normed2, factor2 = normalize(residual)
    lowered2 = (normed2 * gain_two.astype(jnp.float32)).astype(jnp.bfloat16)
    lifted = jnp.dot(lowered2, full_in, preferred_element_type=jnp.float32)
    first_part = lifted[:, :ff_width]
    second_part = lifted[:, ff_width:]
    activated, gelu_pullback = jax.vjp(
        lambda entries: jax.nn.gelu(entries, approximate=False), first_part
    )
    mixed = (activated * second_part).astype(jnp.bfloat16)
    result = (residual + jnp.dot(mixed, full_mlp, preferred_element_type=jnp.float32)).astype(
        jnp.bfloat16
    )
    full_qkv, full_out, full_in, full_mlp, gain_one, gain_two = (
        lax.all_gather(w_qkv, ("dp", "ctx"), axis=0, tiled=True),
        lax.all_gather(w_attn_out, ("dp", "ctx"), axis=0, tiled=True),
        lax.all_gather(w_in, ("dp", "ctx"), axis=0, tiled=True),
        lax.all_gather(w_mlp_out, ("dp", "ctx"), axis=0, tiled=True),
        lax.all_gather(norm_gain1, ("dp", "ctx"), axis=0, tiled=True),
        lax.all_gather(norm_gain2, ("dp", "ctx"), axis=0, tiled=True),
    )
    keys_all, values_all = (
        lax.all_gather(keys_h, "ctx", axis=1, tiled=True),
        lax.all_gather(values_h, "ctx", axis=1, tiled=True),
    )
    grad_top = cotangent.reshape(count_rows, width)
    grad_mlp = jnp.einsum("nf,nd->fd", mixed, grad_top, preferred_element_type=jnp.float32)
    grad_mixed = jnp.einsum("nd,fd->nf", grad_top, full_mlp, preferred_element_type=jnp.float32)
    grad_first = gelu_pullback(grad_mixed * second_part)[0]
    grad_lifted = jnp.concatenate([grad_first, grad_mixed * activated], axis=-1).astype(
        jnp.bfloat16
    )
    grad_inner = jnp.einsum("nd,nf->df", lowered2, grad_lifted, preferred_element_type=jnp.float32)
    grad_lowered2 = jnp.einsum(
        "nf,df->nd", grad_lifted, full_in, preferred_element_type=jnp.float32
    )
    grad_two = jnp.sum(grad_lowered2 * normed2, axis=0)
    grad_residual = grad_top.astype(jnp.float32) + norm_back(
        grad_lowered2 * gain_two.astype(jnp.float32), normed2, factor2
    )
    grad_branch = grad_residual.astype(jnp.bfloat16)
    grad_outproj = jnp.einsum(
        "nd,ne->de", back_rows, grad_branch, preferred_element_type=jnp.float32
    )
    grad_attended = jnp.einsum(
        "ne,de->nd", grad_branch, full_out, preferred_element_type=jnp.float32
    ).astype(jnp.bfloat16)
    grad_attended_h = lax.all_to_all(
        grad_attended.reshape(seqs_here, block_rows, width),
        "head",
        split_axis=2,
        concat_axis=1,
        tiled=True,
    )
    grad_out4 = grad_attended_h.reshape(seqs_here, query_rows, groups, HD)
    along = jnp.transpose(jnp.sum(grad_out4.astype(jnp.float32) * attended, axis=-1), (0, 2, 1))
    grad_queries, grad_keys_all, grad_values_all = attend_backward(
        queries4, keys_all, values_all, grad_out4, log_total, along, key_rows, scale
    )
    grad_keys_sum, grad_values_sum = (
        lax.psum_scatter(
            grad_keys_all.astype(jnp.bfloat16), "ctx", scatter_dimension=1, tiled=True
        ).astype(jnp.float32),
        lax.psum_scatter(
            grad_values_all.astype(jnp.bfloat16), "ctx", scatter_dimension=1, tiled=True
        ).astype(jnp.float32),
    )
    grad_q_low = grad_queries.astype(jnp.bfloat16).reshape(seqs_here, query_rows, width_group)
    grad_q_tok, grad_k_tok, grad_v_tok = (
        lax.all_to_all(grad_q_low, "head", split_axis=1, concat_axis=2, tiled=True),
        lax.all_to_all(
            grad_keys_sum.astype(jnp.bfloat16), "head", split_axis=1, concat_axis=2, tiled=True
        ),
        lax.all_to_all(
            grad_values_sum.astype(jnp.bfloat16), "head", split_axis=1, concat_axis=2, tiled=True
        ),
    )
    unrot_q = rotate(
        grad_q_tok.astype(jnp.float32).reshape(seqs_here, block_rows, heads_all, HD),
        cosine,
        sine_table,
        -1.0,
    )
    unrot_k = rotate(
        grad_k_tok.astype(jnp.float32).reshape(seqs_here, block_rows, heads_all, HD),
        cosine,
        sine_table,
        -1.0,
    )
    grad_projected = jnp.concatenate(
        [
            unrot_q.reshape(count_rows, width),
            unrot_k.reshape(count_rows, width),
            grad_v_tok.astype(jnp.float32).reshape(count_rows, width),
        ],
        axis=-1,
    ).astype(jnp.bfloat16)
    grad_project = jnp.einsum(
        "nd,nf->df", lowered1, grad_projected, preferred_element_type=jnp.float32
    )
    grad_lowered1 = jnp.einsum(
        "nf,df->nd", grad_projected, full_qkv, preferred_element_type=jnp.float32
    )
    grad_one = jnp.sum(grad_lowered1 * normed1, axis=0)
    grad_input = grad_residual + norm_back(
        grad_lowered1 * gain_one.astype(jnp.float32), normed1, factor1
    )
    pieces_one = grad_one.reshape(group_devices, head_devices, -1)
    pieces_two = grad_two.reshape(group_devices, head_devices, -1)
    part_qkv, part_out, part_in, part_mlp, part_one, part_two = (
        lax.psum_scatter(
            grad_project.astype(jnp.bfloat16), ("dp", "ctx"), scatter_dimension=0, tiled=True
        ).astype(jnp.float32),
        lax.psum_scatter(
            grad_outproj.astype(jnp.bfloat16), ("dp", "ctx"), scatter_dimension=0, tiled=True
        ).astype(jnp.float32),
        lax.psum_scatter(
            grad_inner.astype(jnp.bfloat16), ("dp", "ctx"), scatter_dimension=0, tiled=True
        ).astype(jnp.float32),
        lax.psum_scatter(
            grad_mlp.astype(jnp.bfloat16), ("dp", "ctx"), scatter_dimension=0, tiled=True
        ).astype(jnp.float32),
        lax.psum_scatter(
            pieces_one.astype(jnp.bfloat16), ("dp", "ctx"), scatter_dimension=0, tiled=True
        ).astype(jnp.float32),
        lax.psum_scatter(
            pieces_two.astype(jnp.bfloat16), ("dp", "ctx"), scatter_dimension=0, tiled=True
        ).astype(jnp.float32),
    )
    final_qkv, final_out, final_in, final_mlp, final_one, final_two = (
        lax.psum_scatter(
            part_qkv.astype(jnp.bfloat16), "head", scatter_dimension=1, tiled=True
        ).astype(jnp.float32),
        lax.psum_scatter(
            part_out.astype(jnp.bfloat16), "head", scatter_dimension=1, tiled=True
        ).astype(jnp.float32),
        lax.psum_scatter(
            part_in.astype(jnp.bfloat16), "head", scatter_dimension=1, tiled=True
        ).astype(jnp.float32),
        lax.psum_scatter(
            part_mlp.astype(jnp.bfloat16), "head", scatter_dimension=1, tiled=True
        ).astype(jnp.float32),
        lax.psum_scatter(
            part_one.astype(jnp.bfloat16), "head", scatter_dimension=1, tiled=True
        ).astype(jnp.float32),
        lax.psum_scatter(
            part_two.astype(jnp.bfloat16), "head", scatter_dimension=1, tiled=True
        ).astype(jnp.float32),
    )
    return (
        result.reshape(seqs_here, block_rows, width),
        grad_input.reshape(seqs_here, block_rows, width),
        final_qkv,
        final_out,
        final_in,
        final_mlp,
        final_one.reshape(-1),
        final_two.reshape(-1),
    )


F32 = jnp.float32
BF16 = jnp.bfloat16
VMEM_BYTES = 56 * 1024 * 1024
GROUP = ("ctx", "head")


def dot(left, right, dims=((1,), (0,))):
    return lax.dot_general(left, right, (dims, ((), ())), preferred_element_type=F32)


def wide(values):
    return values.astype(F32)


def flat(values):
    return values.reshape(-1, values.shape[-1])


def lane_rotate(values, cosine, sine_signed):
    lane = lax.broadcasted_iota(jnp.int32, values.shape, 1)
    width = values.shape[1]
    partner = jnp.where(
        lane % HD < HD // 2,
        pltpu.roll(values, width - HD // 2, 1),
        pltpu.roll(values, HD // 2, 1),
    )
    return values * cosine + partner * sine_signed


def head_masks(shape):
    lane = lax.broadcasted_iota(jnp.int32, shape, 1)
    return [lane // HD == head for head in range(shape[1] // HD)]


def params():
    return pltpu.CompilerParams(vmem_limit_bytes=VMEM_BYTES)


COST = pl.CostEstimate(flops=1 << 20, transcendentals=0, bytes_accessed=1 << 16)


def whole(array):
    return pl.BlockSpec(array.shape, lambda *_: (0,) * len(array.shape))


SCALARS = pl.BlockSpec(memory_space=pltpu.SMEM)


def project_kernel(place_ref, *refs):
    pieces, weights = refs[:6], refs[6:10]
    cos_ref, sin_ref, low_ref, qkv_ref, w_ref, gain1_ref, gain2_ref, rows_ref = refs[10:]
    block, part = pieces[0].shape[2], w_ref.shape[1] // 3
    rows = gain1_ref.shape[1] // 8

    @pl.when(pl.program_id(0) == 0)
    def _():
        for step, piece in enumerate(weights):
            for turn in range(2):
                at = 2 * (place_ref[8] ^ step) + (place_ref[9] ^ turn)
                w_ref[pl.ds(pl.multiple_of(at * rows, rows), rows), :] = piece[turn, :rows]
                gains = piece[turn, rows:].astype(F32)
                rows_ref[0, pl.ds(at, 1), :] = gains[:1, :rows]
                rows_ref[1, pl.ds(at, 1), :] = gains[1:2, :rows]
        for out, at in ((gain1_ref, 0), (gain2_ref, 1)):
            for row in range(8):
                out[:, row * rows : (row + 1) * rows] = rows_ref[at, row : row + 1, :]

    gain = gain1_ref[...]
    index = 0
    for piece in pieces:
        for inner in range(piece.shape[0]):
            normed, _ = normalize(piece[inner, 0].astype(F32))
            low_ref[index, 0] = (normed * gain).astype(BF16)
            index += 1
    projected = dot(flat(low_ref[:, 0]), w_ref[...])
    cosine, sine = cos_ref[...], sin_ref[...]
    shape = (8, block, part)
    qkv_ref[:, 0, :, :part] = (
        (lane_rotate(projected[:, :part], cosine, sine) * HD**-0.5).astype(BF16).reshape(shape)
    )
    qkv_ref[:, 0, :, part : 2 * part] = (
        lane_rotate(projected[:, part : 2 * part], cosine, sine).astype(BF16).reshape(shape)
    )
    qkv_ref[:, 0, :, 2 * part :] = projected[:, 2 * part :].astype(BF16).reshape(shape)


def project(place, pieces, weights, cosine, sine):
    seqs, block, width = pieces[0].shape[1:]
    own = weights[0].shape[2]

    def by_seq(lead, last):
        return pl.BlockSpec((lead, 1, block, last), lambda s: (0, s, 0, 0))

    return pl.pallas_call(
        project_kernel,
        grid=(seqs,),
        in_specs=[SCALARS]
        + [by_seq(piece.shape[0], width) for piece in pieces]
        + [whole(w) for w in weights]
        + [whole(cosine), whole(sine)],
        out_specs=(
            by_seq(8, width),
            by_seq(8, own),
            pl.BlockSpec((width, own), lambda s: (0, 0)),
            pl.BlockSpec((1, width), lambda s: (0, 0)),
            pl.BlockSpec((1, width), lambda s: (0, 0)),
        ),
        out_shape=(
            jax.ShapeDtypeStruct((8, seqs, block, width), BF16),
            jax.ShapeDtypeStruct((8, seqs, block, own), BF16),
            jax.ShapeDtypeStruct((width, own), BF16),
            jax.ShapeDtypeStruct((1, width), F32),
            jax.ShapeDtypeStruct((1, width), F32),
        ),
        scratch_shapes=[pltpu.VMEM((2, 8, width // 8), F32)],
        compiler_params=params(),
        cost_estimate=COST,
        name="project",
    )(place, *pieces, *weights, cosine, sine)


def attend_kernel(place_ref, q_ref, k_ref, v_ref, *refs):
    att_ref, log_ref, home_ref = refs[-3:]
    step, seq = pl.program_id(0), len(refs) - 3
    if seq:

        @pl.when(step == 0)
        def _():
            home_ref[:, :1] = refs[0][...]

    queries, keys, values = flat(q_ref[...]), flat(k_ref[...]), flat(v_ref[...])
    attended = jnp.zeros(queries.shape, F32)
    logs = jnp.zeros(queries.shape, F32)
    for mask in head_masks(queries.shape):
        scores = dot(jnp.where(mask, queries, 0), keys, ((1,), (1,)))
        peak = jnp.max(scores, axis=1, keepdims=True)
        weights = jnp.exp(scores - peak)
        total = jnp.sum(weights, axis=1, keepdims=True)
        mixed = dot(weights.astype(BF16), values) * (1.0 / total)
        attended = jnp.where(mask, mixed, attended)
        logs = jnp.where(mask, peak + jnp.log(total), logs)
    att_ref[...] = attended.reshape(att_ref.shape)
    log_ref[...] = logs.reshape(log_ref.shape)
    low = attended.astype(BF16).reshape(att_ref.shape)
    for inner in range(2):
        home_ref[place_ref[2 * step + inner], seq] = low[inner, 0]


def attend(place, qkv, *home):
    _, _, block, own = qkv.shape
    part, seq = own // 3, len(home)
    rows = pl.BlockSpec((2, 1, block, part), lambda i: (i, 0, 0, 0))
    shape = (8, 1, block, part)
    return pl.pallas_call(
        attend_kernel,
        grid=(4,),
        in_specs=[
            SCALARS,
            pl.BlockSpec((2, 1, block, part), lambda i: (i, seq, 0, 0)),
            pl.BlockSpec((8, 1, block, part), lambda i: (0, seq, 0, 1)),
            pl.BlockSpec((8, 1, block, part), lambda i: (0, seq, 0, 2)),
            *[whole(h) for h in home],
        ],
        out_specs=(
            rows,
            rows,
            pl.BlockSpec((8, 1 + seq, block, part), lambda i: (0, 0, 0, 0)),
        ),
        out_shape=(
            jax.ShapeDtypeStruct(shape, F32),
            jax.ShapeDtypeStruct(shape, F32),
            jax.ShapeDtypeStruct((8, 1 + seq, block, part), BF16),
        ),
        compiler_params=params(),
        cost_estimate=COST,
        name="attend",
    )(place, qkv, qkv, qkv, *home)


def branch_kernel(place_ref, *refs):
    pieces = refs[:6]
    rows_ref, tokens_ref, gain_ref, residual_ref, low_ref = refs[6:]
    total = flat(tokens_ref[...].astype(F32))
    index = 0
    for piece in pieces:
        for inner in range(piece.shape[0]):
            total += dot(flat(rows_ref[place_ref[index]]), piece[inner])
            index += 1
    normed, _ = normalize(total)
    residual_ref[...] = total.reshape(residual_ref.shape)
    low_ref[...] = (normed * gain_ref[...]).astype(BF16).reshape(low_ref.shape)


def branch(place, pieces, rows, tokens, gain):
    args = (*pieces, rows, tokens, gain)
    return pl.pallas_call(
        branch_kernel,
        in_specs=[SCALARS] + [whole(a) for a in args],
        out_shape=(
            jax.ShapeDtypeStruct(tokens.shape, F32),
            jax.ShapeDtypeStruct(tokens.shape, BF16),
        ),
        compiler_params=params(),
        cost_estimate=COST,
        name="branch",
    )(place, *args)


def combine(*groups):
    parts = [part for group in groups for part in group]
    block = parts[0][0].shape[1:]
    zeros = (0,) * len(block)

    def kernel(*refs):
        at = 0
        for k, group in enumerate(groups):
            total = wide(refs[at][0])
            for ref in refs[at + 1 : at + len(group)]:
                total += wide(ref[0])
            refs[-1][k] = total.astype(BF16)
            at += len(group)

    return pl.pallas_call(
        kernel,
        grid=(1,),
        in_specs=[
            pl.BlockSpec((1, *block), lambda *_, index=index: (index, *zeros))
            for _, index in parts
        ],
        out_specs=pl.BlockSpec((len(groups), *block), lambda *_: (0, *zeros)),
        out_shape=jax.ShapeDtypeStruct((len(groups), *block), BF16),
        compiler_params=params(),
        cost_estimate=COST,
        name="combine",
    )(*[array for array, _ in parts])


def mlp_kernel(*refs, count, ends):
    pieces, tops = refs[:count], refs[count : 2 * count]
    w_ref, out_w_ref = refs[2 * count : 2 * count + 2]
    low_ref, top_ref, mixed_ref, lifted_ref, *out_refs = refs[-4 - len(ends) :]
    step = pl.program_id(0)
    start = 0
    for piece, top in zip(pieces, tops):

        @pl.when((step >= start) & (step < start + piece.shape[0]))
        def _(piece=piece, top=top, start=start):
            low_ref[0] = piece[step - start]
            top_ref[0] = top[step - start]

        start += piece.shape[0]

    hidden = w_ref.shape[1] // 2
    lifted = dot(flat(low_ref[...]), w_ref[...])
    first, second = lifted[:, :hidden], lifted[:, hidden:]
    grad_mixed = dot(flat(top_ref[...]), out_w_ref[...], ((1,), (1,)))
    gate = 0.5 * (1.0 + lax.erf(first * (0.5**0.5)))
    slope = gate + first * jnp.exp(first * first * -0.5) * ((2.0 * math.pi) ** -0.5)
    activated = first * gate
    mixed_ref[...] = (activated * second).astype(BF16).reshape(mixed_ref.shape)
    grad = jnp.concatenate(
        [(grad_mixed * second * slope).astype(BF16), (grad_mixed * activated).astype(BF16)],
        axis=1,
    )
    lifted_ref[...] = grad.reshape(lifted_ref.shape)
    partial = dot(grad, w_ref[...], ((1,), (1,))).astype(BF16).reshape(low_ref.shape)
    start = 0
    for out, end in zip(out_refs, ends):

        @pl.when((step >= start) & (step < end))
        def _(out=out):
            out[...] = partial

        start = end


def mlp(pieces, tops, w, out_w, base, ends, earlier=()):
    seqs, block, width = pieces[0].shape[1:]
    hidden = w.shape[1] // 2
    whole_in = (*pieces, *tops, w, out_w)

    def rows(last):
        return pl.BlockSpec((1, seqs, block, last), lambda i: (i + base, 0, 0, 0))

    def within(start, end):
        return pl.BlockSpec(
            (1, seqs, block, width),
            lambda i: (jnp.clip(i - start, 0, end - start - 1), 0, 0, 0),
        )

    starts = (0, *ends[:-1])
    lasts = (width, width, hidden, 2 * hidden)
    return pl.pallas_call(
        functools.partial(mlp_kernel, count=len(pieces), ends=ends),
        grid=(ends[-1],),
        in_specs=[whole(array) for array in whole_in]
        + [pl.BlockSpec(memory_space=pl.ANY)] * len(earlier),
        out_specs=(
            *[rows(last) for last in lasts],
            *[within(start, end) for start, end in zip(starts, ends)],
        ),
        out_shape=(
            *[jax.ShapeDtypeStruct((8, seqs, block, last), BF16) for last in lasts],
            *[
                jax.ShapeDtypeStruct((end - start, seqs, block, width), BF16)
                for start, end in zip(starts, ends)
            ],
        ),
        input_output_aliases={len(whole_in) + at: at for at in range(len(earlier))},
        compiler_params=params(),
        cost_estimate=COST,
        name="mlp",
    )(*whole_in, *earlier)


def out_grad_kernel(place_ref, rows_ref, grad_ref, keep_ref, send_ref):
    grads = flat(grad_ref[...])
    for index in range(8):
        part = dot(flat(rows_ref[place_ref[index]]), grads, ((0,), (0,))).astype(BF16)
        if index < 5:
            keep_ref[index] = part
        else:
            send_ref[index - 5] = part


def out_grad(place, rows, grads):
    part, width = rows.shape[-1], grads.shape[-1]
    return pl.pallas_call(
        out_grad_kernel,
        in_specs=[SCALARS, whole(rows), whole(grads)],
        out_shape=(
            jax.ShapeDtypeStruct((5, part, width), BF16),
            jax.ShapeDtypeStruct((3, part, width), BF16),
        ),
        compiler_params=params(),
        cost_estimate=COST,
        name="out_grad",
    )(place, rows, grads)


def branch_back_kernel(place_ref, *refs):
    pieces = refs[:6]
    keep_ref, near_ref, own_ref, residual_ref, top_ref, gain_ref = refs[6:12]
    grad_ref, branch_ref, home_ref, sum_ref = refs[12:]
    grad_low = wide(flat(keep_ref[...])) + wide(flat(near_ref[...])) + wide(flat(own_ref[...]))
    normed, factor = normalize(flat(residual_ref[...]))
    sum_ref[...] = jnp.sum(grad_low * normed, axis=0, keepdims=True)
    grad = flat(top_ref[...].astype(F32)) + norm_back(grad_low * gain_ref[...], normed, factor)
    grad_ref[...] = grad.reshape(grad_ref.shape)
    low = grad.astype(BF16)
    branch_ref[...] = low.reshape(branch_ref.shape)
    index = 0
    for piece in pieces:
        for inner in range(piece.shape[0]):
            home_ref[place_ref[index]] = (
                dot(low, piece[inner], ((1,), (1,))).astype(BF16).reshape(home_ref.shape[1:])
            )
            index += 1


def branch_back(place, pieces, keep, near, own, residual, top, gain):
    args = (*pieces, keep, near, own, residual, top, gain)
    seqs, block, width = residual.shape
    shapes = (
        jax.ShapeDtypeStruct(residual.shape, F32),
        jax.ShapeDtypeStruct(residual.shape, BF16),
        jax.ShapeDtypeStruct((8, seqs, block, pieces[0].shape[1]), BF16),
        jax.ShapeDtypeStruct((1, width), F32),
    )
    return pl.pallas_call(
        branch_back_kernel,
        grid=(1,),
        in_specs=[SCALARS]
        + [whole(piece) for piece in pieces]
        + [pl.BlockSpec((1, seqs, block, width), lambda *_: (0, 0, 0, 0))] * 2
        + [whole(a) for a in args[8:]],
        out_specs=tuple(whole(shape) for shape in shapes),
        out_shape=shapes,
        compiler_params=params(),
        cost_estimate=COST,
        name="branch_back",
    )(place, *args)


def attend_back_kernel(
    place_ref, q_ref, k_ref, v_ref, grad_ref, att_ref, log_ref, cosq_ref, sinq_ref, cos_ref,
    sin_ref, w_ref, low_ref, *refs, seq, last,
):
    if last:
        before_ref, keep_ref, send_ref, grad_w_ref, gain_ref, proj_ref, sum_k, sum_v = refs
    else:
        keep_ref, send_ref, before_ref, proj_ref, sum_k, sum_v = refs
    step = pl.program_id(0)
    block, part = q_ref.shape[2], q_ref.shape[3]

    @pl.when(step == 0)
    def _():
        sum_k[...] = jnp.zeros_like(sum_k)
        sum_v[...] = jnp.zeros_like(sum_v)

    queries, keys, values = flat(q_ref[...]), flat(k_ref[...]), flat(v_ref[...])
    grads = jnp.concatenate([grad_ref[place_ref[2 * step + inner], seq] for inner in range(2)])
    along = (grads.astype(F32) * flat(att_ref[...])).T
    logs = flat(log_ref[...]).T
    grad_queries = jnp.zeros(queries.shape, F32)
    for head, mask in enumerate(head_masks(queries.shape)):
        own_q = jnp.where(mask, queries, 0)
        own_g = jnp.where(mask, grads, 0)
        scores = dot(keys, own_q, ((1,), (1,)))
        weights = jnp.exp(scores - logs[head * HD : head * HD + 1])
        lifted = dot(values, own_g, ((1,), (1,)))
        row = jnp.sum(along[head * HD : (head + 1) * HD], axis=0, keepdims=True)
        grad_scores = (weights * (lifted - row)).astype(BF16)
        sum_k[...] += dot(grad_scores, own_q)
        sum_v[...] += dot(weights.astype(BF16), own_g)
        grad_queries = jnp.where(mask, dot(grad_scores, keys, ((0,), (0,))), grad_queries)
    grad_queries = lane_rotate(grad_queries * HD**-0.5, cosq_ref[...], -sinq_ref[...])
    rows = pl.multiple_of(step * 2 * block, 2 * block)
    proj_ref[pl.ds(rows, 2 * block), :part] = grad_queries.astype(BF16)

    @pl.when(step == 3)
    def _():
        grad_keys = lane_rotate(sum_k[...], cos_ref[...], -sin_ref[...])
        proj_ref[:, part : 2 * part] = grad_keys.astype(BF16)
        proj_ref[:, 2 * part :] = sum_v[...].astype(BF16)
        partial = dot(proj_ref[...], w_ref[...], ((1,), (1,))).astype(BF16)
        keep_ref[:, 0] = partial[: 5 * block].reshape(5, block, -1)
        send_ref[:, 0] = partial[5 * block :].reshape(3, block, -1)
        grad_w = dot(proj_ref[...], flat(low_ref[...]), ((0,), (0,)))
        if last:
            grad_w = (grad_w + before_ref[...]).T
            grad_w_ref[...] = grad_w.astype(BF16)
            along_w = jnp.sum(grad_w * w_ref[...].astype(F32), axis=1, keepdims=True)
            gain_ref[...] = jnp.broadcast_to(along_w, (w_ref.shape[0], 128)).T[:8]
        else:
            before_ref[...] = grad_w


def attend_back(place, qkv, grads, attended, logs, cosine, sine, w, low, seq, before=None):
    _, _, block, own = qkv.shape
    part, width = own // 3, w.shape[0]
    last = before is not None
    rows = pl.BlockSpec((2, 1, block, part), lambda i: (i, 0, 0, 0))
    angles = pl.BlockSpec((2 * block, part), lambda i: (i, 0))

    def full(*shape):
        return pl.BlockSpec(shape, lambda i: (0,) * len(shape))

    args = [place, qkv, qkv, qkv, grads, attended, logs, cosine, sine, cosine, sine, w, low]
    in_specs = [
        SCALARS,
        pl.BlockSpec((2, 1, block, part), lambda i: (i, seq, 0, 0)),
        pl.BlockSpec((8, 1, block, part), lambda i: (0, seq, 0, 1)),
        pl.BlockSpec((8, 1, block, part), lambda i: (0, seq, 0, 2)),
        whole(grads),
        rows,
        rows,
        angles,
        angles,
        whole(cosine),
        whole(sine),
        whole(w),
        pl.BlockSpec((8, 1, block, width), lambda i: (0, seq, 0, 0)),
    ]
    shapes = [((5, 1, block, width), BF16), ((3, 1, block, width), BF16)]
    if last:
        args.append(before)
        in_specs.append(whole(before))
        shapes += [((width, own), BF16), ((8, width), F32)]
    else:
        shapes += [((own, width), F32)]
    return pl.pallas_call(
        functools.partial(attend_back_kernel, seq=seq, last=last),
        grid=(4,),
        in_specs=in_specs,
        out_specs=tuple(full(*shape) for shape, _ in shapes),
        out_shape=tuple(jax.ShapeDtypeStruct(shape, kind) for shape, kind in shapes),
        scratch_shapes=[
            pltpu.VMEM((8 * block, own), BF16),
            pltpu.VMEM((8 * block, part), F32),
            pltpu.VMEM((8 * block, part), F32),
        ],
        compiler_params=params(),
        cost_estimate=COST,
        name="attend_back",
    )(*args)


def input_grad_kernel(*refs):
    keeps, (near_ref, own_ref, tokens_ref, residual_ref, gain_ref, out_ref) = refs[:-6], refs[-6:]
    for seq, keep in enumerate(keeps):
        grad = wide(keep[0, 0]) + wide(near_ref[0, seq]) + wide(own_ref[seq])
        normed, factor = normalize(wide(tokens_ref[seq]))
        out_ref[seq] = residual_ref[seq] + norm_back(grad * gain_ref[...], normed, factor)


def input_grad(keeps, near, own, tokens, residual, gain):
    rest = (own, tokens, residual, gain)
    return pl.pallas_call(
        input_grad_kernel,
        grid=(1,),
        in_specs=[
            pl.BlockSpec((1, *array.shape[1:]), lambda *_: (0, 0, 0, 0)) for array in (*keeps, near)
        ]
        + [whole(array) for array in rest],
        out_specs=whole(residual),
        out_shape=jax.ShapeDtypeStruct(residual.shape, F32),
        compiler_params=params(),
        cost_estimate=COST,
        name="input_grad",
    )(*keeps, near, *rest)


class Group:
    def __init__(self):
        self.heads = lax.axis_size("head")
        self.dp = lax.axis_size("dp")
        self.ctx_at = lax.axis_index("ctx")
        self.head_at = lax.axis_index("head")
        self.dp_at = lax.axis_index("dp")
        self.at = self.ctx_at * self.heads + self.head_at
        near, far = [], []
        for c in range(2):
            for h in range(self.heads):
                x, y = (c ^ 1) * self.heads + h, c * self.heads + (h ^ 2)
                near.append((c * self.heads + h, x if h % 2 == 0 else y))
                far.append((c * self.heads + h, y if h % 2 == 0 else x))
        self.near, self.far = near, far

    def order(self):
        first = jnp.where(self.head_at % 2 == 0, 4, 2)
        second = 6 - first
        return jnp.stack(
            [self.at ^ bits for bits in (0, 1, first, first ^ 1, 6, second ^ 1, second, 7)]
        )

    def swap(self, values, bit):
        if bit == 4:
            return lax.ppermute(values, "ctx", [(0, 1), (1, 0)])
        return lax.ppermute(values, "head", [(i, i ^ bit) for i in range(self.heads)])

    def mate(self, values):
        return self.swap(values, 1)

    def to_near(self, values):
        return lax.ppermute(values, GROUP, self.near)

    def to_far(self, values):
        return lax.ppermute(values, GROUP, self.far)

    def rows_in(self, values, place):
        inverse = [place.index(i) for i in range(self.heads)]
        turns = [[], []]
        for source in range(self.dp):
            target = inverse[source]
            for d in range(self.dp):
                step = (d - source) % self.dp
                head = (target & 2) | ((target ^ step) & 1)
                if step:
                    turns[step // 2].append((source * self.heads + head, d * self.heads + target))
        return tuple(lax.ppermute(values, ("dp", "head"), pairs) for pairs in turns)

    def chosen(self, values, first, second, place):
        source = sum(jnp.where(self.head_at == h, place[h], 0) for h in range(self.heads))
        step = (self.dp_at - source) % self.dp
        return jnp.where(step == 0, values, jnp.where(step < 2, first, second))

    def rows_back(self, values, place):
        pairs, same = [], False
        for d in range(self.dp):
            for h in range(self.heads):
                if (d, h) == (place[h], d):
                    same = same | ((self.dp_at == d) & (self.head_at == h))
                else:
                    pairs.append((d * self.heads + h, place[h] * self.heads + d))
        return jnp.where(same, values, lax.ppermute(values, ("dp", "head"), pairs))

    def scatter_dp(self, values):
        step = self.dp // 2
        while step:
            n = values.shape[1] // 2
            bit = (self.dp_at // step) % 2
            sent = lax.dynamic_slice_in_dim(values, (1 - bit) * n, n, 1).astype(BF16)
            kept = lax.dynamic_slice_in_dim(values, bit * n, n, 1)
            values = wide(kept) + wide(self.across(sent, step))
            step //= 2
        return values

    def across(self, values, step):
        return lax.ppermute(values, "dp", [(i, i ^ step) for i in range(self.dp)])

    def total(self, values, bits):
        for bit in bits:
            other = self.swap(values, bit) if bit < 8 else self.across(values, bit // 8)
            values = values + other
        return values


def pick(array, index, axis):
    return lax.dynamic_index_in_dim(array, index, axis, keepdims=False)


def after(values, *earlier):
    return lax.optimization_barrier((values, earlier))[0]


def local_split(tokens, cotangent, w_qkv, w_attn_out, w_in, w_mlp_out, norm_gain1, norm_gain2):
    seqs, block, width = tokens.shape
    group = Group()
    heads, dp = group.heads, group.dp
    at_c, at_h = group.ctx_at, group.head_at
    parts = 2 * heads
    hidden = w_in.shape[1] // 2 // parts
    padded = -(-hidden // 128) * 128
    own_width = width // parts
    half = heads // 2
    rows_here = w_qkv.shape[0]
    place = [2 * (h % half) + h // half for h in range(heads)]
    straight = list(range(heads))
    order = group.order()
    scalars = jnp.concatenate([order, jnp.stack([group.dp_at, at_c])]).astype(jnp.int32)
    mate, near, far = group.mate, group.to_near, group.to_far

    def in_order(own, other):
        return jnp.where(at_c == 0, jnp.stack([own, other]), jnp.stack([other, own]))

    def exchange(values):
        return lax.all_to_all(values, GROUP, split_axis=0, concat_axis=0, tiled=True)


    gains = jnp.pad(
        jnp.stack([norm_gain1, norm_gain2]), ((0, 14), (0, 3 * own_width - rows_here))
    )
    qkv_view = w_qkv.reshape(rows_here, 3, width)

    def qkv_part(at):
        start = (2 * at_h + at) * own_width
        cut = lax.dynamic_slice_in_dim(qkv_view, start, own_width, 2)
        return jnp.concatenate([cut.reshape(rows_here, 3 * own_width), gains])

    x_own = tokens[None]
    x_mate = mate(x_own)
    qkv_other, qkv_own = qkv_part(1 - at_c), qkv_part(at_c)
    qkv_cross = group.swap(after(qkv_other, x_own), 4)
    x_chip = jnp.concatenate([x_own, after(x_mate, qkv_cross, qkv_own)])
    x_near = near(x_chip)
    qkv_pair = jnp.stack([qkv_own, qkv_cross])
    qkv_pieces = [qkv_pair] + [group.across(qkv_pair, step) for step in range(1, dp)]

    in_view = after(w_in, qkv_pair).reshape(rows_here, 2, heads, 2, hidden)
    in_view = pick(in_view, 2 * (at_h % half) + at_h // half, 2)

    def in_part(at):
        cut = pick(in_view, at, 2)
        return jnp.pad(cut, ((0, 0), (0, 0), (0, padded - hidden))).reshape(rows_here, 2 * padded)

    in_other, in_own = in_part(1 - at_c), in_part(at_c)
    in_cross = group.swap(in_other, 4)
    positions = after(order, qkv_pair)[:, None] * block + jnp.arange(block, dtype=jnp.int32)
    lane = jnp.arange(own_width, dtype=jnp.int32)
    frequency = jnp.exp(
        (lane % (HD // 2)).astype(F32) * (-math.log(ROPE_BASE) / (HD // 2))
    )
    angles = wide(positions.reshape(-1))[:, None] * frequency[None, :]
    cosine = jnp.cos(angles)
    sine = jnp.sin(angles) * jnp.where(lane % HD < HD // 2, -1.0, 1.0)[None, :]

    x_near = after(x_near, qkv_pieces[1], in_other, in_own, cosine, sine)
    x_far = far(x_near[:1])
    x_near_mate = mate(x_near)
    out_sent = group.rows_in(after(w_attn_out, x_near), straight)
    mlp_sent = group.rows_in(after(w_mlp_out, x_near), place)
    cot_own = after(cotangent, x_near)[None]
    cot_mate = mate(cot_own)
    x_far = after(x_far, qkv_pieces[2], qkv_pieces[3], cot_mate, in_cross)
    x_far_mate = mate(x_far)

    in_pair = in_order(in_own, in_cross)
    weight_in = lax.all_gather(in_pair, "dp", axis=0).reshape(width, -1)
    cot_chip = jnp.concatenate([cot_own, cot_mate])
    cot_near = near(after(cot_chip, x_far))
    out_own = group.chosen(w_attn_out, *after(out_sent, x_far), straight)[None]
    out_mate = mate(out_own)
    x_pieces = (
        x_own, x_mate, x_near, x_far, x_near_mate, after(x_far_mate, in_pair, cot_chip, out_own)
    )
    low1, qkv, weight_qkv, gain_one, gain_two = project(
        scalars, x_pieces, qkv_pieces, cosine, sine
    )

    out_near = near(jnp.concatenate([out_own, after(out_mate, qkv)]))
    att_0, log_0, home_0 = attend(scalars, after(qkv, out_mate))
    cot_near = after(cot_near, home_0)
    cot_far, cot_near_mate = far(cot_near[:1]), mate(cot_near)
    out_near = after(out_near, home_0)
    out_far, out_near_mate = far(out_near[:1]), mate(out_near)
    weight_mlp = group.chosen(w_mlp_out, *after(mlp_sent, home_0), place)
    weight_mlp = jnp.pad(weight_mlp, ((0, padded - hidden), (0, 0)))
    att_1, log_1, home = attend(scalars, after(qkv, cot_near, out_near, weight_mlp), home_0)
    att_rows = exchange(home)
    out_far_mate, cot_far_mate = mate(after(out_far, home)), mate(after(cot_far, home))
    out_pieces = (out_own, out_mate, out_near, out_far, out_near_mate, out_far_mate)
    residual, low2 = branch(
        scalars, out_pieces, after(att_rows, cot_far_mate), tokens, gain_two
    )

    low_own = low2[None]
    low_mate = mate(low_own)
    low_near = near(jnp.concatenate([low_own, low_mate]))
    *arrays, keep_a = mlp(
        (low_own, low_mate), (cot_own, cot_mate), weight_in, weight_mlp, 0, (2,)
    )
    low_near = after(low_near, keep_a)
    low_far, low_near_mate = far(low_near[:1]), mate(low_near)
    *arrays, keep_b = mlp((low_near,), (cot_near,), weight_in, weight_mlp, 2, (2,), arrays)
    low_far_mate = mate(after(low_far, keep_b))
    low2_all, cot_all, mixed, grad_lifted, keep_c, send = mlp(
        (low_far, low_near_mate, low_far_mate),
        (cot_far, cot_near_mate, cot_far_mate),
        weight_in,
        weight_mlp,
        4,
        (1, 4),
        arrays,
    )

    def over_tokens(left, right):
        return dot(flat(left), flat(right), ((0,), (0,)))

    def scatter(values):
        return lax.psum_scatter(values.astype(BF16), "dp", scatter_dimension=0, tiled=True)

    def columns_first(values):
        return jnp.moveaxis(values.reshape(values.shape[0], dp, -1), 1, 0)

    met = mate(send)
    last = combine([(keep_c, 0), (met, 2)])
    last_far = far(last)
    grad_mlp = columns_first(over_tokens(after(mixed, last), cot_all)[:hidden]).astype(BF16)
    last_far = after(last_far, grad_mlp)
    grad_mlp = scatter(grad_mlp)[0]
    chip = combine([(keep_b, 0), (met, 0), (last_far, 0)], [(keep_b, 1), (met, 1)])
    chip_near = near(chip)
    grad_in = over_tokens(low2_all, after(grad_lifted, chip)).astype(BF16)
    cut = 5 * seqs * block
    mixed_flat = flat(after(mixed, chip))
    out_keep = dot(mixed_flat[:cut], weight_mlp).astype(BF16).reshape(5, seqs, block, width)
    out_send = dot(mixed_flat[cut:], weight_mlp).astype(BF16).reshape(3, seqs, block, width)
    chip_near = after(chip_near, grad_in, out_keep, out_send)
    grad_in = scatter(grad_in)
    home = mate(combine([(keep_a, 1), (chip_near, 1)])[0])
    out_met = mate(after(out_send, chip_near))
    grad_residual, grad_branch, home, gain2_sum = branch_back(
        scalars, out_pieces, keep_a, chip_near, after(home, grad_mlp), residual, cotangent, gain_two
    )
    grad_home = exchange(home)

    rows_keep, rows_send = out_grad(scalars, after(att_rows, home), grad_branch)
    rows_met = mate(rows_send)
    out_last = combine([(after(out_keep, home), 4), (out_met, 2)])
    rows_last = combine([(rows_keep, 4), (rows_met, 2)])
    grad_home = after(grad_home, out_last, rows_last)
    out_far2, rows_far = far(after(out_last, grad_home)), far(after(rows_last, grad_home))
    keep_0, send_0, before = attend_back(
        scalars, qkv, grad_home, att_0, log_0, cosine, sine, weight_qkv, low1, 0
    )
    met_0 = mate(send_0)
    out_far2, rows_far = after((out_far2, rows_far), send_0)
    out_chip = combine(
        [(out_keep, 2), (out_met, 0), (out_far2, 0)], [(out_keep, 3), (out_met, 1)]
    )
    rows_chip = combine(
        [(rows_keep, 2), (rows_met, 0), (rows_far, 0)], [(rows_keep, 3), (rows_met, 1)]
    )
    out_near2, rows_near = near(out_chip), near(rows_chip)
    keep_1, send_1, grad_qkv, gain1_sum = attend_back(
        scalars, qkv, after(grad_home, out_chip, rows_chip), att_1, log_1, cosine, sine,
        weight_qkv, low1, 1, before,
    )

    def rows_here_of(values):
        pair = values.reshape(2, rows_here, -1)
        own = pick(pair, at_c, 0)
        other = group.swap(pick(pair, 1 - at_c, 0), 4)
        return in_order(own, other)

    met_1 = mate(send_1)
    grad_qkv = scatter(grad_qkv)
    out_near2, rows_near = after((out_near2, rows_near), send_1)
    rows_home = mate(combine([(rows_keep, 1), (rows_near, 1)])[0])
    sums = jnp.stack([gain1_sum[0] / gain_one[0], gain2_sum[0]]).reshape(-1, 128)
    sums = group.total(sums, (1,))
    met_1 = after(met_1, rows_home, sums)
    last = combine([(keep_0, 4), (met_0, 2)], [(keep_1, 4), (met_1, 2)])
    last_far = far(last.reshape(seqs, block, width)).reshape(seqs, 1, block, width)

    grad_in = rows_here_of(after(grad_in, last))
    out_home = mate(combine([(after(out_keep, last), 1), (out_near2, 1)])[0])
    grad_out = combine([(rows_keep, 0), (rows_near, 0), (after(rows_home, last)[None], 0)])[0]
    sums = group.total(after(sums, last), (2,))
    last_far = after(last_far, grad_out, out_home, sums)
    chip = combine(
        [(keep_0, 2), (met_0, 0), (last_far, 0)],
        [(keep_1, 2), (met_1, 0), (last_far, 1)],
        [(keep_0, 3), (met_0, 1)],
        [(keep_1, 3), (met_1, 1)],
    )
    chip_near = near(chip.reshape(2, seqs, block, width))

    grad_out = group.scatter_dp(after(grad_out, chip)).astype(BF16)
    result = (
        residual + wide(out_keep[0]) + wide(out_near2[0]) + wide(after(out_home, chip))
    ).astype(BF16)
    late = at_h // half
    grad_in = after(grad_in, chip)
    grad_in = jnp.stack([grad_in[..., :hidden], grad_in[..., padded : padded + hidden]])
    stays = pick(grad_in, late, 0)
    comes = group.swap(pick(grad_in, 1 - late, 0), half)
    sums = group.total(after(sums, chip), (4, 8))
    grad_mlp = group.rows_back(after(grad_mlp, chip), place)
    grad_qkv = rows_here_of(after(grad_qkv, chip))
    chip_near = after(chip_near, sums, comes, result, grad_qkv, grad_mlp, grad_out)
    chip_parts = chip_near.reshape(2 * seqs, 1, block, width)
    home = combine([(keep_0, 1), (chip_parts, 2)], [(keep_1, 1), (chip_parts, 3)])
    home = mate(home.reshape(seqs, block, width))
    sums = group.total(after(sums, home), (16,)).reshape(2, -1)
    grad_out = wide(group.rows_back(grad_out, straight))
    grad_input = input_grad(
        (keep_0, keep_1), chip_near, home, tokens, grad_residual, gain_one
    )

    grad_mlp = wide(grad_mlp)
    grad_in = jnp.where(
        late == 0, jnp.concatenate([stays, comes]), jnp.concatenate([comes, stays])
    )
    grad_in = wide(jnp.moveaxis(grad_in, 0, 1).reshape(rows_here, -1))

    per_device = width // (dp * parts)
    start = (group.dp_at * parts + group.at) * per_device
    grad_gain1, grad_gain2 = (
        lax.dynamic_slice_in_dim(sums[i], start, per_device, 0) for i in range(2)
    )
    grad_qkv = grad_qkv.reshape(2, rows_here, 3, own_width)
    grad_qkv = jnp.moveaxis(grad_qkv, 2, 0)
    odd = at_h % 2
    stays = pick(grad_qkv, odd + late, 0)
    core = group.swap(pick(grad_qkv, 1 - odd + late, 0), 1)
    chip = group.swap(pick(grad_qkv, 2 - 2 * late, 0), 2)
    grad_qkv = jnp.where(
        odd == 0, jnp.concatenate([stays, core, chip]), jnp.concatenate([chip, core, stays])
    )
    grad_qkv = wide(jnp.moveaxis(grad_qkv, 0, 1).reshape(rows_here, -1))

    return (
        result,
        grad_input,
        grad_qkv,
        grad_out,
        grad_in,
        grad_mlp,
        grad_gain1,
        grad_gain2,
    )


def local(tokens, cotangent, w_qkv, w_attn_out, w_in, w_mlp_out, norm_gain1, norm_gain2):
    args = (tokens, cotangent, w_qkv, w_attn_out, w_in, w_mlp_out, norm_gain1, norm_gain2)
    sizes = [lax.axis_size(axis) for axis in ("dp", "ctx", "head")]
    if sizes == [4, 2, 4] and tokens.shape[2] == 8 * 2 * HD and tokens.shape[1] % 16 == 0:
        return local_split(*args)
    return local_general(*args)


def solution(mesh):
    in_specs = (
        P("dp", ("ctx", "head"), None),
        P("dp", ("ctx", "head"), None),
        P(("dp", "ctx"), None),
        P(("dp", "ctx"), None),
        P(("dp", "ctx"), None),
        P(("dp", "ctx"), None),
        P(("dp", "ctx")),
        P(("dp", "ctx")),
    )
    out_specs = (
        P("dp", ("ctx", "head"), None),
        P("dp", ("ctx", "head"), None),
        P(("dp", "ctx"), "head"),
        P(("dp", "ctx"), "head"),
        P(("dp", "ctx"), "head"),
        P(("dp", "ctx"), "head"),
        P(("dp", "ctx", "head")),
        P(("dp", "ctx", "head")),
    )
    return jax.shard_map(local, mesh=mesh, in_specs=in_specs, out_specs=out_specs, check_vma=False)
```

```python
import functools
import math

import jax
import jax.numpy as jnp
from jax import lax
from jax.experimental import pallas as pl
from jax.experimental.pallas import tpu as pltpu
from jax.sharding import PartitionSpec as P

HD = 64


EPSILON = 1e-05
ROPE_BASE = 160000.0


def normalize(values):
    centre = jnp.mean(values, axis=-1, keepdims=True)
    shifted = values - centre
    spread = jnp.mean(shifted * shifted, axis=-1, keepdims=True)
    factor = lax.rsqrt(spread + EPSILON)
    return (shifted * factor, factor)


def norm_back(grad_normed, normed, factor):
    grad_centre = jnp.mean(grad_normed, axis=-1, keepdims=True)
    grad_along = jnp.mean(grad_normed * normed, axis=-1, keepdims=True)
    return (grad_normed - grad_centre - normed * grad_along) * factor


def rope_tables(positions, half_size):
    frequency = jnp.exp(
        jnp.arange(half_size, dtype=jnp.float32) * (-math.log(ROPE_BASE) / half_size)
    )
    angles = positions[:, None] * frequency[None, :]
    return (jnp.cos(angles), jnp.sin(angles))


def rotate(values, cosine, sine_table, direction):
    half_size = cosine.shape[-1]
    first_half = values[..., :half_size]
    second_half = values[..., half_size:]
    cos_part = cosine[:, None, :]
    sin_part = sine_table[:, None, :] * direction
    return jnp.concatenate(
        [
            first_half * cos_part - second_half * sin_part,
            second_half * cos_part + first_half * sin_part,
        ],
        axis=-1,
    )


def block_scores(queries4, keys_block, scale):
    keys4 = keys_block.reshape(
        keys_block.shape[0], keys_block.shape[1], queries4.shape[2], queries4.shape[3]
    )
    return (
        jnp.einsum("sqgd,skgd->sgqk", queries4, keys4, preferred_element_type=jnp.float32) * scale
    )


def attend_forward(queries4, keys_all, values_all, key_rows, scale):
    seqs_here, query_rows, groups, head_size = queries4.shape
    turns = keys_all.shape[1] // key_rows

    def statistics(turn, carry):
        row_peak, row_total = carry
        keys_block = lax.dynamic_slice_in_dim(keys_all, turn * key_rows, key_rows, 1)
        scores = block_scores(queries4, keys_block, scale)
        new_peak = jnp.maximum(row_peak, jnp.max(scores, axis=-1))
        row_total = row_total * jnp.exp(row_peak - new_peak) + jnp.sum(
            jnp.exp(scores - new_peak[..., None]), axis=-1
        )
        return (new_peak, row_total)

    start_peak = jnp.full((seqs_here, groups, query_rows), -1e30, jnp.float32)
    row_peak, row_total = lax.fori_loop(
        0, turns, statistics, (start_peak, jnp.zeros_like(start_peak))
    )
    log_total = row_peak + jnp.log(row_total)

    def accumulate(turn, running):
        keys_block = lax.dynamic_slice_in_dim(keys_all, turn * key_rows, key_rows, 1)
        values_block = lax.dynamic_slice_in_dim(values_all, turn * key_rows, key_rows, 1).reshape(
            seqs_here, key_rows, groups, head_size
        )
        weights = jnp.exp(block_scores(queries4, keys_block, scale) - log_total[..., None]).astype(
            jnp.bfloat16
        )
        return running + jnp.einsum(
            "sgqk,skgd->sqgd", weights, values_block, preferred_element_type=jnp.float32
        )

    attended = lax.fori_loop(
        0, turns, accumulate, jnp.zeros((seqs_here, query_rows, groups, head_size), jnp.float32)
    )
    return (attended, log_total)


def attend_backward(queries4, keys_all, values_all, grad_out4, log_total, along, key_rows, scale):
    seqs_here, query_rows, groups, head_size = queries4.shape
    length = keys_all.shape[1]
    width_group = groups * head_size
    turns = length // key_rows

    def step_back(turn, carry):
        grad_queries, grad_keys, grad_values = carry
        keys_block = lax.dynamic_slice_in_dim(keys_all, turn * key_rows, key_rows, 1)
        keys4 = keys_block.reshape(seqs_here, key_rows, groups, head_size)
        values4 = lax.dynamic_slice_in_dim(values_all, turn * key_rows, key_rows, 1).reshape(
            seqs_here, key_rows, groups, head_size
        )
        weights = jnp.exp(block_scores(queries4, keys_block, scale) - log_total[..., None])
        grad_weights = jnp.einsum(
            "sqgd,skgd->sgqk", grad_out4, values4, preferred_element_type=jnp.float32
        )
        grad_scores = (weights * (grad_weights - along[..., None])).astype(jnp.bfloat16)
        grad_queries = grad_queries + jnp.einsum(
            "sgqk,skgd->sqgd", grad_scores, keys4, preferred_element_type=jnp.float32
        )
        key_part = (
            jnp.einsum("sgqk,sqgd->skgd", grad_scores, queries4, preferred_element_type=jnp.float32)
            * scale
        )
        value_part = jnp.einsum(
            "sgqk,sqgd->skgd",
            weights.astype(jnp.bfloat16),
            grad_out4,
            preferred_element_type=jnp.float32,
        )
        grad_keys = lax.dynamic_update_slice_in_dim(
            grad_keys, key_part.reshape(seqs_here, key_rows, width_group), turn * key_rows, 1
        )
        grad_values = lax.dynamic_update_slice_in_dim(
            grad_values, value_part.reshape(seqs_here, key_rows, width_group), turn * key_rows, 1
        )
        return (grad_queries, grad_keys, grad_values)

    start = (
        jnp.zeros((seqs_here, query_rows, groups, head_size), jnp.float32),
        jnp.zeros((seqs_here, length, width_group), jnp.float32),
        jnp.zeros((seqs_here, length, width_group), jnp.float32),
    )
    grad_queries, grad_keys, grad_values = lax.fori_loop(0, turns, step_back, start)
    return (grad_queries * scale, grad_keys, grad_values)


def local_general(tokens, cotangent, w_qkv, w_attn_out, w_in, w_mlp_out, norm_gain1, norm_gain2):
    seqs_here, block_rows, width = tokens.shape
    count_rows = seqs_here * block_rows
    heads_all = width // HD
    head_devices = lax.axis_size("head")
    group_devices = lax.axis_size(("dp", "ctx"))
    groups = heads_all // head_devices
    width_group = groups * HD
    scale = HD ** (-0.5)
    ff_width = w_in.shape[1] // 2
    full_qkv, full_out, full_in, full_mlp, gain_one, gain_two = (
        lax.all_gather(w_qkv, ("dp", "ctx"), axis=0, tiled=True),
        lax.all_gather(w_attn_out, ("dp", "ctx"), axis=0, tiled=True),
        lax.all_gather(w_in, ("dp", "ctx"), axis=0, tiled=True),
        lax.all_gather(w_mlp_out, ("dp", "ctx"), axis=0, tiled=True),
        lax.all_gather(norm_gain1, ("dp", "ctx"), axis=0, tiled=True),
        lax.all_gather(norm_gain2, ("dp", "ctx"), axis=0, tiled=True),
    )
    x_in = tokens.astype(jnp.float32).reshape(count_rows, width)
    normed1, factor1 = normalize(x_in)
    lowered1 = (normed1 * gain_one.astype(jnp.float32)).astype(jnp.bfloat16)
    projected = jnp.dot(lowered1, full_qkv, preferred_element_type=jnp.float32).reshape(
        seqs_here, block_rows, 3, heads_all, HD
    )
    first_pos = (lax.axis_index("ctx") * head_devices + lax.axis_index("head")) * block_rows
    positions = (first_pos + jnp.arange(block_rows, dtype=jnp.int32)).astype(jnp.float32)
    cosine, sine_table = rope_tables(positions, HD // 2)
    queries = (
        rotate(projected[:, :, 0], cosine, sine_table, 1.0)
        .astype(jnp.bfloat16)
        .reshape(seqs_here, block_rows, width)
    )
    keys_local = (
        rotate(projected[:, :, 1], cosine, sine_table, 1.0)
        .astype(jnp.bfloat16)
        .reshape(seqs_here, block_rows, width)
    )
    values_local = projected[:, :, 2].astype(jnp.bfloat16).reshape(seqs_here, block_rows, width)
    queries_h, keys_h, values_h = (
        lax.all_to_all(queries, "head", split_axis=2, concat_axis=1, tiled=True),
        lax.all_to_all(keys_local, "head", split_axis=2, concat_axis=1, tiled=True),
        lax.all_to_all(values_local, "head", split_axis=2, concat_axis=1, tiled=True),
    )
    query_rows = queries_h.shape[1]
    queries4 = queries_h.reshape(seqs_here, query_rows, groups, HD)
    keys_all, values_all = (
        lax.all_gather(keys_h, "ctx", axis=1, tiled=True),
        lax.all_gather(values_h, "ctx", axis=1, tiled=True),
    )
    key_rows = math.gcd(keys_all.shape[1], 1024)
    attended, log_total = attend_forward(queries4, keys_all, values_all, key_rows, scale)
    attended_low = attended.astype(jnp.bfloat16).reshape(seqs_here, query_rows, width_group)
    back_rows = lax.all_to_all(
        attended_low, "head", split_axis=1, concat_axis=2, tiled=True
    ).reshape(count_rows, width)
    residual = x_in + jnp.dot(back_rows, full_out, preferred_element_type=jnp.float32)
    normed2, factor2 = normalize(residual)
    lowered2 = (normed2 * gain_two.astype(jnp.float32)).astype(jnp.bfloat16)
    lifted = jnp.dot(lowered2, full_in, preferred_element_type=jnp.float32)
    first_part = lifted[:, :ff_width]
    second_part = lifted[:, ff_width:]
    activated, gelu_pullback = jax.vjp(
        lambda entries: jax.nn.gelu(entries, approximate=False), first_part
    )
    mixed = (activated * second_part).astype(jnp.bfloat16)
    result = (residual + jnp.dot(mixed, full_mlp, preferred_element_type=jnp.float32)).astype(
        jnp.bfloat16
    )
    full_qkv, full_out, full_in, full_mlp, gain_one, gain_two = (
        lax.all_gather(w_qkv, ("dp", "ctx"), axis=0, tiled=True),
        lax.all_gather(w_attn_out, ("dp", "ctx"), axis=0, tiled=True),
        lax.all_gather(w_in, ("dp", "ctx"), axis=0, tiled=True),
        lax.all_gather(w_mlp_out, ("dp", "ctx"), axis=0, tiled=True),
        lax.all_gather(norm_gain1, ("dp", "ctx"), axis=0, tiled=True),
        lax.all_gather(norm_gain2, ("dp", "ctx"), axis=0, tiled=True),
    )
    keys_all, values_all = (
        lax.all_gather(keys_h, "ctx", axis=1, tiled=True),
        lax.all_gather(values_h, "ctx", axis=1, tiled=True),
    )
    grad_top = cotangent.reshape(count_rows, width)
    grad_mlp = jnp.einsum("nf,nd->fd", mixed, grad_top, preferred_element_type=jnp.float32)
    grad_mixed = jnp.einsum("nd,fd->nf", grad_top, full_mlp, preferred_element_type=jnp.float32)
    grad_first = gelu_pullback(grad_mixed * second_part)[0]
    grad_lifted = jnp.concatenate([grad_first, grad_mixed * activated], axis=-1).astype(
        jnp.bfloat16
    )
    grad_inner = jnp.einsum("nd,nf->df", lowered2, grad_lifted, preferred_element_type=jnp.float32)
    grad_lowered2 = jnp.einsum(
        "nf,df->nd", grad_lifted, full_in, preferred_element_type=jnp.float32
    )
    grad_two = jnp.sum(grad_lowered2 * normed2, axis=0)
    grad_residual = grad_top.astype(jnp.float32) + norm_back(
        grad_lowered2 * gain_two.astype(jnp.float32), normed2, factor2
    )
    grad_branch = grad_residual.astype(jnp.bfloat16)
    grad_outproj = jnp.einsum(
        "nd,ne->de", back_rows, grad_branch, preferred_element_type=jnp.float32
    )
    grad_attended = jnp.einsum(
        "ne,de->nd", grad_branch, full_out, preferred_element_type=jnp.float32
    ).astype(jnp.bfloat16)
    grad_attended_h = lax.all_to_all(
        grad_attended.reshape(seqs_here, block_rows, width),
        "head",
        split_axis=2,
        concat_axis=1,
        tiled=True,
    )
    grad_out4 = grad_attended_h.reshape(seqs_here, query_rows, groups, HD)
    along = jnp.transpose(jnp.sum(grad_out4.astype(jnp.float32) * attended, axis=-1), (0, 2, 1))
    grad_queries, grad_keys_all, grad_values_all = attend_backward(
        queries4, keys_all, values_all, grad_out4, log_total, along, key_rows, scale
    )
    grad_keys_sum, grad_values_sum = (
        lax.psum_scatter(
            grad_keys_all.astype(jnp.bfloat16), "ctx", scatter_dimension=1, tiled=True
        ).astype(jnp.float32),
        lax.psum_scatter(
            grad_values_all.astype(jnp.bfloat16), "ctx", scatter_dimension=1, tiled=True
        ).astype(jnp.float32),
    )
    grad_q_low = grad_queries.astype(jnp.bfloat16).reshape(seqs_here, query_rows, width_group)
    grad_q_tok, grad_k_tok, grad_v_tok = (
        lax.all_to_all(grad_q_low, "head", split_axis=1, concat_axis=2, tiled=True),
        lax.all_to_all(
            grad_keys_sum.astype(jnp.bfloat16), "head", split_axis=1, concat_axis=2, tiled=True
        ),
        lax.all_to_all(
            grad_values_sum.astype(jnp.bfloat16), "head", split_axis=1, concat_axis=2, tiled=True
        ),
    )
    unrot_q = rotate(
        grad_q_tok.astype(jnp.float32).reshape(seqs_here, block_rows, heads_all, HD),
        cosine,
        sine_table,
        -1.0,
    )
    unrot_k = rotate(
        grad_k_tok.astype(jnp.float32).reshape(seqs_here, block_rows, heads_all, HD),
        cosine,
        sine_table,
        -1.0,
    )
    grad_projected = jnp.concatenate(
        [
            unrot_q.reshape(count_rows, width),
            unrot_k.reshape(count_rows, width),
            grad_v_tok.astype(jnp.float32).reshape(count_rows, width),
        ],
        axis=-1,
    ).astype(jnp.bfloat16)
    grad_project = jnp.einsum(
        "nd,nf->df", lowered1, grad_projected, preferred_element_type=jnp.float32
    )
    grad_lowered1 = jnp.einsum(
        "nf,df->nd", grad_projected, full_qkv, preferred_element_type=jnp.float32
    )
    grad_one = jnp.sum(grad_lowered1 * normed1, axis=0)
    grad_input = grad_residual + norm_back(
        grad_lowered1 * gain_one.astype(jnp.float32), normed1, factor1
    )
    pieces_one = grad_one.reshape(group_devices, head_devices, -1)
    pieces_two = grad_two.reshape(group_devices, head_devices, -1)
    part_qkv, part_out, part_in, part_mlp, part_one, part_two = (
        lax.psum_scatter(
            grad_project.astype(jnp.bfloat16), ("dp", "ctx"), scatter_dimension=0, tiled=True
        ).astype(jnp.float32),
        lax.psum_scatter(
            grad_outproj.astype(jnp.bfloat16), ("dp", "ctx"), scatter_dimension=0, tiled=True
        ).astype(jnp.float32),
        lax.psum_scatter(
            grad_inner.astype(jnp.bfloat16), ("dp", "ctx"), scatter_dimension=0, tiled=True
        ).astype(jnp.float32),
        lax.psum_scatter(
            grad_mlp.astype(jnp.bfloat16), ("dp", "ctx"), scatter_dimension=0, tiled=True
        ).astype(jnp.float32),
        lax.psum_scatter(
            pieces_one.astype(jnp.bfloat16), ("dp", "ctx"), scatter_dimension=0, tiled=True
        ).astype(jnp.float32),
        lax.psum_scatter(
            pieces_two.astype(jnp.bfloat16), ("dp", "ctx"), scatter_dimension=0, tiled=True
        ).astype(jnp.float32),
    )
    final_qkv, final_out, final_in, final_mlp, final_one, final_two = (
        lax.psum_scatter(
            part_qkv.astype(jnp.bfloat16), "head", scatter_dimension=1, tiled=True
        ).astype(jnp.float32),
        lax.psum_scatter(
            part_out.astype(jnp.bfloat16), "head", scatter_dimension=1, tiled=True
        ).astype(jnp.float32),
        lax.psum_scatter(
            part_in.astype(jnp.bfloat16), "head", scatter_dimension=1, tiled=True
        ).astype(jnp.float32),
        lax.psum_scatter(
            part_mlp.astype(jnp.bfloat16), "head", scatter_dimension=1, tiled=True
        ).astype(jnp.float32),
        lax.psum_scatter(
            part_one.astype(jnp.bfloat16), "head", scatter_dimension=1, tiled=True
        ).astype(jnp.float32),
        lax.psum_scatter(
            part_two.astype(jnp.bfloat16), "head", scatter_dimension=1, tiled=True
        ).astype(jnp.float32),
    )
    return (
        result.reshape(seqs_here, block_rows, width),
        grad_input.reshape(seqs_here, block_rows, width),
        final_qkv,
        final_out,
        final_in,
        final_mlp,
        final_one.reshape(-1),
        final_two.reshape(-1),
    )


F32 = jnp.float32
BF16 = jnp.bfloat16
VMEM_BYTES = 56 * 1024 * 1024
GROUP = ("ctx", "head")


def dot(left, right, dims=((1,), (0,))):
    return lax.dot_general(left, right, (dims, ((), ())), preferred_element_type=F32)


def wide(values):
    return values.astype(F32)


def flat(values):
    return values.reshape(-1, values.shape[-1])


def lane_rotate(values, cosine, sine_signed):
    lane = lax.broadcasted_iota(jnp.int32, values.shape, 1)
    width = values.shape[1]
    partner = jnp.where(
        lane % HD < HD // 2,
        pltpu.roll(values, width - HD // 2, 1),
        pltpu.roll(values, HD // 2, 1),
    )
    return values * cosine + partner * sine_signed


def head_masks(shape):
    lane = lax.broadcasted_iota(jnp.int32, shape, 1)
    return [lane // HD == head for head in range(shape[1] // HD)]


def params():
    return pltpu.CompilerParams(vmem_limit_bytes=VMEM_BYTES)


COST = pl.CostEstimate(flops=1 << 20, transcendentals=0, bytes_accessed=1 << 16)


def whole(array):
    return pl.BlockSpec(array.shape, lambda *_: (0,) * len(array.shape))


SCALARS = pl.BlockSpec(memory_space=pltpu.SMEM)


def project_kernel(place_ref, *refs):
    pieces, weights = refs[:6], refs[6:10]
    cos_ref, sin_ref, low_ref, qkv_ref, w_ref, gain1_ref, gain2_ref, rows_ref = refs[10:]
    block, part = pieces[0].shape[2], w_ref.shape[1] // 3
    rows = gain1_ref.shape[1] // 8

    @pl.when(pl.program_id(0) == 0)
    def _():
        for step, piece in enumerate(weights):
            for turn in range(2):
                at = 2 * (place_ref[8] ^ step) + (place_ref[9] ^ turn)
                w_ref[pl.ds(pl.multiple_of(at * rows, rows), rows), :] = piece[turn, :rows]
                gains = piece[turn, rows:].astype(F32)
                rows_ref[0, pl.ds(at, 1), :] = gains[:1, :rows]
                rows_ref[1, pl.ds(at, 1), :] = gains[1:2, :rows]
        for out, at in ((gain1_ref, 0), (gain2_ref, 1)):
            for row in range(8):
                out[:, row * rows : (row + 1) * rows] = rows_ref[at, row : row + 1, :]

    gain = gain1_ref[...]
    index = 0
    for piece in pieces:
        for inner in range(piece.shape[0]):
            normed, _ = normalize(piece[inner, 0].astype(F32))
            low_ref[index, 0] = (normed * gain).astype(BF16)
            index += 1
    projected = dot(flat(low_ref[:, 0]), w_ref[...])
    cosine, sine = cos_ref[...], sin_ref[...]
    shape = (8, block, part)
    qkv_ref[:, 0, :, :part] = (
        (lane_rotate(projected[:, :part], cosine, sine) * HD**-0.5).astype(BF16).reshape(shape)
    )
    qkv_ref[:, 0, :, part : 2 * part] = (
        lane_rotate(projected[:, part : 2 * part], cosine, sine).astype(BF16).reshape(shape)
    )
    qkv_ref[:, 0, :, 2 * part :] = projected[:, 2 * part :].astype(BF16).reshape(shape)


def project(place, pieces, weights, cosine, sine):
    seqs, block, width = pieces[0].shape[1:]
    own = weights[0].shape[2]

    def by_seq(lead, last):
        return pl.BlockSpec((lead, 1, block, last), lambda s: (0, s, 0, 0))

    return pl.pallas_call(
        project_kernel,
        grid=(seqs,),
        in_specs=[SCALARS]
        + [by_seq(piece.shape[0], width) for piece in pieces]
        + [whole(w) for w in weights]
        + [whole(cosine), whole(sine)],
        out_specs=(
            by_seq(8, width),
            by_seq(8, own),
            pl.BlockSpec((width, own), lambda s: (0, 0)),
            pl.BlockSpec((1, width), lambda s: (0, 0)),
            pl.BlockSpec((1, width), lambda s: (0, 0)),
        ),
        out_shape=(
            jax.ShapeDtypeStruct((8, seqs, block, width), BF16),
            jax.ShapeDtypeStruct((8, seqs, block, own), BF16),
            jax.ShapeDtypeStruct((width, own), BF16),
            jax.ShapeDtypeStruct((1, width), F32),
            jax.ShapeDtypeStruct((1, width), F32),
        ),
        scratch_shapes=[pltpu.VMEM((2, 8, width // 8), F32)],
        compiler_params=params(),
        cost_estimate=COST,
        name="project",
    )(place, *pieces, *weights, cosine, sine)


def attend_kernel(place_ref, q_ref, k_ref, v_ref, *refs):
    att_ref, log_ref, home_ref = refs[-3:]
    step, seq = pl.program_id(0), len(refs) - 3
    if seq:

        @pl.when(step == 0)
        def _():
            home_ref[:, :1] = refs[0][...]

    queries, keys, values = flat(q_ref[...]), flat(k_ref[...]), flat(v_ref[...])
    attended = jnp.zeros(queries.shape, F32)
    logs = jnp.zeros(queries.shape, F32)
    for mask in head_masks(queries.shape):
        scores = dot(jnp.where(mask, queries, 0), keys, ((1,), (1,)))
        peak = jnp.max(scores, axis=1, keepdims=True)
        weights = jnp.exp(scores - peak)
        total = jnp.sum(weights, axis=1, keepdims=True)
        mixed = dot(weights.astype(BF16), values) * (1.0 / total)
        attended = jnp.where(mask, mixed, attended)
        logs = jnp.where(mask, peak + jnp.log(total), logs)
    att_ref[...] = attended.reshape(att_ref.shape)
    log_ref[...] = logs.reshape(log_ref.shape)
    low = attended.astype(BF16).reshape(att_ref.shape)
    for inner in range(2):
        home_ref[place_ref[2 * step + inner], seq] = low[inner, 0]


def attend(place, qkv, *home):
    _, _, block, own = qkv.shape
    part, seq = own // 3, len(home)
    rows = pl.BlockSpec((2, 1, block, part), lambda i: (i, 0, 0, 0))
    shape = (8, 1, block, part)
    return pl.pallas_call(
        attend_kernel,
        grid=(4,),
        in_specs=[
            SCALARS,
            pl.BlockSpec((2, 1, block, part), lambda i: (i, seq, 0, 0)),
            pl.BlockSpec((8, 1, block, part), lambda i: (0, seq, 0, 1)),
            pl.BlockSpec((8, 1, block, part), lambda i: (0, seq, 0, 2)),
            *[whole(h) for h in home],
        ],
        out_specs=(
            rows,
            rows,
            pl.BlockSpec((8, 1 + seq, block, part), lambda i: (0, 0, 0, 0)),
        ),
        out_shape=(
            jax.ShapeDtypeStruct(shape, F32),
            jax.ShapeDtypeStruct(shape, F32),
            jax.ShapeDtypeStruct((8, 1 + seq, block, part), BF16),
        ),
        compiler_params=params(),
        cost_estimate=COST,
        name="attend",
    )(place, qkv, qkv, qkv, *home)


def branch_kernel(place_ref, *refs):
    pieces = refs[:6]
    rows_ref, tokens_ref, gain_ref, residual_ref, low_ref = refs[6:]
    total = flat(tokens_ref[...].astype(F32))
    index = 0
    for piece in pieces:
        for inner in range(piece.shape[0]):
            total += dot(flat(rows_ref[place_ref[index]]), piece[inner])
            index += 1
    normed, _ = normalize(total)
    residual_ref[...] = total.reshape(residual_ref.shape)
    low_ref[...] = (normed * gain_ref[...]).astype(BF16).reshape(low_ref.shape)


def branch(place, pieces, rows, tokens, gain):
    args = (*pieces, rows, tokens, gain)
    return pl.pallas_call(
        branch_kernel,
        in_specs=[SCALARS] + [whole(a) for a in args],
        out_shape=(
            jax.ShapeDtypeStruct(tokens.shape, F32),
            jax.ShapeDtypeStruct(tokens.shape, BF16),
        ),
        compiler_params=params(),
        cost_estimate=COST,
        name="branch",
    )(place, *args)


def combine(*groups):
    parts = [part for group in groups for _, parts in group for part in parts]
    rows = sum(count for count, _ in groups[0])
    width = parts[0][0].shape[2]

    def kernel(*refs):
        at = 0
        for k, group in enumerate(groups):
            row = 0
            for count, terms in group:
                total = 0.0
                for _, _, start in terms:
                    total = total + wide(refs[at][0, start : start + count])
                    at += 1
                refs[-1][k, row : row + count] = total.astype(BF16)
                row += count

    return pl.pallas_call(
        kernel,
        grid=(1,),
        in_specs=[
            pl.BlockSpec((1, *array.shape[1:]), lambda *_, index=index: (index, 0, 0))
            for array, index, _ in parts
        ],
        out_specs=pl.BlockSpec((len(groups), rows, width), lambda *_: (0, 0, 0)),
        out_shape=jax.ShapeDtypeStruct((len(groups), rows, width), BF16),
        compiler_params=params(),
        cost_estimate=COST,
        name="combine",
    )(*[array for array, _, _ in parts])


def mlp_kernel(*refs, count, ends):
    pieces, tops = refs[:count], refs[count : 2 * count]
    w_ref, out_w_ref = refs[2 * count : 2 * count + 2]
    low_ref, top_ref, mixed_ref, lifted_ref, *out_refs = refs[-4 - len(ends) :]
    step = pl.program_id(0)
    start = 0
    for piece, top in zip(pieces, tops):

        @pl.when((step >= start) & (step < start + piece.shape[0]))
        def _(piece=piece, top=top, start=start):
            low_ref[0] = piece[step - start]
            top_ref[0] = top[step - start]

        start += piece.shape[0]

    hidden = w_ref.shape[1] // 2
    lifted = dot(flat(low_ref[...]), w_ref[...])
    first, second = lifted[:, :hidden], lifted[:, hidden:]
    grad_mixed = dot(flat(top_ref[...]), out_w_ref[...], ((1,), (1,)))
    gate = 0.5 * (1.0 + lax.erf(first * (0.5**0.5)))
    slope = gate + first * jnp.exp(first * first * -0.5) * ((2.0 * math.pi) ** -0.5)
    activated = first * gate
    mixed_ref[...] = (activated * second).astype(BF16).reshape(mixed_ref.shape)
    grad = jnp.concatenate(
        [(grad_mixed * second * slope).astype(BF16), (grad_mixed * activated).astype(BF16)],
        axis=1,
    )
    lifted_ref[...] = grad.reshape(lifted_ref.shape)
    partial = dot(grad, w_ref[...], ((1,), (1,))).astype(BF16).reshape(low_ref.shape)
    start = 0
    for out, end in zip(out_refs, ends):

        @pl.when((step >= start) & (step < end))
        def _(out=out):
            out[...] = partial

        start = end


def mlp(pieces, tops, w, out_w, base, ends, earlier=()):
    seqs, block, width = pieces[0].shape[1:]
    hidden = w.shape[1] // 2
    whole_in = (*pieces, *tops, w, out_w)

    def rows(last):
        return pl.BlockSpec((1, seqs, block, last), lambda i: (i + base, 0, 0, 0))

    def within(start, end):
        return pl.BlockSpec(
            (1, seqs, block, width),
            lambda i: (jnp.clip(i - start, 0, end - start - 1), 0, 0, 0),
        )

    starts = (0, *ends[:-1])
    lasts = (width, width, hidden, 2 * hidden)
    return pl.pallas_call(
        functools.partial(mlp_kernel, count=len(pieces), ends=ends),
        grid=(ends[-1],),
        in_specs=[whole(array) for array in whole_in]
        + [pl.BlockSpec(memory_space=pl.ANY)] * len(earlier),
        out_specs=(
            *[rows(last) for last in lasts],
            *[within(start, end) for start, end in zip(starts, ends)],
        ),
        out_shape=(
            *[jax.ShapeDtypeStruct((8, seqs, block, last), BF16) for last in lasts],
            *[
                jax.ShapeDtypeStruct((end - start, seqs, block, width), BF16)
                for start, end in zip(starts, ends)
            ],
        ),
        input_output_aliases={len(whole_in) + at: at for at in range(len(earlier))},
        compiler_params=params(),
        cost_estimate=COST,
        name="mlp",
    )(*whole_in, *earlier)


def out_grad_kernel(place_ref, rows_ref, grad_ref, keep_ref, send_ref):
    grads = flat(grad_ref[...])
    for index in range(8):
        part = dot(flat(rows_ref[place_ref[index]]), grads, ((0,), (0,))).astype(BF16)
        if index < 5:
            keep_ref[index] = part
        else:
            send_ref[index - 5] = part


def out_grad(place, rows, grads):
    part, width = rows.shape[-1], grads.shape[-1]
    return pl.pallas_call(
        out_grad_kernel,
        in_specs=[SCALARS, whole(rows), whole(grads)],
        out_shape=(
            jax.ShapeDtypeStruct((5, part, width), BF16),
            jax.ShapeDtypeStruct((3, part, width), BF16),
        ),
        compiler_params=params(),
        cost_estimate=COST,
        name="out_grad",
    )(place, rows, grads)


def branch_back_kernel(place_ref, *refs):
    pieces = refs[:6]
    keep_ref, near_ref, own_ref, residual_ref, top_ref, gain_ref = refs[6:12]
    grad_ref, branch_ref, home_ref, sum_ref = refs[12:]
    grad_low = wide(flat(keep_ref[...])) + wide(flat(near_ref[...])) + wide(flat(own_ref[...]))
    normed, factor = normalize(flat(residual_ref[...]))
    sum_ref[...] = jnp.sum(grad_low * normed, axis=0, keepdims=True)
    grad = flat(top_ref[...].astype(F32)) + norm_back(grad_low * gain_ref[...], normed, factor)
    grad_ref[...] = grad.reshape(grad_ref.shape)
    low = grad.astype(BF16)
    branch_ref[...] = low.reshape(branch_ref.shape)
    index = 0
    for piece in pieces:
        for inner in range(piece.shape[0]):
            home_ref[place_ref[index]] = (
                dot(low, piece[inner], ((1,), (1,))).astype(BF16).reshape(home_ref.shape[1:])
            )
            index += 1


def branch_back(place, pieces, keep, near, own, residual, top, gain):
    args = (*pieces, keep, near, own, residual, top, gain)
    seqs, block, width = residual.shape
    shapes = (
        jax.ShapeDtypeStruct(residual.shape, F32),
        jax.ShapeDtypeStruct(residual.shape, BF16),
        jax.ShapeDtypeStruct((8, seqs, block, pieces[0].shape[1]), BF16),
        jax.ShapeDtypeStruct((1, width), F32),
    )
    return pl.pallas_call(
        branch_back_kernel,
        grid=(1,),
        in_specs=[SCALARS]
        + [whole(piece) for piece in pieces]
        + [pl.BlockSpec((1, seqs * block, width), lambda *_: (0, 0, 0))] * 2
        + [whole(a) for a in args[8:]],
        out_specs=tuple(whole(shape) for shape in shapes),
        out_shape=shapes,
        compiler_params=params(),
        cost_estimate=COST,
        name="branch_back",
    )(place, *args)


def attend_back_kernel(
    place_ref, q_ref, k_ref, v_ref, grad_ref, att_ref, log_ref, cosq_ref, sinq_ref, cos_ref,
    sin_ref, w_ref, low_ref, *refs, seq, last,
):
    if last:
        before_ref, gain1_ref, gain2_ref, keep_ref, send_ref, grad_w_ref, *scratch = refs
    else:
        keep_ref, send_ref, before_ref, *scratch = refs
    proj_ref, sum_k, sum_v = scratch
    step = pl.program_id(0)
    block, part = q_ref.shape[2], q_ref.shape[3]

    @pl.when(step == 0)
    def _():
        sum_k[...] = jnp.zeros_like(sum_k)
        sum_v[...] = jnp.zeros_like(sum_v)

    queries, keys, values = flat(q_ref[...]), flat(k_ref[...]), flat(v_ref[...])
    grads = jnp.concatenate([grad_ref[place_ref[2 * step + inner], seq] for inner in range(2)])
    along = (grads.astype(F32) * flat(att_ref[...])).T
    logs = flat(log_ref[...]).T
    grad_queries = jnp.zeros(queries.shape, F32)
    for head, mask in enumerate(head_masks(queries.shape)):
        own_q = jnp.where(mask, queries, 0)
        own_g = jnp.where(mask, grads, 0)
        scores = dot(keys, own_q, ((1,), (1,)))
        weights = jnp.exp(scores - logs[head * HD : head * HD + 1])
        lifted = dot(values, own_g, ((1,), (1,)))
        row = jnp.sum(along[head * HD : (head + 1) * HD], axis=0, keepdims=True)
        grad_scores = (weights * (lifted - row)).astype(BF16)
        sum_k[...] += dot(grad_scores, own_q)
        sum_v[...] += dot(weights.astype(BF16), own_g)
        grad_queries = jnp.where(mask, dot(grad_scores, keys, ((0,), (0,))), grad_queries)
    grad_queries = lane_rotate(grad_queries * HD**-0.5, cosq_ref[...], -sinq_ref[...])
    rows = pl.multiple_of(step * 2 * block, 2 * block)
    proj_ref[pl.ds(rows, 2 * block), :part] = grad_queries.astype(BF16)

    @pl.when(step == 3)
    def _():
        grad_keys = lane_rotate(sum_k[...], cos_ref[...], -sin_ref[...])
        proj_ref[:, part : 2 * part] = grad_keys.astype(BF16)
        proj_ref[:, 2 * part :] = sum_v[...].astype(BF16)
        partial = dot(proj_ref[...], w_ref[...], ((1,), (1,))).astype(BF16)
        keep_ref[:, :block] = partial[: 5 * block].reshape(5, block, -1)
        send_ref[:, :block] = partial[5 * block :].reshape(3, block, -1)
        grad_w = dot(proj_ref[...], flat(low_ref[...]), ((0,), (0,)))
        if last:
            grad_w = (grad_w + before_ref[...]).T
            grad_w_ref[...] = grad_w.astype(BF16)
            along_w = jnp.sum(grad_w * w_ref[...].astype(F32), axis=1, keepdims=True)
            along_w = jnp.broadcast_to(along_w, (w_ref.shape[0], 128)).T[:1] / gain1_ref[...]
            row = lax.broadcasted_iota(jnp.int32, (GAIN_ROWS, w_ref.shape[0]), 0)
            gains = jnp.where(row == 0, along_w, jnp.where(row == 1, gain2_ref[...], 0.0))
            for out in (keep_ref, send_ref):
                for index in range(out.shape[0]):
                    out[index, block:] = gains.astype(BF16)
        else:
            before_ref[...] = grad_w


GAIN_ROWS = 16


def attend_back(place, qkv, grads, attended, logs, cosine, sine, w, low, seq, *before):
    _, _, block, own = qkv.shape
    part, width = own // 3, w.shape[0]
    last = len(before) > 0
    tall = block + GAIN_ROWS * last
    rows = pl.BlockSpec((2, 1, block, part), lambda i: (i, 0, 0, 0))
    angles = pl.BlockSpec((2 * block, part), lambda i: (i, 0))

    def full(*shape):
        return pl.BlockSpec(shape, lambda i: (0,) * len(shape))

    args = [place, qkv, qkv, qkv, grads, attended, logs, cosine, sine, cosine, sine, w, low]
    in_specs = [
        SCALARS,
        pl.BlockSpec((2, 1, block, part), lambda i: (i, seq, 0, 0)),
        pl.BlockSpec((8, 1, block, part), lambda i: (0, seq, 0, 1)),
        pl.BlockSpec((8, 1, block, part), lambda i: (0, seq, 0, 2)),
        whole(grads),
        rows,
        rows,
        angles,
        angles,
        whole(cosine),
        whole(sine),
        whole(w),
        pl.BlockSpec((8, 1, block, width), lambda i: (0, seq, 0, 0)),
    ]
    shapes = [((5, tall, width), BF16), ((3, tall, width), BF16)]
    if last:
        args += before
        in_specs += [whole(array) for array in before]
        shapes += [((width, own), BF16)]
    else:
        shapes += [((own, width), F32)]
    return pl.pallas_call(
        functools.partial(attend_back_kernel, seq=seq, last=last),
        grid=(4,),
        in_specs=in_specs,
        out_specs=tuple(full(*shape) for shape, _ in shapes),
        out_shape=tuple(jax.ShapeDtypeStruct(shape, kind) for shape, kind in shapes),
        scratch_shapes=[
            pltpu.VMEM((8 * block, own), BF16),
            pltpu.VMEM((8 * block, part), F32),
            pltpu.VMEM((8 * block, part), F32),
        ],
        compiler_params=params(),
        cost_estimate=COST,
        name="attend_back",
    )(*args)


def input_grad_kernel(*refs):
    keeps, (near_ref, own_ref, tokens_ref, residual_ref, gain_ref, out_ref) = refs[:-6], refs[-6:]
    block = tokens_ref.shape[1]
    for seq, keep in enumerate(keeps):
        rows = slice(seq * block, (seq + 1) * block)
        grad = wide(keep[0, :block]) + wide(near_ref[0, rows]) + wide(own_ref[0, rows])
        normed, factor = normalize(wide(tokens_ref[seq]))
        out_ref[seq] = residual_ref[seq] + norm_back(grad * gain_ref[...], normed, factor)


def input_grad(keeps, near, own, tokens, residual, gain):
    rest = (own, tokens, residual, gain)
    return pl.pallas_call(
        input_grad_kernel,
        grid=(1,),
        in_specs=[
            pl.BlockSpec((1, *array.shape[1:]), lambda *_: (0, 0, 0)) for array in (*keeps, near)
        ]
        + [whole(array) for array in rest],
        out_specs=whole(residual),
        out_shape=jax.ShapeDtypeStruct(residual.shape, F32),
        compiler_params=params(),
        cost_estimate=COST,
        name="input_grad",
    )(*keeps, near, *rest)


class Group:
    def __init__(self):
        self.heads = lax.axis_size("head")
        self.dp = lax.axis_size("dp")
        self.ctx_at = lax.axis_index("ctx")
        self.head_at = lax.axis_index("head")
        self.dp_at = lax.axis_index("dp")
        self.at = self.ctx_at * self.heads + self.head_at
        near, far = [], []
        for c in range(2):
            for h in range(self.heads):
                x, y = (c ^ 1) * self.heads + h, c * self.heads + (h ^ 2)
                near.append((c * self.heads + h, x if h % 2 == 0 else y))
                far.append((c * self.heads + h, y if h % 2 == 0 else x))
        self.near, self.far = near, far

    def order(self):
        first = jnp.where(self.head_at % 2 == 0, 4, 2)
        second = 6 - first
        return jnp.stack(
            [self.at ^ bits for bits in (0, 1, first, first ^ 1, 6, second ^ 1, second, 7)]
        )

    def swap(self, values, bit):
        if bit == 4:
            return lax.ppermute(values, "ctx", [(0, 1), (1, 0)])
        return lax.ppermute(values, "head", [(i, i ^ bit) for i in range(self.heads)])

    def mate(self, values):
        return self.swap(values, 1)

    def to_near(self, values):
        return lax.ppermute(values, GROUP, self.near)

    def to_far(self, values):
        return lax.ppermute(values, GROUP, self.far)

    def rows_in(self, values, place):
        inverse = [place.index(i) for i in range(self.heads)]
        turns = [[], []]
        for source in range(self.dp):
            target = inverse[source]
            for d in range(self.dp):
                step = (d - source) % self.dp
                head = (target & 2) | ((target ^ step) & 1)
                if step:
                    turns[step // 2].append((source * self.heads + head, d * self.heads + target))
        return tuple(lax.ppermute(values, ("dp", "head"), pairs) for pairs in turns)

    def chosen(self, values, first, second, place):
        source = sum(jnp.where(self.head_at == h, place[h], 0) for h in range(self.heads))
        step = (self.dp_at - source) % self.dp
        return jnp.where(step == 0, values, jnp.where(step < 2, first, second))

    def rows_back(self, values, place):
        pairs, same = [], False
        for d in range(self.dp):
            for h in range(self.heads):
                if (d, h) == (place[h], d):
                    same = same | ((self.dp_at == d) & (self.head_at == h))
                else:
                    pairs.append((d * self.heads + h, place[h] * self.heads + d))
        return jnp.where(same, values, lax.ppermute(values, ("dp", "head"), pairs))

    def scatter_dp(self, values):
        step = self.dp // 2
        while step:
            n = values.shape[1] // 2
            bit = (self.dp_at // step) % 2
            sent = lax.dynamic_slice_in_dim(values, (1 - bit) * n, n, 1).astype(BF16)
            kept = lax.dynamic_slice_in_dim(values, bit * n, n, 1)
            values = wide(kept) + wide(self.across(sent, step))
            step //= 2
        return values

    def across(self, values, step):
        return lax.ppermute(values, "dp", [(i, i ^ step) for i in range(self.dp)])

    def total_dp(self, values):
        others = [self.across(values, step) for step in range(1, self.dp)]
        return wide(values) + sum(wide(other) for other in others)


def pick(array, index, axis):
    return lax.dynamic_index_in_dim(array, index, axis, keepdims=False)


def after(values, *earlier):
    return lax.optimization_barrier((values, earlier))[0]


def local_split(tokens, cotangent, w_qkv, w_attn_out, w_in, w_mlp_out, norm_gain1, norm_gain2):
    seqs, block, width = tokens.shape
    group = Group()
    heads, dp = group.heads, group.dp
    at_c, at_h = group.ctx_at, group.head_at
    parts = 2 * heads
    hidden = w_in.shape[1] // 2 // parts
    padded = -(-hidden // 128) * 128
    own_width = width // parts
    half = heads // 2
    rows_here = w_qkv.shape[0]
    place = [2 * (h % half) + h // half for h in range(heads)]
    straight = list(range(heads))
    order = group.order()
    scalars = jnp.concatenate([order, jnp.stack([group.dp_at, at_c])]).astype(jnp.int32)
    mate, near, far = group.mate, group.to_near, group.to_far

    def in_order(own, other):
        return jnp.where(at_c == 0, jnp.stack([own, other]), jnp.stack([other, own]))

    def exchange(values):
        return lax.all_to_all(values, GROUP, split_axis=0, concat_axis=0, tiled=True)


    gains = jnp.pad(
        jnp.stack([norm_gain1, norm_gain2]), ((0, 14), (0, 3 * own_width - rows_here))
    )
    qkv_view = w_qkv.reshape(rows_here, 3, width)

    def qkv_part(at):
        start = (2 * at_h + at) * own_width
        cut = lax.dynamic_slice_in_dim(qkv_view, start, own_width, 2)
        return jnp.concatenate([cut.reshape(rows_here, 3 * own_width), gains])

    x_own = tokens[None]
    x_mate = mate(x_own)
    qkv_other, qkv_own = qkv_part(1 - at_c), qkv_part(at_c)
    qkv_cross = group.swap(after(qkv_other, x_own), 4)
    x_chip = jnp.concatenate([x_own, after(x_mate, qkv_cross, qkv_own)])
    x_near = near(x_chip)
    qkv_pair = jnp.stack([qkv_own, qkv_cross])
    qkv_pieces = [qkv_pair] + [group.across(qkv_pair, step) for step in range(1, dp)]

    in_view = after(w_in, qkv_pair).reshape(rows_here, 2, heads, 2, hidden)
    in_view = pick(in_view, 2 * (at_h % half) + at_h // half, 2)

    def in_part(at):
        cut = pick(in_view, at, 2)
        return jnp.pad(cut, ((0, 0), (0, 0), (0, padded - hidden))).reshape(rows_here, 2 * padded)

    in_other, in_own = in_part(1 - at_c), in_part(at_c)
    in_cross = group.swap(in_other, 4)
    positions = after(order, qkv_pair)[:, None] * block + jnp.arange(block, dtype=jnp.int32)
    lane = jnp.arange(own_width, dtype=jnp.int32)
    frequency = jnp.exp(
        (lane % (HD // 2)).astype(F32) * (-math.log(ROPE_BASE) / (HD // 2))
    )
    angles = wide(positions.reshape(-1))[:, None] * frequency[None, :]
    cosine = jnp.cos(angles)
    sine = jnp.sin(angles) * jnp.where(lane % HD < HD // 2, -1.0, 1.0)[None, :]

    x_far = far(x_near[:1])
    x_near = after(x_near, *qkv_pieces, in_other, in_own, cosine, sine)
    x_near_mate = mate(x_near)
    out_sent = group.rows_in(after(w_attn_out, x_near), straight)
    cot_own = after(cotangent, x_near)[None]
    cot_mate = mate(cot_own)
    x_far = after(x_far, cot_mate, in_cross)
    x_far_mate = mate(x_far)

    in_pair, x_far_mate = lax.optimization_barrier((in_order(in_own, in_cross), x_far_mate))
    weight_in = lax.all_gather(in_pair, "dp", axis=0).reshape(width, -1)
    cot_chip = jnp.concatenate([cot_own, cot_mate])
    cot_near = near(after(cot_chip, x_far))
    out_own = group.chosen(w_attn_out, *after(out_sent, x_far), straight)[None]
    out_mate = mate(out_own)
    mlp_sent = group.rows_in(after(w_mlp_out, out_own), place)
    x_pieces = (x_own, x_mate, x_near, x_far, x_near_mate, after(x_far_mate, cot_chip, out_own))
    low1, qkv, weight_qkv, gain_one, gain_two = project(
        scalars, x_pieces, qkv_pieces, cosine, sine
    )

    out_near = near(jnp.concatenate([out_own, after(out_mate, qkv)]))
    att_0, log_0, home_0 = attend(scalars, after(qkv, out_mate))
    cot_near = after(cot_near, home_0)
    cot_far, cot_near_mate = far(cot_near[:1]), mate(cot_near)
    out_near = after(out_near, home_0)
    out_far, out_near_mate = far(out_near[:1]), mate(out_near)
    att_1, log_1, home = attend(scalars, after(qkv, cot_near, out_near), home_0)
    att_rows = exchange(home)
    out_far_mate, cot_far_mate = mate(after(out_far, home)), mate(after(cot_far, home))
    out_pieces = (out_own, out_mate, out_near, out_far, out_near_mate, out_far_mate)
    weight_mlp = group.chosen(w_mlp_out, *after(mlp_sent, home), place)
    weight_mlp = jnp.pad(weight_mlp, ((0, padded - hidden), (0, 0)))
    residual, low2 = branch(
        scalars, out_pieces, after(att_rows, cot_far_mate, weight_mlp), tokens, gain_two
    )

    low_own = low2[None]
    low_mate = mate(low_own)
    low_near = near(jnp.concatenate([low_own, low_mate]))
    *arrays, keep_a = mlp(
        (low_own, low_mate), (cot_own, cot_mate), weight_in, weight_mlp, 0, (2,)
    )
    low_near = after(low_near, keep_a)
    low_far, low_near_mate = far(low_near[:1]), mate(low_near)
    *arrays, keep_b = mlp((low_near,), (cot_near,), weight_in, weight_mlp, 2, (2,), arrays)
    low_far_mate = mate(after(low_far, keep_b))
    low2_all, cot_all, mixed, grad_lifted, keep_c, send = mlp(
        (low_far, low_near_mate, low_far_mate),
        (cot_far, cot_near_mate, cot_far_mate),
        weight_in,
        weight_mlp,
        4,
        (1, 4),
        arrays,
    )

    def over_tokens(left, right):
        return dot(flat(left), flat(right), ((0,), (0,)))

    def scatter(values):
        return lax.psum_scatter(values.astype(BF16), "dp", scatter_dimension=0, tiled=True)

    def columns_first(values):
        return jnp.moveaxis(values.reshape(values.shape[0], dp, -1), 1, 0)

    rows = seqs * block

    def by_rows(values):
        return values.reshape(values.shape[0], -1, width)

    keep_a, keep_b, keep_c, send = (by_rows(array) for array in (keep_a, keep_b, keep_c, send))
    met = mate(send)
    last = combine([(rows, [(keep_c, 0, 0), (met, 2, 0)])])
    last_far = far(last)
    grad_mlp = columns_first(over_tokens(after(mixed, last), cot_all)[:hidden]).astype(BF16)
    last_far = after(last_far, grad_mlp)
    grad_mlp = scatter(grad_mlp)[0]
    chip = combine(
        [(rows, [(keep_b, 0, 0), (met, 0, 0), (last_far, 0, 0)])],
        [(rows, [(keep_b, 1, 0), (met, 1, 0)])],
    )
    chip_near = near(chip)
    grad_in = over_tokens(low2_all, after(grad_lifted, chip)).astype(BF16)
    cut = 5 * rows
    mixed_flat = flat(after(mixed, chip))
    out_keep = dot(mixed_flat[:cut], weight_mlp).astype(BF16).reshape(5, rows, width)
    out_send = dot(mixed_flat[cut:], weight_mlp).astype(BF16).reshape(3, rows, width)
    chip_near = after(chip_near, grad_in, out_keep, out_send)
    grad_in = scatter(grad_in)
    home = mate(combine([(rows, [(keep_a, 1, 0), (chip_near, 1, 0)])])[0])
    out_met = mate(after(out_send, chip_near))
    grad_residual, grad_branch, home, gain2_sum = branch_back(
        scalars, out_pieces, keep_a, chip_near, after(home, grad_mlp), residual, cotangent, gain_two
    )
    grad_home = exchange(home)

    rows_keep, rows_send = out_grad(scalars, after(att_rows, home), grad_branch)
    rows_met = mate(rows_send)
    few = rows_keep.shape[1]

    def ends(index, at, *more):
        kept = [(out_keep, index, 0)], [(rows_keep, index, 0)]
        if at is not None:
            kept[0].append((out_met, at, 0))
            kept[1].append((rows_met, at, 0))
        for array, where in more:
            kept[0].append((array, where, 0))
            kept[1].append((array, where, rows))
        return [(rows, kept[0]), (few, kept[1])]

    end_last = combine(ends(4, 2))
    grad_home = after(grad_home, end_last)
    end_far = far(after(end_last, grad_home))
    keep_0, send_0, before = attend_back(
        scalars, qkv, grad_home, att_0, log_0, cosine, sine, weight_qkv, low1, 0
    )
    met_0 = mate(send_0)
    end_far = after(end_far, send_0)
    end_chip = combine(ends(2, 0, (end_far, 0)), ends(3, 1))
    end_near = near(end_chip)
    keep_1, send_1, grad_qkv = attend_back(
        scalars, qkv, after(grad_home, end_chip), att_1, log_1, cosine, sine,
        weight_qkv, low1, 1, before, gain_one, gain2_sum,
    )

    def rows_here_of(values):
        pair = values.reshape(2, rows_here, -1)
        own = pick(pair, at_c, 0)
        other = group.swap(pick(pair, 1 - at_c, 0), 4)
        return in_order(own, other)

    met_1 = mate(send_1)
    grad_qkv = scatter(grad_qkv)
    tall = send_1.shape[1]

    def both(index, at, *more):
        kept = [(keep_0, index, 0)], [(keep_1, index, 0)]
        if at is not None:
            kept[0].append((met_0, at, 0))
            kept[1].append((met_1, at, 0))
        for array, where in more:
            kept[0].append((array, where, 0))
            kept[1].append((array, where, block))
        return [(block, kept[0]), (tall, kept[1])]

    last = combine(both(4, 2))
    last_far = far(last)

    end_near = after(end_near, last)
    end_home = mate(combine(ends(1, None, (end_near, 1))))
    grad_in = rows_here_of(after(grad_in, last))
    last_far = after(last_far, end_home, grad_in)
    chip = combine(both(2, 0, (last_far, 0)), both(3, 1))
    chip_near = near(chip)

    end_home = after(end_home, chip)
    grad_out = wide(rows_keep[0]) + wide(end_near[0, rows:]) + wide(end_home[0, rows:])
    grad_out = group.scatter_dp(grad_out).astype(BF16)
    result = wide(out_keep[0]) + wide(end_near[0, :rows]) + wide(end_home[0, :rows])
    result = (residual + result.reshape(residual.shape)).astype(BF16)
    late = at_h // half
    grad_in = after(grad_in, chip)
    grad_in = jnp.stack([grad_in[..., :hidden], grad_in[..., padded : padded + hidden]])
    stays = pick(grad_in, late, 0)
    comes = group.swap(pick(grad_in, 1 - late, 0), half)
    grad_mlp = group.rows_back(after(grad_mlp, chip), place)
    grad_qkv = rows_here_of(after(grad_qkv, chip))
    chip_near = after(chip_near, comes, result, grad_qkv, grad_mlp, grad_out)
    home = mate(combine(both(1, None, (chip_near, 1))))
    grad_out = wide(group.rows_back(after(grad_out, chip_near), straight))
    sums = wide(keep_1[0, block:]) + wide(chip_near[0, rows:]) + wide(home[0, rows:])
    sums = group.total_dp(sums.astype(BF16))
    grad_input = input_grad((keep_0, keep_1), chip_near, home, tokens, grad_residual, gain_one)

    grad_mlp = wide(grad_mlp)
    grad_in = jnp.where(
        late == 0, jnp.concatenate([stays, comes]), jnp.concatenate([comes, stays])
    )
    grad_in = wide(jnp.moveaxis(grad_in, 0, 1).reshape(rows_here, -1))

    per_device = width // (dp * parts)
    start = (group.dp_at * parts + group.at) * per_device
    grad_gain1, grad_gain2 = (
        lax.dynamic_slice_in_dim(sums[i], start, per_device, 0) for i in range(2)
    )
    grad_qkv = grad_qkv.reshape(2, rows_here, 3, own_width)
    grad_qkv = jnp.moveaxis(grad_qkv, 2, 0)
    odd = at_h % 2
    stays = pick(grad_qkv, odd + late, 0)
    core = group.swap(pick(grad_qkv, 1 - odd + late, 0), 1)
    chip = group.swap(pick(grad_qkv, 2 - 2 * late, 0), 2)
    grad_qkv = jnp.where(
        odd == 0, jnp.concatenate([stays, core, chip]), jnp.concatenate([chip, core, stays])
    )
    grad_qkv = wide(jnp.moveaxis(grad_qkv, 0, 1).reshape(rows_here, -1))

    return (
        result,
        grad_input,
        grad_qkv,
        grad_out,
        grad_in,
        grad_mlp,
        grad_gain1,
        grad_gain2,
    )


def local(tokens, cotangent, w_qkv, w_attn_out, w_in, w_mlp_out, norm_gain1, norm_gain2):
    args = (tokens, cotangent, w_qkv, w_attn_out, w_in, w_mlp_out, norm_gain1, norm_gain2)
    sizes = [lax.axis_size(axis) for axis in ("dp", "ctx", "head")]
    if sizes == [4, 2, 4] and tokens.shape[2] == 8 * 2 * HD and tokens.shape[1] % 16 == 0:
        return local_split(*args)
    return local_general(*args)


def solution(mesh):
    in_specs = (
        P("dp", ("ctx", "head"), None),
        P("dp", ("ctx", "head"), None),
        P(("dp", "ctx"), None),
        P(("dp", "ctx"), None),
        P(("dp", "ctx"), None),
        P(("dp", "ctx"), None),
        P(("dp", "ctx")),
        P(("dp", "ctx")),
    )
    out_specs = (
        P("dp", ("ctx", "head"), None),
        P("dp", ("ctx", "head"), None),
        P(("dp", "ctx"), "head"),
        P(("dp", "ctx"), "head"),
        P(("dp", "ctx"), "head"),
        P(("dp", "ctx"), "head"),
        P(("dp", "ctx", "head")),
        P(("dp", "ctx", "head")),
    )
    return jax.shard_map(local, mesh=mesh, in_specs=in_specs, out_specs=out_specs, check_vma=False)
```

```python
import functools
import math

import jax
import jax.numpy as jnp
from jax import lax
from jax.experimental import pallas as pl
from jax.experimental.pallas import tpu as pltpu
from jax.sharding import PartitionSpec as P

HD = 64


EPSILON = 1e-05
ROPE_BASE = 160000.0


def normalize(values):
    centre = jnp.mean(values, axis=-1, keepdims=True)
    shifted = values - centre
    spread = jnp.mean(shifted * shifted, axis=-1, keepdims=True)
    factor = lax.rsqrt(spread + EPSILON)
    return (shifted * factor, factor)


def norm_back(grad_normed, normed, factor):
    grad_centre = jnp.mean(grad_normed, axis=-1, keepdims=True)
    grad_along = jnp.mean(grad_normed * normed, axis=-1, keepdims=True)
    return (grad_normed - grad_centre - normed * grad_along) * factor


def rope_tables(positions, half_size):
    frequency = jnp.exp(
        jnp.arange(half_size, dtype=jnp.float32) * (-math.log(ROPE_BASE) / half_size)
    )
    angles = positions[:, None] * frequency[None, :]
    return (jnp.cos(angles), jnp.sin(angles))


def rotate(values, cosine, sine_table, direction):
    half_size = cosine.shape[-1]
    first_half = values[..., :half_size]
    second_half = values[..., half_size:]
    cos_part = cosine[:, None, :]
    sin_part = sine_table[:, None, :] * direction
    return jnp.concatenate(
        [
            first_half * cos_part - second_half * sin_part,
            second_half * cos_part + first_half * sin_part,
        ],
        axis=-1,
    )


def block_scores(queries4, keys_block, scale):
    keys4 = keys_block.reshape(
        keys_block.shape[0], keys_block.shape[1], queries4.shape[2], queries4.shape[3]
    )
    return (
        jnp.einsum("sqgd,skgd->sgqk", queries4, keys4, preferred_element_type=jnp.float32) * scale
    )


def attend_forward(queries4, keys_all, values_all, key_rows, scale):
    seqs_here, query_rows, groups, head_size = queries4.shape
    turns = keys_all.shape[1] // key_rows

    def statistics(turn, carry):
        row_peak, row_total = carry
        keys_block = lax.dynamic_slice_in_dim(keys_all, turn * key_rows, key_rows, 1)
        scores = block_scores(queries4, keys_block, scale)
        new_peak = jnp.maximum(row_peak, jnp.max(scores, axis=-1))
        row_total = row_total * jnp.exp(row_peak - new_peak) + jnp.sum(
            jnp.exp(scores - new_peak[..., None]), axis=-1
        )
        return (new_peak, row_total)

    start_peak = jnp.full((seqs_here, groups, query_rows), -1e30, jnp.float32)
    row_peak, row_total = lax.fori_loop(
        0, turns, statistics, (start_peak, jnp.zeros_like(start_peak))
    )
    log_total = row_peak + jnp.log(row_total)

    def accumulate(turn, running):
        keys_block = lax.dynamic_slice_in_dim(keys_all, turn * key_rows, key_rows, 1)
        values_block = lax.dynamic_slice_in_dim(values_all, turn * key_rows, key_rows, 1).reshape(
            seqs_here, key_rows, groups, head_size
        )
        weights = jnp.exp(block_scores(queries4, keys_block, scale) - log_total[..., None]).astype(
            jnp.bfloat16
        )
        return running + jnp.einsum(
            "sgqk,skgd->sqgd", weights, values_block, preferred_element_type=jnp.float32
        )

    attended = lax.fori_loop(
        0, turns, accumulate, jnp.zeros((seqs_here, query_rows, groups, head_size), jnp.float32)
    )
    return (attended, log_total)


def attend_backward(queries4, keys_all, values_all, grad_out4, log_total, along, key_rows, scale):
    seqs_here, query_rows, groups, head_size = queries4.shape
    length = keys_all.shape[1]
    width_group = groups * head_size
    turns = length // key_rows

    def step_back(turn, carry):
        grad_queries, grad_keys, grad_values = carry
        keys_block = lax.dynamic_slice_in_dim(keys_all, turn * key_rows, key_rows, 1)
        keys4 = keys_block.reshape(seqs_here, key_rows, groups, head_size)
        values4 = lax.dynamic_slice_in_dim(values_all, turn * key_rows, key_rows, 1).reshape(
            seqs_here, key_rows, groups, head_size
        )
        weights = jnp.exp(block_scores(queries4, keys_block, scale) - log_total[..., None])
        grad_weights = jnp.einsum(
            "sqgd,skgd->sgqk", grad_out4, values4, preferred_element_type=jnp.float32
        )
        grad_scores = (weights * (grad_weights - along[..., None])).astype(jnp.bfloat16)
        grad_queries = grad_queries + jnp.einsum(
            "sgqk,skgd->sqgd", grad_scores, keys4, preferred_element_type=jnp.float32
        )
        key_part = (
            jnp.einsum("sgqk,sqgd->skgd", grad_scores, queries4, preferred_element_type=jnp.float32)
            * scale
        )
        value_part = jnp.einsum(
            "sgqk,sqgd->skgd",
            weights.astype(jnp.bfloat16),
            grad_out4,
            preferred_element_type=jnp.float32,
        )
        grad_keys = lax.dynamic_update_slice_in_dim(
            grad_keys, key_part.reshape(seqs_here, key_rows, width_group), turn * key_rows, 1
        )
        grad_values = lax.dynamic_update_slice_in_dim(
            grad_values, value_part.reshape(seqs_here, key_rows, width_group), turn * key_rows, 1
        )
        return (grad_queries, grad_keys, grad_values)

    start = (
        jnp.zeros((seqs_here, query_rows, groups, head_size), jnp.float32),
        jnp.zeros((seqs_here, length, width_group), jnp.float32),
        jnp.zeros((seqs_here, length, width_group), jnp.float32),
    )
    grad_queries, grad_keys, grad_values = lax.fori_loop(0, turns, step_back, start)
    return (grad_queries * scale, grad_keys, grad_values)


def local_general(tokens, cotangent, w_qkv, w_attn_out, w_in, w_mlp_out, norm_gain1, norm_gain2):
    seqs_here, block_rows, width = tokens.shape
    count_rows = seqs_here * block_rows
    heads_all = width // HD
    head_devices = lax.axis_size("head")
    group_devices = lax.axis_size(("dp", "ctx"))
    groups = heads_all // head_devices
    width_group = groups * HD
    scale = HD ** (-0.5)
    ff_width = w_in.shape[1] // 2
    full_qkv, full_out, full_in, full_mlp, gain_one, gain_two = (
        lax.all_gather(w_qkv, ("dp", "ctx"), axis=0, tiled=True),
        lax.all_gather(w_attn_out, ("dp", "ctx"), axis=0, tiled=True),
        lax.all_gather(w_in, ("dp", "ctx"), axis=0, tiled=True),
        lax.all_gather(w_mlp_out, ("dp", "ctx"), axis=0, tiled=True),
        lax.all_gather(norm_gain1, ("dp", "ctx"), axis=0, tiled=True),
        lax.all_gather(norm_gain2, ("dp", "ctx"), axis=0, tiled=True),
    )
    x_in = tokens.astype(jnp.float32).reshape(count_rows, width)
    normed1, factor1 = normalize(x_in)
    lowered1 = (normed1 * gain_one.astype(jnp.float32)).astype(jnp.bfloat16)
    projected = jnp.dot(lowered1, full_qkv, preferred_element_type=jnp.float32).reshape(
        seqs_here, block_rows, 3, heads_all, HD
    )
    first_pos = (lax.axis_index("ctx") * head_devices + lax.axis_index("head")) * block_rows
    positions = (first_pos + jnp.arange(block_rows, dtype=jnp.int32)).astype(jnp.float32)
    cosine, sine_table = rope_tables(positions, HD // 2)
    queries = (
        rotate(projected[:, :, 0], cosine, sine_table, 1.0)
        .astype(jnp.bfloat16)
        .reshape(seqs_here, block_rows, width)
    )
    keys_local = (
        rotate(projected[:, :, 1], cosine, sine_table, 1.0)
        .astype(jnp.bfloat16)
        .reshape(seqs_here, block_rows, width)
    )
    values_local = projected[:, :, 2].astype(jnp.bfloat16).reshape(seqs_here, block_rows, width)
    queries_h, keys_h, values_h = (
        lax.all_to_all(queries, "head", split_axis=2, concat_axis=1, tiled=True),
        lax.all_to_all(keys_local, "head", split_axis=2, concat_axis=1, tiled=True),
        lax.all_to_all(values_local, "head", split_axis=2, concat_axis=1, tiled=True),
    )
    query_rows = queries_h.shape[1]
    queries4 = queries_h.reshape(seqs_here, query_rows, groups, HD)
    keys_all, values_all = (
        lax.all_gather(keys_h, "ctx", axis=1, tiled=True),
        lax.all_gather(values_h, "ctx", axis=1, tiled=True),
    )
    key_rows = math.gcd(keys_all.shape[1], 1024)
    attended, log_total = attend_forward(queries4, keys_all, values_all, key_rows, scale)
    attended_low = attended.astype(jnp.bfloat16).reshape(seqs_here, query_rows, width_group)
    back_rows = lax.all_to_all(
        attended_low, "head", split_axis=1, concat_axis=2, tiled=True
    ).reshape(count_rows, width)
    residual = x_in + jnp.dot(back_rows, full_out, preferred_element_type=jnp.float32)
    normed2, factor2 = normalize(residual)
    lowered2 = (normed2 * gain_two.astype(jnp.float32)).astype(jnp.bfloat16)
    lifted = jnp.dot(lowered2, full_in, preferred_element_type=jnp.float32)
    first_part = lifted[:, :ff_width]
    second_part = lifted[:, ff_width:]
    activated, gelu_pullback = jax.vjp(
        lambda entries: jax.nn.gelu(entries, approximate=False), first_part
    )
    mixed = (activated * second_part).astype(jnp.bfloat16)
    result = (residual + jnp.dot(mixed, full_mlp, preferred_element_type=jnp.float32)).astype(
        jnp.bfloat16
    )
    full_qkv, full_out, full_in, full_mlp, gain_one, gain_two = (
        lax.all_gather(w_qkv, ("dp", "ctx"), axis=0, tiled=True),
        lax.all_gather(w_attn_out, ("dp", "ctx"), axis=0, tiled=True),
        lax.all_gather(w_in, ("dp", "ctx"), axis=0, tiled=True),
        lax.all_gather(w_mlp_out, ("dp", "ctx"), axis=0, tiled=True),
        lax.all_gather(norm_gain1, ("dp", "ctx"), axis=0, tiled=True),
        lax.all_gather(norm_gain2, ("dp", "ctx"), axis=0, tiled=True),
    )
    keys_all, values_all = (
        lax.all_gather(keys_h, "ctx", axis=1, tiled=True),
        lax.all_gather(values_h, "ctx", axis=1, tiled=True),
    )
    grad_top = cotangent.reshape(count_rows, width)
    grad_mlp = jnp.einsum("nf,nd->fd", mixed, grad_top, preferred_element_type=jnp.float32)
    grad_mixed = jnp.einsum("nd,fd->nf", grad_top, full_mlp, preferred_element_type=jnp.float32)
    grad_first = gelu_pullback(grad_mixed * second_part)[0]
    grad_lifted = jnp.concatenate([grad_first, grad_mixed * activated], axis=-1).astype(
        jnp.bfloat16
    )
    grad_inner = jnp.einsum("nd,nf->df", lowered2, grad_lifted, preferred_element_type=jnp.float32)
    grad_lowered2 = jnp.einsum(
        "nf,df->nd", grad_lifted, full_in, preferred_element_type=jnp.float32
    )
    grad_two = jnp.sum(grad_lowered2 * normed2, axis=0)
    grad_residual = grad_top.astype(jnp.float32) + norm_back(
        grad_lowered2 * gain_two.astype(jnp.float32), normed2, factor2
    )
    grad_branch = grad_residual.astype(jnp.bfloat16)
    grad_outproj = jnp.einsum(
        "nd,ne->de", back_rows, grad_branch, preferred_element_type=jnp.float32
    )
    grad_attended = jnp.einsum(
        "ne,de->nd", grad_branch, full_out, preferred_element_type=jnp.float32
    ).astype(jnp.bfloat16)
    grad_attended_h = lax.all_to_all(
        grad_attended.reshape(seqs_here, block_rows, width),
        "head",
        split_axis=2,
        concat_axis=1,
        tiled=True,
    )
    grad_out4 = grad_attended_h.reshape(seqs_here, query_rows, groups, HD)
    along = jnp.transpose(jnp.sum(grad_out4.astype(jnp.float32) * attended, axis=-1), (0, 2, 1))
    grad_queries, grad_keys_all, grad_values_all = attend_backward(
        queries4, keys_all, values_all, grad_out4, log_total, along, key_rows, scale
    )
    grad_keys_sum, grad_values_sum = (
        lax.psum_scatter(
            grad_keys_all.astype(jnp.bfloat16), "ctx", scatter_dimension=1, tiled=True
        ).astype(jnp.float32),
        lax.psum_scatter(
            grad_values_all.astype(jnp.bfloat16), "ctx", scatter_dimension=1, tiled=True
        ).astype(jnp.float32),
    )
    grad_q_low = grad_queries.astype(jnp.bfloat16).reshape(seqs_here, query_rows, width_group)
    grad_q_tok, grad_k_tok, grad_v_tok = (
        lax.all_to_all(grad_q_low, "head", split_axis=1, concat_axis=2, tiled=True),
        lax.all_to_all(
            grad_keys_sum.astype(jnp.bfloat16), "head", split_axis=1, concat_axis=2, tiled=True
        ),
        lax.all_to_all(
            grad_values_sum.astype(jnp.bfloat16), "head", split_axis=1, concat_axis=2, tiled=True
        ),
    )
    unrot_q = rotate(
        grad_q_tok.astype(jnp.float32).reshape(seqs_here, block_rows, heads_all, HD),
        cosine,
        sine_table,
        -1.0,
    )
    unrot_k = rotate(
        grad_k_tok.astype(jnp.float32).reshape(seqs_here, block_rows, heads_all, HD),
        cosine,
        sine_table,
        -1.0,
    )
    grad_projected = jnp.concatenate(
        [
            unrot_q.reshape(count_rows, width),
            unrot_k.reshape(count_rows, width),
            grad_v_tok.astype(jnp.float32).reshape(count_rows, width),
        ],
        axis=-1,
    ).astype(jnp.bfloat16)
    grad_project = jnp.einsum(
        "nd,nf->df", lowered1, grad_projected, preferred_element_type=jnp.float32
    )
    grad_lowered1 = jnp.einsum(
        "nf,df->nd", grad_projected, full_qkv, preferred_element_type=jnp.float32
    )
    grad_one = jnp.sum(grad_lowered1 * normed1, axis=0)
    grad_input = grad_residual + norm_back(
        grad_lowered1 * gain_one.astype(jnp.float32), normed1, factor1
    )
    pieces_one = grad_one.reshape(group_devices, head_devices, -1)
    pieces_two = grad_two.reshape(group_devices, head_devices, -1)
    part_qkv, part_out, part_in, part_mlp, part_one, part_two = (
        lax.psum_scatter(
            grad_project.astype(jnp.bfloat16), ("dp", "ctx"), scatter_dimension=0, tiled=True
        ).astype(jnp.float32),
        lax.psum_scatter(
            grad_outproj.astype(jnp.bfloat16), ("dp", "ctx"), scatter_dimension=0, tiled=True
        ).astype(jnp.float32),
        lax.psum_scatter(
            grad_inner.astype(jnp.bfloat16), ("dp", "ctx"), scatter_dimension=0, tiled=True
        ).astype(jnp.float32),
        lax.psum_scatter(
            grad_mlp.astype(jnp.bfloat16), ("dp", "ctx"), scatter_dimension=0, tiled=True
        ).astype(jnp.float32),
        lax.psum_scatter(
            pieces_one.astype(jnp.bfloat16), ("dp", "ctx"), scatter_dimension=0, tiled=True
        ).astype(jnp.float32),
        lax.psum_scatter(
            pieces_two.astype(jnp.bfloat16), ("dp", "ctx"), scatter_dimension=0, tiled=True
        ).astype(jnp.float32),
    )
    final_qkv, final_out, final_in, final_mlp, final_one, final_two = (
        lax.psum_scatter(
            part_qkv.astype(jnp.bfloat16), "head", scatter_dimension=1, tiled=True
        ).astype(jnp.float32),
        lax.psum_scatter(
            part_out.astype(jnp.bfloat16), "head", scatter_dimension=1, tiled=True
        ).astype(jnp.float32),
        lax.psum_scatter(
            part_in.astype(jnp.bfloat16), "head", scatter_dimension=1, tiled=True
        ).astype(jnp.float32),
        lax.psum_scatter(
            part_mlp.astype(jnp.bfloat16), "head", scatter_dimension=1, tiled=True
        ).astype(jnp.float32),
        lax.psum_scatter(
            part_one.astype(jnp.bfloat16), "head", scatter_dimension=1, tiled=True
        ).astype(jnp.float32),
        lax.psum_scatter(
            part_two.astype(jnp.bfloat16), "head", scatter_dimension=1, tiled=True
        ).astype(jnp.float32),
    )
    return (
        result.reshape(seqs_here, block_rows, width),
        grad_input.reshape(seqs_here, block_rows, width),
        final_qkv,
        final_out,
        final_in,
        final_mlp,
        final_one.reshape(-1),
        final_two.reshape(-1),
    )


F32 = jnp.float32
BF16 = jnp.bfloat16
VMEM_BYTES = 56 * 1024 * 1024
GROUP = ("ctx", "head")


def dot(left, right, dims=((1,), (0,))):
    return lax.dot_general(left, right, (dims, ((), ())), preferred_element_type=F32)


def wide(values):
    return values.astype(F32)


def flat(values):
    return values.reshape(-1, values.shape[-1])


def lane_rotate(values, cosine, sine_signed):
    lane = lax.broadcasted_iota(jnp.int32, values.shape, 1)
    width = values.shape[1]
    partner = jnp.where(
        lane % HD < HD // 2,
        pltpu.roll(values, width - HD // 2, 1),
        pltpu.roll(values, HD // 2, 1),
    )
    return values * cosine + partner * sine_signed


def head_masks(shape):
    lane = lax.broadcasted_iota(jnp.int32, shape, 1)
    return [lane // HD == head for head in range(shape[1] // HD)]


def params():
    return pltpu.CompilerParams(vmem_limit_bytes=VMEM_BYTES)


COST = pl.CostEstimate(flops=1 << 20, transcendentals=0, bytes_accessed=1 << 16)


def whole(array):
    return pl.BlockSpec(array.shape, lambda *_: (0,) * len(array.shape))


SCALARS = pl.BlockSpec(memory_space=pltpu.SMEM)


def project_kernel(place_ref, *refs):
    pieces, weights = refs[:6], refs[6:10]
    cos_ref, sin_ref, low_ref, qkv_ref, w_ref, gain1_ref, gain2_ref, rows_ref = refs[10:]
    block, part = pieces[0].shape[2], w_ref.shape[1] // 3
    rows = gain1_ref.shape[1] // 8

    @pl.when(pl.program_id(0) == 0)
    def _():
        for step, piece in enumerate(weights):
            for turn in range(2):
                at = 2 * (place_ref[8] ^ step) + (place_ref[9] ^ turn)
                w_ref[pl.ds(pl.multiple_of(at * rows, rows), rows), :] = piece[turn, :rows]
                gains = piece[turn, rows:].astype(F32)
                rows_ref[0, pl.ds(at, 1), :] = gains[:1, :rows]
                rows_ref[1, pl.ds(at, 1), :] = gains[1:2, :rows]
        for out, at in ((gain1_ref, 0), (gain2_ref, 1)):
            for row in range(8):
                out[:, row * rows : (row + 1) * rows] = rows_ref[at, row : row + 1, :]

    gain = gain1_ref[...]
    index = 0
    for piece in pieces:
        for inner in range(piece.shape[0]):
            normed, _ = normalize(piece[inner, 0].astype(F32))
            low_ref[index, 0] = (normed * gain).astype(BF16)
            index += 1
    projected = dot(flat(low_ref[:, 0]), w_ref[...])
    cosine, sine = cos_ref[...], sin_ref[...]
    shape = (8, block, part)
    qkv_ref[:, 0, :, :part] = (
        (lane_rotate(projected[:, :part], cosine, sine) * HD**-0.5).astype(BF16).reshape(shape)
    )
    qkv_ref[:, 0, :, part : 2 * part] = (
        lane_rotate(projected[:, part : 2 * part], cosine, sine).astype(BF16).reshape(shape)
    )
    qkv_ref[:, 0, :, 2 * part :] = projected[:, 2 * part :].astype(BF16).reshape(shape)


def project(place, pieces, weights, cosine, sine):
    seqs, block, width = pieces[0].shape[1:]
    own = weights[0].shape[2]

    def by_seq(lead, last):
        return pl.BlockSpec((lead, 1, block, last), lambda s: (0, s, 0, 0))

    return pl.pallas_call(
        project_kernel,
        grid=(seqs,),
        in_specs=[SCALARS]
        + [by_seq(piece.shape[0], width) for piece in pieces]
        + [whole(w) for w in weights]
        + [whole(cosine), whole(sine)],
        out_specs=(
            by_seq(8, width),
            by_seq(8, own),
            pl.BlockSpec((width, own), lambda s: (0, 0)),
            pl.BlockSpec((1, width), lambda s: (0, 0)),
            pl.BlockSpec((1, width), lambda s: (0, 0)),
        ),
        out_shape=(
            jax.ShapeDtypeStruct((8, seqs, block, width), BF16),
            jax.ShapeDtypeStruct((8, seqs, block, own), BF16),
            jax.ShapeDtypeStruct((width, own), BF16),
            jax.ShapeDtypeStruct((1, width), F32),
            jax.ShapeDtypeStruct((1, width), F32),
        ),
        scratch_shapes=[pltpu.VMEM((2, 8, width // 8), F32)],
        compiler_params=params(),
        cost_estimate=COST,
        name="project",
    )(place, *pieces, *weights, cosine, sine)


def attend_kernel(place_ref, q_ref, k_ref, v_ref, *refs):
    att_ref, log_ref, home_ref = refs[-3:]
    step, seq = pl.program_id(0), len(refs) - 3
    if seq:

        @pl.when(step == 0)
        def _():
            home_ref[:, :1] = refs[0][...]

    queries, keys, values = flat(q_ref[...]), flat(k_ref[...]), flat(v_ref[...])
    attended = jnp.zeros(queries.shape, F32)
    logs = jnp.zeros(queries.shape, F32)
    for mask in head_masks(queries.shape):
        scores = dot(jnp.where(mask, queries, 0), keys, ((1,), (1,)))
        peak = jnp.max(scores, axis=1, keepdims=True)
        weights = jnp.exp(scores - peak)
        total = jnp.sum(weights, axis=1, keepdims=True)
        mixed = dot(weights.astype(BF16), values) * (1.0 / total)
        attended = jnp.where(mask, mixed, attended)
        logs = jnp.where(mask, peak + jnp.log(total), logs)
    att_ref[...] = attended.reshape(att_ref.shape)
    log_ref[...] = logs.reshape(log_ref.shape)
    low = attended.astype(BF16).reshape(att_ref.shape)
    for inner in range(2):
        home_ref[place_ref[2 * step + inner], seq] = low[inner, 0]


def attend(place, qkv, *home):
    _, _, block, own = qkv.shape
    part, seq = own // 3, len(home)
    rows = pl.BlockSpec((2, 1, block, part), lambda i: (i, 0, 0, 0))
    shape = (8, 1, block, part)
    return pl.pallas_call(
        attend_kernel,
        grid=(4,),
        in_specs=[
            SCALARS,
            pl.BlockSpec((2, 1, block, part), lambda i: (i, seq, 0, 0)),
            pl.BlockSpec((8, 1, block, part), lambda i: (0, seq, 0, 1)),
            pl.BlockSpec((8, 1, block, part), lambda i: (0, seq, 0, 2)),
            *[whole(h) for h in home],
        ],
        out_specs=(
            rows,
            rows,
            pl.BlockSpec((8, 1 + seq, block, part), lambda i: (0, 0, 0, 0)),
        ),
        out_shape=(
            jax.ShapeDtypeStruct(shape, F32),
            jax.ShapeDtypeStruct(shape, F32),
            jax.ShapeDtypeStruct((8, 1 + seq, block, part), BF16),
        ),
        compiler_params=params(),
        cost_estimate=COST,
        name="attend",
    )(place, qkv, qkv, qkv, *home)


def branch_kernel(place_ref, *refs):
    pieces = refs[:6]
    rows_ref, tokens_ref, gain_ref, residual_ref, low_ref, side_ref, total_ref = refs[6:]
    heads = rows_ref.shape[0] // 2
    for c in range(2):
        side_ref[c] = jnp.concatenate([flat(rows_ref[c * heads + d]) for d in range(heads)], axis=1)
    total_ref[...] = flat(wide(tokens_ref[...]))
    index = 0
    for piece in pieces:
        n = piece.shape[2]
        for inner in range(piece.shape[0]):
            at = place_ref[index]
            columns = pl.ds(pl.multiple_of((at % heads) * n, n), n)
            total_ref[:, columns] += dot(side_ref[at // heads], piece[inner])
            index += 1
    total = total_ref[...]
    normed, _ = normalize(total)
    residual_ref[...] = total.reshape(residual_ref.shape)
    low_ref[...] = (normed * gain_ref[...]).astype(BF16).reshape(low_ref.shape)


def branch(place, pieces, rows, tokens, gain):
    args = (*pieces, rows, tokens, gain)
    seqs, block, width = tokens.shape
    return pl.pallas_call(
        branch_kernel,
        in_specs=[SCALARS] + [whole(a) for a in args],
        out_shape=(
            jax.ShapeDtypeStruct(tokens.shape, F32),
            jax.ShapeDtypeStruct(tokens.shape, BF16),
        ),
        scratch_shapes=[
            pltpu.VMEM((2, seqs * block, pieces[0].shape[1]), BF16),
            pltpu.VMEM((seqs * block, width), F32),
        ],
        compiler_params=params(),
        cost_estimate=COST,
        name="branch",
    )(place, *args)


def combine(*groups):
    parts = [part for group in groups for _, parts in group for part in parts]
    rows = sum(count for count, _ in groups[0])
    width = parts[0][0].shape[2]

    def kernel(*refs):
        at = 0
        for k, group in enumerate(groups):
            row = 0
            for count, terms in group:
                total = 0.0
                for _, _, start in terms:
                    total = total + wide(refs[at][0, start : start + count])
                    at += 1
                refs[-1][k, row : row + count] = total.astype(BF16)
                row += count

    return pl.pallas_call(
        kernel,
        grid=(1,),
        in_specs=[
            pl.BlockSpec((1, *array.shape[1:]), lambda *_, index=index: (index, 0, 0))
            for array, index, _ in parts
        ],
        out_specs=pl.BlockSpec((len(groups), rows, width), lambda *_: (0, 0, 0)),
        out_shape=jax.ShapeDtypeStruct((len(groups), rows, width), BF16),
        compiler_params=params(),
        cost_estimate=COST,
        name="combine",
    )(*[array for array, _, _ in parts])


def mlp_kernel(*refs, count, ends):
    pieces, tops = refs[:count], refs[count : 2 * count]
    w_ref, out_w_ref = refs[2 * count : 2 * count + 2]
    low_ref, top_ref, mixed_ref, lifted_ref, *out_refs = refs[-4 - len(ends) :]
    step = pl.program_id(0)
    start = 0
    for piece, top in zip(pieces, tops):

        @pl.when((step >= start) & (step < start + piece.shape[0]))
        def _(piece=piece, top=top, start=start):
            low_ref[0] = piece[step - start]
            top_ref[0] = top[step - start]

        start += piece.shape[0]

    hidden = w_ref.shape[1] // 2
    lifted = dot(flat(low_ref[...]), w_ref[...])
    first, second = lifted[:, :hidden], lifted[:, hidden:]
    grad_mixed = dot(flat(top_ref[...]), out_w_ref[...], ((1,), (1,)))
    gate = 0.5 * (1.0 + lax.erf(first * (0.5**0.5)))
    slope = gate + first * jnp.exp(first * first * -0.5) * ((2.0 * math.pi) ** -0.5)
    activated = first * gate
    mixed_ref[...] = (activated * second).astype(BF16).reshape(mixed_ref.shape)
    grad = jnp.concatenate(
        [(grad_mixed * second * slope).astype(BF16), (grad_mixed * activated).astype(BF16)],
        axis=1,
    )
    lifted_ref[...] = grad.reshape(lifted_ref.shape)
    partial = dot(grad, w_ref[...], ((1,), (1,))).astype(BF16).reshape(low_ref.shape)
    start = 0
    for out, end in zip(out_refs, ends):

        @pl.when((step >= start) & (step < end))
        def _(out=out):
            out[...] = partial

        start = end


def mlp(pieces, tops, w, out_w, base, ends, earlier=()):
    seqs, block, width = pieces[0].shape[1:]
    hidden = w.shape[1] // 2
    whole_in = (*pieces, *tops, w, out_w)

    def rows(last):
        return pl.BlockSpec((1, seqs, block, last), lambda i: (i + base, 0, 0, 0))

    def within(start, end):
        return pl.BlockSpec(
            (1, seqs, block, width),
            lambda i: (jnp.clip(i - start, 0, end - start - 1), 0, 0, 0),
        )

    starts = (0, *ends[:-1])
    lasts = (width, width, hidden, 2 * hidden)
    return pl.pallas_call(
        functools.partial(mlp_kernel, count=len(pieces), ends=ends),
        grid=(ends[-1],),
        in_specs=[whole(array) for array in whole_in]
        + [pl.BlockSpec(memory_space=pl.ANY)] * len(earlier),
        out_specs=(
            *[rows(last) for last in lasts],
            *[within(start, end) for start, end in zip(starts, ends)],
        ),
        out_shape=(
            *[jax.ShapeDtypeStruct((8, seqs, block, last), BF16) for last in lasts],
            *[
                jax.ShapeDtypeStruct((end - start, seqs, block, width), BF16)
                for start, end in zip(starts, ends)
            ],
        ),
        input_output_aliases={len(whole_in) + at: at for at in range(len(earlier))},
        compiler_params=params(),
        cost_estimate=COST,
        name="mlp",
    )(*whole_in, *earlier)


def out_grad_kernel(place_ref, rows_ref, grad_ref, keep_ref, send_ref):
    grads = flat(grad_ref[...])
    for index in range(8):
        part = dot(flat(rows_ref[place_ref[index]]), grads, ((0,), (0,))).astype(BF16)
        if index < 5:
            keep_ref[index] = part
        else:
            send_ref[index - 5] = part


def out_grad(place, rows, grads):
    part, width = rows.shape[-1], grads.shape[-1]
    return pl.pallas_call(
        out_grad_kernel,
        in_specs=[SCALARS, whole(rows), whole(grads)],
        out_shape=(
            jax.ShapeDtypeStruct((5, part, width), BF16),
            jax.ShapeDtypeStruct((3, part, width), BF16),
        ),
        compiler_params=params(),
        cost_estimate=COST,
        name="out_grad",
    )(place, rows, grads)


def branch_back_kernel(place_ref, *refs):
    pieces = refs[:6]
    keep_ref, near_ref, own_ref, residual_ref, top_ref, gain_ref = refs[6:12]
    grad_ref, branch_ref, home_ref, sum_ref, low_ref, side_ref = refs[12:]
    grad_low = wide(flat(keep_ref[...])) + wide(flat(near_ref[...])) + wide(flat(own_ref[...]))
    normed, factor = normalize(flat(residual_ref[...]))
    sum_ref[...] = jnp.sum(grad_low * normed, axis=0, keepdims=True)
    grad = flat(wide(top_ref[...])) + norm_back(grad_low * gain_ref[...], normed, factor)
    grad_ref[...] = grad.reshape(grad_ref.shape)
    low_ref[...] = grad.astype(BF16)
    branch_ref[...] = low_ref[...].reshape(branch_ref.shape)
    heads = home_ref.shape[0] // 2
    side_ref[...] = jnp.zeros_like(side_ref)
    index = 0
    for piece in pieces:
        n = piece.shape[2]
        for inner in range(piece.shape[0]):
            at = place_ref[index]
            columns = pl.ds(pl.multiple_of((at % heads) * n, n), n)
            side_ref[at // heads] += dot(low_ref[:, columns], piece[inner], ((1,), (1,)))
            index += 1
    part = home_ref.shape[3]
    for c in range(2):
        for d in range(heads):
            home = side_ref[c, :, d * part : (d + 1) * part].astype(BF16)
            home_ref[c * heads + d] = home.reshape(home_ref.shape[1:])


def branch_back(place, pieces, keep, near, own, residual, top, gain):
    args = (*pieces, keep, near, own, residual, top, gain)
    seqs, block, width = residual.shape
    tall = pieces[0].shape[1]
    shapes = (
        jax.ShapeDtypeStruct(residual.shape, F32),
        jax.ShapeDtypeStruct(residual.shape, BF16),
        jax.ShapeDtypeStruct((8, seqs, block, tall // 4), BF16),
        jax.ShapeDtypeStruct((1, width), F32),
    )
    return pl.pallas_call(
        branch_back_kernel,
        grid=(1,),
        in_specs=[SCALARS]
        + [whole(piece) for piece in pieces]
        + [pl.BlockSpec((1, seqs * block, width), lambda *_: (0, 0, 0))] * 2
        + [whole(a) for a in args[8:]],
        out_specs=tuple(whole(shape) for shape in shapes),
        out_shape=shapes,
        scratch_shapes=[
            pltpu.VMEM((seqs * block, width), BF16),
            pltpu.VMEM((2, seqs * block, tall), F32),
        ],
        compiler_params=params(),
        cost_estimate=COST,
        name="branch_back",
    )(place, *args)


def attend_back_kernel(
    place_ref, q_ref, k_ref, v_ref, grad_ref, att_ref, log_ref, cosq_ref, sinq_ref, cos_ref,
    sin_ref, w_ref, low_ref, *refs, seq, last,
):
    if last:
        before_ref, gain1_ref, gain2_ref, keep_ref, send_ref, grad_w_ref, *scratch = refs
    else:
        keep_ref, send_ref, before_ref, *scratch = refs
    proj_ref, sum_k, sum_v = scratch
    step = pl.program_id(0)
    block, part = q_ref.shape[2], q_ref.shape[3]

    @pl.when(step == 0)
    def _():
        sum_k[...] = jnp.zeros_like(sum_k)
        sum_v[...] = jnp.zeros_like(sum_v)

    queries, keys, values = flat(q_ref[...]), flat(k_ref[...]), flat(v_ref[...])
    grads = jnp.concatenate([grad_ref[place_ref[2 * step + inner], seq] for inner in range(2)])
    along = (grads.astype(F32) * flat(att_ref[...])).T
    logs = flat(log_ref[...]).T
    grad_queries = jnp.zeros(queries.shape, F32)
    for head, mask in enumerate(head_masks(queries.shape)):
        own_q = jnp.where(mask, queries, 0)
        own_g = jnp.where(mask, grads, 0)
        scores = dot(keys, own_q, ((1,), (1,)))
        weights = jnp.exp(scores - logs[head * HD : head * HD + 1])
        lifted = dot(values, own_g, ((1,), (1,)))
        row = jnp.sum(along[head * HD : (head + 1) * HD], axis=0, keepdims=True)
        grad_scores = (weights * (lifted - row)).astype(BF16)
        sum_k[...] += dot(grad_scores, own_q)
        sum_v[...] += dot(weights.astype(BF16), own_g)
        grad_queries = jnp.where(mask, dot(grad_scores, keys, ((0,), (0,))), grad_queries)
    grad_queries = lane_rotate(grad_queries * HD**-0.5, cosq_ref[...], -sinq_ref[...])
    rows = pl.multiple_of(step * 2 * block, 2 * block)
    proj_ref[pl.ds(rows, 2 * block), :part] = grad_queries.astype(BF16)

    @pl.when(step == 3)
    def _():
        grad_keys = lane_rotate(sum_k[...], cos_ref[...], -sin_ref[...])
        proj_ref[:, part : 2 * part] = grad_keys.astype(BF16)
        proj_ref[:, 2 * part :] = sum_v[...].astype(BF16)
        partial = dot(proj_ref[...], w_ref[...], ((1,), (1,))).astype(BF16)
        keep_ref[...] = partial[: 5 * block].reshape(5, block, -1)
        send_ref[...] = partial[5 * block :].reshape(3, block, -1)
        grad_w = dot(proj_ref[...], flat(low_ref[...]), ((0,), (0,)))
        if last:
            grad_w = (grad_w + before_ref[...]).T
            along_w = jnp.sum(grad_w * wide(w_ref[...]), axis=1, keepdims=True)
            along_w = jnp.broadcast_to(along_w, (w_ref.shape[0], 128)).T[:1] / gain1_ref[...]
            row = lax.broadcasted_iota(jnp.int32, (GAIN_ROWS, w_ref.shape[0]), 0)
            gains = jnp.where(row == 0, along_w, jnp.where(row == 1, gain2_ref[...], 0.0))
            n = grad_w_ref.shape[1] - GAIN_ROWS
            for at in range(grad_w_ref.shape[0]):
                part_rows = slice(at * n, (at + 1) * n)
                grad_w_ref[at, :n] = grad_w[part_rows].astype(BF16)
                grad_w_ref[at, n:, :n] = gains[:, part_rows].astype(BF16)
                rest = grad_w_ref.shape[2] - n
                grad_w_ref[at, n:, n:] = jnp.zeros((GAIN_ROWS, rest), BF16)
        else:
            before_ref[...] = grad_w


GAIN_ROWS = 16


def attend_back(place, qkv, grads, attended, logs, cosine, sine, w, low, seq, *before, dp=1):
    _, _, block, own = qkv.shape
    part, width = own // 3, w.shape[0]
    last = len(before) > 0
    rows = pl.BlockSpec((2, 1, block, part), lambda i: (i, 0, 0, 0))
    angles = pl.BlockSpec((2 * block, part), lambda i: (i, 0))

    def full(*shape):
        return pl.BlockSpec(shape, lambda i: (0,) * len(shape))

    args = [place, qkv, qkv, qkv, grads, attended, logs, cosine, sine, cosine, sine, w, low]
    in_specs = [
        SCALARS,
        pl.BlockSpec((2, 1, block, part), lambda i: (i, seq, 0, 0)),
        pl.BlockSpec((8, 1, block, part), lambda i: (0, seq, 0, 1)),
        pl.BlockSpec((8, 1, block, part), lambda i: (0, seq, 0, 2)),
        whole(grads),
        rows,
        rows,
        angles,
        angles,
        whole(cosine),
        whole(sine),
        whole(w),
        pl.BlockSpec((8, 1, block, width), lambda i: (0, seq, 0, 0)),
    ]
    shapes = [((5, block, width), BF16), ((3, block, width), BF16)]
    if last:
        args += before
        in_specs += [whole(array) for array in before]
        shapes += [((dp, width // dp + GAIN_ROWS, own), BF16)]
    else:
        shapes += [((own, width), F32)]
    return pl.pallas_call(
        functools.partial(attend_back_kernel, seq=seq, last=last),
        grid=(4,),
        in_specs=in_specs,
        out_specs=tuple(full(*shape) for shape, _ in shapes),
        out_shape=tuple(jax.ShapeDtypeStruct(shape, kind) for shape, kind in shapes),
        scratch_shapes=[
            pltpu.VMEM((8 * block, own), BF16),
            pltpu.VMEM((8 * block, part), F32),
            pltpu.VMEM((8 * block, part), F32),
        ],
        compiler_params=params(),
        cost_estimate=COST,
        name="attend_back",
    )(*args)


def input_grad_kernel(*refs):
    keeps, (near_ref, own_ref, tokens_ref, residual_ref, gain_ref, out_ref) = refs[:-6], refs[-6:]
    block = tokens_ref.shape[1]
    for seq, keep in enumerate(keeps):
        rows = slice(seq * block, (seq + 1) * block)
        grad = wide(keep[0, :block]) + wide(near_ref[0, rows]) + wide(own_ref[0, rows])
        normed, factor = normalize(wide(tokens_ref[seq]))
        out_ref[seq] = residual_ref[seq] + norm_back(grad * gain_ref[...], normed, factor)


def input_grad(keeps, near, own, tokens, residual, gain):
    rest = (own, tokens, residual, gain)
    return pl.pallas_call(
        input_grad_kernel,
        grid=(1,),
        in_specs=[
            pl.BlockSpec((1, *array.shape[1:]), lambda *_: (0, 0, 0)) for array in (*keeps, near)
        ]
        + [whole(array) for array in rest],
        out_specs=whole(residual),
        out_shape=jax.ShapeDtypeStruct(residual.shape, F32),
        compiler_params=params(),
        cost_estimate=COST,
        name="input_grad",
    )(*keeps, near, *rest)


class Group:
    def __init__(self):
        self.heads = lax.axis_size("head")
        self.dp = lax.axis_size("dp")
        self.ctx_at = lax.axis_index("ctx")
        self.head_at = lax.axis_index("head")
        self.dp_at = lax.axis_index("dp")
        self.at = self.ctx_at * self.heads + self.head_at
        near, far = [], []
        for c in range(2):
            for h in range(self.heads):
                x, y = (c ^ 1) * self.heads + h, c * self.heads + (h ^ 2)
                near.append((c * self.heads + h, x if h % 2 == 0 else y))
                far.append((c * self.heads + h, y if h % 2 == 0 else x))
        self.near, self.far = near, far

    def order(self):
        first = jnp.where(self.head_at % 2 == 0, 4, 2)
        second = 6 - first
        return jnp.stack(
            [self.at ^ bits for bits in (0, 1, first, first ^ 1, 6, second ^ 1, second, 7)]
        )

    def swap(self, values, bit):
        if bit == 4:
            return lax.ppermute(values, "ctx", [(0, 1), (1, 0)])
        return lax.ppermute(values, "head", [(i, i ^ bit) for i in range(self.heads)])

    def mate(self, values):
        return self.swap(values, 1)

    def to_near(self, values):
        return lax.ppermute(values, GROUP, self.near)

    def to_far(self, values):
        return lax.ppermute(values, GROUP, self.far)

    def rows_back(self, values, place):
        pairs, same = [], False
        for d in range(self.dp):
            for h in range(self.heads):
                if (d, h) == (place[h], d):
                    same = same | ((self.dp_at == d) & (self.head_at == h))
                else:
                    pairs.append((d * self.heads + h, place[h] * self.heads + d))
        return jnp.where(same, values, lax.ppermute(values, ("dp", "head"), pairs))

    def scatter_dp(self, values):
        step = self.dp // 2
        while step:
            n = values.shape[1] // 2
            bit = (self.dp_at // step) % 2
            sent = lax.dynamic_slice_in_dim(values, (1 - bit) * n, n, 1).astype(BF16)
            kept = lax.dynamic_slice_in_dim(values, bit * n, n, 1)
            values = wide(kept) + wide(self.across(sent, step))
            step //= 2
        return values

    def across(self, values, step):
        return lax.ppermute(values, "dp", [(i, i ^ step) for i in range(self.dp)])


def pick(array, index, axis):
    return lax.dynamic_index_in_dim(array, index, axis, keepdims=False)


def after(values, *earlier):
    return lax.optimization_barrier((values, earlier))[0]


def local_split(tokens, cotangent, w_qkv, w_attn_out, w_in, w_mlp_out, norm_gain1, norm_gain2):
    seqs, block, width = tokens.shape
    group = Group()
    heads, dp = group.heads, group.dp
    at_c, at_h = group.ctx_at, group.head_at
    parts = 2 * heads
    hidden = w_in.shape[1] // 2 // parts
    padded = -(-hidden // 128) * 128
    own_width = width // parts
    half = heads // 2
    rows_here = w_qkv.shape[0]
    place = [2 * (h % half) + h // half for h in range(heads)]
    straight = list(range(heads))
    order = group.order()
    scalars = jnp.concatenate([order, jnp.stack([group.dp_at, at_c])]).astype(jnp.int32)
    mate, near, far = group.mate, group.to_near, group.to_far

    def in_order(own, other):
        return jnp.where(at_c == 0, jnp.stack([own, other]), jnp.stack([other, own]))

    def exchange(values):
        return lax.all_to_all(values, GROUP, split_axis=0, concat_axis=0, tiled=True)


    gains = jnp.pad(
        jnp.stack([norm_gain1, norm_gain2]), ((0, 14), (0, 3 * own_width - rows_here))
    )
    qkv_view = w_qkv.reshape(rows_here, 3, width)

    def qkv_part(at):
        start = (2 * at_h + at) * own_width
        cut = lax.dynamic_slice_in_dim(qkv_view, start, own_width, 2)
        return jnp.concatenate([cut.reshape(rows_here, 3 * own_width), gains])

    x_own = tokens[None]
    x_mate = mate(x_own)
    qkv_other, qkv_own = qkv_part(1 - at_c), qkv_part(at_c)
    qkv_cross = group.swap(after(qkv_other, x_own), 4)
    in_view = after(w_in, qkv_other).reshape(rows_here, 2, heads, 2, hidden)
    in_view = pick(in_view, 2 * (at_h % half) + at_h // half, 2)

    def in_part(at):
        cut = pick(in_view, at, 2)
        return jnp.pad(cut, ((0, 0), (0, 0), (0, padded - hidden))).reshape(rows_here, 2 * padded)

    in_other, in_own = in_part(1 - at_c), in_part(at_c)
    in_cross = group.swap(in_other, 4)
    x_chip = jnp.concatenate([x_own, after(x_mate, qkv_cross, qkv_own, in_cross, in_own)])
    x_near = near(x_chip)
    qkv_pair = jnp.stack([qkv_own, qkv_cross])
    qkv_pieces = [qkv_pair] + [group.across(qkv_pair, step) for step in range(1, dp)]

    slices = jnp.concatenate([w_attn_out, w_mlp_out])
    slices = after(slices, qkv_pair)
    slices = lax.dynamic_slice_in_dim(slices, at_h * (width // heads), width // heads, 1)
    slices = lax.all_gather(slices, "dp", axis=0)
    positions = after(order, qkv_pair)[:, None] * block + jnp.arange(block, dtype=jnp.int32)
    lane = jnp.arange(own_width, dtype=jnp.int32)
    frequency = jnp.exp(
        (lane % (HD // 2)).astype(F32) * (-math.log(ROPE_BASE) / (HD // 2))
    )
    angles = wide(positions.reshape(-1))[:, None] * frequency[None, :]
    cosine = jnp.cos(angles)
    sine = jnp.sin(angles) * jnp.where(lane % HD < HD // 2, -1.0, 1.0)[None, :]

    x_far = far(x_near[:1])
    x_near, in_pair = lax.optimization_barrier(
        (after(x_near, *qkv_pieces, slices, cosine, sine), in_order(in_own, in_cross))
    )
    weight_in = lax.all_gather(in_pair, "dp", axis=0).reshape(width, -1)
    x_near_mate = mate(x_near)
    cot_own = after(cotangent, x_near)[None]
    cot_mate = mate(cot_own)
    x_far = after(x_far, cot_mate)
    x_far_mate = mate(x_far)

    cot_chip = jnp.concatenate([cot_own, cot_mate])
    cot_near = near(after(cot_chip, x_far))
    out_rows = w_attn_out.shape[0]
    out_own = slices[:, :out_rows].reshape(1, dp * out_rows, -1)
    out_mate = mate(after(out_own, x_far))
    x_pieces = (x_own, x_mate, x_near, x_far, x_near_mate, after(x_far_mate, cot_chip, out_own))
    low1, qkv, weight_qkv, gain_one, gain_two = project(
        scalars, x_pieces, qkv_pieces, cosine, sine
    )

    out_near = near(jnp.concatenate([out_own, after(out_mate, qkv)]))
    mlp_slices = jnp.stack([slices[place[h], out_rows:] for h in range(heads)])
    mlp_slices = after(mlp_slices, qkv)
    mlp_slices = lax.all_to_all(mlp_slices, "head", split_axis=0, concat_axis=0, tiled=True)
    att_0, log_0, home_0 = attend(scalars, after(qkv, out_mate))
    cot_near = after(cot_near, home_0)
    cot_far, cot_near_mate = far(cot_near[:1]), mate(cot_near)
    out_near = after(out_near, home_0)
    out_far, out_near_mate = far(out_near[:1]), mate(out_near)
    weight_mlp = jnp.moveaxis(after(mlp_slices, home_0), 0, 1).reshape(hidden, width)
    weight_mlp = jnp.pad(weight_mlp, ((0, padded - hidden), (0, 0)))
    att_1, log_1, home = attend(scalars, after(qkv, cot_near, out_near, weight_mlp), home_0)
    att_rows = exchange(home)
    out_far_mate, cot_far_mate = mate(after(out_far, home)), mate(after(cot_far, home))
    out_pieces = (out_own, out_mate, out_near, out_far, out_near_mate, out_far_mate)
    residual, low2 = branch(
        scalars, out_pieces, after(att_rows, cot_far_mate), tokens, gain_two
    )

    low_own = low2[None]
    low_mate = mate(low_own)
    low_near = near(jnp.concatenate([low_own, low_mate]))
    *arrays, keep_a = mlp(
        (low_own, low_mate), (cot_own, cot_mate), weight_in, weight_mlp, 0, (2,)
    )
    low_near = after(low_near, keep_a)
    low_far, low_near_mate = far(low_near[:1]), mate(low_near)
    *arrays, keep_b = mlp((low_near,), (cot_near,), weight_in, weight_mlp, 2, (2,), arrays)
    low_far_mate = mate(after(low_far, keep_b))
    low2_all, cot_all, mixed, grad_lifted, keep_c, send = mlp(
        (low_far, low_near_mate, low_far_mate),
        (cot_far, cot_near_mate, cot_far_mate),
        weight_in,
        weight_mlp,
        4,
        (1, 4),
        arrays,
    )

    def over_tokens(left, right):
        return dot(flat(left), flat(right), ((0,), (0,)))

    def scatter(values):
        return lax.psum_scatter(values.astype(BF16), "dp", scatter_dimension=0, tiled=True)

    def columns_first(values):
        return jnp.moveaxis(values.reshape(values.shape[0], dp, -1), 1, 0)

    rows = seqs * block

    def by_rows(values):
        return values.reshape(values.shape[0], -1, width)

    keep_a, keep_b, keep_c, send = (by_rows(array) for array in (keep_a, keep_b, keep_c, send))
    met = mate(send)
    last = combine([(rows, [(keep_c, 0, 0), (met, 2, 0)])])
    last_far = far(last)
    grad_mlp = columns_first(over_tokens(after(mixed, last), cot_all)[:hidden]).astype(BF16)
    last_far = after(last_far, grad_mlp)
    grad_mlp = scatter(grad_mlp)[0]
    chip = combine(
        [(rows, [(keep_b, 0, 0), (met, 0, 0), (last_far, 0, 0)])],
        [(rows, [(keep_b, 1, 0), (met, 1, 0)])],
    )
    chip_near = near(chip)
    grad_in = over_tokens(low2_all, after(grad_lifted, chip)).astype(BF16)
    cut = 5 * rows
    mixed_flat = flat(after(mixed, chip))
    out_keep = dot(mixed_flat[:cut], weight_mlp).astype(BF16).reshape(5, rows, width)
    out_send = dot(mixed_flat[cut:], weight_mlp).astype(BF16).reshape(3, rows, width)
    chip_near = after(chip_near, grad_in, out_keep, out_send)
    grad_in = scatter(grad_in)
    home = mate(combine([(rows, [(keep_a, 1, 0), (chip_near, 1, 0)])])[0])
    out_met = mate(after(out_send, chip_near))
    grad_residual, grad_branch, home, gain2_sum = branch_back(
        scalars, out_pieces, keep_a, chip_near, after(home, grad_mlp), residual, cotangent, gain_two
    )
    grad_home = exchange(home)

    rows_keep, rows_send = out_grad(scalars, after(att_rows, home), grad_branch)
    rows_met = mate(rows_send)
    few = rows_keep.shape[1]

    def ends(index, at, *more):
        kept = [(out_keep, index, 0)], [(rows_keep, index, 0)]
        if at is not None:
            kept[0].append((out_met, at, 0))
            kept[1].append((rows_met, at, 0))
        for array, where in more:
            kept[0].append((array, where, 0))
            kept[1].append((array, where, rows))
        return [(rows, kept[0]), (few, kept[1])]

    end_last = combine(ends(4, 2))
    grad_home = after(grad_home, end_last)
    end_far = far(after(end_last, grad_home))
    keep_0, send_0, before = attend_back(
        scalars, qkv, grad_home, att_0, log_0, cosine, sine, weight_qkv, low1, 0
    )
    met_0 = mate(send_0)
    end_far = after(end_far, send_0)
    end_chip = combine(ends(2, 0, (end_far, 0)), ends(3, 1))
    end_near = near(end_chip)
    keep_1, send_1, grad_qkv = attend_back(
        scalars, qkv, after(grad_home, end_chip), att_1, log_1, cosine, sine,
        weight_qkv, low1, 1, before, gain_one, gain2_sum, dp=dp,
    )

    grad_qkv = scatter(grad_qkv.reshape(-1, grad_qkv.shape[2]))
    met_1 = mate(send_1)
    in_parts = after(grad_in, send_1).reshape(2, rows_here, -1)
    in_cross = group.swap(pick(in_parts, 1 - at_c, 0), 4)

    def both(index, at, *more):
        kept = [(keep_0, index, 0)], [(keep_1, index, 0)]
        if at is not None:
            kept[0].append((met_0, at, 0))
            kept[1].append((met_1, at, 0))
        for array, where in more:
            kept[0].append((array, where, 0))
            kept[1].append((array, where, block))
        return [(block, kept[0]), (block, kept[1])]

    last = combine(both(4, 2))
    last_far = far(after(last, in_cross))
    grad_in = in_order(after(pick(in_parts, at_c, 0), last), in_cross)
    late = at_h // half
    grad_in = jnp.stack([grad_in[..., :hidden], grad_in[..., padded : padded + hidden]])
    last_far = after(last_far, grad_in)
    chip = combine(both(2, 0, (last_far, 0)), both(3, 1))
    chip_near = near(chip)

    end_home = mate(combine(ends(1, None, (after(end_near, chip), 1))))
    grad_out = wide(rows_keep[0]) + wide(end_near[0, rows:]) + wide(end_home[0, rows:])
    grad_out = group.scatter_dp(grad_out).astype(BF16)
    result = wide(out_keep[0]) + wide(end_near[0, :rows]) + wide(end_home[0, :rows])
    result = (residual + result.reshape(residual.shape)).astype(BF16)
    grad_in = after(grad_in, chip)
    stays = pick(grad_in, late, 0)
    comes = group.swap(pick(grad_in, 1 - late, 0), half)
    grad_mlp = group.rows_back(after(grad_mlp, chip), place)
    grad_qkv = after(grad_qkv, chip)
    both_rows = 2 * rows_here
    qkv_parts = grad_qkv[:both_rows].reshape(2, rows_here, -1)
    gains = grad_qkv[both_rows:]
    cross = jnp.concatenate([pick(qkv_parts, 1 - at_c, 0), gains])
    cross = group.swap(cross, 4)
    chip_near = after(chip_near, comes, result, cross, grad_mlp, grad_out)
    home = mate(combine(both(1, None, (chip_near, 1))))
    cross = after(cross, chip_near)
    grad_qkv = in_order(pick(qkv_parts, at_c, 0), cross[:rows_here])
    gains = (wide(gains) + wide(cross[rows_here:])).astype(BF16)
    gains = wide(gains) + sum(wide(group.swap(gains, bit)) for bit in range(1, heads))
    grad_out = wide(group.rows_back(after(grad_out, chip_near), straight))
    grad_input = input_grad((keep_0, keep_1), chip_near, home, tokens, grad_residual, gain_one)

    grad_mlp = wide(grad_mlp)
    grad_in = jnp.where(
        late == 0, jnp.concatenate([stays, comes]), jnp.concatenate([comes, stays])
    )
    grad_in = wide(jnp.moveaxis(grad_in, 0, 1).reshape(rows_here, -1))

    per_device = width // (dp * parts)
    start = group.at * per_device
    grad_gain1, grad_gain2 = (
        lax.dynamic_slice_in_dim(gains[i], start, per_device, 0) for i in range(2)
    )
    grad_qkv = grad_qkv.reshape(2, rows_here, 3, own_width)
    grad_qkv = jnp.moveaxis(grad_qkv, 2, 0)
    odd = at_h % 2
    stays = pick(grad_qkv, odd + late, 0)
    core = group.swap(pick(grad_qkv, 1 - odd + late, 0), 1)
    chip = group.swap(pick(grad_qkv, 2 - 2 * late, 0), 2)
    grad_qkv = jnp.where(
        odd == 0, jnp.concatenate([stays, core, chip]), jnp.concatenate([chip, core, stays])
    )
    grad_qkv = wide(jnp.moveaxis(grad_qkv, 0, 1).reshape(rows_here, -1))

    return (
        result,
        grad_input,
        grad_qkv,
        grad_out,
        grad_in,
        grad_mlp,
        grad_gain1,
        grad_gain2,
    )


def local(tokens, cotangent, w_qkv, w_attn_out, w_in, w_mlp_out, norm_gain1, norm_gain2):
    args = (tokens, cotangent, w_qkv, w_attn_out, w_in, w_mlp_out, norm_gain1, norm_gain2)
    sizes = [lax.axis_size(axis) for axis in ("dp", "ctx", "head")]
    if sizes == [4, 2, 4] and tokens.shape[2] == 8 * 2 * HD and tokens.shape[1] % 16 == 0:
        return local_split(*args)
    return local_general(*args)


def solution(mesh):
    in_specs = (
        P("dp", ("ctx", "head"), None),
        P("dp", ("ctx", "head"), None),
        P(("dp", "ctx"), None),
        P(("dp", "ctx"), None),
        P(("dp", "ctx"), None),
        P(("dp", "ctx"), None),
        P(("dp", "ctx")),
        P(("dp", "ctx")),
    )
    out_specs = (
        P("dp", ("ctx", "head"), None),
        P("dp", ("ctx", "head"), None),
        P(("dp", "ctx"), "head"),
        P(("dp", "ctx"), "head"),
        P(("dp", "ctx"), "head"),
        P(("dp", "ctx"), "head"),
        P(("dp", "ctx", "head")),
        P(("dp", "ctx", "head")),
    )
    return jax.shard_map(local, mesh=mesh, in_specs=in_specs, out_specs=out_specs, check_vma=False)
```

```python
import functools
import math

import jax
import jax.numpy as jnp
from jax import lax
from jax.experimental import pallas as pl
from jax.experimental.pallas import tpu as pltpu
from jax.sharding import PartitionSpec as P

HD = 64


EPSILON = 1e-05
ROPE_BASE = 160000.0


def normalize(values):
    centre = jnp.mean(values, axis=-1, keepdims=True)
    shifted = values - centre
    spread = jnp.mean(shifted * shifted, axis=-1, keepdims=True)
    factor = lax.rsqrt(spread + EPSILON)
    return (shifted * factor, factor)


def norm_back(grad_normed, normed, factor):
    grad_centre = jnp.mean(grad_normed, axis=-1, keepdims=True)
    grad_along = jnp.mean(grad_normed * normed, axis=-1, keepdims=True)
    return (grad_normed - grad_centre - normed * grad_along) * factor


def rope_tables(positions, half_size):
    frequency = jnp.exp(
        jnp.arange(half_size, dtype=jnp.float32) * (-math.log(ROPE_BASE) / half_size)
    )
    angles = positions[:, None] * frequency[None, :]
    return (jnp.cos(angles), jnp.sin(angles))


def rotate(values, cosine, sine_table, direction):
    half_size = cosine.shape[-1]
    first_half = values[..., :half_size]
    second_half = values[..., half_size:]
    cos_part = cosine[:, None, :]
    sin_part = sine_table[:, None, :] * direction
    return jnp.concatenate(
        [
            first_half * cos_part - second_half * sin_part,
            second_half * cos_part + first_half * sin_part,
        ],
        axis=-1,
    )


def block_scores(queries4, keys_block, scale):
    keys4 = keys_block.reshape(
        keys_block.shape[0], keys_block.shape[1], queries4.shape[2], queries4.shape[3]
    )
    return (
        jnp.einsum("sqgd,skgd->sgqk", queries4, keys4, preferred_element_type=jnp.float32) * scale
    )


def attend_forward(queries4, keys_all, values_all, key_rows, scale):
    seqs_here, query_rows, groups, head_size = queries4.shape
    turns = keys_all.shape[1] // key_rows

    def statistics(turn, carry):
        row_peak, row_total = carry
        keys_block = lax.dynamic_slice_in_dim(keys_all, turn * key_rows, key_rows, 1)
        scores = block_scores(queries4, keys_block, scale)
        new_peak = jnp.maximum(row_peak, jnp.max(scores, axis=-1))
        row_total = row_total * jnp.exp(row_peak - new_peak) + jnp.sum(
            jnp.exp(scores - new_peak[..., None]), axis=-1
        )
        return (new_peak, row_total)

    start_peak = jnp.full((seqs_here, groups, query_rows), -1e30, jnp.float32)
    row_peak, row_total = lax.fori_loop(
        0, turns, statistics, (start_peak, jnp.zeros_like(start_peak))
    )
    log_total = row_peak + jnp.log(row_total)

    def accumulate(turn, running):
        keys_block = lax.dynamic_slice_in_dim(keys_all, turn * key_rows, key_rows, 1)
        values_block = lax.dynamic_slice_in_dim(values_all, turn * key_rows, key_rows, 1).reshape(
            seqs_here, key_rows, groups, head_size
        )
        weights = jnp.exp(block_scores(queries4, keys_block, scale) - log_total[..., None]).astype(
            jnp.bfloat16
        )
        return running + jnp.einsum(
            "sgqk,skgd->sqgd", weights, values_block, preferred_element_type=jnp.float32
        )

    attended = lax.fori_loop(
        0, turns, accumulate, jnp.zeros((seqs_here, query_rows, groups, head_size), jnp.float32)
    )
    return (attended, log_total)


def attend_backward(queries4, keys_all, values_all, grad_out4, log_total, along, key_rows, scale):
    seqs_here, query_rows, groups, head_size = queries4.shape
    length = keys_all.shape[1]
    width_group = groups * head_size
    turns = length // key_rows

    def step_back(turn, carry):
        grad_queries, grad_keys, grad_values = carry
        keys_block = lax.dynamic_slice_in_dim(keys_all, turn * key_rows, key_rows, 1)
        keys4 = keys_block.reshape(seqs_here, key_rows, groups, head_size)
        values4 = lax.dynamic_slice_in_dim(values_all, turn * key_rows, key_rows, 1).reshape(
            seqs_here, key_rows, groups, head_size
        )
        weights = jnp.exp(block_scores(queries4, keys_block, scale) - log_total[..., None])
        grad_weights = jnp.einsum(
            "sqgd,skgd->sgqk", grad_out4, values4, preferred_element_type=jnp.float32
        )
        grad_scores = (weights * (grad_weights - along[..., None])).astype(jnp.bfloat16)
        grad_queries = grad_queries + jnp.einsum(
            "sgqk,skgd->sqgd", grad_scores, keys4, preferred_element_type=jnp.float32
        )
        key_part = (
            jnp.einsum("sgqk,sqgd->skgd", grad_scores, queries4, preferred_element_type=jnp.float32)
            * scale
        )
        value_part = jnp.einsum(
            "sgqk,sqgd->skgd",
            weights.astype(jnp.bfloat16),
            grad_out4,
            preferred_element_type=jnp.float32,
        )
        grad_keys = lax.dynamic_update_slice_in_dim(
            grad_keys, key_part.reshape(seqs_here, key_rows, width_group), turn * key_rows, 1
        )
        grad_values = lax.dynamic_update_slice_in_dim(
            grad_values, value_part.reshape(seqs_here, key_rows, width_group), turn * key_rows, 1
        )
        return (grad_queries, grad_keys, grad_values)

    start = (
        jnp.zeros((seqs_here, query_rows, groups, head_size), jnp.float32),
        jnp.zeros((seqs_here, length, width_group), jnp.float32),
        jnp.zeros((seqs_here, length, width_group), jnp.float32),
    )
    grad_queries, grad_keys, grad_values = lax.fori_loop(0, turns, step_back, start)
    return (grad_queries * scale, grad_keys, grad_values)


def local_general(tokens, cotangent, w_qkv, w_attn_out, w_in, w_mlp_out, norm_gain1, norm_gain2):
    seqs_here, block_rows, width = tokens.shape
    count_rows = seqs_here * block_rows
    heads_all = width // HD
    head_devices = lax.axis_size("head")
    group_devices = lax.axis_size(("dp", "ctx"))
    groups = heads_all // head_devices
    width_group = groups * HD
    scale = HD ** (-0.5)
    ff_width = w_in.shape[1] // 2
    full_qkv, full_out, full_in, full_mlp, gain_one, gain_two = (
        lax.all_gather(w_qkv, ("dp", "ctx"), axis=0, tiled=True),
        lax.all_gather(w_attn_out, ("dp", "ctx"), axis=0, tiled=True),
        lax.all_gather(w_in, ("dp", "ctx"), axis=0, tiled=True),
        lax.all_gather(w_mlp_out, ("dp", "ctx"), axis=0, tiled=True),
        lax.all_gather(norm_gain1, ("dp", "ctx"), axis=0, tiled=True),
        lax.all_gather(norm_gain2, ("dp", "ctx"), axis=0, tiled=True),
    )
    x_in = tokens.astype(jnp.float32).reshape(count_rows, width)
    normed1, factor1 = normalize(x_in)
    lowered1 = (normed1 * gain_one.astype(jnp.float32)).astype(jnp.bfloat16)
    projected = jnp.dot(lowered1, full_qkv, preferred_element_type=jnp.float32).reshape(
        seqs_here, block_rows, 3, heads_all, HD
    )
    first_pos = (lax.axis_index("ctx") * head_devices + lax.axis_index("head")) * block_rows
    positions = (first_pos + jnp.arange(block_rows, dtype=jnp.int32)).astype(jnp.float32)
    cosine, sine_table = rope_tables(positions, HD // 2)
    queries = (
        rotate(projected[:, :, 0], cosine, sine_table, 1.0)
        .astype(jnp.bfloat16)
        .reshape(seqs_here, block_rows, width)
    )
    keys_local = (
        rotate(projected[:, :, 1], cosine, sine_table, 1.0)
        .astype(jnp.bfloat16)
        .reshape(seqs_here, block_rows, width)
    )
    values_local = projected[:, :, 2].astype(jnp.bfloat16).reshape(seqs_here, block_rows, width)
    queries_h, keys_h, values_h = (
        lax.all_to_all(queries, "head", split_axis=2, concat_axis=1, tiled=True),
        lax.all_to_all(keys_local, "head", split_axis=2, concat_axis=1, tiled=True),
        lax.all_to_all(values_local, "head", split_axis=2, concat_axis=1, tiled=True),
    )
    query_rows = queries_h.shape[1]
    queries4 = queries_h.reshape(seqs_here, query_rows, groups, HD)
    keys_all, values_all = (
        lax.all_gather(keys_h, "ctx", axis=1, tiled=True),
        lax.all_gather(values_h, "ctx", axis=1, tiled=True),
    )
    key_rows = math.gcd(keys_all.shape[1], 1024)
    attended, log_total = attend_forward(queries4, keys_all, values_all, key_rows, scale)
    attended_low = attended.astype(jnp.bfloat16).reshape(seqs_here, query_rows, width_group)
    back_rows = lax.all_to_all(
        attended_low, "head", split_axis=1, concat_axis=2, tiled=True
    ).reshape(count_rows, width)
    residual = x_in + jnp.dot(back_rows, full_out, preferred_element_type=jnp.float32)
    normed2, factor2 = normalize(residual)
    lowered2 = (normed2 * gain_two.astype(jnp.float32)).astype(jnp.bfloat16)
    lifted = jnp.dot(lowered2, full_in, preferred_element_type=jnp.float32)
    first_part = lifted[:, :ff_width]
    second_part = lifted[:, ff_width:]
    activated, gelu_pullback = jax.vjp(
        lambda entries: jax.nn.gelu(entries, approximate=False), first_part
    )
    mixed = (activated * second_part).astype(jnp.bfloat16)
    result = (residual + jnp.dot(mixed, full_mlp, preferred_element_type=jnp.float32)).astype(
        jnp.bfloat16
    )
    full_qkv, full_out, full_in, full_mlp, gain_one, gain_two = (
        lax.all_gather(w_qkv, ("dp", "ctx"), axis=0, tiled=True),
        lax.all_gather(w_attn_out, ("dp", "ctx"), axis=0, tiled=True),
        lax.all_gather(w_in, ("dp", "ctx"), axis=0, tiled=True),
        lax.all_gather(w_mlp_out, ("dp", "ctx"), axis=0, tiled=True),
        lax.all_gather(norm_gain1, ("dp", "ctx"), axis=0, tiled=True),
        lax.all_gather(norm_gain2, ("dp", "ctx"), axis=0, tiled=True),
    )
    keys_all, values_all = (
        lax.all_gather(keys_h, "ctx", axis=1, tiled=True),
        lax.all_gather(values_h, "ctx", axis=1, tiled=True),
    )
    grad_top = cotangent.reshape(count_rows, width)
    grad_mlp = jnp.einsum("nf,nd->fd", mixed, grad_top, preferred_element_type=jnp.float32)
    grad_mixed = jnp.einsum("nd,fd->nf", grad_top, full_mlp, preferred_element_type=jnp.float32)
    grad_first = gelu_pullback(grad_mixed * second_part)[0]
    grad_lifted = jnp.concatenate([grad_first, grad_mixed * activated], axis=-1).astype(
        jnp.bfloat16
    )
    grad_inner = jnp.einsum("nd,nf->df", lowered2, grad_lifted, preferred_element_type=jnp.float32)
    grad_lowered2 = jnp.einsum(
        "nf,df->nd", grad_lifted, full_in, preferred_element_type=jnp.float32
    )
    grad_two = jnp.sum(grad_lowered2 * normed2, axis=0)
    grad_residual = grad_top.astype(jnp.float32) + norm_back(
        grad_lowered2 * gain_two.astype(jnp.float32), normed2, factor2
    )
    grad_branch = grad_residual.astype(jnp.bfloat16)
    grad_outproj = jnp.einsum(
        "nd,ne->de", back_rows, grad_branch, preferred_element_type=jnp.float32
    )
    grad_attended = jnp.einsum(
        "ne,de->nd", grad_branch, full_out, preferred_element_type=jnp.float32
    ).astype(jnp.bfloat16)
    grad_attended_h = lax.all_to_all(
        grad_attended.reshape(seqs_here, block_rows, width),
        "head",
        split_axis=2,
        concat_axis=1,
        tiled=True,
    )
    grad_out4 = grad_attended_h.reshape(seqs_here, query_rows, groups, HD)
    along = jnp.transpose(jnp.sum(grad_out4.astype(jnp.float32) * attended, axis=-1), (0, 2, 1))
    grad_queries, grad_keys_all, grad_values_all = attend_backward(
        queries4, keys_all, values_all, grad_out4, log_total, along, key_rows, scale
    )
    grad_keys_sum, grad_values_sum = (
        lax.psum_scatter(
            grad_keys_all.astype(jnp.bfloat16), "ctx", scatter_dimension=1, tiled=True
        ).astype(jnp.float32),
        lax.psum_scatter(
            grad_values_all.astype(jnp.bfloat16), "ctx", scatter_dimension=1, tiled=True
        ).astype(jnp.float32),
    )
    grad_q_low = grad_queries.astype(jnp.bfloat16).reshape(seqs_here, query_rows, width_group)
    grad_q_tok, grad_k_tok, grad_v_tok = (
        lax.all_to_all(grad_q_low, "head", split_axis=1, concat_axis=2, tiled=True),
        lax.all_to_all(
            grad_keys_sum.astype(jnp.bfloat16), "head", split_axis=1, concat_axis=2, tiled=True
        ),
        lax.all_to_all(
            grad_values_sum.astype(jnp.bfloat16), "head", split_axis=1, concat_axis=2, tiled=True
        ),
    )
    unrot_q = rotate(
        grad_q_tok.astype(jnp.float32).reshape(seqs_here, block_rows, heads_all, HD),
        cosine,
        sine_table,
        -1.0,
    )
    unrot_k = rotate(
        grad_k_tok.astype(jnp.float32).reshape(seqs_here, block_rows, heads_all, HD),
        cosine,
        sine_table,
        -1.0,
    )
    grad_projected = jnp.concatenate(
        [
            unrot_q.reshape(count_rows, width),
            unrot_k.reshape(count_rows, width),
            grad_v_tok.astype(jnp.float32).reshape(count_rows, width),
        ],
        axis=-1,
    ).astype(jnp.bfloat16)
    grad_project = jnp.einsum(
        "nd,nf->df", lowered1, grad_projected, preferred_element_type=jnp.float32
    )
    grad_lowered1 = jnp.einsum(
        "nf,df->nd", grad_projected, full_qkv, preferred_element_type=jnp.float32
    )
    grad_one = jnp.sum(grad_lowered1 * normed1, axis=0)
    grad_input = grad_residual + norm_back(
        grad_lowered1 * gain_one.astype(jnp.float32), normed1, factor1
    )
    pieces_one = grad_one.reshape(group_devices, head_devices, -1)
    pieces_two = grad_two.reshape(group_devices, head_devices, -1)
    part_qkv, part_out, part_in, part_mlp, part_one, part_two = (
        lax.psum_scatter(
            grad_project.astype(jnp.bfloat16), ("dp", "ctx"), scatter_dimension=0, tiled=True
        ).astype(jnp.float32),
        lax.psum_scatter(
            grad_outproj.astype(jnp.bfloat16), ("dp", "ctx"), scatter_dimension=0, tiled=True
        ).astype(jnp.float32),
        lax.psum_scatter(
            grad_inner.astype(jnp.bfloat16), ("dp", "ctx"), scatter_dimension=0, tiled=True
        ).astype(jnp.float32),
        lax.psum_scatter(
            grad_mlp.astype(jnp.bfloat16), ("dp", "ctx"), scatter_dimension=0, tiled=True
        ).astype(jnp.float32),
        lax.psum_scatter(
            pieces_one.astype(jnp.bfloat16), ("dp", "ctx"), scatter_dimension=0, tiled=True
        ).astype(jnp.float32),
        lax.psum_scatter(
            pieces_two.astype(jnp.bfloat16), ("dp", "ctx"), scatter_dimension=0, tiled=True
        ).astype(jnp.float32),
    )
    final_qkv, final_out, final_in, final_mlp, final_one, final_two = (
        lax.psum_scatter(
            part_qkv.astype(jnp.bfloat16), "head", scatter_dimension=1, tiled=True
        ).astype(jnp.float32),
        lax.psum_scatter(
            part_out.astype(jnp.bfloat16), "head", scatter_dimension=1, tiled=True
        ).astype(jnp.float32),
        lax.psum_scatter(
            part_in.astype(jnp.bfloat16), "head", scatter_dimension=1, tiled=True
        ).astype(jnp.float32),
        lax.psum_scatter(
            part_mlp.astype(jnp.bfloat16), "head", scatter_dimension=1, tiled=True
        ).astype(jnp.float32),
        lax.psum_scatter(
            part_one.astype(jnp.bfloat16), "head", scatter_dimension=1, tiled=True
        ).astype(jnp.float32),
        lax.psum_scatter(
            part_two.astype(jnp.bfloat16), "head", scatter_dimension=1, tiled=True
        ).astype(jnp.float32),
    )
    return (
        result.reshape(seqs_here, block_rows, width),
        grad_input.reshape(seqs_here, block_rows, width),
        final_qkv,
        final_out,
        final_in,
        final_mlp,
        final_one.reshape(-1),
        final_two.reshape(-1),
    )


F32 = jnp.float32
BF16 = jnp.bfloat16
VMEM_BYTES = 56 * 1024 * 1024
GROUP = ("ctx", "head")


def dot(left, right, dims=((1,), (0,))):
    return lax.dot_general(left, right, (dims, ((), ())), preferred_element_type=F32)


def wide(values):
    return values.astype(F32)


def flat(values):
    return values.reshape(-1, values.shape[-1])


def lane_rotate(values, cosine, sine_signed):
    lane = lax.broadcasted_iota(jnp.int32, values.shape, 1)
    width = values.shape[1]
    partner = jnp.where(
        lane % HD < HD // 2,
        pltpu.roll(values, width - HD // 2, 1),
        pltpu.roll(values, HD // 2, 1),
    )
    return values * cosine + partner * sine_signed


def head_masks(shape):
    lane = lax.broadcasted_iota(jnp.int32, shape, 1)
    return [lane // HD == head for head in range(shape[1] // HD)]


def params():
    return pltpu.CompilerParams(vmem_limit_bytes=VMEM_BYTES)


COST = pl.CostEstimate(flops=1 << 20, transcendentals=0, bytes_accessed=1 << 16)


def whole(array):
    return pl.BlockSpec(array.shape, lambda *_: (0,) * len(array.shape))


SCALARS = pl.BlockSpec(memory_space=pltpu.SMEM)


def project_kernel(place_ref, *refs):
    pieces, weights = refs[:6], refs[6:10]
    cos_ref, sin_ref, low_ref, qkv_ref, w_ref, gain1_ref, gain2_ref, rows_ref = refs[10:]
    block, part = pieces[0].shape[2], w_ref.shape[1] // 3
    rows = gain1_ref.shape[1] // 8

    @pl.when(pl.program_id(0) == 0)
    def _():
        for step, piece in enumerate(weights):
            for turn in range(2):
                at = 2 * (place_ref[8] ^ step) + (place_ref[9] ^ turn)
                w_ref[pl.ds(pl.multiple_of(at * rows, rows), rows), :] = piece[turn, :rows]
                gains = piece[turn, rows:].astype(F32)
                rows_ref[0, pl.ds(at, 1), :] = gains[:1, :rows]
                rows_ref[1, pl.ds(at, 1), :] = gains[1:2, :rows]
        for out, at in ((gain1_ref, 0), (gain2_ref, 1)):
            for row in range(8):
                out[:, row * rows : (row + 1) * rows] = rows_ref[at, row : row + 1, :]

    gain = gain1_ref[...]
    index = 0
    for piece in pieces:
        for inner in range(piece.shape[0]):
            normed, _ = normalize(piece[inner, 0].astype(F32))
            low_ref[index, 0] = (normed * gain).astype(BF16)
            index += 1
    projected = dot(flat(low_ref[:, 0]), w_ref[...])
    cosine, sine = cos_ref[...], sin_ref[...]
    shape = (8, block, part)
    qkv_ref[:, 0, :, :part] = (
        (lane_rotate(projected[:, :part], cosine, sine) * HD**-0.5).astype(BF16).reshape(shape)
    )
    qkv_ref[:, 0, :, part : 2 * part] = (
        lane_rotate(projected[:, part : 2 * part], cosine, sine).astype(BF16).reshape(shape)
    )
    qkv_ref[:, 0, :, 2 * part :] = projected[:, 2 * part :].astype(BF16).reshape(shape)


def project(place, pieces, weights, cosine, sine):
    seqs, block, width = pieces[0].shape[1:]
    own = weights[0].shape[2]

    def by_seq(lead, last):
        return pl.BlockSpec((lead, 1, block, last), lambda s: (0, s, 0, 0))

    return pl.pallas_call(
        project_kernel,
        grid=(seqs,),
        in_specs=[SCALARS]
        + [by_seq(piece.shape[0], width) for piece in pieces]
        + [whole(w) for w in weights]
        + [whole(cosine), whole(sine)],
        out_specs=(
            by_seq(8, width),
            by_seq(8, own),
            pl.BlockSpec((width, own), lambda s: (0, 0)),
            pl.BlockSpec((1, width), lambda s: (0, 0)),
            pl.BlockSpec((1, width), lambda s: (0, 0)),
        ),
        out_shape=(
            jax.ShapeDtypeStruct((8, seqs, block, width), BF16),
            jax.ShapeDtypeStruct((8, seqs, block, own), BF16),
            jax.ShapeDtypeStruct((width, own), BF16),
            jax.ShapeDtypeStruct((1, width), F32),
            jax.ShapeDtypeStruct((1, width), F32),
        ),
        scratch_shapes=[pltpu.VMEM((2, 8, width // 8), F32)],
        compiler_params=params(),
        cost_estimate=COST,
        name="project",
    )(place, *pieces, *weights, cosine, sine)


def attend_kernel(place_ref, q_ref, k_ref, v_ref, *refs):
    att_ref, log_ref, home_ref = refs[-3:]
    step, seq = pl.program_id(0), len(refs) - 3
    if seq:

        @pl.when(step == 0)
        def _():
            home_ref[:, :1] = refs[0][...]

    queries, keys, values = flat(q_ref[...]), flat(k_ref[...]), flat(v_ref[...])
    attended = jnp.zeros(queries.shape, F32)
    logs = jnp.zeros(queries.shape, F32)
    for mask in head_masks(queries.shape):
        scores = dot(jnp.where(mask, queries, 0), keys, ((1,), (1,)))
        peak = jnp.max(scores, axis=1, keepdims=True)
        weights = jnp.exp(scores - peak)
        total = jnp.sum(weights, axis=1, keepdims=True)
        mixed = dot(weights.astype(BF16), values) * (1.0 / total)
        attended = jnp.where(mask, mixed, attended)
        logs = jnp.where(mask, peak + jnp.log(total), logs)
    att_ref[...] = attended.reshape(att_ref.shape)
    log_ref[...] = logs.reshape(log_ref.shape)
    low = attended.astype(BF16).reshape(att_ref.shape)
    for inner in range(2):
        home_ref[place_ref[2 * step + inner], seq] = low[inner, 0]


def attend(place, qkv, *home):
    _, _, block, own = qkv.shape
    part, seq = own // 3, len(home)
    rows = pl.BlockSpec((2, 1, block, part), lambda i: (i, 0, 0, 0))
    shape = (8, 1, block, part)
    return pl.pallas_call(
        attend_kernel,
        grid=(4,),
        in_specs=[
            SCALARS,
            pl.BlockSpec((2, 1, block, part), lambda i: (i, seq, 0, 0)),
            pl.BlockSpec((8, 1, block, part), lambda i: (0, seq, 0, 1)),
            pl.BlockSpec((8, 1, block, part), lambda i: (0, seq, 0, 2)),
            *[whole(h) for h in home],
        ],
        out_specs=(
            rows,
            rows,
            pl.BlockSpec((8, 1 + seq, block, part), lambda i: (0, 0, 0, 0)),
        ),
        out_shape=(
            jax.ShapeDtypeStruct(shape, F32),
            jax.ShapeDtypeStruct(shape, F32),
            jax.ShapeDtypeStruct((8, 1 + seq, block, part), BF16),
        ),
        compiler_params=params(),
        cost_estimate=COST,
        name="attend",
    )(place, qkv, qkv, qkv, *home)


def branch_kernel(place_ref, *refs):
    pieces = refs[:6]
    rows_ref, tokens_ref, gain_ref, residual_ref, low_ref, side_ref, total_ref = refs[6:]
    heads = rows_ref.shape[0] // 2
    for c in range(2):
        side_ref[c] = jnp.concatenate([flat(rows_ref[c * heads + d]) for d in range(heads)], axis=1)
    total_ref[...] = flat(wide(tokens_ref[...]))
    index = 0
    for piece in pieces:
        n = piece.shape[2]
        for inner in range(piece.shape[0]):
            at = place_ref[index]
            columns = pl.ds(pl.multiple_of((at % heads) * n, n), n)
            total_ref[:, columns] += dot(side_ref[at // heads], piece[inner])
            index += 1
    total = total_ref[...]
    normed, _ = normalize(total)
    residual_ref[...] = total.reshape(residual_ref.shape)
    low_ref[...] = (normed * gain_ref[...]).astype(BF16).reshape(low_ref.shape)


def branch(place, pieces, rows, tokens, gain):
    args = (*pieces, rows, tokens, gain)
    seqs, block, width = tokens.shape
    return pl.pallas_call(
        branch_kernel,
        in_specs=[SCALARS] + [whole(a) for a in args],
        out_shape=(
            jax.ShapeDtypeStruct(tokens.shape, F32),
            jax.ShapeDtypeStruct(tokens.shape, BF16),
        ),
        scratch_shapes=[
            pltpu.VMEM((2, seqs * block, pieces[0].shape[1]), BF16),
            pltpu.VMEM((seqs * block, width), F32),
        ],
        compiler_params=params(),
        cost_estimate=COST,
        name="branch",
    )(place, *args)


def combine(*groups):
    parts = [part for group in groups for _, parts in group for part in parts]
    rows = sum(count for count, _ in groups[0])
    width = parts[0][0].shape[2]

    def kernel(*refs):
        at = 0
        for k, group in enumerate(groups):
            row = 0
            for count, terms in group:
                total = 0.0
                for _, _, start in terms:
                    total = total + wide(refs[at][0, start : start + count])
                    at += 1
                refs[-1][k, row : row + count] = total.astype(BF16)
                row += count

    return pl.pallas_call(
        kernel,
        grid=(1,),
        in_specs=[
            pl.BlockSpec((1, *array.shape[1:]), lambda *_, index=index: (index, 0, 0))
            for array, index, _ in parts
        ],
        out_specs=pl.BlockSpec((len(groups), rows, width), lambda *_: (0, 0, 0)),
        out_shape=jax.ShapeDtypeStruct((len(groups), rows, width), BF16),
        compiler_params=params(),
        cost_estimate=COST,
        name="combine",
    )(*[array for array, _, _ in parts])


def mlp_kernel(*refs, count, ends):
    pieces, tops = refs[:count], refs[count : 2 * count]
    w_ref, out_w_ref = refs[2 * count : 2 * count + 2]
    low_ref, top_ref, mixed_ref, lifted_ref, *out_refs = refs[-4 - len(ends) :]
    step = pl.program_id(0)
    start = 0
    for piece, top in zip(pieces, tops):

        @pl.when((step >= start) & (step < start + piece.shape[0]))
        def _(piece=piece, top=top, start=start):
            low_ref[0] = piece[step - start]
            top_ref[0] = top[step - start]

        start += piece.shape[0]

    hidden = w_ref.shape[1] // 2
    lifted = dot(flat(low_ref[...]), w_ref[...])
    first, second = lifted[:, :hidden], lifted[:, hidden:]
    grad_mixed = dot(flat(top_ref[...]), out_w_ref[...], ((1,), (1,)))
    gate = 0.5 * (1.0 + lax.erf(first * (0.5**0.5)))
    slope = gate + first * jnp.exp(first * first * -0.5) * ((2.0 * math.pi) ** -0.5)
    activated = first * gate
    mixed_ref[...] = (activated * second).astype(BF16).reshape(mixed_ref.shape)
    grad = jnp.concatenate(
        [(grad_mixed * second * slope).astype(BF16), (grad_mixed * activated).astype(BF16)],
        axis=1,
    )
    lifted_ref[...] = grad.reshape(lifted_ref.shape)
    partial = dot(grad, w_ref[...], ((1,), (1,))).astype(BF16).reshape(low_ref.shape)
    start = 0
    for out, end in zip(out_refs, ends):

        @pl.when((step >= start) & (step < end))
        def _(out=out):
            out[...] = partial

        start = end


def mlp(pieces, tops, w, out_w, base, ends, earlier=()):
    seqs, block, width = pieces[0].shape[1:]
    hidden = w.shape[1] // 2
    whole_in = (*pieces, *tops, w, out_w)

    def rows(last):
        return pl.BlockSpec((1, seqs, block, last), lambda i: (i + base, 0, 0, 0))

    def within(start, end):
        return pl.BlockSpec(
            (1, seqs, block, width),
            lambda i: (jnp.clip(i - start, 0, end - start - 1), 0, 0, 0),
        )

    starts = (0, *ends[:-1])
    lasts = (width, width, hidden, 2 * hidden)
    return pl.pallas_call(
        functools.partial(mlp_kernel, count=len(pieces), ends=ends),
        grid=(ends[-1],),
        in_specs=[whole(array) for array in whole_in]
        + [pl.BlockSpec(memory_space=pl.ANY)] * len(earlier),
        out_specs=(
            *[rows(last) for last in lasts],
            *[within(start, end) for start, end in zip(starts, ends)],
        ),
        out_shape=(
            *[jax.ShapeDtypeStruct((8, seqs, block, last), BF16) for last in lasts],
            *[
                jax.ShapeDtypeStruct((end - start, seqs, block, width), BF16)
                for start, end in zip(starts, ends)
            ],
        ),
        input_output_aliases={len(whole_in) + at: at for at in range(len(earlier))},
        compiler_params=params(),
        cost_estimate=COST,
        name="mlp",
    )(*whole_in, *earlier)


def out_grad_kernel(place_ref, rows_ref, grad_ref, keep_ref, send_ref):
    grads = flat(grad_ref[...])
    for index in range(8):
        part = dot(flat(rows_ref[place_ref[index]]), grads, ((0,), (0,))).astype(BF16)
        if index < 5:
            keep_ref[index] = part
        else:
            send_ref[index - 5] = part


def out_grad(place, rows, grads):
    part, width = rows.shape[-1], grads.shape[-1]
    return pl.pallas_call(
        out_grad_kernel,
        in_specs=[SCALARS, whole(rows), whole(grads)],
        out_shape=(
            jax.ShapeDtypeStruct((5, part, width), BF16),
            jax.ShapeDtypeStruct((3, part, width), BF16),
        ),
        compiler_params=params(),
        cost_estimate=COST,
        name="out_grad",
    )(place, rows, grads)


def branch_back_kernel(place_ref, *refs):
    pieces = refs[:6]
    keep_ref, near_ref, own_ref, residual_ref, top_ref, gain_ref = refs[6:12]
    grad_ref, branch_ref, home_ref, sum_ref, low_ref, side_ref = refs[12:]
    grad_low = wide(flat(keep_ref[...])) + wide(flat(near_ref[...])) + wide(flat(own_ref[...]))
    normed, factor = normalize(flat(residual_ref[...]))
    sum_ref[...] = jnp.sum(grad_low * normed, axis=0, keepdims=True)
    grad = flat(wide(top_ref[...])) + norm_back(grad_low * gain_ref[...], normed, factor)
    grad_ref[...] = grad.reshape(grad_ref.shape)
    low_ref[...] = grad.astype(BF16)
    branch_ref[...] = low_ref[...].reshape(branch_ref.shape)
    heads = home_ref.shape[0] // 2
    side_ref[...] = jnp.zeros_like(side_ref)
    index = 0
    for piece in pieces:
        n = piece.shape[2]
        for inner in range(piece.shape[0]):
            at = place_ref[index]
            columns = pl.ds(pl.multiple_of((at % heads) * n, n), n)
            side_ref[at // heads] += dot(low_ref[:, columns], piece[inner], ((1,), (1,)))
            index += 1
    part = home_ref.shape[3]
    for c in range(2):
        for d in range(heads):
            home = side_ref[c, :, d * part : (d + 1) * part].astype(BF16)
            home_ref[c * heads + d] = home.reshape(home_ref.shape[1:])


def branch_back(place, pieces, keep, near, own, residual, top, gain):
    args = (*pieces, keep, near, own, residual, top, gain)
    seqs, block, width = residual.shape
    tall = pieces[0].shape[1]
    shapes = (
        jax.ShapeDtypeStruct(residual.shape, F32),
        jax.ShapeDtypeStruct(residual.shape, BF16),
        jax.ShapeDtypeStruct((8, seqs, block, tall // 4), BF16),
        jax.ShapeDtypeStruct((1, width), F32),
    )
    return pl.pallas_call(
        branch_back_kernel,
        grid=(1,),
        in_specs=[SCALARS]
        + [whole(piece) for piece in pieces]
        + [pl.BlockSpec((1, seqs * block, width), lambda *_: (0, 0, 0))] * 2
        + [whole(a) for a in args[8:]],
        out_specs=tuple(whole(shape) for shape in shapes),
        out_shape=shapes,
        scratch_shapes=[
            pltpu.VMEM((seqs * block, width), BF16),
            pltpu.VMEM((2, seqs * block, tall), F32),
        ],
        compiler_params=params(),
        cost_estimate=COST,
        name="branch_back",
    )(place, *args)


def attend_back_kernel(
    place_ref, q_ref, k_ref, v_ref, grad_ref, att_ref, log_ref, cosq_ref, sinq_ref, cos_ref,
    sin_ref, w_ref, low_ref, *refs, seq, last,
):
    if last:
        before_ref, gain1_ref, gain2_ref, keep_ref, send_ref, grad_w_ref, *scratch = refs
    else:
        keep_ref, send_ref, before_ref, *scratch = refs
    proj_ref, sum_k, sum_v = scratch
    step = pl.program_id(0)
    block, part = q_ref.shape[2], q_ref.shape[3]

    @pl.when(step == 0)
    def _():
        sum_k[...] = jnp.zeros_like(sum_k)
        sum_v[...] = jnp.zeros_like(sum_v)

    queries, keys, values = flat(q_ref[...]), flat(k_ref[...]), flat(v_ref[...])
    grads = jnp.concatenate([grad_ref[place_ref[2 * step + inner], seq] for inner in range(2)])
    along = (grads.astype(F32) * flat(att_ref[...])).T
    logs = flat(log_ref[...]).T
    grad_queries = jnp.zeros(queries.shape, F32)
    for head, mask in enumerate(head_masks(queries.shape)):
        own_q = jnp.where(mask, queries, 0)
        own_g = jnp.where(mask, grads, 0)
        scores = dot(keys, own_q, ((1,), (1,)))
        weights = jnp.exp(scores - logs[head * HD : head * HD + 1])
        lifted = dot(values, own_g, ((1,), (1,)))
        row = jnp.sum(along[head * HD : (head + 1) * HD], axis=0, keepdims=True)
        grad_scores = (weights * (lifted - row)).astype(BF16)
        sum_k[...] += dot(grad_scores, own_q)
        sum_v[...] += dot(weights.astype(BF16), own_g)
        grad_queries = jnp.where(mask, dot(grad_scores, keys, ((0,), (0,))), grad_queries)
    grad_queries = lane_rotate(grad_queries * HD**-0.5, cosq_ref[...], -sinq_ref[...])
    rows = pl.multiple_of(step * 2 * block, 2 * block)
    proj_ref[pl.ds(rows, 2 * block), :part] = grad_queries.astype(BF16)

    @pl.when(step == 3)
    def _():
        grad_keys = lane_rotate(sum_k[...], cos_ref[...], -sin_ref[...])
        proj_ref[:, part : 2 * part] = grad_keys.astype(BF16)
        proj_ref[:, 2 * part :] = sum_v[...].astype(BF16)
        partial = dot(proj_ref[...], w_ref[...], ((1,), (1,))).astype(BF16)
        keep_ref[...] = partial[: 5 * block].reshape(5, block, -1)
        send_ref[...] = partial[5 * block :].reshape(3, block, -1)
        grad_w = dot(proj_ref[...], flat(low_ref[...]), ((0,), (0,)))
        if last:
            grad_w = (grad_w + before_ref[...]).T
            along_w = jnp.sum(grad_w * wide(w_ref[...]), axis=1, keepdims=True)
            along_w = jnp.broadcast_to(along_w, (w_ref.shape[0], 128)).T[:1] / gain1_ref[...]
            row = lax.broadcasted_iota(jnp.int32, (GAIN_ROWS, w_ref.shape[0]), 0)
            gains = jnp.where(row == 0, along_w, jnp.where(row == 1, gain2_ref[...], 0.0))
            n = grad_w_ref.shape[1] - GAIN_ROWS
            for at in range(grad_w_ref.shape[0]):
                part_rows = slice(at * n, (at + 1) * n)
                grad_w_ref[at, :n] = grad_w[part_rows].astype(BF16)
                grad_w_ref[at, n:, :n] = gains[:, part_rows].astype(BF16)
                rest = grad_w_ref.shape[2] - n
                grad_w_ref[at, n:, n:] = jnp.zeros((GAIN_ROWS, rest), BF16)
        else:
            before_ref[...] = grad_w


GAIN_ROWS = 16


def attend_back(place, qkv, grads, attended, logs, cosine, sine, w, low, seq, *before, dp=1):
    _, _, block, own = qkv.shape
    part, width = own // 3, w.shape[0]
    last = len(before) > 0
    rows = pl.BlockSpec((2, 1, block, part), lambda i: (i, 0, 0, 0))
    angles = pl.BlockSpec((2 * block, part), lambda i: (i, 0))

    def full(*shape):
        return pl.BlockSpec(shape, lambda i: (0,) * len(shape))

    args = [place, qkv, qkv, qkv, grads, attended, logs, cosine, sine, cosine, sine, w, low]
    in_specs = [
        SCALARS,
        pl.BlockSpec((2, 1, block, part), lambda i: (i, seq, 0, 0)),
        pl.BlockSpec((8, 1, block, part), lambda i: (0, seq, 0, 1)),
        pl.BlockSpec((8, 1, block, part), lambda i: (0, seq, 0, 2)),
        whole(grads),
        rows,
        rows,
        angles,
        angles,
        whole(cosine),
        whole(sine),
        whole(w),
        pl.BlockSpec((8, 1, block, width), lambda i: (0, seq, 0, 0)),
    ]
    shapes = [((5, block, width), BF16), ((3, block, width), BF16)]
    if last:
        args += before
        in_specs += [whole(array) for array in before]
        shapes += [((dp, width // dp + GAIN_ROWS, own), BF16)]
    else:
        shapes += [((own, width), F32)]
    return pl.pallas_call(
        functools.partial(attend_back_kernel, seq=seq, last=last),
        grid=(4,),
        in_specs=in_specs,
        out_specs=tuple(full(*shape) for shape, _ in shapes),
        out_shape=tuple(jax.ShapeDtypeStruct(shape, kind) for shape, kind in shapes),
        scratch_shapes=[
            pltpu.VMEM((8 * block, own), BF16),
            pltpu.VMEM((8 * block, part), F32),
            pltpu.VMEM((8 * block, part), F32),
        ],
        compiler_params=params(),
        cost_estimate=COST,
        name="attend_back",
    )(*args)


def input_grad_kernel(*refs):
    keeps, (near_ref, own_ref, tokens_ref, residual_ref, gain_ref, out_ref) = refs[:-6], refs[-6:]
    block = tokens_ref.shape[1]
    for seq, keep in enumerate(keeps):
        rows = slice(seq * block, (seq + 1) * block)
        grad = wide(keep[0, :block]) + wide(near_ref[0, rows]) + wide(own_ref[0, rows])
        normed, factor = normalize(wide(tokens_ref[seq]))
        out_ref[seq] = residual_ref[seq] + norm_back(grad * gain_ref[...], normed, factor)


def input_grad(keeps, near, own, tokens, residual, gain):
    rest = (own, tokens, residual, gain)
    return pl.pallas_call(
        input_grad_kernel,
        grid=(1,),
        in_specs=[
            pl.BlockSpec((1, *array.shape[1:]), lambda *_: (0, 0, 0)) for array in (*keeps, near)
        ]
        + [whole(array) for array in rest],
        out_specs=whole(residual),
        out_shape=jax.ShapeDtypeStruct(residual.shape, F32),
        compiler_params=params(),
        cost_estimate=COST,
        name="input_grad",
    )(*keeps, near, *rest)


class Group:
    def __init__(self):
        self.heads = lax.axis_size("head")
        self.dp = lax.axis_size("dp")
        self.ctx_at = lax.axis_index("ctx")
        self.head_at = lax.axis_index("head")
        self.dp_at = lax.axis_index("dp")
        self.at = self.ctx_at * self.heads + self.head_at
        near, far = [], []
        for c in range(2):
            for h in range(self.heads):
                x, y = (c ^ 1) * self.heads + h, c * self.heads + (h ^ 2)
                near.append((c * self.heads + h, x if h % 2 == 0 else y))
                far.append((c * self.heads + h, y if h % 2 == 0 else x))
        self.near, self.far = near, far

    def order(self):
        first = jnp.where(self.head_at % 2 == 0, 4, 2)
        second = 6 - first
        return jnp.stack(
            [self.at ^ bits for bits in (0, 1, first, first ^ 1, 6, second ^ 1, second, 7)]
        )

    def swap(self, values, bit):
        if bit == 4:
            return lax.ppermute(values, "ctx", [(0, 1), (1, 0)])
        return lax.ppermute(values, "head", [(i, i ^ bit) for i in range(self.heads)])

    def mate(self, values):
        return self.swap(values, 1)

    def to_near(self, values):
        return lax.ppermute(values, GROUP, self.near)

    def to_far(self, values):
        return lax.ppermute(values, GROUP, self.far)

    def rows_back(self, values, place):
        pairs, same = [], False
        for d in range(self.dp):
            for h in range(self.heads):
                if (d, h) == (place[h], d):
                    same = same | ((self.dp_at == d) & (self.head_at == h))
                else:
                    pairs.append((d * self.heads + h, place[h] * self.heads + d))
        return jnp.where(same, values, lax.ppermute(values, ("dp", "head"), pairs))

    def across(self, values, step):
        return lax.ppermute(values, "dp", [(i, i ^ step) for i in range(self.dp)])


def pick(array, index, axis):
    return lax.dynamic_index_in_dim(array, index, axis, keepdims=False)


def after(values, *earlier):
    return lax.optimization_barrier((values, earlier))[0]


def local_split(tokens, cotangent, w_qkv, w_attn_out, w_in, w_mlp_out, norm_gain1, norm_gain2):
    seqs, block, width = tokens.shape
    group = Group()
    heads, dp = group.heads, group.dp
    at_c, at_h = group.ctx_at, group.head_at
    parts = 2 * heads
    hidden = w_in.shape[1] // 2 // parts
    padded = -(-hidden // 128) * 128
    own_width = width // parts
    half = heads // 2
    rows_here = w_qkv.shape[0]
    place = [2 * (h % half) + h // half for h in range(heads)]
    straight = list(range(heads))
    order = group.order()
    scalars = jnp.concatenate([order, jnp.stack([group.dp_at, at_c])]).astype(jnp.int32)
    mate, near, far = group.mate, group.to_near, group.to_far

    def in_order(own, other):
        return jnp.where(at_c == 0, jnp.stack([own, other]), jnp.stack([other, own]))

    def exchange(values):
        return lax.all_to_all(values, GROUP, split_axis=0, concat_axis=0, tiled=True)


    gains = jnp.pad(
        jnp.stack([norm_gain1, norm_gain2]), ((0, 14), (0, 3 * own_width - rows_here))
    )
    qkv_view = w_qkv.reshape(rows_here, 3, width)

    def qkv_part(at):
        start = (2 * at_h + at) * own_width
        cut = lax.dynamic_slice_in_dim(qkv_view, start, own_width, 2)
        return jnp.concatenate([cut.reshape(rows_here, 3 * own_width), gains])

    x_own = tokens[None]
    x_mate = mate(x_own)
    qkv_other, qkv_own = qkv_part(1 - at_c), qkv_part(at_c)
    qkv_cross = group.swap(after(qkv_other, x_own), 4)
    in_view = after(w_in, qkv_other).reshape(rows_here, 2, heads, 2, hidden)
    in_view = pick(in_view, 2 * (at_h % half) + at_h // half, 2)

    def in_part(at):
        cut = pick(in_view, at, 2)
        return jnp.pad(cut, ((0, 0), (0, 0), (0, padded - hidden))).reshape(rows_here, 2 * padded)

    in_other, in_own = in_part(1 - at_c), in_part(at_c)
    in_cross = group.swap(in_other, 4)
    x_chip = jnp.concatenate([x_own, after(x_mate, qkv_cross, qkv_own, in_cross, in_own)])
    x_near = near(x_chip)
    qkv_pair = jnp.stack([qkv_own, qkv_cross])
    qkv_pieces = [qkv_pair] + [group.across(qkv_pair, step) for step in range(1, dp)]

    slices = jnp.concatenate([w_attn_out, w_mlp_out])
    slices = after(slices, qkv_pair)
    slices = lax.dynamic_slice_in_dim(slices, at_h * (width // heads), width // heads, 1)
    slices = jnp.pad(slices, ((0, 64), (0, 0)))
    slices = lax.all_gather(slices, "dp", axis=0)
    positions = after(order, qkv_pair)[:, None] * block + jnp.arange(block, dtype=jnp.int32)
    lane = jnp.arange(own_width, dtype=jnp.int32)
    frequency = jnp.exp(
        (lane % (HD // 2)).astype(F32) * (-math.log(ROPE_BASE) / (HD // 2))
    )
    angles = wide(positions.reshape(-1))[:, None] * frequency[None, :]
    cosine = jnp.cos(angles)
    sine = jnp.sin(angles) * jnp.where(lane % HD < HD // 2, -1.0, 1.0)[None, :]

    x_far = far(x_near[:1])
    x_near, in_pair = lax.optimization_barrier(
        (after(x_near, *qkv_pieces, cosine, sine), in_order(in_own, in_cross))
    )
    weight_in = lax.all_gather(in_pair, "dp", axis=0).reshape(width, -1)
    x_near_mate = mate(x_near)
    cot_own = after(cotangent, x_near)[None]
    cot_mate = mate(cot_own)
    x_far = after(x_far, cot_mate)
    x_far_mate = mate(x_far)

    cot_chip = jnp.concatenate([cot_own, cot_mate])
    cot_near = near(after(cot_chip, x_far))
    out_rows = w_attn_out.shape[0]
    x_pieces = (x_own, x_mate, x_near, x_far, x_near_mate, after(x_far_mate, cot_chip))
    low1, qkv, weight_qkv, gain_one, gain_two = project(
        scalars, x_pieces, qkv_pieces, cosine, sine
    )

    slices = after(slices, qkv)
    out_own = slices[:, :out_rows].reshape(1, dp * out_rows, -1)
    out_mate = mate(out_own)
    mlp_slices = jnp.stack(
        [slices[place[h], out_rows : out_rows + hidden] for h in range(heads)]
    )
    mlp_slices = lax.all_to_all(mlp_slices, "head", split_axis=0, concat_axis=0, tiled=True)
    out_near = near(jnp.concatenate([out_own, out_mate]))
    att_0, log_0, home_0 = attend(scalars, after(qkv, out_mate))
    cot_near = after(cot_near, home_0)
    cot_far, cot_near_mate = far(cot_near[:1]), mate(cot_near)
    out_near = after(out_near, home_0)
    out_far, out_near_mate = far(out_near[:1]), mate(out_near)
    att_1, log_1, home = attend(scalars, after(qkv, cot_near, out_near), home_0)
    att_rows = exchange(home)
    out_far_mate, cot_far_mate = mate(after(out_far, home)), mate(after(cot_far, home))
    out_pieces = (out_own, out_mate, out_near, out_far, out_near_mate, out_far_mate)
    weight_mlp = jnp.moveaxis(after(mlp_slices, home), 0, 1).reshape(hidden, width)
    weight_mlp = jnp.pad(weight_mlp, ((0, padded - hidden), (0, 0)))
    residual, low2 = branch(
        scalars, out_pieces, after(att_rows, cot_far_mate, weight_mlp, weight_in), tokens, gain_two
    )

    low_own = low2[None]
    low_mate = mate(low_own)
    low_near = near(jnp.concatenate([low_own, low_mate]))
    *arrays, keep_a = mlp(
        (low_own, low_mate), (cot_own, cot_mate), weight_in, weight_mlp, 0, (2,)
    )
    low_near = after(low_near, keep_a)
    low_far, low_near_mate = far(low_near[:1]), mate(low_near)
    *arrays, keep_b = mlp((low_near,), (cot_near,), weight_in, weight_mlp, 2, (2,), arrays)
    low_far_mate = mate(after(low_far, keep_b))
    low2_all, cot_all, mixed, grad_lifted, keep_c, send = mlp(
        (low_far, low_near_mate, low_far_mate),
        (cot_far, cot_near_mate, cot_far_mate),
        weight_in,
        weight_mlp,
        4,
        (1, 4),
        arrays,
    )

    def over_tokens(left, right):
        return dot(flat(left), flat(right), ((0,), (0,)))

    def scatter(values):
        return lax.psum_scatter(values.astype(BF16), "dp", scatter_dimension=0, tiled=True)

    def columns_first(values):
        return jnp.moveaxis(values.reshape(values.shape[0], dp, -1), 1, 0)

    rows = seqs * block

    def by_rows(values):
        return values.reshape(values.shape[0], -1, width)

    keep_a, keep_b, keep_c, send = (by_rows(array) for array in (keep_a, keep_b, keep_c, send))
    met = mate(send)
    last = combine([(rows, [(keep_c, 0, 0), (met, 2, 0)])])
    last_far = far(last)
    grad_mlp = columns_first(over_tokens(after(mixed, last), cot_all)[:hidden]).astype(BF16)
    last_far = after(last_far, grad_mlp)
    grad_mlp = scatter(grad_mlp)[0]
    chip = combine(
        [(rows, [(keep_b, 0, 0), (met, 0, 0), (last_far, 0, 0)])],
        [(rows, [(keep_b, 1, 0), (met, 1, 0)])],
    )
    chip_near = near(chip)
    grad_in = over_tokens(low2_all, after(grad_lifted, chip)).astype(BF16)
    cut = 5 * rows
    mixed_flat = flat(after(mixed, chip))
    out_keep = dot(mixed_flat[:cut], weight_mlp).astype(BF16).reshape(5, rows, width)
    out_send = dot(mixed_flat[cut:], weight_mlp).astype(BF16).reshape(3, rows, width)
    chip_near = after(chip_near, grad_in, out_keep, out_send)
    grad_in = scatter(grad_in)
    home = mate(combine([(rows, [(keep_a, 1, 0), (chip_near, 1, 0)])])[0])
    out_met = mate(after(out_send, chip_near))
    grad_residual, grad_branch, home, gain2_sum = branch_back(
        scalars, out_pieces, keep_a, chip_near, after(home, grad_mlp), residual, cotangent, gain_two
    )
    grad_home = exchange(home)

    rows_keep, rows_send = out_grad(scalars, after(att_rows, home), grad_branch)
    rows_met = mate(rows_send)
    few = rows_keep.shape[1]

    def ends(index, at, *more):
        kept = [(out_keep, index, 0)], [(rows_keep, index, 0)]
        if at is not None:
            kept[0].append((out_met, at, 0))
            kept[1].append((rows_met, at, 0))
        for array, where in more:
            kept[0].append((array, where, 0))
            kept[1].append((array, where, rows))
        return [(rows, kept[0]), (few, kept[1])]

    end_last = combine(ends(4, 2))
    grad_home = after(grad_home, end_last)
    end_far = far(after(end_last, grad_home))
    keep_0, send_0, before = attend_back(
        scalars, qkv, grad_home, att_0, log_0, cosine, sine, weight_qkv, low1, 0
    )
    met_0 = mate(send_0)
    end_far, grad_in = lax.optimization_barrier((after(end_far, send_0), grad_in))
    in_parts = grad_in.reshape(2, rows_here, -1)
    in_cross = group.swap(pick(in_parts, 1 - at_c, 0), 4)
    end_chip = combine(ends(2, 0, (end_far, 0)), ends(3, 1))
    end_near = near(after(end_chip, in_cross))
    keep_1, send_1, grad_qkv = attend_back(
        scalars, qkv, after(grad_home, end_chip), att_1, log_1, cosine, sine,
        weight_qkv, low1, 1, before, gain_one, gain2_sum, dp=dp,
    )

    grad_qkv = scatter(grad_qkv.reshape(-1, grad_qkv.shape[2]))
    met_1 = mate(send_1)

    def both(index, at, *more):
        kept = [(keep_0, index, 0)], [(keep_1, index, 0)]
        if at is not None:
            kept[0].append((met_0, at, 0))
            kept[1].append((met_1, at, 0))
        for array, where in more:
            kept[0].append((array, where, 0))
            kept[1].append((array, where, block))
        return [(block, kept[0]), (block, kept[1])]

    last = combine(both(4, 2))
    last_far = far(last)
    end_home = mate(combine(ends(1, None, (after(end_near, last), 1))))
    grad_in = in_order(after(pick(in_parts, at_c, 0), last), in_cross)
    late = at_h // half
    grad_in = jnp.stack([grad_in[..., :hidden], grad_in[..., padded : padded + hidden]])
    last_far = after(last_far, grad_in, end_home)
    chip = combine(both(2, 0, (last_far, 0)), both(3, 1))
    chip_near = near(chip)

    end_home = after(end_home, chip)
    grad_out = wide(rows_keep[0]) + wide(end_near[0, rows:]) + wide(end_home[0, rows:])
    grad_out = scatter(columns_first(grad_out.astype(BF16)))[0]
    result = wide(out_keep[0]) + wide(end_near[0, :rows]) + wide(end_home[0, :rows])
    result = (residual + result.reshape(residual.shape)).astype(BF16)
    grad_in = after(grad_in, chip)
    stays = pick(grad_in, late, 0)
    comes = group.swap(pick(grad_in, 1 - late, 0), half)
    grad_mlp = group.rows_back(after(grad_mlp, chip), place)
    grad_qkv = after(grad_qkv, chip)
    both_rows = 2 * rows_here
    qkv_parts = grad_qkv[:both_rows].reshape(2, rows_here, -1)
    gains = grad_qkv[both_rows:]
    cross = jnp.concatenate([pick(qkv_parts, 1 - at_c, 0), gains])
    cross = group.swap(cross, 4)
    chip_near = after(chip_near, comes, result, cross, grad_mlp)
    home = mate(combine(both(1, None, (chip_near, 1))))
    cross = after(cross, chip_near)
    grad_qkv = in_order(pick(qkv_parts, at_c, 0), cross[:rows_here])
    gains = (wide(gains) + wide(cross[rows_here:])).astype(BF16)
    gains = wide(gains) + sum(wide(group.swap(gains, bit)) for bit in range(1, heads))
    grad_out = wide(group.rows_back(grad_out, straight))
    grad_input = input_grad((keep_0, keep_1), chip_near, home, tokens, grad_residual, gain_one)

    grad_mlp = wide(grad_mlp)
    grad_in = jnp.where(
        late == 0, jnp.concatenate([stays, comes]), jnp.concatenate([comes, stays])
    )
    grad_in = wide(jnp.moveaxis(grad_in, 0, 1).reshape(rows_here, -1))

    per_device = width // (dp * parts)
    start = group.at * per_device
    grad_gain1, grad_gain2 = (
        lax.dynamic_slice_in_dim(gains[i], start, per_device, 0) for i in range(2)
    )
    grad_qkv = grad_qkv.reshape(2, rows_here, 3, own_width)
    grad_qkv = jnp.moveaxis(grad_qkv, 2, 0)
    odd = at_h % 2
    stays = pick(grad_qkv, odd + late, 0)
    core = group.swap(pick(grad_qkv, 1 - odd + late, 0), 1)
    chip = group.swap(pick(grad_qkv, 2 - 2 * late, 0), 2)
    grad_qkv = jnp.where(
        odd == 0, jnp.concatenate([stays, core, chip]), jnp.concatenate([chip, core, stays])
    )
    grad_qkv = wide(jnp.moveaxis(grad_qkv, 0, 1).reshape(rows_here, -1))

    return (
        result,
        grad_input,
        grad_qkv,
        grad_out,
        grad_in,
        grad_mlp,
        grad_gain1,
        grad_gain2,
    )


def local(tokens, cotangent, w_qkv, w_attn_out, w_in, w_mlp_out, norm_gain1, norm_gain2):
    args = (tokens, cotangent, w_qkv, w_attn_out, w_in, w_mlp_out, norm_gain1, norm_gain2)
    sizes = [lax.axis_size(axis) for axis in ("dp", "ctx", "head")]
    if sizes == [4, 2, 4] and tokens.shape[2] == 8 * 2 * HD and tokens.shape[1] % 16 == 0:
        return local_split(*args)
    return local_general(*args)


def solution(mesh):
    in_specs = (
        P("dp", ("ctx", "head"), None),
        P("dp", ("ctx", "head"), None),
        P(("dp", "ctx"), None),
        P(("dp", "ctx"), None),
        P(("dp", "ctx"), None),
        P(("dp", "ctx"), None),
        P(("dp", "ctx")),
        P(("dp", "ctx")),
    )
    out_specs = (
        P("dp", ("ctx", "head"), None),
        P("dp", ("ctx", "head"), None),
        P(("dp", "ctx"), "head"),
        P(("dp", "ctx"), "head"),
        P(("dp", "ctx"), "head"),
        P(("dp", "ctx"), "head"),
        P(("dp", "ctx", "head")),
        P(("dp", "ctx", "head")),
    )
    return jax.shard_map(local, mesh=mesh, in_specs=in_specs, out_specs=out_specs, check_vma=False)
```

```python
import functools
import math

import jax
import jax.numpy as jnp
from jax import lax
from jax.experimental import pallas as pl
from jax.experimental.pallas import tpu as pltpu
from jax.sharding import PartitionSpec as P

HD = 64


EPSILON = 1e-05
ROPE_BASE = 160000.0


def normalize(values):
    centre = jnp.mean(values, axis=-1, keepdims=True)
    shifted = values - centre
    spread = jnp.mean(shifted * shifted, axis=-1, keepdims=True)
    factor = lax.rsqrt(spread + EPSILON)
    return (shifted * factor, factor)


def norm_back(grad_normed, normed, factor):
    grad_centre = jnp.mean(grad_normed, axis=-1, keepdims=True)
    grad_along = jnp.mean(grad_normed * normed, axis=-1, keepdims=True)
    return (grad_normed - grad_centre - normed * grad_along) * factor


def rope_tables(positions, half_size):
    frequency = jnp.exp(
        jnp.arange(half_size, dtype=jnp.float32) * (-math.log(ROPE_BASE) / half_size)
    )
    angles = positions[:, None] * frequency[None, :]
    return (jnp.cos(angles), jnp.sin(angles))


def rotate(values, cosine, sine_table, direction):
    half_size = cosine.shape[-1]
    first_half = values[..., :half_size]
    second_half = values[..., half_size:]
    cos_part = cosine[:, None, :]
    sin_part = sine_table[:, None, :] * direction
    return jnp.concatenate(
        [
            first_half * cos_part - second_half * sin_part,
            second_half * cos_part + first_half * sin_part,
        ],
        axis=-1,
    )


def block_scores(queries4, keys_block, scale):
    keys4 = keys_block.reshape(
        keys_block.shape[0], keys_block.shape[1], queries4.shape[2], queries4.shape[3]
    )
    return (
        jnp.einsum("sqgd,skgd->sgqk", queries4, keys4, preferred_element_type=jnp.float32) * scale
    )


def attend_forward(queries4, keys_all, values_all, key_rows, scale):
    seqs_here, query_rows, groups, head_size = queries4.shape
    turns = keys_all.shape[1] // key_rows

    def statistics(turn, carry):
        row_peak, row_total = carry
        keys_block = lax.dynamic_slice_in_dim(keys_all, turn * key_rows, key_rows, 1)
        scores = block_scores(queries4, keys_block, scale)
        new_peak = jnp.maximum(row_peak, jnp.max(scores, axis=-1))
        row_total = row_total * jnp.exp(row_peak - new_peak) + jnp.sum(
            jnp.exp(scores - new_peak[..., None]), axis=-1
        )
        return (new_peak, row_total)

    start_peak = jnp.full((seqs_here, groups, query_rows), -1e30, jnp.float32)
    row_peak, row_total = lax.fori_loop(
        0, turns, statistics, (start_peak, jnp.zeros_like(start_peak))
    )
    log_total = row_peak + jnp.log(row_total)

    def accumulate(turn, running):
        keys_block = lax.dynamic_slice_in_dim(keys_all, turn * key_rows, key_rows, 1)
        values_block = lax.dynamic_slice_in_dim(values_all, turn * key_rows, key_rows, 1).reshape(
            seqs_here, key_rows, groups, head_size
        )
        weights = jnp.exp(block_scores(queries4, keys_block, scale) - log_total[..., None]).astype(
            jnp.bfloat16
        )
        return running + jnp.einsum(
            "sgqk,skgd->sqgd", weights, values_block, preferred_element_type=jnp.float32
        )

    attended = lax.fori_loop(
        0, turns, accumulate, jnp.zeros((seqs_here, query_rows, groups, head_size), jnp.float32)
    )
    return (attended, log_total)


def attend_backward(queries4, keys_all, values_all, grad_out4, log_total, along, key_rows, scale):
    seqs_here, query_rows, groups, head_size = queries4.shape
    length = keys_all.shape[1]
    width_group = groups * head_size
    turns = length // key_rows

    def step_back(turn, carry):
        grad_queries, grad_keys, grad_values = carry
        keys_block = lax.dynamic_slice_in_dim(keys_all, turn * key_rows, key_rows, 1)
        keys4 = keys_block.reshape(seqs_here, key_rows, groups, head_size)
        values4 = lax.dynamic_slice_in_dim(values_all, turn * key_rows, key_rows, 1).reshape(
            seqs_here, key_rows, groups, head_size
        )
        weights = jnp.exp(block_scores(queries4, keys_block, scale) - log_total[..., None])
        grad_weights = jnp.einsum(
            "sqgd,skgd->sgqk", grad_out4, values4, preferred_element_type=jnp.float32
        )
        grad_scores = (weights * (grad_weights - along[..., None])).astype(jnp.bfloat16)
        grad_queries = grad_queries + jnp.einsum(
            "sgqk,skgd->sqgd", grad_scores, keys4, preferred_element_type=jnp.float32
        )
        key_part = (
            jnp.einsum("sgqk,sqgd->skgd", grad_scores, queries4, preferred_element_type=jnp.float32)
            * scale
        )
        value_part = jnp.einsum(
            "sgqk,sqgd->skgd",
            weights.astype(jnp.bfloat16),
            grad_out4,
            preferred_element_type=jnp.float32,
        )
        grad_keys = lax.dynamic_update_slice_in_dim(
            grad_keys, key_part.reshape(seqs_here, key_rows, width_group), turn * key_rows, 1
        )
        grad_values = lax.dynamic_update_slice_in_dim(
            grad_values, value_part.reshape(seqs_here, key_rows, width_group), turn * key_rows, 1
        )
        return (grad_queries, grad_keys, grad_values)

    start = (
        jnp.zeros((seqs_here, query_rows, groups, head_size), jnp.float32),
        jnp.zeros((seqs_here, length, width_group), jnp.float32),
        jnp.zeros((seqs_here, length, width_group), jnp.float32),
    )
    grad_queries, grad_keys, grad_values = lax.fori_loop(0, turns, step_back, start)
    return (grad_queries * scale, grad_keys, grad_values)


def local_general(tokens, cotangent, w_qkv, w_attn_out, w_in, w_mlp_out, norm_gain1, norm_gain2):
    seqs_here, block_rows, width = tokens.shape
    count_rows = seqs_here * block_rows
    heads_all = width // HD
    head_devices = lax.axis_size("head")
    group_devices = lax.axis_size(("dp", "ctx"))
    groups = heads_all // head_devices
    width_group = groups * HD
    scale = HD ** (-0.5)
    ff_width = w_in.shape[1] // 2
    full_qkv, full_out, full_in, full_mlp, gain_one, gain_two = (
        lax.all_gather(w_qkv, ("dp", "ctx"), axis=0, tiled=True),
        lax.all_gather(w_attn_out, ("dp", "ctx"), axis=0, tiled=True),
        lax.all_gather(w_in, ("dp", "ctx"), axis=0, tiled=True),
        lax.all_gather(w_mlp_out, ("dp", "ctx"), axis=0, tiled=True),
        lax.all_gather(norm_gain1, ("dp", "ctx"), axis=0, tiled=True),
        lax.all_gather(norm_gain2, ("dp", "ctx"), axis=0, tiled=True),
    )
    x_in = tokens.astype(jnp.float32).reshape(count_rows, width)
    normed1, factor1 = normalize(x_in)
    lowered1 = (normed1 * gain_one.astype(jnp.float32)).astype(jnp.bfloat16)
    projected = jnp.dot(lowered1, full_qkv, preferred_element_type=jnp.float32).reshape(
        seqs_here, block_rows, 3, heads_all, HD
    )
    first_pos = (lax.axis_index("ctx") * head_devices + lax.axis_index("head")) * block_rows
    positions = (first_pos + jnp.arange(block_rows, dtype=jnp.int32)).astype(jnp.float32)
    cosine, sine_table = rope_tables(positions, HD // 2)
    queries = (
        rotate(projected[:, :, 0], cosine, sine_table, 1.0)
        .astype(jnp.bfloat16)
        .reshape(seqs_here, block_rows, width)
    )
    keys_local = (
        rotate(projected[:, :, 1], cosine, sine_table, 1.0)
        .astype(jnp.bfloat16)
        .reshape(seqs_here, block_rows, width)
    )
    values_local = projected[:, :, 2].astype(jnp.bfloat16).reshape(seqs_here, block_rows, width)
    queries_h, keys_h, values_h = (
        lax.all_to_all(queries, "head", split_axis=2, concat_axis=1, tiled=True),
        lax.all_to_all(keys_local, "head", split_axis=2, concat_axis=1, tiled=True),
        lax.all_to_all(values_local, "head", split_axis=2, concat_axis=1, tiled=True),
    )
    query_rows = queries_h.shape[1]
    queries4 = queries_h.reshape(seqs_here, query_rows, groups, HD)
    keys_all, values_all = (
        lax.all_gather(keys_h, "ctx", axis=1, tiled=True),
        lax.all_gather(values_h, "ctx", axis=1, tiled=True),
    )
    key_rows = math.gcd(keys_all.shape[1], 1024)
    attended, log_total = attend_forward(queries4, keys_all, values_all, key_rows, scale)
    attended_low = attended.astype(jnp.bfloat16).reshape(seqs_here, query_rows, width_group)
    back_rows = lax.all_to_all(
        attended_low, "head", split_axis=1, concat_axis=2, tiled=True
    ).reshape(count_rows, width)
    residual = x_in + jnp.dot(back_rows, full_out, preferred_element_type=jnp.float32)
    normed2, factor2 = normalize(residual)
    lowered2 = (normed2 * gain_two.astype(jnp.float32)).astype(jnp.bfloat16)
    lifted = jnp.dot(lowered2, full_in, preferred_element_type=jnp.float32)
    first_part = lifted[:, :ff_width]
    second_part = lifted[:, ff_width:]
    activated, gelu_pullback = jax.vjp(
        lambda entries: jax.nn.gelu(entries, approximate=False), first_part
    )
    mixed = (activated * second_part).astype(jnp.bfloat16)
    result = (residual + jnp.dot(mixed, full_mlp, preferred_element_type=jnp.float32)).astype(
        jnp.bfloat16
    )
    full_qkv, full_out, full_in, full_mlp, gain_one, gain_two = (
        lax.all_gather(w_qkv, ("dp", "ctx"), axis=0, tiled=True),
        lax.all_gather(w_attn_out, ("dp", "ctx"), axis=0, tiled=True),
        lax.all_gather(w_in, ("dp", "ctx"), axis=0, tiled=True),
        lax.all_gather(w_mlp_out, ("dp", "ctx"), axis=0, tiled=True),
        lax.all_gather(norm_gain1, ("dp", "ctx"), axis=0, tiled=True),
        lax.all_gather(norm_gain2, ("dp", "ctx"), axis=0, tiled=True),
    )
    keys_all, values_all = (
        lax.all_gather(keys_h, "ctx", axis=1, tiled=True),
        lax.all_gather(values_h, "ctx", axis=1, tiled=True),
    )
    grad_top = cotangent.reshape(count_rows, width)
    grad_mlp = jnp.einsum("nf,nd->fd", mixed, grad_top, preferred_element_type=jnp.float32)
    grad_mixed = jnp.einsum("nd,fd->nf", grad_top, full_mlp, preferred_element_type=jnp.float32)
    grad_first = gelu_pullback(grad_mixed * second_part)[0]
    grad_lifted = jnp.concatenate([grad_first, grad_mixed * activated], axis=-1).astype(
        jnp.bfloat16
    )
    grad_inner = jnp.einsum("nd,nf->df", lowered2, grad_lifted, preferred_element_type=jnp.float32)
    grad_lowered2 = jnp.einsum(
        "nf,df->nd", grad_lifted, full_in, preferred_element_type=jnp.float32
    )
    grad_two = jnp.sum(grad_lowered2 * normed2, axis=0)
    grad_residual = grad_top.astype(jnp.float32) + norm_back(
        grad_lowered2 * gain_two.astype(jnp.float32), normed2, factor2
    )
    grad_branch = grad_residual.astype(jnp.bfloat16)
    grad_outproj = jnp.einsum(
        "nd,ne->de", back_rows, grad_branch, preferred_element_type=jnp.float32
    )
    grad_attended = jnp.einsum(
        "ne,de->nd", grad_branch, full_out, preferred_element_type=jnp.float32
    ).astype(jnp.bfloat16)
    grad_attended_h = lax.all_to_all(
        grad_attended.reshape(seqs_here, block_rows, width),
        "head",
        split_axis=2,
        concat_axis=1,
        tiled=True,
    )
    grad_out4 = grad_attended_h.reshape(seqs_here, query_rows, groups, HD)
    along = jnp.transpose(jnp.sum(grad_out4.astype(jnp.float32) * attended, axis=-1), (0, 2, 1))
    grad_queries, grad_keys_all, grad_values_all = attend_backward(
        queries4, keys_all, values_all, grad_out4, log_total, along, key_rows, scale
    )
    grad_keys_sum, grad_values_sum = (
        lax.psum_scatter(
            grad_keys_all.astype(jnp.bfloat16), "ctx", scatter_dimension=1, tiled=True
        ).astype(jnp.float32),
        lax.psum_scatter(
            grad_values_all.astype(jnp.bfloat16), "ctx", scatter_dimension=1, tiled=True
        ).astype(jnp.float32),
    )
    grad_q_low = grad_queries.astype(jnp.bfloat16).reshape(seqs_here, query_rows, width_group)
    grad_q_tok, grad_k_tok, grad_v_tok = (
        lax.all_to_all(grad_q_low, "head", split_axis=1, concat_axis=2, tiled=True),
        lax.all_to_all(
            grad_keys_sum.astype(jnp.bfloat16), "head", split_axis=1, concat_axis=2, tiled=True
        ),
        lax.all_to_all(
            grad_values_sum.astype(jnp.bfloat16), "head", split_axis=1, concat_axis=2, tiled=True
        ),
    )
    unrot_q = rotate(
        grad_q_tok.astype(jnp.float32).reshape(seqs_here, block_rows, heads_all, HD),
        cosine,
        sine_table,
        -1.0,
    )
    unrot_k = rotate(
        grad_k_tok.astype(jnp.float32).reshape(seqs_here, block_rows, heads_all, HD),
        cosine,
        sine_table,
        -1.0,
    )
    grad_projected = jnp.concatenate(
        [
            unrot_q.reshape(count_rows, width),
            unrot_k.reshape(count_rows, width),
            grad_v_tok.astype(jnp.float32).reshape(count_rows, width),
        ],
        axis=-1,
    ).astype(jnp.bfloat16)
    grad_project = jnp.einsum(
        "nd,nf->df", lowered1, grad_projected, preferred_element_type=jnp.float32
    )
    grad_lowered1 = jnp.einsum(
        "nf,df->nd", grad_projected, full_qkv, preferred_element_type=jnp.float32
    )
    grad_one = jnp.sum(grad_lowered1 * normed1, axis=0)
    grad_input = grad_residual + norm_back(
        grad_lowered1 * gain_one.astype(jnp.float32), normed1, factor1
    )
    pieces_one = grad_one.reshape(group_devices, head_devices, -1)
    pieces_two = grad_two.reshape(group_devices, head_devices, -1)
    part_qkv, part_out, part_in, part_mlp, part_one, part_two = (
        lax.psum_scatter(
            grad_project.astype(jnp.bfloat16), ("dp", "ctx"), scatter_dimension=0, tiled=True
        ).astype(jnp.float32),
        lax.psum_scatter(
            grad_outproj.astype(jnp.bfloat16), ("dp", "ctx"), scatter_dimension=0, tiled=True
        ).astype(jnp.float32),
        lax.psum_scatter(
            grad_inner.astype(jnp.bfloat16), ("dp", "ctx"), scatter_dimension=0, tiled=True
        ).astype(jnp.float32),
        lax.psum_scatter(
            grad_mlp.astype(jnp.bfloat16), ("dp", "ctx"), scatter_dimension=0, tiled=True
        ).astype(jnp.float32),
        lax.psum_scatter(
            pieces_one.astype(jnp.bfloat16), ("dp", "ctx"), scatter_dimension=0, tiled=True
        ).astype(jnp.float32),
        lax.psum_scatter(
            pieces_two.astype(jnp.bfloat16), ("dp", "ctx"), scatter_dimension=0, tiled=True
        ).astype(jnp.float32),
    )
    final_qkv, final_out, final_in, final_mlp, final_one, final_two = (
        lax.psum_scatter(
            part_qkv.astype(jnp.bfloat16), "head", scatter_dimension=1, tiled=True
        ).astype(jnp.float32),
        lax.psum_scatter(
            part_out.astype(jnp.bfloat16), "head", scatter_dimension=1, tiled=True
        ).astype(jnp.float32),
        lax.psum_scatter(
            part_in.astype(jnp.bfloat16), "head", scatter_dimension=1, tiled=True
        ).astype(jnp.float32),
        lax.psum_scatter(
            part_mlp.astype(jnp.bfloat16), "head", scatter_dimension=1, tiled=True
        ).astype(jnp.float32),
        lax.psum_scatter(
            part_one.astype(jnp.bfloat16), "head", scatter_dimension=1, tiled=True
        ).astype(jnp.float32),
        lax.psum_scatter(
            part_two.astype(jnp.bfloat16), "head", scatter_dimension=1, tiled=True
        ).astype(jnp.float32),
    )
    return (
        result.reshape(seqs_here, block_rows, width),
        grad_input.reshape(seqs_here, block_rows, width),
        final_qkv,
        final_out,
        final_in,
        final_mlp,
        final_one.reshape(-1),
        final_two.reshape(-1),
    )


F32 = jnp.float32
BF16 = jnp.bfloat16
GROUP = ("ctx", "head")


def dot(left, right, dims=((1,), (0,))):
    return lax.dot_general(left, right, (dims, ((), ())), preferred_element_type=F32)


def wide(values):
    return values.astype(F32)


def flat(values):
    return values.reshape(-1, values.shape[-1])


def lane_rotate(values, cosine, sine_signed):
    lane = lax.broadcasted_iota(jnp.int32, values.shape, 1)
    width = values.shape[1]
    partner = jnp.where(
        lane % HD < HD // 2,
        pltpu.roll(values, width - HD // 2, 1),
        pltpu.roll(values, HD // 2, 1),
    )
    return values * cosine + partner * sine_signed


def head_masks(shape):
    lane = lax.broadcasted_iota(jnp.int32, shape, 1)
    return [lane // HD == head for head in range(shape[1] // HD)]


def params(mebibytes):
    return pltpu.CompilerParams(vmem_limit_bytes=mebibytes * 1024 * 1024)


COST = pl.CostEstimate(flops=1 << 20, transcendentals=0, bytes_accessed=1 << 16)


def whole(array):
    return pl.BlockSpec(array.shape, lambda *_: (0,) * len(array.shape))


SCALARS = pl.BlockSpec(memory_space=pltpu.SMEM)


def project_kernel(place_ref, *refs):
    pieces, weights = refs[:6], refs[6:10]
    cos_ref, sin_ref, low_ref, qkv_ref, w_ref, gain1_ref, gain2_ref, rows_ref = refs[10:]
    block, part = pieces[0].shape[2], w_ref.shape[1] // 3
    rows = gain1_ref.shape[1] // 8

    @pl.when(pl.program_id(0) == 0)
    def _():
        for step, piece in enumerate(weights):
            for turn in range(2):
                at = 2 * (place_ref[8] ^ step) + (place_ref[9] ^ turn)
                w_ref[pl.ds(pl.multiple_of(at * rows, rows), rows), :] = piece[turn, :rows]
                gains = piece[turn, rows:].astype(F32)
                rows_ref[0, pl.ds(at, 1), :] = gains[:1, :rows]
                rows_ref[1, pl.ds(at, 1), :] = gains[1:2, :rows]
        for out, at in ((gain1_ref, 0), (gain2_ref, 1)):
            for row in range(8):
                out[:, row * rows : (row + 1) * rows] = rows_ref[at, row : row + 1, :]

    gain = gain1_ref[...]
    index = 0
    for piece in pieces:
        for inner in range(piece.shape[0]):
            normed, _ = normalize(piece[inner, 0].astype(F32))
            low_ref[index, 0] = (normed * gain).astype(BF16)
            index += 1
    projected = dot(flat(low_ref[:, 0]), w_ref[...])
    cosine, sine = cos_ref[...], sin_ref[...]
    shape = (8, block, part)
    qkv_ref[:, 0, :, :part] = (
        (lane_rotate(projected[:, :part], cosine, sine) * HD**-0.5).astype(BF16).reshape(shape)
    )
    qkv_ref[:, 0, :, part : 2 * part] = (
        lane_rotate(projected[:, part : 2 * part], cosine, sine).astype(BF16).reshape(shape)
    )
    qkv_ref[:, 0, :, 2 * part :] = projected[:, 2 * part :].astype(BF16).reshape(shape)


def project(place, pieces, weights, cosine, sine):
    seqs, block, width = pieces[0].shape[1:]
    own = weights[0].shape[2]

    def by_seq(lead, last):
        return pl.BlockSpec((lead, 1, block, last), lambda s: (0, s, 0, 0))

    return pl.pallas_call(
        project_kernel,
        grid=(seqs,),
        in_specs=[SCALARS]
        + [by_seq(piece.shape[0], width) for piece in pieces]
        + [whole(w) for w in weights]
        + [whole(cosine), whole(sine)],
        out_specs=(
            by_seq(8, width),
            by_seq(8, own),
            pl.BlockSpec((width, own), lambda s: (0, 0)),
            pl.BlockSpec((1, width), lambda s: (0, 0)),
            pl.BlockSpec((1, width), lambda s: (0, 0)),
        ),
        out_shape=(
            jax.ShapeDtypeStruct((8, seqs, block, width), BF16),
            jax.ShapeDtypeStruct((8, seqs, block, own), BF16),
            jax.ShapeDtypeStruct((width, own), BF16),
            jax.ShapeDtypeStruct((1, width), F32),
            jax.ShapeDtypeStruct((1, width), F32),
        ),
        scratch_shapes=[pltpu.VMEM((2, 8, width // 8), F32)],
        compiler_params=params(36),
        cost_estimate=COST,
        name="project",
    )(place, *pieces, *weights, cosine, sine)


def attend_kernel(place_ref, q_ref, k_ref, v_ref, *refs):
    att_ref, log_ref, home_ref = refs[-3:]
    step, seq = pl.program_id(0), len(refs) - 3
    if seq:

        @pl.when(step == 0)
        def _():
            home_ref[:, :1] = refs[0][...]

    queries, keys, values = flat(q_ref[...]), flat(k_ref[...]), flat(v_ref[...])
    attended = jnp.zeros(queries.shape, F32)
    logs = jnp.zeros(queries.shape, F32)
    for mask in head_masks(queries.shape):
        scores = dot(jnp.where(mask, queries, 0), keys, ((1,), (1,)))
        peak = jnp.max(scores, axis=1, keepdims=True)
        weights = jnp.exp(scores - peak)
        total = jnp.sum(weights, axis=1, keepdims=True)
        mixed = dot(weights.astype(BF16), values) * (1.0 / total)
        attended = jnp.where(mask, mixed, attended)
        logs = jnp.where(mask, peak + jnp.log(total), logs)
    att_ref[...] = attended.reshape(att_ref.shape)
    log_ref[...] = logs.reshape(log_ref.shape)
    low = attended.astype(BF16).reshape(att_ref.shape)
    for inner in range(2):
        home_ref[place_ref[2 * step + inner], seq] = low[inner, 0]


def attend(place, qkv, *home):
    _, _, block, own = qkv.shape
    part, seq = own // 3, len(home)
    rows = pl.BlockSpec((2, 1, block, part), lambda i: (i, 0, 0, 0))
    shape = (8, 1, block, part)
    return pl.pallas_call(
        attend_kernel,
        grid=(4,),
        in_specs=[
            SCALARS,
            pl.BlockSpec((2, 1, block, part), lambda i: (i, seq, 0, 0)),
            pl.BlockSpec((8, 1, block, part), lambda i: (0, seq, 0, 1)),
            pl.BlockSpec((8, 1, block, part), lambda i: (0, seq, 0, 2)),
            *[whole(h) for h in home],
        ],
        out_specs=(
            rows,
            rows,
            pl.BlockSpec((8, 1 + seq, block, part), lambda i: (0, 0, 0, 0)),
        ),
        out_shape=(
            jax.ShapeDtypeStruct(shape, F32),
            jax.ShapeDtypeStruct(shape, F32),
            jax.ShapeDtypeStruct((8, 1 + seq, block, part), BF16),
        ),
        compiler_params=params(24),
        cost_estimate=COST,
        name="attend",
    )(place, qkv, qkv, qkv, *home)


def branch_kernel(place_ref, *refs):
    pieces = refs[:6]
    rows_ref, tokens_ref, gain_ref, residual_ref, low_ref, side_ref, total_ref = refs[6:]
    heads = rows_ref.shape[0] // 2
    for c in range(2):
        side_ref[c] = jnp.concatenate([flat(rows_ref[c * heads + d]) for d in range(heads)], axis=1)
    total_ref[...] = flat(wide(tokens_ref[...]))
    index = 0
    for piece in pieces:
        n = piece.shape[2]
        for inner in range(piece.shape[0]):
            at = place_ref[index]
            columns = pl.ds(pl.multiple_of((at % heads) * n, n), n)
            total_ref[:, columns] += dot(side_ref[at // heads], piece[inner])
            index += 1
    total = total_ref[...]
    normed, _ = normalize(total)
    residual_ref[...] = total.reshape(residual_ref.shape)
    low_ref[...] = (normed * gain_ref[...]).astype(BF16).reshape(low_ref.shape)


def branch(place, pieces, rows, tokens, gain):
    args = (*pieces, rows, tokens, gain)
    seqs, block, width = tokens.shape
    return pl.pallas_call(
        branch_kernel,
        in_specs=[SCALARS] + [whole(a) for a in args],
        out_shape=(
            jax.ShapeDtypeStruct(tokens.shape, F32),
            jax.ShapeDtypeStruct(tokens.shape, BF16),
        ),
        scratch_shapes=[
            pltpu.VMEM((2, seqs * block, pieces[0].shape[1]), BF16),
            pltpu.VMEM((seqs * block, width), F32),
        ],
        compiler_params=params(16),
        cost_estimate=COST,
        name="branch",
    )(place, *args)


def combine(*groups):
    parts = [part for group in groups for _, parts in group for part in parts]
    rows = sum(count for count, _ in groups[0])
    width = parts[0][0].shape[2]

    def kernel(*refs):
        at = 0
        for k, group in enumerate(groups):
            row = 0
            for count, terms in group:
                total = 0.0
                for _, _, start in terms:
                    total = total + wide(refs[at][0, start : start + count])
                    at += 1
                refs[-1][k, row : row + count] = total.astype(BF16)
                row += count

    return pl.pallas_call(
        kernel,
        grid=(1,),
        in_specs=[
            pl.BlockSpec((1, *array.shape[1:]), lambda *_, index=index: (index, 0, 0))
            for array, index, _ in parts
        ],
        out_specs=pl.BlockSpec((len(groups), rows, width), lambda *_: (0, 0, 0)),
        out_shape=jax.ShapeDtypeStruct((len(groups), rows, width), BF16),
        compiler_params=params(16),
        cost_estimate=COST,
        name="combine",
    )(*[array for array, _, _ in parts])


def mlp_kernel(*refs, count, ends):
    pieces, tops = refs[:count], refs[count : 2 * count]
    w_ref, out_w_ref = refs[2 * count : 2 * count + 2]
    low_ref, top_ref, mixed_ref, lifted_ref, *out_refs = refs[-4 - len(ends) :]
    step = pl.program_id(0)
    start = 0
    for piece, top in zip(pieces, tops):

        @pl.when((step >= start) & (step < start + piece.shape[0]))
        def _(piece=piece, top=top, start=start):
            low_ref[0] = piece[step - start]
            top_ref[0] = top[step - start]

        start += piece.shape[0]

    hidden = w_ref.shape[1] // 2
    lifted = dot(flat(low_ref[...]), w_ref[...])
    first, second = lifted[:, :hidden], lifted[:, hidden:]
    grad_mixed = dot(flat(top_ref[...]), out_w_ref[...], ((1,), (1,)))
    gate = 0.5 * (1.0 + lax.erf(first * (0.5**0.5)))
    slope = gate + first * jnp.exp(first * first * -0.5) * ((2.0 * math.pi) ** -0.5)
    activated = first * gate
    mixed_ref[...] = (activated * second).astype(BF16).reshape(mixed_ref.shape)
    grad = jnp.concatenate(
        [(grad_mixed * second * slope).astype(BF16), (grad_mixed * activated).astype(BF16)],
        axis=1,
    )
    lifted_ref[...] = grad.reshape(lifted_ref.shape)
    partial = dot(grad, w_ref[...], ((1,), (1,))).astype(BF16).reshape(low_ref.shape)
    start = 0
    for out, end in zip(out_refs, ends):

        @pl.when((step >= start) & (step < end))
        def _(out=out):
            out[...] = partial

        start = end


def mlp(pieces, tops, w, out_w, base, ends, earlier=()):
    seqs, block, width = pieces[0].shape[1:]
    hidden = w.shape[1] // 2
    whole_in = (*pieces, *tops, w, out_w)

    def rows(last):
        return pl.BlockSpec((1, seqs, block, last), lambda i: (i + base, 0, 0, 0))

    def within(start, end):
        return pl.BlockSpec(
            (1, seqs, block, width),
            lambda i: (jnp.clip(i - start, 0, end - start - 1), 0, 0, 0),
        )

    starts = (0, *ends[:-1])
    lasts = (width, width, hidden, 2 * hidden)
    return pl.pallas_call(
        functools.partial(mlp_kernel, count=len(pieces), ends=ends),
        grid=(ends[-1],),
        in_specs=[whole(array) for array in whole_in]
        + [pl.BlockSpec(memory_space=pl.ANY)] * len(earlier),
        out_specs=(
            *[rows(last) for last in lasts],
            *[within(start, end) for start, end in zip(starts, ends)],
        ),
        out_shape=(
            *[jax.ShapeDtypeStruct((8, seqs, block, last), BF16) for last in lasts],
            *[
                jax.ShapeDtypeStruct((end - start, seqs, block, width), BF16)
                for start, end in zip(starts, ends)
            ],
        ),
        input_output_aliases={len(whole_in) + at: at for at in range(len(earlier))},
        compiler_params=params(32),
        cost_estimate=COST,
        name="mlp",
    )(*whole_in, *earlier)


def out_grad_kernel(place_ref, rows_ref, grad_ref, keep_ref, send_ref):
    grads = flat(grad_ref[...])
    for index in range(8):
        part = dot(flat(rows_ref[place_ref[index]]), grads, ((0,), (0,))).astype(BF16)
        if index < 5:
            keep_ref[index] = part
        else:
            send_ref[index - 5] = part


def out_grad(place, rows, grads):
    part, width = rows.shape[-1], grads.shape[-1]
    return pl.pallas_call(
        out_grad_kernel,
        in_specs=[SCALARS, whole(rows), whole(grads)],
        out_shape=(
            jax.ShapeDtypeStruct((5, part, width), BF16),
            jax.ShapeDtypeStruct((3, part, width), BF16),
        ),
        compiler_params=params(16),
        cost_estimate=COST,
        name="out_grad",
    )(place, rows, grads)


def branch_back_kernel(place_ref, *refs):
    pieces = refs[:6]
    keep_ref, near_ref, own_ref, residual_ref, top_ref, gain_ref = refs[6:12]
    grad_ref, branch_ref, home_ref, sum_ref, low_ref, side_ref = refs[12:]
    grad_low = wide(flat(keep_ref[...])) + wide(flat(near_ref[...])) + wide(flat(own_ref[...]))
    normed, factor = normalize(flat(residual_ref[...]))
    sum_ref[...] = jnp.sum(grad_low * normed, axis=0, keepdims=True)
    grad = flat(wide(top_ref[...])) + norm_back(grad_low * gain_ref[...], normed, factor)
    grad_ref[...] = grad.reshape(grad_ref.shape)
    low_ref[...] = grad.astype(BF16)
    branch_ref[...] = low_ref[...].reshape(branch_ref.shape)
    heads = home_ref.shape[0] // 2
    side_ref[...] = jnp.zeros_like(side_ref)
    index = 0
    for piece in pieces:
        n = piece.shape[2]
        for inner in range(piece.shape[0]):
            at = place_ref[index]
            columns = pl.ds(pl.multiple_of((at % heads) * n, n), n)
            side_ref[at // heads] += dot(low_ref[:, columns], piece[inner], ((1,), (1,)))
            index += 1
    part = home_ref.shape[3]
    for c in range(2):
        for d in range(heads):
            home = side_ref[c, :, d * part : (d + 1) * part].astype(BF16)
            home_ref[c * heads + d] = home.reshape(home_ref.shape[1:])


def branch_back(place, pieces, keep, near, own, residual, top, gain):
    args = (*pieces, keep, near, own, residual, top, gain)
    seqs, block, width = residual.shape
    tall = pieces[0].shape[1]
    shapes = (
        jax.ShapeDtypeStruct(residual.shape, F32),
        jax.ShapeDtypeStruct(residual.shape, BF16),
        jax.ShapeDtypeStruct((8, seqs, block, tall // 4), BF16),
        jax.ShapeDtypeStruct((1, width), F32),
    )
    return pl.pallas_call(
        branch_back_kernel,
        grid=(1,),
        in_specs=[SCALARS]
        + [whole(piece) for piece in pieces]
        + [pl.BlockSpec((1, seqs * block, width), lambda *_: (0, 0, 0))] * 2
        + [whole(a) for a in args[8:]],
        out_specs=tuple(whole(shape) for shape in shapes),
        out_shape=shapes,
        scratch_shapes=[
            pltpu.VMEM((seqs * block, width), BF16),
            pltpu.VMEM((2, seqs * block, tall), F32),
        ],
        compiler_params=params(24),
        cost_estimate=COST,
        name="branch_back",
    )(place, *args)


def attend_back_kernel(
    place_ref, q_ref, k_ref, v_ref, grad_ref, att_ref, log_ref, cosq_ref, sinq_ref, cos_ref,
    sin_ref, w_ref, low_ref, *refs, seq, last,
):
    if last:
        before_ref, gain1_ref, gain2_ref, keep_ref, send_ref, grad_w_ref, *scratch = refs
    else:
        keep_ref, send_ref, before_ref, *scratch = refs
    proj_ref, sum_k, sum_v = scratch
    step = pl.program_id(0)
    block, part = q_ref.shape[2], q_ref.shape[3]

    @pl.when(step == 0)
    def _():
        sum_k[...] = jnp.zeros_like(sum_k)
        sum_v[...] = jnp.zeros_like(sum_v)

    queries, keys, values = flat(q_ref[...]), flat(k_ref[...]), flat(v_ref[...])
    grads = jnp.concatenate([grad_ref[place_ref[2 * step + inner], seq] for inner in range(2)])
    along = (grads.astype(F32) * flat(att_ref[...])).T
    logs = flat(log_ref[...]).T
    grad_queries = jnp.zeros(queries.shape, F32)
    for head, mask in enumerate(head_masks(queries.shape)):
        own_q = jnp.where(mask, queries, 0)
        own_g = jnp.where(mask, grads, 0)
        scores = dot(keys, own_q, ((1,), (1,)))
        weights = jnp.exp(scores - logs[head * HD : head * HD + 1])
        lifted = dot(values, own_g, ((1,), (1,)))
        row = jnp.sum(along[head * HD : (head + 1) * HD], axis=0, keepdims=True)
        grad_scores = (weights * (lifted - row)).astype(BF16)
        sum_k[...] += dot(grad_scores, own_q)
        sum_v[...] += dot(weights.astype(BF16), own_g)
        grad_queries = jnp.where(mask, dot(grad_scores, keys, ((0,), (0,))), grad_queries)
    grad_queries = lane_rotate(grad_queries * HD**-0.5, cosq_ref[...], -sinq_ref[...])
    rows = pl.multiple_of(step * 2 * block, 2 * block)
    proj_ref[pl.ds(rows, 2 * block), :part] = grad_queries.astype(BF16)

    @pl.when(step == 3)
    def _():
        grad_keys = lane_rotate(sum_k[...], cos_ref[...], -sin_ref[...])
        proj_ref[:, part : 2 * part] = grad_keys.astype(BF16)
        proj_ref[:, 2 * part :] = sum_v[...].astype(BF16)
        partial = dot(proj_ref[...], w_ref[...], ((1,), (1,))).astype(BF16)
        keep_ref[...] = partial[: 5 * block].reshape(5, block, -1)
        send_ref[...] = partial[5 * block :].reshape(3, block, -1)
        grad_w = dot(proj_ref[...], flat(low_ref[...]), ((0,), (0,)))
        if last:
            grad_w = (grad_w + before_ref[...]).T
            along_w = jnp.sum(grad_w * wide(w_ref[...]), axis=1, keepdims=True)
            along_w = jnp.broadcast_to(along_w, (w_ref.shape[0], 128)).T[:1] / gain1_ref[...]
            row = lax.broadcasted_iota(jnp.int32, (GAIN_ROWS, w_ref.shape[0]), 0)
            gains = jnp.where(row == 0, along_w, jnp.where(row == 1, gain2_ref[...], 0.0))
            n = grad_w_ref.shape[1] - GAIN_ROWS
            for at in range(grad_w_ref.shape[0]):
                part_rows = slice(at * n, (at + 1) * n)
                grad_w_ref[at, :n] = grad_w[part_rows].astype(BF16)
                grad_w_ref[at, n:, :n] = gains[:, part_rows].astype(BF16)
                rest = grad_w_ref.shape[2] - n
                grad_w_ref[at, n:, n:] = jnp.zeros((GAIN_ROWS, rest), BF16)
        else:
            before_ref[...] = grad_w


GAIN_ROWS = 16


def attend_back(place, qkv, grads, attended, logs, cosine, sine, w, low, seq, *before, dp=1):
    _, _, block, own = qkv.shape
    part, width = own // 3, w.shape[0]
    last = len(before) > 0
    rows = pl.BlockSpec((2, 1, block, part), lambda i: (i, 0, 0, 0))
    angles = pl.BlockSpec((2 * block, part), lambda i: (i, 0))

    def full(*shape):
        return pl.BlockSpec(shape, lambda i: (0,) * len(shape))

    args = [place, qkv, qkv, qkv, grads, attended, logs, cosine, sine, cosine, sine, w, low]
    in_specs = [
        SCALARS,
        pl.BlockSpec((2, 1, block, part), lambda i: (i, seq, 0, 0)),
        pl.BlockSpec((8, 1, block, part), lambda i: (0, seq, 0, 1)),
        pl.BlockSpec((8, 1, block, part), lambda i: (0, seq, 0, 2)),
        whole(grads),
        rows,
        rows,
        angles,
        angles,
        whole(cosine),
        whole(sine),
        whole(w),
        pl.BlockSpec((8, 1, block, width), lambda i: (0, seq, 0, 0)),
    ]
    shapes = [((5, block, width), BF16), ((3, block, width), BF16)]
    if last:
        args += before
        in_specs += [whole(array) for array in before]
        shapes += [((dp, width // dp + GAIN_ROWS, own), BF16)]
    else:
        shapes += [((own, width), F32)]
    return pl.pallas_call(
        functools.partial(attend_back_kernel, seq=seq, last=last),
        grid=(4,),
        in_specs=in_specs,
        out_specs=tuple(full(*shape) for shape, _ in shapes),
        out_shape=tuple(jax.ShapeDtypeStruct(shape, kind) for shape, kind in shapes),
        scratch_shapes=[
            pltpu.VMEM((8 * block, own), BF16),
            pltpu.VMEM((8 * block, part), F32),
            pltpu.VMEM((8 * block, part), F32),
        ],
        compiler_params=params(40),
        cost_estimate=COST,
        name="attend_back",
    )(*args)


def input_grad_kernel(*refs):
    keeps, (near_ref, own_ref, tokens_ref, residual_ref, gain_ref, out_ref) = refs[:-6], refs[-6:]
    block = tokens_ref.shape[1]
    for seq, keep in enumerate(keeps):
        rows = slice(seq * block, (seq + 1) * block)
        grad = wide(keep[0, :block]) + wide(near_ref[0, rows]) + wide(own_ref[0, rows])
        normed, factor = normalize(wide(tokens_ref[seq]))
        out_ref[seq] = residual_ref[seq] + norm_back(grad * gain_ref[...], normed, factor)


def input_grad(keeps, near, own, tokens, residual, gain):
    rest = (own, tokens, residual, gain)
    return pl.pallas_call(
        input_grad_kernel,
        grid=(1,),
        in_specs=[
            pl.BlockSpec((1, *array.shape[1:]), lambda *_: (0, 0, 0)) for array in (*keeps, near)
        ]
        + [whole(array) for array in rest],
        out_specs=whole(residual),
        out_shape=jax.ShapeDtypeStruct(residual.shape, F32),
        compiler_params=params(16),
        cost_estimate=COST,
        name="input_grad",
    )(*keeps, near, *rest)


class Group:
    def __init__(self):
        self.heads = lax.axis_size("head")
        self.dp = lax.axis_size("dp")
        self.ctx_at = lax.axis_index("ctx")
        self.head_at = lax.axis_index("head")
        self.dp_at = lax.axis_index("dp")
        self.at = self.ctx_at * self.heads + self.head_at
        near, far = [], []
        for c in range(2):
            for h in range(self.heads):
                x, y = (c ^ 1) * self.heads + h, c * self.heads + (h ^ 2)
                near.append((c * self.heads + h, x if h % 2 == 0 else y))
                far.append((c * self.heads + h, y if h % 2 == 0 else x))
        self.near, self.far = near, far

    def order(self):
        first = jnp.where(self.head_at % 2 == 0, 4, 2)
        second = 6 - first
        return jnp.stack(
            [self.at ^ bits for bits in (0, 1, first, first ^ 1, 6, second ^ 1, second, 7)]
        )

    def swap(self, values, bit):
        if bit == 4:
            return lax.ppermute(values, "ctx", [(0, 1), (1, 0)])
        return lax.ppermute(values, "head", [(i, i ^ bit) for i in range(self.heads)])

    def mate(self, values):
        return self.swap(values, 1)

    def to_near(self, values):
        return lax.ppermute(values, GROUP, self.near)

    def to_far(self, values):
        return lax.ppermute(values, GROUP, self.far)

    def rows_back(self, values, place):
        pairs, same = [], False
        for d in range(self.dp):
            for h in range(self.heads):
                if (d, h) == (place[h], d):
                    same = same | ((self.dp_at == d) & (self.head_at == h))
                else:
                    pairs.append((d * self.heads + h, place[h] * self.heads + d))
        return jnp.where(same, values, lax.ppermute(values, ("dp", "head"), pairs))

    def across(self, values, step):
        return lax.ppermute(values, "dp", [(i, i ^ step) for i in range(self.dp)])


def pick(array, index, axis):
    return lax.dynamic_index_in_dim(array, index, axis, keepdims=False)


def after(values, *earlier):
    return lax.optimization_barrier((values, earlier))[0]


def local_split(tokens, cotangent, w_qkv, w_attn_out, w_in, w_mlp_out, norm_gain1, norm_gain2):
    seqs, block, width = tokens.shape
    group = Group()
    heads, dp = group.heads, group.dp
    at_c, at_h = group.ctx_at, group.head_at
    parts = 2 * heads
    hidden = w_in.shape[1] // 2 // parts
    padded = -(-hidden // 128) * 128
    own_width = width // parts
    half = heads // 2
    rows_here = w_qkv.shape[0]
    place = [2 * (h % half) + h // half for h in range(heads)]
    straight = list(range(heads))
    order = group.order()
    scalars = jnp.concatenate([order, jnp.stack([group.dp_at, at_c])]).astype(jnp.int32)
    mate, near, far = group.mate, group.to_near, group.to_far

    def in_order(own, other):
        return jnp.where(at_c == 0, jnp.stack([own, other]), jnp.stack([other, own]))

    def exchange(values):
        return lax.all_to_all(values, GROUP, split_axis=0, concat_axis=0, tiled=True)


    gains = jnp.pad(
        jnp.stack([norm_gain1, norm_gain2]), ((0, 14), (0, 3 * own_width - rows_here))
    )
    qkv_view = w_qkv.reshape(rows_here, 3, width)

    def qkv_part(at):
        start = (2 * at_h + at) * own_width
        cut = lax.dynamic_slice_in_dim(qkv_view, start, own_width, 2)
        return jnp.concatenate([cut.reshape(rows_here, 3 * own_width), gains])

    x_own = tokens[None]
    x_mate = mate(x_own)
    qkv_other, qkv_own = qkv_part(1 - at_c), qkv_part(at_c)
    qkv_cross = group.swap(after(qkv_other, x_own), 4)
    in_view = after(w_in, qkv_other).reshape(rows_here, 2, heads, 2, hidden)
    in_view = pick(in_view, 2 * (at_h % half) + at_h // half, 2)

    def in_part(at):
        cut = pick(in_view, at, 2)
        return jnp.pad(cut, ((0, 0), (0, 0), (0, padded - hidden))).reshape(rows_here, 2 * padded)

    in_other, in_own = in_part(1 - at_c), in_part(at_c)
    in_cross = group.swap(in_other, 4)
    x_chip = jnp.concatenate([x_own, after(x_mate, qkv_cross, qkv_own, in_cross, in_own)])
    x_near = near(x_chip)
    qkv_pair = jnp.stack([qkv_own, qkv_cross])
    qkv_pieces = [qkv_pair] + [group.across(qkv_pair, step) for step in range(1, dp)]

    slices = jnp.concatenate([w_attn_out, w_mlp_out])
    slices = after(slices, *qkv_pieces)
    slices = lax.dynamic_slice_in_dim(slices, at_h * (width // heads), width // heads, 1)
    slices = jnp.pad(slices, ((0, 64), (0, 0)))
    slices = lax.all_gather(slices, "dp", axis=0)
    positions = after(order, qkv_pair)[:, None] * block + jnp.arange(block, dtype=jnp.int32)
    lane = jnp.arange(own_width, dtype=jnp.int32)
    frequency = jnp.exp(
        (lane % (HD // 2)).astype(F32) * (-math.log(ROPE_BASE) / (HD // 2))
    )
    angles = wide(positions.reshape(-1))[:, None] * frequency[None, :]
    cosine = jnp.cos(angles)
    sine = jnp.sin(angles) * jnp.where(lane % HD < HD // 2, -1.0, 1.0)[None, :]

    x_far = far(x_near[:1])
    x_near = after(x_near, *qkv_pieces, cosine, sine)
    x_near_mate = mate(x_near)
    cot_own = after(cotangent, x_near)[None]
    cot_mate = mate(cot_own)
    in_pair, x_far = lax.optimization_barrier((in_order(in_own, in_cross), x_far))
    weight_in = lax.all_gather(in_pair, "dp", axis=0).reshape(width, -1)
    x_far = after(x_far, cot_mate)
    x_far_mate = mate(x_far)

    cot_chip = jnp.concatenate([cot_own, cot_mate])
    cot_near = near(after(cot_chip, x_far))
    out_rows = w_attn_out.shape[0]
    x_pieces = (x_own, x_mate, x_near, x_far, x_near_mate, after(x_far_mate, cot_chip))
    low1, qkv, weight_qkv, gain_one, gain_two = project(
        scalars, x_pieces, qkv_pieces, cosine, sine
    )

    slices = after(slices, qkv)
    out_own = slices[:, :out_rows].reshape(1, dp * out_rows, -1)
    out_mate = mate(out_own)
    mlp_slices = jnp.stack(
        [slices[place[h], out_rows : out_rows + hidden] for h in range(heads)]
    )
    mlp_slices = lax.all_to_all(mlp_slices, "head", split_axis=0, concat_axis=0, tiled=True)
    out_near = near(jnp.concatenate([out_own, out_mate]))
    att_0, log_0, home_0 = attend(scalars, after(qkv, out_mate))
    cot_near = after(cot_near, home_0)
    cot_far, cot_near_mate = far(cot_near[:1]), mate(cot_near)
    out_near = after(out_near, home_0)
    out_far, out_near_mate = far(out_near[:1]), mate(out_near)
    att_1, log_1, home = attend(scalars, after(qkv, cot_near, out_near), home_0)
    att_rows = exchange(home)
    out_far_mate, cot_far_mate = mate(after(out_far, home)), mate(after(cot_far, home))
    out_pieces = (out_own, out_mate, out_near, out_far, out_near_mate, out_far_mate)
    weight_mlp = jnp.moveaxis(after(mlp_slices, home), 0, 1).reshape(hidden, width)
    weight_mlp = jnp.pad(weight_mlp, ((0, padded - hidden), (0, 0)))
    residual, low2 = branch(
        scalars, out_pieces, after(att_rows, cot_far_mate, weight_mlp, weight_in), tokens, gain_two
    )

    low_own = low2[None]
    low_mate = mate(low_own)
    low_near = near(jnp.concatenate([low_own, low_mate]))
    *arrays, keep_a = mlp(
        (low_own, low_mate), (cot_own, cot_mate), weight_in, weight_mlp, 0, (2,)
    )
    low_near = after(low_near, keep_a)
    low_far, low_near_mate = far(low_near[:1]), mate(low_near)
    *arrays, keep_b = mlp((low_near,), (cot_near,), weight_in, weight_mlp, 2, (2,), arrays)
    low_far_mate = mate(after(low_far, keep_b))
    low2_all, cot_all, mixed, grad_lifted, keep_c, send = mlp(
        (low_far, low_near_mate, low_far_mate),
        (cot_far, cot_near_mate, cot_far_mate),
        weight_in,
        weight_mlp,
        4,
        (1, 4),
        arrays,
    )

    def over_tokens(left, right):
        return dot(flat(left), flat(right), ((0,), (0,)))

    def scatter(values):
        return lax.psum_scatter(values.astype(BF16), "dp", scatter_dimension=0, tiled=True)

    def columns_first(values):
        return jnp.moveaxis(values.reshape(values.shape[0], dp, -1), 1, 0)

    rows = seqs * block

    def by_rows(values):
        return values.reshape(values.shape[0], -1, width)

    keep_a, keep_b, keep_c, send = (by_rows(array) for array in (keep_a, keep_b, keep_c, send))
    met = mate(send)
    last = combine([(rows, [(keep_c, 0, 0), (met, 2, 0)])])
    last_far = far(last)
    grad_mlp = columns_first(over_tokens(after(mixed, last), cot_all)[:hidden]).astype(BF16)
    last_far = after(last_far, grad_mlp)
    grad_mlp = scatter(grad_mlp)[0]
    chip = combine(
        [(rows, [(keep_b, 0, 0), (met, 0, 0), (last_far, 0, 0)])],
        [(rows, [(keep_b, 1, 0), (met, 1, 0)])],
    )
    chip_near = near(chip)
    grad_in = over_tokens(low2_all, after(grad_lifted, chip)).astype(BF16)
    cut = 5 * rows
    mixed_flat = flat(after(mixed, chip))
    out_keep = dot(mixed_flat[:cut], weight_mlp).astype(BF16).reshape(5, rows, width)
    out_send = dot(mixed_flat[cut:], weight_mlp).astype(BF16).reshape(3, rows, width)
    chip_near = after(chip_near, grad_in, out_keep, out_send)
    grad_in = scatter(grad_in)
    home = mate(combine([(rows, [(keep_a, 1, 0), (chip_near, 1, 0)])])[0])
    out_met = mate(after(out_send, chip_near))
    grad_residual, grad_branch, home, gain2_sum = branch_back(
        scalars, out_pieces, keep_a, chip_near, home, residual, cotangent, gain_two
    )
    grad_home = exchange(home)

    rows_keep, rows_send = out_grad(scalars, after(att_rows, home), grad_branch)
    rows_met = mate(rows_send)
    few = rows_keep.shape[1]

    def ends(index, at, *more):
        kept = [(out_keep, index, 0)], [(rows_keep, index, 0)]
        if at is not None:
            kept[0].append((out_met, at, 0))
            kept[1].append((rows_met, at, 0))
        for array, where in more:
            kept[0].append((array, where, 0))
            kept[1].append((array, where, rows))
        return [(rows, kept[0]), (few, kept[1])]

    end_last = combine(ends(4, 2))
    grad_home = after(grad_home, end_last, grad_mlp)
    end_far = far(after(end_last, grad_home))
    keep_0, send_0, before = attend_back(
        scalars, qkv, grad_home, att_0, log_0, cosine, sine, weight_qkv, low1, 0
    )
    met_0 = mate(send_0)
    end_far, grad_in = lax.optimization_barrier((after(end_far, send_0), grad_in))
    in_parts = grad_in.reshape(2, rows_here, -1)
    in_cross = group.swap(pick(in_parts, 1 - at_c, 0), 4)
    end_chip = combine(ends(2, 0, (end_far, 0)), ends(3, 1))
    end_near = near(after(end_chip, in_cross))
    keep_1, send_1, grad_qkv = attend_back(
        scalars, qkv, after(grad_home, end_chip), att_1, log_1, cosine, sine,
        weight_qkv, low1, 1, before, gain_one, gain2_sum, dp=dp,
    )

    grad_qkv = scatter(grad_qkv.reshape(-1, grad_qkv.shape[2]))
    met_1 = mate(send_1)

    def both(index, at, *more):
        kept = [(keep_0, index, 0)], [(keep_1, index, 0)]
        if at is not None:
            kept[0].append((met_0, at, 0))
            kept[1].append((met_1, at, 0))
        for array, where in more:
            kept[0].append((array, where, 0))
            kept[1].append((array, where, block))
        return [(block, kept[0]), (block, kept[1])]

    last = combine(both(4, 2))
    last_far = far(last)
    end_home = mate(combine(ends(1, None, (after(end_near, last), 1))))
    last_far = after(last_far, end_home)
    chip = combine(both(2, 0, (last_far, 0)), both(3, 1))
    chip_near = near(chip)

    end_home = after(end_home, chip)
    grad_out = wide(rows_keep[0]) + wide(end_near[0, rows:]) + wide(end_home[0, rows:])
    grad_out = scatter(columns_first(grad_out.astype(BF16)))[0]
    result = wide(out_keep[0]) + wide(end_near[0, :rows]) + wide(end_home[0, :rows])
    result = (residual + result.reshape(residual.shape)).astype(BF16)
    grad_in = in_order(after(pick(in_parts, at_c, 0), chip), in_cross)
    late = at_h // half
    grad_in = jnp.stack([grad_in[..., :hidden], grad_in[..., padded : padded + hidden]])
    stays = pick(grad_in, late, 0)
    comes = group.swap(pick(grad_in, 1 - late, 0), half)
    grad_mlp = group.rows_back(after(grad_mlp, chip), place)
    grad_qkv = after(grad_qkv, chip)
    both_rows = 2 * rows_here
    qkv_parts = grad_qkv[:both_rows].reshape(2, rows_here, -1)
    gains = grad_qkv[both_rows:]
    cross = jnp.concatenate([pick(qkv_parts, 1 - at_c, 0), gains])
    cross = group.swap(cross, 4)
    chip_near = after(chip_near, comes, result, cross, grad_mlp)
    home = combine(both(1, None, (chip_near, 1)))
    cross, grad_out = lax.optimization_barrier((after(cross, home), grad_out))
    home = mate(home)
    grad_qkv = in_order(pick(qkv_parts, at_c, 0), cross[:rows_here])
    gains = (wide(gains) + wide(cross[rows_here:])).astype(BF16)
    gains = wide(gains) + sum(wide(group.swap(gains, bit)) for bit in range(1, heads))
    grad_out = wide(group.rows_back(grad_out, straight))
    grad_input = input_grad((keep_0, keep_1), chip_near, home, tokens, grad_residual, gain_one)

    grad_mlp = wide(grad_mlp)
    grad_in = jnp.where(
        late == 0, jnp.concatenate([stays, comes]), jnp.concatenate([comes, stays])
    )
    grad_in = wide(jnp.moveaxis(grad_in, 0, 1).reshape(rows_here, -1))

    per_device = width // (dp * parts)
    start = group.at * per_device
    grad_gain1, grad_gain2 = (
        lax.dynamic_slice_in_dim(gains[i], start, per_device, 0) for i in range(2)
    )
    grad_qkv = grad_qkv.reshape(2, rows_here, 3, own_width)
    grad_qkv = jnp.moveaxis(grad_qkv, 2, 0)
    odd = at_h % 2
    stays = pick(grad_qkv, odd + late, 0)
    core = group.swap(pick(grad_qkv, 1 - odd + late, 0), 1)
    chip = group.swap(pick(grad_qkv, 2 - 2 * late, 0), 2)
    grad_qkv = jnp.where(
        odd == 0, jnp.concatenate([stays, core, chip]), jnp.concatenate([chip, core, stays])
    )
    grad_qkv = wide(jnp.moveaxis(grad_qkv, 0, 1).reshape(rows_here, -1))

    return (
        result,
        grad_input,
        grad_qkv,
        grad_out,
        grad_in,
        grad_mlp,
        grad_gain1,
        grad_gain2,
    )


def local(tokens, cotangent, w_qkv, w_attn_out, w_in, w_mlp_out, norm_gain1, norm_gain2):
    args = (tokens, cotangent, w_qkv, w_attn_out, w_in, w_mlp_out, norm_gain1, norm_gain2)
    sizes = [lax.axis_size(axis) for axis in ("dp", "ctx", "head")]
    if sizes == [4, 2, 4] and tokens.shape[2] == 8 * 2 * HD and tokens.shape[1] % 16 == 0:
        return local_split(*args)
    return local_general(*args)


def solution(mesh):
    in_specs = (
        P("dp", ("ctx", "head"), None),
        P("dp", ("ctx", "head"), None),
        P(("dp", "ctx"), None),
        P(("dp", "ctx"), None),
        P(("dp", "ctx"), None),
        P(("dp", "ctx"), None),
        P(("dp", "ctx")),
        P(("dp", "ctx")),
    )
    out_specs = (
        P("dp", ("ctx", "head"), None),
        P("dp", ("ctx", "head"), None),
        P(("dp", "ctx"), "head"),
        P(("dp", "ctx"), "head"),
        P(("dp", "ctx"), "head"),
        P(("dp", "ctx"), "head"),
        P(("dp", "ctx", "head")),
        P(("dp", "ctx", "head")),
    )
    return jax.shard_map(local, mesh=mesh, in_specs=in_specs, out_specs=out_specs, check_vma=False)
```

```python
import functools
import math

import jax
import jax.numpy as jnp
from jax import lax
from jax.experimental import pallas as pl
from jax.experimental.pallas import tpu as pltpu
from jax.sharding import PartitionSpec as P

HD = 64


EPSILON = 1e-05
ROPE_BASE = 160000.0


def normalize(values):
    centre = jnp.mean(values, axis=-1, keepdims=True)
    shifted = values - centre
    spread = jnp.mean(shifted * shifted, axis=-1, keepdims=True)
    factor = lax.rsqrt(spread + EPSILON)
    return (shifted * factor, factor)


def norm_back(grad_normed, normed, factor):
    grad_centre = jnp.mean(grad_normed, axis=-1, keepdims=True)
    grad_along = jnp.mean(grad_normed * normed, axis=-1, keepdims=True)
    return (grad_normed - grad_centre - normed * grad_along) * factor


def rope_tables(positions, half_size):
    frequency = jnp.exp(
        jnp.arange(half_size, dtype=jnp.float32) * (-math.log(ROPE_BASE) / half_size)
    )
    angles = positions[:, None] * frequency[None, :]
    return (jnp.cos(angles), jnp.sin(angles))


def rotate(values, cosine, sine_table, direction):
    half_size = cosine.shape[-1]
    first_half = values[..., :half_size]
    second_half = values[..., half_size:]
    cos_part = cosine[:, None, :]
    sin_part = sine_table[:, None, :] * direction
    return jnp.concatenate(
        [
            first_half * cos_part - second_half * sin_part,
            second_half * cos_part + first_half * sin_part,
        ],
        axis=-1,
    )


def block_scores(queries4, keys_block, scale):
    keys4 = keys_block.reshape(
        keys_block.shape[0], keys_block.shape[1], queries4.shape[2], queries4.shape[3]
    )
    return (
        jnp.einsum("sqgd,skgd->sgqk", queries4, keys4, preferred_element_type=jnp.float32) * scale
    )


def attend_forward(queries4, keys_all, values_all, key_rows, scale):
    seqs_here, query_rows, groups, head_size = queries4.shape
    turns = keys_all.shape[1] // key_rows

    def statistics(turn, carry):
        row_peak, row_total = carry
        keys_block = lax.dynamic_slice_in_dim(keys_all, turn * key_rows, key_rows, 1)
        scores = block_scores(queries4, keys_block, scale)
        new_peak = jnp.maximum(row_peak, jnp.max(scores, axis=-1))
        row_total = row_total * jnp.exp(row_peak - new_peak) + jnp.sum(
            jnp.exp(scores - new_peak[..., None]), axis=-1
        )
        return (new_peak, row_total)

    start_peak = jnp.full((seqs_here, groups, query_rows), -1e30, jnp.float32)
    row_peak, row_total = lax.fori_loop(
        0, turns, statistics, (start_peak, jnp.zeros_like(start_peak))
    )
    log_total = row_peak + jnp.log(row_total)

    def accumulate(turn, running):
        keys_block = lax.dynamic_slice_in_dim(keys_all, turn * key_rows, key_rows, 1)
        values_block = lax.dynamic_slice_in_dim(values_all, turn * key_rows, key_rows, 1).reshape(
            seqs_here, key_rows, groups, head_size
        )
        weights = jnp.exp(block_scores(queries4, keys_block, scale) - log_total[..., None]).astype(
            jnp.bfloat16
        )
        return running + jnp.einsum(
            "sgqk,skgd->sqgd", weights, values_block, preferred_element_type=jnp.float32
        )

    attended = lax.fori_loop(
        0, turns, accumulate, jnp.zeros((seqs_here, query_rows, groups, head_size), jnp.float32)
    )
    return (attended, log_total)


def attend_backward(queries4, keys_all, values_all, grad_out4, log_total, along, key_rows, scale):
    seqs_here, query_rows, groups, head_size = queries4.shape
    length = keys_all.shape[1]
    width_group = groups * head_size
    turns = length // key_rows

    def step_back(turn, carry):
        grad_queries, grad_keys, grad_values = carry
        keys_block = lax.dynamic_slice_in_dim(keys_all, turn * key_rows, key_rows, 1)
        keys4 = keys_block.reshape(seqs_here, key_rows, groups, head_size)
        values4 = lax.dynamic_slice_in_dim(values_all, turn * key_rows, key_rows, 1).reshape(
            seqs_here, key_rows, groups, head_size
        )
        weights = jnp.exp(block_scores(queries4, keys_block, scale) - log_total[..., None])
        grad_weights = jnp.einsum(
            "sqgd,skgd->sgqk", grad_out4, values4, preferred_element_type=jnp.float32
        )
        grad_scores = (weights * (grad_weights - along[..., None])).astype(jnp.bfloat16)
        grad_queries = grad_queries + jnp.einsum(
            "sgqk,skgd->sqgd", grad_scores, keys4, preferred_element_type=jnp.float32
        )
        key_part = (
            jnp.einsum("sgqk,sqgd->skgd", grad_scores, queries4, preferred_element_type=jnp.float32)
            * scale
        )
        value_part = jnp.einsum(
            "sgqk,sqgd->skgd",
            weights.astype(jnp.bfloat16),
            grad_out4,
            preferred_element_type=jnp.float32,
        )
        grad_keys = lax.dynamic_update_slice_in_dim(
            grad_keys, key_part.reshape(seqs_here, key_rows, width_group), turn * key_rows, 1
        )
        grad_values = lax.dynamic_update_slice_in_dim(
            grad_values, value_part.reshape(seqs_here, key_rows, width_group), turn * key_rows, 1
        )
        return (grad_queries, grad_keys, grad_values)

    start = (
        jnp.zeros((seqs_here, query_rows, groups, head_size), jnp.float32),
        jnp.zeros((seqs_here, length, width_group), jnp.float32),
        jnp.zeros((seqs_here, length, width_group), jnp.float32),
    )
    grad_queries, grad_keys, grad_values = lax.fori_loop(0, turns, step_back, start)
    return (grad_queries * scale, grad_keys, grad_values)


def local_general(tokens, cotangent, w_qkv, w_attn_out, w_in, w_mlp_out, norm_gain1, norm_gain2):
    seqs_here, block_rows, width = tokens.shape
    count_rows = seqs_here * block_rows
    heads_all = width // HD
    head_devices = lax.axis_size("head")
    group_devices = lax.axis_size(("dp", "ctx"))
    groups = heads_all // head_devices
    width_group = groups * HD
    scale = HD ** (-0.5)
    ff_width = w_in.shape[1] // 2
    full_qkv, full_out, full_in, full_mlp, gain_one, gain_two = (
        lax.all_gather(w_qkv, ("dp", "ctx"), axis=0, tiled=True),
        lax.all_gather(w_attn_out, ("dp", "ctx"), axis=0, tiled=True),
        lax.all_gather(w_in, ("dp", "ctx"), axis=0, tiled=True),
        lax.all_gather(w_mlp_out, ("dp", "ctx"), axis=0, tiled=True),
        lax.all_gather(norm_gain1, ("dp", "ctx"), axis=0, tiled=True),
        lax.all_gather(norm_gain2, ("dp", "ctx"), axis=0, tiled=True),
    )
    x_in = tokens.astype(jnp.float32).reshape(count_rows, width)
    normed1, factor1 = normalize(x_in)
    lowered1 = (normed1 * gain_one.astype(jnp.float32)).astype(jnp.bfloat16)
    projected = jnp.dot(lowered1, full_qkv, preferred_element_type=jnp.float32).reshape(
        seqs_here, block_rows, 3, heads_all, HD
    )
    first_pos = (lax.axis_index("ctx") * head_devices + lax.axis_index("head")) * block_rows
    positions = (first_pos + jnp.arange(block_rows, dtype=jnp.int32)).astype(jnp.float32)
    cosine, sine_table = rope_tables(positions, HD // 2)
    queries = (
        rotate(projected[:, :, 0], cosine, sine_table, 1.0)
        .astype(jnp.bfloat16)
        .reshape(seqs_here, block_rows, width)
    )
    keys_local = (
        rotate(projected[:, :, 1], cosine, sine_table, 1.0)
        .astype(jnp.bfloat16)
        .reshape(seqs_here, block_rows, width)
    )
    values_local = projected[:, :, 2].astype(jnp.bfloat16).reshape(seqs_here, block_rows, width)
    queries_h, keys_h, values_h = (
        lax.all_to_all(queries, "head", split_axis=2, concat_axis=1, tiled=True),
        lax.all_to_all(keys_local, "head", split_axis=2, concat_axis=1, tiled=True),
        lax.all_to_all(values_local, "head", split_axis=2, concat_axis=1, tiled=True),
    )
    query_rows = queries_h.shape[1]
    queries4 = queries_h.reshape(seqs_here, query_rows, groups, HD)
    keys_all, values_all = (
        lax.all_gather(keys_h, "ctx", axis=1, tiled=True),
        lax.all_gather(values_h, "ctx", axis=1, tiled=True),
    )
    key_rows = math.gcd(keys_all.shape[1], 1024)
    attended, log_total = attend_forward(queries4, keys_all, values_all, key_rows, scale)
    attended_low = attended.astype(jnp.bfloat16).reshape(seqs_here, query_rows, width_group)
    back_rows = lax.all_to_all(
        attended_low, "head", split_axis=1, concat_axis=2, tiled=True
    ).reshape(count_rows, width)
    residual = x_in + jnp.dot(back_rows, full_out, preferred_element_type=jnp.float32)
    normed2, factor2 = normalize(residual)
    lowered2 = (normed2 * gain_two.astype(jnp.float32)).astype(jnp.bfloat16)
    lifted = jnp.dot(lowered2, full_in, preferred_element_type=jnp.float32)
    first_part = lifted[:, :ff_width]
    second_part = lifted[:, ff_width:]
    activated, gelu_pullback = jax.vjp(
        lambda entries: jax.nn.gelu(entries, approximate=False), first_part
    )
    mixed = (activated * second_part).astype(jnp.bfloat16)
    result = (residual + jnp.dot(mixed, full_mlp, preferred_element_type=jnp.float32)).astype(
        jnp.bfloat16
    )
    full_qkv, full_out, full_in, full_mlp, gain_one, gain_two = (
        lax.all_gather(w_qkv, ("dp", "ctx"), axis=0, tiled=True),
        lax.all_gather(w_attn_out, ("dp", "ctx"), axis=0, tiled=True),
        lax.all_gather(w_in, ("dp", "ctx"), axis=0, tiled=True),
        lax.all_gather(w_mlp_out, ("dp", "ctx"), axis=0, tiled=True),
        lax.all_gather(norm_gain1, ("dp", "ctx"), axis=0, tiled=True),
        lax.all_gather(norm_gain2, ("dp", "ctx"), axis=0, tiled=True),
    )
    keys_all, values_all = (
        lax.all_gather(keys_h, "ctx", axis=1, tiled=True),
        lax.all_gather(values_h, "ctx", axis=1, tiled=True),
    )
    grad_top = cotangent.reshape(count_rows, width)
    grad_mlp = jnp.einsum("nf,nd->fd", mixed, grad_top, preferred_element_type=jnp.float32)
    grad_mixed = jnp.einsum("nd,fd->nf", grad_top, full_mlp, preferred_element_type=jnp.float32)
    grad_first = gelu_pullback(grad_mixed * second_part)[0]
    grad_lifted = jnp.concatenate([grad_first, grad_mixed * activated], axis=-1).astype(
        jnp.bfloat16
    )
    grad_inner = jnp.einsum("nd,nf->df", lowered2, grad_lifted, preferred_element_type=jnp.float32)
    grad_lowered2 = jnp.einsum(
        "nf,df->nd", grad_lifted, full_in, preferred_element_type=jnp.float32
    )
    grad_two = jnp.sum(grad_lowered2 * normed2, axis=0)
    grad_residual = grad_top.astype(jnp.float32) + norm_back(
        grad_lowered2 * gain_two.astype(jnp.float32), normed2, factor2
    )
    grad_branch = grad_residual.astype(jnp.bfloat16)
    grad_outproj = jnp.einsum(
        "nd,ne->de", back_rows, grad_branch, preferred_element_type=jnp.float32
    )
    grad_attended = jnp.einsum(
        "ne,de->nd", grad_branch, full_out, preferred_element_type=jnp.float32
    ).astype(jnp.bfloat16)
    grad_attended_h = lax.all_to_all(
        grad_attended.reshape(seqs_here, block_rows, width),
        "head",
        split_axis=2,
        concat_axis=1,
        tiled=True,
    )
    grad_out4 = grad_attended_h.reshape(seqs_here, query_rows, groups, HD)
    along = jnp.transpose(jnp.sum(grad_out4.astype(jnp.float32) * attended, axis=-1), (0, 2, 1))
    grad_queries, grad_keys_all, grad_values_all = attend_backward(
        queries4, keys_all, values_all, grad_out4, log_total, along, key_rows, scale
    )
    grad_keys_sum, grad_values_sum = (
        lax.psum_scatter(
            grad_keys_all.astype(jnp.bfloat16), "ctx", scatter_dimension=1, tiled=True
        ).astype(jnp.float32),
        lax.psum_scatter(
            grad_values_all.astype(jnp.bfloat16), "ctx", scatter_dimension=1, tiled=True
        ).astype(jnp.float32),
    )
    grad_q_low = grad_queries.astype(jnp.bfloat16).reshape(seqs_here, query_rows, width_group)
    grad_q_tok, grad_k_tok, grad_v_tok = (
        lax.all_to_all(grad_q_low, "head", split_axis=1, concat_axis=2, tiled=True),
        lax.all_to_all(
            grad_keys_sum.astype(jnp.bfloat16), "head", split_axis=1, concat_axis=2, tiled=True
        ),
        lax.all_to_all(
            grad_values_sum.astype(jnp.bfloat16), "head", split_axis=1, concat_axis=2, tiled=True
        ),
    )
    unrot_q = rotate(
        grad_q_tok.astype(jnp.float32).reshape(seqs_here, block_rows, heads_all, HD),
        cosine,
        sine_table,
        -1.0,
    )
    unrot_k = rotate(
        grad_k_tok.astype(jnp.float32).reshape(seqs_here, block_rows, heads_all, HD),
        cosine,
        sine_table,
        -1.0,
    )
    grad_projected = jnp.concatenate(
        [
            unrot_q.reshape(count_rows, width),
            unrot_k.reshape(count_rows, width),
            grad_v_tok.astype(jnp.float32).reshape(count_rows, width),
        ],
        axis=-1,
    ).astype(jnp.bfloat16)
    grad_project = jnp.einsum(
        "nd,nf->df", lowered1, grad_projected, preferred_element_type=jnp.float32
    )
    grad_lowered1 = jnp.einsum(
        "nf,df->nd", grad_projected, full_qkv, preferred_element_type=jnp.float32
    )
    grad_one = jnp.sum(grad_lowered1 * normed1, axis=0)
    grad_input = grad_residual + norm_back(
        grad_lowered1 * gain_one.astype(jnp.float32), normed1, factor1
    )
    pieces_one = grad_one.reshape(group_devices, head_devices, -1)
    pieces_two = grad_two.reshape(group_devices, head_devices, -1)
    part_qkv, part_out, part_in, part_mlp, part_one, part_two = (
        lax.psum_scatter(
            grad_project.astype(jnp.bfloat16), ("dp", "ctx"), scatter_dimension=0, tiled=True
        ).astype(jnp.float32),
        lax.psum_scatter(
            grad_outproj.astype(jnp.bfloat16), ("dp", "ctx"), scatter_dimension=0, tiled=True
        ).astype(jnp.float32),
        lax.psum_scatter(
            grad_inner.astype(jnp.bfloat16), ("dp", "ctx"), scatter_dimension=0, tiled=True
        ).astype(jnp.float32),
        lax.psum_scatter(
            grad_mlp.astype(jnp.bfloat16), ("dp", "ctx"), scatter_dimension=0, tiled=True
        ).astype(jnp.float32),
        lax.psum_scatter(
            pieces_one.astype(jnp.bfloat16), ("dp", "ctx"), scatter_dimension=0, tiled=True
        ).astype(jnp.float32),
        lax.psum_scatter(
            pieces_two.astype(jnp.bfloat16), ("dp", "ctx"), scatter_dimension=0, tiled=True
        ).astype(jnp.float32),
    )
    final_qkv, final_out, final_in, final_mlp, final_one, final_two = (
        lax.psum_scatter(
            part_qkv.astype(jnp.bfloat16), "head", scatter_dimension=1, tiled=True
        ).astype(jnp.float32),
        lax.psum_scatter(
            part_out.astype(jnp.bfloat16), "head", scatter_dimension=1, tiled=True
        ).astype(jnp.float32),
        lax.psum_scatter(
            part_in.astype(jnp.bfloat16), "head", scatter_dimension=1, tiled=True
        ).astype(jnp.float32),
        lax.psum_scatter(
            part_mlp.astype(jnp.bfloat16), "head", scatter_dimension=1, tiled=True
        ).astype(jnp.float32),
        lax.psum_scatter(
            part_one.astype(jnp.bfloat16), "head", scatter_dimension=1, tiled=True
        ).astype(jnp.float32),
        lax.psum_scatter(
            part_two.astype(jnp.bfloat16), "head", scatter_dimension=1, tiled=True
        ).astype(jnp.float32),
    )
    return (
        result.reshape(seqs_here, block_rows, width),
        grad_input.reshape(seqs_here, block_rows, width),
        final_qkv,
        final_out,
        final_in,
        final_mlp,
        final_one.reshape(-1),
        final_two.reshape(-1),
    )


F32 = jnp.float32
BF16 = jnp.bfloat16
GROUP = ("ctx", "head")


def dot(left, right, dims=((1,), (0,))):
    return lax.dot_general(left, right, (dims, ((), ())), preferred_element_type=F32)


def wide(values):
    return values.astype(F32)


def flat(values):
    return values.reshape(-1, values.shape[-1])


def lane_rotate(values, cosine, sine_signed):
    lane = lax.broadcasted_iota(jnp.int32, values.shape, 1)
    width = values.shape[1]
    partner = jnp.where(
        lane % HD < HD // 2,
        pltpu.roll(values, width - HD // 2, 1),
        pltpu.roll(values, HD // 2, 1),
    )
    return values * cosine + partner * sine_signed


def head_masks(shape):
    lane = lax.broadcasted_iota(jnp.int32, shape, 1)
    return [lane // HD == head for head in range(shape[1] // HD)]


def params(mebibytes):
    return pltpu.CompilerParams(vmem_limit_bytes=mebibytes * 1024 * 1024)


COST = pl.CostEstimate(flops=1 << 20, transcendentals=0, bytes_accessed=1 << 16)


def whole(array):
    return pl.BlockSpec(array.shape, lambda *_: (0,) * len(array.shape))


SCALARS = pl.BlockSpec(memory_space=pltpu.SMEM)


def project_kernel(place_ref, *refs):
    pieces, weights = refs[:6], refs[6:10]
    cos_ref, sin_ref, low_ref, qkv_ref, w_ref, gain1_ref, gain2_ref, rows_ref = refs[10:]
    block, part = pieces[0].shape[2], w_ref.shape[1] // 3
    rows = gain1_ref.shape[1] // 8

    @pl.when(pl.program_id(0) == 0)
    def _():
        for step, piece in enumerate(weights):
            for turn in range(2):
                at = 2 * (place_ref[8] ^ step) + (place_ref[9] ^ turn)
                w_ref[pl.ds(pl.multiple_of(at * rows, rows), rows), :] = piece[turn, :rows]
                gains = piece[turn, rows:].astype(F32)
                rows_ref[0, pl.ds(at, 1), :] = gains[:1, :rows]
                rows_ref[1, pl.ds(at, 1), :] = gains[1:2, :rows]
        for out, at in ((gain1_ref, 0), (gain2_ref, 1)):
            for row in range(8):
                out[:, row * rows : (row + 1) * rows] = rows_ref[at, row : row + 1, :]

    gain = gain1_ref[...]
    index = 0
    for piece in pieces:
        for inner in range(piece.shape[0]):
            normed, _ = normalize(piece[inner, 0].astype(F32))
            low_ref[index, 0] = (normed * gain).astype(BF16)
            index += 1
    projected = dot(flat(low_ref[:, 0]), w_ref[...])
    cosine, sine = cos_ref[...], sin_ref[...]
    shape = (8, block, part)
    qkv_ref[:, 0, :, :part] = (
        (lane_rotate(projected[:, :part], cosine, sine) * HD**-0.5).astype(BF16).reshape(shape)
    )
    qkv_ref[:, 0, :, part : 2 * part] = (
        lane_rotate(projected[:, part : 2 * part], cosine, sine).astype(BF16).reshape(shape)
    )
    qkv_ref[:, 0, :, 2 * part :] = projected[:, 2 * part :].astype(BF16).reshape(shape)


def project(place, pieces, weights, cosine, sine):
    seqs, block, width = pieces[0].shape[1:]
    own = weights[0].shape[2]

    def by_seq(lead, last):
        return pl.BlockSpec((lead, 1, block, last), lambda s: (0, s, 0, 0))

    return pl.pallas_call(
        project_kernel,
        grid=(seqs,),
        in_specs=[SCALARS]
        + [by_seq(piece.shape[0], width) for piece in pieces]
        + [whole(w) for w in weights]
        + [whole(cosine), whole(sine)],
        out_specs=(
            by_seq(8, width),
            by_seq(8, own),
            pl.BlockSpec((width, own), lambda s: (0, 0)),
            pl.BlockSpec((1, width), lambda s: (0, 0)),
            pl.BlockSpec((1, width), lambda s: (0, 0)),
        ),
        out_shape=(
            jax.ShapeDtypeStruct((8, seqs, block, width), BF16),
            jax.ShapeDtypeStruct((8, seqs, block, own), BF16),
            jax.ShapeDtypeStruct((width, own), BF16),
            jax.ShapeDtypeStruct((1, width), F32),
            jax.ShapeDtypeStruct((1, width), F32),
        ),
        scratch_shapes=[pltpu.VMEM((2, 8, width // 8), F32)],
        compiler_params=params(60),
        cost_estimate=COST,
        name="project",
    )(place, *pieces, *weights, cosine, sine)


def attend_kernel(place_ref, q_ref, k_ref, v_ref, *refs):
    att_ref, log_ref, home_ref = refs[-3:]
    step, seq = pl.program_id(0), len(refs) - 3
    if seq:

        @pl.when(step == 0)
        def _():
            home_ref[:, :1] = refs[0][...]

    queries, keys, values = flat(q_ref[...]), flat(k_ref[...]), flat(v_ref[...])
    attended = jnp.zeros(queries.shape, F32)
    logs = jnp.zeros(queries.shape, F32)
    for mask in head_masks(queries.shape):
        scores = dot(jnp.where(mask, queries, 0), keys, ((1,), (1,)))
        peak = jnp.max(scores, axis=1, keepdims=True)
        weights = jnp.exp(scores - peak)
        total = jnp.sum(weights, axis=1, keepdims=True)
        mixed = dot(weights.astype(BF16), values) * (1.0 / total)
        attended = jnp.where(mask, mixed, attended)
        logs = jnp.where(mask, peak + jnp.log(total), logs)
    att_ref[...] = attended.reshape(att_ref.shape)
    log_ref[...] = logs.reshape(log_ref.shape)
    low = attended.astype(BF16).reshape(att_ref.shape)
    for inner in range(2):
        home_ref[place_ref[2 * step + inner], seq] = low[inner, 0]


def attend(place, qkv, *home):
    _, _, block, own = qkv.shape
    part, seq = own // 3, len(home)
    rows = pl.BlockSpec((2, 1, block, part), lambda i: (i, 0, 0, 0))
    shape = (8, 1, block, part)
    return pl.pallas_call(
        attend_kernel,
        grid=(4,),
        in_specs=[
            SCALARS,
            pl.BlockSpec((2, 1, block, part), lambda i: (i, seq, 0, 0)),
            pl.BlockSpec((8, 1, block, part), lambda i: (0, seq, 0, 1)),
            pl.BlockSpec((8, 1, block, part), lambda i: (0, seq, 0, 2)),
            *[whole(h) for h in home],
        ],
        out_specs=(
            rows,
            rows,
            pl.BlockSpec((8, 1 + seq, block, part), lambda i: (0, 0, 0, 0)),
        ),
        out_shape=(
            jax.ShapeDtypeStruct(shape, F32),
            jax.ShapeDtypeStruct(shape, F32),
            jax.ShapeDtypeStruct((8, 1 + seq, block, part), BF16),
        ),
        compiler_params=params(24),
        cost_estimate=COST,
        name="attend",
    )(place, qkv, qkv, qkv, *home)


def branch_kernel(place_ref, *refs):
    pieces = refs[:6]
    rows_ref, tokens_ref, gain_ref, residual_ref, low_ref, side_ref, total_ref = refs[6:]
    heads = rows_ref.shape[0] // 2
    for c in range(2):
        side_ref[c] = jnp.concatenate([flat(rows_ref[c * heads + d]) for d in range(heads)], axis=1)
    total_ref[...] = flat(wide(tokens_ref[...]))
    index = 0
    for piece in pieces:
        n = piece.shape[2]
        for inner in range(piece.shape[0]):
            at = place_ref[index]
            columns = pl.ds(pl.multiple_of((at % heads) * n, n), n)
            total_ref[:, columns] += dot(side_ref[at // heads], piece[inner])
            index += 1
    total = total_ref[...]
    normed, _ = normalize(total)
    residual_ref[...] = total.reshape(residual_ref.shape)
    low_ref[...] = (normed * gain_ref[...]).astype(BF16).reshape(low_ref.shape)


def branch(place, pieces, rows, tokens, gain):
    args = (*pieces, rows, tokens, gain)
    seqs, block, width = tokens.shape
    return pl.pallas_call(
        branch_kernel,
        in_specs=[SCALARS] + [whole(a) for a in args],
        out_shape=(
            jax.ShapeDtypeStruct(tokens.shape, F32),
            jax.ShapeDtypeStruct(tokens.shape, BF16),
        ),
        scratch_shapes=[
            pltpu.VMEM((2, seqs * block, pieces[0].shape[1]), BF16),
            pltpu.VMEM((seqs * block, width), F32),
        ],
        compiler_params=params(16),
        cost_estimate=COST,
        name="branch",
    )(place, *args)


def combine(*groups):
    parts = [part for group in groups for _, parts in group for part in parts]
    rows = sum(count for count, _ in groups[0])
    width = parts[0][0].shape[2]

    def kernel(*refs):
        at = 0
        for k, group in enumerate(groups):
            row = 0
            for count, terms in group:
                total = 0.0
                for _, _, start in terms:
                    total = total + wide(refs[at][0, start : start + count])
                    at += 1
                refs[-1][k, row : row + count] = total.astype(BF16)
                row += count

    return pl.pallas_call(
        kernel,
        grid=(1,),
        in_specs=[
            pl.BlockSpec((1, *array.shape[1:]), lambda *_, index=index: (index, 0, 0))
            for array, index, _ in parts
        ],
        out_specs=pl.BlockSpec((len(groups), rows, width), lambda *_: (0, 0, 0)),
        out_shape=jax.ShapeDtypeStruct((len(groups), rows, width), BF16),
        compiler_params=params(16),
        cost_estimate=COST,
        name="combine",
    )(*[array for array, _, _ in parts])


def mlp_kernel(*refs, count, ends):
    pieces, tops = refs[:count], refs[count : 2 * count]
    w_ref, out_w_ref = refs[2 * count : 2 * count + 2]
    low_ref, top_ref, mixed_ref, lifted_ref, *out_refs = refs[-4 - len(ends) :]
    step = pl.program_id(0)
    start = 0
    for piece, top in zip(pieces, tops):

        @pl.when((step >= start) & (step < start + piece.shape[0]))
        def _(piece=piece, top=top, start=start):
            low_ref[0] = piece[step - start]
            top_ref[0] = top[step - start]

        start += piece.shape[0]

    hidden = w_ref.shape[1] // 2
    lifted = dot(flat(low_ref[...]), w_ref[...])
    first, second = lifted[:, :hidden], lifted[:, hidden:]
    grad_mixed = dot(flat(top_ref[...]), out_w_ref[...], ((1,), (1,)))
    gate = 0.5 * (1.0 + lax.erf(first * (0.5**0.5)))
    slope = gate + first * jnp.exp(first * first * -0.5) * ((2.0 * math.pi) ** -0.5)
    activated = first * gate
    mixed_ref[...] = (activated * second).astype(BF16).reshape(mixed_ref.shape)
    grad = jnp.concatenate(
        [(grad_mixed * second * slope).astype(BF16), (grad_mixed * activated).astype(BF16)],
        axis=1,
    )
    lifted_ref[...] = grad.reshape(lifted_ref.shape)
    partial = dot(grad, w_ref[...], ((1,), (1,))).astype(BF16).reshape(low_ref.shape)
    start = 0
    for out, end in zip(out_refs, ends):

        @pl.when((step >= start) & (step < end))
        def _(out=out):
            out[...] = partial

        start = end


def mlp(pieces, tops, w, out_w, base, ends, earlier=()):
    seqs, block, width = pieces[0].shape[1:]
    hidden = w.shape[1] // 2
    whole_in = (*pieces, *tops, w, out_w)

    def rows(last):
        return pl.BlockSpec((1, seqs, block, last), lambda i: (i + base, 0, 0, 0))

    def within(start, end):
        return pl.BlockSpec(
            (1, seqs, block, width),
            lambda i: (jnp.clip(i - start, 0, end - start - 1), 0, 0, 0),
        )

    starts = (0, *ends[:-1])
    lasts = (width, width, hidden, 2 * hidden)
    return pl.pallas_call(
        functools.partial(mlp_kernel, count=len(pieces), ends=ends),
        grid=(ends[-1],),
        in_specs=[whole(array) for array in whole_in]
        + [pl.BlockSpec(memory_space=pl.ANY)] * len(earlier),
        out_specs=(
            *[rows(last) for last in lasts],
            *[within(start, end) for start, end in zip(starts, ends)],
        ),
        out_shape=(
            *[jax.ShapeDtypeStruct((8, seqs, block, last), BF16) for last in lasts],
            *[
                jax.ShapeDtypeStruct((end - start, seqs, block, width), BF16)
                for start, end in zip(starts, ends)
            ],
        ),
        input_output_aliases={len(whole_in) + at: at for at in range(len(earlier))},
        compiler_params=params(32),
        cost_estimate=COST,
        name="mlp",
    )(*whole_in, *earlier)


def out_grad_kernel(place_ref, rows_ref, grad_ref, keep_ref, send_ref):
    grads = flat(grad_ref[...])
    for index in range(8):
        part = dot(flat(rows_ref[place_ref[index]]), grads, ((0,), (0,))).astype(BF16)
        if index < 5:
            keep_ref[index] = part
        else:
            send_ref[index - 5] = part


def out_grad(place, rows, grads):
    part, width = rows.shape[-1], grads.shape[-1]
    return pl.pallas_call(
        out_grad_kernel,
        in_specs=[SCALARS, whole(rows), whole(grads)],
        out_shape=(
            jax.ShapeDtypeStruct((5, part, width), BF16),
            jax.ShapeDtypeStruct((3, part, width), BF16),
        ),
        compiler_params=params(16),
        cost_estimate=COST,
        name="out_grad",
    )(place, rows, grads)


def branch_back_kernel(place_ref, *refs):
    pieces = refs[:6]
    keep_ref, near_ref, own_ref, residual_ref, top_ref, gain_ref = refs[6:12]
    grad_ref, branch_ref, home_ref, sum_ref, low_ref, side_ref = refs[12:]
    grad_low = wide(flat(keep_ref[...])) + wide(flat(near_ref[...])) + wide(flat(own_ref[...]))
    normed, factor = normalize(flat(residual_ref[...]))
    sum_ref[...] = jnp.sum(grad_low * normed, axis=0, keepdims=True)
    grad = flat(wide(top_ref[...])) + norm_back(grad_low * gain_ref[...], normed, factor)
    grad_ref[...] = grad.reshape(grad_ref.shape)
    low_ref[...] = grad.astype(BF16)
    branch_ref[...] = low_ref[...].reshape(branch_ref.shape)
    heads = home_ref.shape[0] // 2
    side_ref[...] = jnp.zeros_like(side_ref)
    index = 0
    for piece in pieces:
        n = piece.shape[2]
        for inner in range(piece.shape[0]):
            at = place_ref[index]
            columns = pl.ds(pl.multiple_of((at % heads) * n, n), n)
            side_ref[at // heads] += dot(low_ref[:, columns], piece[inner], ((1,), (1,)))
            index += 1
    part = home_ref.shape[3]
    for c in range(2):
        for d in range(heads):
            home = side_ref[c, :, d * part : (d + 1) * part].astype(BF16)
            home_ref[c * heads + d] = home.reshape(home_ref.shape[1:])


def branch_back(place, pieces, keep, near, own, residual, top, gain):
    args = (*pieces, keep, near, own, residual, top, gain)
    seqs, block, width = residual.shape
    tall = pieces[0].shape[1]
    shapes = (
        jax.ShapeDtypeStruct(residual.shape, F32),
        jax.ShapeDtypeStruct(residual.shape, BF16),
        jax.ShapeDtypeStruct((8, seqs, block, tall // 4), BF16),
        jax.ShapeDtypeStruct((1, width), F32),
    )
    return pl.pallas_call(
        branch_back_kernel,
        grid=(1,),
        in_specs=[SCALARS]
        + [whole(piece) for piece in pieces]
        + [pl.BlockSpec((1, seqs * block, width), lambda *_: (0, 0, 0))] * 2
        + [whole(a) for a in args[8:]],
        out_specs=tuple(whole(shape) for shape in shapes),
        out_shape=shapes,
        scratch_shapes=[
            pltpu.VMEM((seqs * block, width), BF16),
            pltpu.VMEM((2, seqs * block, tall), F32),
        ],
        compiler_params=params(24),
        cost_estimate=COST,
        name="branch_back",
    )(place, *args)


def attend_back_kernel(
    place_ref, q_ref, k_ref, v_ref, grad_ref, att_ref, log_ref, cosq_ref, sinq_ref, cos_ref,
    sin_ref, w_ref, low_ref, *refs, seq, last,
):
    if last:
        before_ref, gain1_ref, gain2_ref, keep_ref, send_ref, grad_w_ref, *scratch = refs
    else:
        keep_ref, send_ref, before_ref, *scratch = refs
    proj_ref, sum_k, sum_v = scratch
    step = pl.program_id(0)
    block, part = q_ref.shape[2], q_ref.shape[3]

    @pl.when(step == 0)
    def _():
        sum_k[...] = jnp.zeros_like(sum_k)
        sum_v[...] = jnp.zeros_like(sum_v)

    queries, keys, values = flat(q_ref[...]), flat(k_ref[...]), flat(v_ref[...])
    grads = jnp.concatenate([grad_ref[place_ref[2 * step + inner], seq] for inner in range(2)])
    along = (grads.astype(F32) * flat(att_ref[...])).T
    logs = flat(log_ref[...]).T
    grad_queries = jnp.zeros(queries.shape, F32)
    for head, mask in enumerate(head_masks(queries.shape)):
        own_q = jnp.where(mask, queries, 0)
        own_g = jnp.where(mask, grads, 0)
        scores = dot(keys, own_q, ((1,), (1,)))
        weights = jnp.exp(scores - logs[head * HD : head * HD + 1])
        lifted = dot(values, own_g, ((1,), (1,)))
        row = jnp.sum(along[head * HD : (head + 1) * HD], axis=0, keepdims=True)
        grad_scores = (weights * (lifted - row)).astype(BF16)
        sum_k[...] += dot(grad_scores, own_q)
        sum_v[...] += dot(weights.astype(BF16), own_g)
        grad_queries = jnp.where(mask, dot(grad_scores, keys, ((0,), (0,))), grad_queries)
    grad_queries = lane_rotate(grad_queries * HD**-0.5, cosq_ref[...], -sinq_ref[...])
    rows = pl.multiple_of(step * 2 * block, 2 * block)
    proj_ref[pl.ds(rows, 2 * block), :part] = grad_queries.astype(BF16)

    @pl.when(step == 3)
    def _():
        grad_keys = lane_rotate(sum_k[...], cos_ref[...], -sin_ref[...])
        proj_ref[:, part : 2 * part] = grad_keys.astype(BF16)
        proj_ref[:, 2 * part :] = sum_v[...].astype(BF16)
        partial = dot(proj_ref[...], w_ref[...], ((1,), (1,))).astype(BF16)
        keep_ref[...] = partial[: 5 * block].reshape(5, block, -1)
        send_ref[...] = partial[5 * block :].reshape(3, block, -1)
        grad_w = dot(proj_ref[...], flat(low_ref[...]), ((0,), (0,)))
        if last:
            grad_w = (grad_w + before_ref[...]).T
            along_w = jnp.sum(grad_w * wide(w_ref[...]), axis=1, keepdims=True)
            along_w = jnp.broadcast_to(along_w, (w_ref.shape[0], 128)).T[:1] / gain1_ref[...]
            row = lax.broadcasted_iota(jnp.int32, (GAIN_ROWS, w_ref.shape[0]), 0)
            gains = jnp.where(row == 0, along_w, jnp.where(row == 1, gain2_ref[...], 0.0))
            n = grad_w_ref.shape[1] - GAIN_ROWS
            for at in range(grad_w_ref.shape[0]):
                part_rows = slice(at * n, (at + 1) * n)
                grad_w_ref[at, :n] = grad_w[part_rows].astype(BF16)
                grad_w_ref[at, n:, :n] = gains[:, part_rows].astype(BF16)
                rest = grad_w_ref.shape[2] - n
                grad_w_ref[at, n:, n:] = jnp.zeros((GAIN_ROWS, rest), BF16)
        else:
            before_ref[...] = grad_w


GAIN_ROWS = 16


def attend_back(place, qkv, grads, attended, logs, cosine, sine, w, low, seq, *before, dp=1):
    _, _, block, own = qkv.shape
    part, width = own // 3, w.shape[0]
    last = len(before) > 0
    rows = pl.BlockSpec((2, 1, block, part), lambda i: (i, 0, 0, 0))
    angles = pl.BlockSpec((2 * block, part), lambda i: (i, 0))

    def full(*shape):
        return pl.BlockSpec(shape, lambda i: (0,) * len(shape))

    args = [place, qkv, qkv, qkv, grads, attended, logs, cosine, sine, cosine, sine, w, low]
    in_specs = [
        SCALARS,
        pl.BlockSpec((2, 1, block, part), lambda i: (i, seq, 0, 0)),
        pl.BlockSpec((8, 1, block, part), lambda i: (0, seq, 0, 1)),
        pl.BlockSpec((8, 1, block, part), lambda i: (0, seq, 0, 2)),
        whole(grads),
        rows,
        rows,
        angles,
        angles,
        whole(cosine),
        whole(sine),
        whole(w),
        pl.BlockSpec((8, 1, block, width), lambda i: (0, seq, 0, 0)),
    ]
    shapes = [((5, block, width), BF16), ((3, block, width), BF16)]
    if last:
        args += before
        in_specs += [whole(array) for array in before]
        shapes += [((dp, width // dp + GAIN_ROWS, own), BF16)]
    else:
        shapes += [((own, width), F32)]
    return pl.pallas_call(
        functools.partial(attend_back_kernel, seq=seq, last=last),
        grid=(4,),
        in_specs=in_specs,
        out_specs=tuple(full(*shape) for shape, _ in shapes),
        out_shape=tuple(jax.ShapeDtypeStruct(shape, kind) for shape, kind in shapes),
        scratch_shapes=[
            pltpu.VMEM((8 * block, own), BF16),
            pltpu.VMEM((8 * block, part), F32),
            pltpu.VMEM((8 * block, part), F32),
        ],
        compiler_params=params(60),
        cost_estimate=COST,
        name="attend_back",
    )(*args)


def input_grad_kernel(*refs):
    keeps, (near_ref, own_ref, tokens_ref, residual_ref, gain_ref, out_ref) = refs[:-6], refs[-6:]
    block = tokens_ref.shape[1]
    for seq, keep in enumerate(keeps):
        rows = slice(seq * block, (seq + 1) * block)
        grad = wide(keep[0, :block]) + wide(near_ref[0, rows]) + wide(own_ref[0, rows])
        normed, factor = normalize(wide(tokens_ref[seq]))
        out_ref[seq] = residual_ref[seq] + norm_back(grad * gain_ref[...], normed, factor)


def input_grad(keeps, near, own, tokens, residual, gain):
    rest = (own, tokens, residual, gain)
    return pl.pallas_call(
        input_grad_kernel,
        grid=(1,),
        in_specs=[
            pl.BlockSpec((1, *array.shape[1:]), lambda *_: (0, 0, 0)) for array in (*keeps, near)
        ]
        + [whole(array) for array in rest],
        out_specs=whole(residual),
        out_shape=jax.ShapeDtypeStruct(residual.shape, F32),
        compiler_params=params(16),
        cost_estimate=COST,
        name="input_grad",
    )(*keeps, near, *rest)


class Group:
    def __init__(self):
        self.heads = lax.axis_size("head")
        self.dp = lax.axis_size("dp")
        self.ctx_at = lax.axis_index("ctx")
        self.head_at = lax.axis_index("head")
        self.dp_at = lax.axis_index("dp")
        self.at = self.ctx_at * self.heads + self.head_at
        near, far = [], []
        for c in range(2):
            for h in range(self.heads):
                x, y = (c ^ 1) * self.heads + h, c * self.heads + (h ^ 2)
                near.append((c * self.heads + h, x if h % 2 == 0 else y))
                far.append((c * self.heads + h, y if h % 2 == 0 else x))
        self.near, self.far = near, far

    def order(self):
        first = jnp.where(self.head_at % 2 == 0, 4, 2)
        second = 6 - first
        return jnp.stack(
            [self.at ^ bits for bits in (0, 1, first, first ^ 1, 6, second ^ 1, second, 7)]
        )

    def swap(self, values, bit):
        if bit == 4:
            return lax.ppermute(values, "ctx", [(0, 1), (1, 0)])
        return lax.ppermute(values, "head", [(i, i ^ bit) for i in range(self.heads)])

    def mate(self, values):
        return self.swap(values, 1)

    def to_near(self, values):
        return lax.ppermute(values, GROUP, self.near)

    def to_far(self, values):
        return lax.ppermute(values, GROUP, self.far)

    def rows_back(self, values, place):
        pairs, same = [], False
        for d in range(self.dp):
            for h in range(self.heads):
                if (d, h) == (place[h], d):
                    same = same | ((self.dp_at == d) & (self.head_at == h))
                else:
                    pairs.append((d * self.heads + h, place[h] * self.heads + d))
        return jnp.where(same, values, lax.ppermute(values, ("dp", "head"), pairs))

    def across(self, values, step):
        return lax.ppermute(values, "dp", [(i, i ^ step) for i in range(self.dp)])


def pick(array, index, axis):
    return lax.dynamic_index_in_dim(array, index, axis, keepdims=False)


def after(values, *earlier):
    return lax.optimization_barrier((values, earlier))[0]


def local_split(tokens, cotangent, w_qkv, w_attn_out, w_in, w_mlp_out, norm_gain1, norm_gain2):
    seqs, block, width = tokens.shape
    group = Group()
    heads, dp = group.heads, group.dp
    at_c, at_h = group.ctx_at, group.head_at
    parts = 2 * heads
    hidden = w_in.shape[1] // 2 // parts
    padded = -(-hidden // 128) * 128
    own_width = width // parts
    half = heads // 2
    rows_here = w_qkv.shape[0]
    place = [2 * (h % half) + h // half for h in range(heads)]
    straight = list(range(heads))
    order = group.order()
    scalars = jnp.concatenate([order, jnp.stack([group.dp_at, at_c])]).astype(jnp.int32)
    mate, near, far = group.mate, group.to_near, group.to_far

    def in_order(own, other):
        return jnp.where(at_c == 0, jnp.stack([own, other]), jnp.stack([other, own]))

    def exchange(values):
        return lax.all_to_all(values, GROUP, split_axis=0, concat_axis=0, tiled=True)


    gains = jnp.pad(
        jnp.stack([norm_gain1, norm_gain2]), ((0, 14), (0, 3 * own_width - rows_here))
    )
    qkv_view = w_qkv.reshape(rows_here, 3, width)

    def qkv_part(at):
        start = (2 * at_h + at) * own_width
        cut = lax.dynamic_slice_in_dim(qkv_view, start, own_width, 2)
        return jnp.concatenate([cut.reshape(rows_here, 3 * own_width), gains])

    x_own = tokens[None]
    x_mate = mate(x_own)
    qkv_other, qkv_own = qkv_part(1 - at_c), qkv_part(at_c)
    qkv_cross = group.swap(after(qkv_other, x_own), 4)
    in_view = after(w_in, qkv_other).reshape(rows_here, 2, heads, 2, hidden)
    in_view = pick(in_view, 2 * (at_h % half) + at_h // half, 2)

    def in_part(at):
        cut = pick(in_view, at, 2)
        return jnp.pad(cut, ((0, 0), (0, 0), (0, padded - hidden))).reshape(rows_here, 2 * padded)

    in_other, in_own = in_part(1 - at_c), in_part(at_c)
    in_cross = group.swap(in_other, 4)
    x_chip = jnp.concatenate([x_own, after(x_mate, qkv_cross, qkv_own, in_cross, in_own)])
    x_near = near(x_chip)
    qkv_pair = jnp.stack([qkv_own, qkv_cross])
    qkv_pieces = [qkv_pair] + [group.across(qkv_pair, step) for step in range(1, dp)]

    slices = jnp.concatenate([w_attn_out, w_mlp_out])
    slices = after(slices, *qkv_pieces)
    slices = lax.dynamic_slice_in_dim(slices, at_h * (width // heads), width // heads, 1)
    slices = jnp.pad(slices, ((0, 64), (0, 0)))
    slices = lax.all_gather(slices, "dp", axis=0)
    positions = after(order, qkv_pair)[:, None] * block + jnp.arange(block, dtype=jnp.int32)
    lane = jnp.arange(own_width, dtype=jnp.int32)
    frequency = jnp.exp(
        (lane % (HD // 2)).astype(F32) * (-math.log(ROPE_BASE) / (HD // 2))
    )
    angles = wide(positions.reshape(-1))[:, None] * frequency[None, :]
    cosine = jnp.cos(angles)
    sine = jnp.sin(angles) * jnp.where(lane % HD < HD // 2, -1.0, 1.0)[None, :]

    x_far = far(x_near[:1])
    x_near = after(x_near, *qkv_pieces, cosine, sine)
    x_near_mate = mate(x_near)
    cot_own = after(cotangent, x_near)[None]
    cot_mate = mate(cot_own)
    in_pair, x_far = lax.optimization_barrier((in_order(in_own, in_cross), x_far))
    weight_in = lax.all_gather(in_pair, "dp", axis=0).reshape(width, -1)
    cot_chip = jnp.concatenate([cot_own, cot_mate])
    x_far = after(x_far, cot_chip)
    x_far_mate = mate(x_far)

    cot_near = near(after(cot_chip, x_far))
    out_rows = w_attn_out.shape[0]
    x_pieces = (x_own, x_mate, x_near, x_far, x_near_mate, x_far_mate)
    low1, qkv, weight_qkv, gain_one, gain_two = project(
        scalars, x_pieces, qkv_pieces, cosine, sine
    )

    slices = after(slices, qkv)
    out_own = slices[:, :out_rows].reshape(1, dp * out_rows, -1)
    out_mate = mate(out_own)
    mlp_slices = jnp.stack(
        [slices[place[h], out_rows : out_rows + hidden] for h in range(heads)]
    )
    mlp_slices = lax.all_to_all(mlp_slices, "head", split_axis=0, concat_axis=0, tiled=True)
    out_near = near(jnp.concatenate([out_own, out_mate]))
    att_0, log_0, home_0 = attend(scalars, after(qkv, out_mate))
    cot_near = after(cot_near, home_0)
    cot_far, cot_near_mate = far(cot_near[:1]), mate(cot_near)
    out_near = after(out_near, home_0)
    out_far, out_near_mate = far(out_near[:1]), mate(out_near)
    att_1, log_1, home = attend(scalars, after(qkv, cot_near, out_near), home_0)
    home, cot_far, out_far = lax.optimization_barrier((home, cot_far, out_far))
    att_rows = exchange(home)
    out_far_mate, cot_far_mate = mate(after(out_far, home)), mate(after(cot_far, home))
    out_pieces = (out_own, out_mate, out_near, out_far, out_near_mate, out_far_mate)
    weight_mlp = jnp.moveaxis(after(mlp_slices, home), 0, 1).reshape(hidden, width)
    weight_mlp = jnp.pad(weight_mlp, ((0, padded - hidden), (0, 0)))
    residual, low2 = branch(
        scalars, out_pieces, after(att_rows, cot_far_mate, weight_mlp, weight_in), tokens, gain_two
    )

    low_own = low2[None]
    low_mate = mate(low_own)
    low_near = near(jnp.concatenate([low_own, low_mate]))
    *arrays, keep_a = mlp(
        (low_own, low_mate), (cot_own, cot_mate), weight_in, weight_mlp, 0, (2,)
    )
    low_near = after(low_near, keep_a)
    low_far, low_near_mate = far(low_near[:1]), mate(low_near)
    *arrays, keep_b = mlp((low_near,), (cot_near,), weight_in, weight_mlp, 2, (2,), arrays)
    low_far_mate = mate(after(low_far, keep_b))
    low2_all, cot_all, mixed, grad_lifted, keep_c, send = mlp(
        (low_far, low_near_mate, low_far_mate),
        (cot_far, cot_near_mate, cot_far_mate),
        weight_in,
        weight_mlp,
        4,
        (1, 4),
        arrays,
    )

    def over_tokens(left, right):
        return dot(flat(left), flat(right), ((0,), (0,)))

    def scatter(values):
        return lax.psum_scatter(values.astype(BF16), "dp", scatter_dimension=0, tiled=True)

    def columns_first(values):
        return jnp.moveaxis(values.reshape(values.shape[0], dp, -1), 1, 0)

    rows = seqs * block

    def by_rows(values):
        return values.reshape(values.shape[0], -1, width)

    keep_a, keep_b, keep_c, send = (by_rows(array) for array in (keep_a, keep_b, keep_c, send))
    met = mate(send)
    last = combine([(rows, [(keep_c, 0, 0), (met, 2, 0)])])
    last_far = far(last)
    grad_mlp = columns_first(over_tokens(after(mixed, last), cot_all)[:hidden]).astype(BF16)
    last_far = after(last_far, grad_mlp)
    grad_mlp = scatter(grad_mlp)[0]
    chip = combine(
        [(rows, [(keep_b, 0, 0), (met, 0, 0), (last_far, 0, 0)])],
        [(rows, [(keep_b, 1, 0), (met, 1, 0)])],
    )
    chip_near = near(chip)
    grad_in = over_tokens(low2_all, after(grad_lifted, chip)).astype(BF16)
    cut = 5 * rows
    mixed_flat = flat(after(mixed, chip))
    out_keep = dot(mixed_flat[:cut], weight_mlp).astype(BF16).reshape(5, rows, width)
    out_send = dot(mixed_flat[cut:], weight_mlp).astype(BF16).reshape(3, rows, width)
    chip_near = after(chip_near, grad_in, out_keep, out_send)
    grad_in = scatter(grad_in)
    home = mate(combine([(rows, [(keep_a, 1, 0), (chip_near, 1, 0)])])[0])
    out_met = mate(after(out_send, chip_near))
    grad_residual, grad_branch, home, gain2_sum = branch_back(
        scalars, out_pieces, keep_a, chip_near, home, residual, cotangent, gain_two
    )
    grad_home = exchange(home)

    rows_keep, rows_send = out_grad(scalars, after(att_rows, home), grad_branch)
    rows_met = mate(rows_send)
    few = rows_keep.shape[1]

    def ends(index, at, *more):
        kept = [(out_keep, index, 0)], [(rows_keep, index, 0)]
        if at is not None:
            kept[0].append((out_met, at, 0))
            kept[1].append((rows_met, at, 0))
        for array, where in more:
            kept[0].append((array, where, 0))
            kept[1].append((array, where, rows))
        return [(rows, kept[0]), (few, kept[1])]

    end_last = combine(ends(4, 2))
    grad_home = after(grad_home, end_last, grad_mlp)
    end_far = far(after(end_last, grad_home))
    keep_0, send_0, before = attend_back(
        scalars, qkv, grad_home, att_0, log_0, cosine, sine, weight_qkv, low1, 0
    )
    met_0 = mate(send_0)
    end_far, grad_in = lax.optimization_barrier((after(end_far, send_0), grad_in))
    in_parts = grad_in.reshape(2, rows_here, -1)
    in_cross = group.swap(pick(in_parts, 1 - at_c, 0), 4)
    end_chip = combine(ends(2, 0, (end_far, 0)), ends(3, 1))
    end_near = near(after(end_chip, in_cross))
    keep_1, send_1, grad_qkv = attend_back(
        scalars, qkv, after(grad_home, end_chip), att_1, log_1, cosine, sine,
        weight_qkv, low1, 1, before, gain_one, gain2_sum, dp=dp,
    )

    grad_qkv = scatter(grad_qkv.reshape(-1, grad_qkv.shape[2]))
    met_1 = mate(send_1)
    end_home = combine(ends(1, None, (after(end_near, send_1), 1)))
    met_1, end_home = lax.optimization_barrier((met_1, end_home))
    end_home = mate(end_home)

    def both(index, at, *more):
        kept = [(keep_0, index, 0)], [(keep_1, index, 0)]
        if at is not None:
            kept[0].append((met_0, at, 0))
            kept[1].append((met_1, at, 0))
        for array, where in more:
            kept[0].append((array, where, 0))
            kept[1].append((array, where, block))
        return [(block, kept[0]), (block, kept[1])]

    last = combine(both(4, 2))
    last_far = far(last)
    end_home = after(end_home, last)
    grad_out = wide(rows_keep[0]) + wide(end_near[0, rows:]) + wide(end_home[0, rows:])
    grad_out = columns_first(grad_out.astype(BF16))
    last_far, grad_out = lax.optimization_barrier((last_far, grad_out))
    grad_out = scatter(grad_out)[0]
    chip = combine(both(2, 0, (last_far, 0)), both(3, 1))
    chip_near = near(chip)

    end_home = after(end_home, chip)
    result = wide(out_keep[0]) + wide(end_near[0, :rows]) + wide(end_home[0, :rows])
    result = (residual + result.reshape(residual.shape)).astype(BF16)
    grad_in = in_order(after(pick(in_parts, at_c, 0), chip), in_cross)
    late = at_h // half
    grad_in = jnp.stack([grad_in[..., :hidden], grad_in[..., padded : padded + hidden]])
    stays = pick(grad_in, late, 0)
    comes = group.swap(pick(grad_in, 1 - late, 0), half)
    grad_mlp = group.rows_back(after(grad_mlp, chip), place)
    grad_qkv = after(grad_qkv, chip)
    both_rows = 2 * rows_here
    qkv_parts = grad_qkv[:both_rows].reshape(2, rows_here, -1)
    gains = grad_qkv[both_rows:]
    cross = jnp.concatenate([pick(qkv_parts, 1 - at_c, 0), gains])
    cross = group.swap(cross, 4)
    chip_near = after(chip_near, comes, result, cross, grad_mlp)
    home = combine(both(1, None, (chip_near, 1)))
    cross = after(cross, home)
    home = mate(home)
    grad_qkv = in_order(pick(qkv_parts, at_c, 0), cross[:rows_here])
    gains = (wide(gains) + wide(cross[rows_here:])).astype(BF16)
    gains = wide(gains) + sum(wide(group.swap(gains, bit)) for bit in range(1, heads))
    grad_input = input_grad((keep_0, keep_1), chip_near, home, tokens, grad_residual, gain_one)
    grad_out, grad_input = lax.optimization_barrier((grad_out, grad_input))
    grad_out = wide(group.rows_back(grad_out, straight))

    grad_mlp = wide(grad_mlp)
    grad_in = jnp.where(
        late == 0, jnp.concatenate([stays, comes]), jnp.concatenate([comes, stays])
    )
    grad_in = wide(jnp.moveaxis(grad_in, 0, 1).reshape(rows_here, -1))

    per_device = width // (dp * parts)
    start = group.at * per_device
    grad_gain1, grad_gain2 = (
        lax.dynamic_slice_in_dim(gains[i], start, per_device, 0) for i in range(2)
    )
    grad_qkv = grad_qkv.reshape(2, rows_here, 3, own_width)
    grad_qkv = jnp.moveaxis(grad_qkv, 2, 0)
    odd = at_h % 2
    stays = pick(grad_qkv, odd + late, 0)
    core = group.swap(pick(grad_qkv, 1 - odd + late, 0), 1)
    chip = group.swap(pick(grad_qkv, 2 - 2 * late, 0), 2)
    grad_qkv = jnp.where(
        odd == 0, jnp.concatenate([stays, core, chip]), jnp.concatenate([chip, core, stays])
    )
    grad_qkv = wide(jnp.moveaxis(grad_qkv, 0, 1).reshape(rows_here, -1))

    return (
        result,
        grad_input,
        grad_qkv,
        grad_out,
        grad_in,
        grad_mlp,
        grad_gain1,
        grad_gain2,
    )


def local(tokens, cotangent, w_qkv, w_attn_out, w_in, w_mlp_out, norm_gain1, norm_gain2):
    args = (tokens, cotangent, w_qkv, w_attn_out, w_in, w_mlp_out, norm_gain1, norm_gain2)
    sizes = [lax.axis_size(axis) for axis in ("dp", "ctx", "head")]
    if sizes == [4, 2, 4] and tokens.shape[2] == 8 * 2 * HD and tokens.shape[1] % 16 == 0:
        return local_split(*args)
    return local_general(*args)


def solution(mesh):
    in_specs = (
        P("dp", ("ctx", "head"), None),
        P("dp", ("ctx", "head"), None),
        P(("dp", "ctx"), None),
        P(("dp", "ctx"), None),
        P(("dp", "ctx"), None),
        P(("dp", "ctx"), None),
        P(("dp", "ctx")),
        P(("dp", "ctx")),
    )
    out_specs = (
        P("dp", ("ctx", "head"), None),
        P("dp", ("ctx", "head"), None),
        P(("dp", "ctx"), "head"),
        P(("dp", "ctx"), "head"),
        P(("dp", "ctx"), "head"),
        P(("dp", "ctx"), "head"),
        P(("dp", "ctx", "head")),
        P(("dp", "ctx", "head")),
    )
    return jax.shard_map(local, mesh=mesh, in_specs=in_specs, out_specs=out_specs, check_vma=False)
```

```python
import functools
import math

import jax
import jax.numpy as jnp
from jax import lax
from jax.experimental import pallas as pl
from jax.experimental.pallas import tpu as pltpu
from jax.sharding import PartitionSpec as P

HD = 64


EPSILON = 1e-05
ROPE_BASE = 160000.0


def normalize(values):
    centre = jnp.mean(values, axis=-1, keepdims=True)
    shifted = values - centre
    spread = jnp.mean(shifted * shifted, axis=-1, keepdims=True)
    factor = lax.rsqrt(spread + EPSILON)
    return (shifted * factor, factor)


def norm_back(grad_normed, normed, factor):
    grad_centre = jnp.mean(grad_normed, axis=-1, keepdims=True)
    grad_along = jnp.mean(grad_normed * normed, axis=-1, keepdims=True)
    return (grad_normed - grad_centre - normed * grad_along) * factor


def rope_tables(positions, half_size):
    frequency = jnp.exp(
        jnp.arange(half_size, dtype=jnp.float32) * (-math.log(ROPE_BASE) / half_size)
    )
    angles = positions[:, None] * frequency[None, :]
    return (jnp.cos(angles), jnp.sin(angles))


def rotate(values, cosine, sine_table, direction):
    half_size = cosine.shape[-1]
    first_half = values[..., :half_size]
    second_half = values[..., half_size:]
    cos_part = cosine[:, None, :]
    sin_part = sine_table[:, None, :] * direction
    return jnp.concatenate(
        [
            first_half * cos_part - second_half * sin_part,
            second_half * cos_part + first_half * sin_part,
        ],
        axis=-1,
    )


def block_scores(queries4, keys_block, scale):
    keys4 = keys_block.reshape(
        keys_block.shape[0], keys_block.shape[1], queries4.shape[2], queries4.shape[3]
    )
    return (
        jnp.einsum("sqgd,skgd->sgqk", queries4, keys4, preferred_element_type=jnp.float32) * scale
    )


def attend_forward(queries4, keys_all, values_all, key_rows, scale):
    seqs_here, query_rows, groups, head_size = queries4.shape
    turns = keys_all.shape[1] // key_rows

    def statistics(turn, carry):
        row_peak, row_total = carry
        keys_block = lax.dynamic_slice_in_dim(keys_all, turn * key_rows, key_rows, 1)
        scores = block_scores(queries4, keys_block, scale)
        new_peak = jnp.maximum(row_peak, jnp.max(scores, axis=-1))
        row_total = row_total * jnp.exp(row_peak - new_peak) + jnp.sum(
            jnp.exp(scores - new_peak[..., None]), axis=-1
        )
        return (new_peak, row_total)

    start_peak = jnp.full((seqs_here, groups, query_rows), -1e30, jnp.float32)
    row_peak, row_total = lax.fori_loop(
        0, turns, statistics, (start_peak, jnp.zeros_like(start_peak))
    )
    log_total = row_peak + jnp.log(row_total)

    def accumulate(turn, running):
        keys_block = lax.dynamic_slice_in_dim(keys_all, turn * key_rows, key_rows, 1)
        values_block = lax.dynamic_slice_in_dim(values_all, turn * key_rows, key_rows, 1).reshape(
            seqs_here, key_rows, groups, head_size
        )
        weights = jnp.exp(block_scores(queries4, keys_block, scale) - log_total[..., None]).astype(
            jnp.bfloat16
        )
        return running + jnp.einsum(
            "sgqk,skgd->sqgd", weights, values_block, preferred_element_type=jnp.float32
        )

    attended = lax.fori_loop(
        0, turns, accumulate, jnp.zeros((seqs_here, query_rows, groups, head_size), jnp.float32)
    )
    return (attended, log_total)


def attend_backward(queries4, keys_all, values_all, grad_out4, log_total, along, key_rows, scale):
    seqs_here, query_rows, groups, head_size = queries4.shape
    length = keys_all.shape[1]
    width_group = groups * head_size
    turns = length // key_rows

    def step_back(turn, carry):
        grad_queries, grad_keys, grad_values = carry
        keys_block = lax.dynamic_slice_in_dim(keys_all, turn * key_rows, key_rows, 1)
        keys4 = keys_block.reshape(seqs_here, key_rows, groups, head_size)
        values4 = lax.dynamic_slice_in_dim(values_all, turn * key_rows, key_rows, 1).reshape(
            seqs_here, key_rows, groups, head_size
        )
        weights = jnp.exp(block_scores(queries4, keys_block, scale) - log_total[..., None])
        grad_weights = jnp.einsum(
            "sqgd,skgd->sgqk", grad_out4, values4, preferred_element_type=jnp.float32
        )
        grad_scores = (weights * (grad_weights - along[..., None])).astype(jnp.bfloat16)
        grad_queries = grad_queries + jnp.einsum(
            "sgqk,skgd->sqgd", grad_scores, keys4, preferred_element_type=jnp.float32
        )
        key_part = (
            jnp.einsum("sgqk,sqgd->skgd", grad_scores, queries4, preferred_element_type=jnp.float32)
            * scale
        )
        value_part = jnp.einsum(
            "sgqk,sqgd->skgd",
            weights.astype(jnp.bfloat16),
            grad_out4,
            preferred_element_type=jnp.float32,
        )
        grad_keys = lax.dynamic_update_slice_in_dim(
            grad_keys, key_part.reshape(seqs_here, key_rows, width_group), turn * key_rows, 1
        )
        grad_values = lax.dynamic_update_slice_in_dim(
            grad_values, value_part.reshape(seqs_here, key_rows, width_group), turn * key_rows, 1
        )
        return (grad_queries, grad_keys, grad_values)

    start = (
        jnp.zeros((seqs_here, query_rows, groups, head_size), jnp.float32),
        jnp.zeros((seqs_here, length, width_group), jnp.float32),
        jnp.zeros((seqs_here, length, width_group), jnp.float32),
    )
    grad_queries, grad_keys, grad_values = lax.fori_loop(0, turns, step_back, start)
    return (grad_queries * scale, grad_keys, grad_values)


def local_general(tokens, cotangent, w_qkv, w_attn_out, w_in, w_mlp_out, norm_gain1, norm_gain2):
    seqs_here, block_rows, width = tokens.shape
    count_rows = seqs_here * block_rows
    heads_all = width // HD
    head_devices = lax.axis_size("head")
    group_devices = lax.axis_size(("dp", "ctx"))
    groups = heads_all // head_devices
    width_group = groups * HD
    scale = HD ** (-0.5)
    ff_width = w_in.shape[1] // 2
    full_qkv, full_out, full_in, full_mlp, gain_one, gain_two = (
        lax.all_gather(w_qkv, ("dp", "ctx"), axis=0, tiled=True),
        lax.all_gather(w_attn_out, ("dp", "ctx"), axis=0, tiled=True),
        lax.all_gather(w_in, ("dp", "ctx"), axis=0, tiled=True),
        lax.all_gather(w_mlp_out, ("dp", "ctx"), axis=0, tiled=True),
        lax.all_gather(norm_gain1, ("dp", "ctx"), axis=0, tiled=True),
        lax.all_gather(norm_gain2, ("dp", "ctx"), axis=0, tiled=True),
    )
    x_in = tokens.astype(jnp.float32).reshape(count_rows, width)
    normed1, factor1 = normalize(x_in)
    lowered1 = (normed1 * gain_one.astype(jnp.float32)).astype(jnp.bfloat16)
    projected = jnp.dot(lowered1, full_qkv, preferred_element_type=jnp.float32).reshape(
        seqs_here, block_rows, 3, heads_all, HD
    )
    first_pos = (lax.axis_index("ctx") * head_devices + lax.axis_index("head")) * block_rows
    positions = (first_pos + jnp.arange(block_rows, dtype=jnp.int32)).astype(jnp.float32)
    cosine, sine_table = rope_tables(positions, HD // 2)
    queries = (
        rotate(projected[:, :, 0], cosine, sine_table, 1.0)
        .astype(jnp.bfloat16)
        .reshape(seqs_here, block_rows, width)
    )
    keys_local = (
        rotate(projected[:, :, 1], cosine, sine_table, 1.0)
        .astype(jnp.bfloat16)
        .reshape(seqs_here, block_rows, width)
    )
    values_local = projected[:, :, 2].astype(jnp.bfloat16).reshape(seqs_here, block_rows, width)
    queries_h, keys_h, values_h = (
        lax.all_to_all(queries, "head", split_axis=2, concat_axis=1, tiled=True),
        lax.all_to_all(keys_local, "head", split_axis=2, concat_axis=1, tiled=True),
        lax.all_to_all(values_local, "head", split_axis=2, concat_axis=1, tiled=True),
    )
    query_rows = queries_h.shape[1]
    queries4 = queries_h.reshape(seqs_here, query_rows, groups, HD)
    keys_all, values_all = (
        lax.all_gather(keys_h, "ctx", axis=1, tiled=True),
        lax.all_gather(values_h, "ctx", axis=1, tiled=True),
    )
    key_rows = math.gcd(keys_all.shape[1], 1024)
    attended, log_total = attend_forward(queries4, keys_all, values_all, key_rows, scale)
    attended_low = attended.astype(jnp.bfloat16).reshape(seqs_here, query_rows, width_group)
    back_rows = lax.all_to_all(
        attended_low, "head", split_axis=1, concat_axis=2, tiled=True
    ).reshape(count_rows, width)
    residual = x_in + jnp.dot(back_rows, full_out, preferred_element_type=jnp.float32)
    normed2, factor2 = normalize(residual)
    lowered2 = (normed2 * gain_two.astype(jnp.float32)).astype(jnp.bfloat16)
    lifted = jnp.dot(lowered2, full_in, preferred_element_type=jnp.float32)
    first_part = lifted[:, :ff_width]
    second_part = lifted[:, ff_width:]
    activated, gelu_pullback = jax.vjp(
        lambda entries: jax.nn.gelu(entries, approximate=False), first_part
    )
    mixed = (activated * second_part).astype(jnp.bfloat16)
    result = (residual + jnp.dot(mixed, full_mlp, preferred_element_type=jnp.float32)).astype(
        jnp.bfloat16
    )
    full_qkv, full_out, full_in, full_mlp, gain_one, gain_two = (
        lax.all_gather(w_qkv, ("dp", "ctx"), axis=0, tiled=True),
        lax.all_gather(w_attn_out, ("dp", "ctx"), axis=0, tiled=True),
        lax.all_gather(w_in, ("dp", "ctx"), axis=0, tiled=True),
        lax.all_gather(w_mlp_out, ("dp", "ctx"), axis=0, tiled=True),
        lax.all_gather(norm_gain1, ("dp", "ctx"), axis=0, tiled=True),
        lax.all_gather(norm_gain2, ("dp", "ctx"), axis=0, tiled=True),
    )
    keys_all, values_all = (
        lax.all_gather(keys_h, "ctx", axis=1, tiled=True),
        lax.all_gather(values_h, "ctx", axis=1, tiled=True),
    )
    grad_top = cotangent.reshape(count_rows, width)
    grad_mlp = jnp.einsum("nf,nd->fd", mixed, grad_top, preferred_element_type=jnp.float32)
    grad_mixed = jnp.einsum("nd,fd->nf", grad_top, full_mlp, preferred_element_type=jnp.float32)
    grad_first = gelu_pullback(grad_mixed * second_part)[0]
    grad_lifted = jnp.concatenate([grad_first, grad_mixed * activated], axis=-1).astype(
        jnp.bfloat16
    )
    grad_inner = jnp.einsum("nd,nf->df", lowered2, grad_lifted, preferred_element_type=jnp.float32)
    grad_lowered2 = jnp.einsum(
        "nf,df->nd", grad_lifted, full_in, preferred_element_type=jnp.float32
    )
    grad_two = jnp.sum(grad_lowered2 * normed2, axis=0)
    grad_residual = grad_top.astype(jnp.float32) + norm_back(
        grad_lowered2 * gain_two.astype(jnp.float32), normed2, factor2
    )
    grad_branch = grad_residual.astype(jnp.bfloat16)
    grad_outproj = jnp.einsum(
        "nd,ne->de", back_rows, grad_branch, preferred_element_type=jnp.float32
    )
    grad_attended = jnp.einsum(
        "ne,de->nd", grad_branch, full_out, preferred_element_type=jnp.float32
    ).astype(jnp.bfloat16)
    grad_attended_h = lax.all_to_all(
        grad_attended.reshape(seqs_here, block_rows, width),
        "head",
        split_axis=2,
        concat_axis=1,
        tiled=True,
    )
    grad_out4 = grad_attended_h.reshape(seqs_here, query_rows, groups, HD)
    along = jnp.transpose(jnp.sum(grad_out4.astype(jnp.float32) * attended, axis=-1), (0, 2, 1))
    grad_queries, grad_keys_all, grad_values_all = attend_backward(
        queries4, keys_all, values_all, grad_out4, log_total, along, key_rows, scale
    )
    grad_keys_sum, grad_values_sum = (
        lax.psum_scatter(
            grad_keys_all.astype(jnp.bfloat16), "ctx", scatter_dimension=1, tiled=True
        ).astype(jnp.float32),
        lax.psum_scatter(
            grad_values_all.astype(jnp.bfloat16), "ctx", scatter_dimension=1, tiled=True
        ).astype(jnp.float32),
    )
    grad_q_low = grad_queries.astype(jnp.bfloat16).reshape(seqs_here, query_rows, width_group)
    grad_q_tok, grad_k_tok, grad_v_tok = (
        lax.all_to_all(grad_q_low, "head", split_axis=1, concat_axis=2, tiled=True),
        lax.all_to_all(
            grad_keys_sum.astype(jnp.bfloat16), "head", split_axis=1, concat_axis=2, tiled=True
        ),
        lax.all_to_all(
            grad_values_sum.astype(jnp.bfloat16), "head", split_axis=1, concat_axis=2, tiled=True
        ),
    )
    unrot_q = rotate(
        grad_q_tok.astype(jnp.float32).reshape(seqs_here, block_rows, heads_all, HD),
        cosine,
        sine_table,
        -1.0,
    )
    unrot_k = rotate(
        grad_k_tok.astype(jnp.float32).reshape(seqs_here, block_rows, heads_all, HD),
        cosine,
        sine_table,
        -1.0,
    )
    grad_projected = jnp.concatenate(
        [
            unrot_q.reshape(count_rows, width),
            unrot_k.reshape(count_rows, width),
            grad_v_tok.astype(jnp.float32).reshape(count_rows, width),
        ],
        axis=-1,
    ).astype(jnp.bfloat16)
    grad_project = jnp.einsum(
        "nd,nf->df", lowered1, grad_projected, preferred_element_type=jnp.float32
    )
    grad_lowered1 = jnp.einsum(
        "nf,df->nd", grad_projected, full_qkv, preferred_element_type=jnp.float32
    )
    grad_one = jnp.sum(grad_lowered1 * normed1, axis=0)
    grad_input = grad_residual + norm_back(
        grad_lowered1 * gain_one.astype(jnp.float32), normed1, factor1
    )
    pieces_one = grad_one.reshape(group_devices, head_devices, -1)
    pieces_two = grad_two.reshape(group_devices, head_devices, -1)
    part_qkv, part_out, part_in, part_mlp, part_one, part_two = (
        lax.psum_scatter(
            grad_project.astype(jnp.bfloat16), ("dp", "ctx"), scatter_dimension=0, tiled=True
        ).astype(jnp.float32),
        lax.psum_scatter(
            grad_outproj.astype(jnp.bfloat16), ("dp", "ctx"), scatter_dimension=0, tiled=True
        ).astype(jnp.float32),
        lax.psum_scatter(
            grad_inner.astype(jnp.bfloat16), ("dp", "ctx"), scatter_dimension=0, tiled=True
        ).astype(jnp.float32),
        lax.psum_scatter(
            grad_mlp.astype(jnp.bfloat16), ("dp", "ctx"), scatter_dimension=0, tiled=True
        ).astype(jnp.float32),
        lax.psum_scatter(
            pieces_one.astype(jnp.bfloat16), ("dp", "ctx"), scatter_dimension=0, tiled=True
        ).astype(jnp.float32),
        lax.psum_scatter(
            pieces_two.astype(jnp.bfloat16), ("dp", "ctx"), scatter_dimension=0, tiled=True
        ).astype(jnp.float32),
    )
    final_qkv, final_out, final_in, final_mlp, final_one, final_two = (
        lax.psum_scatter(
            part_qkv.astype(jnp.bfloat16), "head", scatter_dimension=1, tiled=True
        ).astype(jnp.float32),
        lax.psum_scatter(
            part_out.astype(jnp.bfloat16), "head", scatter_dimension=1, tiled=True
        ).astype(jnp.float32),
        lax.psum_scatter(
            part_in.astype(jnp.bfloat16), "head", scatter_dimension=1, tiled=True
        ).astype(jnp.float32),
        lax.psum_scatter(
            part_mlp.astype(jnp.bfloat16), "head", scatter_dimension=1, tiled=True
        ).astype(jnp.float32),
        lax.psum_scatter(
            part_one.astype(jnp.bfloat16), "head", scatter_dimension=1, tiled=True
        ).astype(jnp.float32),
        lax.psum_scatter(
            part_two.astype(jnp.bfloat16), "head", scatter_dimension=1, tiled=True
        ).astype(jnp.float32),
    )
    return (
        result.reshape(seqs_here, block_rows, width),
        grad_input.reshape(seqs_here, block_rows, width),
        final_qkv,
        final_out,
        final_in,
        final_mlp,
        final_one.reshape(-1),
        final_two.reshape(-1),
    )


F32 = jnp.float32
BF16 = jnp.bfloat16
GROUP = ("ctx", "head")


def dot(left, right, dims=((1,), (0,))):
    return lax.dot_general(left, right, (dims, ((), ())), preferred_element_type=F32)


def wide(values):
    return values.astype(F32)


def flat(values):
    return values.reshape(-1, values.shape[-1])


def lane_rotate(values, cosine, sine_signed):
    lane = lax.broadcasted_iota(jnp.int32, values.shape, 1)
    width = values.shape[1]
    partner = jnp.where(
        lane % HD < HD // 2,
        pltpu.roll(values, width - HD // 2, 1),
        pltpu.roll(values, HD // 2, 1),
    )
    return values * cosine + partner * sine_signed


def head_masks(shape):
    lane = lax.broadcasted_iota(jnp.int32, shape, 1)
    return [lane // HD == head for head in range(shape[1] // HD)]


def params(mebibytes):
    return pltpu.CompilerParams(vmem_limit_bytes=mebibytes * 1024 * 1024)


COST = pl.CostEstimate(flops=1 << 20, transcendentals=0, bytes_accessed=1 << 16)


def whole(array):
    return pl.BlockSpec(array.shape, lambda *_: (0,) * len(array.shape))


SCALARS = pl.BlockSpec(memory_space=pltpu.SMEM)


def project_kernel(place_ref, *refs):
    pieces, weights = refs[:6], refs[6:10]
    cos_ref, sin_ref, low_ref, qkv_ref, w_ref, gain1_ref, gain2_ref, rows_ref = refs[10:]
    block, part = pieces[0].shape[2], w_ref.shape[1] // 3
    rows = gain1_ref.shape[1] // 8

    @pl.when(pl.program_id(0) == 0)
    def _():
        for step, piece in enumerate(weights):
            for turn in range(2):
                at = 2 * (place_ref[8] ^ step) + (place_ref[9] ^ turn)
                w_ref[pl.ds(pl.multiple_of(at * rows, rows), rows), :] = piece[turn, :rows]
                gains = piece[turn, rows:].astype(F32)
                rows_ref[0, pl.ds(at, 1), :] = gains[:1, :rows]
                rows_ref[1, pl.ds(at, 1), :] = gains[1:2, :rows]
        for out, at in ((gain1_ref, 0), (gain2_ref, 1)):
            for row in range(8):
                out[:, row * rows : (row + 1) * rows] = rows_ref[at, row : row + 1, :]

    gain = gain1_ref[...]
    index = 0
    for piece in pieces:
        for inner in range(piece.shape[0]):
            normed, _ = normalize(piece[inner, 0].astype(F32))
            low_ref[index, 0] = (normed * gain).astype(BF16)
            index += 1
    projected = dot(flat(low_ref[:, 0]), w_ref[...])
    cosine, sine = cos_ref[...], sin_ref[...]
    shape = (8, block, part)
    qkv_ref[:, 0, :, :part] = (
        (lane_rotate(projected[:, :part], cosine, sine) * HD**-0.5).astype(BF16).reshape(shape)
    )
    qkv_ref[:, 0, :, part : 2 * part] = (
        lane_rotate(projected[:, part : 2 * part], cosine, sine).astype(BF16).reshape(shape)
    )
    qkv_ref[:, 0, :, 2 * part :] = projected[:, 2 * part :].astype(BF16).reshape(shape)


def project(place, pieces, weights, cosine, sine):
    seqs, block, width = pieces[0].shape[1:]
    own = weights[0].shape[2]

    def by_seq(lead, last):
        return pl.BlockSpec((lead, 1, block, last), lambda s: (0, s, 0, 0))

    return pl.pallas_call(
        project_kernel,
        grid=(seqs,),
        in_specs=[SCALARS]
        + [by_seq(piece.shape[0], width) for piece in pieces]
        + [whole(w) for w in weights]
        + [whole(cosine), whole(sine)],
        out_specs=(
            by_seq(8, width),
            by_seq(8, own),
            pl.BlockSpec((width, own), lambda s: (0, 0)),
            pl.BlockSpec((1, width), lambda s: (0, 0)),
            pl.BlockSpec((1, width), lambda s: (0, 0)),
        ),
        out_shape=(
            jax.ShapeDtypeStruct((8, seqs, block, width), BF16),
            jax.ShapeDtypeStruct((8, seqs, block, own), BF16),
            jax.ShapeDtypeStruct((width, own), BF16),
            jax.ShapeDtypeStruct((1, width), F32),
            jax.ShapeDtypeStruct((1, width), F32),
        ),
        scratch_shapes=[pltpu.VMEM((2, 8, width // 8), F32)],
        compiler_params=params(60),
        cost_estimate=COST,
        name="project",
    )(place, *pieces, *weights, cosine, sine)


def attend_kernel(place_ref, q_ref, k_ref, v_ref, *refs):
    att_ref, log_ref, home_ref = refs[-3:]
    step, seq = pl.program_id(0), len(refs) - 3
    if seq:

        @pl.when(step == 0)
        def _():
            home_ref[:, :1] = refs[0][...]

    queries, keys, values = flat(q_ref[...]), flat(k_ref[...]), flat(v_ref[...])
    attended = jnp.zeros(queries.shape, F32)
    logs = jnp.zeros(queries.shape, F32)
    for mask in head_masks(queries.shape):
        scores = dot(jnp.where(mask, queries, 0), keys, ((1,), (1,)))
        peak = jnp.max(scores, axis=1, keepdims=True)
        weights = jnp.exp(scores - peak)
        total = jnp.sum(weights, axis=1, keepdims=True)
        mixed = dot(weights.astype(BF16), values) * (1.0 / total)
        attended = jnp.where(mask, mixed, attended)
        logs = jnp.where(mask, peak + jnp.log(total), logs)
    att_ref[...] = attended.reshape(att_ref.shape)
    log_ref[...] = logs.reshape(log_ref.shape)
    low = attended.astype(BF16).reshape(att_ref.shape)
    for inner in range(2):
        home_ref[place_ref[2 * step + inner], seq] = low[inner, 0]


def attend(place, qkv, *home):
    _, _, block, own = qkv.shape
    part, seq = own // 3, len(home)
    rows = pl.BlockSpec((2, 1, block, part), lambda i: (i, 0, 0, 0))
    shape = (8, 1, block, part)
    return pl.pallas_call(
        attend_kernel,
        grid=(4,),
        in_specs=[
            SCALARS,
            pl.BlockSpec((2, 1, block, part), lambda i: (i, seq, 0, 0)),
            pl.BlockSpec((8, 1, block, part), lambda i: (0, seq, 0, 1)),
            pl.BlockSpec((8, 1, block, part), lambda i: (0, seq, 0, 2)),
            *[whole(h) for h in home],
        ],
        out_specs=(
            rows,
            rows,
            pl.BlockSpec((8, 1 + seq, block, part), lambda i: (0, 0, 0, 0)),
        ),
        out_shape=(
            jax.ShapeDtypeStruct(shape, F32),
            jax.ShapeDtypeStruct(shape, F32),
            jax.ShapeDtypeStruct((8, 1 + seq, block, part), BF16),
        ),
        compiler_params=params(24),
        cost_estimate=COST,
        name="attend",
    )(place, qkv, qkv, qkv, *home)


def branch_kernel(place_ref, *refs):
    pieces = refs[:6]
    rows_ref, tokens_ref, gain_ref, residual_ref, low_ref, side_ref, total_ref = refs[6:]
    heads = rows_ref.shape[0] // 2
    for c in range(2):
        side_ref[c] = jnp.concatenate([flat(rows_ref[c * heads + d]) for d in range(heads)], axis=1)
    total_ref[...] = flat(wide(tokens_ref[...]))
    index = 0
    for piece in pieces:
        n = piece.shape[2]
        for inner in range(piece.shape[0]):
            at = place_ref[index]
            columns = pl.ds(pl.multiple_of((at % heads) * n, n), n)
            total_ref[:, columns] += dot(side_ref[at // heads], piece[inner])
            index += 1
    total = total_ref[...]
    normed, _ = normalize(total)
    residual_ref[...] = total.reshape(residual_ref.shape)
    low_ref[...] = (normed * gain_ref[...]).astype(BF16).reshape(low_ref.shape)


def branch(place, pieces, rows, tokens, gain):
    args = (*pieces, rows, tokens, gain)
    seqs, block, width = tokens.shape
    return pl.pallas_call(
        branch_kernel,
        in_specs=[SCALARS] + [whole(a) for a in args],
        out_shape=(
            jax.ShapeDtypeStruct(tokens.shape, F32),
            jax.ShapeDtypeStruct(tokens.shape, BF16),
        ),
        scratch_shapes=[
            pltpu.VMEM((2, seqs * block, pieces[0].shape[1]), BF16),
            pltpu.VMEM((seqs * block, width), F32),
        ],
        compiler_params=params(16),
        cost_estimate=COST,
        name="branch",
    )(place, *args)


def combine(*groups):
    parts = [part for group in groups for _, parts in group for part in parts]
    rows = sum(count for count, _ in groups[0])
    width = parts[0][0].shape[2]

    def kernel(*refs):
        at = 0
        for k, group in enumerate(groups):
            row = 0
            for count, terms in group:
                total = 0.0
                for _, _, start in terms:
                    total = total + wide(refs[at][0, start : start + count])
                    at += 1
                refs[-1][k, row : row + count] = total.astype(BF16)
                row += count

    return pl.pallas_call(
        kernel,
        grid=(1,),
        in_specs=[
            pl.BlockSpec((1, *array.shape[1:]), lambda *_, index=index: (index, 0, 0))
            for array, index, _ in parts
        ],
        out_specs=pl.BlockSpec((len(groups), rows, width), lambda *_: (0, 0, 0)),
        out_shape=jax.ShapeDtypeStruct((len(groups), rows, width), BF16),
        compiler_params=params(16),
        cost_estimate=COST,
        name="combine",
    )(*[array for array, _, _ in parts])


def mlp_kernel(*refs, count, ends):
    pieces, tops = refs[:count], refs[count : 2 * count]
    w_ref, out_w_ref = refs[2 * count : 2 * count + 2]
    low_ref, top_ref, mixed_ref, lifted_ref, *out_refs = refs[-4 - len(ends) :]
    step = pl.program_id(0)
    start = 0
    for piece, top in zip(pieces, tops):

        @pl.when((step >= start) & (step < start + piece.shape[0]))
        def _(piece=piece, top=top, start=start):
            low_ref[0] = piece[step - start]
            top_ref[0] = top[step - start]

        start += piece.shape[0]

    hidden = w_ref.shape[1] // 2
    lifted = dot(flat(low_ref[...]), w_ref[...])
    first, second = lifted[:, :hidden], lifted[:, hidden:]
    grad_mixed = dot(flat(top_ref[...]), out_w_ref[...], ((1,), (1,)))
    gate = 0.5 * (1.0 + lax.erf(first * (0.5**0.5)))
    slope = gate + first * jnp.exp(first * first * -0.5) * ((2.0 * math.pi) ** -0.5)
    activated = first * gate
    mixed_ref[...] = (activated * second).astype(BF16).reshape(mixed_ref.shape)
    grad = jnp.concatenate(
        [(grad_mixed * second * slope).astype(BF16), (grad_mixed * activated).astype(BF16)],
        axis=1,
    )
    lifted_ref[...] = grad.reshape(lifted_ref.shape)
    partial = dot(grad, w_ref[...], ((1,), (1,))).astype(BF16).reshape(low_ref.shape)
    start = 0
    for out, end in zip(out_refs, ends):

        @pl.when((step >= start) & (step < end))
        def _(out=out):
            out[...] = partial

        start = end


def mlp(pieces, tops, w, out_w, base, ends, earlier=()):
    seqs, block, width = pieces[0].shape[1:]
    hidden = w.shape[1] // 2
    whole_in = (*pieces, *tops, w, out_w)

    def rows(last):
        return pl.BlockSpec((1, seqs, block, last), lambda i: (i + base, 0, 0, 0))

    def within(start, end):
        return pl.BlockSpec(
            (1, seqs, block, width),
            lambda i: (jnp.clip(i - start, 0, end - start - 1), 0, 0, 0),
        )

    starts = (0, *ends[:-1])
    lasts = (width, width, hidden, 2 * hidden)
    return pl.pallas_call(
        functools.partial(mlp_kernel, count=len(pieces), ends=ends),
        grid=(ends[-1],),
        in_specs=[whole(array) for array in whole_in]
        + [pl.BlockSpec(memory_space=pl.ANY)] * len(earlier),
        out_specs=(
            *[rows(last) for last in lasts],
            *[within(start, end) for start, end in zip(starts, ends)],
        ),
        out_shape=(
            *[jax.ShapeDtypeStruct((8, seqs, block, last), BF16) for last in lasts],
            *[
                jax.ShapeDtypeStruct((end - start, seqs, block, width), BF16)
                for start, end in zip(starts, ends)
            ],
        ),
        input_output_aliases={len(whole_in) + at: at for at in range(len(earlier))},
        compiler_params=params(32),
        cost_estimate=COST,
        name="mlp",
    )(*whole_in, *earlier)


def out_grad_kernel(place_ref, rows_ref, grad_ref, keep_ref, send_ref):
    grads = flat(grad_ref[...])
    for index in range(8):
        part = dot(flat(rows_ref[place_ref[index]]), grads, ((0,), (0,))).astype(BF16)
        if index < 5:
            keep_ref[index] = part
        else:
            send_ref[index - 5] = part


def out_grad(place, rows, grads):
    part, width = rows.shape[-1], grads.shape[-1]
    return pl.pallas_call(
        out_grad_kernel,
        in_specs=[SCALARS, whole(rows), whole(grads)],
        out_shape=(
            jax.ShapeDtypeStruct((5, part, width), BF16),
            jax.ShapeDtypeStruct((3, part, width), BF16),
        ),
        compiler_params=params(16),
        cost_estimate=COST,
        name="out_grad",
    )(place, rows, grads)


def branch_back_kernel(place_ref, *refs):
    pieces = refs[:6]
    keep_ref, near_ref, own_ref, residual_ref, top_ref, gain_ref = refs[6:12]
    grad_ref, branch_ref, home_ref, sum_ref, low_ref, side_ref = refs[12:]
    grad_low = wide(flat(keep_ref[...])) + wide(flat(near_ref[...])) + wide(flat(own_ref[...]))
    normed, factor = normalize(flat(residual_ref[...]))
    sum_ref[...] = jnp.sum(grad_low * normed, axis=0, keepdims=True)
    grad = flat(wide(top_ref[...])) + norm_back(grad_low * gain_ref[...], normed, factor)
    grad_ref[...] = grad.reshape(grad_ref.shape)
    low_ref[...] = grad.astype(BF16)
    branch_ref[...] = low_ref[...].reshape(branch_ref.shape)
    heads = home_ref.shape[0] // 2
    side_ref[...] = jnp.zeros_like(side_ref)
    index = 0
    for piece in pieces:
        n = piece.shape[2]
        for inner in range(piece.shape[0]):
            at = place_ref[index]
            columns = pl.ds(pl.multiple_of((at % heads) * n, n), n)
            side_ref[at // heads] += dot(low_ref[:, columns], piece[inner], ((1,), (1,)))
            index += 1
    part = home_ref.shape[3]
    for c in range(2):
        for d in range(heads):
            home = side_ref[c, :, d * part : (d + 1) * part].astype(BF16)
            home_ref[c * heads + d] = home.reshape(home_ref.shape[1:])


def branch_back(place, pieces, keep, near, own, residual, top, gain):
    args = (*pieces, keep, near, own, residual, top, gain)
    seqs, block, width = residual.shape
    tall = pieces[0].shape[1]
    shapes = (
        jax.ShapeDtypeStruct(residual.shape, F32),
        jax.ShapeDtypeStruct(residual.shape, BF16),
        jax.ShapeDtypeStruct((8, seqs, block, tall // 4), BF16),
        jax.ShapeDtypeStruct((1, width), F32),
    )
    return pl.pallas_call(
        branch_back_kernel,
        grid=(1,),
        in_specs=[SCALARS]
        + [whole(piece) for piece in pieces]
        + [pl.BlockSpec((1, seqs * block, width), lambda *_: (0, 0, 0))] * 2
        + [whole(a) for a in args[8:]],
        out_specs=tuple(whole(shape) for shape in shapes),
        out_shape=shapes,
        scratch_shapes=[
            pltpu.VMEM((seqs * block, width), BF16),
            pltpu.VMEM((2, seqs * block, tall), F32),
        ],
        compiler_params=params(24),
        cost_estimate=COST,
        name="branch_back",
    )(place, *args)


def attend_back_kernel(
    place_ref, q_ref, k_ref, v_ref, grad_ref, att_ref, log_ref, cosq_ref, sinq_ref, cos_ref,
    sin_ref, w_ref, low_ref, *refs, seq, last,
):
    if last:
        before_ref, gain1_ref, gain2_ref, keep_ref, send_ref, grad_w_ref, *scratch = refs
    else:
        keep_ref, send_ref, before_ref, *scratch = refs
    proj_ref, sum_k, sum_v = scratch
    step = pl.program_id(0)
    block, part = q_ref.shape[2], q_ref.shape[3]

    @pl.when(step == 0)
    def _():
        sum_k[...] = jnp.zeros_like(sum_k)
        sum_v[...] = jnp.zeros_like(sum_v)

    queries, keys, values = flat(q_ref[...]), flat(k_ref[...]), flat(v_ref[...])
    grads = jnp.concatenate([grad_ref[place_ref[2 * step + inner], seq] for inner in range(2)])
    along = (grads.astype(F32) * flat(att_ref[...])).T
    logs = flat(log_ref[...]).T
    grad_queries = jnp.zeros(queries.shape, F32)
    for head, mask in enumerate(head_masks(queries.shape)):
        own_q = jnp.where(mask, queries, 0)
        own_g = jnp.where(mask, grads, 0)
        scores = dot(keys, own_q, ((1,), (1,)))
        weights = jnp.exp(scores - logs[head * HD : head * HD + 1])
        lifted = dot(values, own_g, ((1,), (1,)))
        row = jnp.sum(along[head * HD : (head + 1) * HD], axis=0, keepdims=True)
        grad_scores = (weights * (lifted - row)).astype(BF16)
        sum_k[...] += dot(grad_scores, own_q)
        sum_v[...] += dot(weights.astype(BF16), own_g)
        grad_queries = jnp.where(mask, dot(grad_scores, keys, ((0,), (0,))), grad_queries)
    grad_queries = lane_rotate(grad_queries * HD**-0.5, cosq_ref[...], -sinq_ref[...])
    rows = pl.multiple_of(step * 2 * block, 2 * block)
    proj_ref[pl.ds(rows, 2 * block), :part] = grad_queries.astype(BF16)

    @pl.when(step == 3)
    def _():
        grad_keys = lane_rotate(sum_k[...], cos_ref[...], -sin_ref[...])
        proj_ref[:, part : 2 * part] = grad_keys.astype(BF16)
        proj_ref[:, 2 * part :] = sum_v[...].astype(BF16)
        partial = dot(proj_ref[...], w_ref[...], ((1,), (1,))).astype(BF16)
        keep_ref[...] = partial[: 5 * block].reshape(5, block, -1)
        send_ref[...] = partial[5 * block :].reshape(3, block, -1)
        grad_w = dot(proj_ref[...], flat(low_ref[...]), ((0,), (0,)))
        if last:
            grad_w = (grad_w + before_ref[...]).T
            along_w = jnp.sum(grad_w * wide(w_ref[...]), axis=1, keepdims=True)
            along_w = jnp.broadcast_to(along_w, (w_ref.shape[0], 128)).T[:1] / gain1_ref[...]
            row = lax.broadcasted_iota(jnp.int32, (GAIN_ROWS, w_ref.shape[0]), 0)
            gains = jnp.where(row == 0, along_w, jnp.where(row == 1, gain2_ref[...], 0.0))
            n = grad_w_ref.shape[1] - GAIN_ROWS
            for at in range(grad_w_ref.shape[0]):
                part_rows = slice(at * n, (at + 1) * n)
                grad_w_ref[at, :n] = grad_w[part_rows].astype(BF16)
                grad_w_ref[at, n:, :n] = gains[:, part_rows].astype(BF16)
                rest = grad_w_ref.shape[2] - n
                grad_w_ref[at, n:, n:] = jnp.zeros((GAIN_ROWS, rest), BF16)
        else:
            before_ref[...] = grad_w


GAIN_ROWS = 16


def attend_back(place, qkv, grads, attended, logs, cosine, sine, w, low, seq, *before, dp=1):
    _, _, block, own = qkv.shape
    part, width = own // 3, w.shape[0]
    last = len(before) > 0
    rows = pl.BlockSpec((2, 1, block, part), lambda i: (i, 0, 0, 0))
    angles = pl.BlockSpec((2 * block, part), lambda i: (i, 0))

    def full(*shape):
        return pl.BlockSpec(shape, lambda i: (0,) * len(shape))

    args = [place, qkv, qkv, qkv, grads, attended, logs, cosine, sine, cosine, sine, w, low]
    in_specs = [
        SCALARS,
        pl.BlockSpec((2, 1, block, part), lambda i: (i, seq, 0, 0)),
        pl.BlockSpec((8, 1, block, part), lambda i: (0, seq, 0, 1)),
        pl.BlockSpec((8, 1, block, part), lambda i: (0, seq, 0, 2)),
        whole(grads),
        rows,
        rows,
        angles,
        angles,
        whole(cosine),
        whole(sine),
        whole(w),
        pl.BlockSpec((8, 1, block, width), lambda i: (0, seq, 0, 0)),
    ]
    shapes = [((5, block, width), BF16), ((3, block, width), BF16)]
    if last:
        args += before
        in_specs += [whole(array) for array in before]
        shapes += [((dp, width // dp + GAIN_ROWS, own), BF16)]
    else:
        shapes += [((own, width), F32)]
    return pl.pallas_call(
        functools.partial(attend_back_kernel, seq=seq, last=last),
        grid=(4,),
        in_specs=in_specs,
        out_specs=tuple(full(*shape) for shape, _ in shapes),
        out_shape=tuple(jax.ShapeDtypeStruct(shape, kind) for shape, kind in shapes),
        scratch_shapes=[
            pltpu.VMEM((8 * block, own), BF16),
            pltpu.VMEM((8 * block, part), F32),
            pltpu.VMEM((8 * block, part), F32),
        ],
        compiler_params=params(60),
        cost_estimate=COST,
        name="attend_back",
    )(*args)


def input_grad_kernel(*refs):
    keeps, (near_ref, own_ref, tokens_ref, residual_ref, gain_ref, out_ref) = refs[:-6], refs[-6:]
    block = tokens_ref.shape[1]
    for seq, keep in enumerate(keeps):
        rows = slice(seq * block, (seq + 1) * block)
        grad = wide(keep[0, :block]) + wide(near_ref[0, rows]) + wide(own_ref[0, rows])
        normed, factor = normalize(wide(tokens_ref[seq]))
        out_ref[seq] = residual_ref[seq] + norm_back(grad * gain_ref[...], normed, factor)


def input_grad(keeps, near, own, tokens, residual, gain):
    rest = (own, tokens, residual, gain)
    return pl.pallas_call(
        input_grad_kernel,
        grid=(1,),
        in_specs=[
            pl.BlockSpec((1, *array.shape[1:]), lambda *_: (0, 0, 0)) for array in (*keeps, near)
        ]
        + [whole(array) for array in rest],
        out_specs=whole(residual),
        out_shape=jax.ShapeDtypeStruct(residual.shape, F32),
        compiler_params=params(16),
        cost_estimate=COST,
        name="input_grad",
    )(*keeps, near, *rest)


def finish_kernel(keep_ref, rows_ref, near_ref, home_ref, residual_ref, out_ref, grad_ref):
    rows = keep_ref.shape[1]
    total = wide(keep_ref[0]) + wide(near_ref[0, :rows]) + wide(home_ref[0, :rows])
    out_ref[...] = (residual_ref[...] + total.reshape(residual_ref.shape)).astype(BF16)
    total = wide(rows_ref[0]) + wide(near_ref[0, rows:]) + wide(home_ref[0, rows:])
    n = grad_ref.shape[2]
    for at in range(grad_ref.shape[0]):
        grad_ref[at] = total[:, at * n : (at + 1) * n].astype(BF16)


def finish(keep, rows, near, home, residual, dp):
    args = (keep, rows, near, home)
    shapes = (
        jax.ShapeDtypeStruct(residual.shape, BF16),
        jax.ShapeDtypeStruct((dp, rows.shape[1], rows.shape[2] // dp), BF16),
    )
    return pl.pallas_call(
        finish_kernel,
        grid=(1,),
        in_specs=[pl.BlockSpec((1, *array.shape[1:]), lambda *_: (0, 0, 0)) for array in args]
        + [whole(residual)],
        out_specs=tuple(whole(shape) for shape in shapes),
        out_shape=shapes,
        compiler_params=params(16),
        cost_estimate=COST,
        name="finish",
    )(*args, residual)


class Group:
    def __init__(self):
        self.heads = lax.axis_size("head")
        self.dp = lax.axis_size("dp")
        self.ctx_at = lax.axis_index("ctx")
        self.head_at = lax.axis_index("head")
        self.dp_at = lax.axis_index("dp")
        self.at = self.ctx_at * self.heads + self.head_at
        near, far = [], []
        for c in range(2):
            for h in range(self.heads):
                x, y = (c ^ 1) * self.heads + h, c * self.heads + (h ^ 2)
                near.append((c * self.heads + h, x if h % 2 == 0 else y))
                far.append((c * self.heads + h, y if h % 2 == 0 else x))
        self.near, self.far = near, far

    def order(self):
        first = jnp.where(self.head_at % 2 == 0, 4, 2)
        second = 6 - first
        return jnp.stack(
            [self.at ^ bits for bits in (0, 1, first, first ^ 1, 6, second ^ 1, second, 7)]
        )

    def swap(self, values, bit):
        if bit == 4:
            return lax.ppermute(values, "ctx", [(0, 1), (1, 0)])
        return lax.ppermute(values, "head", [(i, i ^ bit) for i in range(self.heads)])

    def mate(self, values):
        return self.swap(values, 1)

    def to_near(self, values):
        return lax.ppermute(values, GROUP, self.near)

    def to_far(self, values):
        return lax.ppermute(values, GROUP, self.far)

    def rows_back(self, values, place):
        pairs, same = [], False
        for d in range(self.dp):
            for h in range(self.heads):
                if (d, h) == (place[h], d):
                    same = same | ((self.dp_at == d) & (self.head_at == h))
                else:
                    pairs.append((d * self.heads + h, place[h] * self.heads + d))
        return jnp.where(same, values, lax.ppermute(values, ("dp", "head"), pairs))

    def across(self, values, step):
        return lax.ppermute(values, "dp", [(i, i ^ step) for i in range(self.dp)])


def pick(array, index, axis):
    return lax.dynamic_index_in_dim(array, index, axis, keepdims=False)


def after(values, *earlier):
    return lax.optimization_barrier((values, earlier))[0]


def local_split(tokens, cotangent, w_qkv, w_attn_out, w_in, w_mlp_out, norm_gain1, norm_gain2):
    seqs, block, width = tokens.shape
    group = Group()
    heads, dp = group.heads, group.dp
    at_c, at_h = group.ctx_at, group.head_at
    parts = 2 * heads
    hidden = w_in.shape[1] // 2 // parts
    padded = -(-hidden // 128) * 128
    own_width = width // parts
    half = heads // 2
    rows_here = w_qkv.shape[0]
    place = [2 * (h % half) + h // half for h in range(heads)]
    straight = list(range(heads))
    order = group.order()
    scalars = jnp.concatenate([order, jnp.stack([group.dp_at, at_c])]).astype(jnp.int32)
    mate, near, far = group.mate, group.to_near, group.to_far

    def in_order(own, other):
        return jnp.where(at_c == 0, jnp.stack([own, other]), jnp.stack([other, own]))

    def exchange(values):
        return lax.all_to_all(values, GROUP, split_axis=0, concat_axis=0, tiled=True)


    gains = jnp.pad(
        jnp.stack([norm_gain1, norm_gain2]), ((0, 14), (0, 3 * own_width - rows_here))
    )
    qkv_view = w_qkv.reshape(rows_here, 3, width)

    def qkv_part(at):
        start = (2 * at_h + at) * own_width
        cut = lax.dynamic_slice_in_dim(qkv_view, start, own_width, 2)
        return jnp.concatenate([cut.reshape(rows_here, 3 * own_width), gains])

    x_own = tokens[None]
    x_mate = mate(x_own)
    qkv_other, qkv_own = qkv_part(1 - at_c), qkv_part(at_c)
    qkv_cross = group.swap(after(qkv_other, x_own), 4)
    in_view = after(w_in, qkv_other).reshape(rows_here, 2, heads, 2, hidden)
    in_view = pick(in_view, 2 * (at_h % half) + at_h // half, 2)

    def in_part(at):
        cut = pick(in_view, at, 2)
        return jnp.pad(cut, ((0, 0), (0, 0), (0, padded - hidden))).reshape(rows_here, 2 * padded)

    in_other, in_own = in_part(1 - at_c), in_part(at_c)
    in_cross = group.swap(in_other, 4)
    x_chip = jnp.concatenate([x_own, after(x_mate, qkv_cross, qkv_own, in_cross, in_own)])
    x_near = near(x_chip)
    qkv_pair = jnp.stack([qkv_own, qkv_cross])
    qkv_pieces = [qkv_pair] + [group.across(qkv_pair, step) for step in range(1, dp)]

    slices = jnp.concatenate([w_attn_out, w_mlp_out])
    slices = after(slices, x_near, *qkv_pieces)
    slices = lax.dynamic_slice_in_dim(slices, at_h * (width // heads), width // heads, 1)
    slices = jnp.pad(slices, ((0, 64), (0, 0)))
    slices = lax.all_gather(slices, "dp", axis=0)
    positions = after(order, qkv_pair)[:, None] * block + jnp.arange(block, dtype=jnp.int32)
    lane = jnp.arange(own_width, dtype=jnp.int32)
    frequency = jnp.exp(
        (lane % (HD // 2)).astype(F32) * (-math.log(ROPE_BASE) / (HD // 2))
    )
    angles = wide(positions.reshape(-1))[:, None] * frequency[None, :]
    cosine = jnp.cos(angles)
    sine = jnp.sin(angles) * jnp.where(lane % HD < HD // 2, -1.0, 1.0)[None, :]

    x_far = far(x_near[:1])
    x_near = after(x_near, *qkv_pieces, cosine, sine)
    x_near_mate = mate(x_near)
    cot_own = after(cotangent, x_near)[None]
    cot_mate = mate(cot_own)
    in_pair, x_far = lax.optimization_barrier((in_order(in_own, in_cross), x_far))
    weight_in = lax.all_gather(in_pair, "dp", axis=0).reshape(width, -1)
    cot_chip = jnp.concatenate([cot_own, cot_mate])
    x_far = after(x_far, cot_chip)
    x_far_mate = mate(x_far)

    cot_near = near(after(cot_chip, x_far))
    out_rows = w_attn_out.shape[0]
    x_pieces = (x_own, x_mate, x_near, x_far, x_near_mate, x_far_mate)
    low1, qkv, weight_qkv, gain_one, gain_two = project(
        scalars, x_pieces, qkv_pieces, cosine, sine
    )

    slices = after(slices, qkv)
    out_own = slices[:, :out_rows].reshape(1, dp * out_rows, -1)
    out_mate = mate(out_own)
    mlp_slices = jnp.stack(
        [slices[place[h], out_rows : out_rows + hidden] for h in range(heads)]
    )
    mlp_slices = lax.all_to_all(mlp_slices, "head", split_axis=0, concat_axis=0, tiled=True)
    out_near = near(jnp.concatenate([out_own, out_mate]))
    att_0, log_0, home_0 = attend(scalars, after(qkv, out_mate))
    cot_near = after(cot_near, home_0)
    cot_far, cot_near_mate = far(cot_near[:1]), mate(cot_near)
    out_near = after(out_near, home_0)
    out_far, out_near_mate = far(out_near[:1]), mate(out_near)
    att_1, log_1, home = attend(scalars, after(qkv, cot_near, out_near), home_0)
    home, cot_far, out_far = lax.optimization_barrier((home, cot_far, out_far))
    att_rows = exchange(home)
    out_far_mate, cot_far_mate = mate(after(out_far, home)), mate(after(cot_far, home))
    out_pieces = (out_own, out_mate, out_near, out_far, out_near_mate, out_far_mate)
    weight_mlp = jnp.moveaxis(after(mlp_slices, home), 0, 1).reshape(hidden, width)
    weight_mlp = jnp.pad(weight_mlp, ((0, padded - hidden), (0, 0)))
    residual, low2 = branch(
        scalars, out_pieces, after(att_rows, cot_far_mate, weight_mlp, weight_in), tokens, gain_two
    )

    low_own = low2[None]
    low_mate = mate(low_own)
    low_near = near(jnp.concatenate([low_own, low_mate]))
    *arrays, keep_a = mlp(
        (low_own, low_mate), (cot_own, cot_mate), weight_in, weight_mlp, 0, (2,)
    )
    low_near = after(low_near, keep_a)
    low_far, low_near_mate = far(low_near[:1]), mate(low_near)
    *arrays, keep_b = mlp((low_near,), (cot_near,), weight_in, weight_mlp, 2, (2,), arrays)
    low_far_mate = mate(after(low_far, keep_b))
    low2_all, cot_all, mixed, grad_lifted, keep_c, send = mlp(
        (low_far, low_near_mate, low_far_mate),
        (cot_far, cot_near_mate, cot_far_mate),
        weight_in,
        weight_mlp,
        4,
        (1, 4),
        arrays,
    )

    def over_tokens(left, right):
        return dot(flat(left), flat(right), ((0,), (0,)))

    def scatter(values):
        return lax.psum_scatter(values.astype(BF16), "dp", scatter_dimension=0, tiled=True)

    def columns_first(values):
        return jnp.moveaxis(values.reshape(values.shape[0], dp, -1), 1, 0)

    rows = seqs * block

    def by_rows(values):
        return values.reshape(values.shape[0], -1, width)

    keep_a, keep_b, keep_c, send = (by_rows(array) for array in (keep_a, keep_b, keep_c, send))
    met = mate(send)
    last = combine([(rows, [(keep_c, 0, 0), (met, 2, 0)])])
    last_far = far(last)
    grad_in = over_tokens(low2_all, after(grad_lifted, last)).astype(BF16)
    last_far, grad_in = lax.optimization_barrier((last_far, grad_in))
    grad_in = scatter(grad_in)
    chip = combine(
        [(rows, [(keep_b, 0, 0), (met, 0, 0), (last_far, 0, 0)])],
        [(rows, [(keep_b, 1, 0), (met, 1, 0)])],
    )
    chip_near = near(chip)
    mixed = after(mixed, chip)
    grad_mlp = columns_first(over_tokens(mixed, cot_all)[:hidden]).astype(BF16)
    cut = 5 * rows
    mixed_flat = flat(mixed)
    out_keep = dot(mixed_flat[:cut], weight_mlp).astype(BF16).reshape(5, rows, width)
    out_send = dot(mixed_flat[cut:], weight_mlp).astype(BF16).reshape(3, rows, width)
    chip_near, grad_mlp = lax.optimization_barrier(
        (after(chip_near, out_keep, out_send), grad_mlp)
    )
    grad_mlp = scatter(grad_mlp)[0]
    home = mate(combine([(rows, [(keep_a, 1, 0), (chip_near, 1, 0)])])[0])
    out_met = mate(after(out_send, chip_near))
    grad_residual, grad_branch, home, gain2_sum = branch_back(
        scalars, out_pieces, keep_a, chip_near, home, residual, cotangent, gain_two
    )
    grad_home = exchange(home)

    rows_keep, rows_send = out_grad(scalars, after(att_rows, home), grad_branch)
    rows_met = mate(rows_send)
    few = rows_keep.shape[1]

    def ends(index, at, *more):
        kept = [(out_keep, index, 0)], [(rows_keep, index, 0)]
        if at is not None:
            kept[0].append((out_met, at, 0))
            kept[1].append((rows_met, at, 0))
        for array, where in more:
            kept[0].append((array, where, 0))
            kept[1].append((array, where, rows))
        return [(rows, kept[0]), (few, kept[1])]

    end_last = combine(ends(4, 2))
    in_parts = after(grad_in, home).reshape(2, rows_here, -1)
    in_cross = group.swap(pick(in_parts, 1 - at_c, 0), 4)
    grad_home = after(grad_home, end_last, in_cross)
    end_far = far(after(end_last, grad_home))
    grad_mlp = group.rows_back(after(grad_mlp, grad_home), place)
    keep_0, send_0, before = attend_back(
        scalars, qkv, grad_home, att_0, log_0, cosine, sine, weight_qkv, low1, 0
    )
    met_0 = mate(send_0)
    end_far = after(end_far, send_0)
    end_chip = combine(ends(2, 0, (end_far, 0)), ends(3, 1))
    end_near = near(end_chip)
    keep_1, send_1, grad_qkv = attend_back(
        scalars, qkv, after(grad_home, end_chip), att_1, log_1, cosine, sine,
        weight_qkv, low1, 1, before, gain_one, gain2_sum, dp=dp,
    )

    grad_qkv = scatter(grad_qkv.reshape(-1, grad_qkv.shape[2]))
    met_1 = mate(send_1)

    def both(index, at, *more):
        kept = [(keep_0, index, 0)], [(keep_1, index, 0)]
        if at is not None:
            kept[0].append((met_0, at, 0))
            kept[1].append((met_1, at, 0))
        for array, where in more:
            kept[0].append((array, where, 0))
            kept[1].append((array, where, block))
        return [(block, kept[0]), (block, kept[1])]

    last = combine(both(4, 2))
    last_far = far(last)
    grad_in = in_order(after(pick(in_parts, at_c, 0), last), in_cross)
    late = at_h // half
    grad_in = jnp.stack([grad_in[..., :hidden], grad_in[..., padded : padded + hidden]])
    last_far, grad_in = lax.optimization_barrier((last_far, grad_in))
    chip = combine(both(2, 0, (last_far, 0)), both(3, 1))
    chip_near = near(chip)

    end_home = mate(combine(ends(1, None, (after(end_near, chip), 1))))
    result, grad_out = finish(out_keep, rows_keep, end_near, end_home, residual, dp)
    chip_near, grad_out = lax.optimization_barrier((chip_near, grad_out))
    grad_out = scatter(grad_out)[0]
    grad_in = after(grad_in, chip)
    stays = pick(grad_in, late, 0)
    comes = group.swap(pick(grad_in, 1 - late, 0), half)
    grad_qkv = after(grad_qkv, chip)
    both_rows = 2 * rows_here
    qkv_parts = grad_qkv[:both_rows].reshape(2, rows_here, -1)
    gains = grad_qkv[both_rows:]
    cross = jnp.concatenate([pick(qkv_parts, 1 - at_c, 0), gains])
    cross = group.swap(cross, 4)
    chip_near = after(chip_near, comes, result, cross)
    home = combine(both(1, None, (chip_near, 1)))
    cross = after(cross, home)
    home = mate(home)
    grad_qkv = in_order(pick(qkv_parts, at_c, 0), cross[:rows_here])
    gains = (wide(gains) + wide(cross[rows_here:])).astype(BF16)
    gains = wide(gains) + sum(wide(group.swap(gains, bit)) for bit in range(1, heads))
    grad_input = input_grad((keep_0, keep_1), chip_near, home, tokens, grad_residual, gain_one)
    grad_out, grad_input = lax.optimization_barrier((grad_out, grad_input))
    grad_out = wide(group.rows_back(grad_out, straight))

    grad_mlp = wide(grad_mlp)
    grad_in = jnp.where(
        late == 0, jnp.concatenate([stays, comes]), jnp.concatenate([comes, stays])
    )
    grad_in = wide(jnp.moveaxis(grad_in, 0, 1).reshape(rows_here, -1))

    per_device = width // (dp * parts)
    start = group.at * per_device
    grad_gain1, grad_gain2 = (
        lax.dynamic_slice_in_dim(gains[i], start, per_device, 0) for i in range(2)
    )
    grad_qkv = grad_qkv.reshape(2, rows_here, 3, own_width)
    grad_qkv = jnp.moveaxis(grad_qkv, 2, 0)
    odd = at_h % 2
    stays = pick(grad_qkv, odd + late, 0)
    core = group.swap(pick(grad_qkv, 1 - odd + late, 0), 1)
    chip = group.swap(pick(grad_qkv, 2 - 2 * late, 0), 2)
    grad_qkv = jnp.where(
        odd == 0, jnp.concatenate([stays, core, chip]), jnp.concatenate([chip, core, stays])
    )
    grad_qkv = wide(jnp.moveaxis(grad_qkv, 0, 1).reshape(rows_here, -1))

    return (
        result,
        grad_input,
        grad_qkv,
        grad_out,
        grad_in,
        grad_mlp,
        grad_gain1,
        grad_gain2,
    )


def local(tokens, cotangent, w_qkv, w_attn_out, w_in, w_mlp_out, norm_gain1, norm_gain2):
    args = (tokens, cotangent, w_qkv, w_attn_out, w_in, w_mlp_out, norm_gain1, norm_gain2)
    sizes = [lax.axis_size(axis) for axis in ("dp", "ctx", "head")]
    if sizes == [4, 2, 4] and tokens.shape[2] == 8 * 2 * HD and tokens.shape[1] % 16 == 0:
        return local_split(*args)
    return local_general(*args)


def solution(mesh):
    in_specs = (
        P("dp", ("ctx", "head"), None),
        P("dp", ("ctx", "head"), None),
        P(("dp", "ctx"), None),
        P(("dp", "ctx"), None),
        P(("dp", "ctx"), None),
        P(("dp", "ctx"), None),
        P(("dp", "ctx")),
        P(("dp", "ctx")),
    )
    out_specs = (
        P("dp", ("ctx", "head"), None),
        P("dp", ("ctx", "head"), None),
        P(("dp", "ctx"), "head"),
        P(("dp", "ctx"), "head"),
        P(("dp", "ctx"), "head"),
        P(("dp", "ctx"), "head"),
        P(("dp", "ctx", "head")),
        P(("dp", "ctx", "head")),
    )
    return jax.shard_map(local, mesh=mesh, in_specs=in_specs, out_specs=out_specs, check_vma=False)
```

```python
import functools
import math

import jax
import jax.numpy as jnp
from jax import lax
from jax.experimental import pallas as pl
from jax.experimental.pallas import tpu as pltpu
from jax.sharding import PartitionSpec as P

HD = 64


EPSILON = 1e-05
ROPE_BASE = 160000.0


def normalize(values):
    centre = jnp.mean(values, axis=-1, keepdims=True)
    shifted = values - centre
    spread = jnp.mean(shifted * shifted, axis=-1, keepdims=True)
    factor = lax.rsqrt(spread + EPSILON)
    return (shifted * factor, factor)


def norm_back(grad_normed, normed, factor):
    grad_centre = jnp.mean(grad_normed, axis=-1, keepdims=True)
    grad_along = jnp.mean(grad_normed * normed, axis=-1, keepdims=True)
    return (grad_normed - grad_centre - normed * grad_along) * factor


def rope_tables(positions, half_size):
    frequency = jnp.exp(
        jnp.arange(half_size, dtype=jnp.float32) * (-math.log(ROPE_BASE) / half_size)
    )
    angles = positions[:, None] * frequency[None, :]
    return (jnp.cos(angles), jnp.sin(angles))


def rotate(values, cosine, sine_table, direction):
    half_size = cosine.shape[-1]
    first_half = values[..., :half_size]
    second_half = values[..., half_size:]
    cos_part = cosine[:, None, :]
    sin_part = sine_table[:, None, :] * direction
    return jnp.concatenate(
        [
            first_half * cos_part - second_half * sin_part,
            second_half * cos_part + first_half * sin_part,
        ],
        axis=-1,
    )


def block_scores(queries4, keys_block, scale):
    keys4 = keys_block.reshape(
        keys_block.shape[0], keys_block.shape[1], queries4.shape[2], queries4.shape[3]
    )
    return (
        jnp.einsum("sqgd,skgd->sgqk", queries4, keys4, preferred_element_type=jnp.float32) * scale
    )


def attend_forward(queries4, keys_all, values_all, key_rows, scale):
    seqs_here, query_rows, groups, head_size = queries4.shape
    turns = keys_all.shape[1] // key_rows

    def statistics(turn, carry):
        row_peak, row_total = carry
        keys_block = lax.dynamic_slice_in_dim(keys_all, turn * key_rows, key_rows, 1)
        scores = block_scores(queries4, keys_block, scale)
        new_peak = jnp.maximum(row_peak, jnp.max(scores, axis=-1))
        row_total = row_total * jnp.exp(row_peak - new_peak) + jnp.sum(
            jnp.exp(scores - new_peak[..., None]), axis=-1
        )
        return (new_peak, row_total)

    start_peak = jnp.full((seqs_here, groups, query_rows), -1e30, jnp.float32)
    row_peak, row_total = lax.fori_loop(
        0, turns, statistics, (start_peak, jnp.zeros_like(start_peak))
    )
    log_total = row_peak + jnp.log(row_total)

    def accumulate(turn, running):
        keys_block = lax.dynamic_slice_in_dim(keys_all, turn * key_rows, key_rows, 1)
        values_block = lax.dynamic_slice_in_dim(values_all, turn * key_rows, key_rows, 1).reshape(
            seqs_here, key_rows, groups, head_size
        )
        weights = jnp.exp(block_scores(queries4, keys_block, scale) - log_total[..., None]).astype(
            jnp.bfloat16
        )
        return running + jnp.einsum(
            "sgqk,skgd->sqgd", weights, values_block, preferred_element_type=jnp.float32
        )

    attended = lax.fori_loop(
        0, turns, accumulate, jnp.zeros((seqs_here, query_rows, groups, head_size), jnp.float32)
    )
    return (attended, log_total)


def attend_backward(queries4, keys_all, values_all, grad_out4, log_total, along, key_rows, scale):
    seqs_here, query_rows, groups, head_size = queries4.shape
    length = keys_all.shape[1]
    width_group = groups * head_size
    turns = length // key_rows

    def step_back(turn, carry):
        grad_queries, grad_keys, grad_values = carry
        keys_block = lax.dynamic_slice_in_dim(keys_all, turn * key_rows, key_rows, 1)
        keys4 = keys_block.reshape(seqs_here, key_rows, groups, head_size)
        values4 = lax.dynamic_slice_in_dim(values_all, turn * key_rows, key_rows, 1).reshape(
            seqs_here, key_rows, groups, head_size
        )
        weights = jnp.exp(block_scores(queries4, keys_block, scale) - log_total[..., None])
        grad_weights = jnp.einsum(
            "sqgd,skgd->sgqk", grad_out4, values4, preferred_element_type=jnp.float32
        )
        grad_scores = (weights * (grad_weights - along[..., None])).astype(jnp.bfloat16)
        grad_queries = grad_queries + jnp.einsum(
            "sgqk,skgd->sqgd", grad_scores, keys4, preferred_element_type=jnp.float32
        )
        key_part = (
            jnp.einsum("sgqk,sqgd->skgd", grad_scores, queries4, preferred_element_type=jnp.float32)
            * scale
        )
        value_part = jnp.einsum(
            "sgqk,sqgd->skgd",
            weights.astype(jnp.bfloat16),
            grad_out4,
            preferred_element_type=jnp.float32,
        )
        grad_keys = lax.dynamic_update_slice_in_dim(
            grad_keys, key_part.reshape(seqs_here, key_rows, width_group), turn * key_rows, 1
        )
        grad_values = lax.dynamic_update_slice_in_dim(
            grad_values, value_part.reshape(seqs_here, key_rows, width_group), turn * key_rows, 1
        )
        return (grad_queries, grad_keys, grad_values)

    start = (
        jnp.zeros((seqs_here, query_rows, groups, head_size), jnp.float32),
        jnp.zeros((seqs_here, length, width_group), jnp.float32),
        jnp.zeros((seqs_here, length, width_group), jnp.float32),
    )
    grad_queries, grad_keys, grad_values = lax.fori_loop(0, turns, step_back, start)
    return (grad_queries * scale, grad_keys, grad_values)


def local_general(tokens, cotangent, w_qkv, w_attn_out, w_in, w_mlp_out, norm_gain1, norm_gain2):
    seqs_here, block_rows, width = tokens.shape
    count_rows = seqs_here * block_rows
    heads_all = width // HD
    head_devices = lax.axis_size("head")
    group_devices = lax.axis_size(("dp", "ctx"))
    groups = heads_all // head_devices
    width_group = groups * HD
    scale = HD ** (-0.5)
    ff_width = w_in.shape[1] // 2
    full_qkv, full_out, full_in, full_mlp, gain_one, gain_two = (
        lax.all_gather(w_qkv, ("dp", "ctx"), axis=0, tiled=True),
        lax.all_gather(w_attn_out, ("dp", "ctx"), axis=0, tiled=True),
        lax.all_gather(w_in, ("dp", "ctx"), axis=0, tiled=True),
        lax.all_gather(w_mlp_out, ("dp", "ctx"), axis=0, tiled=True),
        lax.all_gather(norm_gain1, ("dp", "ctx"), axis=0, tiled=True),
        lax.all_gather(norm_gain2, ("dp", "ctx"), axis=0, tiled=True),
    )
    x_in = tokens.astype(jnp.float32).reshape(count_rows, width)
    normed1, factor1 = normalize(x_in)
    lowered1 = (normed1 * gain_one.astype(jnp.float32)).astype(jnp.bfloat16)
    projected = jnp.dot(lowered1, full_qkv, preferred_element_type=jnp.float32).reshape(
        seqs_here, block_rows, 3, heads_all, HD
    )
    first_pos = (lax.axis_index("ctx") * head_devices + lax.axis_index("head")) * block_rows
    positions = (first_pos + jnp.arange(block_rows, dtype=jnp.int32)).astype(jnp.float32)
    cosine, sine_table = rope_tables(positions, HD // 2)
    queries = (
        rotate(projected[:, :, 0], cosine, sine_table, 1.0)
        .astype(jnp.bfloat16)
        .reshape(seqs_here, block_rows, width)
    )
    keys_local = (
        rotate(projected[:, :, 1], cosine, sine_table, 1.0)
        .astype(jnp.bfloat16)
        .reshape(seqs_here, block_rows, width)
    )
    values_local = projected[:, :, 2].astype(jnp.bfloat16).reshape(seqs_here, block_rows, width)
    queries_h, keys_h, values_h = (
        lax.all_to_all(queries, "head", split_axis=2, concat_axis=1, tiled=True),
        lax.all_to_all(keys_local, "head", split_axis=2, concat_axis=1, tiled=True),
        lax.all_to_all(values_local, "head", split_axis=2, concat_axis=1, tiled=True),
    )
    query_rows = queries_h.shape[1]
    queries4 = queries_h.reshape(seqs_here, query_rows, groups, HD)
    keys_all, values_all = (
        lax.all_gather(keys_h, "ctx", axis=1, tiled=True),
        lax.all_gather(values_h, "ctx", axis=1, tiled=True),
    )
    key_rows = math.gcd(keys_all.shape[1], 1024)
    attended, log_total = attend_forward(queries4, keys_all, values_all, key_rows, scale)
    attended_low = attended.astype(jnp.bfloat16).reshape(seqs_here, query_rows, width_group)
    back_rows = lax.all_to_all(
        attended_low, "head", split_axis=1, concat_axis=2, tiled=True
    ).reshape(count_rows, width)
    residual = x_in + jnp.dot(back_rows, full_out, preferred_element_type=jnp.float32)
    normed2, factor2 = normalize(residual)
    lowered2 = (normed2 * gain_two.astype(jnp.float32)).astype(jnp.bfloat16)
    lifted = jnp.dot(lowered2, full_in, preferred_element_type=jnp.float32)
    first_part = lifted[:, :ff_width]
    second_part = lifted[:, ff_width:]
    activated, gelu_pullback = jax.vjp(
        lambda entries: jax.nn.gelu(entries, approximate=False), first_part
    )
    mixed = (activated * second_part).astype(jnp.bfloat16)
    result = (residual + jnp.dot(mixed, full_mlp, preferred_element_type=jnp.float32)).astype(
        jnp.bfloat16
    )
    full_qkv, full_out, full_in, full_mlp, gain_one, gain_two = (
        lax.all_gather(w_qkv, ("dp", "ctx"), axis=0, tiled=True),
        lax.all_gather(w_attn_out, ("dp", "ctx"), axis=0, tiled=True),
        lax.all_gather(w_in, ("dp", "ctx"), axis=0, tiled=True),
        lax.all_gather(w_mlp_out, ("dp", "ctx"), axis=0, tiled=True),
        lax.all_gather(norm_gain1, ("dp", "ctx"), axis=0, tiled=True),
        lax.all_gather(norm_gain2, ("dp", "ctx"), axis=0, tiled=True),
    )
    keys_all, values_all = (
        lax.all_gather(keys_h, "ctx", axis=1, tiled=True),
        lax.all_gather(values_h, "ctx", axis=1, tiled=True),
    )
    grad_top = cotangent.reshape(count_rows, width)
    grad_mlp = jnp.einsum("nf,nd->fd", mixed, grad_top, preferred_element_type=jnp.float32)
    grad_mixed = jnp.einsum("nd,fd->nf", grad_top, full_mlp, preferred_element_type=jnp.float32)
    grad_first = gelu_pullback(grad_mixed * second_part)[0]
    grad_lifted = jnp.concatenate([grad_first, grad_mixed * activated], axis=-1).astype(
        jnp.bfloat16
    )
    grad_inner = jnp.einsum("nd,nf->df", lowered2, grad_lifted, preferred_element_type=jnp.float32)
    grad_lowered2 = jnp.einsum(
        "nf,df->nd", grad_lifted, full_in, preferred_element_type=jnp.float32
    )
    grad_two = jnp.sum(grad_lowered2 * normed2, axis=0)
    grad_residual = grad_top.astype(jnp.float32) + norm_back(
        grad_lowered2 * gain_two.astype(jnp.float32), normed2, factor2
    )
    grad_branch = grad_residual.astype(jnp.bfloat16)
    grad_outproj = jnp.einsum(
        "nd,ne->de", back_rows, grad_branch, preferred_element_type=jnp.float32
    )
    grad_attended = jnp.einsum(
        "ne,de->nd", grad_branch, full_out, preferred_element_type=jnp.float32
    ).astype(jnp.bfloat16)
    grad_attended_h = lax.all_to_all(
        grad_attended.reshape(seqs_here, block_rows, width),
        "head",
        split_axis=2,
        concat_axis=1,
        tiled=True,
    )
    grad_out4 = grad_attended_h.reshape(seqs_here, query_rows, groups, HD)
    along = jnp.transpose(jnp.sum(grad_out4.astype(jnp.float32) * attended, axis=-1), (0, 2, 1))
    grad_queries, grad_keys_all, grad_values_all = attend_backward(
        queries4, keys_all, values_all, grad_out4, log_total, along, key_rows, scale
    )
    grad_keys_sum, grad_values_sum = (
        lax.psum_scatter(
            grad_keys_all.astype(jnp.bfloat16), "ctx", scatter_dimension=1, tiled=True
        ).astype(jnp.float32),
        lax.psum_scatter(
            grad_values_all.astype(jnp.bfloat16), "ctx", scatter_dimension=1, tiled=True
        ).astype(jnp.float32),
    )
    grad_q_low = grad_queries.astype(jnp.bfloat16).reshape(seqs_here, query_rows, width_group)
    grad_q_tok, grad_k_tok, grad_v_tok = (
        lax.all_to_all(grad_q_low, "head", split_axis=1, concat_axis=2, tiled=True),
        lax.all_to_all(
            grad_keys_sum.astype(jnp.bfloat16), "head", split_axis=1, concat_axis=2, tiled=True
        ),
        lax.all_to_all(
            grad_values_sum.astype(jnp.bfloat16), "head", split_axis=1, concat_axis=2, tiled=True
        ),
    )
    unrot_q = rotate(
        grad_q_tok.astype(jnp.float32).reshape(seqs_here, block_rows, heads_all, HD),
        cosine,
        sine_table,
        -1.0,
    )
    unrot_k = rotate(
        grad_k_tok.astype(jnp.float32).reshape(seqs_here, block_rows, heads_all, HD),
        cosine,
        sine_table,
        -1.0,
    )
    grad_projected = jnp.concatenate(
        [
            unrot_q.reshape(count_rows, width),
            unrot_k.reshape(count_rows, width),
            grad_v_tok.astype(jnp.float32).reshape(count_rows, width),
        ],
        axis=-1,
    ).astype(jnp.bfloat16)
    grad_project = jnp.einsum(
        "nd,nf->df", lowered1, grad_projected, preferred_element_type=jnp.float32
    )
    grad_lowered1 = jnp.einsum(
        "nf,df->nd", grad_projected, full_qkv, preferred_element_type=jnp.float32
    )
    grad_one = jnp.sum(grad_lowered1 * normed1, axis=0)
    grad_input = grad_residual + norm_back(
        grad_lowered1 * gain_one.astype(jnp.float32), normed1, factor1
    )
    pieces_one = grad_one.reshape(group_devices, head_devices, -1)
    pieces_two = grad_two.reshape(group_devices, head_devices, -1)
    part_qkv, part_out, part_in, part_mlp, part_one, part_two = (
        lax.psum_scatter(
            grad_project.astype(jnp.bfloat16), ("dp", "ctx"), scatter_dimension=0, tiled=True
        ).astype(jnp.float32),
        lax.psum_scatter(
            grad_outproj.astype(jnp.bfloat16), ("dp", "ctx"), scatter_dimension=0, tiled=True
        ).astype(jnp.float32),
        lax.psum_scatter(
            grad_inner.astype(jnp.bfloat16), ("dp", "ctx"), scatter_dimension=0, tiled=True
        ).astype(jnp.float32),
        lax.psum_scatter(
            grad_mlp.astype(jnp.bfloat16), ("dp", "ctx"), scatter_dimension=0, tiled=True
        ).astype(jnp.float32),
        lax.psum_scatter(
            pieces_one.astype(jnp.bfloat16), ("dp", "ctx"), scatter_dimension=0, tiled=True
        ).astype(jnp.float32),
        lax.psum_scatter(
            pieces_two.astype(jnp.bfloat16), ("dp", "ctx"), scatter_dimension=0, tiled=True
        ).astype(jnp.float32),
    )
    final_qkv, final_out, final_in, final_mlp, final_one, final_two = (
        lax.psum_scatter(
            part_qkv.astype(jnp.bfloat16), "head", scatter_dimension=1, tiled=True
        ).astype(jnp.float32),
        lax.psum_scatter(
            part_out.astype(jnp.bfloat16), "head", scatter_dimension=1, tiled=True
        ).astype(jnp.float32),
        lax.psum_scatter(
            part_in.astype(jnp.bfloat16), "head", scatter_dimension=1, tiled=True
        ).astype(jnp.float32),
        lax.psum_scatter(
            part_mlp.astype(jnp.bfloat16), "head", scatter_dimension=1, tiled=True
        ).astype(jnp.float32),
        lax.psum_scatter(
            part_one.astype(jnp.bfloat16), "head", scatter_dimension=1, tiled=True
        ).astype(jnp.float32),
        lax.psum_scatter(
            part_two.astype(jnp.bfloat16), "head", scatter_dimension=1, tiled=True
        ).astype(jnp.float32),
    )
    return (
        result.reshape(seqs_here, block_rows, width),
        grad_input.reshape(seqs_here, block_rows, width),
        final_qkv,
        final_out,
        final_in,
        final_mlp,
        final_one.reshape(-1),
        final_two.reshape(-1),
    )


F32 = jnp.float32
BF16 = jnp.bfloat16
GROUP = ("ctx", "head")


def dot(left, right, dims=((1,), (0,))):
    return lax.dot_general(left, right, (dims, ((), ())), preferred_element_type=F32)


def wide(values):
    return values.astype(F32)


def flat(values):
    return values.reshape(-1, values.shape[-1])


def lane_rotate(values, cosine, sine_signed):
    lane = lax.broadcasted_iota(jnp.int32, values.shape, 1)
    width = values.shape[1]
    partner = jnp.where(
        lane % HD < HD // 2,
        pltpu.roll(values, width - HD // 2, 1),
        pltpu.roll(values, HD // 2, 1),
    )
    return values * cosine + partner * sine_signed


def head_masks(shape):
    lane = lax.broadcasted_iota(jnp.int32, shape, 1)
    return [lane // HD == head for head in range(shape[1] // HD)]


def params(mebibytes):
    return pltpu.CompilerParams(vmem_limit_bytes=mebibytes * 1024 * 1024)


COST = pl.CostEstimate(flops=1 << 20, transcendentals=0, bytes_accessed=1 << 16)


def whole(array):
    return pl.BlockSpec(array.shape, lambda *_: (0,) * len(array.shape))


SCALARS = pl.BlockSpec(memory_space=pltpu.SMEM)


def project_kernel(place_ref, *refs):
    pieces, weights = refs[:6], refs[6:10]
    cos_ref, sin_ref, low_ref, qkv_ref, w_ref, gain1_ref, gain2_ref, rows_ref = refs[10:]
    block, part = pieces[0].shape[2], w_ref.shape[1] // 3
    rows = gain1_ref.shape[1] // 8

    @pl.when(pl.program_id(0) == 0)
    def _():
        for step, piece in enumerate(weights):
            for turn in range(2):
                at = 2 * (place_ref[8] ^ step) + (place_ref[9] ^ turn)
                w_ref[pl.ds(pl.multiple_of(at * rows, rows), rows), :] = piece[turn, :rows]
                gains = piece[turn, rows:].astype(F32)
                rows_ref[0, pl.ds(at, 1), :] = gains[:1, :rows]
                rows_ref[1, pl.ds(at, 1), :] = gains[1:2, :rows]
        for out, at in ((gain1_ref, 0), (gain2_ref, 1)):
            for row in range(8):
                out[:, row * rows : (row + 1) * rows] = rows_ref[at, row : row + 1, :]

    gain = gain1_ref[...]
    index = 0
    for piece in pieces:
        for inner in range(piece.shape[0]):
            normed, _ = normalize(piece[inner, 0].astype(F32))
            low_ref[index, 0] = (normed * gain).astype(BF16)
            index += 1
    projected = dot(flat(low_ref[:, 0]), w_ref[...])
    cosine, sine = cos_ref[...], sin_ref[...]
    shape = (8, block, part)
    qkv_ref[:, 0, :, :part] = (
        (lane_rotate(projected[:, :part], cosine, sine) * HD**-0.5).astype(BF16).reshape(shape)
    )
    qkv_ref[:, 0, :, part : 2 * part] = (
        lane_rotate(projected[:, part : 2 * part], cosine, sine).astype(BF16).reshape(shape)
    )
    qkv_ref[:, 0, :, 2 * part :] = projected[:, 2 * part :].astype(BF16).reshape(shape)


def project(place, pieces, weights, cosine, sine):
    seqs, block, width = pieces[0].shape[1:]
    own = weights[0].shape[2]

    def by_seq(lead, last):
        return pl.BlockSpec((lead, 1, block, last), lambda s: (0, s, 0, 0))

    return pl.pallas_call(
        project_kernel,
        grid=(seqs,),
        in_specs=[SCALARS]
        + [by_seq(piece.shape[0], width) for piece in pieces]
        + [whole(w) for w in weights]
        + [whole(cosine), whole(sine)],
        out_specs=(
            by_seq(8, width),
            by_seq(8, own),
            pl.BlockSpec((width, own), lambda s: (0, 0)),
            pl.BlockSpec((1, width), lambda s: (0, 0)),
            pl.BlockSpec((1, width), lambda s: (0, 0)),
        ),
        out_shape=(
            jax.ShapeDtypeStruct((8, seqs, block, width), BF16),
            jax.ShapeDtypeStruct((8, seqs, block, own), BF16),
            jax.ShapeDtypeStruct((width, own), BF16),
            jax.ShapeDtypeStruct((1, width), F32),
            jax.ShapeDtypeStruct((1, width), F32),
        ),
        scratch_shapes=[pltpu.VMEM((2, 8, width // 8), F32)],
        compiler_params=params(60),
        cost_estimate=COST,
        name="project",
    )(place, *pieces, *weights, cosine, sine)


def attend_kernel(place_ref, q_ref, k_ref, v_ref, *refs):
    att_ref, log_ref, home_ref = refs[-3:]
    step, seq = pl.program_id(0), len(refs) - 3
    if seq:

        @pl.when(step == 0)
        def _():
            home_ref[:, :1] = refs[0][...]

    queries, keys, values = flat(q_ref[...]), flat(k_ref[...]), flat(v_ref[...])
    attended = jnp.zeros(queries.shape, F32)
    logs = jnp.zeros(queries.shape, F32)
    for mask in head_masks(queries.shape):
        scores = dot(jnp.where(mask, queries, 0), keys, ((1,), (1,)))
        peak = jnp.max(scores, axis=1, keepdims=True)
        weights = jnp.exp(scores - peak)
        total = jnp.sum(weights, axis=1, keepdims=True)
        mixed = dot(weights.astype(BF16), values) * (1.0 / total)
        attended = jnp.where(mask, mixed, attended)
        logs = jnp.where(mask, peak + jnp.log(total), logs)
    att_ref[...] = attended.reshape(att_ref.shape)
    log_ref[...] = logs.reshape(log_ref.shape)
    low = attended.astype(BF16).reshape(att_ref.shape)
    for inner in range(2):
        home_ref[place_ref[2 * step + inner], seq] = low[inner, 0]


def attend(place, qkv, *home):
    _, _, block, own = qkv.shape
    part, seq = own // 3, len(home)
    rows = pl.BlockSpec((2, 1, block, part), lambda i: (i, 0, 0, 0))
    shape = (8, 1, block, part)
    return pl.pallas_call(
        attend_kernel,
        grid=(4,),
        in_specs=[
            SCALARS,
            pl.BlockSpec((2, 1, block, part), lambda i: (i, seq, 0, 0)),
            pl.BlockSpec((8, 1, block, part), lambda i: (0, seq, 0, 1)),
            pl.BlockSpec((8, 1, block, part), lambda i: (0, seq, 0, 2)),
            *[whole(h) for h in home],
        ],
        out_specs=(
            rows,
            rows,
            pl.BlockSpec((8, 1 + seq, block, part), lambda i: (0, 0, 0, 0)),
        ),
        out_shape=(
            jax.ShapeDtypeStruct(shape, F32),
            jax.ShapeDtypeStruct(shape, F32),
            jax.ShapeDtypeStruct((8, 1 + seq, block, part), BF16),
        ),
        compiler_params=params(24),
        cost_estimate=COST,
        name="attend",
    )(place, qkv, qkv, qkv, *home)


def branch_kernel(place_ref, *refs):
    pieces = refs[:6]
    rows_ref, tokens_ref, gain_ref, residual_ref, low_ref, side_ref, total_ref = refs[6:]
    heads = rows_ref.shape[0] // 2
    for c in range(2):
        side_ref[c] = jnp.concatenate([flat(rows_ref[c * heads + d]) for d in range(heads)], axis=1)
    total_ref[...] = flat(wide(tokens_ref[...]))
    index = 0
    for piece in pieces:
        n = piece.shape[2]
        for inner in range(piece.shape[0]):
            at = place_ref[index]
            columns = pl.ds(pl.multiple_of((at % heads) * n, n), n)
            total_ref[:, columns] += dot(side_ref[at // heads], piece[inner])
            index += 1
    total = total_ref[...]
    normed, _ = normalize(total)
    residual_ref[...] = total.reshape(residual_ref.shape)
    low_ref[...] = (normed * gain_ref[...]).astype(BF16).reshape(low_ref.shape)


def branch(place, pieces, rows, tokens, gain):
    args = (*pieces, rows, tokens, gain)
    seqs, block, width = tokens.shape
    return pl.pallas_call(
        branch_kernel,
        in_specs=[SCALARS] + [whole(a) for a in args],
        out_shape=(
            jax.ShapeDtypeStruct(tokens.shape, F32),
            jax.ShapeDtypeStruct(tokens.shape, BF16),
        ),
        scratch_shapes=[
            pltpu.VMEM((2, seqs * block, pieces[0].shape[1]), BF16),
            pltpu.VMEM((seqs * block, width), F32),
        ],
        compiler_params=params(16),
        cost_estimate=COST,
        name="branch",
    )(place, *args)


def combine(*groups):
    parts = [part for group in groups for _, parts in group for part in parts]
    rows = sum(count for count, _ in groups[0])
    width = parts[0][0].shape[2]

    def kernel(*refs):
        at = 0
        for k, group in enumerate(groups):
            row = 0
            for count, terms in group:
                total = 0.0
                for _, _, start in terms:
                    total = total + wide(refs[at][0, start : start + count])
                    at += 1
                refs[-1][k, row : row + count] = total.astype(BF16)
                row += count

    return pl.pallas_call(
        kernel,
        grid=(1,),
        in_specs=[
            pl.BlockSpec((1, *array.shape[1:]), lambda *_, index=index: (index, 0, 0))
            for array, index, _ in parts
        ],
        out_specs=pl.BlockSpec((len(groups), rows, width), lambda *_: (0, 0, 0)),
        out_shape=jax.ShapeDtypeStruct((len(groups), rows, width), BF16),
        compiler_params=params(16),
        cost_estimate=COST,
        name="combine",
    )(*[array for array, _, _ in parts])


def mlp_kernel(*refs, count, ends):
    pieces, tops = refs[:count], refs[count : 2 * count]
    w_ref, out_w_ref = refs[2 * count : 2 * count + 2]
    low_ref, top_ref, mixed_ref, lifted_ref, *out_refs = refs[-4 - len(ends) :]
    step = pl.program_id(0)
    start = 0
    for piece, top in zip(pieces, tops):

        @pl.when((step >= start) & (step < start + piece.shape[0]))
        def _(piece=piece, top=top, start=start):
            low_ref[0] = piece[step - start]
            top_ref[0] = top[step - start]

        start += piece.shape[0]

    hidden = w_ref.shape[1] // 2
    lifted = dot(flat(low_ref[...]), w_ref[...])
    first, second = lifted[:, :hidden], lifted[:, hidden:]
    grad_mixed = dot(flat(top_ref[...]), out_w_ref[...], ((1,), (1,)))
    gate = 0.5 * (1.0 + lax.erf(first * (0.5**0.5)))
    slope = gate + first * jnp.exp(first * first * -0.5) * ((2.0 * math.pi) ** -0.5)
    activated = first * gate
    mixed_ref[...] = (activated * second).astype(BF16).reshape(mixed_ref.shape)
    grad = jnp.concatenate(
        [(grad_mixed * second * slope).astype(BF16), (grad_mixed * activated).astype(BF16)],
        axis=1,
    )
    lifted_ref[...] = grad.reshape(lifted_ref.shape)
    partial = dot(grad, w_ref[...], ((1,), (1,))).astype(BF16).reshape(low_ref.shape)
    start = 0
    for out, end in zip(out_refs, ends):

        @pl.when((step >= start) & (step < end))
        def _(out=out):
            out[...] = partial

        start = end


def mlp(pieces, tops, w, out_w, base, ends, earlier=()):
    seqs, block, width = pieces[0].shape[1:]
    hidden = w.shape[1] // 2
    whole_in = (*pieces, *tops, w, out_w)

    def rows(last):
        return pl.BlockSpec((1, seqs, block, last), lambda i: (i + base, 0, 0, 0))

    def within(start, end):
        return pl.BlockSpec(
            (1, seqs, block, width),
            lambda i: (jnp.clip(i - start, 0, end - start - 1), 0, 0, 0),
        )

    starts = (0, *ends[:-1])
    lasts = (width, width, hidden, 2 * hidden)
    return pl.pallas_call(
        functools.partial(mlp_kernel, count=len(pieces), ends=ends),
        grid=(ends[-1],),
        in_specs=[whole(array) for array in whole_in]
        + [pl.BlockSpec(memory_space=pl.ANY)] * len(earlier),
        out_specs=(
            *[rows(last) for last in lasts],
            *[within(start, end) for start, end in zip(starts, ends)],
        ),
        out_shape=(
            *[jax.ShapeDtypeStruct((8, seqs, block, last), BF16) for last in lasts],
            *[
                jax.ShapeDtypeStruct((end - start, seqs, block, width), BF16)
                for start, end in zip(starts, ends)
            ],
        ),
        input_output_aliases={len(whole_in) + at: at for at in range(len(earlier))},
        compiler_params=params(32),
        cost_estimate=COST,
        name="mlp",
    )(*whole_in, *earlier)


def out_grad_kernel(place_ref, rows_ref, grad_ref, keep_ref, send_ref):
    grads = flat(grad_ref[...])
    for index in range(8):
        part = dot(flat(rows_ref[place_ref[index]]), grads, ((0,), (0,))).astype(BF16)
        if index < 5:
            keep_ref[index] = part
        else:
            send_ref[index - 5] = part


def out_grad(place, rows, grads):
    part, width = rows.shape[-1], grads.shape[-1]
    return pl.pallas_call(
        out_grad_kernel,
        in_specs=[SCALARS, whole(rows), whole(grads)],
        out_shape=(
            jax.ShapeDtypeStruct((5, part, width), BF16),
            jax.ShapeDtypeStruct((3, part, width), BF16),
        ),
        compiler_params=params(16),
        cost_estimate=COST,
        name="out_grad",
    )(place, rows, grads)


def branch_back_kernel(place_ref, *refs):
    pieces = refs[:6]
    keep_ref, near_ref, own_ref, residual_ref, top_ref, gain_ref = refs[6:12]
    grad_ref, branch_ref, home_ref, sum_ref, low_ref, side_ref = refs[12:]
    grad_low = wide(flat(keep_ref[...])) + wide(flat(near_ref[...])) + wide(flat(own_ref[...]))
    normed, factor = normalize(flat(residual_ref[...]))
    sum_ref[...] = jnp.sum(grad_low * normed, axis=0, keepdims=True)
    grad = flat(wide(top_ref[...])) + norm_back(grad_low * gain_ref[...], normed, factor)
    grad_ref[...] = grad.reshape(grad_ref.shape)
    low_ref[...] = grad.astype(BF16)
    branch_ref[...] = low_ref[...].reshape(branch_ref.shape)
    heads = home_ref.shape[0] // 2
    side_ref[...] = jnp.zeros_like(side_ref)
    index = 0
    for piece in pieces:
        n = piece.shape[2]
        for inner in range(piece.shape[0]):
            at = place_ref[index]
            columns = pl.ds(pl.multiple_of((at % heads) * n, n), n)
            side_ref[at // heads] += dot(low_ref[:, columns], piece[inner], ((1,), (1,)))
            index += 1
    part = home_ref.shape[3]
    for c in range(2):
        for d in range(heads):
            home = side_ref[c, :, d * part : (d + 1) * part].astype(BF16)
            home_ref[c * heads + d] = home.reshape(home_ref.shape[1:])


def branch_back(place, pieces, keep, near, own, residual, top, gain):
    args = (*pieces, keep, near, own, residual, top, gain)
    seqs, block, width = residual.shape
    tall = pieces[0].shape[1]
    shapes = (
        jax.ShapeDtypeStruct(residual.shape, F32),
        jax.ShapeDtypeStruct(residual.shape, BF16),
        jax.ShapeDtypeStruct((8, seqs, block, tall // 4), BF16),
        jax.ShapeDtypeStruct((1, width), F32),
    )
    return pl.pallas_call(
        branch_back_kernel,
        grid=(1,),
        in_specs=[SCALARS]
        + [whole(piece) for piece in pieces]
        + [pl.BlockSpec((1, seqs * block, width), lambda *_: (0, 0, 0))] * 2
        + [whole(a) for a in args[8:]],
        out_specs=tuple(whole(shape) for shape in shapes),
        out_shape=shapes,
        scratch_shapes=[
            pltpu.VMEM((seqs * block, width), BF16),
            pltpu.VMEM((2, seqs * block, tall), F32),
        ],
        compiler_params=params(24),
        cost_estimate=COST,
        name="branch_back",
    )(place, *args)


def attend_back_kernel(
    place_ref, q_ref, k_ref, v_ref, grad_ref, att_ref, log_ref, cosq_ref, sinq_ref, cos_ref,
    sin_ref, w_ref, low_ref, *refs, seq, last,
):
    if last:
        before_ref, gain1_ref, gain2_ref, keep_ref, send_ref, grad_w_ref, *scratch = refs
    else:
        keep_ref, send_ref, before_ref, *scratch = refs
    proj_ref, sum_k, sum_v = scratch
    step = pl.program_id(0)
    block, part = q_ref.shape[2], q_ref.shape[3]

    @pl.when(step == 0)
    def _():
        sum_k[...] = jnp.zeros_like(sum_k)
        sum_v[...] = jnp.zeros_like(sum_v)

    queries, keys, values = flat(q_ref[...]), flat(k_ref[...]), flat(v_ref[...])
    grads = jnp.concatenate([grad_ref[place_ref[2 * step + inner], seq] for inner in range(2)])
    along = (grads.astype(F32) * flat(att_ref[...])).T
    logs = flat(log_ref[...]).T
    grad_queries = jnp.zeros(queries.shape, F32)
    for head, mask in enumerate(head_masks(queries.shape)):
        own_q = jnp.where(mask, queries, 0)
        own_g = jnp.where(mask, grads, 0)
        scores = dot(keys, own_q, ((1,), (1,)))
        weights = jnp.exp(scores - logs[head * HD : head * HD + 1])
        lifted = dot(values, own_g, ((1,), (1,)))
        row = jnp.sum(along[head * HD : (head + 1) * HD], axis=0, keepdims=True)
        grad_scores = (weights * (lifted - row)).astype(BF16)
        sum_k[...] += dot(grad_scores, own_q)
        sum_v[...] += dot(weights.astype(BF16), own_g)
        grad_queries = jnp.where(mask, dot(grad_scores, keys, ((0,), (0,))), grad_queries)
    grad_queries = lane_rotate(grad_queries * HD**-0.5, cosq_ref[...], -sinq_ref[...])
    rows = pl.multiple_of(step * 2 * block, 2 * block)
    proj_ref[pl.ds(rows, 2 * block), :part] = grad_queries.astype(BF16)

    @pl.when(step == 3)
    def _():
        grad_keys = lane_rotate(sum_k[...], cos_ref[...], -sin_ref[...])
        proj_ref[:, part : 2 * part] = grad_keys.astype(BF16)
        proj_ref[:, 2 * part :] = sum_v[...].astype(BF16)
        partial = dot(proj_ref[...], w_ref[...], ((1,), (1,))).astype(BF16)
        keep_ref[...] = partial[: 5 * block].reshape(5, block, -1)
        send_ref[...] = partial[5 * block :].reshape(3, block, -1)
        grad_w = dot(proj_ref[...], flat(low_ref[...]), ((0,), (0,)))
        if last:
            grad_w = (grad_w + before_ref[...]).T
            along_w = jnp.sum(grad_w * wide(w_ref[...]), axis=1, keepdims=True)
            along_w = jnp.broadcast_to(along_w, (w_ref.shape[0], 128)).T[:1] / gain1_ref[...]
            row = lax.broadcasted_iota(jnp.int32, (GAIN_ROWS, w_ref.shape[0]), 0)
            gains = jnp.where(row == 0, along_w, jnp.where(row == 1, gain2_ref[...], 0.0))
            n = grad_w_ref.shape[1] - GAIN_ROWS
            for at in range(grad_w_ref.shape[0]):
                part_rows = slice(at * n, (at + 1) * n)
                grad_w_ref[at, :n] = grad_w[part_rows].astype(BF16)
                grad_w_ref[at, n:, :n] = gains[:, part_rows].astype(BF16)
                rest = grad_w_ref.shape[2] - n
                grad_w_ref[at, n:, n:] = jnp.zeros((GAIN_ROWS, rest), BF16)
        else:
            before_ref[...] = grad_w


GAIN_ROWS = 16


def attend_back(place, qkv, grads, attended, logs, cosine, sine, w, low, seq, *before, dp=1):
    _, _, block, own = qkv.shape
    part, width = own // 3, w.shape[0]
    last = len(before) > 0
    rows = pl.BlockSpec((2, 1, block, part), lambda i: (i, 0, 0, 0))
    angles = pl.BlockSpec((2 * block, part), lambda i: (i, 0))

    def full(*shape):
        return pl.BlockSpec(shape, lambda i: (0,) * len(shape))

    args = [place, qkv, qkv, qkv, grads, attended, logs, cosine, sine, cosine, sine, w, low]
    in_specs = [
        SCALARS,
        pl.BlockSpec((2, 1, block, part), lambda i: (i, seq, 0, 0)),
        pl.BlockSpec((8, 1, block, part), lambda i: (0, seq, 0, 1)),
        pl.BlockSpec((8, 1, block, part), lambda i: (0, seq, 0, 2)),
        whole(grads),
        rows,
        rows,
        angles,
        angles,
        whole(cosine),
        whole(sine),
        whole(w),
        pl.BlockSpec((8, 1, block, width), lambda i: (0, seq, 0, 0)),
    ]
    shapes = [((5, block, width), BF16), ((3, block, width), BF16)]
    if last:
        args += before
        in_specs += [whole(array) for array in before]
        shapes += [((dp, width // dp + GAIN_ROWS, own), BF16)]
    else:
        shapes += [((own, width), F32)]
    return pl.pallas_call(
        functools.partial(attend_back_kernel, seq=seq, last=last),
        grid=(4,),
        in_specs=in_specs,
        out_specs=tuple(full(*shape) for shape, _ in shapes),
        out_shape=tuple(jax.ShapeDtypeStruct(shape, kind) for shape, kind in shapes),
        scratch_shapes=[
            pltpu.VMEM((8 * block, own), BF16),
            pltpu.VMEM((8 * block, part), F32),
            pltpu.VMEM((8 * block, part), F32),
        ],
        compiler_params=params(60),
        cost_estimate=COST,
        name="attend_back",
    )(*args)


def input_grad_kernel(*refs):
    keeps, (near_ref, own_ref, tokens_ref, residual_ref, gain_ref, out_ref) = refs[:-6], refs[-6:]
    block = tokens_ref.shape[1]
    for seq, keep in enumerate(keeps):
        rows = slice(seq * block, (seq + 1) * block)
        grad = wide(keep[0, :block]) + wide(near_ref[0, rows]) + wide(own_ref[0, rows])
        normed, factor = normalize(wide(tokens_ref[seq]))
        out_ref[seq] = residual_ref[seq] + norm_back(grad * gain_ref[...], normed, factor)


def input_grad(keeps, near, own, tokens, residual, gain):
    rest = (own, tokens, residual, gain)
    return pl.pallas_call(
        input_grad_kernel,
        grid=(1,),
        in_specs=[
            pl.BlockSpec((1, *array.shape[1:]), lambda *_: (0, 0, 0)) for array in (*keeps, near)
        ]
        + [whole(array) for array in rest],
        out_specs=whole(residual),
        out_shape=jax.ShapeDtypeStruct(residual.shape, F32),
        compiler_params=params(16),
        cost_estimate=COST,
        name="input_grad",
    )(*keeps, near, *rest)


def finish_kernel(keep_ref, rows_ref, near_ref, home_ref, residual_ref, out_ref, grad_ref):
    rows = keep_ref.shape[1]
    total = wide(keep_ref[0]) + wide(near_ref[0, :rows]) + wide(home_ref[0, :rows])
    out_ref[...] = (residual_ref[...] + total.reshape(residual_ref.shape)).astype(BF16)
    total = wide(rows_ref[0]) + wide(near_ref[0, rows:]) + wide(home_ref[0, rows:])
    n = grad_ref.shape[2]
    for at in range(grad_ref.shape[0]):
        grad_ref[at] = total[:, at * n : (at + 1) * n].astype(BF16)


def finish(keep, rows, near, home, residual, dp):
    args = (keep, rows, near, home)
    shapes = (
        jax.ShapeDtypeStruct(residual.shape, BF16),
        jax.ShapeDtypeStruct((dp, rows.shape[1], rows.shape[2] // dp), BF16),
    )
    return pl.pallas_call(
        finish_kernel,
        grid=(1,),
        in_specs=[pl.BlockSpec((1, *array.shape[1:]), lambda *_: (0, 0, 0)) for array in args]
        + [whole(residual)],
        out_specs=tuple(whole(shape) for shape in shapes),
        out_shape=shapes,
        compiler_params=params(16),
        cost_estimate=COST,
        name="finish",
    )(*args, residual)


class Group:
    def __init__(self):
        self.heads = lax.axis_size("head")
        self.dp = lax.axis_size("dp")
        self.ctx_at = lax.axis_index("ctx")
        self.head_at = lax.axis_index("head")
        self.dp_at = lax.axis_index("dp")
        self.at = self.ctx_at * self.heads + self.head_at
        near, far = [], []
        for c in range(2):
            for h in range(self.heads):
                x, y = (c ^ 1) * self.heads + h, c * self.heads + (h ^ 2)
                near.append((c * self.heads + h, x if h % 2 == 0 else y))
                far.append((c * self.heads + h, y if h % 2 == 0 else x))
        self.near, self.far = near, far

    def order(self):
        first = jnp.where(self.head_at % 2 == 0, 4, 2)
        second = 6 - first
        return jnp.stack(
            [self.at ^ bits for bits in (0, 1, first, first ^ 1, 6, second ^ 1, second, 7)]
        )

    def swap(self, values, bit):
        if bit == 4:
            return lax.ppermute(values, "ctx", [(0, 1), (1, 0)])
        return lax.ppermute(values, "head", [(i, i ^ bit) for i in range(self.heads)])

    def mate(self, values):
        return self.swap(values, 1)

    def to_near(self, values):
        return lax.ppermute(values, GROUP, self.near)

    def to_far(self, values):
        return lax.ppermute(values, GROUP, self.far)

    def rows_back(self, values, place):
        pairs, same = [], False
        for d in range(self.dp):
            for h in range(self.heads):
                if (d, h) == (place[h], d):
                    same = same | ((self.dp_at == d) & (self.head_at == h))
                else:
                    pairs.append((d * self.heads + h, place[h] * self.heads + d))
        return jnp.where(same, values, lax.ppermute(values, ("dp", "head"), pairs))

    def across(self, values, step):
        return lax.ppermute(values, "dp", [(i, i ^ step) for i in range(self.dp)])


def pick(array, index, axis):
    return lax.dynamic_index_in_dim(array, index, axis, keepdims=False)


def after(values, *earlier):
    return lax.optimization_barrier((values, earlier))[0]


def local_split(tokens, cotangent, w_qkv, w_attn_out, w_in, w_mlp_out, norm_gain1, norm_gain2):
    seqs, block, width = tokens.shape
    group = Group()
    heads, dp = group.heads, group.dp
    at_c, at_h = group.ctx_at, group.head_at
    parts = 2 * heads
    hidden = w_in.shape[1] // 2 // parts
    padded = -(-hidden // 128) * 128
    own_width = width // parts
    half = heads // 2
    rows_here = w_qkv.shape[0]
    place = [2 * (h % half) + h // half for h in range(heads)]
    straight = list(range(heads))
    order = group.order()
    scalars = jnp.concatenate([order, jnp.stack([group.dp_at, at_c])]).astype(jnp.int32)
    mate, near, far = group.mate, group.to_near, group.to_far

    def in_order(own, other):
        return jnp.where(at_c == 0, jnp.stack([own, other]), jnp.stack([other, own]))

    def exchange(values):
        return lax.all_to_all(values, GROUP, split_axis=0, concat_axis=0, tiled=True)


    gains = jnp.pad(
        jnp.stack([norm_gain1, norm_gain2]), ((0, 14), (0, 3 * own_width - rows_here))
    )
    qkv_view = w_qkv.reshape(rows_here, 3, width)

    def qkv_part(at):
        start = (2 * at_h + at) * own_width
        cut = lax.dynamic_slice_in_dim(qkv_view, start, own_width, 2)
        return jnp.concatenate([cut.reshape(rows_here, 3 * own_width), gains])

    x_own = tokens[None]
    x_mate = mate(x_own)
    qkv_other, qkv_own = qkv_part(1 - at_c), qkv_part(at_c)
    qkv_cross = group.swap(after(qkv_other, x_own), 4)
    in_view = after(w_in, qkv_other).reshape(rows_here, 2, heads, 2, hidden)
    in_view = pick(in_view, 2 * (at_h % half) + at_h // half, 2)

    def in_part(at):
        cut = pick(in_view, at, 2)
        return jnp.pad(cut, ((0, 0), (0, 0), (0, padded - hidden))).reshape(rows_here, 2 * padded)

    in_other, in_own = in_part(1 - at_c), in_part(at_c)
    in_cross = group.swap(after(in_other, qkv_cross), 4)
    x_chip = jnp.concatenate([x_own, after(x_mate, qkv_cross, qkv_own, in_cross, in_own)])
    x_near = near(x_chip)
    qkv_pair = jnp.stack([qkv_own, qkv_cross])
    qkv_pieces = [qkv_pair] + [group.across(qkv_pair, step) for step in range(1, dp)]

    slices = jnp.concatenate([w_attn_out, w_mlp_out])
    slices = after(slices, x_near, *qkv_pieces)
    slices = lax.dynamic_slice_in_dim(slices, at_h * (width // heads), width // heads, 1)
    slices = jnp.pad(slices, ((0, 64), (0, 0)))
    slices = lax.all_gather(slices, "dp", axis=0)
    positions = after(order, qkv_pair)[:, None] * block + jnp.arange(block, dtype=jnp.int32)
    lane = jnp.arange(own_width, dtype=jnp.int32)
    frequency = jnp.exp(
        (lane % (HD // 2)).astype(F32) * (-math.log(ROPE_BASE) / (HD // 2))
    )
    angles = wide(positions.reshape(-1))[:, None] * frequency[None, :]
    cosine = jnp.cos(angles)
    sine = jnp.sin(angles) * jnp.where(lane % HD < HD // 2, -1.0, 1.0)[None, :]

    x_far = far(x_near[:1])
    x_near = after(x_near, *qkv_pieces, cosine, sine)
    x_near_mate = mate(x_near)
    cot_own = after(cotangent, x_near)[None]
    cot_mate = mate(cot_own)
    in_pair, x_far = lax.optimization_barrier((in_order(in_own, in_cross), x_far))
    weight_in = lax.all_gather(in_pair, "dp", axis=0).reshape(width, -1)
    cot_chip = jnp.concatenate([cot_own, cot_mate])
    x_far = after(x_far, cot_chip)
    x_far_mate = mate(x_far)

    cot_near = near(after(cot_chip, x_far))
    out_rows = w_attn_out.shape[0]
    x_pieces = (x_own, x_mate, x_near, x_far, x_near_mate, x_far_mate)
    low1, qkv, weight_qkv, gain_one, gain_two = project(
        scalars, x_pieces, qkv_pieces, cosine, sine
    )

    slices = after(slices, qkv)
    out_own = slices[:, :out_rows].reshape(1, dp * out_rows, -1)
    out_mate = mate(out_own)
    mlp_slices = jnp.stack(
        [slices[place[h], out_rows : out_rows + hidden] for h in range(heads)]
    )
    mlp_slices = lax.all_to_all(mlp_slices, "head", split_axis=0, concat_axis=0, tiled=True)
    out_near = near(jnp.concatenate([out_own, out_mate]))
    att_0, log_0, home_0 = attend(scalars, after(qkv, out_mate))
    cot_near = after(cot_near, home_0)
    cot_far, cot_near_mate = far(cot_near[:1]), mate(cot_near)
    out_near = after(out_near, home_0)
    out_far, out_near_mate = far(out_near[:1]), mate(out_near)
    att_1, log_1, home = attend(scalars, after(qkv, cot_near, out_near), home_0)
    home, cot_far, out_far = lax.optimization_barrier((home, cot_far, out_far))
    att_rows = exchange(home)
    out_far_mate, cot_far_mate = mate(after(out_far, home)), mate(after(cot_far, home))
    out_pieces = (out_own, out_mate, out_near, out_far, out_near_mate, out_far_mate)
    weight_mlp = jnp.moveaxis(after(mlp_slices, home), 0, 1).reshape(hidden, width)
    weight_mlp = jnp.pad(weight_mlp, ((0, padded - hidden), (0, 0)))
    residual, low2 = branch(
        scalars, out_pieces, after(att_rows, cot_far_mate, weight_mlp, weight_in), tokens, gain_two
    )

    low_own = low2[None]
    low_mate = mate(low_own)
    low_near = near(jnp.concatenate([low_own, low_mate]))
    *arrays, keep_a = mlp(
        (low_own, low_mate), (cot_own, cot_mate), weight_in, weight_mlp, 0, (2,)
    )
    low_near = after(low_near, keep_a)
    low_far, low_near_mate = far(low_near[:1]), mate(low_near)
    *arrays, keep_b = mlp((low_near,), (cot_near,), weight_in, weight_mlp, 2, (2,), arrays)
    low_far_mate = mate(after(low_far, keep_b))
    low2_all, cot_all, mixed, grad_lifted, keep_c, send = mlp(
        (low_far, low_near_mate, low_far_mate),
        (cot_far, cot_near_mate, cot_far_mate),
        weight_in,
        weight_mlp,
        4,
        (1, 4),
        arrays,
    )

    def over_tokens(left, right):
        return dot(flat(left), flat(right), ((0,), (0,)))

    def scatter(values):
        return lax.psum_scatter(values.astype(BF16), "dp", scatter_dimension=0, tiled=True)

    def columns_first(values):
        return jnp.moveaxis(values.reshape(values.shape[0], dp, -1), 1, 0)

    rows = seqs * block

    def by_rows(values):
        return values.reshape(values.shape[0], -1, width)

    keep_a, keep_b, keep_c, send = (by_rows(array) for array in (keep_a, keep_b, keep_c, send))
    met = mate(send)
    last = combine([(rows, [(keep_c, 0, 0), (met, 2, 0)])])
    last_far = far(last)
    grad_mlp = columns_first(over_tokens(after(mixed, last), cot_all)[:hidden]).astype(BF16)
    last_far = after(last_far, grad_mlp)
    grad_mlp = scatter(grad_mlp)[0]
    chip = combine(
        [(rows, [(keep_b, 0, 0), (met, 0, 0), (last_far, 0, 0)])],
        [(rows, [(keep_b, 1, 0), (met, 1, 0)])],
    )
    chip_near = near(chip)
    grad_in = over_tokens(low2_all, after(grad_lifted, chip)).astype(BF16)
    cut = 5 * rows
    mixed_flat = flat(after(mixed, chip))
    out_keep = dot(mixed_flat[:cut], weight_mlp).astype(BF16).reshape(5, rows, width)
    out_send = dot(mixed_flat[cut:], weight_mlp).astype(BF16).reshape(3, rows, width)
    chip_near = after(chip_near, grad_in, out_keep, out_send)
    grad_in = scatter(grad_in)
    home = mate(combine([(rows, [(keep_a, 1, 0), (chip_near, 1, 0)])])[0])
    out_met = mate(after(out_send, chip_near))
    grad_residual, grad_branch, home, gain2_sum = branch_back(
        scalars, out_pieces, keep_a, chip_near, home, residual, cotangent, gain_two
    )
    grad_home = exchange(home)

    rows_keep, rows_send = out_grad(scalars, after(att_rows, home), grad_branch)
    rows_met = mate(rows_send)
    few = rows_keep.shape[1]

    def ends(index, at, *more):
        kept = [(out_keep, index, 0)], [(rows_keep, index, 0)]
        if at is not None:
            kept[0].append((out_met, at, 0))
            kept[1].append((rows_met, at, 0))
        for array, where in more:
            kept[0].append((array, where, 0))
            kept[1].append((array, where, rows))
        return [(rows, kept[0]), (few, kept[1])]

    end_last = combine(ends(4, 2))
    grad_home = after(grad_home, end_last, grad_mlp)
    end_far = far(after(end_last, grad_home))
    grad_mlp = group.rows_back(after(grad_mlp, grad_home), place)
    keep_0, send_0, before = attend_back(
        scalars, qkv, grad_home, att_0, log_0, cosine, sine, weight_qkv, low1, 0
    )
    met_0 = mate(send_0)
    end_far, grad_in = lax.optimization_barrier((after(end_far, send_0), grad_in))
    in_parts = grad_in.reshape(2, rows_here, -1)
    in_cross = group.swap(pick(in_parts, 1 - at_c, 0), 4)
    end_chip = combine(ends(2, 0, (end_far, 0)), ends(3, 1))
    end_near = near(after(end_chip, in_cross))
    keep_1, send_1, grad_qkv = attend_back(
        scalars, qkv, after(grad_home, end_chip), att_1, log_1, cosine, sine,
        weight_qkv, low1, 1, before, gain_one, gain2_sum, dp=dp,
    )

    grad_qkv = scatter(grad_qkv.reshape(-1, grad_qkv.shape[2]))
    met_1 = mate(send_1)
    end_home = combine(ends(1, None, (after(end_near, send_1), 1)))
    met_1, end_home = lax.optimization_barrier((after(met_1, grad_mlp), end_home))
    end_home = mate(end_home)

    def both(index, at, *more):
        kept = [(keep_0, index, 0)], [(keep_1, index, 0)]
        if at is not None:
            kept[0].append((met_0, at, 0))
            kept[1].append((met_1, at, 0))
        for array, where in more:
            kept[0].append((array, where, 0))
            kept[1].append((array, where, block))
        return [(block, kept[0]), (block, kept[1])]

    last = combine(both(4, 2))
    last_far = far(last)
    result, grad_out = finish(
        out_keep, rows_keep, end_near, after(end_home, last), residual, dp
    )
    last_far, grad_out = lax.optimization_barrier((last_far, grad_out))
    grad_out = scatter(grad_out)[0]
    chip = combine(both(2, 0, (last_far, 0)), both(3, 1))
    chip_near = near(chip)

    grad_in = in_order(after(pick(in_parts, at_c, 0), chip), in_cross)
    late = at_h // half
    grad_in = jnp.stack([grad_in[..., :hidden], grad_in[..., padded : padded + hidden]])
    stays = pick(grad_in, late, 0)
    comes = group.swap(pick(grad_in, 1 - late, 0), half)
    grad_qkv = after(grad_qkv, chip)
    both_rows = 2 * rows_here
    qkv_parts = grad_qkv[:both_rows].reshape(2, rows_here, -1)
    gains = grad_qkv[both_rows:]
    cross = jnp.concatenate([pick(qkv_parts, 1 - at_c, 0), gains])
    cross = group.swap(cross, 4)
    chip_near = after(chip_near, comes, cross)
    home = combine(both(1, None, (chip_near, 1)))
    cross = after(cross, home)
    home = mate(home)
    grad_qkv = in_order(pick(qkv_parts, at_c, 0), cross[:rows_here])
    gains = (wide(gains) + wide(cross[rows_here:])).astype(BF16)
    gains = wide(gains) + sum(wide(group.swap(gains, bit)) for bit in range(1, heads))
    grad_input = input_grad((keep_0, keep_1), chip_near, home, tokens, grad_residual, gain_one)
    grad_out, grad_input = lax.optimization_barrier((grad_out, grad_input))
    grad_out = wide(group.rows_back(grad_out, straight))

    grad_mlp = wide(grad_mlp)
    grad_in = jnp.where(
        late == 0, jnp.concatenate([stays, comes]), jnp.concatenate([comes, stays])
    )
    grad_in = wide(jnp.moveaxis(grad_in, 0, 1).reshape(rows_here, -1))

    per_device = width // (dp * parts)
    start = group.at * per_device
    grad_gain1, grad_gain2 = (
        lax.dynamic_slice_in_dim(gains[i], start, per_device, 0) for i in range(2)
    )
    grad_qkv = grad_qkv.reshape(2, rows_here, 3, own_width)
    grad_qkv = jnp.moveaxis(grad_qkv, 2, 0)
    odd = at_h % 2
    stays = pick(grad_qkv, odd + late, 0)
    core = group.swap(pick(grad_qkv, 1 - odd + late, 0), 1)
    chip = group.swap(pick(grad_qkv, 2 - 2 * late, 0), 2)
    grad_qkv = jnp.where(
        odd == 0, jnp.concatenate([stays, core, chip]), jnp.concatenate([chip, core, stays])
    )
    grad_qkv = wide(jnp.moveaxis(grad_qkv, 0, 1).reshape(rows_here, -1))

    return (
        result,
        grad_input,
        grad_qkv,
        grad_out,
        grad_in,
        grad_mlp,
        grad_gain1,
        grad_gain2,
    )


def local(tokens, cotangent, w_qkv, w_attn_out, w_in, w_mlp_out, norm_gain1, norm_gain2):
    args = (tokens, cotangent, w_qkv, w_attn_out, w_in, w_mlp_out, norm_gain1, norm_gain2)
    sizes = [lax.axis_size(axis) for axis in ("dp", "ctx", "head")]
    if sizes == [4, 2, 4] and tokens.shape[2] == 8 * 2 * HD and tokens.shape[1] % 16 == 0:
        return local_split(*args)
    return local_general(*args)


def solution(mesh):
    in_specs = (
        P("dp", ("ctx", "head"), None),
        P("dp", ("ctx", "head"), None),
        P(("dp", "ctx"), None),
        P(("dp", "ctx"), None),
        P(("dp", "ctx"), None),
        P(("dp", "ctx"), None),
        P(("dp", "ctx")),
        P(("dp", "ctx")),
    )
    out_specs = (
        P("dp", ("ctx", "head"), None),
        P("dp", ("ctx", "head"), None),
        P(("dp", "ctx"), "head"),
        P(("dp", "ctx"), "head"),
        P(("dp", "ctx"), "head"),
        P(("dp", "ctx"), "head"),
        P(("dp", "ctx", "head")),
        P(("dp", "ctx", "head")),
    )
    return jax.shard_map(local, mesh=mesh, in_specs=in_specs, out_specs=out_specs, check_vma=False)
```

```python
import functools
import math

import jax
import jax.numpy as jnp
from jax import lax
from jax.experimental import pallas as pl
from jax.experimental.pallas import tpu as pltpu
from jax.sharding import PartitionSpec as P

HD = 64


EPSILON = 1e-05
ROPE_BASE = 160000.0


def normalize(values):
    centre = jnp.mean(values, axis=-1, keepdims=True)
    shifted = values - centre
    spread = jnp.mean(shifted * shifted, axis=-1, keepdims=True)
    factor = lax.rsqrt(spread + EPSILON)
    return (shifted * factor, factor)


def norm_back(grad_normed, normed, factor):
    grad_centre = jnp.mean(grad_normed, axis=-1, keepdims=True)
    grad_along = jnp.mean(grad_normed * normed, axis=-1, keepdims=True)
    return (grad_normed - grad_centre - normed * grad_along) * factor


def rope_tables(positions, half_size):
    frequency = jnp.exp(
        jnp.arange(half_size, dtype=jnp.float32) * (-math.log(ROPE_BASE) / half_size)
    )
    angles = positions[:, None] * frequency[None, :]
    return (jnp.cos(angles), jnp.sin(angles))


def rotate(values, cosine, sine_table, direction):
    half_size = cosine.shape[-1]
    first_half = values[..., :half_size]
    second_half = values[..., half_size:]
    cos_part = cosine[:, None, :]
    sin_part = sine_table[:, None, :] * direction
    return jnp.concatenate(
        [
            first_half * cos_part - second_half * sin_part,
            second_half * cos_part + first_half * sin_part,
        ],
        axis=-1,
    )


def block_scores(queries4, keys_block, scale):
    keys4 = keys_block.reshape(
        keys_block.shape[0], keys_block.shape[1], queries4.shape[2], queries4.shape[3]
    )
    return (
        jnp.einsum("sqgd,skgd->sgqk", queries4, keys4, preferred_element_type=jnp.float32) * scale
    )


def attend_forward(queries4, keys_all, values_all, key_rows, scale):
    seqs_here, query_rows, groups, head_size = queries4.shape
    turns = keys_all.shape[1] // key_rows

    def statistics(turn, carry):
        row_peak, row_total = carry
        keys_block = lax.dynamic_slice_in_dim(keys_all, turn * key_rows, key_rows, 1)
        scores = block_scores(queries4, keys_block, scale)
        new_peak = jnp.maximum(row_peak, jnp.max(scores, axis=-1))
        row_total = row_total * jnp.exp(row_peak - new_peak) + jnp.sum(
            jnp.exp(scores - new_peak[..., None]), axis=-1
        )
        return (new_peak, row_total)

    start_peak = jnp.full((seqs_here, groups, query_rows), -1e30, jnp.float32)
    row_peak, row_total = lax.fori_loop(
        0, turns, statistics, (start_peak, jnp.zeros_like(start_peak))
    )
    log_total = row_peak + jnp.log(row_total)

    def accumulate(turn, running):
        keys_block = lax.dynamic_slice_in_dim(keys_all, turn * key_rows, key_rows, 1)
        values_block = lax.dynamic_slice_in_dim(values_all, turn * key_rows, key_rows, 1).reshape(
            seqs_here, key_rows, groups, head_size
        )
        weights = jnp.exp(block_scores(queries4, keys_block, scale) - log_total[..., None]).astype(
            jnp.bfloat16
        )
        return running + jnp.einsum(
            "sgqk,skgd->sqgd", weights, values_block, preferred_element_type=jnp.float32
        )

    attended = lax.fori_loop(
        0, turns, accumulate, jnp.zeros((seqs_here, query_rows, groups, head_size), jnp.float32)
    )
    return (attended, log_total)


def attend_backward(queries4, keys_all, values_all, grad_out4, log_total, along, key_rows, scale):
    seqs_here, query_rows, groups, head_size = queries4.shape
    length = keys_all.shape[1]
    width_group = groups * head_size
    turns = length // key_rows

    def step_back(turn, carry):
        grad_queries, grad_keys, grad_values = carry
        keys_block = lax.dynamic_slice_in_dim(keys_all, turn * key_rows, key_rows, 1)
        keys4 = keys_block.reshape(seqs_here, key_rows, groups, head_size)
        values4 = lax.dynamic_slice_in_dim(values_all, turn * key_rows, key_rows, 1).reshape(
            seqs_here, key_rows, groups, head_size
        )
        weights = jnp.exp(block_scores(queries4, keys_block, scale) - log_total[..., None])
        grad_weights = jnp.einsum(
            "sqgd,skgd->sgqk", grad_out4, values4, preferred_element_type=jnp.float32
        )
        grad_scores = (weights * (grad_weights - along[..., None])).astype(jnp.bfloat16)
        grad_queries = grad_queries + jnp.einsum(
            "sgqk,skgd->sqgd", grad_scores, keys4, preferred_element_type=jnp.float32
        )
        key_part = (
            jnp.einsum("sgqk,sqgd->skgd", grad_scores, queries4, preferred_element_type=jnp.float32)
            * scale
        )
        value_part = jnp.einsum(
            "sgqk,sqgd->skgd",
            weights.astype(jnp.bfloat16),
            grad_out4,
            preferred_element_type=jnp.float32,
        )
        grad_keys = lax.dynamic_update_slice_in_dim(
            grad_keys, key_part.reshape(seqs_here, key_rows, width_group), turn * key_rows, 1
        )
        grad_values = lax.dynamic_update_slice_in_dim(
            grad_values, value_part.reshape(seqs_here, key_rows, width_group), turn * key_rows, 1
        )
        return (grad_queries, grad_keys, grad_values)

    start = (
        jnp.zeros((seqs_here, query_rows, groups, head_size), jnp.float32),
        jnp.zeros((seqs_here, length, width_group), jnp.float32),
        jnp.zeros((seqs_here, length, width_group), jnp.float32),
    )
    grad_queries, grad_keys, grad_values = lax.fori_loop(0, turns, step_back, start)
    return (grad_queries * scale, grad_keys, grad_values)


def local_general(tokens, cotangent, w_qkv, w_attn_out, w_in, w_mlp_out, norm_gain1, norm_gain2):
    seqs_here, block_rows, width = tokens.shape
    count_rows = seqs_here * block_rows
    heads_all = width // HD
    head_devices = lax.axis_size("head")
    group_devices = lax.axis_size(("dp", "ctx"))
    groups = heads_all // head_devices
    width_group = groups * HD
    scale = HD ** (-0.5)
    ff_width = w_in.shape[1] // 2
    full_qkv, full_out, full_in, full_mlp, gain_one, gain_two = (
        lax.all_gather(w_qkv, ("dp", "ctx"), axis=0, tiled=True),
        lax.all_gather(w_attn_out, ("dp", "ctx"), axis=0, tiled=True),
        lax.all_gather(w_in, ("dp", "ctx"), axis=0, tiled=True),
        lax.all_gather(w_mlp_out, ("dp", "ctx"), axis=0, tiled=True),
        lax.all_gather(norm_gain1, ("dp", "ctx"), axis=0, tiled=True),
        lax.all_gather(norm_gain2, ("dp", "ctx"), axis=0, tiled=True),
    )
    x_in = tokens.astype(jnp.float32).reshape(count_rows, width)
    normed1, factor1 = normalize(x_in)
    lowered1 = (normed1 * gain_one.astype(jnp.float32)).astype(jnp.bfloat16)
    projected = jnp.dot(lowered1, full_qkv, preferred_element_type=jnp.float32).reshape(
        seqs_here, block_rows, 3, heads_all, HD
    )
    first_pos = (lax.axis_index("ctx") * head_devices + lax.axis_index("head")) * block_rows
    positions = (first_pos + jnp.arange(block_rows, dtype=jnp.int32)).astype(jnp.float32)
    cosine, sine_table = rope_tables(positions, HD // 2)
    queries = (
        rotate(projected[:, :, 0], cosine, sine_table, 1.0)
        .astype(jnp.bfloat16)
        .reshape(seqs_here, block_rows, width)
    )
    keys_local = (
        rotate(projected[:, :, 1], cosine, sine_table, 1.0)
        .astype(jnp.bfloat16)
        .reshape(seqs_here, block_rows, width)
    )
    values_local = projected[:, :, 2].astype(jnp.bfloat16).reshape(seqs_here, block_rows, width)
    queries_h, keys_h, values_h = (
        lax.all_to_all(queries, "head", split_axis=2, concat_axis=1, tiled=True),
        lax.all_to_all(keys_local, "head", split_axis=2, concat_axis=1, tiled=True),
        lax.all_to_all(values_local, "head", split_axis=2, concat_axis=1, tiled=True),
    )
    query_rows = queries_h.shape[1]
    queries4 = queries_h.reshape(seqs_here, query_rows, groups, HD)
    keys_all, values_all = (
        lax.all_gather(keys_h, "ctx", axis=1, tiled=True),
        lax.all_gather(values_h, "ctx", axis=1, tiled=True),
    )
    key_rows = math.gcd(keys_all.shape[1], 1024)
    attended, log_total = attend_forward(queries4, keys_all, values_all, key_rows, scale)
    attended_low = attended.astype(jnp.bfloat16).reshape(seqs_here, query_rows, width_group)
    back_rows = lax.all_to_all(
        attended_low, "head", split_axis=1, concat_axis=2, tiled=True
    ).reshape(count_rows, width)
    residual = x_in + jnp.dot(back_rows, full_out, preferred_element_type=jnp.float32)
    normed2, factor2 = normalize(residual)
    lowered2 = (normed2 * gain_two.astype(jnp.float32)).astype(jnp.bfloat16)
    lifted = jnp.dot(lowered2, full_in, preferred_element_type=jnp.float32)
    first_part = lifted[:, :ff_width]
    second_part = lifted[:, ff_width:]
    activated, gelu_pullback = jax.vjp(
        lambda entries: jax.nn.gelu(entries, approximate=False), first_part
    )
    mixed = (activated * second_part).astype(jnp.bfloat16)
    result = (residual + jnp.dot(mixed, full_mlp, preferred_element_type=jnp.float32)).astype(
        jnp.bfloat16
    )
    full_qkv, full_out, full_in, full_mlp, gain_one, gain_two = (
        lax.all_gather(w_qkv, ("dp", "ctx"), axis=0, tiled=True),
        lax.all_gather(w_attn_out, ("dp", "ctx"), axis=0, tiled=True),
        lax.all_gather(w_in, ("dp", "ctx"), axis=0, tiled=True),
        lax.all_gather(w_mlp_out, ("dp", "ctx"), axis=0, tiled=True),
        lax.all_gather(norm_gain1, ("dp", "ctx"), axis=0, tiled=True),
        lax.all_gather(norm_gain2, ("dp", "ctx"), axis=0, tiled=True),
    )
    keys_all, values_all = (
        lax.all_gather(keys_h, "ctx", axis=1, tiled=True),
        lax.all_gather(values_h, "ctx", axis=1, tiled=True),
    )
    grad_top = cotangent.reshape(count_rows, width)
    grad_mlp = jnp.einsum("nf,nd->fd", mixed, grad_top, preferred_element_type=jnp.float32)
    grad_mixed = jnp.einsum("nd,fd->nf", grad_top, full_mlp, preferred_element_type=jnp.float32)
    grad_first = gelu_pullback(grad_mixed * second_part)[0]
    grad_lifted = jnp.concatenate([grad_first, grad_mixed * activated], axis=-1).astype(
        jnp.bfloat16
    )
    grad_inner = jnp.einsum("nd,nf->df", lowered2, grad_lifted, preferred_element_type=jnp.float32)
    grad_lowered2 = jnp.einsum(
        "nf,df->nd", grad_lifted, full_in, preferred_element_type=jnp.float32
    )
    grad_two = jnp.sum(grad_lowered2 * normed2, axis=0)
    grad_residual = grad_top.astype(jnp.float32) + norm_back(
        grad_lowered2 * gain_two.astype(jnp.float32), normed2, factor2
    )
    grad_branch = grad_residual.astype(jnp.bfloat16)
    grad_outproj = jnp.einsum(
        "nd,ne->de", back_rows, grad_branch, preferred_element_type=jnp.float32
    )
    grad_attended = jnp.einsum(
        "ne,de->nd", grad_branch, full_out, preferred_element_type=jnp.float32
    ).astype(jnp.bfloat16)
    grad_attended_h = lax.all_to_all(
        grad_attended.reshape(seqs_here, block_rows, width),
        "head",
        split_axis=2,
        concat_axis=1,
        tiled=True,
    )
    grad_out4 = grad_attended_h.reshape(seqs_here, query_rows, groups, HD)
    along = jnp.transpose(jnp.sum(grad_out4.astype(jnp.float32) * attended, axis=-1), (0, 2, 1))
    grad_queries, grad_keys_all, grad_values_all = attend_backward(
        queries4, keys_all, values_all, grad_out4, log_total, along, key_rows, scale
    )
    grad_keys_sum, grad_values_sum = (
        lax.psum_scatter(
            grad_keys_all.astype(jnp.bfloat16), "ctx", scatter_dimension=1, tiled=True
        ).astype(jnp.float32),
        lax.psum_scatter(
            grad_values_all.astype(jnp.bfloat16), "ctx", scatter_dimension=1, tiled=True
        ).astype(jnp.float32),
    )
    grad_q_low = grad_queries.astype(jnp.bfloat16).reshape(seqs_here, query_rows, width_group)
    grad_q_tok, grad_k_tok, grad_v_tok = (
        lax.all_to_all(grad_q_low, "head", split_axis=1, concat_axis=2, tiled=True),
        lax.all_to_all(
            grad_keys_sum.astype(jnp.bfloat16), "head", split_axis=1, concat_axis=2, tiled=True
        ),
        lax.all_to_all(
            grad_values_sum.astype(jnp.bfloat16), "head", split_axis=1, concat_axis=2, tiled=True
        ),
    )
    unrot_q = rotate(
        grad_q_tok.astype(jnp.float32).reshape(seqs_here, block_rows, heads_all, HD),
        cosine,
        sine_table,
        -1.0,
    )
    unrot_k = rotate(
        grad_k_tok.astype(jnp.float32).reshape(seqs_here, block_rows, heads_all, HD),
        cosine,
        sine_table,
        -1.0,
    )
    grad_projected = jnp.concatenate(
        [
            unrot_q.reshape(count_rows, width),
            unrot_k.reshape(count_rows, width),
            grad_v_tok.astype(jnp.float32).reshape(count_rows, width),
        ],
        axis=-1,
    ).astype(jnp.bfloat16)
    grad_project = jnp.einsum(
        "nd,nf->df", lowered1, grad_projected, preferred_element_type=jnp.float32
    )
    grad_lowered1 = jnp.einsum(
        "nf,df->nd", grad_projected, full_qkv, preferred_element_type=jnp.float32
    )
    grad_one = jnp.sum(grad_lowered1 * normed1, axis=0)
    grad_input = grad_residual + norm_back(
        grad_lowered1 * gain_one.astype(jnp.float32), normed1, factor1
    )
    pieces_one = grad_one.reshape(group_devices, head_devices, -1)
    pieces_two = grad_two.reshape(group_devices, head_devices, -1)
    part_qkv, part_out, part_in, part_mlp, part_one, part_two = (
        lax.psum_scatter(
            grad_project.astype(jnp.bfloat16), ("dp", "ctx"), scatter_dimension=0, tiled=True
        ).astype(jnp.float32),
        lax.psum_scatter(
            grad_outproj.astype(jnp.bfloat16), ("dp", "ctx"), scatter_dimension=0, tiled=True
        ).astype(jnp.float32),
        lax.psum_scatter(
            grad_inner.astype(jnp.bfloat16), ("dp", "ctx"), scatter_dimension=0, tiled=True
        ).astype(jnp.float32),
        lax.psum_scatter(
            grad_mlp.astype(jnp.bfloat16), ("dp", "ctx"), scatter_dimension=0, tiled=True
        ).astype(jnp.float32),
        lax.psum_scatter(
            pieces_one.astype(jnp.bfloat16), ("dp", "ctx"), scatter_dimension=0, tiled=True
        ).astype(jnp.float32),
        lax.psum_scatter(
            pieces_two.astype(jnp.bfloat16), ("dp", "ctx"), scatter_dimension=0, tiled=True
        ).astype(jnp.float32),
    )
    final_qkv, final_out, final_in, final_mlp, final_one, final_two = (
        lax.psum_scatter(
            part_qkv.astype(jnp.bfloat16), "head", scatter_dimension=1, tiled=True
        ).astype(jnp.float32),
        lax.psum_scatter(
            part_out.astype(jnp.bfloat16), "head", scatter_dimension=1, tiled=True
        ).astype(jnp.float32),
        lax.psum_scatter(
            part_in.astype(jnp.bfloat16), "head", scatter_dimension=1, tiled=True
        ).astype(jnp.float32),
        lax.psum_scatter(
            part_mlp.astype(jnp.bfloat16), "head", scatter_dimension=1, tiled=True
        ).astype(jnp.float32),
        lax.psum_scatter(
            part_one.astype(jnp.bfloat16), "head", scatter_dimension=1, tiled=True
        ).astype(jnp.float32),
        lax.psum_scatter(
            part_two.astype(jnp.bfloat16), "head", scatter_dimension=1, tiled=True
        ).astype(jnp.float32),
    )
    return (
        result.reshape(seqs_here, block_rows, width),
        grad_input.reshape(seqs_here, block_rows, width),
        final_qkv,
        final_out,
        final_in,
        final_mlp,
        final_one.reshape(-1),
        final_two.reshape(-1),
    )


F32 = jnp.float32
BF16 = jnp.bfloat16
GROUP = ("ctx", "head")


def dot(left, right, dims=((1,), (0,))):
    return lax.dot_general(left, right, (dims, ((), ())), preferred_element_type=F32)


def wide(values):
    return values.astype(F32)


def flat(values):
    return values.reshape(-1, values.shape[-1])


def lane_rotate(values, cosine, sine_signed):
    lane = lax.broadcasted_iota(jnp.int32, values.shape, 1)
    width = values.shape[1]
    partner = jnp.where(
        lane % HD < HD // 2,
        pltpu.roll(values, width - HD // 2, 1),
        pltpu.roll(values, HD // 2, 1),
    )
    return values * cosine + partner * sine_signed


def head_masks(shape):
    lane = lax.broadcasted_iota(jnp.int32, shape, 1)
    return [lane // HD == head for head in range(shape[1] // HD)]


def params(mebibytes):
    return pltpu.CompilerParams(vmem_limit_bytes=mebibytes * 1024 * 1024)


COST = pl.CostEstimate(flops=1 << 20, transcendentals=0, bytes_accessed=1 << 16)


def whole(array):
    return pl.BlockSpec(array.shape, lambda *_: (0,) * len(array.shape))


SCALARS = pl.BlockSpec(memory_space=pltpu.SMEM)


def project_kernel(place_ref, *refs):
    pieces, weights = refs[:6], refs[6:10]
    cos_ref, sin_ref, low_ref, qkv_ref, w_ref, gain1_ref, gain2_ref, rows_ref = refs[10:]
    block, part = pieces[0].shape[2], w_ref.shape[1] // 3
    rows = gain1_ref.shape[1] // 8

    @pl.when(pl.program_id(0) == 0)
    def _():
        for step, piece in enumerate(weights):
            for turn in range(2):
                at = 2 * (place_ref[8] ^ step) + (place_ref[9] ^ turn)
                w_ref[pl.ds(pl.multiple_of(at * rows, rows), rows), :] = piece[turn, :rows]
                gains = piece[turn, rows:].astype(F32)
                rows_ref[0, pl.ds(at, 1), :] = gains[:1, :rows]
                rows_ref[1, pl.ds(at, 1), :] = gains[1:2, :rows]
        for out, at in ((gain1_ref, 0), (gain2_ref, 1)):
            for row in range(8):
                out[:, row * rows : (row + 1) * rows] = rows_ref[at, row : row + 1, :]

    gain = gain1_ref[...]
    index = 0
    for piece in pieces:
        for inner in range(piece.shape[0]):
            normed, _ = normalize(piece[inner, 0].astype(F32))
            low_ref[index, 0] = (normed * gain).astype(BF16)
            index += 1
    projected = dot(flat(low_ref[:, 0]), w_ref[...])
    cosine, sine = cos_ref[...], sin_ref[...]
    shape = (8, block, part)
    qkv_ref[:, 0, :, :part] = (
        (lane_rotate(projected[:, :part], cosine, sine) * HD**-0.5).astype(BF16).reshape(shape)
    )
    qkv_ref[:, 0, :, part : 2 * part] = (
        lane_rotate(projected[:, part : 2 * part], cosine, sine).astype(BF16).reshape(shape)
    )
    qkv_ref[:, 0, :, 2 * part :] = projected[:, 2 * part :].astype(BF16).reshape(shape)


def project(place, pieces, weights, cosine, sine):
    seqs, block, width = pieces[0].shape[1:]
    own = weights[0].shape[2]

    def by_seq(lead, last):
        return pl.BlockSpec((lead, 1, block, last), lambda s: (0, s, 0, 0))

    return pl.pallas_call(
        project_kernel,
        grid=(seqs,),
        in_specs=[SCALARS]
        + [by_seq(piece.shape[0], width) for piece in pieces]
        + [whole(w) for w in weights]
        + [whole(cosine), whole(sine)],
        out_specs=(
            by_seq(8, width),
            by_seq(8, own),
            pl.BlockSpec((width, own), lambda s: (0, 0)),
            pl.BlockSpec((1, width), lambda s: (0, 0)),
            pl.BlockSpec((1, width), lambda s: (0, 0)),
        ),
        out_shape=(
            jax.ShapeDtypeStruct((8, seqs, block, width), BF16),
            jax.ShapeDtypeStruct((8, seqs, block, own), BF16),
            jax.ShapeDtypeStruct((width, own), BF16),
            jax.ShapeDtypeStruct((1, width), F32),
            jax.ShapeDtypeStruct((1, width), F32),
        ),
        scratch_shapes=[pltpu.VMEM((2, 8, width // 8), F32)],
        compiler_params=params(60),
        cost_estimate=COST,
        name="project",
    )(place, *pieces, *weights, cosine, sine)


def attend_kernel(place_ref, q_ref, k_ref, v_ref, *refs):
    att_ref, log_ref, home_ref = refs[-3:]
    step, seq = pl.program_id(0), len(refs) - 3
    if seq:

        @pl.when(step == 0)
        def _():
            home_ref[:, :1] = refs[0][...]

    queries, keys, values = flat(q_ref[...]), flat(k_ref[...]), flat(v_ref[...])
    attended = jnp.zeros(queries.shape, F32)
    logs = jnp.zeros(queries.shape, F32)
    for mask in head_masks(queries.shape):
        scores = dot(jnp.where(mask, queries, 0), keys, ((1,), (1,)))
        peak = jnp.max(scores, axis=1, keepdims=True)
        weights = jnp.exp(scores - peak)
        total = jnp.sum(weights, axis=1, keepdims=True)
        mixed = dot(weights.astype(BF16), values) * (1.0 / total)
        attended = jnp.where(mask, mixed, attended)
        logs = jnp.where(mask, peak + jnp.log(total), logs)
    att_ref[...] = attended.reshape(att_ref.shape)
    log_ref[...] = logs.reshape(log_ref.shape)
    low = attended.astype(BF16).reshape(att_ref.shape)
    for inner in range(2):
        home_ref[place_ref[2 * step + inner], seq] = low[inner, 0]


def attend(place, qkv, *home):
    _, _, block, own = qkv.shape
    part, seq = own // 3, len(home)
    rows = pl.BlockSpec((2, 1, block, part), lambda i: (i, 0, 0, 0))
    shape = (8, 1, block, part)
    return pl.pallas_call(
        attend_kernel,
        grid=(4,),
        in_specs=[
            SCALARS,
            pl.BlockSpec((2, 1, block, part), lambda i: (i, seq, 0, 0)),
            pl.BlockSpec((8, 1, block, part), lambda i: (0, seq, 0, 1)),
            pl.BlockSpec((8, 1, block, part), lambda i: (0, seq, 0, 2)),
            *[whole(h) for h in home],
        ],
        out_specs=(
            rows,
            rows,
            pl.BlockSpec((8, 1 + seq, block, part), lambda i: (0, 0, 0, 0)),
        ),
        out_shape=(
            jax.ShapeDtypeStruct(shape, F32),
            jax.ShapeDtypeStruct(shape, F32),
            jax.ShapeDtypeStruct((8, 1 + seq, block, part), BF16),
        ),
        compiler_params=params(24),
        cost_estimate=COST,
        name="attend",
    )(place, qkv, qkv, qkv, *home)


def branch_kernel(place_ref, *refs):
    pieces = refs[:6]
    rows_ref, tokens_ref, gain_ref, residual_ref, low_ref, side_ref, total_ref = refs[6:]
    heads = rows_ref.shape[0] // 2
    for c in range(2):
        side_ref[c] = jnp.concatenate([flat(rows_ref[c * heads + d]) for d in range(heads)], axis=1)
    total_ref[...] = flat(wide(tokens_ref[...]))
    index = 0
    for piece in pieces:
        n = piece.shape[2]
        for inner in range(piece.shape[0]):
            at = place_ref[index]
            columns = pl.ds(pl.multiple_of((at % heads) * n, n), n)
            total_ref[:, columns] += dot(side_ref[at // heads], piece[inner])
            index += 1
    total = total_ref[...]
    normed, _ = normalize(total)
    residual_ref[...] = total.reshape(residual_ref.shape)
    low_ref[...] = (normed * gain_ref[...]).astype(BF16).reshape(low_ref.shape)


def branch(place, pieces, rows, tokens, gain):
    args = (*pieces, rows, tokens, gain)
    seqs, block, width = tokens.shape
    return pl.pallas_call(
        branch_kernel,
        in_specs=[SCALARS] + [whole(a) for a in args],
        out_shape=(
            jax.ShapeDtypeStruct(tokens.shape, F32),
            jax.ShapeDtypeStruct(tokens.shape, BF16),
        ),
        scratch_shapes=[
            pltpu.VMEM((2, seqs * block, pieces[0].shape[1]), BF16),
            pltpu.VMEM((seqs * block, width), F32),
        ],
        compiler_params=params(16),
        cost_estimate=COST,
        name="branch",
    )(place, *args)


def combine(*groups):
    parts = [part for group in groups for _, parts in group for part in parts]
    rows = sum(count for count, _ in groups[0])
    width = parts[0][0].shape[2]

    def kernel(*refs):
        at = 0
        for k, group in enumerate(groups):
            row = 0
            for count, terms in group:
                total = 0.0
                for _, _, start in terms:
                    total = total + wide(refs[at][0, start : start + count])
                    at += 1
                refs[-1][k, row : row + count] = total.astype(BF16)
                row += count

    return pl.pallas_call(
        kernel,
        grid=(1,),
        in_specs=[
            pl.BlockSpec((1, *array.shape[1:]), lambda *_, index=index: (index, 0, 0))
            for array, index, _ in parts
        ],
        out_specs=pl.BlockSpec((len(groups), rows, width), lambda *_: (0, 0, 0)),
        out_shape=jax.ShapeDtypeStruct((len(groups), rows, width), BF16),
        compiler_params=params(16),
        cost_estimate=COST,
        name="combine",
    )(*[array for array, _, _ in parts])


def mlp_kernel(*refs, count, ends):
    pieces, tops = refs[:count], refs[count : 2 * count]
    w_ref, out_w_ref = refs[2 * count : 2 * count + 2]
    low_ref, top_ref, mixed_ref, lifted_ref, *out_refs = refs[-4 - len(ends) :]
    step = pl.program_id(0)
    start = 0
    for piece, top in zip(pieces, tops):

        @pl.when((step >= start) & (step < start + piece.shape[0]))
        def _(piece=piece, top=top, start=start):
            low_ref[0] = piece[step - start]
            top_ref[0] = top[step - start]

        start += piece.shape[0]

    hidden = w_ref.shape[1] // 2
    lifted = dot(flat(low_ref[...]), w_ref[...])
    first, second = lifted[:, :hidden], lifted[:, hidden:]
    grad_mixed = dot(flat(top_ref[...]), out_w_ref[...], ((1,), (1,)))
    gate = 0.5 * (1.0 + lax.erf(first * (0.5**0.5)))
    slope = gate + first * jnp.exp(first * first * -0.5) * ((2.0 * math.pi) ** -0.5)
    activated = first * gate
    mixed_ref[...] = (activated * second).astype(BF16).reshape(mixed_ref.shape)
    grad = jnp.concatenate(
        [(grad_mixed * second * slope).astype(BF16), (grad_mixed * activated).astype(BF16)],
        axis=1,
    )
    lifted_ref[...] = grad.reshape(lifted_ref.shape)
    partial = dot(grad, w_ref[...], ((1,), (1,))).astype(BF16).reshape(low_ref.shape)
    start = 0
    for out, end in zip(out_refs, ends):

        @pl.when((step >= start) & (step < end))
        def _(out=out):
            out[...] = partial

        start = end


def mlp(pieces, tops, w, out_w, base, ends, earlier=()):
    seqs, block, width = pieces[0].shape[1:]
    hidden = w.shape[1] // 2
    whole_in = (*pieces, *tops, w, out_w)

    def rows(last):
        return pl.BlockSpec((1, seqs, block, last), lambda i: (i + base, 0, 0, 0))

    def within(start, end):
        return pl.BlockSpec(
            (1, seqs, block, width),
            lambda i: (jnp.clip(i - start, 0, end - start - 1), 0, 0, 0),
        )

    starts = (0, *ends[:-1])
    lasts = (width, width, hidden, 2 * hidden)
    return pl.pallas_call(
        functools.partial(mlp_kernel, count=len(pieces), ends=ends),
        grid=(ends[-1],),
        in_specs=[whole(array) for array in whole_in]
        + [pl.BlockSpec(memory_space=pl.ANY)] * len(earlier),
        out_specs=(
            *[rows(last) for last in lasts],
            *[within(start, end) for start, end in zip(starts, ends)],
        ),
        out_shape=(
            *[jax.ShapeDtypeStruct((8, seqs, block, last), BF16) for last in lasts],
            *[
                jax.ShapeDtypeStruct((end - start, seqs, block, width), BF16)
                for start, end in zip(starts, ends)
            ],
        ),
        input_output_aliases={len(whole_in) + at: at for at in range(len(earlier))},
        compiler_params=params(32),
        cost_estimate=COST,
        name="mlp",
    )(*whole_in, *earlier)


def out_grad_kernel(place_ref, rows_ref, grad_ref, keep_ref, send_ref):
    grads = flat(grad_ref[...])
    for index in range(8):
        part = dot(flat(rows_ref[place_ref[index]]), grads, ((0,), (0,))).astype(BF16)
        if index < 5:
            keep_ref[index] = part
        else:
            send_ref[index - 5] = part


def out_grad(place, rows, grads):
    part, width = rows.shape[-1], grads.shape[-1]
    return pl.pallas_call(
        out_grad_kernel,
        in_specs=[SCALARS, whole(rows), whole(grads)],
        out_shape=(
            jax.ShapeDtypeStruct((5, part, width), BF16),
            jax.ShapeDtypeStruct((3, part, width), BF16),
        ),
        compiler_params=params(16),
        cost_estimate=COST,
        name="out_grad",
    )(place, rows, grads)


def branch_back_kernel(place_ref, *refs):
    pieces = refs[:6]
    keep_ref, near_ref, own_ref, residual_ref, top_ref, gain_ref = refs[6:12]
    grad_ref, branch_ref, home_ref, sum_ref, low_ref, side_ref = refs[12:]
    grad_low = wide(flat(keep_ref[...])) + wide(flat(near_ref[...])) + wide(flat(own_ref[...]))
    normed, factor = normalize(flat(residual_ref[...]))
    sum_ref[...] = jnp.sum(grad_low * normed, axis=0, keepdims=True)
    grad = flat(wide(top_ref[...])) + norm_back(grad_low * gain_ref[...], normed, factor)
    grad_ref[...] = grad.reshape(grad_ref.shape)
    low_ref[...] = grad.astype(BF16)
    branch_ref[...] = low_ref[...].reshape(branch_ref.shape)
    heads = home_ref.shape[0] // 2
    side_ref[...] = jnp.zeros_like(side_ref)
    index = 0
    for piece in pieces:
        n = piece.shape[2]
        for inner in range(piece.shape[0]):
            at = place_ref[index]
            columns = pl.ds(pl.multiple_of((at % heads) * n, n), n)
            side_ref[at // heads] += dot(low_ref[:, columns], piece[inner], ((1,), (1,)))
            index += 1
    part = home_ref.shape[3]
    for c in range(2):
        for d in range(heads):
            home = side_ref[c, :, d * part : (d + 1) * part].astype(BF16)
            home_ref[c * heads + d] = home.reshape(home_ref.shape[1:])


def branch_back(place, pieces, keep, near, own, residual, top, gain):
    args = (*pieces, keep, near, own, residual, top, gain)
    seqs, block, width = residual.shape
    tall = pieces[0].shape[1]
    shapes = (
        jax.ShapeDtypeStruct(residual.shape, F32),
        jax.ShapeDtypeStruct(residual.shape, BF16),
        jax.ShapeDtypeStruct((8, seqs, block, tall // 4), BF16),
        jax.ShapeDtypeStruct((1, width), F32),
    )
    return pl.pallas_call(
        branch_back_kernel,
        grid=(1,),
        in_specs=[SCALARS]
        + [whole(piece) for piece in pieces]
        + [pl.BlockSpec((1, seqs * block, width), lambda *_: (0, 0, 0))] * 2
        + [whole(a) for a in args[8:]],
        out_specs=tuple(whole(shape) for shape in shapes),
        out_shape=shapes,
        scratch_shapes=[
            pltpu.VMEM((seqs * block, width), BF16),
            pltpu.VMEM((2, seqs * block, tall), F32),
        ],
        compiler_params=params(24),
        cost_estimate=COST,
        name="branch_back",
    )(place, *args)


def attend_back_kernel(
    place_ref, q_ref, k_ref, v_ref, grad_ref, att_ref, log_ref, cosq_ref, sinq_ref, cos_ref,
    sin_ref, w_ref, low_ref, *refs, seq, last,
):
    if last:
        before_ref, gain1_ref, gain2_ref, keep_ref, send_ref, grad_w_ref, *scratch = refs
    else:
        keep_ref, send_ref, before_ref, *scratch = refs
    proj_ref, sum_k, sum_v = scratch
    step = pl.program_id(0)
    block, part = q_ref.shape[2], q_ref.shape[3]

    @pl.when(step == 0)
    def _():
        sum_k[...] = jnp.zeros_like(sum_k)
        sum_v[...] = jnp.zeros_like(sum_v)

    queries, keys, values = flat(q_ref[...]), flat(k_ref[...]), flat(v_ref[...])
    grads = jnp.concatenate([grad_ref[place_ref[2 * step + inner], seq] for inner in range(2)])
    along = (grads.astype(F32) * flat(att_ref[...])).T
    logs = flat(log_ref[...]).T
    grad_queries = jnp.zeros(queries.shape, F32)
    for head, mask in enumerate(head_masks(queries.shape)):
        own_q = jnp.where(mask, queries, 0)
        own_g = jnp.where(mask, grads, 0)
        scores = dot(keys, own_q, ((1,), (1,)))
        weights = jnp.exp(scores - logs[head * HD : head * HD + 1])
        lifted = dot(values, own_g, ((1,), (1,)))
        row = jnp.sum(along[head * HD : (head + 1) * HD], axis=0, keepdims=True)
        grad_scores = (weights * (lifted - row)).astype(BF16)
        sum_k[...] += dot(grad_scores, own_q)
        sum_v[...] += dot(weights.astype(BF16), own_g)
        grad_queries = jnp.where(mask, dot(grad_scores, keys, ((0,), (0,))), grad_queries)
    grad_queries = lane_rotate(grad_queries * HD**-0.5, cosq_ref[...], -sinq_ref[...])
    rows = pl.multiple_of(step * 2 * block, 2 * block)
    proj_ref[pl.ds(rows, 2 * block), :part] = grad_queries.astype(BF16)

    @pl.when(step == 3)
    def _():
        grad_keys = lane_rotate(sum_k[...], cos_ref[...], -sin_ref[...])
        proj_ref[:, part : 2 * part] = grad_keys.astype(BF16)
        proj_ref[:, 2 * part :] = sum_v[...].astype(BF16)
        partial = dot(proj_ref[...], w_ref[...], ((1,), (1,))).astype(BF16)
        keep_ref[...] = partial[: 5 * block].reshape(5, block, -1)
        send_ref[...] = partial[5 * block :].reshape(3, block, -1)
        grad_w = dot(proj_ref[...], flat(low_ref[...]), ((0,), (0,)))
        if last:
            grad_w = (grad_w + before_ref[...]).T
            along_w = jnp.sum(grad_w * wide(w_ref[...]), axis=1, keepdims=True)
            along_w = jnp.broadcast_to(along_w, (w_ref.shape[0], 128)).T[:1] / gain1_ref[...]
            row = lax.broadcasted_iota(jnp.int32, (GAIN_ROWS, w_ref.shape[0]), 0)
            gains = jnp.where(row == 0, along_w, jnp.where(row == 1, gain2_ref[...], 0.0))
            n = grad_w_ref.shape[1] - GAIN_ROWS
            for at in range(grad_w_ref.shape[0]):
                part_rows = slice(at * n, (at + 1) * n)
                grad_w_ref[at, :n] = grad_w[part_rows].astype(BF16)
                grad_w_ref[at, n:, :n] = gains[:, part_rows].astype(BF16)
                rest = grad_w_ref.shape[2] - n
                grad_w_ref[at, n:, n:] = jnp.zeros((GAIN_ROWS, rest), BF16)
        else:
            before_ref[...] = grad_w


GAIN_ROWS = 16


def attend_back(place, qkv, grads, attended, logs, cosine, sine, w, low, seq, *before, dp=1):
    _, _, block, own = qkv.shape
    part, width = own // 3, w.shape[0]
    last = len(before) > 0
    rows = pl.BlockSpec((2, 1, block, part), lambda i: (i, 0, 0, 0))
    angles = pl.BlockSpec((2 * block, part), lambda i: (i, 0))

    def full(*shape):
        return pl.BlockSpec(shape, lambda i: (0,) * len(shape))

    args = [place, qkv, qkv, qkv, grads, attended, logs, cosine, sine, cosine, sine, w, low]
    in_specs = [
        SCALARS,
        pl.BlockSpec((2, 1, block, part), lambda i: (i, seq, 0, 0)),
        pl.BlockSpec((8, 1, block, part), lambda i: (0, seq, 0, 1)),
        pl.BlockSpec((8, 1, block, part), lambda i: (0, seq, 0, 2)),
        whole(grads),
        rows,
        rows,
        angles,
        angles,
        whole(cosine),
        whole(sine),
        whole(w),
        pl.BlockSpec((8, 1, block, width), lambda i: (0, seq, 0, 0)),
    ]
    shapes = [((5, block, width), BF16), ((3, block, width), BF16)]
    if last:
        args += before
        in_specs += [whole(array) for array in before]
        shapes += [((dp, width // dp + GAIN_ROWS, own), BF16)]
    else:
        shapes += [((own, width), F32)]
    return pl.pallas_call(
        functools.partial(attend_back_kernel, seq=seq, last=last),
        grid=(4,),
        in_specs=in_specs,
        out_specs=tuple(full(*shape) for shape, _ in shapes),
        out_shape=tuple(jax.ShapeDtypeStruct(shape, kind) for shape, kind in shapes),
        scratch_shapes=[
            pltpu.VMEM((8 * block, own), BF16),
            pltpu.VMEM((8 * block, part), F32),
            pltpu.VMEM((8 * block, part), F32),
        ],
        compiler_params=params(60),
        cost_estimate=COST,
        name="attend_back",
    )(*args)


def input_grad_kernel(*refs):
    keeps, (near_ref, own_ref, tokens_ref, residual_ref, gain_ref, out_ref) = refs[:-6], refs[-6:]
    block = tokens_ref.shape[1]
    for seq, keep in enumerate(keeps):
        rows = slice(seq * block, (seq + 1) * block)
        grad = wide(keep[0, :block]) + wide(near_ref[0, rows]) + wide(own_ref[0, rows])
        normed, factor = normalize(wide(tokens_ref[seq]))
        out_ref[seq] = residual_ref[seq] + norm_back(grad * gain_ref[...], normed, factor)


def input_grad(keeps, near, own, tokens, residual, gain):
    rest = (own, tokens, residual, gain)
    return pl.pallas_call(
        input_grad_kernel,
        grid=(1,),
        in_specs=[
            pl.BlockSpec((1, *array.shape[1:]), lambda *_: (0, 0, 0)) for array in (*keeps, near)
        ]
        + [whole(array) for array in rest],
        out_specs=whole(residual),
        out_shape=jax.ShapeDtypeStruct(residual.shape, F32),
        compiler_params=params(16),
        cost_estimate=COST,
        name="input_grad",
    )(*keeps, near, *rest)


def finish_kernel(keep_ref, rows_ref, near_ref, home_ref, residual_ref, out_ref, grad_ref):
    rows = keep_ref.shape[1]
    total = wide(keep_ref[0]) + wide(near_ref[0, :rows]) + wide(home_ref[0, :rows])
    out_ref[...] = (residual_ref[...] + total.reshape(residual_ref.shape)).astype(BF16)
    total = wide(rows_ref[0]) + wide(near_ref[0, rows:]) + wide(home_ref[0, rows:])
    n = grad_ref.shape[2]
    for at in range(grad_ref.shape[0]):
        grad_ref[at] = total[:, at * n : (at + 1) * n].astype(BF16)


def finish(keep, rows, near, home, residual, dp):
    args = (keep, rows, near, home)
    shapes = (
        jax.ShapeDtypeStruct(residual.shape, BF16),
        jax.ShapeDtypeStruct((dp, rows.shape[1], rows.shape[2] // dp), BF16),
    )
    return pl.pallas_call(
        finish_kernel,
        grid=(1,),
        in_specs=[pl.BlockSpec((1, *array.shape[1:]), lambda *_: (0, 0, 0)) for array in args]
        + [whole(residual)],
        out_specs=tuple(whole(shape) for shape in shapes),
        out_shape=shapes,
        compiler_params=params(16),
        cost_estimate=COST,
        name="finish",
    )(*args, residual)


class Group:
    def __init__(self):
        self.heads = lax.axis_size("head")
        self.dp = lax.axis_size("dp")
        self.ctx_at = lax.axis_index("ctx")
        self.head_at = lax.axis_index("head")
        self.dp_at = lax.axis_index("dp")
        self.at = self.ctx_at * self.heads + self.head_at
        near, far = [], []
        for c in range(2):
            for h in range(self.heads):
                x, y = (c ^ 1) * self.heads + h, c * self.heads + (h ^ 2)
                near.append((c * self.heads + h, x if h % 2 == 0 else y))
                far.append((c * self.heads + h, y if h % 2 == 0 else x))
        self.near, self.far = near, far

    def order(self):
        first = jnp.where(self.head_at % 2 == 0, 4, 2)
        second = 6 - first
        return jnp.stack(
            [self.at ^ bits for bits in (0, 1, first, first ^ 1, 6, second ^ 1, second, 7)]
        )

    def swap(self, values, bit):
        if bit == 4:
            return lax.ppermute(values, "ctx", [(0, 1), (1, 0)])
        return lax.ppermute(values, "head", [(i, i ^ bit) for i in range(self.heads)])

    def mate(self, values):
        return self.swap(values, 1)

    def to_near(self, values):
        return lax.ppermute(values, GROUP, self.near)

    def to_far(self, values):
        return lax.ppermute(values, GROUP, self.far)

    def rows_back(self, values, place):
        pairs, same = [], False
        for d in range(self.dp):
            for h in range(self.heads):
                if (d, h) == (place[h], d):
                    same = same | ((self.dp_at == d) & (self.head_at == h))
                else:
                    pairs.append((d * self.heads + h, place[h] * self.heads + d))
        return jnp.where(same, values, lax.ppermute(values, ("dp", "head"), pairs))

    def across(self, values, step):
        return lax.ppermute(values, "dp", [(i, i ^ step) for i in range(self.dp)])


def pick(array, index, axis):
    return lax.dynamic_index_in_dim(array, index, axis, keepdims=False)


def after(values, *earlier):
    return lax.optimization_barrier((values, earlier))[0]


def local_split(tokens, cotangent, w_qkv, w_attn_out, w_in, w_mlp_out, norm_gain1, norm_gain2):
    seqs, block, width = tokens.shape
    group = Group()
    heads, dp = group.heads, group.dp
    at_c, at_h = group.ctx_at, group.head_at
    parts = 2 * heads
    hidden = w_in.shape[1] // 2 // parts
    padded = -(-hidden // 128) * 128
    own_width = width // parts
    half = heads // 2
    rows_here = w_qkv.shape[0]
    place = [2 * (h % half) + h // half for h in range(heads)]
    straight = list(range(heads))
    order = group.order()
    scalars = jnp.concatenate([order, jnp.stack([group.dp_at, at_c])]).astype(jnp.int32)
    mate, near, far = group.mate, group.to_near, group.to_far

    def in_order(own, other):
        return jnp.where(at_c == 0, jnp.stack([own, other]), jnp.stack([other, own]))

    def exchange(values):
        return lax.all_to_all(values, GROUP, split_axis=0, concat_axis=0, tiled=True)


    gains = jnp.pad(
        jnp.stack([norm_gain1, norm_gain2]), ((0, 14), (0, 3 * own_width - rows_here))
    )
    qkv_view = w_qkv.reshape(rows_here, 3, width)

    def qkv_part(at):
        start = (2 * at_h + at) * own_width
        cut = lax.dynamic_slice_in_dim(qkv_view, start, own_width, 2)
        return jnp.concatenate([cut.reshape(rows_here, 3 * own_width), gains])

    x_own = tokens[None]
    x_mate = mate(x_own)
    qkv_other, qkv_own = qkv_part(1 - at_c), qkv_part(at_c)
    qkv_cross = group.swap(after(qkv_other, x_own), 4)
    in_view = after(w_in, qkv_other).reshape(rows_here, 2, heads, 2, hidden)
    in_view = pick(in_view, 2 * (at_h % half) + at_h // half, 2)

    def in_part(at):
        cut = pick(in_view, at, 2)
        return jnp.pad(cut, ((0, 0), (0, 0), (0, padded - hidden))).reshape(rows_here, 2 * padded)

    in_other, in_own = in_part(1 - at_c), in_part(at_c)
    in_cross = group.swap(after(in_other, qkv_cross), 4)
    x_chip = jnp.concatenate([x_own, after(x_mate, qkv_cross, qkv_own)])
    x_near = near(x_chip)
    qkv_pair = jnp.stack([qkv_own, qkv_cross])
    qkv_pieces = [qkv_pair] + [group.across(qkv_pair, step) for step in range(1, dp)]

    slices = jnp.concatenate([w_attn_out, w_mlp_out])
    slices = after(slices, x_near, *qkv_pieces)
    slices = lax.dynamic_slice_in_dim(slices, at_h * (width // heads), width // heads, 1)
    slices = jnp.pad(slices, ((0, 64), (0, 0)))
    slices = lax.all_gather(slices, "dp", axis=0)
    positions = after(order, qkv_pair)[:, None] * block + jnp.arange(block, dtype=jnp.int32)
    lane = jnp.arange(own_width, dtype=jnp.int32)
    frequency = jnp.exp(
        (lane % (HD // 2)).astype(F32) * (-math.log(ROPE_BASE) / (HD // 2))
    )
    angles = wide(positions.reshape(-1))[:, None] * frequency[None, :]
    cosine = jnp.cos(angles)
    sine = jnp.sin(angles) * jnp.where(lane % HD < HD // 2, -1.0, 1.0)[None, :]

    x_far = far(x_near[:1])
    x_near = after(x_near, *qkv_pieces, cosine, sine, in_cross, in_own)
    x_near_mate = mate(x_near)
    cot_own = after(cotangent, x_near)[None]
    cot_mate = mate(cot_own)
    in_pair, x_far = lax.optimization_barrier((in_order(in_own, in_cross), x_far))
    weight_in = lax.all_gather(in_pair, "dp", axis=0).reshape(width, -1)
    cot_chip = jnp.concatenate([cot_own, cot_mate])
    x_far = after(x_far, cot_chip)
    x_far_mate = mate(x_far)

    cot_near = near(after(cot_chip, x_far))
    out_rows = w_attn_out.shape[0]
    x_pieces = (x_own, x_mate, x_near, x_far, x_near_mate, x_far_mate)
    low1, qkv, weight_qkv, gain_one, gain_two = project(
        scalars, x_pieces, qkv_pieces, cosine, sine
    )

    slices = after(slices, qkv)
    out_own = slices[:, :out_rows].reshape(1, dp * out_rows, -1)
    out_mate = mate(out_own)
    mlp_slices = jnp.stack(
        [slices[place[h], out_rows : out_rows + hidden] for h in range(heads)]
    )
    mlp_slices = lax.all_to_all(mlp_slices, "head", split_axis=0, concat_axis=0, tiled=True)
    out_near = near(jnp.concatenate([out_own, out_mate]))
    att_0, log_0, home_0 = attend(scalars, after(qkv, out_mate))
    cot_near = after(cot_near, home_0)
    cot_far, cot_near_mate = far(cot_near[:1]), mate(cot_near)
    out_near = after(out_near, home_0)
    out_far, out_near_mate = far(out_near[:1]), mate(out_near)
    att_1, log_1, home = attend(scalars, after(qkv, cot_near, out_near), home_0)
    home, cot_far, out_far = lax.optimization_barrier((home, cot_far, out_far))
    att_rows = exchange(home)
    out_far_mate, cot_far_mate = mate(after(out_far, home)), mate(after(cot_far, home))
    out_pieces = (out_own, out_mate, out_near, out_far, out_near_mate, out_far_mate)
    weight_mlp = jnp.moveaxis(after(mlp_slices, home), 0, 1).reshape(hidden, width)
    weight_mlp = jnp.pad(weight_mlp, ((0, padded - hidden), (0, 0)))
    residual, low2 = branch(
        scalars, out_pieces, after(att_rows, cot_far_mate, weight_mlp, weight_in), tokens, gain_two
    )

    low_own = low2[None]
    low_mate = mate(low_own)
    low_near = near(jnp.concatenate([low_own, low_mate]))
    *arrays, keep_a = mlp(
        (low_own, low_mate), (cot_own, cot_mate), weight_in, weight_mlp, 0, (2,)
    )
    low_near = after(low_near, keep_a)
    low_far, low_near_mate = far(low_near[:1]), mate(low_near)
    *arrays, keep_b = mlp((low_near,), (cot_near,), weight_in, weight_mlp, 2, (2,), arrays)
    low_far_mate = mate(after(low_far, keep_b))
    low2_all, cot_all, mixed, grad_lifted, keep_c, send = mlp(
        (low_far, low_near_mate, low_far_mate),
        (cot_far, cot_near_mate, cot_far_mate),
        weight_in,
        weight_mlp,
        4,
        (1, 4),
        arrays,
    )

    def over_tokens(left, right):
        return dot(flat(left), flat(right), ((0,), (0,)))

    def scatter(values):
        return lax.psum_scatter(values.astype(BF16), "dp", scatter_dimension=0, tiled=True)

    def columns_first(values):
        return jnp.moveaxis(values.reshape(values.shape[0], dp, -1), 1, 0)

    rows = seqs * block

    def by_rows(values):
        return values.reshape(values.shape[0], -1, width)

    keep_a, keep_b, keep_c, send = (by_rows(array) for array in (keep_a, keep_b, keep_c, send))
    met = mate(send)
    last = combine([(rows, [(keep_c, 0, 0), (met, 2, 0)])])
    last_far = far(last)
    grad_mlp = columns_first(over_tokens(after(mixed, last), cot_all)[:hidden]).astype(BF16)
    last_far = after(last_far, grad_mlp)
    grad_mlp = scatter(grad_mlp)[0]
    chip = combine(
        [(rows, [(keep_b, 0, 0), (met, 0, 0), (last_far, 0, 0)])],
        [(rows, [(keep_b, 1, 0), (met, 1, 0)])],
    )
    chip_near = near(chip)
    grad_in = over_tokens(low2_all, after(grad_lifted, chip)).astype(BF16)
    cut = 5 * rows
    mixed_flat = flat(after(mixed, chip))
    out_keep = dot(mixed_flat[:cut], weight_mlp).astype(BF16).reshape(5, rows, width)
    out_send = dot(mixed_flat[cut:], weight_mlp).astype(BF16).reshape(3, rows, width)
    chip_near = after(chip_near, grad_in, out_keep, out_send)
    grad_in = scatter(grad_in)
    home = mate(combine([(rows, [(keep_a, 1, 0), (chip_near, 1, 0)])])[0])
    out_met = mate(after(out_send, chip_near))
    grad_residual, grad_branch, home, gain2_sum = branch_back(
        scalars, out_pieces, keep_a, chip_near, home, residual, cotangent, gain_two
    )
    grad_home = exchange(home)

    rows_keep, rows_send = out_grad(scalars, after(att_rows, home), grad_branch)
    rows_met = mate(rows_send)
    few = rows_keep.shape[1]

    def ends(index, at, *more):
        kept = [(out_keep, index, 0)], [(rows_keep, index, 0)]
        if at is not None:
            kept[0].append((out_met, at, 0))
            kept[1].append((rows_met, at, 0))
        for array, where in more:
            kept[0].append((array, where, 0))
            kept[1].append((array, where, rows))
        return [(rows, kept[0]), (few, kept[1])]

    end_last = combine(ends(4, 2))
    grad_home = after(grad_home, end_last, grad_mlp)
    end_far = far(after(end_last, grad_home))
    keep_0, send_0, before = attend_back(
        scalars, qkv, grad_home, att_0, log_0, cosine, sine, weight_qkv, low1, 0
    )
    met_0 = mate(send_0)
    end_far, grad_in = lax.optimization_barrier((after(end_far, send_0), grad_in))
    in_parts = grad_in.reshape(2, rows_here, -1)
    in_cross = group.swap(pick(in_parts, 1 - at_c, 0), 4)
    end_chip = combine(ends(2, 0, (end_far, 0)), ends(3, 1))
    end_near = near(after(end_chip, in_cross))
    keep_1, send_1, grad_qkv = attend_back(
        scalars, qkv, after(grad_home, end_chip), att_1, log_1, cosine, sine,
        weight_qkv, low1, 1, before, gain_one, gain2_sum, dp=dp,
    )

    grad_qkv = scatter(grad_qkv.reshape(-1, grad_qkv.shape[2]))
    met_1 = mate(send_1)
    end_home = combine(ends(1, None, (after(end_near, send_1), 1)))
    met_1, end_home = lax.optimization_barrier((met_1, end_home))
    end_home = mate(end_home)

    def both(index, at, *more):
        kept = [(keep_0, index, 0)], [(keep_1, index, 0)]
        if at is not None:
            kept[0].append((met_0, at, 0))
            kept[1].append((met_1, at, 0))
        for array, where in more:
            kept[0].append((array, where, 0))
            kept[1].append((array, where, block))
        return [(block, kept[0]), (block, kept[1])]

    last = combine(both(4, 2))
    last_far = far(last)
    result, grad_out = finish(
        out_keep, rows_keep, end_near, after(end_home, last), residual, dp
    )
    last_far, grad_out = lax.optimization_barrier((last_far, grad_out))
    grad_out = scatter(grad_out)[0]
    chip = combine(both(2, 0, (last_far, 0)), both(3, 1))
    chip_near = near(chip)

    grad_in = in_order(after(pick(in_parts, at_c, 0), chip), in_cross)
    late = at_h // half
    grad_in = jnp.stack([grad_in[..., :hidden], grad_in[..., padded : padded + hidden]])
    stays = pick(grad_in, late, 0)
    comes = group.swap(pick(grad_in, 1 - late, 0), half)
    grad_qkv = after(grad_qkv, chip)
    both_rows = 2 * rows_here
    qkv_parts = grad_qkv[:both_rows].reshape(2, rows_here, -1)
    gains = grad_qkv[both_rows:]
    cross = jnp.concatenate([pick(qkv_parts, 1 - at_c, 0), gains])
    cross = group.swap(cross, 4)
    chip_near = after(chip_near, comes, cross)
    home = combine(both(1, None, (chip_near, 1)))
    cross = after(cross, home)
    home = mate(home)
    grad_qkv = in_order(pick(qkv_parts, at_c, 0), cross[:rows_here])
    gains = (wide(gains) + wide(cross[rows_here:])).astype(BF16)
    gains = wide(gains) + sum(wide(group.swap(gains, bit)) for bit in range(1, heads))
    grad_input = input_grad((keep_0, keep_1), chip_near, home, tokens, grad_residual, gain_one)
    grad_out, grad_mlp, grad_input = lax.optimization_barrier((grad_out, grad_mlp, grad_input))
    grad_mlp = group.rows_back(grad_mlp, place)
    grad_out = wide(group.rows_back(grad_out, straight))

    grad_mlp = wide(grad_mlp)
    grad_in = jnp.where(
        late == 0, jnp.concatenate([stays, comes]), jnp.concatenate([comes, stays])
    )
    grad_in = wide(jnp.moveaxis(grad_in, 0, 1).reshape(rows_here, -1))

    per_device = width // (dp * parts)
    start = group.at * per_device
    grad_gain1, grad_gain2 = (
        lax.dynamic_slice_in_dim(gains[i], start, per_device, 0) for i in range(2)
    )
    grad_qkv = grad_qkv.reshape(2, rows_here, 3, own_width)
    grad_qkv = jnp.moveaxis(grad_qkv, 2, 0)
    odd = at_h % 2
    stays = pick(grad_qkv, odd + late, 0)
    core = group.swap(pick(grad_qkv, 1 - odd + late, 0), 1)
    chip = group.swap(pick(grad_qkv, 2 - 2 * late, 0), 2)
    grad_qkv = jnp.where(
        odd == 0, jnp.concatenate([stays, core, chip]), jnp.concatenate([chip, core, stays])
    )
    grad_qkv = wide(jnp.moveaxis(grad_qkv, 0, 1).reshape(rows_here, -1))

    return (
        result,
        grad_input,
        grad_qkv,
        grad_out,
        grad_in,
        grad_mlp,
        grad_gain1,
        grad_gain2,
    )


def local(tokens, cotangent, w_qkv, w_attn_out, w_in, w_mlp_out, norm_gain1, norm_gain2):
    args = (tokens, cotangent, w_qkv, w_attn_out, w_in, w_mlp_out, norm_gain1, norm_gain2)
    sizes = [lax.axis_size(axis) for axis in ("dp", "ctx", "head")]
    if sizes == [4, 2, 4] and tokens.shape[2] == 8 * 2 * HD and tokens.shape[1] % 16 == 0:
        return local_split(*args)
    return local_general(*args)


def solution(mesh):
    in_specs = (
        P("dp", ("ctx", "head"), None),
        P("dp", ("ctx", "head"), None),
        P(("dp", "ctx"), None),
        P(("dp", "ctx"), None),
        P(("dp", "ctx"), None),
        P(("dp", "ctx"), None),
        P(("dp", "ctx")),
        P(("dp", "ctx")),
    )
    out_specs = (
        P("dp", ("ctx", "head"), None),
        P("dp", ("ctx", "head"), None),
        P(("dp", "ctx"), "head"),
        P(("dp", "ctx"), "head"),
        P(("dp", "ctx"), "head"),
        P(("dp", "ctx"), "head"),
        P(("dp", "ctx", "head")),
        P(("dp", "ctx", "head")),
    )
    return jax.shard_map(local, mesh=mesh, in_specs=in_specs, out_specs=out_specs, check_vma=False)
```

```python
import functools
import math

import jax
import jax.numpy as jnp
from jax import lax
from jax.experimental import pallas as pl
from jax.experimental.pallas import tpu as pltpu
from jax.sharding import PartitionSpec as P

HD = 64


EPSILON = 1e-05
ROPE_BASE = 160000.0


def normalize(values):
    centre = jnp.mean(values, axis=-1, keepdims=True)
    shifted = values - centre
    spread = jnp.mean(shifted * shifted, axis=-1, keepdims=True)
    factor = lax.rsqrt(spread + EPSILON)
    return (shifted * factor, factor)


def norm_back(grad_normed, normed, factor):
    grad_centre = jnp.mean(grad_normed, axis=-1, keepdims=True)
    grad_along = jnp.mean(grad_normed * normed, axis=-1, keepdims=True)
    return (grad_normed - grad_centre - normed * grad_along) * factor


def rope_tables(positions, half_size):
    frequency = jnp.exp(
        jnp.arange(half_size, dtype=jnp.float32) * (-math.log(ROPE_BASE) / half_size)
    )
    angles = positions[:, None] * frequency[None, :]
    return (jnp.cos(angles), jnp.sin(angles))


def rotate(values, cosine, sine_table, direction):
    half_size = cosine.shape[-1]
    first_half = values[..., :half_size]
    second_half = values[..., half_size:]
    cos_part = cosine[:, None, :]
    sin_part = sine_table[:, None, :] * direction
    return jnp.concatenate(
        [
            first_half * cos_part - second_half * sin_part,
            second_half * cos_part + first_half * sin_part,
        ],
        axis=-1,
    )


def block_scores(queries4, keys_block, scale):
    keys4 = keys_block.reshape(
        keys_block.shape[0], keys_block.shape[1], queries4.shape[2], queries4.shape[3]
    )
    return (
        jnp.einsum("sqgd,skgd->sgqk", queries4, keys4, preferred_element_type=jnp.float32) * scale
    )


def attend_forward(queries4, keys_all, values_all, key_rows, scale):
    seqs_here, query_rows, groups, head_size = queries4.shape
    turns = keys_all.shape[1] // key_rows

    def statistics(turn, carry):
        row_peak, row_total = carry
        keys_block = lax.dynamic_slice_in_dim(keys_all, turn * key_rows, key_rows, 1)
        scores = block_scores(queries4, keys_block, scale)
        new_peak = jnp.maximum(row_peak, jnp.max(scores, axis=-1))
        row_total = row_total * jnp.exp(row_peak - new_peak) + jnp.sum(
            jnp.exp(scores - new_peak[..., None]), axis=-1
        )
        return (new_peak, row_total)

    start_peak = jnp.full((seqs_here, groups, query_rows), -1e30, jnp.float32)
    row_peak, row_total = lax.fori_loop(
        0, turns, statistics, (start_peak, jnp.zeros_like(start_peak))
    )
    log_total = row_peak + jnp.log(row_total)

    def accumulate(turn, running):
        keys_block = lax.dynamic_slice_in_dim(keys_all, turn * key_rows, key_rows, 1)
        values_block = lax.dynamic_slice_in_dim(values_all, turn * key_rows, key_rows, 1).reshape(
            seqs_here, key_rows, groups, head_size
        )
        weights = jnp.exp(block_scores(queries4, keys_block, scale) - log_total[..., None]).astype(
            jnp.bfloat16
        )
        return running + jnp.einsum(
            "sgqk,skgd->sqgd", weights, values_block, preferred_element_type=jnp.float32
        )

    attended = lax.fori_loop(
        0, turns, accumulate, jnp.zeros((seqs_here, query_rows, groups, head_size), jnp.float32)
    )
    return (attended, log_total)


def attend_backward(queries4, keys_all, values_all, grad_out4, log_total, along, key_rows, scale):
    seqs_here, query_rows, groups, head_size = queries4.shape
    length = keys_all.shape[1]
    width_group = groups * head_size
    turns = length // key_rows

    def step_back(turn, carry):
        grad_queries, grad_keys, grad_values = carry
        keys_block = lax.dynamic_slice_in_dim(keys_all, turn * key_rows, key_rows, 1)
        keys4 = keys_block.reshape(seqs_here, key_rows, groups, head_size)
        values4 = lax.dynamic_slice_in_dim(values_all, turn * key_rows, key_rows, 1).reshape(
            seqs_here, key_rows, groups, head_size
        )
        weights = jnp.exp(block_scores(queries4, keys_block, scale) - log_total[..., None])
        grad_weights = jnp.einsum(
            "sqgd,skgd->sgqk", grad_out4, values4, preferred_element_type=jnp.float32
        )
        grad_scores = (weights * (grad_weights - along[..., None])).astype(jnp.bfloat16)
        grad_queries = grad_queries + jnp.einsum(
            "sgqk,skgd->sqgd", grad_scores, keys4, preferred_element_type=jnp.float32
        )
        key_part = (
            jnp.einsum("sgqk,sqgd->skgd", grad_scores, queries4, preferred_element_type=jnp.float32)
            * scale
        )
        value_part = jnp.einsum(
            "sgqk,sqgd->skgd",
            weights.astype(jnp.bfloat16),
            grad_out4,
            preferred_element_type=jnp.float32,
        )
        grad_keys = lax.dynamic_update_slice_in_dim(
            grad_keys, key_part.reshape(seqs_here, key_rows, width_group), turn * key_rows, 1
        )
        grad_values = lax.dynamic_update_slice_in_dim(
            grad_values, value_part.reshape(seqs_here, key_rows, width_group), turn * key_rows, 1
        )
        return (grad_queries, grad_keys, grad_values)

    start = (
        jnp.zeros((seqs_here, query_rows, groups, head_size), jnp.float32),
        jnp.zeros((seqs_here, length, width_group), jnp.float32),
        jnp.zeros((seqs_here, length, width_group), jnp.float32),
    )
    grad_queries, grad_keys, grad_values = lax.fori_loop(0, turns, step_back, start)
    return (grad_queries * scale, grad_keys, grad_values)


def local_general(tokens, cotangent, w_qkv, w_attn_out, w_in, w_mlp_out, norm_gain1, norm_gain2):
    seqs_here, block_rows, width = tokens.shape
    count_rows = seqs_here * block_rows
    heads_all = width // HD
    head_devices = lax.axis_size("head")
    group_devices = lax.axis_size(("dp", "ctx"))
    groups = heads_all // head_devices
    width_group = groups * HD
    scale = HD ** (-0.5)
    ff_width = w_in.shape[1] // 2
    full_qkv, full_out, full_in, full_mlp, gain_one, gain_two = (
        lax.all_gather(w_qkv, ("dp", "ctx"), axis=0, tiled=True),
        lax.all_gather(w_attn_out, ("dp", "ctx"), axis=0, tiled=True),
        lax.all_gather(w_in, ("dp", "ctx"), axis=0, tiled=True),
        lax.all_gather(w_mlp_out, ("dp", "ctx"), axis=0, tiled=True),
        lax.all_gather(norm_gain1, ("dp", "ctx"), axis=0, tiled=True),
        lax.all_gather(norm_gain2, ("dp", "ctx"), axis=0, tiled=True),
    )
    x_in = tokens.astype(jnp.float32).reshape(count_rows, width)
    normed1, factor1 = normalize(x_in)
    lowered1 = (normed1 * gain_one.astype(jnp.float32)).astype(jnp.bfloat16)
    projected = jnp.dot(lowered1, full_qkv, preferred_element_type=jnp.float32).reshape(
        seqs_here, block_rows, 3, heads_all, HD
    )
    first_pos = (lax.axis_index("ctx") * head_devices + lax.axis_index("head")) * block_rows
    positions = (first_pos + jnp.arange(block_rows, dtype=jnp.int32)).astype(jnp.float32)
    cosine, sine_table = rope_tables(positions, HD // 2)
    queries = (
        rotate(projected[:, :, 0], cosine, sine_table, 1.0)
        .astype(jnp.bfloat16)
        .reshape(seqs_here, block_rows, width)
    )
    keys_local = (
        rotate(projected[:, :, 1], cosine, sine_table, 1.0)
        .astype(jnp.bfloat16)
        .reshape(seqs_here, block_rows, width)
    )
    values_local = projected[:, :, 2].astype(jnp.bfloat16).reshape(seqs_here, block_rows, width)
    queries_h, keys_h, values_h = (
        lax.all_to_all(queries, "head", split_axis=2, concat_axis=1, tiled=True),
        lax.all_to_all(keys_local, "head", split_axis=2, concat_axis=1, tiled=True),
        lax.all_to_all(values_local, "head", split_axis=2, concat_axis=1, tiled=True),
    )
    query_rows = queries_h.shape[1]
    queries4 = queries_h.reshape(seqs_here, query_rows, groups, HD)
    keys_all, values_all = (
        lax.all_gather(keys_h, "ctx", axis=1, tiled=True),
        lax.all_gather(values_h, "ctx", axis=1, tiled=True),
    )
    key_rows = math.gcd(keys_all.shape[1], 1024)
    attended, log_total = attend_forward(queries4, keys_all, values_all, key_rows, scale)
    attended_low = attended.astype(jnp.bfloat16).reshape(seqs_here, query_rows, width_group)
    back_rows = lax.all_to_all(
        attended_low, "head", split_axis=1, concat_axis=2, tiled=True
    ).reshape(count_rows, width)
    residual = x_in + jnp.dot(back_rows, full_out, preferred_element_type=jnp.float32)
    normed2, factor2 = normalize(residual)
    lowered2 = (normed2 * gain_two.astype(jnp.float32)).astype(jnp.bfloat16)
    lifted = jnp.dot(lowered2, full_in, preferred_element_type=jnp.float32)
    first_part = lifted[:, :ff_width]
    second_part = lifted[:, ff_width:]
    activated, gelu_pullback = jax.vjp(
        lambda entries: jax.nn.gelu(entries, approximate=False), first_part
    )
    mixed = (activated * second_part).astype(jnp.bfloat16)
    result = (residual + jnp.dot(mixed, full_mlp, preferred_element_type=jnp.float32)).astype(
        jnp.bfloat16
    )
    full_qkv, full_out, full_in, full_mlp, gain_one, gain_two = (
        lax.all_gather(w_qkv, ("dp", "ctx"), axis=0, tiled=True),
        lax.all_gather(w_attn_out, ("dp", "ctx"), axis=0, tiled=True),
        lax.all_gather(w_in, ("dp", "ctx"), axis=0, tiled=True),
        lax.all_gather(w_mlp_out, ("dp", "ctx"), axis=0, tiled=True),
        lax.all_gather(norm_gain1, ("dp", "ctx"), axis=0, tiled=True),
        lax.all_gather(norm_gain2, ("dp", "ctx"), axis=0, tiled=True),
    )
    keys_all, values_all = (
        lax.all_gather(keys_h, "ctx", axis=1, tiled=True),
        lax.all_gather(values_h, "ctx", axis=1, tiled=True),
    )
    grad_top = cotangent.reshape(count_rows, width)
    grad_mlp = jnp.einsum("nf,nd->fd", mixed, grad_top, preferred_element_type=jnp.float32)
    grad_mixed = jnp.einsum("nd,fd->nf", grad_top, full_mlp, preferred_element_type=jnp.float32)
    grad_first = gelu_pullback(grad_mixed * second_part)[0]
    grad_lifted = jnp.concatenate([grad_first, grad_mixed * activated], axis=-1).astype(
        jnp.bfloat16
    )
    grad_inner = jnp.einsum("nd,nf->df", lowered2, grad_lifted, preferred_element_type=jnp.float32)
    grad_lowered2 = jnp.einsum(
        "nf,df->nd", grad_lifted, full_in, preferred_element_type=jnp.float32
    )
    grad_two = jnp.sum(grad_lowered2 * normed2, axis=0)
    grad_residual = grad_top.astype(jnp.float32) + norm_back(
        grad_lowered2 * gain_two.astype(jnp.float32), normed2, factor2
    )
    grad_branch = grad_residual.astype(jnp.bfloat16)
    grad_outproj = jnp.einsum(
        "nd,ne->de", back_rows, grad_branch, preferred_element_type=jnp.float32
    )
    grad_attended = jnp.einsum(
        "ne,de->nd", grad_branch, full_out, preferred_element_type=jnp.float32
    ).astype(jnp.bfloat16)
    grad_attended_h = lax.all_to_all(
        grad_attended.reshape(seqs_here, block_rows, width),
        "head",
        split_axis=2,
        concat_axis=1,
        tiled=True,
    )
    grad_out4 = grad_attended_h.reshape(seqs_here, query_rows, groups, HD)
    along = jnp.transpose(jnp.sum(grad_out4.astype(jnp.float32) * attended, axis=-1), (0, 2, 1))
    grad_queries, grad_keys_all, grad_values_all = attend_backward(
        queries4, keys_all, values_all, grad_out4, log_total, along, key_rows, scale
    )
    grad_keys_sum, grad_values_sum = (
        lax.psum_scatter(
            grad_keys_all.astype(jnp.bfloat16), "ctx", scatter_dimension=1, tiled=True
        ).astype(jnp.float32),
        lax.psum_scatter(
            grad_values_all.astype(jnp.bfloat16), "ctx", scatter_dimension=1, tiled=True
        ).astype(jnp.float32),
    )
    grad_q_low = grad_queries.astype(jnp.bfloat16).reshape(seqs_here, query_rows, width_group)
    grad_q_tok, grad_k_tok, grad_v_tok = (
        lax.all_to_all(grad_q_low, "head", split_axis=1, concat_axis=2, tiled=True),
        lax.all_to_all(
            grad_keys_sum.astype(jnp.bfloat16), "head", split_axis=1, concat_axis=2, tiled=True
        ),
        lax.all_to_all(
            grad_values_sum.astype(jnp.bfloat16), "head", split_axis=1, concat_axis=2, tiled=True
        ),
    )
    unrot_q = rotate(
        grad_q_tok.astype(jnp.float32).reshape(seqs_here, block_rows, heads_all, HD),
        cosine,
        sine_table,
        -1.0,
    )
    unrot_k = rotate(
        grad_k_tok.astype(jnp.float32).reshape(seqs_here, block_rows, heads_all, HD),
        cosine,
        sine_table,
        -1.0,
    )
    grad_projected = jnp.concatenate(
        [
            unrot_q.reshape(count_rows, width),
            unrot_k.reshape(count_rows, width),
            grad_v_tok.astype(jnp.float32).reshape(count_rows, width),
        ],
        axis=-1,
    ).astype(jnp.bfloat16)
    grad_project = jnp.einsum(
        "nd,nf->df", lowered1, grad_projected, preferred_element_type=jnp.float32
    )
    grad_lowered1 = jnp.einsum(
        "nf,df->nd", grad_projected, full_qkv, preferred_element_type=jnp.float32
    )
    grad_one = jnp.sum(grad_lowered1 * normed1, axis=0)
    grad_input = grad_residual + norm_back(
        grad_lowered1 * gain_one.astype(jnp.float32), normed1, factor1
    )
    pieces_one = grad_one.reshape(group_devices, head_devices, -1)
    pieces_two = grad_two.reshape(group_devices, head_devices, -1)
    part_qkv, part_out, part_in, part_mlp, part_one, part_two = (
        lax.psum_scatter(
            grad_project.astype(jnp.bfloat16), ("dp", "ctx"), scatter_dimension=0, tiled=True
        ).astype(jnp.float32),
        lax.psum_scatter(
            grad_outproj.astype(jnp.bfloat16), ("dp", "ctx"), scatter_dimension=0, tiled=True
        ).astype(jnp.float32),
        lax.psum_scatter(
            grad_inner.astype(jnp.bfloat16), ("dp", "ctx"), scatter_dimension=0, tiled=True
        ).astype(jnp.float32),
        lax.psum_scatter(
            grad_mlp.astype(jnp.bfloat16), ("dp", "ctx"), scatter_dimension=0, tiled=True
        ).astype(jnp.float32),
        lax.psum_scatter(
            pieces_one.astype(jnp.bfloat16), ("dp", "ctx"), scatter_dimension=0, tiled=True
        ).astype(jnp.float32),
        lax.psum_scatter(
            pieces_two.astype(jnp.bfloat16), ("dp", "ctx"), scatter_dimension=0, tiled=True
        ).astype(jnp.float32),
    )
    final_qkv, final_out, final_in, final_mlp, final_one, final_two = (
        lax.psum_scatter(
            part_qkv.astype(jnp.bfloat16), "head", scatter_dimension=1, tiled=True
        ).astype(jnp.float32),
        lax.psum_scatter(
            part_out.astype(jnp.bfloat16), "head", scatter_dimension=1, tiled=True
        ).astype(jnp.float32),
        lax.psum_scatter(
            part_in.astype(jnp.bfloat16), "head", scatter_dimension=1, tiled=True
        ).astype(jnp.float32),
        lax.psum_scatter(
            part_mlp.astype(jnp.bfloat16), "head", scatter_dimension=1, tiled=True
        ).astype(jnp.float32),
        lax.psum_scatter(
            part_one.astype(jnp.bfloat16), "head", scatter_dimension=1, tiled=True
        ).astype(jnp.float32),
        lax.psum_scatter(
            part_two.astype(jnp.bfloat16), "head", scatter_dimension=1, tiled=True
        ).astype(jnp.float32),
    )
    return (
        result.reshape(seqs_here, block_rows, width),
        grad_input.reshape(seqs_here, block_rows, width),
        final_qkv,
        final_out,
        final_in,
        final_mlp,
        final_one.reshape(-1),
        final_two.reshape(-1),
    )


F32 = jnp.float32
BF16 = jnp.bfloat16
GROUP = ("ctx", "head")


def dot(left, right, dims=((1,), (0,))):
    return lax.dot_general(left, right, (dims, ((), ())), preferred_element_type=F32)


def wide(values):
    return values.astype(F32)


def flat(values):
    return values.reshape(-1, values.shape[-1])


def lane_rotate(values, cosine, sine_signed):
    lane = lax.broadcasted_iota(jnp.int32, values.shape, 1)
    width = values.shape[1]
    partner = jnp.where(
        lane % HD < HD // 2,
        pltpu.roll(values, width - HD // 2, 1),
        pltpu.roll(values, HD // 2, 1),
    )
    return values * cosine + partner * sine_signed


def head_masks(shape):
    lane = lax.broadcasted_iota(jnp.int32, shape, 1)
    return [lane // HD == head for head in range(shape[1] // HD)]


def params(mebibytes):
    return pltpu.CompilerParams(vmem_limit_bytes=mebibytes * 1024 * 1024)


COST = pl.CostEstimate(flops=1 << 20, transcendentals=0, bytes_accessed=1 << 16)


def whole(array):
    return pl.BlockSpec(array.shape, lambda *_: (0,) * len(array.shape))


SCALARS = pl.BlockSpec(memory_space=pltpu.SMEM)


def project_kernel(place_ref, *refs):
    pieces, weights = refs[:6], refs[6:10]
    cos_ref, sin_ref, low_ref, qkv_ref, w_ref, gain1_ref, gain2_ref, rows_ref = refs[10:]
    block, part = pieces[0].shape[2], w_ref.shape[1] // 3
    rows = gain1_ref.shape[1] // 8

    @pl.when(pl.program_id(0) == 0)
    def _():
        for step, piece in enumerate(weights):
            for turn in range(2):
                at = 2 * (place_ref[8] ^ step) + (place_ref[9] ^ turn)
                w_ref[pl.ds(pl.multiple_of(at * rows, rows), rows), :] = piece[turn, :rows]
                gains = piece[turn, rows:].astype(F32)
                rows_ref[0, pl.ds(at, 1), :] = gains[:1, :rows]
                rows_ref[1, pl.ds(at, 1), :] = gains[1:2, :rows]
        for out, at in ((gain1_ref, 0), (gain2_ref, 1)):
            for row in range(8):
                out[:, row * rows : (row + 1) * rows] = rows_ref[at, row : row + 1, :]

    gain = gain1_ref[...]
    index = 0
    for piece in pieces:
        for inner in range(piece.shape[0]):
            normed, _ = normalize(piece[inner, 0].astype(F32))
            low_ref[index, 0] = (normed * gain).astype(BF16)
            index += 1
    projected = dot(flat(low_ref[:, 0]), w_ref[...])
    cosine, sine = cos_ref[...], sin_ref[...]
    shape = (8, block, part)
    qkv_ref[:, 0, :, :part] = (
        (lane_rotate(projected[:, :part], cosine, sine) * HD**-0.5).astype(BF16).reshape(shape)
    )
    qkv_ref[:, 0, :, part : 2 * part] = (
        lane_rotate(projected[:, part : 2 * part], cosine, sine).astype(BF16).reshape(shape)
    )
    qkv_ref[:, 0, :, 2 * part :] = projected[:, 2 * part :].astype(BF16).reshape(shape)


def project(place, pieces, weights, cosine, sine):
    seqs, block, width = pieces[0].shape[1:]
    own = weights[0].shape[2]

    def by_seq(lead, last):
        return pl.BlockSpec((lead, 1, block, last), lambda s: (0, s, 0, 0))

    return pl.pallas_call(
        project_kernel,
        grid=(seqs,),
        in_specs=[SCALARS]
        + [by_seq(piece.shape[0], width) for piece in pieces]
        + [whole(w) for w in weights]
        + [whole(cosine), whole(sine)],
        out_specs=(
            by_seq(8, width),
            by_seq(8, own),
            pl.BlockSpec((width, own), lambda s: (0, 0)),
            pl.BlockSpec((1, width), lambda s: (0, 0)),
            pl.BlockSpec((1, width), lambda s: (0, 0)),
        ),
        out_shape=(
            jax.ShapeDtypeStruct((8, seqs, block, width), BF16),
            jax.ShapeDtypeStruct((8, seqs, block, own), BF16),
            jax.ShapeDtypeStruct((width, own), BF16),
            jax.ShapeDtypeStruct((1, width), F32),
            jax.ShapeDtypeStruct((1, width), F32),
        ),
        scratch_shapes=[pltpu.VMEM((2, 8, width // 8), F32)],
        compiler_params=params(60),
        cost_estimate=COST,
        name="project",
    )(place, *pieces, *weights, cosine, sine)


def attend_kernel(place_ref, q_ref, k_ref, v_ref, *refs):
    att_ref, log_ref, home_ref = refs[-3:]
    step, seq = pl.program_id(0), len(refs) - 3
    if seq:

        @pl.when(step == 0)
        def _():
            home_ref[:, :1] = refs[0][...]

    queries, keys, values = flat(q_ref[...]), flat(k_ref[...]), flat(v_ref[...])
    attended = jnp.zeros(queries.shape, F32)
    logs = jnp.zeros(queries.shape, F32)
    for mask in head_masks(queries.shape):
        scores = dot(jnp.where(mask, queries, 0), keys, ((1,), (1,)))
        peak = jnp.max(scores, axis=1, keepdims=True)
        weights = jnp.exp(scores - peak)
        total = jnp.sum(weights, axis=1, keepdims=True)
        mixed = dot(weights.astype(BF16), values) * (1.0 / total)
        attended = jnp.where(mask, mixed, attended)
        logs = jnp.where(mask, peak + jnp.log(total), logs)
    att_ref[...] = attended.reshape(att_ref.shape)
    log_ref[...] = logs.reshape(log_ref.shape)
    low = attended.astype(BF16).reshape(att_ref.shape)
    for inner in range(2):
        home_ref[place_ref[2 * step + inner], seq] = low[inner, 0]


def attend(place, qkv, *home):
    _, _, block, own = qkv.shape
    part, seq = own // 3, len(home)
    rows = pl.BlockSpec((2, 1, block, part), lambda i: (i, 0, 0, 0))
    shape = (8, 1, block, part)
    return pl.pallas_call(
        attend_kernel,
        grid=(4,),
        in_specs=[
            SCALARS,
            pl.BlockSpec((2, 1, block, part), lambda i: (i, seq, 0, 0)),
            pl.BlockSpec((8, 1, block, part), lambda i: (0, seq, 0, 1)),
            pl.BlockSpec((8, 1, block, part), lambda i: (0, seq, 0, 2)),
            *[whole(h) for h in home],
        ],
        out_specs=(
            rows,
            rows,
            pl.BlockSpec((8, 1 + seq, block, part), lambda i: (0, 0, 0, 0)),
        ),
        out_shape=(
            jax.ShapeDtypeStruct(shape, F32),
            jax.ShapeDtypeStruct(shape, F32),
            jax.ShapeDtypeStruct((8, 1 + seq, block, part), BF16),
        ),
        compiler_params=params(24),
        cost_estimate=COST,
        name="attend",
    )(place, qkv, qkv, qkv, *home)


def branch_kernel(place_ref, *refs):
    pieces = refs[:6]
    rows_ref, tokens_ref, gain_ref, residual_ref, low_ref, side_ref, total_ref = refs[6:]
    heads = rows_ref.shape[0] // 2
    for c in range(2):
        side_ref[c] = jnp.concatenate([flat(rows_ref[c * heads + d]) for d in range(heads)], axis=1)
    total_ref[...] = flat(wide(tokens_ref[...]))
    index = 0
    for piece in pieces:
        n = piece.shape[2]
        for inner in range(piece.shape[0]):
            at = place_ref[index]
            columns = pl.ds(pl.multiple_of((at % heads) * n, n), n)
            total_ref[:, columns] += dot(side_ref[at // heads], piece[inner])
            index += 1
    total = total_ref[...]
    normed, _ = normalize(total)
    residual_ref[...] = total.reshape(residual_ref.shape)
    low_ref[...] = (normed * gain_ref[...]).astype(BF16).reshape(low_ref.shape)


def branch(place, pieces, rows, tokens, gain):
    args = (*pieces, rows, tokens, gain)
    seqs, block, width = tokens.shape
    return pl.pallas_call(
        branch_kernel,
        in_specs=[SCALARS] + [whole(a) for a in args],
        out_shape=(
            jax.ShapeDtypeStruct(tokens.shape, F32),
            jax.ShapeDtypeStruct(tokens.shape, BF16),
        ),
        scratch_shapes=[
            pltpu.VMEM((2, seqs * block, pieces[0].shape[1]), BF16),
            pltpu.VMEM((seqs * block, width), F32),
        ],
        compiler_params=params(16),
        cost_estimate=COST,
        name="branch",
    )(place, *args)


def combine(*groups, mebibytes=16):
    parts = [part for group in groups for _, parts in group for part in parts]
    rows = sum(count for count, _ in groups[0])
    width = parts[0][0].shape[2]

    def kernel(*refs):
        at = 0
        for k, group in enumerate(groups):
            row = 0
            for count, terms in group:
                total = 0.0
                for _, _, start in terms:
                    total = total + wide(refs[at][0, start : start + count])
                    at += 1
                refs[-1][k, row : row + count] = total.astype(BF16)
                row += count

    return pl.pallas_call(
        kernel,
        grid=(1,),
        in_specs=[
            pl.BlockSpec((1, *array.shape[1:]), lambda *_, index=index: (index, 0, 0))
            for array, index, _ in parts
        ],
        out_specs=pl.BlockSpec((len(groups), rows, width), lambda *_: (0, 0, 0)),
        out_shape=jax.ShapeDtypeStruct((len(groups), rows, width), BF16),
        compiler_params=params(mebibytes),
        cost_estimate=COST,
        name="combine",
    )(*[array for array, _, _ in parts])


def mlp_kernel(*refs, count, ends):
    pieces, tops = refs[:count], refs[count : 2 * count]
    w_ref, out_w_ref = refs[2 * count : 2 * count + 2]
    low_ref, top_ref, mixed_ref, lifted_ref, *out_refs = refs[-4 - len(ends) :]
    step = pl.program_id(0)
    start = 0
    for piece, top in zip(pieces, tops):

        @pl.when((step >= start) & (step < start + piece.shape[0]))
        def _(piece=piece, top=top, start=start):
            low_ref[0] = piece[step - start]
            top_ref[0] = top[step - start]

        start += piece.shape[0]

    hidden = w_ref.shape[1] // 2
    lifted = dot(flat(low_ref[...]), w_ref[...])
    first, second = lifted[:, :hidden], lifted[:, hidden:]
    grad_mixed = dot(flat(top_ref[...]), out_w_ref[...], ((1,), (1,)))
    gate = 0.5 * (1.0 + lax.erf(first * (0.5**0.5)))
    slope = gate + first * jnp.exp(first * first * -0.5) * ((2.0 * math.pi) ** -0.5)
    activated = first * gate
    mixed_ref[...] = (activated * second).astype(BF16).reshape(mixed_ref.shape)
    grad = jnp.concatenate(
        [(grad_mixed * second * slope).astype(BF16), (grad_mixed * activated).astype(BF16)],
        axis=1,
    )
    lifted_ref[...] = grad.reshape(lifted_ref.shape)
    partial = dot(grad, w_ref[...], ((1,), (1,))).astype(BF16).reshape(low_ref.shape)
    start = 0
    for out, end in zip(out_refs, ends):

        @pl.when((step >= start) & (step < end))
        def _(out=out):
            out[...] = partial

        start = end


def mlp(pieces, tops, w, out_w, base, ends, earlier=()):
    seqs, block, width = pieces[0].shape[1:]
    hidden = w.shape[1] // 2
    whole_in = (*pieces, *tops, w, out_w)

    def rows(last):
        return pl.BlockSpec((1, seqs, block, last), lambda i: (i + base, 0, 0, 0))

    def within(start, end):
        return pl.BlockSpec(
            (1, seqs, block, width),
            lambda i: (jnp.clip(i - start, 0, end - start - 1), 0, 0, 0),
        )

    starts = (0, *ends[:-1])
    lasts = (width, width, hidden, 2 * hidden)
    return pl.pallas_call(
        functools.partial(mlp_kernel, count=len(pieces), ends=ends),
        grid=(ends[-1],),
        in_specs=[whole(array) for array in whole_in]
        + [pl.BlockSpec(memory_space=pl.ANY)] * len(earlier),
        out_specs=(
            *[rows(last) for last in lasts],
            *[within(start, end) for start, end in zip(starts, ends)],
        ),
        out_shape=(
            *[jax.ShapeDtypeStruct((8, seqs, block, last), BF16) for last in lasts],
            *[
                jax.ShapeDtypeStruct((end - start, seqs, block, width), BF16)
                for start, end in zip(starts, ends)
            ],
        ),
        input_output_aliases={len(whole_in) + at: at for at in range(len(earlier))},
        compiler_params=params(32),
        cost_estimate=COST,
        name="mlp",
    )(*whole_in, *earlier)


def out_grad_kernel(place_ref, rows_ref, grad_ref, keep_ref, send_ref):
    grads = flat(grad_ref[...])
    for index in range(8):
        part = dot(flat(rows_ref[place_ref[index]]), grads, ((0,), (0,))).astype(BF16)
        if index < 5:
            keep_ref[index] = part
        else:
            send_ref[index - 5] = part


def out_grad(place, rows, grads):
    part, width = rows.shape[-1], grads.shape[-1]
    return pl.pallas_call(
        out_grad_kernel,
        in_specs=[SCALARS, whole(rows), whole(grads)],
        out_shape=(
            jax.ShapeDtypeStruct((5, part, width), BF16),
            jax.ShapeDtypeStruct((3, part, width), BF16),
        ),
        compiler_params=params(16),
        cost_estimate=COST,
        name="out_grad",
    )(place, rows, grads)


def branch_back_kernel(place_ref, *refs):
    pieces = refs[:6]
    keep_ref, near_ref, own_ref, residual_ref, top_ref, gain_ref = refs[6:12]
    grad_ref, branch_ref, home_ref, sum_ref, low_ref, side_ref = refs[12:]
    grad_low = wide(flat(keep_ref[...])) + wide(flat(near_ref[...])) + wide(flat(own_ref[...]))
    normed, factor = normalize(flat(residual_ref[...]))
    sum_ref[...] = jnp.sum(grad_low * normed, axis=0, keepdims=True)
    grad = flat(wide(top_ref[...])) + norm_back(grad_low * gain_ref[...], normed, factor)
    grad_ref[...] = grad.reshape(grad_ref.shape)
    low_ref[...] = grad.astype(BF16)
    branch_ref[...] = low_ref[...].reshape(branch_ref.shape)
    heads = home_ref.shape[0] // 2
    side_ref[...] = jnp.zeros_like(side_ref)
    index = 0
    for piece in pieces:
        n = piece.shape[2]
        for inner in range(piece.shape[0]):
            at = place_ref[index]
            columns = pl.ds(pl.multiple_of((at % heads) * n, n), n)
            side_ref[at // heads] += dot(low_ref[:, columns], piece[inner], ((1,), (1,)))
            index += 1
    part = home_ref.shape[3]
    for c in range(2):
        for d in range(heads):
            home = side_ref[c, :, d * part : (d + 1) * part].astype(BF16)
            home_ref[c * heads + d] = home.reshape(home_ref.shape[1:])


def branch_back(place, pieces, keep, near, own, residual, top, gain):
    args = (*pieces, keep, near, own, residual, top, gain)
    seqs, block, width = residual.shape
    tall = pieces[0].shape[1]
    shapes = (
        jax.ShapeDtypeStruct(residual.shape, F32),
        jax.ShapeDtypeStruct(residual.shape, BF16),
        jax.ShapeDtypeStruct((8, seqs, block, tall // 4), BF16),
        jax.ShapeDtypeStruct((1, width), F32),
    )
    return pl.pallas_call(
        branch_back_kernel,
        grid=(1,),
        in_specs=[SCALARS]
        + [whole(piece) for piece in pieces]
        + [pl.BlockSpec((1, seqs * block, width), lambda *_: (0, 0, 0))] * 2
        + [whole(a) for a in args[8:]],
        out_specs=tuple(whole(shape) for shape in shapes),
        out_shape=shapes,
        scratch_shapes=[
            pltpu.VMEM((seqs * block, width), BF16),
            pltpu.VMEM((2, seqs * block, tall), F32),
        ],
        compiler_params=params(24),
        cost_estimate=COST,
        name="branch_back",
    )(place, *args)


def attend_back_kernel(
    place_ref, q_ref, k_ref, v_ref, grad_ref, att_ref, log_ref, cosq_ref, sinq_ref, cos_ref,
    sin_ref, w_ref, low_ref, *refs, seq, last,
):
    if last:
        before_ref, gain1_ref, gain2_ref, keep_ref, send_ref, grad_w_ref, *scratch = refs
    else:
        keep_ref, send_ref, before_ref, *scratch = refs
    proj_ref, sum_k, sum_v = scratch
    step = pl.program_id(0)
    block, part = q_ref.shape[2], q_ref.shape[3]

    @pl.when(step == 0)
    def _():
        sum_k[...] = jnp.zeros_like(sum_k)
        sum_v[...] = jnp.zeros_like(sum_v)

    queries, keys, values = flat(q_ref[...]), flat(k_ref[...]), flat(v_ref[...])
    grads = jnp.concatenate([grad_ref[place_ref[2 * step + inner], seq] for inner in range(2)])
    along = (grads.astype(F32) * flat(att_ref[...])).T
    logs = flat(log_ref[...]).T
    grad_queries = jnp.zeros(queries.shape, F32)
    for head, mask in enumerate(head_masks(queries.shape)):
        own_q = jnp.where(mask, queries, 0)
        own_g = jnp.where(mask, grads, 0)
        scores = dot(keys, own_q, ((1,), (1,)))
        weights = jnp.exp(scores - logs[head * HD : head * HD + 1])
        lifted = dot(values, own_g, ((1,), (1,)))
        row = jnp.sum(along[head * HD : (head + 1) * HD], axis=0, keepdims=True)
        grad_scores = (weights * (lifted - row)).astype(BF16)
        sum_k[...] += dot(grad_scores, own_q)
        sum_v[...] += dot(weights.astype(BF16), own_g)
        grad_queries = jnp.where(mask, dot(grad_scores, keys, ((0,), (0,))), grad_queries)
    grad_queries = lane_rotate(grad_queries * HD**-0.5, cosq_ref[...], -sinq_ref[...])
    rows = pl.multiple_of(step * 2 * block, 2 * block)
    proj_ref[pl.ds(rows, 2 * block), :part] = grad_queries.astype(BF16)

    @pl.when(step == 3)
    def _():
        grad_keys = lane_rotate(sum_k[...], cos_ref[...], -sin_ref[...])
        proj_ref[:, part : 2 * part] = grad_keys.astype(BF16)
        proj_ref[:, 2 * part :] = sum_v[...].astype(BF16)
        partial = dot(proj_ref[...], w_ref[...], ((1,), (1,))).astype(BF16)
        keep_ref[...] = partial[: 5 * block].reshape(5, block, -1)
        send_ref[...] = partial[5 * block :].reshape(3, block, -1)
        grad_w = dot(proj_ref[...], flat(low_ref[...]), ((0,), (0,)))
        if last:
            grad_w = (grad_w + before_ref[...]).T
            along_w = jnp.sum(grad_w * wide(w_ref[...]), axis=1, keepdims=True)
            along_w = jnp.broadcast_to(along_w, (w_ref.shape[0], 128)).T[:1] / gain1_ref[...]
            row = lax.broadcasted_iota(jnp.int32, (GAIN_ROWS, w_ref.shape[0]), 0)
            gains = jnp.where(row == 0, along_w, jnp.where(row == 1, gain2_ref[...], 0.0))
            n = grad_w_ref.shape[1] - GAIN_ROWS
            for at in range(grad_w_ref.shape[0]):
                part_rows = slice(at * n, (at + 1) * n)
                grad_w_ref[at, :n] = grad_w[part_rows].astype(BF16)
                grad_w_ref[at, n:, :n] = gains[:, part_rows].astype(BF16)
                rest = grad_w_ref.shape[2] - n
                grad_w_ref[at, n:, n:] = jnp.zeros((GAIN_ROWS, rest), BF16)
        else:
            before_ref[...] = grad_w


GAIN_ROWS = 16


def attend_back(place, qkv, grads, attended, logs, cosine, sine, w, low, seq, *before, dp=1):
    _, _, block, own = qkv.shape
    part, width = own // 3, w.shape[0]
    last = len(before) > 0
    rows = pl.BlockSpec((2, 1, block, part), lambda i: (i, 0, 0, 0))
    angles = pl.BlockSpec((2 * block, part), lambda i: (i, 0))

    def full(*shape):
        return pl.BlockSpec(shape, lambda i: (0,) * len(shape))

    args = [place, qkv, qkv, qkv, grads, attended, logs, cosine, sine, cosine, sine, w, low]
    in_specs = [
        SCALARS,
        pl.BlockSpec((2, 1, block, part), lambda i: (i, seq, 0, 0)),
        pl.BlockSpec((8, 1, block, part), lambda i: (0, seq, 0, 1)),
        pl.BlockSpec((8, 1, block, part), lambda i: (0, seq, 0, 2)),
        whole(grads),
        rows,
        rows,
        angles,
        angles,
        whole(cosine),
        whole(sine),
        whole(w),
        pl.BlockSpec((8, 1, block, width), lambda i: (0, seq, 0, 0)),
    ]
    shapes = [((5, block, width), BF16), ((3, block, width), BF16)]
    if last:
        args += before
        in_specs += [whole(array) for array in before]
        shapes += [((dp, width // dp + GAIN_ROWS, own), BF16)]
    else:
        shapes += [((own, width), F32)]
    return pl.pallas_call(
        functools.partial(attend_back_kernel, seq=seq, last=last),
        grid=(4,),
        in_specs=in_specs,
        out_specs=tuple(full(*shape) for shape, _ in shapes),
        out_shape=tuple(jax.ShapeDtypeStruct(shape, kind) for shape, kind in shapes),
        scratch_shapes=[
            pltpu.VMEM((8 * block, own), BF16),
            pltpu.VMEM((8 * block, part), F32),
            pltpu.VMEM((8 * block, part), F32),
        ],
        compiler_params=params(60),
        cost_estimate=COST,
        name="attend_back",
    )(*args)


def input_grad_kernel(*refs):
    keeps, (near_ref, own_ref, tokens_ref, residual_ref, gain_ref, out_ref) = refs[:-6], refs[-6:]
    block = tokens_ref.shape[1]
    for seq, keep in enumerate(keeps):
        rows = slice(seq * block, (seq + 1) * block)
        grad = wide(keep[0, :block]) + wide(near_ref[0, rows]) + wide(own_ref[0, rows])
        normed, factor = normalize(wide(tokens_ref[seq]))
        out_ref[seq] = residual_ref[seq] + norm_back(grad * gain_ref[...], normed, factor)


def input_grad(keeps, near, own, tokens, residual, gain):
    rest = (own, tokens, residual, gain)
    return pl.pallas_call(
        input_grad_kernel,
        grid=(1,),
        in_specs=[
            pl.BlockSpec((1, *array.shape[1:]), lambda *_: (0, 0, 0)) for array in (*keeps, near)
        ]
        + [whole(array) for array in rest],
        out_specs=whole(residual),
        out_shape=jax.ShapeDtypeStruct(residual.shape, F32),
        compiler_params=params(16),
        cost_estimate=COST,
        name="input_grad",
    )(*keeps, near, *rest)


def finish_kernel(keep_ref, rows_ref, near_ref, home_ref, residual_ref, out_ref, grad_ref):
    rows = keep_ref.shape[1]
    total = wide(keep_ref[0]) + wide(near_ref[0, :rows]) + wide(home_ref[0, :rows])
    out_ref[...] = (residual_ref[...] + total.reshape(residual_ref.shape)).astype(BF16)
    total = wide(rows_ref[0]) + wide(near_ref[0, rows:]) + wide(home_ref[0, rows:])
    n = grad_ref.shape[2]
    for at in range(grad_ref.shape[0]):
        grad_ref[at] = total[:, at * n : (at + 1) * n].astype(BF16)


def finish(keep, rows, near, home, residual, dp):
    args = (keep, rows, near, home)
    shapes = (
        jax.ShapeDtypeStruct(residual.shape, BF16),
        jax.ShapeDtypeStruct((dp, rows.shape[1], rows.shape[2] // dp), BF16),
    )
    return pl.pallas_call(
        finish_kernel,
        grid=(1,),
        in_specs=[pl.BlockSpec((1, *array.shape[1:]), lambda *_: (0, 0, 0)) for array in args]
        + [whole(residual)],
        out_specs=tuple(whole(shape) for shape in shapes),
        out_shape=shapes,
        compiler_params=params(16),
        cost_estimate=COST,
        name="finish",
    )(*args, residual)


class Group:
    def __init__(self):
        self.heads = lax.axis_size("head")
        self.dp = lax.axis_size("dp")
        self.ctx_at = lax.axis_index("ctx")
        self.head_at = lax.axis_index("head")
        self.dp_at = lax.axis_index("dp")
        self.at = self.ctx_at * self.heads + self.head_at
        near, far = [], []
        for c in range(2):
            for h in range(self.heads):
                x, y = (c ^ 1) * self.heads + h, c * self.heads + (h ^ 2)
                near.append((c * self.heads + h, x if h % 2 == 0 else y))
                far.append((c * self.heads + h, y if h % 2 == 0 else x))
        self.near, self.far = near, far

    def order(self):
        first = jnp.where(self.head_at % 2 == 0, 4, 2)
        second = 6 - first
        return jnp.stack(
            [self.at ^ bits for bits in (0, 1, first, first ^ 1, 6, second ^ 1, second, 7)]
        )

    def swap(self, values, bit):
        if bit == 4:
            return lax.ppermute(values, "ctx", [(0, 1), (1, 0)])
        return lax.ppermute(values, "head", [(i, i ^ bit) for i in range(self.heads)])

    def mate(self, values):
        return self.swap(values, 1)

    def to_near(self, values):
        return lax.ppermute(values, GROUP, self.near)

    def to_far(self, values):
        return lax.ppermute(values, GROUP, self.far)

    def rows_back(self, values, place):
        pairs, same = [], False
        for d in range(self.dp):
            for h in range(self.heads):
                if (d, h) == (place[h], d):
                    same = same | ((self.dp_at == d) & (self.head_at == h))
                else:
                    pairs.append((d * self.heads + h, place[h] * self.heads + d))
        return jnp.where(same, values, lax.ppermute(values, ("dp", "head"), pairs))

    def across(self, values, step):
        return lax.ppermute(values, "dp", [(i, i ^ step) for i in range(self.dp)])


def pick(array, index, axis):
    return lax.dynamic_index_in_dim(array, index, axis, keepdims=False)


def after(values, *earlier):
    return lax.optimization_barrier((values, earlier))[0]


def local_split(tokens, cotangent, w_qkv, w_attn_out, w_in, w_mlp_out, norm_gain1, norm_gain2):
    seqs, block, width = tokens.shape
    group = Group()
    heads, dp = group.heads, group.dp
    at_c, at_h = group.ctx_at, group.head_at
    parts = 2 * heads
    hidden = w_in.shape[1] // 2 // parts
    padded = -(-hidden // 128) * 128
    own_width = width // parts
    half = heads // 2
    rows_here = w_qkv.shape[0]
    place = [2 * (h % half) + h // half for h in range(heads)]
    straight = list(range(heads))
    order = group.order()
    scalars = jnp.concatenate([order, jnp.stack([group.dp_at, at_c])]).astype(jnp.int32)
    mate, near, far = group.mate, group.to_near, group.to_far

    def in_order(own, other):
        return jnp.where(at_c == 0, jnp.stack([own, other]), jnp.stack([other, own]))

    def exchange(values):
        return lax.all_to_all(values, GROUP, split_axis=0, concat_axis=0, tiled=True)


    gains = jnp.pad(
        jnp.stack([norm_gain1, norm_gain2]), ((0, 14), (0, 3 * own_width - rows_here))
    )
    qkv_view = w_qkv.reshape(rows_here, 3, width)

    def qkv_part(at):
        start = (2 * at_h + at) * own_width
        cut = lax.dynamic_slice_in_dim(qkv_view, start, own_width, 2)
        return jnp.concatenate([cut.reshape(rows_here, 3 * own_width), gains])

    x_own = tokens[None]
    x_mate = mate(x_own)
    qkv_other, qkv_own = qkv_part(1 - at_c), qkv_part(at_c)
    qkv_cross = group.swap(after(qkv_other, x_own), 4)
    in_view = after(w_in, qkv_other).reshape(rows_here, 2, heads, 2, hidden)
    in_view = pick(in_view, 2 * (at_h % half) + at_h // half, 2)

    def in_part(at):
        cut = pick(in_view, at, 2)
        return jnp.pad(cut, ((0, 0), (0, 0), (0, padded - hidden))).reshape(rows_here, 2 * padded)

    in_other, in_own = in_part(1 - at_c), in_part(at_c)
    in_cross = group.swap(after(in_other, qkv_cross), 4)
    x_chip = jnp.concatenate([x_own, after(x_mate, qkv_cross, qkv_own)])
    x_near = near(x_chip)
    qkv_pair = jnp.stack([qkv_own, qkv_cross])
    qkv_pieces = [qkv_pair] + [group.across(qkv_pair, step) for step in range(1, dp)]

    positions = after(order, qkv_pair)[:, None] * block + jnp.arange(block, dtype=jnp.int32)
    lane = jnp.arange(own_width, dtype=jnp.int32)
    frequency = jnp.exp(
        (lane % (HD // 2)).astype(F32) * (-math.log(ROPE_BASE) / (HD // 2))
    )
    angles = wide(positions.reshape(-1))[:, None] * frequency[None, :]
    cosine = jnp.cos(angles)
    sine = jnp.sin(angles) * jnp.where(lane % HD < HD // 2, -1.0, 1.0)[None, :]

    x_far = far(x_near[:1])
    slices = jnp.concatenate([w_attn_out, w_mlp_out])
    slices = after(slices, x_far, in_other, in_own, cosine, sine, *qkv_pieces)
    slices = lax.dynamic_slice_in_dim(slices, at_h * (width // heads), width // heads, 1)
    slices = jnp.pad(slices, ((0, 64), (0, 0)))
    slices = lax.all_gather(slices, "dp", axis=0)
    x_near = after(x_near, *qkv_pieces, cosine, sine, in_cross, in_own)
    x_near_mate = mate(x_near)
    cot_own = after(cotangent, x_near)[None]
    cot_mate = mate(cot_own)
    in_pair, x_far = lax.optimization_barrier((in_order(in_own, in_cross), x_far))
    weight_in = lax.all_gather(in_pair, "dp", axis=0).reshape(width, -1)
    cot_chip = jnp.concatenate([cot_own, cot_mate])
    x_far = after(x_far, cot_chip)
    x_far_mate = mate(x_far)

    cot_near = near(after(cot_chip, x_far))
    out_rows = w_attn_out.shape[0]
    x_pieces = (x_own, x_mate, x_near, x_far, x_near_mate, x_far_mate)
    low1, qkv, weight_qkv, gain_one, gain_two = project(
        scalars, x_pieces, qkv_pieces, cosine, sine
    )

    slices = after(slices, qkv)
    out_own = slices[:, :out_rows].reshape(1, dp * out_rows, -1)
    out_mate = mate(out_own)
    mlp_slices = jnp.stack(
        [slices[place[h], out_rows : out_rows + hidden] for h in range(heads)]
    )
    mlp_slices = lax.all_to_all(mlp_slices, "head", split_axis=0, concat_axis=0, tiled=True)
    out_near = near(jnp.concatenate([out_own, out_mate]))
    att_0, log_0, home_0 = attend(scalars, after(qkv, out_mate))
    cot_near = after(cot_near, home_0)
    cot_far, cot_near_mate = far(cot_near[:1]), mate(cot_near)
    out_near = after(out_near, home_0)
    out_far, out_near_mate = far(out_near[:1]), mate(out_near)
    att_1, log_1, home = attend(scalars, after(qkv, cot_near, out_near), home_0)
    home, cot_far, out_far = lax.optimization_barrier((home, cot_far, out_far))
    att_rows = exchange(home)
    out_far_mate, cot_far_mate = mate(after(out_far, home)), mate(after(cot_far, home))
    out_pieces = (out_own, out_mate, out_near, out_far, out_near_mate, out_far_mate)
    weight_mlp = jnp.moveaxis(after(mlp_slices, home), 0, 1).reshape(hidden, width)
    weight_mlp = jnp.pad(weight_mlp, ((0, padded - hidden), (0, 0)))
    residual, low2 = branch(
        scalars, out_pieces, after(att_rows, cot_far_mate, weight_mlp, weight_in), tokens, gain_two
    )

    low_own = low2[None]
    low_mate = mate(low_own)
    low_near = near(jnp.concatenate([low_own, low_mate]))
    *arrays, keep_a = mlp(
        (low_own, low_mate), (cot_own, cot_mate), weight_in, weight_mlp, 0, (2,)
    )
    low_near = after(low_near, keep_a)
    low_far, low_near_mate = far(low_near[:1]), mate(low_near)
    *arrays, keep_b = mlp((low_near,), (cot_near,), weight_in, weight_mlp, 2, (2,), arrays)
    low_far_mate = mate(after(low_far, keep_b))
    low2_all, cot_all, mixed, grad_lifted, keep_c, send = mlp(
        (low_far, low_near_mate, low_far_mate),
        (cot_far, cot_near_mate, cot_far_mate),
        weight_in,
        weight_mlp,
        4,
        (1, 4),
        arrays,
    )

    def over_tokens(left, right):
        return dot(flat(left), flat(right), ((0,), (0,)))

    def scatter(values):
        return lax.psum_scatter(values.astype(BF16), "dp", scatter_dimension=0, tiled=True)

    def columns_first(values):
        return jnp.moveaxis(values.reshape(values.shape[0], dp, -1), 1, 0)

    rows = seqs * block

    def by_rows(values):
        return values.reshape(values.shape[0], -1, width)

    keep_a, keep_b, keep_c, send = (by_rows(array) for array in (keep_a, keep_b, keep_c, send))
    met = mate(send)
    last = combine([(rows, [(keep_c, 0, 0), (met, 2, 0)])])
    last_far = far(last)
    grad_mlp = columns_first(over_tokens(after(mixed, last), cot_all)[:hidden]).astype(BF16)
    last_far = after(last_far, grad_mlp)
    grad_mlp = scatter(grad_mlp)[0]
    chip = combine(
        [(rows, [(keep_b, 0, 0), (met, 0, 0), (last_far, 0, 0)])],
        [(rows, [(keep_b, 1, 0), (met, 1, 0)])],
    )
    chip_near = near(chip)
    grad_in = over_tokens(low2_all, after(grad_lifted, chip)).astype(BF16)
    cut = 5 * rows
    mixed_flat = flat(after(mixed, chip))
    out_keep = dot(mixed_flat[:cut], weight_mlp).astype(BF16).reshape(5, rows, width)
    out_send = dot(mixed_flat[cut:], weight_mlp).astype(BF16).reshape(3, rows, width)
    chip_near = after(chip_near, grad_in, out_keep, out_send)
    grad_in = scatter(grad_in)
    home = mate(combine([(rows, [(keep_a, 1, 0), (chip_near, 1, 0)])])[0])
    out_met = mate(after(out_send, chip_near))
    grad_residual, grad_branch, home, gain2_sum = branch_back(
        scalars, out_pieces, keep_a, chip_near, home, residual, cotangent, gain_two
    )
    grad_home = exchange(home)

    rows_keep, rows_send = out_grad(scalars, after(att_rows, home), grad_branch)
    rows_met = mate(rows_send)
    few = rows_keep.shape[1]

    def ends(index, at, *more):
        kept = [(out_keep, index, 0)], [(rows_keep, index, 0)]
        if at is not None:
            kept[0].append((out_met, at, 0))
            kept[1].append((rows_met, at, 0))
        for array, where in more:
            kept[0].append((array, where, 0))
            kept[1].append((array, where, rows))
        return [(rows, kept[0]), (few, kept[1])]

    end_last = combine(ends(4, 2))
    grad_home = after(grad_home, end_last, grad_mlp)
    end_far = far(after(end_last, grad_home))
    keep_0, send_0, before = attend_back(
        scalars, qkv, grad_home, att_0, log_0, cosine, sine, weight_qkv, low1, 0
    )
    met_0 = mate(send_0)
    end_far = after(end_far, send_0)
    end_chip = combine(ends(2, 0, (end_far, 0)), ends(3, 1))
    end_near = near(end_chip)
    keep_1, send_1, grad_qkv = attend_back(
        scalars, qkv, after(grad_home, end_chip), att_1, log_1, cosine, sine,
        weight_qkv, low1, 1, before, gain_one, gain2_sum, dp=dp,
    )

    grad_qkv = scatter(grad_qkv.reshape(-1, grad_qkv.shape[2]))
    met_1 = mate(send_1)
    end_home = combine(ends(1, None, (after(end_near, send_1), 1)))
    in_parts = after(grad_in, send_1).reshape(2, rows_here, -1)
    in_other = pick(in_parts, 1 - at_c, 0)
    met_1, end_home, in_other = lax.optimization_barrier((met_1, end_home, in_other))
    in_cross = group.swap(in_other, 4)
    end_home = mate(end_home)

    def both(index, at, *more):
        kept = [(keep_0, index, 0)], [(keep_1, index, 0)]
        if at is not None:
            kept[0].append((met_0, at, 0))
            kept[1].append((met_1, at, 0))
        for array, where in more:
            kept[0].append((array, where, 0))
            kept[1].append((array, where, block))
        return [(block, kept[0]), (block, kept[1])]

    last = combine(both(4, 2))
    last_far = far(last)
    result, grad_out = finish(
        out_keep, rows_keep, end_near, after(end_home, last), residual, dp
    )
    last_far, grad_out = lax.optimization_barrier((last_far, grad_out))
    grad_out = scatter(grad_out)[0]
    chip = combine(both(2, 0, (last_far, 0)), both(3, 1), mebibytes=60)
    chip_near = near(chip)

    grad_in = in_order(after(pick(in_parts, at_c, 0), chip), in_cross)
    late = at_h // half
    grad_in = jnp.stack([grad_in[..., :hidden], grad_in[..., padded : padded + hidden]])
    stays = pick(grad_in, late, 0)
    comes = group.swap(pick(grad_in, 1 - late, 0), half)
    grad_qkv = after(grad_qkv, chip)
    both_rows = 2 * rows_here
    qkv_parts = grad_qkv[:both_rows].reshape(2, rows_here, -1)
    gains = grad_qkv[both_rows:]
    cross = jnp.concatenate([pick(qkv_parts, 1 - at_c, 0), gains])
    cross = group.swap(cross, 4)
    chip_near = after(chip_near, comes, cross)
    home = combine(both(1, None, (chip_near, 1)))
    cross = after(cross, home)
    home = mate(home)
    grad_qkv = in_order(pick(qkv_parts, at_c, 0), cross[:rows_here])
    gains = (wide(gains) + wide(cross[rows_here:])).astype(BF16)
    gains = wide(gains) + sum(wide(group.swap(gains, bit)) for bit in range(1, heads))
    grad_input = input_grad((keep_0, keep_1), chip_near, home, tokens, grad_residual, gain_one)
    grad_out, grad_mlp, grad_input = lax.optimization_barrier((grad_out, grad_mlp, grad_input))
    grad_mlp = group.rows_back(grad_mlp, place)
    grad_out = wide(group.rows_back(grad_out, straight))

    grad_mlp = wide(grad_mlp)
    grad_in = jnp.where(
        late == 0, jnp.concatenate([stays, comes]), jnp.concatenate([comes, stays])
    )
    grad_in = wide(jnp.moveaxis(grad_in, 0, 1).reshape(rows_here, -1))

    per_device = width // (dp * parts)
    start = group.at * per_device
    grad_gain1, grad_gain2 = (
        lax.dynamic_slice_in_dim(gains[i], start, per_device, 0) for i in range(2)
    )
    grad_qkv = grad_qkv.reshape(2, rows_here, 3, own_width)
    grad_qkv = jnp.moveaxis(grad_qkv, 2, 0)
    odd = at_h % 2
    stays = pick(grad_qkv, odd + late, 0)
    core = group.swap(pick(grad_qkv, 1 - odd + late, 0), 1)
    chip = group.swap(pick(grad_qkv, 2 - 2 * late, 0), 2)
    grad_qkv = jnp.where(
        odd == 0, jnp.concatenate([stays, core, chip]), jnp.concatenate([chip, core, stays])
    )
    grad_qkv = wide(jnp.moveaxis(grad_qkv, 0, 1).reshape(rows_here, -1))

    return (
        result,
        grad_input,
        grad_qkv,
        grad_out,
        grad_in,
        grad_mlp,
        grad_gain1,
        grad_gain2,
    )


def local(tokens, cotangent, w_qkv, w_attn_out, w_in, w_mlp_out, norm_gain1, norm_gain2):
    args = (tokens, cotangent, w_qkv, w_attn_out, w_in, w_mlp_out, norm_gain1, norm_gain2)
    sizes = [lax.axis_size(axis) for axis in ("dp", "ctx", "head")]
    if sizes == [4, 2, 4] and tokens.shape[2] == 8 * 2 * HD and tokens.shape[1] % 16 == 0:
        return local_split(*args)
    return local_general(*args)


def solution(mesh):
    in_specs = (
        P("dp", ("ctx", "head"), None),
        P("dp", ("ctx", "head"), None),
        P(("dp", "ctx"), None),
        P(("dp", "ctx"), None),
        P(("dp", "ctx"), None),
        P(("dp", "ctx"), None),
        P(("dp", "ctx")),
        P(("dp", "ctx")),
    )
    out_specs = (
        P("dp", ("ctx", "head"), None),
        P("dp", ("ctx", "head"), None),
        P(("dp", "ctx"), "head"),
        P(("dp", "ctx"), "head"),
        P(("dp", "ctx"), "head"),
        P(("dp", "ctx"), "head"),
        P(("dp", "ctx", "head")),
        P(("dp", "ctx", "head")),
    )
    return jax.shard_map(local, mesh=mesh, in_specs=in_specs, out_specs=out_specs, check_vma=False)
```

```python
import functools
import math

import jax
import jax.numpy as jnp
from jax import lax
from jax.experimental import pallas as pl
from jax.experimental.pallas import tpu as pltpu
from jax.sharding import PartitionSpec as P

HD = 64


EPSILON = 1e-05
ROPE_BASE = 160000.0


def normalize(values):
    centre = jnp.mean(values, axis=-1, keepdims=True)
    shifted = values - centre
    spread = jnp.mean(shifted * shifted, axis=-1, keepdims=True)
    factor = lax.rsqrt(spread + EPSILON)
    return (shifted * factor, factor)


def norm_back(grad_normed, normed, factor):
    grad_centre = jnp.mean(grad_normed, axis=-1, keepdims=True)
    grad_along = jnp.mean(grad_normed * normed, axis=-1, keepdims=True)
    return (grad_normed - grad_centre - normed * grad_along) * factor


def rope_tables(positions, half_size):
    frequency = jnp.exp(
        jnp.arange(half_size, dtype=jnp.float32) * (-math.log(ROPE_BASE) / half_size)
    )
    angles = positions[:, None] * frequency[None, :]
    return (jnp.cos(angles), jnp.sin(angles))


def rotate(values, cosine, sine_table, direction):
    half_size = cosine.shape[-1]
    first_half = values[..., :half_size]
    second_half = values[..., half_size:]
    cos_part = cosine[:, None, :]
    sin_part = sine_table[:, None, :] * direction
    return jnp.concatenate(
        [
            first_half * cos_part - second_half * sin_part,
            second_half * cos_part + first_half * sin_part,
        ],
        axis=-1,
    )


def block_scores(queries4, keys_block, scale):
    keys4 = keys_block.reshape(
        keys_block.shape[0], keys_block.shape[1], queries4.shape[2], queries4.shape[3]
    )
    return (
        jnp.einsum("sqgd,skgd->sgqk", queries4, keys4, preferred_element_type=jnp.float32) * scale
    )


def attend_forward(queries4, keys_all, values_all, key_rows, scale):
    seqs_here, query_rows, groups, head_size = queries4.shape
    turns = keys_all.shape[1] // key_rows

    def statistics(turn, carry):
        row_peak, row_total = carry
        keys_block = lax.dynamic_slice_in_dim(keys_all, turn * key_rows, key_rows, 1)
        scores = block_scores(queries4, keys_block, scale)
        new_peak = jnp.maximum(row_peak, jnp.max(scores, axis=-1))
        row_total = row_total * jnp.exp(row_peak - new_peak) + jnp.sum(
            jnp.exp(scores - new_peak[..., None]), axis=-1
        )
        return (new_peak, row_total)

    start_peak = jnp.full((seqs_here, groups, query_rows), -1e30, jnp.float32)
    row_peak, row_total = lax.fori_loop(
        0, turns, statistics, (start_peak, jnp.zeros_like(start_peak))
    )
    log_total = row_peak + jnp.log(row_total)

    def accumulate(turn, running):
        keys_block = lax.dynamic_slice_in_dim(keys_all, turn * key_rows, key_rows, 1)
        values_block = lax.dynamic_slice_in_dim(values_all, turn * key_rows, key_rows, 1).reshape(
            seqs_here, key_rows, groups, head_size
        )
        weights = jnp.exp(block_scores(queries4, keys_block, scale) - log_total[..., None]).astype(
            jnp.bfloat16
        )
        return running + jnp.einsum(
            "sgqk,skgd->sqgd", weights, values_block, preferred_element_type=jnp.float32
        )

    attended = lax.fori_loop(
        0, turns, accumulate, jnp.zeros((seqs_here, query_rows, groups, head_size), jnp.float32)
    )
    return (attended, log_total)


def attend_backward(queries4, keys_all, values_all, grad_out4, log_total, along, key_rows, scale):
    seqs_here, query_rows, groups, head_size = queries4.shape
    length = keys_all.shape[1]
    width_group = groups * head_size
    turns = length // key_rows

    def step_back(turn, carry):
        grad_queries, grad_keys, grad_values = carry
        keys_block = lax.dynamic_slice_in_dim(keys_all, turn * key_rows, key_rows, 1)
        keys4 = keys_block.reshape(seqs_here, key_rows, groups, head_size)
        values4 = lax.dynamic_slice_in_dim(values_all, turn * key_rows, key_rows, 1).reshape(
            seqs_here, key_rows, groups, head_size
        )
        weights = jnp.exp(block_scores(queries4, keys_block, scale) - log_total[..., None])
        grad_weights = jnp.einsum(
            "sqgd,skgd->sgqk", grad_out4, values4, preferred_element_type=jnp.float32
        )
        grad_scores = (weights * (grad_weights - along[..., None])).astype(jnp.bfloat16)
        grad_queries = grad_queries + jnp.einsum(
            "sgqk,skgd->sqgd", grad_scores, keys4, preferred_element_type=jnp.float32
        )
        key_part = (
            jnp.einsum("sgqk,sqgd->skgd", grad_scores, queries4, preferred_element_type=jnp.float32)
            * scale
        )
        value_part = jnp.einsum(
            "sgqk,sqgd->skgd",
            weights.astype(jnp.bfloat16),
            grad_out4,
            preferred_element_type=jnp.float32,
        )
        grad_keys = lax.dynamic_update_slice_in_dim(
            grad_keys, key_part.reshape(seqs_here, key_rows, width_group), turn * key_rows, 1
        )
        grad_values = lax.dynamic_update_slice_in_dim(
            grad_values, value_part.reshape(seqs_here, key_rows, width_group), turn * key_rows, 1
        )
        return (grad_queries, grad_keys, grad_values)

    start = (
        jnp.zeros((seqs_here, query_rows, groups, head_size), jnp.float32),
        jnp.zeros((seqs_here, length, width_group), jnp.float32),
        jnp.zeros((seqs_here, length, width_group), jnp.float32),
    )
    grad_queries, grad_keys, grad_values = lax.fori_loop(0, turns, step_back, start)
    return (grad_queries * scale, grad_keys, grad_values)


def local_general(tokens, cotangent, w_qkv, w_attn_out, w_in, w_mlp_out, norm_gain1, norm_gain2):
    seqs_here, block_rows, width = tokens.shape
    count_rows = seqs_here * block_rows
    heads_all = width // HD
    head_devices = lax.axis_size("head")
    group_devices = lax.axis_size(("dp", "ctx"))
    groups = heads_all // head_devices
    width_group = groups * HD
    scale = HD ** (-0.5)
    ff_width = w_in.shape[1] // 2
    full_qkv, full_out, full_in, full_mlp, gain_one, gain_two = (
        lax.all_gather(w_qkv, ("dp", "ctx"), axis=0, tiled=True),
        lax.all_gather(w_attn_out, ("dp", "ctx"), axis=0, tiled=True),
        lax.all_gather(w_in, ("dp", "ctx"), axis=0, tiled=True),
        lax.all_gather(w_mlp_out, ("dp", "ctx"), axis=0, tiled=True),
        lax.all_gather(norm_gain1, ("dp", "ctx"), axis=0, tiled=True),
        lax.all_gather(norm_gain2, ("dp", "ctx"), axis=0, tiled=True),
    )
    x_in = tokens.astype(jnp.float32).reshape(count_rows, width)
    normed1, factor1 = normalize(x_in)
    lowered1 = (normed1 * gain_one.astype(jnp.float32)).astype(jnp.bfloat16)
    projected = jnp.dot(lowered1, full_qkv, preferred_element_type=jnp.float32).reshape(
        seqs_here, block_rows, 3, heads_all, HD
    )
    first_pos = (lax.axis_index("ctx") * head_devices + lax.axis_index("head")) * block_rows
    positions = (first_pos + jnp.arange(block_rows, dtype=jnp.int32)).astype(jnp.float32)
    cosine, sine_table = rope_tables(positions, HD // 2)
    queries = (
        rotate(projected[:, :, 0], cosine, sine_table, 1.0)
        .astype(jnp.bfloat16)
        .reshape(seqs_here, block_rows, width)
    )
    keys_local = (
        rotate(projected[:, :, 1], cosine, sine_table, 1.0)
        .astype(jnp.bfloat16)
        .reshape(seqs_here, block_rows, width)
    )
    values_local = projected[:, :, 2].astype(jnp.bfloat16).reshape(seqs_here, block_rows, width)
    queries_h, keys_h, values_h = (
        lax.all_to_all(queries, "head", split_axis=2, concat_axis=1, tiled=True),
        lax.all_to_all(keys_local, "head", split_axis=2, concat_axis=1, tiled=True),
        lax.all_to_all(values_local, "head", split_axis=2, concat_axis=1, tiled=True),
    )
    query_rows = queries_h.shape[1]
    queries4 = queries_h.reshape(seqs_here, query_rows, groups, HD)
    keys_all, values_all = (
        lax.all_gather(keys_h, "ctx", axis=1, tiled=True),
        lax.all_gather(values_h, "ctx", axis=1, tiled=True),
    )
    key_rows = math.gcd(keys_all.shape[1], 1024)
    attended, log_total = attend_forward(queries4, keys_all, values_all, key_rows, scale)
    attended_low = attended.astype(jnp.bfloat16).reshape(seqs_here, query_rows, width_group)
    back_rows = lax.all_to_all(
        attended_low, "head", split_axis=1, concat_axis=2, tiled=True
    ).reshape(count_rows, width)
    residual = x_in + jnp.dot(back_rows, full_out, preferred_element_type=jnp.float32)
    normed2, factor2 = normalize(residual)
    lowered2 = (normed2 * gain_two.astype(jnp.float32)).astype(jnp.bfloat16)
    lifted = jnp.dot(lowered2, full_in, preferred_element_type=jnp.float32)
    first_part = lifted[:, :ff_width]
    second_part = lifted[:, ff_width:]
    activated, gelu_pullback = jax.vjp(
        lambda entries: jax.nn.gelu(entries, approximate=False), first_part
    )
    mixed = (activated * second_part).astype(jnp.bfloat16)
    result = (residual + jnp.dot(mixed, full_mlp, preferred_element_type=jnp.float32)).astype(
        jnp.bfloat16
    )
    full_qkv, full_out, full_in, full_mlp, gain_one, gain_two = (
        lax.all_gather(w_qkv, ("dp", "ctx"), axis=0, tiled=True),
        lax.all_gather(w_attn_out, ("dp", "ctx"), axis=0, tiled=True),
        lax.all_gather(w_in, ("dp", "ctx"), axis=0, tiled=True),
        lax.all_gather(w_mlp_out, ("dp", "ctx"), axis=0, tiled=True),
        lax.all_gather(norm_gain1, ("dp", "ctx"), axis=0, tiled=True),
        lax.all_gather(norm_gain2, ("dp", "ctx"), axis=0, tiled=True),
    )
    keys_all, values_all = (
        lax.all_gather(keys_h, "ctx", axis=1, tiled=True),
        lax.all_gather(values_h, "ctx", axis=1, tiled=True),
    )
    grad_top = cotangent.reshape(count_rows, width)
    grad_mlp = jnp.einsum("nf,nd->fd", mixed, grad_top, preferred_element_type=jnp.float32)
    grad_mixed = jnp.einsum("nd,fd->nf", grad_top, full_mlp, preferred_element_type=jnp.float32)
    grad_first = gelu_pullback(grad_mixed * second_part)[0]
    grad_lifted = jnp.concatenate([grad_first, grad_mixed * activated], axis=-1).astype(
        jnp.bfloat16
    )
    grad_inner = jnp.einsum("nd,nf->df", lowered2, grad_lifted, preferred_element_type=jnp.float32)
    grad_lowered2 = jnp.einsum(
        "nf,df->nd", grad_lifted, full_in, preferred_element_type=jnp.float32
    )
    grad_two = jnp.sum(grad_lowered2 * normed2, axis=0)
    grad_residual = grad_top.astype(jnp.float32) + norm_back(
        grad_lowered2 * gain_two.astype(jnp.float32), normed2, factor2
    )
    grad_branch = grad_residual.astype(jnp.bfloat16)
    grad_outproj = jnp.einsum(
        "nd,ne->de", back_rows, grad_branch, preferred_element_type=jnp.float32
    )
    grad_attended = jnp.einsum(
        "ne,de->nd", grad_branch, full_out, preferred_element_type=jnp.float32
    ).astype(jnp.bfloat16)
    grad_attended_h = lax.all_to_all(
        grad_attended.reshape(seqs_here, block_rows, width),
        "head",
        split_axis=2,
        concat_axis=1,
        tiled=True,
    )
    grad_out4 = grad_attended_h.reshape(seqs_here, query_rows, groups, HD)
    along = jnp.transpose(jnp.sum(grad_out4.astype(jnp.float32) * attended, axis=-1), (0, 2, 1))
    grad_queries, grad_keys_all, grad_values_all = attend_backward(
        queries4, keys_all, values_all, grad_out4, log_total, along, key_rows, scale
    )
    grad_keys_sum, grad_values_sum = (
        lax.psum_scatter(
            grad_keys_all.astype(jnp.bfloat16), "ctx", scatter_dimension=1, tiled=True
        ).astype(jnp.float32),
        lax.psum_scatter(
            grad_values_all.astype(jnp.bfloat16), "ctx", scatter_dimension=1, tiled=True
        ).astype(jnp.float32),
    )
    grad_q_low = grad_queries.astype(jnp.bfloat16).reshape(seqs_here, query_rows, width_group)
    grad_q_tok, grad_k_tok, grad_v_tok = (
        lax.all_to_all(grad_q_low, "head", split_axis=1, concat_axis=2, tiled=True),
        lax.all_to_all(
            grad_keys_sum.astype(jnp.bfloat16), "head", split_axis=1, concat_axis=2, tiled=True
        ),
        lax.all_to_all(
            grad_values_sum.astype(jnp.bfloat16), "head", split_axis=1, concat_axis=2, tiled=True
        ),
    )
    unrot_q = rotate(
        grad_q_tok.astype(jnp.float32).reshape(seqs_here, block_rows, heads_all, HD),
        cosine,
        sine_table,
        -1.0,
    )
    unrot_k = rotate(
        grad_k_tok.astype(jnp.float32).reshape(seqs_here, block_rows, heads_all, HD),
        cosine,
        sine_table,
        -1.0,
    )
    grad_projected = jnp.concatenate(
        [
            unrot_q.reshape(count_rows, width),
            unrot_k.reshape(count_rows, width),
            grad_v_tok.astype(jnp.float32).reshape(count_rows, width),
        ],
        axis=-1,
    ).astype(jnp.bfloat16)
    grad_project = jnp.einsum(
        "nd,nf->df", lowered1, grad_projected, preferred_element_type=jnp.float32
    )
    grad_lowered1 = jnp.einsum(
        "nf,df->nd", grad_projected, full_qkv, preferred_element_type=jnp.float32
    )
    grad_one = jnp.sum(grad_lowered1 * normed1, axis=0)
    grad_input = grad_residual + norm_back(
        grad_lowered1 * gain_one.astype(jnp.float32), normed1, factor1
    )
    pieces_one = grad_one.reshape(group_devices, head_devices, -1)
    pieces_two = grad_two.reshape(group_devices, head_devices, -1)
    part_qkv, part_out, part_in, part_mlp, part_one, part_two = (
        lax.psum_scatter(
            grad_project.astype(jnp.bfloat16), ("dp", "ctx"), scatter_dimension=0, tiled=True
        ).astype(jnp.float32),
        lax.psum_scatter(
            grad_outproj.astype(jnp.bfloat16), ("dp", "ctx"), scatter_dimension=0, tiled=True
        ).astype(jnp.float32),
        lax.psum_scatter(
            grad_inner.astype(jnp.bfloat16), ("dp", "ctx"), scatter_dimension=0, tiled=True
        ).astype(jnp.float32),
        lax.psum_scatter(
            grad_mlp.astype(jnp.bfloat16), ("dp", "ctx"), scatter_dimension=0, tiled=True
        ).astype(jnp.float32),
        lax.psum_scatter(
            pieces_one.astype(jnp.bfloat16), ("dp", "ctx"), scatter_dimension=0, tiled=True
        ).astype(jnp.float32),
        lax.psum_scatter(
            pieces_two.astype(jnp.bfloat16), ("dp", "ctx"), scatter_dimension=0, tiled=True
        ).astype(jnp.float32),
    )
    final_qkv, final_out, final_in, final_mlp, final_one, final_two = (
        lax.psum_scatter(
            part_qkv.astype(jnp.bfloat16), "head", scatter_dimension=1, tiled=True
        ).astype(jnp.float32),
        lax.psum_scatter(
            part_out.astype(jnp.bfloat16), "head", scatter_dimension=1, tiled=True
        ).astype(jnp.float32),
        lax.psum_scatter(
            part_in.astype(jnp.bfloat16), "head", scatter_dimension=1, tiled=True
        ).astype(jnp.float32),
        lax.psum_scatter(
            part_mlp.astype(jnp.bfloat16), "head", scatter_dimension=1, tiled=True
        ).astype(jnp.float32),
        lax.psum_scatter(
            part_one.astype(jnp.bfloat16), "head", scatter_dimension=1, tiled=True
        ).astype(jnp.float32),
        lax.psum_scatter(
            part_two.astype(jnp.bfloat16), "head", scatter_dimension=1, tiled=True
        ).astype(jnp.float32),
    )
    return (
        result.reshape(seqs_here, block_rows, width),
        grad_input.reshape(seqs_here, block_rows, width),
        final_qkv,
        final_out,
        final_in,
        final_mlp,
        final_one.reshape(-1),
        final_two.reshape(-1),
    )


F32 = jnp.float32
BF16 = jnp.bfloat16
GROUP = ("ctx", "head")


def dot(left, right, dims=((1,), (0,))):
    return lax.dot_general(left, right, (dims, ((), ())), preferred_element_type=F32)


def wide(values):
    return values.astype(F32)


def flat(values):
    return values.reshape(-1, values.shape[-1])


def lane_rotate(values, cosine, sine_signed):
    lane = lax.broadcasted_iota(jnp.int32, values.shape, 1)
    width = values.shape[1]
    partner = jnp.where(
        lane % HD < HD // 2,
        pltpu.roll(values, width - HD // 2, 1),
        pltpu.roll(values, HD // 2, 1),
    )
    return values * cosine + partner * sine_signed


def head_masks(shape):
    lane = lax.broadcasted_iota(jnp.int32, shape, 1)
    return [lane // HD == head for head in range(shape[1] // HD)]


def params(mebibytes):
    return pltpu.CompilerParams(vmem_limit_bytes=mebibytes * 1024 * 1024)


COST = pl.CostEstimate(flops=1 << 20, transcendentals=0, bytes_accessed=1 << 16)


def whole(array):
    return pl.BlockSpec(array.shape, lambda *_: (0,) * len(array.shape))


SCALARS = pl.BlockSpec(memory_space=pltpu.SMEM)


def project_kernel(place_ref, *refs):
    pieces, weights = refs[:6], refs[6:10]
    cos_ref, sin_ref, low_ref, qkv_ref, w_ref, gain1_ref, gain2_ref, rows_ref = refs[10:]
    block, part = pieces[0].shape[2], w_ref.shape[1] // 3
    rows = gain1_ref.shape[1] // 8

    @pl.when(pl.program_id(0) == 0)
    def _():
        for step, piece in enumerate(weights):
            for turn in range(2):
                at = 2 * (place_ref[8] ^ step) + (place_ref[9] ^ turn)
                w_ref[pl.ds(pl.multiple_of(at * rows, rows), rows), :] = piece[turn, :rows]
                gains = piece[turn, rows:].astype(F32)
                rows_ref[0, pl.ds(at, 1), :] = gains[:1, :rows]
                rows_ref[1, pl.ds(at, 1), :] = gains[1:2, :rows]
        for out, at in ((gain1_ref, 0), (gain2_ref, 1)):
            for row in range(8):
                out[:, row * rows : (row + 1) * rows] = rows_ref[at, row : row + 1, :]

    gain = gain1_ref[...]
    index = 0
    for piece in pieces:
        for inner in range(piece.shape[0]):
            normed, _ = normalize(piece[inner, 0].astype(F32))
            low_ref[index, 0] = (normed * gain).astype(BF16)
            index += 1
    projected = dot(flat(low_ref[:, 0]), w_ref[...])
    cosine, sine = cos_ref[...], sin_ref[...]
    shape = (8, block, part)
    qkv_ref[:, 0, :, :part] = (
        (lane_rotate(projected[:, :part], cosine, sine) * HD**-0.5).astype(BF16).reshape(shape)
    )
    qkv_ref[:, 0, :, part : 2 * part] = (
        lane_rotate(projected[:, part : 2 * part], cosine, sine).astype(BF16).reshape(shape)
    )
    qkv_ref[:, 0, :, 2 * part :] = projected[:, 2 * part :].astype(BF16).reshape(shape)


def project(place, pieces, weights, cosine, sine):
    seqs, block, width = pieces[0].shape[1:]
    own = weights[0].shape[2]

    def by_seq(lead, last):
        return pl.BlockSpec((lead, 1, block, last), lambda s: (0, s, 0, 0))

    return pl.pallas_call(
        project_kernel,
        grid=(seqs,),
        in_specs=[SCALARS]
        + [by_seq(piece.shape[0], width) for piece in pieces]
        + [whole(w) for w in weights]
        + [whole(cosine), whole(sine)],
        out_specs=(
            by_seq(8, width),
            by_seq(8, own),
            pl.BlockSpec((width, own), lambda s: (0, 0)),
            pl.BlockSpec((1, width), lambda s: (0, 0)),
            pl.BlockSpec((1, width), lambda s: (0, 0)),
        ),
        out_shape=(
            jax.ShapeDtypeStruct((8, seqs, block, width), BF16),
            jax.ShapeDtypeStruct((8, seqs, block, own), BF16),
            jax.ShapeDtypeStruct((width, own), BF16),
            jax.ShapeDtypeStruct((1, width), F32),
            jax.ShapeDtypeStruct((1, width), F32),
        ),
        scratch_shapes=[pltpu.VMEM((2, 8, width // 8), F32)],
        compiler_params=params(60),
        cost_estimate=COST,
        name="project",
    )(place, *pieces, *weights, cosine, sine)


def attend_kernel(place_ref, q_ref, k_ref, v_ref, *refs):
    att_ref, log_ref, home_ref = refs[-3:]
    step, seq = pl.program_id(0), len(refs) - 3
    if seq:

        @pl.when(step == 0)
        def _():
            home_ref[:, :1] = refs[0][...]

    queries, keys, values = flat(q_ref[...]), flat(k_ref[...]), flat(v_ref[...])
    attended = jnp.zeros(queries.shape, F32)
    logs = jnp.zeros(queries.shape, F32)
    for mask in head_masks(queries.shape):
        scores = dot(jnp.where(mask, queries, 0), keys, ((1,), (1,)))
        peak = jnp.max(scores, axis=1, keepdims=True)
        weights = jnp.exp(scores - peak)
        total = jnp.sum(weights, axis=1, keepdims=True)
        mixed = dot(weights.astype(BF16), values) * (1.0 / total)
        attended = jnp.where(mask, mixed, attended)
        logs = jnp.where(mask, peak + jnp.log(total), logs)
    att_ref[...] = attended.reshape(att_ref.shape)
    log_ref[...] = logs.reshape(log_ref.shape)
    low = attended.astype(BF16).reshape(att_ref.shape)
    for inner in range(2):
        home_ref[place_ref[2 * step + inner], seq] = low[inner, 0]


def attend(place, qkv, *home):
    _, _, block, own = qkv.shape
    part, seq = own // 3, len(home)
    rows = pl.BlockSpec((2, 1, block, part), lambda i: (i, 0, 0, 0))
    shape = (8, 1, block, part)
    return pl.pallas_call(
        attend_kernel,
        grid=(4,),
        in_specs=[
            SCALARS,
            pl.BlockSpec((2, 1, block, part), lambda i: (i, seq, 0, 0)),
            pl.BlockSpec((8, 1, block, part), lambda i: (0, seq, 0, 1)),
            pl.BlockSpec((8, 1, block, part), lambda i: (0, seq, 0, 2)),
            *[whole(h) for h in home],
        ],
        out_specs=(
            rows,
            rows,
            pl.BlockSpec((8, 1 + seq, block, part), lambda i: (0, 0, 0, 0)),
        ),
        out_shape=(
            jax.ShapeDtypeStruct(shape, F32),
            jax.ShapeDtypeStruct(shape, F32),
            jax.ShapeDtypeStruct((8, 1 + seq, block, part), BF16),
        ),
        compiler_params=params(24),
        cost_estimate=COST,
        name="attend",
    )(place, qkv, qkv, qkv, *home)


def branch_kernel(place_ref, *refs):
    pieces = refs[:6]
    rows_ref, tokens_ref, gain_ref, residual_ref, low_ref, side_ref, total_ref = refs[6:]
    heads = rows_ref.shape[0] // 2
    for c in range(2):
        side_ref[c] = jnp.concatenate([flat(rows_ref[c * heads + d]) for d in range(heads)], axis=1)
    total_ref[...] = flat(wide(tokens_ref[...]))
    index = 0
    for piece in pieces:
        n = piece.shape[2]
        for inner in range(piece.shape[0]):
            at = place_ref[index]
            columns = pl.ds(pl.multiple_of((at % heads) * n, n), n)
            total_ref[:, columns] += dot(side_ref[at // heads], piece[inner])
            index += 1
    total = total_ref[...]
    normed, _ = normalize(total)
    residual_ref[...] = total.reshape(residual_ref.shape)
    low_ref[...] = (normed * gain_ref[...]).astype(BF16).reshape(low_ref.shape)


def branch(place, pieces, rows, tokens, gain):
    args = (*pieces, rows, tokens, gain)
    seqs, block, width = tokens.shape
    return pl.pallas_call(
        branch_kernel,
        in_specs=[SCALARS] + [whole(a) for a in args],
        out_shape=(
            jax.ShapeDtypeStruct(tokens.shape, F32),
            jax.ShapeDtypeStruct(tokens.shape, BF16),
        ),
        scratch_shapes=[
            pltpu.VMEM((2, seqs * block, pieces[0].shape[1]), BF16),
            pltpu.VMEM((seqs * block, width), F32),
        ],
        compiler_params=params(16),
        cost_estimate=COST,
        name="branch",
    )(place, *args)


def combine(*groups, mebibytes=16):
    parts = [part for group in groups for _, parts in group for part in parts]
    rows = sum(count for count, _ in groups[0])
    width = parts[0][0].shape[2]

    def kernel(*refs):
        at = 0
        for k, group in enumerate(groups):
            row = 0
            for count, terms in group:
                total = 0.0
                for _, _, start in terms:
                    total = total + wide(refs[at][0, start : start + count])
                    at += 1
                refs[-1][k, row : row + count] = total.astype(BF16)
                row += count

    return pl.pallas_call(
        kernel,
        grid=(1,),
        in_specs=[
            pl.BlockSpec((1, *array.shape[1:]), lambda *_, index=index: (index, 0, 0))
            for array, index, _ in parts
        ],
        out_specs=pl.BlockSpec((len(groups), rows, width), lambda *_: (0, 0, 0)),
        out_shape=jax.ShapeDtypeStruct((len(groups), rows, width), BF16),
        compiler_params=params(mebibytes),
        cost_estimate=COST,
        name="combine",
    )(*[array for array, _, _ in parts])


def mlp_kernel(*refs, count, ends):
    pieces, tops = refs[:count], refs[count : 2 * count]
    w_ref, out_w_ref = refs[2 * count : 2 * count + 2]
    low_ref, top_ref, mixed_ref, lifted_ref, *out_refs = refs[-4 - len(ends) :]
    step = pl.program_id(0)
    start = 0
    for piece, top in zip(pieces, tops):

        @pl.when((step >= start) & (step < start + piece.shape[0]))
        def _(piece=piece, top=top, start=start):
            low_ref[0] = piece[step - start]
            top_ref[0] = top[step - start]

        start += piece.shape[0]

    hidden = w_ref.shape[1] // 2
    lifted = dot(flat(low_ref[...]), w_ref[...])
    first, second = lifted[:, :hidden], lifted[:, hidden:]
    grad_mixed = dot(flat(top_ref[...]), out_w_ref[...], ((1,), (1,)))
    gate = 0.5 * (1.0 + lax.erf(first * (0.5**0.5)))
    slope = gate + first * jnp.exp(first * first * -0.5) * ((2.0 * math.pi) ** -0.5)
    activated = first * gate
    mixed_ref[...] = (activated * second).astype(BF16).reshape(mixed_ref.shape)
    grad = jnp.concatenate(
        [(grad_mixed * second * slope).astype(BF16), (grad_mixed * activated).astype(BF16)],
        axis=1,
    )
    lifted_ref[...] = grad.reshape(lifted_ref.shape)
    partial = dot(grad, w_ref[...], ((1,), (1,))).astype(BF16).reshape(low_ref.shape)
    start = 0
    for out, end in zip(out_refs, ends):

        @pl.when((step >= start) & (step < end))
        def _(out=out):
            out[...] = partial

        start = end


def mlp(pieces, tops, w, out_w, base, ends, earlier=()):
    seqs, block, width = pieces[0].shape[1:]
    hidden = w.shape[1] // 2
    whole_in = (*pieces, *tops, w, out_w)

    def rows(last):
        return pl.BlockSpec((1, seqs, block, last), lambda i: (i + base, 0, 0, 0))

    def within(start, end):
        return pl.BlockSpec(
            (1, seqs, block, width),
            lambda i: (jnp.clip(i - start, 0, end - start - 1), 0, 0, 0),
        )

    starts = (0, *ends[:-1])
    lasts = (width, width, hidden, 2 * hidden)
    return pl.pallas_call(
        functools.partial(mlp_kernel, count=len(pieces), ends=ends),
        grid=(ends[-1],),
        in_specs=[whole(array) for array in whole_in]
        + [pl.BlockSpec(memory_space=pl.ANY)] * len(earlier),
        out_specs=(
            *[rows(last) for last in lasts],
            *[within(start, end) for start, end in zip(starts, ends)],
        ),
        out_shape=(
            *[jax.ShapeDtypeStruct((8, seqs, block, last), BF16) for last in lasts],
            *[
                jax.ShapeDtypeStruct((end - start, seqs, block, width), BF16)
                for start, end in zip(starts, ends)
            ],
        ),
        input_output_aliases={len(whole_in) + at: at for at in range(len(earlier))},
        compiler_params=params(32),
        cost_estimate=COST,
        name="mlp",
    )(*whole_in, *earlier)


def out_grad_kernel(place_ref, rows_ref, grad_ref, keep_ref, send_ref):
    grads = flat(grad_ref[...])
    for index in range(8):
        part = dot(flat(rows_ref[place_ref[index]]), grads, ((0,), (0,))).astype(BF16)
        if index < 5:
            keep_ref[index] = part
        else:
            send_ref[index - 5] = part


def out_grad(place, rows, grads):
    part, width = rows.shape[-1], grads.shape[-1]
    return pl.pallas_call(
        out_grad_kernel,
        in_specs=[SCALARS, whole(rows), whole(grads)],
        out_shape=(
            jax.ShapeDtypeStruct((5, part, width), BF16),
            jax.ShapeDtypeStruct((3, part, width), BF16),
        ),
        compiler_params=params(16),
        cost_estimate=COST,
        name="out_grad",
    )(place, rows, grads)


def branch_back_kernel(place_ref, *refs):
    pieces = refs[:6]
    keep_ref, near_ref, own_ref, residual_ref, top_ref, gain_ref = refs[6:12]
    grad_ref, branch_ref, home_ref, sum_ref, low_ref, side_ref = refs[12:]
    grad_low = wide(flat(keep_ref[...])) + wide(flat(near_ref[...])) + wide(flat(own_ref[...]))
    normed, factor = normalize(flat(residual_ref[...]))
    sum_ref[...] = jnp.sum(grad_low * normed, axis=0, keepdims=True)
    grad = flat(wide(top_ref[...])) + norm_back(grad_low * gain_ref[...], normed, factor)
    grad_ref[...] = grad.reshape(grad_ref.shape)
    low_ref[...] = grad.astype(BF16)
    branch_ref[...] = low_ref[...].reshape(branch_ref.shape)
    heads = home_ref.shape[0] // 2
    side_ref[...] = jnp.zeros_like(side_ref)
    index = 0
    for piece in pieces:
        n = piece.shape[2]
        for inner in range(piece.shape[0]):
            at = place_ref[index]
            columns = pl.ds(pl.multiple_of((at % heads) * n, n), n)
            side_ref[at // heads] += dot(low_ref[:, columns], piece[inner], ((1,), (1,)))
            index += 1
    part = home_ref.shape[3]
    for c in range(2):
        for d in range(heads):
            home = side_ref[c, :, d * part : (d + 1) * part].astype(BF16)
            home_ref[c * heads + d] = home.reshape(home_ref.shape[1:])


def branch_back(place, pieces, keep, near, own, residual, top, gain):
    args = (*pieces, keep, near, own, residual, top, gain)
    seqs, block, width = residual.shape
    tall = pieces[0].shape[1]
    shapes = (
        jax.ShapeDtypeStruct(residual.shape, F32),
        jax.ShapeDtypeStruct(residual.shape, BF16),
        jax.ShapeDtypeStruct((8, seqs, block, tall // 4), BF16),
        jax.ShapeDtypeStruct((1, width), F32),
    )
    return pl.pallas_call(
        branch_back_kernel,
        grid=(1,),
        in_specs=[SCALARS]
        + [whole(piece) for piece in pieces]
        + [pl.BlockSpec((1, seqs * block, width), lambda *_: (0, 0, 0))] * 2
        + [whole(a) for a in args[8:]],
        out_specs=tuple(whole(shape) for shape in shapes),
        out_shape=shapes,
        scratch_shapes=[
            pltpu.VMEM((seqs * block, width), BF16),
            pltpu.VMEM((2, seqs * block, tall), F32),
        ],
        compiler_params=params(24),
        cost_estimate=COST,
        name="branch_back",
    )(place, *args)


def attend_back_kernel(
    place_ref, q_ref, k_ref, v_ref, grad_ref, att_ref, log_ref, cosq_ref, sinq_ref, cos_ref,
    sin_ref, w_ref, low_ref, *refs, seq, last,
):
    if last:
        before_ref, gain1_ref, gain2_ref, keep_ref, send_ref, grad_w_ref, *scratch = refs
    else:
        keep_ref, send_ref, before_ref, *scratch = refs
    proj_ref, sum_k, sum_v = scratch
    step = pl.program_id(0)
    block, part = q_ref.shape[2], q_ref.shape[3]

    @pl.when(step == 0)
    def _():
        sum_k[...] = jnp.zeros_like(sum_k)
        sum_v[...] = jnp.zeros_like(sum_v)

    queries, keys, values = flat(q_ref[...]), flat(k_ref[...]), flat(v_ref[...])
    grads = jnp.concatenate([grad_ref[place_ref[2 * step + inner], seq] for inner in range(2)])
    along = (grads.astype(F32) * flat(att_ref[...])).T
    logs = flat(log_ref[...]).T
    grad_queries = jnp.zeros(queries.shape, F32)
    for head, mask in enumerate(head_masks(queries.shape)):
        own_q = jnp.where(mask, queries, 0)
        own_g = jnp.where(mask, grads, 0)
        scores = dot(keys, own_q, ((1,), (1,)))
        weights = jnp.exp(scores - logs[head * HD : head * HD + 1])
        lifted = dot(values, own_g, ((1,), (1,)))
        row = jnp.sum(along[head * HD : (head + 1) * HD], axis=0, keepdims=True)
        grad_scores = (weights * (lifted - row)).astype(BF16)
        sum_k[...] += dot(grad_scores, own_q)
        sum_v[...] += dot(weights.astype(BF16), own_g)
        grad_queries = jnp.where(mask, dot(grad_scores, keys, ((0,), (0,))), grad_queries)
    grad_queries = lane_rotate(grad_queries * HD**-0.5, cosq_ref[...], -sinq_ref[...])
    rows = pl.multiple_of(step * 2 * block, 2 * block)
    proj_ref[pl.ds(rows, 2 * block), :part] = grad_queries.astype(BF16)

    @pl.when(step == 3)
    def _():
        grad_keys = lane_rotate(sum_k[...], cos_ref[...], -sin_ref[...])
        proj_ref[:, part : 2 * part] = grad_keys.astype(BF16)
        proj_ref[:, 2 * part :] = sum_v[...].astype(BF16)
        partial = dot(proj_ref[...], w_ref[...], ((1,), (1,))).astype(BF16)
        keep_ref[...] = partial[: 5 * block].reshape(5, block, -1)
        send_ref[...] = partial[5 * block :].reshape(3, block, -1)
        grad_w = dot(proj_ref[...], flat(low_ref[...]), ((0,), (0,)))
        if last:
            grad_w = (grad_w + before_ref[...]).T
            along_w = jnp.sum(grad_w * wide(w_ref[...]), axis=1, keepdims=True)
            along_w = jnp.broadcast_to(along_w, (w_ref.shape[0], 128)).T[:1] / gain1_ref[...]
            row = lax.broadcasted_iota(jnp.int32, (GAIN_ROWS, w_ref.shape[0]), 0)
            gains = jnp.where(row == 0, along_w, jnp.where(row == 1, gain2_ref[...], 0.0))
            n = grad_w_ref.shape[1] - GAIN_ROWS
            for at in range(grad_w_ref.shape[0]):
                part_rows = slice(at * n, (at + 1) * n)
                grad_w_ref[at, :n] = grad_w[part_rows].astype(BF16)
                grad_w_ref[at, n:, :n] = gains[:, part_rows].astype(BF16)
                rest = grad_w_ref.shape[2] - n
                grad_w_ref[at, n:, n:] = jnp.zeros((GAIN_ROWS, rest), BF16)
        else:
            before_ref[...] = grad_w


GAIN_ROWS = 16


def attend_back(place, qkv, grads, attended, logs, cosine, sine, w, low, seq, *before, dp=1):
    _, _, block, own = qkv.shape
    part, width = own // 3, w.shape[0]
    last = len(before) > 0
    rows = pl.BlockSpec((2, 1, block, part), lambda i: (i, 0, 0, 0))
    angles = pl.BlockSpec((2 * block, part), lambda i: (i, 0))

    def full(*shape):
        return pl.BlockSpec(shape, lambda i: (0,) * len(shape))

    args = [place, qkv, qkv, qkv, grads, attended, logs, cosine, sine, cosine, sine, w, low]
    in_specs = [
        SCALARS,
        pl.BlockSpec((2, 1, block, part), lambda i: (i, seq, 0, 0)),
        pl.BlockSpec((8, 1, block, part), lambda i: (0, seq, 0, 1)),
        pl.BlockSpec((8, 1, block, part), lambda i: (0, seq, 0, 2)),
        whole(grads),
        rows,
        rows,
        angles,
        angles,
        whole(cosine),
        whole(sine),
        whole(w),
        pl.BlockSpec((8, 1, block, width), lambda i: (0, seq, 0, 0)),
    ]
    shapes = [((5, block, width), BF16), ((3, block, width), BF16)]
    if last:
        args += before
        in_specs += [whole(array) for array in before]
        shapes += [((dp, width // dp + GAIN_ROWS, own), BF16)]
    else:
        shapes += [((own, width), F32)]
    return pl.pallas_call(
        functools.partial(attend_back_kernel, seq=seq, last=last),
        grid=(4,),
        in_specs=in_specs,
        out_specs=tuple(full(*shape) for shape, _ in shapes),
        out_shape=tuple(jax.ShapeDtypeStruct(shape, kind) for shape, kind in shapes),
        scratch_shapes=[
            pltpu.VMEM((8 * block, own), BF16),
            pltpu.VMEM((8 * block, part), F32),
            pltpu.VMEM((8 * block, part), F32),
        ],
        compiler_params=params(60),
        cost_estimate=COST,
        name="attend_back",
    )(*args)


def input_grad_kernel(*refs):
    keeps, (near_ref, own_ref, tokens_ref, residual_ref, gain_ref, out_ref) = refs[:-6], refs[-6:]
    block = tokens_ref.shape[1]
    for seq, keep in enumerate(keeps):
        rows = slice(seq * block, (seq + 1) * block)
        grad = wide(keep[0, :block]) + wide(near_ref[0, rows]) + wide(own_ref[0, rows])
        normed, factor = normalize(wide(tokens_ref[seq]))
        out_ref[seq] = residual_ref[seq] + norm_back(grad * gain_ref[...], normed, factor)


def input_grad(keeps, near, own, tokens, residual, gain):
    rest = (own, tokens, residual, gain)
    return pl.pallas_call(
        input_grad_kernel,
        grid=(1,),
        in_specs=[
            pl.BlockSpec((1, *array.shape[1:]), lambda *_: (0, 0, 0)) for array in (*keeps, near)
        ]
        + [whole(array) for array in rest],
        out_specs=whole(residual),
        out_shape=jax.ShapeDtypeStruct(residual.shape, F32),
        compiler_params=params(16),
        cost_estimate=COST,
        name="input_grad",
    )(*keeps, near, *rest)


def finish_kernel(keep_ref, rows_ref, near_ref, home_ref, residual_ref, out_ref, grad_ref):
    rows = keep_ref.shape[1]
    total = wide(keep_ref[0]) + wide(near_ref[0, :rows]) + wide(home_ref[0, :rows])
    out_ref[...] = (residual_ref[...] + total.reshape(residual_ref.shape)).astype(BF16)
    total = wide(rows_ref[0]) + wide(near_ref[0, rows:]) + wide(home_ref[0, rows:])
    n = grad_ref.shape[2]
    for at in range(grad_ref.shape[0]):
        grad_ref[at] = total[:, at * n : (at + 1) * n].astype(BF16)


def finish(keep, rows, near, home, residual, dp):
    args = (keep, rows, near, home)
    shapes = (
        jax.ShapeDtypeStruct(residual.shape, BF16),
        jax.ShapeDtypeStruct((dp, rows.shape[1], rows.shape[2] // dp), BF16),
    )
    return pl.pallas_call(
        finish_kernel,
        grid=(1,),
        in_specs=[pl.BlockSpec((1, *array.shape[1:]), lambda *_: (0, 0, 0)) for array in args]
        + [whole(residual)],
        out_specs=tuple(whole(shape) for shape in shapes),
        out_shape=shapes,
        compiler_params=params(16),
        cost_estimate=COST,
        name="finish",
    )(*args, residual)


class Group:
    def __init__(self):
        self.heads = lax.axis_size("head")
        self.dp = lax.axis_size("dp")
        self.ctx_at = lax.axis_index("ctx")
        self.head_at = lax.axis_index("head")
        self.dp_at = lax.axis_index("dp")
        self.at = self.ctx_at * self.heads + self.head_at
        near, far = [], []
        for c in range(2):
            for h in range(self.heads):
                x, y = (c ^ 1) * self.heads + h, c * self.heads + (h ^ 2)
                near.append((c * self.heads + h, x if h % 2 == 0 else y))
                far.append((c * self.heads + h, y if h % 2 == 0 else x))
        self.near, self.far = near, far

    def order(self):
        first = jnp.where(self.head_at % 2 == 0, 4, 2)
        second = 6 - first
        return jnp.stack(
            [self.at ^ bits for bits in (0, 1, first, first ^ 1, 6, second ^ 1, second, 7)]
        )

    def swap(self, values, bit):
        if bit == 4:
            return lax.ppermute(values, "ctx", [(0, 1), (1, 0)])
        return lax.ppermute(values, "head", [(i, i ^ bit) for i in range(self.heads)])

    def mate(self, values):
        return self.swap(values, 1)

    def to_near(self, values):
        return lax.ppermute(values, GROUP, self.near)

    def to_far(self, values):
        return lax.ppermute(values, GROUP, self.far)

    def rows_back(self, values, place):
        pairs, same = [], False
        for d in range(self.dp):
            for h in range(self.heads):
                if (d, h) == (place[h], d):
                    same = same | ((self.dp_at == d) & (self.head_at == h))
                else:
                    pairs.append((d * self.heads + h, place[h] * self.heads + d))
        return jnp.where(same, values, lax.ppermute(values, ("dp", "head"), pairs))

    def across(self, values, step):
        return lax.ppermute(values, "dp", [(i, i ^ step) for i in range(self.dp)])


def pick(array, index, axis):
    return lax.dynamic_index_in_dim(array, index, axis, keepdims=False)


def after(values, *earlier):
    return lax.optimization_barrier((values, earlier))[0]


def local_split(tokens, cotangent, w_qkv, w_attn_out, w_in, w_mlp_out, norm_gain1, norm_gain2):
    seqs, block, width = tokens.shape
    group = Group()
    heads, dp = group.heads, group.dp
    at_c, at_h = group.ctx_at, group.head_at
    parts = 2 * heads
    hidden = w_in.shape[1] // 2 // parts
    padded = -(-hidden // 128) * 128
    own_width = width // parts
    half = heads // 2
    rows_here = w_qkv.shape[0]
    place = [2 * (h % half) + h // half for h in range(heads)]
    straight = list(range(heads))
    order = group.order()
    scalars = jnp.concatenate([order, jnp.stack([group.dp_at, at_c])]).astype(jnp.int32)
    mate, near, far = group.mate, group.to_near, group.to_far

    def in_order(own, other):
        return jnp.where(at_c == 0, jnp.stack([own, other]), jnp.stack([other, own]))

    def exchange(values):
        return lax.all_to_all(values, GROUP, split_axis=0, concat_axis=0, tiled=True)


    gains = jnp.pad(
        jnp.stack([norm_gain1, norm_gain2]), ((0, 14), (0, 3 * own_width - rows_here))
    )
    qkv_view = w_qkv.reshape(rows_here, 3, width)

    def qkv_part(at):
        start = (2 * at_h + at) * own_width
        cut = lax.dynamic_slice_in_dim(qkv_view, start, own_width, 2)
        return jnp.concatenate([cut.reshape(rows_here, 3 * own_width), gains])

    x_own = tokens[None]
    x_mate = mate(x_own)
    qkv_other, qkv_own = qkv_part(1 - at_c), qkv_part(at_c)
    qkv_cross = group.swap(after(qkv_other, x_own), 4)
    in_view = after(w_in, qkv_other).reshape(rows_here, 2, heads, 2, hidden)
    in_view = pick(in_view, 2 * (at_h % half) + at_h // half, 2)

    def in_part(at):
        cut = pick(in_view, at, 2)
        return jnp.pad(cut, ((0, 0), (0, 0), (0, padded - hidden))).reshape(rows_here, 2 * padded)

    in_other, in_own = in_part(1 - at_c), in_part(at_c)
    in_cross = group.swap(after(in_other, qkv_cross), 4)
    x_chip = jnp.concatenate([x_own, after(x_mate, qkv_cross, qkv_own)])
    x_near = near(x_chip)
    qkv_pair = jnp.stack([qkv_own, qkv_cross])
    qkv_pieces = [qkv_pair] + [group.across(qkv_pair, step) for step in range(1, dp)]

    positions = after(order, qkv_pair)[:, None] * block + jnp.arange(block, dtype=jnp.int32)
    lane = jnp.arange(own_width, dtype=jnp.int32)
    frequency = jnp.exp(
        (lane % (HD // 2)).astype(F32) * (-math.log(ROPE_BASE) / (HD // 2))
    )
    angles = wide(positions.reshape(-1))[:, None] * frequency[None, :]
    cosine = jnp.cos(angles)
    sine = jnp.sin(angles) * jnp.where(lane % HD < HD // 2, -1.0, 1.0)[None, :]

    x_far = far(x_near[:1])
    slices = jnp.concatenate([w_attn_out, w_mlp_out])
    slices = after(slices, x_far, in_other, in_own, cosine, sine, *qkv_pieces)
    slices = lax.dynamic_slice_in_dim(slices, at_h * (width // heads), width // heads, 1)
    slices = jnp.pad(slices, ((0, 64), (0, 0)))
    slices = lax.all_gather(slices, "dp", axis=0)
    x_near = after(x_near, *qkv_pieces, cosine, sine, in_cross, in_own)
    x_near_mate = mate(x_near)
    cot_own = after(cotangent, x_near)[None]
    cot_mate = mate(cot_own)
    in_pair, x_far = lax.optimization_barrier((in_order(in_own, in_cross), x_far))
    weight_in = lax.all_gather(in_pair, "dp", axis=0).reshape(width, -1)
    cot_chip = jnp.concatenate([cot_own, cot_mate])
    x_far = after(x_far, cot_chip)
    x_far_mate = mate(x_far)

    cot_near = near(after(cot_chip, x_far))
    out_rows = w_attn_out.shape[0]
    x_pieces = (x_own, x_mate, x_near, x_far, x_near_mate, x_far_mate)
    low1, qkv, weight_qkv, gain_one, gain_two = project(
        scalars, x_pieces, qkv_pieces, cosine, sine
    )

    att_0, log_0, home_0 = attend(scalars, qkv)
    cot_near = after(cot_near, home_0)
    cot_far, cot_near_mate = far(cot_near[:1]), mate(cot_near)
    slices = after(slices, home_0)
    out_own = slices[:, :out_rows].reshape(1, dp * out_rows, -1)
    out_mate = mate(out_own)
    out_chip = jnp.concatenate([out_own, out_mate])
    out_near = near(out_chip)
    mlp_slices = jnp.stack(
        [slices[place[h], out_rows : out_rows + hidden] for h in range(heads)]
    )
    mlp_slices = lax.all_to_all(mlp_slices, "head", split_axis=0, concat_axis=0, tiled=True)
    att_1, log_1, home = attend(scalars, after(qkv, cot_near, out_chip), home_0)
    home, cot_far, out_near = lax.optimization_barrier((home, cot_far, out_near))
    att_rows = exchange(home)
    out_far, out_near_mate = far(out_near[:1]), mate(out_near)
    out_far_mate, cot_far_mate = mate(after(out_far, home)), mate(after(cot_far, home))
    out_pieces = (out_own, out_mate, out_near, out_far, out_near_mate, out_far_mate)
    weight_mlp = jnp.moveaxis(after(mlp_slices, home), 0, 1).reshape(hidden, width)
    weight_mlp = jnp.pad(weight_mlp, ((0, padded - hidden), (0, 0)))
    residual, low2 = branch(
        scalars, out_pieces, after(att_rows, cot_far_mate, weight_mlp, weight_in), tokens, gain_two
    )

    low_own = low2[None]
    low_mate = mate(low_own)
    low_near = near(jnp.concatenate([low_own, low_mate]))
    *arrays, keep_a = mlp(
        (low_own, low_mate), (cot_own, cot_mate), weight_in, weight_mlp, 0, (2,)
    )
    low_near = after(low_near, keep_a)
    low_far, low_near_mate = far(low_near[:1]), mate(low_near)
    *arrays, keep_b = mlp((low_near,), (cot_near,), weight_in, weight_mlp, 2, (2,), arrays)
    low_far_mate = mate(after(low_far, keep_b))
    low2_all, cot_all, mixed, grad_lifted, keep_c, send = mlp(
        (low_far, low_near_mate, low_far_mate),
        (cot_far, cot_near_mate, cot_far_mate),
        weight_in,
        weight_mlp,
        4,
        (1, 4),
        arrays,
    )

    def over_tokens(left, right):
        return dot(flat(left), flat(right), ((0,), (0,)))

    def scatter(values):
        return lax.psum_scatter(values.astype(BF16), "dp", scatter_dimension=0, tiled=True)

    def columns_first(values):
        return jnp.moveaxis(values.reshape(values.shape[0], dp, -1), 1, 0)

    rows = seqs * block

    def by_rows(values):
        return values.reshape(values.shape[0], -1, width)

    keep_a, keep_b, keep_c, send = (by_rows(array) for array in (keep_a, keep_b, keep_c, send))
    met = mate(send)
    last = combine([(rows, [(keep_c, 0, 0), (met, 2, 0)])])
    last_far = far(last)
    grad_mlp = columns_first(over_tokens(after(mixed, last), cot_all)[:hidden]).astype(BF16)
    last_far = after(last_far, grad_mlp)
    grad_mlp = scatter(grad_mlp)[0]
    chip = combine(
        [(rows, [(keep_b, 0, 0), (met, 0, 0), (last_far, 0, 0)])],
        [(rows, [(keep_b, 1, 0), (met, 1, 0)])],
    )
    chip_near = near(chip)
    grad_in = over_tokens(low2_all, after(grad_lifted, chip)).astype(BF16)
    cut = 5 * rows
    mixed_flat = flat(after(mixed, chip))
    out_keep = dot(mixed_flat[:cut], weight_mlp).astype(BF16).reshape(5, rows, width)
    out_send = dot(mixed_flat[cut:], weight_mlp).astype(BF16).reshape(3, rows, width)
    chip_near = after(chip_near, grad_in, out_keep, out_send)
    grad_in = scatter(grad_in)
    home = mate(combine([(rows, [(keep_a, 1, 0), (chip_near, 1, 0)])])[0])
    out_met = mate(after(out_send, chip_near))
    grad_residual, grad_branch, home, gain2_sum = branch_back(
        scalars, out_pieces, keep_a, chip_near, home, residual, cotangent, gain_two
    )
    grad_home = exchange(home)

    rows_keep, rows_send = out_grad(scalars, after(att_rows, home), grad_branch)
    rows_met = mate(rows_send)
    few = rows_keep.shape[1]

    def ends(index, at, *more):
        kept = [(out_keep, index, 0)], [(rows_keep, index, 0)]
        if at is not None:
            kept[0].append((out_met, at, 0))
            kept[1].append((rows_met, at, 0))
        for array, where in more:
            kept[0].append((array, where, 0))
            kept[1].append((array, where, rows))
        return [(rows, kept[0]), (few, kept[1])]

    end_last = combine(ends(4, 2))
    grad_home = after(grad_home, end_last, grad_mlp)
    end_far = far(after(end_last, grad_home))
    keep_0, send_0, before = attend_back(
        scalars, qkv, grad_home, att_0, log_0, cosine, sine, weight_qkv, low1, 0
    )
    met_0 = mate(send_0)
    end_far = after(end_far, send_0)
    end_chip = combine(ends(2, 0, (end_far, 0)), ends(3, 1))
    end_near = near(end_chip)
    keep_1, send_1, grad_qkv = attend_back(
        scalars, qkv, after(grad_home, end_chip), att_1, log_1, cosine, sine,
        weight_qkv, low1, 1, before, gain_one, gain2_sum, dp=dp,
    )

    grad_qkv = scatter(grad_qkv.reshape(-1, grad_qkv.shape[2]))
    met_1 = mate(send_1)
    end_home = combine(ends(1, None, (after(end_near, send_1), 1)))
    in_parts = after(grad_in, send_1).reshape(2, rows_here, -1)
    in_other = pick(in_parts, 1 - at_c, 0)
    met_1, end_home, in_other = lax.optimization_barrier((met_1, end_home, in_other))
    in_cross = group.swap(in_other, 4)
    end_home = mate(end_home)

    def both(index, at, *more):
        kept = [(keep_0, index, 0)], [(keep_1, index, 0)]
        if at is not None:
            kept[0].append((met_0, at, 0))
            kept[1].append((met_1, at, 0))
        for array, where in more:
            kept[0].append((array, where, 0))
            kept[1].append((array, where, block))
        return [(block, kept[0]), (block, kept[1])]

    last = combine(both(4, 2))
    last_far = far(last)
    result, grad_out = finish(
        out_keep, rows_keep, end_near, after(end_home, last), residual, dp
    )
    last_far, grad_out = lax.optimization_barrier((after(last_far, in_cross), grad_out))
    grad_out = scatter(grad_out)[0]
    chip = combine(both(2, 0, (last_far, 0)), both(3, 1), mebibytes=60)
    chip_near = near(chip)

    grad_in = in_order(after(pick(in_parts, at_c, 0), chip), in_cross)
    late = at_h // half
    grad_in = jnp.stack([grad_in[..., :hidden], grad_in[..., padded : padded + hidden]])
    stays = pick(grad_in, late, 0)
    comes = group.swap(pick(grad_in, 1 - late, 0), half)
    grad_qkv = after(grad_qkv, chip)
    both_rows = 2 * rows_here
    qkv_parts = grad_qkv[:both_rows].reshape(2, rows_here, -1)
    gains = grad_qkv[both_rows:]
    cross = jnp.concatenate([pick(qkv_parts, 1 - at_c, 0), gains])
    cross = group.swap(cross, 4)
    chip_near = after(chip_near, comes, cross)
    home = combine(both(1, None, (chip_near, 1)))
    cross = after(cross, home)
    home = mate(home)
    grad_qkv = in_order(pick(qkv_parts, at_c, 0), cross[:rows_here])
    gains = (wide(gains) + wide(cross[rows_here:])).astype(BF16)
    gains = wide(gains) + sum(wide(group.swap(gains, bit)) for bit in range(1, heads))
    grad_input = input_grad((keep_0, keep_1), chip_near, home, tokens, grad_residual, gain_one)
    grad_out, grad_mlp, grad_input = lax.optimization_barrier((grad_out, grad_mlp, grad_input))
    grad_mlp = group.rows_back(grad_mlp, place)
    grad_out = wide(group.rows_back(grad_out, straight))

    grad_mlp = wide(grad_mlp)
    grad_in = jnp.where(
        late == 0, jnp.concatenate([stays, comes]), jnp.concatenate([comes, stays])
    )
    grad_in = wide(jnp.moveaxis(grad_in, 0, 1).reshape(rows_here, -1))

    per_device = width // (dp * parts)
    start = group.at * per_device
    grad_gain1, grad_gain2 = (
        lax.dynamic_slice_in_dim(gains[i], start, per_device, 0) for i in range(2)
    )
    grad_qkv = grad_qkv.reshape(2, rows_here, 3, own_width)
    grad_qkv = jnp.moveaxis(grad_qkv, 2, 0)
    odd = at_h % 2
    stays = pick(grad_qkv, odd + late, 0)
    core = group.swap(pick(grad_qkv, 1 - odd + late, 0), 1)
    chip = group.swap(pick(grad_qkv, 2 - 2 * late, 0), 2)
    grad_qkv = jnp.where(
        odd == 0, jnp.concatenate([stays, core, chip]), jnp.concatenate([chip, core, stays])
    )
    grad_qkv = wide(jnp.moveaxis(grad_qkv, 0, 1).reshape(rows_here, -1))

    return (
        result,
        grad_input,
        grad_qkv,
        grad_out,
        grad_in,
        grad_mlp,
        grad_gain1,
        grad_gain2,
    )


def local(tokens, cotangent, w_qkv, w_attn_out, w_in, w_mlp_out, norm_gain1, norm_gain2):
    args = (tokens, cotangent, w_qkv, w_attn_out, w_in, w_mlp_out, norm_gain1, norm_gain2)
    sizes = [lax.axis_size(axis) for axis in ("dp", "ctx", "head")]
    if sizes == [4, 2, 4] and tokens.shape[2] == 8 * 2 * HD and tokens.shape[1] % 16 == 0:
        return local_split(*args)
    return local_general(*args)


def solution(mesh):
    in_specs = (
        P("dp", ("ctx", "head"), None),
        P("dp", ("ctx", "head"), None),
        P(("dp", "ctx"), None),
        P(("dp", "ctx"), None),
        P(("dp", "ctx"), None),
        P(("dp", "ctx"), None),
        P(("dp", "ctx")),
        P(("dp", "ctx")),
    )
    out_specs = (
        P("dp", ("ctx", "head"), None),
        P("dp", ("ctx", "head"), None),
        P(("dp", "ctx"), "head"),
        P(("dp", "ctx"), "head"),
        P(("dp", "ctx"), "head"),
        P(("dp", "ctx"), "head"),
        P(("dp", "ctx", "head")),
        P(("dp", "ctx", "head")),
    )
    return jax.shard_map(local, mesh=mesh, in_specs=in_specs, out_specs=out_specs, check_vma=False)
```

```python
import functools
import math

import jax
import jax.numpy as jnp
from jax import lax
from jax.experimental import pallas as pl
from jax.experimental.pallas import tpu as pltpu
from jax.sharding import PartitionSpec as P

HD = 64


EPSILON = 1e-05
ROPE_BASE = 160000.0


def normalize(values):
    centre = jnp.mean(values, axis=-1, keepdims=True)
    shifted = values - centre
    spread = jnp.mean(shifted * shifted, axis=-1, keepdims=True)
    factor = lax.rsqrt(spread + EPSILON)
    return (shifted * factor, factor)


def norm_back(grad_normed, normed, factor):
    grad_centre = jnp.mean(grad_normed, axis=-1, keepdims=True)
    grad_along = jnp.mean(grad_normed * normed, axis=-1, keepdims=True)
    return (grad_normed - grad_centre - normed * grad_along) * factor


def rope_tables(positions, half_size):
    frequency = jnp.exp(
        jnp.arange(half_size, dtype=jnp.float32) * (-math.log(ROPE_BASE) / half_size)
    )
    angles = positions[:, None] * frequency[None, :]
    return (jnp.cos(angles), jnp.sin(angles))


def rotate(values, cosine, sine_table, direction):
    half_size = cosine.shape[-1]
    first_half = values[..., :half_size]
    second_half = values[..., half_size:]
    cos_part = cosine[:, None, :]
    sin_part = sine_table[:, None, :] * direction
    return jnp.concatenate(
        [
            first_half * cos_part - second_half * sin_part,
            second_half * cos_part + first_half * sin_part,
        ],
        axis=-1,
    )


def block_scores(queries4, keys_block, scale):
    keys4 = keys_block.reshape(
        keys_block.shape[0], keys_block.shape[1], queries4.shape[2], queries4.shape[3]
    )
    return (
        jnp.einsum("sqgd,skgd->sgqk", queries4, keys4, preferred_element_type=jnp.float32) * scale
    )


def attend_forward(queries4, keys_all, values_all, key_rows, scale):
    seqs_here, query_rows, groups, head_size = queries4.shape
    turns = keys_all.shape[1] // key_rows

    def statistics(turn, carry):
        row_peak, row_total = carry
        keys_block = lax.dynamic_slice_in_dim(keys_all, turn * key_rows, key_rows, 1)
        scores = block_scores(queries4, keys_block, scale)
        new_peak = jnp.maximum(row_peak, jnp.max(scores, axis=-1))
        row_total = row_total * jnp.exp(row_peak - new_peak) + jnp.sum(
            jnp.exp(scores - new_peak[..., None]), axis=-1
        )
        return (new_peak, row_total)

    start_peak = jnp.full((seqs_here, groups, query_rows), -1e30, jnp.float32)
    row_peak, row_total = lax.fori_loop(
        0, turns, statistics, (start_peak, jnp.zeros_like(start_peak))
    )
    log_total = row_peak + jnp.log(row_total)

    def accumulate(turn, running):
        keys_block = lax.dynamic_slice_in_dim(keys_all, turn * key_rows, key_rows, 1)
        values_block = lax.dynamic_slice_in_dim(values_all, turn * key_rows, key_rows, 1).reshape(
            seqs_here, key_rows, groups, head_size
        )
        weights = jnp.exp(block_scores(queries4, keys_block, scale) - log_total[..., None]).astype(
            jnp.bfloat16
        )
        return running + jnp.einsum(
            "sgqk,skgd->sqgd", weights, values_block, preferred_element_type=jnp.float32
        )

    attended = lax.fori_loop(
        0, turns, accumulate, jnp.zeros((seqs_here, query_rows, groups, head_size), jnp.float32)
    )
    return (attended, log_total)


def attend_backward(queries4, keys_all, values_all, grad_out4, log_total, along, key_rows, scale):
    seqs_here, query_rows, groups, head_size = queries4.shape
    length = keys_all.shape[1]
    width_group = groups * head_size
    turns = length // key_rows

    def step_back(turn, carry):
        grad_queries, grad_keys, grad_values = carry
        keys_block = lax.dynamic_slice_in_dim(keys_all, turn * key_rows, key_rows, 1)
        keys4 = keys_block.reshape(seqs_here, key_rows, groups, head_size)
        values4 = lax.dynamic_slice_in_dim(values_all, turn * key_rows, key_rows, 1).reshape(
            seqs_here, key_rows, groups, head_size
        )
        weights = jnp.exp(block_scores(queries4, keys_block, scale) - log_total[..., None])
        grad_weights = jnp.einsum(
            "sqgd,skgd->sgqk", grad_out4, values4, preferred_element_type=jnp.float32
        )
        grad_scores = (weights * (grad_weights - along[..., None])).astype(jnp.bfloat16)
        grad_queries = grad_queries + jnp.einsum(
            "sgqk,skgd->sqgd", grad_scores, keys4, preferred_element_type=jnp.float32
        )
        key_part = (
            jnp.einsum("sgqk,sqgd->skgd", grad_scores, queries4, preferred_element_type=jnp.float32)
            * scale
        )
        value_part = jnp.einsum(
            "sgqk,sqgd->skgd",
            weights.astype(jnp.bfloat16),
            grad_out4,
            preferred_element_type=jnp.float32,
        )
        grad_keys = lax.dynamic_update_slice_in_dim(
            grad_keys, key_part.reshape(seqs_here, key_rows, width_group), turn * key_rows, 1
        )
        grad_values = lax.dynamic_update_slice_in_dim(
            grad_values, value_part.reshape(seqs_here, key_rows, width_group), turn * key_rows, 1
        )
        return (grad_queries, grad_keys, grad_values)

    start = (
        jnp.zeros((seqs_here, query_rows, groups, head_size), jnp.float32),
        jnp.zeros((seqs_here, length, width_group), jnp.float32),
        jnp.zeros((seqs_here, length, width_group), jnp.float32),
    )
    grad_queries, grad_keys, grad_values = lax.fori_loop(0, turns, step_back, start)
    return (grad_queries * scale, grad_keys, grad_values)


def local_general(tokens, cotangent, w_qkv, w_attn_out, w_in, w_mlp_out, norm_gain1, norm_gain2):
    seqs_here, block_rows, width = tokens.shape
    count_rows = seqs_here * block_rows
    heads_all = width // HD
    head_devices = lax.axis_size("head")
    group_devices = lax.axis_size(("dp", "ctx"))
    groups = heads_all // head_devices
    width_group = groups * HD
    scale = HD ** (-0.5)
    ff_width = w_in.shape[1] // 2
    full_qkv, full_out, full_in, full_mlp, gain_one, gain_two = (
        lax.all_gather(w_qkv, ("dp", "ctx"), axis=0, tiled=True),
        lax.all_gather(w_attn_out, ("dp", "ctx"), axis=0, tiled=True),
        lax.all_gather(w_in, ("dp", "ctx"), axis=0, tiled=True),
        lax.all_gather(w_mlp_out, ("dp", "ctx"), axis=0, tiled=True),
        lax.all_gather(norm_gain1, ("dp", "ctx"), axis=0, tiled=True),
        lax.all_gather(norm_gain2, ("dp", "ctx"), axis=0, tiled=True),
    )
    x_in = tokens.astype(jnp.float32).reshape(count_rows, width)
    normed1, factor1 = normalize(x_in)
    lowered1 = (normed1 * gain_one.astype(jnp.float32)).astype(jnp.bfloat16)
    projected = jnp.dot(lowered1, full_qkv, preferred_element_type=jnp.float32).reshape(
        seqs_here, block_rows, 3, heads_all, HD
    )
    first_pos = (lax.axis_index("ctx") * head_devices + lax.axis_index("head")) * block_rows
    positions = (first_pos + jnp.arange(block_rows, dtype=jnp.int32)).astype(jnp.float32)
    cosine, sine_table = rope_tables(positions, HD // 2)
    queries = (
        rotate(projected[:, :, 0], cosine, sine_table, 1.0)
        .astype(jnp.bfloat16)
        .reshape(seqs_here, block_rows, width)
    )
    keys_local = (
        rotate(projected[:, :, 1], cosine, sine_table, 1.0)
        .astype(jnp.bfloat16)
        .reshape(seqs_here, block_rows, width)
    )
    values_local = projected[:, :, 2].astype(jnp.bfloat16).reshape(seqs_here, block_rows, width)
    queries_h, keys_h, values_h = (
        lax.all_to_all(queries, "head", split_axis=2, concat_axis=1, tiled=True),
        lax.all_to_all(keys_local, "head", split_axis=2, concat_axis=1, tiled=True),
        lax.all_to_all(values_local, "head", split_axis=2, concat_axis=1, tiled=True),
    )
    query_rows = queries_h.shape[1]
    queries4 = queries_h.reshape(seqs_here, query_rows, groups, HD)
    keys_all, values_all = (
        lax.all_gather(keys_h, "ctx", axis=1, tiled=True),
        lax.all_gather(values_h, "ctx", axis=1, tiled=True),
    )
    key_rows = math.gcd(keys_all.shape[1], 1024)
    attended, log_total = attend_forward(queries4, keys_all, values_all, key_rows, scale)
    attended_low = attended.astype(jnp.bfloat16).reshape(seqs_here, query_rows, width_group)
    back_rows = lax.all_to_all(
        attended_low, "head", split_axis=1, concat_axis=2, tiled=True
    ).reshape(count_rows, width)
    residual = x_in + jnp.dot(back_rows, full_out, preferred_element_type=jnp.float32)
    normed2, factor2 = normalize(residual)
    lowered2 = (normed2 * gain_two.astype(jnp.float32)).astype(jnp.bfloat16)
    lifted = jnp.dot(lowered2, full_in, preferred_element_type=jnp.float32)
    first_part = lifted[:, :ff_width]
    second_part = lifted[:, ff_width:]
    activated, gelu_pullback = jax.vjp(
        lambda entries: jax.nn.gelu(entries, approximate=False), first_part
    )
    mixed = (activated * second_part).astype(jnp.bfloat16)
    result = (residual + jnp.dot(mixed, full_mlp, preferred_element_type=jnp.float32)).astype(
        jnp.bfloat16
    )
    full_qkv, full_out, full_in, full_mlp, gain_one, gain_two = (
        lax.all_gather(w_qkv, ("dp", "ctx"), axis=0, tiled=True),
        lax.all_gather(w_attn_out, ("dp", "ctx"), axis=0, tiled=True),
        lax.all_gather(w_in, ("dp", "ctx"), axis=0, tiled=True),
        lax.all_gather(w_mlp_out, ("dp", "ctx"), axis=0, tiled=True),
        lax.all_gather(norm_gain1, ("dp", "ctx"), axis=0, tiled=True),
        lax.all_gather(norm_gain2, ("dp", "ctx"), axis=0, tiled=True),
    )
    keys_all, values_all = (
        lax.all_gather(keys_h, "ctx", axis=1, tiled=True),
        lax.all_gather(values_h, "ctx", axis=1, tiled=True),
    )
    grad_top = cotangent.reshape(count_rows, width)
    grad_mlp = jnp.einsum("nf,nd->fd", mixed, grad_top, preferred_element_type=jnp.float32)
    grad_mixed = jnp.einsum("nd,fd->nf", grad_top, full_mlp, preferred_element_type=jnp.float32)
    grad_first = gelu_pullback(grad_mixed * second_part)[0]
    grad_lifted = jnp.concatenate([grad_first, grad_mixed * activated], axis=-1).astype(
        jnp.bfloat16
    )
    grad_inner = jnp.einsum("nd,nf->df", lowered2, grad_lifted, preferred_element_type=jnp.float32)
    grad_lowered2 = jnp.einsum(
        "nf,df->nd", grad_lifted, full_in, preferred_element_type=jnp.float32
    )
    grad_two = jnp.sum(grad_lowered2 * normed2, axis=0)
    grad_residual = grad_top.astype(jnp.float32) + norm_back(
        grad_lowered2 * gain_two.astype(jnp.float32), normed2, factor2
    )
    grad_branch = grad_residual.astype(jnp.bfloat16)
    grad_outproj = jnp.einsum(
        "nd,ne->de", back_rows, grad_branch, preferred_element_type=jnp.float32
    )
    grad_attended = jnp.einsum(
        "ne,de->nd", grad_branch, full_out, preferred_element_type=jnp.float32
    ).astype(jnp.bfloat16)
    grad_attended_h = lax.all_to_all(
        grad_attended.reshape(seqs_here, block_rows, width),
        "head",
        split_axis=2,
        concat_axis=1,
        tiled=True,
    )
    grad_out4 = grad_attended_h.reshape(seqs_here, query_rows, groups, HD)
    along = jnp.transpose(jnp.sum(grad_out4.astype(jnp.float32) * attended, axis=-1), (0, 2, 1))
    grad_queries, grad_keys_all, grad_values_all = attend_backward(
        queries4, keys_all, values_all, grad_out4, log_total, along, key_rows, scale
    )
    grad_keys_sum, grad_values_sum = (
        lax.psum_scatter(
            grad_keys_all.astype(jnp.bfloat16), "ctx", scatter_dimension=1, tiled=True
        ).astype(jnp.float32),
        lax.psum_scatter(
            grad_values_all.astype(jnp.bfloat16), "ctx", scatter_dimension=1, tiled=True
        ).astype(jnp.float32),
    )
    grad_q_low = grad_queries.astype(jnp.bfloat16).reshape(seqs_here, query_rows, width_group)
    grad_q_tok, grad_k_tok, grad_v_tok = (
        lax.all_to_all(grad_q_low, "head", split_axis=1, concat_axis=2, tiled=True),
        lax.all_to_all(
            grad_keys_sum.astype(jnp.bfloat16), "head", split_axis=1, concat_axis=2, tiled=True
        ),
        lax.all_to_all(
            grad_values_sum.astype(jnp.bfloat16), "head", split_axis=1, concat_axis=2, tiled=True
        ),
    )
    unrot_q = rotate(
        grad_q_tok.astype(jnp.float32).reshape(seqs_here, block_rows, heads_all, HD),
        cosine,
        sine_table,
        -1.0,
    )
    unrot_k = rotate(
        grad_k_tok.astype(jnp.float32).reshape(seqs_here, block_rows, heads_all, HD),
        cosine,
        sine_table,
        -1.0,
    )
    grad_projected = jnp.concatenate(
        [
            unrot_q.reshape(count_rows, width),
            unrot_k.reshape(count_rows, width),
            grad_v_tok.astype(jnp.float32).reshape(count_rows, width),
        ],
        axis=-1,
    ).astype(jnp.bfloat16)
    grad_project = jnp.einsum(
        "nd,nf->df", lowered1, grad_projected, preferred_element_type=jnp.float32
    )
    grad_lowered1 = jnp.einsum(
        "nf,df->nd", grad_projected, full_qkv, preferred_element_type=jnp.float32
    )
    grad_one = jnp.sum(grad_lowered1 * normed1, axis=0)
    grad_input = grad_residual + norm_back(
        grad_lowered1 * gain_one.astype(jnp.float32), normed1, factor1
    )
    pieces_one = grad_one.reshape(group_devices, head_devices, -1)
    pieces_two = grad_two.reshape(group_devices, head_devices, -1)
    part_qkv, part_out, part_in, part_mlp, part_one, part_two = (
        lax.psum_scatter(
            grad_project.astype(jnp.bfloat16), ("dp", "ctx"), scatter_dimension=0, tiled=True
        ).astype(jnp.float32),
        lax.psum_scatter(
            grad_outproj.astype(jnp.bfloat16), ("dp", "ctx"), scatter_dimension=0, tiled=True
        ).astype(jnp.float32),
        lax.psum_scatter(
            grad_inner.astype(jnp.bfloat16), ("dp", "ctx"), scatter_dimension=0, tiled=True
        ).astype(jnp.float32),
        lax.psum_scatter(
            grad_mlp.astype(jnp.bfloat16), ("dp", "ctx"), scatter_dimension=0, tiled=True
        ).astype(jnp.float32),
        lax.psum_scatter(
            pieces_one.astype(jnp.bfloat16), ("dp", "ctx"), scatter_dimension=0, tiled=True
        ).astype(jnp.float32),
        lax.psum_scatter(
            pieces_two.astype(jnp.bfloat16), ("dp", "ctx"), scatter_dimension=0, tiled=True
        ).astype(jnp.float32),
    )
    final_qkv, final_out, final_in, final_mlp, final_one, final_two = (
        lax.psum_scatter(
            part_qkv.astype(jnp.bfloat16), "head", scatter_dimension=1, tiled=True
        ).astype(jnp.float32),
        lax.psum_scatter(
            part_out.astype(jnp.bfloat16), "head", scatter_dimension=1, tiled=True
        ).astype(jnp.float32),
        lax.psum_scatter(
            part_in.astype(jnp.bfloat16), "head", scatter_dimension=1, tiled=True
        ).astype(jnp.float32),
        lax.psum_scatter(
            part_mlp.astype(jnp.bfloat16), "head", scatter_dimension=1, tiled=True
        ).astype(jnp.float32),
        lax.psum_scatter(
            part_one.astype(jnp.bfloat16), "head", scatter_dimension=1, tiled=True
        ).astype(jnp.float32),
        lax.psum_scatter(
            part_two.astype(jnp.bfloat16), "head", scatter_dimension=1, tiled=True
        ).astype(jnp.float32),
    )
    return (
        result.reshape(seqs_here, block_rows, width),
        grad_input.reshape(seqs_here, block_rows, width),
        final_qkv,
        final_out,
        final_in,
        final_mlp,
        final_one.reshape(-1),
        final_two.reshape(-1),
    )


F32 = jnp.float32
BF16 = jnp.bfloat16
GROUP = ("ctx", "head")


def dot(left, right, dims=((1,), (0,))):
    return lax.dot_general(left, right, (dims, ((), ())), preferred_element_type=F32)


def wide(values):
    return values.astype(F32)


def flat(values):
    return values.reshape(-1, values.shape[-1])


def lane_rotate(values, cosine, sine_signed):
    lane = lax.broadcasted_iota(jnp.int32, values.shape, 1)
    width = values.shape[1]
    partner = jnp.where(
        lane % HD < HD // 2,
        pltpu.roll(values, width - HD // 2, 1),
        pltpu.roll(values, HD // 2, 1),
    )
    return values * cosine + partner * sine_signed


def head_masks(shape):
    lane = lax.broadcasted_iota(jnp.int32, shape, 1)
    return [lane // HD == head for head in range(shape[1] // HD)]


def params(mebibytes):
    return pltpu.CompilerParams(vmem_limit_bytes=mebibytes * 1024 * 1024)


COST = pl.CostEstimate(flops=1 << 20, transcendentals=0, bytes_accessed=1 << 16)


def whole(array):
    return pl.BlockSpec(array.shape, lambda *_: (0,) * len(array.shape))


SCALARS = pl.BlockSpec(memory_space=pltpu.SMEM)


def project_kernel(place_ref, *refs):
    pieces, weights = refs[:6], refs[6:10]
    cos_ref, sin_ref, low_ref, qkv_ref, w_ref, gain1_ref, gain2_ref, rows_ref = refs[10:]
    block, part = pieces[0].shape[2], w_ref.shape[1] // 3
    rows = gain1_ref.shape[1] // 8

    @pl.when(pl.program_id(0) == 0)
    def _():
        for step, piece in enumerate(weights):
            for turn in range(2):
                at = 2 * (place_ref[8] ^ step) + (place_ref[9] ^ turn)
                w_ref[pl.ds(pl.multiple_of(at * rows, rows), rows), :] = piece[turn, :rows]
                gains = piece[turn, rows:].astype(F32)
                rows_ref[0, pl.ds(at, 1), :] = gains[:1, :rows]
                rows_ref[1, pl.ds(at, 1), :] = gains[1:2, :rows]
        for out, at in ((gain1_ref, 0), (gain2_ref, 1)):
            for row in range(8):
                out[:, row * rows : (row + 1) * rows] = rows_ref[at, row : row + 1, :]

    gain = gain1_ref[...]
    index = 0
    for piece in pieces:
        for inner in range(piece.shape[0]):
            normed, _ = normalize(piece[inner, 0].astype(F32))
            low_ref[index, 0] = (normed * gain).astype(BF16)
            index += 1
    projected = dot(flat(low_ref[:, 0]), w_ref[...])
    cosine, sine = cos_ref[...], sin_ref[...]
    shape = (8, block, part)
    qkv_ref[:, 0, :, :part] = (
        (lane_rotate(projected[:, :part], cosine, sine) * HD**-0.5).astype(BF16).reshape(shape)
    )
    qkv_ref[:, 0, :, part : 2 * part] = (
        lane_rotate(projected[:, part : 2 * part], cosine, sine).astype(BF16).reshape(shape)
    )
    qkv_ref[:, 0, :, 2 * part :] = projected[:, 2 * part :].astype(BF16).reshape(shape)


def project(place, pieces, weights, cosine, sine):
    seqs, block, width = pieces[0].shape[1:]
    own = weights[0].shape[2]

    def by_seq(lead, last):
        return pl.BlockSpec((lead, 1, block, last), lambda s: (0, s, 0, 0))

    return pl.pallas_call(
        project_kernel,
        grid=(seqs,),
        in_specs=[SCALARS]
        + [by_seq(piece.shape[0], width) for piece in pieces]
        + [whole(w) for w in weights]
        + [whole(cosine), whole(sine)],
        out_specs=(
            by_seq(8, width),
            by_seq(8, own),
            pl.BlockSpec((width, own), lambda s: (0, 0)),
            pl.BlockSpec((1, width), lambda s: (0, 0)),
            pl.BlockSpec((1, width), lambda s: (0, 0)),
        ),
        out_shape=(
            jax.ShapeDtypeStruct((8, seqs, block, width), BF16),
            jax.ShapeDtypeStruct((8, seqs, block, own), BF16),
            jax.ShapeDtypeStruct((width, own), BF16),
            jax.ShapeDtypeStruct((1, width), F32),
            jax.ShapeDtypeStruct((1, width), F32),
        ),
        scratch_shapes=[pltpu.VMEM((2, 8, width // 8), F32)],
        compiler_params=params(60),
        cost_estimate=COST,
        name="project",
    )(place, *pieces, *weights, cosine, sine)


def attend_kernel(place_ref, q_ref, k_ref, v_ref, *refs):
    att_ref, log_ref, home_ref = refs[-3:]
    step, seq = pl.program_id(0), len(refs) - 3
    if seq:

        @pl.when(step == 0)
        def _():
            home_ref[:, :1] = refs[0][...]

    queries, keys, values = flat(q_ref[...]), flat(k_ref[...]), flat(v_ref[...])
    attended = jnp.zeros(queries.shape, F32)
    logs = jnp.zeros(queries.shape, F32)
    for mask in head_masks(queries.shape):
        scores = dot(jnp.where(mask, queries, 0), keys, ((1,), (1,)))
        peak = jnp.max(scores, axis=1, keepdims=True)
        weights = jnp.exp(scores - peak)
        total = jnp.sum(weights, axis=1, keepdims=True)
        mixed = dot(weights.astype(BF16), values) * (1.0 / total)
        attended = jnp.where(mask, mixed, attended)
        logs = jnp.where(mask, peak + jnp.log(total), logs)
    att_ref[...] = attended.reshape(att_ref.shape)
    log_ref[...] = logs.reshape(log_ref.shape)
    low = attended.astype(BF16).reshape(att_ref.shape)
    for inner in range(2):
        home_ref[place_ref[2 * step + inner], seq] = low[inner, 0]


def attend(place, qkv, *home):
    _, _, block, own = qkv.shape
    part, seq = own // 3, len(home)
    rows = pl.BlockSpec((2, 1, block, part), lambda i: (i, 0, 0, 0))
    shape = (8, 1, block, part)
    return pl.pallas_call(
        attend_kernel,
        grid=(4,),
        in_specs=[
            SCALARS,
            pl.BlockSpec((2, 1, block, part), lambda i: (i, seq, 0, 0)),
            pl.BlockSpec((8, 1, block, part), lambda i: (0, seq, 0, 1)),
            pl.BlockSpec((8, 1, block, part), lambda i: (0, seq, 0, 2)),
            *[whole(h) for h in home],
        ],
        out_specs=(
            rows,
            rows,
            pl.BlockSpec((8, 1 + seq, block, part), lambda i: (0, 0, 0, 0)),
        ),
        out_shape=(
            jax.ShapeDtypeStruct(shape, F32),
            jax.ShapeDtypeStruct(shape, F32),
            jax.ShapeDtypeStruct((8, 1 + seq, block, part), BF16),
        ),
        compiler_params=params(24),
        cost_estimate=COST,
        name="attend",
    )(place, qkv, qkv, qkv, *home)


def branch_kernel(place_ref, *refs):
    pieces = refs[:6]
    rows_ref, tokens_ref, gain_ref, residual_ref, low_ref, side_ref, total_ref = refs[6:]
    heads = rows_ref.shape[0] // 2
    for c in range(2):
        side_ref[c] = jnp.concatenate([flat(rows_ref[c * heads + d]) for d in range(heads)], axis=1)
    total_ref[...] = flat(wide(tokens_ref[...]))
    index = 0
    for piece in pieces:
        n = piece.shape[2]
        for inner in range(piece.shape[0]):
            at = place_ref[index]
            columns = pl.ds(pl.multiple_of((at % heads) * n, n), n)
            total_ref[:, columns] += dot(side_ref[at // heads], piece[inner])
            index += 1
    total = total_ref[...]
    normed, _ = normalize(total)
    residual_ref[...] = total.reshape(residual_ref.shape)
    low_ref[...] = (normed * gain_ref[...]).astype(BF16).reshape(low_ref.shape)


def branch(place, pieces, rows, tokens, gain):
    args = (*pieces, rows, tokens, gain)
    seqs, block, width = tokens.shape
    return pl.pallas_call(
        branch_kernel,
        in_specs=[SCALARS] + [whole(a) for a in args],
        out_shape=(
            jax.ShapeDtypeStruct(tokens.shape, F32),
            jax.ShapeDtypeStruct(tokens.shape, BF16),
        ),
        scratch_shapes=[
            pltpu.VMEM((2, seqs * block, pieces[0].shape[1]), BF16),
            pltpu.VMEM((seqs * block, width), F32),
        ],
        compiler_params=params(16),
        cost_estimate=COST,
        name="branch",
    )(place, *args)


def combine(*groups, mebibytes=16):
    parts = [part for group in groups for _, parts in group for part in parts]
    rows = sum(count for count, _ in groups[0])
    width = parts[0][0].shape[2]

    def kernel(*refs):
        at = 0
        for k, group in enumerate(groups):
            row = 0
            for count, terms in group:
                total = 0.0
                for _, _, start in terms:
                    total = total + wide(refs[at][0, start : start + count])
                    at += 1
                refs[-1][k, row : row + count] = total.astype(BF16)
                row += count

    return pl.pallas_call(
        kernel,
        grid=(1,),
        in_specs=[
            pl.BlockSpec((1, *array.shape[1:]), lambda *_, index=index: (index, 0, 0))
            for array, index, _ in parts
        ],
        out_specs=pl.BlockSpec((len(groups), rows, width), lambda *_: (0, 0, 0)),
        out_shape=jax.ShapeDtypeStruct((len(groups), rows, width), BF16),
        compiler_params=params(mebibytes),
        cost_estimate=COST,
        name="combine",
    )(*[array for array, _, _ in parts])


def mlp_kernel(*refs, count, ends):
    pieces, tops = refs[:count], refs[count : 2 * count]
    w_ref, out_w_ref = refs[2 * count : 2 * count + 2]
    low_ref, top_ref, mixed_ref, lifted_ref, *out_refs = refs[-4 - len(ends) :]
    step = pl.program_id(0)
    start = 0
    for piece, top in zip(pieces, tops):

        @pl.when((step >= start) & (step < start + piece.shape[0]))
        def _(piece=piece, top=top, start=start):
            low_ref[0] = piece[step - start]
            top_ref[0] = top[step - start]

        start += piece.shape[0]

    hidden = w_ref.shape[1] // 2
    lifted = dot(flat(low_ref[...]), w_ref[...])
    first, second = lifted[:, :hidden], lifted[:, hidden:]
    grad_mixed = dot(flat(top_ref[...]), out_w_ref[...], ((1,), (1,)))
    gate = 0.5 * (1.0 + lax.erf(first * (0.5**0.5)))
    slope = gate + first * jnp.exp(first * first * -0.5) * ((2.0 * math.pi) ** -0.5)
    activated = first * gate
    mixed_ref[...] = (activated * second).astype(BF16).reshape(mixed_ref.shape)
    grad = jnp.concatenate(
        [(grad_mixed * second * slope).astype(BF16), (grad_mixed * activated).astype(BF16)],
        axis=1,
    )
    lifted_ref[...] = grad.reshape(lifted_ref.shape)
    partial = dot(grad, w_ref[...], ((1,), (1,))).astype(BF16).reshape(low_ref.shape)
    start = 0
    for out, end in zip(out_refs, ends):

        @pl.when((step >= start) & (step < end))
        def _(out=out):
            out[...] = partial

        start = end


def mlp(pieces, tops, w, out_w, base, ends, earlier=()):
    seqs, block, width = pieces[0].shape[1:]
    hidden = w.shape[1] // 2
    whole_in = (*pieces, *tops, w, out_w)

    def rows(last):
        return pl.BlockSpec((1, seqs, block, last), lambda i: (i + base, 0, 0, 0))

    def within(start, end):
        return pl.BlockSpec(
            (1, seqs, block, width),
            lambda i: (jnp.clip(i - start, 0, end - start - 1), 0, 0, 0),
        )

    starts = (0, *ends[:-1])
    lasts = (width, width, hidden, 2 * hidden)
    return pl.pallas_call(
        functools.partial(mlp_kernel, count=len(pieces), ends=ends),
        grid=(ends[-1],),
        in_specs=[whole(array) for array in whole_in]
        + [pl.BlockSpec(memory_space=pl.ANY)] * len(earlier),
        out_specs=(
            *[rows(last) for last in lasts],
            *[within(start, end) for start, end in zip(starts, ends)],
        ),
        out_shape=(
            *[jax.ShapeDtypeStruct((8, seqs, block, last), BF16) for last in lasts],
            *[
                jax.ShapeDtypeStruct((end - start, seqs, block, width), BF16)
                for start, end in zip(starts, ends)
            ],
        ),
        input_output_aliases={len(whole_in) + at: at for at in range(len(earlier))},
        compiler_params=params(32),
        cost_estimate=COST,
        name="mlp",
    )(*whole_in, *earlier)


def out_grad_kernel(place_ref, rows_ref, grad_ref, keep_ref, send_ref):
    grads = flat(grad_ref[...])
    for index in range(8):
        part = dot(flat(rows_ref[place_ref[index]]), grads, ((0,), (0,))).astype(BF16)
        if index < 5:
            keep_ref[index] = part
        else:
            send_ref[index - 5] = part


def out_grad(place, rows, grads):
    part, width = rows.shape[-1], grads.shape[-1]
    return pl.pallas_call(
        out_grad_kernel,
        in_specs=[SCALARS, whole(rows), whole(grads)],
        out_shape=(
            jax.ShapeDtypeStruct((5, part, width), BF16),
            jax.ShapeDtypeStruct((3, part, width), BF16),
        ),
        compiler_params=params(16),
        cost_estimate=COST,
        name="out_grad",
    )(place, rows, grads)


def branch_back_kernel(place_ref, *refs):
    pieces = refs[:6]
    keep_ref, near_ref, own_ref, residual_ref, top_ref, gain_ref = refs[6:12]
    grad_ref, branch_ref, home_ref, sum_ref, low_ref, side_ref = refs[12:]
    grad_low = wide(flat(keep_ref[...])) + wide(flat(near_ref[...])) + wide(flat(own_ref[...]))
    normed, factor = normalize(flat(residual_ref[...]))
    sum_ref[...] = jnp.sum(grad_low * normed, axis=0, keepdims=True)
    grad = flat(wide(top_ref[...])) + norm_back(grad_low * gain_ref[...], normed, factor)
    grad_ref[...] = grad.reshape(grad_ref.shape)
    low_ref[...] = grad.astype(BF16)
    branch_ref[...] = low_ref[...].reshape(branch_ref.shape)
    heads = home_ref.shape[0] // 2
    side_ref[...] = jnp.zeros_like(side_ref)
    index = 0
    for piece in pieces:
        n = piece.shape[2]
        for inner in range(piece.shape[0]):
            at = place_ref[index]
            columns = pl.ds(pl.multiple_of((at % heads) * n, n), n)
            side_ref[at // heads] += dot(low_ref[:, columns], piece[inner], ((1,), (1,)))
            index += 1
    part = home_ref.shape[3]
    for c in range(2):
        for d in range(heads):
            home = side_ref[c, :, d * part : (d + 1) * part].astype(BF16)
            home_ref[c * heads + d] = home.reshape(home_ref.shape[1:])


def branch_back(place, pieces, keep, near, own, residual, top, gain):
    args = (*pieces, keep, near, own, residual, top, gain)
    seqs, block, width = residual.shape
    tall = pieces[0].shape[1]
    shapes = (
        jax.ShapeDtypeStruct(residual.shape, F32),
        jax.ShapeDtypeStruct(residual.shape, BF16),
        jax.ShapeDtypeStruct((8, seqs, block, tall // 4), BF16),
        jax.ShapeDtypeStruct((1, width), F32),
    )
    return pl.pallas_call(
        branch_back_kernel,
        grid=(1,),
        in_specs=[SCALARS]
        + [whole(piece) for piece in pieces]
        + [pl.BlockSpec((1, seqs * block, width), lambda *_: (0, 0, 0))] * 2
        + [whole(a) for a in args[8:]],
        out_specs=tuple(whole(shape) for shape in shapes),
        out_shape=shapes,
        scratch_shapes=[
            pltpu.VMEM((seqs * block, width), BF16),
            pltpu.VMEM((2, seqs * block, tall), F32),
        ],
        compiler_params=params(24),
        cost_estimate=COST,
        name="branch_back",
    )(place, *args)


def attend_back_kernel(
    place_ref, q_ref, k_ref, v_ref, grad_ref, att_ref, log_ref, cosq_ref, sinq_ref, cos_ref,
    sin_ref, w_ref, low_ref, *refs, seq, last,
):
    if last:
        before_ref, gain1_ref, gain2_ref, keep_ref, send_ref, grad_w_ref, *scratch = refs
    else:
        keep_ref, send_ref, before_ref, *scratch = refs
    proj_ref, sum_k, sum_v = scratch
    step = pl.program_id(0)
    block, part = q_ref.shape[2], q_ref.shape[3]

    @pl.when(step == 0)
    def _():
        sum_k[...] = jnp.zeros_like(sum_k)
        sum_v[...] = jnp.zeros_like(sum_v)

    queries, keys, values = flat(q_ref[...]), flat(k_ref[...]), flat(v_ref[...])
    grads = jnp.concatenate([grad_ref[place_ref[2 * step + inner], seq] for inner in range(2)])
    along = (grads.astype(F32) * flat(att_ref[...])).T
    logs = flat(log_ref[...]).T
    grad_queries = jnp.zeros(queries.shape, F32)
    for head, mask in enumerate(head_masks(queries.shape)):
        own_q = jnp.where(mask, queries, 0)
        own_g = jnp.where(mask, grads, 0)
        scores = dot(keys, own_q, ((1,), (1,)))
        weights = jnp.exp(scores - logs[head * HD : head * HD + 1])
        lifted = dot(values, own_g, ((1,), (1,)))
        row = jnp.sum(along[head * HD : (head + 1) * HD], axis=0, keepdims=True)
        grad_scores = (weights * (lifted - row)).astype(BF16)
        sum_k[...] += dot(grad_scores, own_q)
        sum_v[...] += dot(weights.astype(BF16), own_g)
        grad_queries = jnp.where(mask, dot(grad_scores, keys, ((0,), (0,))), grad_queries)
    grad_queries = lane_rotate(grad_queries * HD**-0.5, cosq_ref[...], -sinq_ref[...])
    rows = pl.multiple_of(step * 2 * block, 2 * block)
    proj_ref[pl.ds(rows, 2 * block), :part] = grad_queries.astype(BF16)

    @pl.when(step == 3)
    def _():
        grad_keys = lane_rotate(sum_k[...], cos_ref[...], -sin_ref[...])
        proj_ref[:, part : 2 * part] = grad_keys.astype(BF16)
        proj_ref[:, 2 * part :] = sum_v[...].astype(BF16)
        partial = dot(proj_ref[...], w_ref[...], ((1,), (1,))).astype(BF16)
        keep_ref[...] = partial[: 5 * block].reshape(5, block, -1)
        send_ref[...] = partial[5 * block :].reshape(3, block, -1)
        grad_w = dot(proj_ref[...], flat(low_ref[...]), ((0,), (0,)))
        if last:
            grad_w = (grad_w + before_ref[...]).T
            along_w = jnp.sum(grad_w * wide(w_ref[...]), axis=1, keepdims=True)
            along_w = jnp.broadcast_to(along_w, (w_ref.shape[0], 128)).T[:1] / gain1_ref[...]
            row = lax.broadcasted_iota(jnp.int32, (GAIN_ROWS, w_ref.shape[0]), 0)
            gains = jnp.where(row == 0, along_w, jnp.where(row == 1, gain2_ref[...], 0.0))
            n = grad_w_ref.shape[1] - GAIN_ROWS
            for at in range(grad_w_ref.shape[0]):
                part_rows = slice(at * n, (at + 1) * n)
                grad_w_ref[at, :n] = grad_w[part_rows].astype(BF16)
                grad_w_ref[at, n:, :n] = gains[:, part_rows].astype(BF16)
                rest = grad_w_ref.shape[2] - n
                grad_w_ref[at, n:, n:] = jnp.zeros((GAIN_ROWS, rest), BF16)
        else:
            before_ref[...] = grad_w


GAIN_ROWS = 16


def attend_back(place, qkv, grads, attended, logs, cosine, sine, w, low, seq, *before, dp=1):
    _, _, block, own = qkv.shape
    part, width = own // 3, w.shape[0]
    last = len(before) > 0
    rows = pl.BlockSpec((2, 1, block, part), lambda i: (i, 0, 0, 0))
    angles = pl.BlockSpec((2 * block, part), lambda i: (i, 0))

    def full(*shape):
        return pl.BlockSpec(shape, lambda i: (0,) * len(shape))

    args = [place, qkv, qkv, qkv, grads, attended, logs, cosine, sine, cosine, sine, w, low]
    in_specs = [
        SCALARS,
        pl.BlockSpec((2, 1, block, part), lambda i: (i, seq, 0, 0)),
        pl.BlockSpec((8, 1, block, part), lambda i: (0, seq, 0, 1)),
        pl.BlockSpec((8, 1, block, part), lambda i: (0, seq, 0, 2)),
        whole(grads),
        rows,
        rows,
        angles,
        angles,
        whole(cosine),
        whole(sine),
        whole(w),
        pl.BlockSpec((8, 1, block, width), lambda i: (0, seq, 0, 0)),
    ]
    shapes = [((5, block, width), BF16), ((3, block, width), BF16)]
    if last:
        args += before
        in_specs += [whole(array) for array in before]
        shapes += [((dp, width // dp + GAIN_ROWS, own), BF16)]
    else:
        shapes += [((own, width), F32)]
    return pl.pallas_call(
        functools.partial(attend_back_kernel, seq=seq, last=last),
        grid=(4,),
        in_specs=in_specs,
        out_specs=tuple(full(*shape) for shape, _ in shapes),
        out_shape=tuple(jax.ShapeDtypeStruct(shape, kind) for shape, kind in shapes),
        scratch_shapes=[
            pltpu.VMEM((8 * block, own), BF16),
            pltpu.VMEM((8 * block, part), F32),
            pltpu.VMEM((8 * block, part), F32),
        ],
        compiler_params=params(60),
        cost_estimate=COST,
        name="attend_back",
    )(*args)


def input_grad_kernel(*refs):
    keeps, (near_ref, own_ref, tokens_ref, residual_ref, gain_ref, out_ref) = refs[:-6], refs[-6:]
    block = tokens_ref.shape[1]
    for seq, keep in enumerate(keeps):
        rows = slice(seq * block, (seq + 1) * block)
        grad = wide(keep[0, :block]) + wide(near_ref[0, rows]) + wide(own_ref[0, rows])
        normed, factor = normalize(wide(tokens_ref[seq]))
        out_ref[seq] = residual_ref[seq] + norm_back(grad * gain_ref[...], normed, factor)


def input_grad(keeps, near, own, tokens, residual, gain):
    rest = (own, tokens, residual, gain)
    return pl.pallas_call(
        input_grad_kernel,
        grid=(1,),
        in_specs=[
            pl.BlockSpec((1, *array.shape[1:]), lambda *_: (0, 0, 0)) for array in (*keeps, near)
        ]
        + [whole(array) for array in rest],
        out_specs=whole(residual),
        out_shape=jax.ShapeDtypeStruct(residual.shape, F32),
        compiler_params=params(16),
        cost_estimate=COST,
        name="input_grad",
    )(*keeps, near, *rest)


def finish_kernel(keep_ref, rows_ref, near_ref, home_ref, residual_ref, out_ref, grad_ref):
    rows = keep_ref.shape[1]
    total = wide(keep_ref[0]) + wide(near_ref[0, :rows]) + wide(home_ref[0, :rows])
    out_ref[...] = (residual_ref[...] + total.reshape(residual_ref.shape)).astype(BF16)
    total = wide(rows_ref[0]) + wide(near_ref[0, rows:]) + wide(home_ref[0, rows:])
    n = grad_ref.shape[2]
    for at in range(grad_ref.shape[0]):
        grad_ref[at] = total[:, at * n : (at + 1) * n].astype(BF16)


def finish(keep, rows, near, home, residual, dp):
    args = (keep, rows, near, home)
    shapes = (
        jax.ShapeDtypeStruct(residual.shape, BF16),
        jax.ShapeDtypeStruct((dp, rows.shape[1], rows.shape[2] // dp), BF16),
    )
    return pl.pallas_call(
        finish_kernel,
        grid=(1,),
        in_specs=[pl.BlockSpec((1, *array.shape[1:]), lambda *_: (0, 0, 0)) for array in args]
        + [whole(residual)],
        out_specs=tuple(whole(shape) for shape in shapes),
        out_shape=shapes,
        compiler_params=params(16),
        cost_estimate=COST,
        name="finish",
    )(*args, residual)


class Group:
    def __init__(self):
        self.heads = lax.axis_size("head")
        self.dp = lax.axis_size("dp")
        self.ctx_at = lax.axis_index("ctx")
        self.head_at = lax.axis_index("head")
        self.dp_at = lax.axis_index("dp")
        self.at = self.ctx_at * self.heads + self.head_at
        near, far = [], []
        for c in range(2):
            for h in range(self.heads):
                x, y = (c ^ 1) * self.heads + h, c * self.heads + (h ^ 2)
                near.append((c * self.heads + h, x if h % 2 == 0 else y))
                far.append((c * self.heads + h, y if h % 2 == 0 else x))
        self.near, self.far = near, far

    def order(self):
        first = jnp.where(self.head_at % 2 == 0, 4, 2)
        second = 6 - first
        return jnp.stack(
            [self.at ^ bits for bits in (0, 1, first, first ^ 1, 6, second ^ 1, second, 7)]
        )

    def swap(self, values, bit):
        if bit == 4:
            return lax.ppermute(values, "ctx", [(0, 1), (1, 0)])
        return lax.ppermute(values, "head", [(i, i ^ bit) for i in range(self.heads)])

    def mate(self, values):
        return self.swap(values, 1)

    def to_near(self, values):
        return lax.ppermute(values, GROUP, self.near)

    def to_far(self, values):
        return lax.ppermute(values, GROUP, self.far)

    def rows_back(self, values, place):
        pairs, same = [], False
        for d in range(self.dp):
            for h in range(self.heads):
                if (d, h) == (place[h], d):
                    same = same | ((self.dp_at == d) & (self.head_at == h))
                else:
                    pairs.append((d * self.heads + h, place[h] * self.heads + d))
        return jnp.where(same, values, lax.ppermute(values, ("dp", "head"), pairs))

    def across(self, values, step):
        return lax.ppermute(values, "dp", [(i, i ^ step) for i in range(self.dp)])


def pick(array, index, axis):
    return lax.dynamic_index_in_dim(array, index, axis, keepdims=False)


def after(values, *earlier):
    return lax.optimization_barrier((values, earlier))[0]


def local_split(tokens, cotangent, w_qkv, w_attn_out, w_in, w_mlp_out, norm_gain1, norm_gain2):
    seqs, block, width = tokens.shape
    group = Group()
    heads, dp = group.heads, group.dp
    at_c, at_h = group.ctx_at, group.head_at
    parts = 2 * heads
    hidden = w_in.shape[1] // 2 // parts
    padded = -(-hidden // 128) * 128
    own_width = width // parts
    half = heads // 2
    rows_here = w_qkv.shape[0]
    place = [2 * (h % half) + h // half for h in range(heads)]
    straight = list(range(heads))
    order = group.order()
    scalars = jnp.concatenate([order, jnp.stack([group.dp_at, at_c])]).astype(jnp.int32)
    mate, near, far = group.mate, group.to_near, group.to_far

    def in_order(own, other):
        return jnp.where(at_c == 0, jnp.stack([own, other]), jnp.stack([other, own]))

    def exchange(values):
        return lax.all_to_all(values, GROUP, split_axis=0, concat_axis=0, tiled=True)


    gains = jnp.pad(
        jnp.stack([norm_gain1, norm_gain2]), ((0, 14), (0, 3 * own_width - rows_here))
    )
    qkv_view = w_qkv.reshape(rows_here, 3, width)

    def qkv_part(at):
        start = (2 * at_h + at) * own_width
        cut = lax.dynamic_slice_in_dim(qkv_view, start, own_width, 2)
        return jnp.concatenate([cut.reshape(rows_here, 3 * own_width), gains])

    x_own = tokens[None]
    x_mate = mate(x_own)
    qkv_other, qkv_own = qkv_part(1 - at_c), qkv_part(at_c)
    qkv_cross = group.swap(after(qkv_other, x_own), 4)
    in_view = after(w_in, qkv_other).reshape(rows_here, 2, heads, 2, hidden)
    in_view = pick(in_view, 2 * (at_h % half) + at_h // half, 2)

    def in_part(at):
        cut = pick(in_view, at, 2)
        return jnp.pad(cut, ((0, 0), (0, 0), (0, padded - hidden))).reshape(rows_here, 2 * padded)

    in_other, in_own = in_part(1 - at_c), in_part(at_c)
    in_cross = group.swap(after(in_other, qkv_cross), 4)
    x_chip = jnp.concatenate([x_own, after(x_mate, qkv_cross, qkv_own)])
    x_near = near(x_chip)
    qkv_pair = jnp.stack([qkv_own, qkv_cross])
    qkv_pieces = [qkv_pair] + [group.across(qkv_pair, step) for step in range(1, dp)]

    positions = after(order, qkv_pair)[:, None] * block + jnp.arange(block, dtype=jnp.int32)
    lane = jnp.arange(own_width, dtype=jnp.int32)
    frequency = jnp.exp(
        (lane % (HD // 2)).astype(F32) * (-math.log(ROPE_BASE) / (HD // 2))
    )
    angles = wide(positions.reshape(-1))[:, None] * frequency[None, :]
    cosine = jnp.cos(angles)
    sine = jnp.sin(angles) * jnp.where(lane % HD < HD // 2, -1.0, 1.0)[None, :]

    x_far = far(x_near[:1])
    slices = jnp.concatenate([w_attn_out, w_mlp_out])
    slices = after(slices, x_far, in_other, in_own, cosine, sine, *qkv_pieces)
    slices = lax.dynamic_slice_in_dim(slices, at_h * (width // heads), width // heads, 1)
    slices = jnp.pad(slices, ((0, 64), (0, 0)))
    slices = lax.all_gather(slices, "dp", axis=0)
    x_near = after(x_near, *qkv_pieces, cosine, sine, in_cross, in_own)
    x_near_mate = mate(x_near)
    cot_own = after(cotangent, x_near)[None]
    cot_mate = mate(cot_own)
    in_pair, x_far = lax.optimization_barrier((in_order(in_own, in_cross), x_far))
    weight_in = lax.all_gather(in_pair, "dp", axis=0).reshape(width, -1)
    cot_chip = jnp.concatenate([cot_own, cot_mate])
    x_far = after(x_far, cot_chip)
    x_far_mate = mate(x_far)

    cot_near = near(after(cot_chip, x_far))
    out_rows = w_attn_out.shape[0]
    x_pieces = (x_own, x_mate, x_near, x_far, x_near_mate, x_far_mate)
    low1, qkv, weight_qkv, gain_one, gain_two = project(
        scalars, x_pieces, qkv_pieces, cosine, sine
    )

    att_0, log_0, home_0 = attend(scalars, qkv)
    cot_near = after(cot_near, home_0)
    cot_far, cot_near_mate = far(cot_near[:1]), mate(cot_near)
    slices = after(slices, home_0)
    out_own = slices[:, :out_rows].reshape(1, dp * out_rows, -1)
    out_mate = mate(out_own)
    out_chip = jnp.concatenate([out_own, out_mate])
    out_near = near(out_chip)
    mlp_slices = jnp.stack(
        [slices[place[h], out_rows : out_rows + hidden] for h in range(heads)]
    )
    mlp_slices = lax.all_to_all(mlp_slices, "head", split_axis=0, concat_axis=0, tiled=True)
    att_1, log_1, home = attend(scalars, after(qkv, cot_near, out_chip), home_0)
    home, cot_far, out_near = lax.optimization_barrier((home, cot_far, out_near))
    att_rows = exchange(home)
    out_far, out_near_mate = far(out_near[:1]), mate(out_near)
    out_far_mate, cot_far_mate = mate(after(out_far, home)), mate(after(cot_far, home))
    out_pieces = (out_own, out_mate, out_near, out_far, out_near_mate, out_far_mate)
    weight_mlp = jnp.moveaxis(after(mlp_slices, home), 0, 1).reshape(hidden, width)
    weight_mlp = jnp.pad(weight_mlp, ((0, padded - hidden), (0, 0)))
    residual, low2 = branch(
        scalars, out_pieces, after(att_rows, cot_far_mate, weight_mlp), tokens, gain_two
    )

    low_own = low2[None]
    low_mate = mate(low_own)
    low_near = near(jnp.concatenate([low_own, after(low_mate, weight_in)]))
    *arrays, keep_a = mlp(
        (low_own, low_mate), (cot_own, cot_mate), weight_in, weight_mlp, 0, (2,)
    )
    low_near = after(low_near, keep_a)
    low_far, low_near_mate = far(low_near[:1]), mate(low_near)
    *arrays, keep_b = mlp((low_near,), (cot_near,), weight_in, weight_mlp, 2, (2,), arrays)
    low_far_mate = mate(after(low_far, keep_b))
    low2_all, cot_all, mixed, grad_lifted, keep_c, send = mlp(
        (low_far, low_near_mate, low_far_mate),
        (cot_far, cot_near_mate, cot_far_mate),
        weight_in,
        weight_mlp,
        4,
        (1, 4),
        arrays,
    )

    def over_tokens(left, right):
        return dot(flat(left), flat(right), ((0,), (0,)))

    def scatter(values):
        return lax.psum_scatter(values.astype(BF16), "dp", scatter_dimension=0, tiled=True)

    def columns_first(values):
        return jnp.moveaxis(values.reshape(values.shape[0], dp, -1), 1, 0)

    rows = seqs * block

    def by_rows(values):
        return values.reshape(values.shape[0], -1, width)

    keep_a, keep_b, keep_c, send = (by_rows(array) for array in (keep_a, keep_b, keep_c, send))
    met = mate(send)
    last = combine([(rows, [(keep_c, 0, 0), (met, 2, 0)])])
    last_far = far(last)
    grad_mlp = columns_first(over_tokens(after(mixed, last), cot_all)[:hidden]).astype(BF16)
    last_far = after(last_far, grad_mlp)
    grad_mlp = scatter(grad_mlp)[0]
    chip = combine(
        [(rows, [(keep_b, 0, 0), (met, 0, 0), (last_far, 0, 0)])],
        [(rows, [(keep_b, 1, 0), (met, 1, 0)])],
    )
    chip_near = near(chip)
    grad_in = over_tokens(low2_all, after(grad_lifted, chip)).astype(BF16)
    cut = 5 * rows
    mixed_flat = flat(after(mixed, chip))
    out_keep = dot(mixed_flat[:cut], weight_mlp).astype(BF16).reshape(5, rows, width)
    out_send = dot(mixed_flat[cut:], weight_mlp).astype(BF16).reshape(3, rows, width)
    chip_near = after(chip_near, grad_in, out_keep, out_send)
    grad_in = scatter(grad_in)
    home = mate(combine([(rows, [(keep_a, 1, 0), (chip_near, 1, 0)])])[0])
    out_met = mate(after(out_send, chip_near))
    grad_residual, grad_branch, home, gain2_sum = branch_back(
        scalars, out_pieces, keep_a, chip_near, home, residual, cotangent, gain_two
    )
    grad_home = exchange(home)

    rows_keep, rows_send = out_grad(scalars, after(att_rows, home), grad_branch)
    rows_met = mate(rows_send)
    few = rows_keep.shape[1]

    def ends(index, at, *more):
        kept = [(out_keep, index, 0)], [(rows_keep, index, 0)]
        if at is not None:
            kept[0].append((out_met, at, 0))
            kept[1].append((rows_met, at, 0))
        for array, where in more:
            kept[0].append((array, where, 0))
            kept[1].append((array, where, rows))
        return [(rows, kept[0]), (few, kept[1])]

    end_last = combine(ends(4, 2))
    grad_home = after(grad_home, end_last, grad_mlp)
    end_far = far(after(end_last, grad_home))
    keep_0, send_0, before = attend_back(
        scalars, qkv, grad_home, att_0, log_0, cosine, sine, weight_qkv, low1, 0
    )
    met_0 = mate(send_0)
    end_far = after(end_far, send_0)
    end_chip = combine(ends(2, 0, (end_far, 0)), ends(3, 1))
    end_near = near(end_chip)
    keep_1, send_1, grad_qkv = attend_back(
        scalars, qkv, after(grad_home, end_chip), att_1, log_1, cosine, sine,
        weight_qkv, low1, 1, before, gain_one, gain2_sum, dp=dp,
    )

    grad_qkv = scatter(grad_qkv.reshape(-1, grad_qkv.shape[2]))
    met_1 = mate(send_1)
    end_home = combine(ends(1, None, (after(end_near, send_1), 1)))
    in_parts = after(grad_in, send_1).reshape(2, rows_here, -1)
    in_other = pick(in_parts, 1 - at_c, 0)
    met_1, end_home, in_other = lax.optimization_barrier((met_1, end_home, in_other))
    in_cross = group.swap(in_other, 4)
    end_home = mate(end_home)

    def both(index, at, *more):
        kept = [(keep_0, index, 0)], [(keep_1, index, 0)]
        if at is not None:
            kept[0].append((met_0, at, 0))
            kept[1].append((met_1, at, 0))
        for array, where in more:
            kept[0].append((array, where, 0))
            kept[1].append((array, where, block))
        return [(block, kept[0]), (block, kept[1])]

    last = combine(both(4, 2))
    last_far = far(last)
    result, grad_out = finish(
        out_keep, rows_keep, end_near, after(end_home, last), residual, dp
    )
    last_far, grad_out = lax.optimization_barrier((after(last_far, in_cross), grad_out))
    grad_out = scatter(grad_out)[0]
    chip = combine(both(2, 0, (last_far, 0)), both(3, 1), mebibytes=60)
    chip_near = near(chip)

    grad_in = in_order(after(pick(in_parts, at_c, 0), chip), in_cross)
    late = at_h // half
    grad_in = jnp.stack([grad_in[..., :hidden], grad_in[..., padded : padded + hidden]])
    stays = pick(grad_in, late, 0)
    comes = group.swap(pick(grad_in, 1 - late, 0), half)
    grad_qkv = after(grad_qkv, chip)
    both_rows = 2 * rows_here
    qkv_parts = grad_qkv[:both_rows].reshape(2, rows_here, -1)
    gains = grad_qkv[both_rows:]
    cross = jnp.concatenate([pick(qkv_parts, 1 - at_c, 0), gains])
    cross = group.swap(cross, 4)
    chip_near = after(chip_near, comes, cross)
    home = combine(both(1, None, (chip_near, 1)))
    home = mate(home)
    grad_input = input_grad((keep_0, keep_1), chip_near, home, tokens, grad_residual, gain_one)
    cross = after(cross, grad_input)
    grad_qkv = in_order(pick(qkv_parts, at_c, 0), cross[:rows_here])
    gains = (wide(gains) + wide(cross[rows_here:])).astype(BF16)
    gains = wide(gains) + sum(wide(group.swap(gains, bit)) for bit in range(1, heads))
    grad_out, grad_mlp, grad_input = lax.optimization_barrier((grad_out, grad_mlp, grad_input))
    grad_mlp = group.rows_back(grad_mlp, place)
    grad_out = wide(group.rows_back(grad_out, straight))

    grad_mlp = wide(grad_mlp)
    grad_in = jnp.where(
        late == 0, jnp.concatenate([stays, comes]), jnp.concatenate([comes, stays])
    )
    grad_in = wide(jnp.moveaxis(grad_in, 0, 1).reshape(rows_here, -1))

    per_device = width // (dp * parts)
    start = group.at * per_device
    grad_gain1, grad_gain2 = (
        lax.dynamic_slice_in_dim(gains[i], start, per_device, 0) for i in range(2)
    )
    grad_qkv = grad_qkv.reshape(2, rows_here, 3, own_width)
    grad_qkv = jnp.moveaxis(grad_qkv, 2, 0)
    odd = at_h % 2
    stays = pick(grad_qkv, odd + late, 0)
    core = group.swap(pick(grad_qkv, 1 - odd + late, 0), 1)
    chip = group.swap(pick(grad_qkv, 2 - 2 * late, 0), 2)
    grad_qkv = jnp.where(
        odd == 0, jnp.concatenate([stays, core, chip]), jnp.concatenate([chip, core, stays])
    )
    grad_qkv = wide(jnp.moveaxis(grad_qkv, 0, 1).reshape(rows_here, -1))

    return (
        result,
        grad_input,
        grad_qkv,
        grad_out,
        grad_in,
        grad_mlp,
        grad_gain1,
        grad_gain2,
    )


def local(tokens, cotangent, w_qkv, w_attn_out, w_in, w_mlp_out, norm_gain1, norm_gain2):
    args = (tokens, cotangent, w_qkv, w_attn_out, w_in, w_mlp_out, norm_gain1, norm_gain2)
    sizes = [lax.axis_size(axis) for axis in ("dp", "ctx", "head")]
    if sizes == [4, 2, 4] and tokens.shape[2] == 8 * 2 * HD and tokens.shape[1] % 16 == 0:
        return local_split(*args)
    return local_general(*args)


def solution(mesh):
    in_specs = (
        P("dp", ("ctx", "head"), None),
        P("dp", ("ctx", "head"), None),
        P(("dp", "ctx"), None),
        P(("dp", "ctx"), None),
        P(("dp", "ctx"), None),
        P(("dp", "ctx"), None),
        P(("dp", "ctx")),
        P(("dp", "ctx")),
    )
    out_specs = (
        P("dp", ("ctx", "head"), None),
        P("dp", ("ctx", "head"), None),
        P(("dp", "ctx"), "head"),
        P(("dp", "ctx"), "head"),
        P(("dp", "ctx"), "head"),
        P(("dp", "ctx"), "head"),
        P(("dp", "ctx", "head")),
        P(("dp", "ctx", "head")),
    )
    return jax.shard_map(local, mesh=mesh, in_specs=in_specs, out_specs=out_specs, check_vma=False)
```
